32 devices in a mesh: dp: 8 (over z, x), mp: 4 (over y, core).
Axes of the slice: x: 2, y: 2, z: 4, core: 2. Of those that a mesh axis runs over, the one named last changes fastest.
Arguments:
- tokens: bfloat16 [8192, 2048], P('dp'), may hold values from -6 to 6
- cotangent: bfloat16 [8192, 2048], P('dp'), may hold values from -6 to 6
- segment_ids: int32 [8, 1024], P('dp'), may hold values from 0 to 10, never falling along the last dimension, each value on 1 to 512 neighbouring positions
- attend_gain: float32 [2048], replicated, may hold values from 0.25 to 1.75
- expand_gain: float32 [2048], replicated, may hold values from 0.25 to 1.75
- heads_base: bfloat16 [3, 2048, 2048], P(None, None, 'mp'), may hold values from -0.125 to 0.125
- heads_left: float32 [3, 2048, 16], replicated, may hold values from -0.125 to 0.125
- heads_right: float32 [3, 16, 2048], P(None, None, 'mp'), may hold values from -0.375 to 0.375
- heads_magnitude: float32 [3, 2048], P(None, 'mp'), may hold values from 0.5 to 2
- output_base: bfloat16 [2048, 2048], P('mp'), may hold values from -0.5 to 0.5
- output_left: float32 [2048, 16], P('mp'), may hold values from -0.125 to 0.125
- output_right: float32 [16, 2048], replicated, may hold values from -1.5 to 1.5
- output_magnitude: float32 [2048], replicated, may hold values from 2 to 8
- expand_base: bfloat16 [2, 2048, 5632], P(None, None, 'mp'), may hold values from -0.125 to 0.125
- expand_left: float32 [2, 2048, 16], replicated, may hold values from -0.125 to 0.125
- expand_right: float32 [2, 16, 5632], P(None, None, 'mp'), may hold values from -0.375 to 0.375
- expand_magnitude: float32 [2, 5632], P(None, 'mp'), may hold values from 0.5 to 2
- shrink_base: bfloat16 [5632, 2048], P('mp'), may hold values from -0.078125 to 0.078125
- shrink_left: float32 [5632, 16], P('mp'), may hold values from -0.078125 to 0.078125
- shrink_right: float32 [16, 2048], replicated, may hold values from -0.375 to 0.375
- shrink_magnitude: float32 [2048], replicated, may hold values from 0.7 to 3
Outputs:
- mixed_tokens: bfloat16 [8192, 2048], P(('dp', 'mp'))
- grad_tokens: float32 [8192, 2048], P(('dp', 'mp'))
- grad_attend_gain: float32 [2048], replicated
- grad_expand_gain: float32 [2048], replicated
- grad_heads_left: float32 [3, 2048, 16], replicated
- grad_heads_right: float32 [3, 16, 2048], P(None, None, 'mp')
- grad_heads_magnitude: float32 [3, 2048], P(None, 'mp')
- grad_output_left: float32 [2048, 16], P('mp')
- grad_output_right: float32 [16, 2048], replicated
- grad_output_magnitude: float32 [2048], replicated
- grad_expand_left: float32 [2, 2048, 16], replicated
- grad_expand_right: float32 [2, 16, 5632], P(None, None, 'mp')
- grad_expand_magnitude: float32 [2, 5632], P(None, 'mp')
- grad_shrink_left: float32 [5632, 16], P('mp')
- grad_shrink_right: float32 [16, 2048], replicated
- grad_shrink_magnitude: float32 [2048], replicated
The draws below stay inside these ranges and needn't reach their ends.
Inputs may be any that keep to these rules, and one draw needn't show every extreme that they name: `segment_ids`: along each packed row the ids never fall; one id marks one instruction pair.
All inputs are finite; a program needn't handle non-finite values.
Results may differ from the reference program's by a relative error of at most 0.015.
The reference program's roundings to bfloat16 on the way count: a program that leaves them out, or rounds other values in their place, can miss the bound.
Values may be sent and summed in bfloat16 or wider, within the bound.
A program may use at most 384 MiB of HBM per device.

```python
import math
import jax
import jax.numpy as jnp
import numpy as np
from jax import lax

D = 2048
HEADS = 16
HEAD_DIM = 128
FF = 5632
RANK = 16
SEQ = 1024
ROWS = 8
TOKENS = 8192


def block_levels(key, shape, cuts, low, high):
    loudness, own = 1.0, jax.random.fold_in(key, 6)
    for dim, parts in cuts:
        draws = jnp.exp(jax.random.uniform(jax.random.fold_in(own, dim), (parts,), jnp.float32, low / len(cuts), high / len(cuts)))
        loudness = loudness * jnp.repeat(draws, shape[dim] // parts).reshape([-1 if axis == dim else 1 for axis in range(len(shape))])
    return loudness


def profile(count, total, most, slope):
    weights = [(1 << 20) // math.isqrt(rank ** slope) + 1 for rank in range(2, count + 1)]
    spare, holding = total - most - (count - 1), [1] * (count - 1)
    while spare > 0:
        candidates = [i for i in range(count - 1) if holding[i] < most]
        pool, left = sum([weights[i] for i in candidates]), spare
        for i in candidates:
            extra = min(most - holding[i], max(1, left * weights[i] // pool), spare)
            holding[i] = holding[i] + extra
            spare = spare - extra
    return np.array([most] + holding)


def uneven_parts(stream_key, amount, total, limit, skew):
    if amount == 2:
        one = jax.random.randint(stream_key, (), max(1, total - limit), min(limit, total - 1) + 1)
        return jnp.stack([one, total - one])
    tallies = jnp.asarray(profile(amount, total, limit, skew), jnp.int32)
    couples = (amount - 1) // 2
    source_of, taker = tallies[1:1 + 2 * couples:2], tallies[2:2 + 2 * couples:2]
    slack = jnp.minimum(source_of - 1, limit - taker)
    passed = jax.random.randint(jax.random.fold_in(stream_key, 1), (couples,), 0, 1 << 20) % (slack + 1)
    tallies = tallies.at[1:1 + 2 * couples:2].set(source_of - passed).at[2:2 + 2 * couples:2].set(taker + passed)
    return tallies[jax.random.permutation(jax.random.fold_in(stream_key, 2), amount)]


def gaussian(own_key, shape, spread, limit, cuts=(), kind=jnp.bfloat16):
    array = jax.random.normal(own_key, shape, jnp.float32) * spread
    if len(cuts) > 0:
        array = block_levels(own_key, shape, cuts, -0.22, 0.18) * array
    return jnp.clip(array, min=-limit, max=limit).astype(kind)


def setup_inputs(seed: int = 0) -> dict:
    keys = jax.random.split(jax.random.key(seed), 22)
    return {
        "tokens": gaussian(keys[0], (TOKENS, D), 1.0, 6.0, ((0, 8),)),
        "cotangent": gaussian(keys[1], (TOKENS, D), 1.0, 6.0, ((0, 8),)),
        "segment_ids": jax.vmap(lambda own: jnp.searchsorted(jnp.cumsum(uneven_parts(own, SEQ // 128 + 3, SEQ, SEQ // 2, 0)), jnp.arange(SEQ), side="right"))(jax.random.split(keys[2], ROWS)).reshape((ROWS, SEQ)).astype(jnp.int32),
        "attend_gain": jnp.clip(1.0 + 0.15 * jax.random.normal(keys[3], (D,), jnp.float32), 0.25, 1.75),
        "expand_gain": jnp.clip(1.0 + 0.15 * jax.random.normal(keys[4], (D,), jnp.float32), 0.25, 1.75),
        "heads_base": gaussian(keys[5], (3, D, HEADS * HEAD_DIM), D ** -0.5, 0.125, ((2, 4),)),
        "heads_left": gaussian(keys[6], (3, D, RANK), D ** -0.5, 0.125, (), jnp.float32),
        "heads_right": gaussian(keys[7], (3, RANK, HEADS * HEAD_DIM), (16 * RANK) ** -0.5, 0.375, ((2, 4),), jnp.float32),
        "heads_magnitude": jnp.clip(jnp.exp(math.log(2.0) - 1.3862944 * jax.random.uniform(keys[8], (3, HEADS * HEAD_DIM), jnp.float32) ** block_levels(keys[8], (3, HEADS * HEAD_DIM), ((1, 4),), -0.2, 0.2)), 0.5, 2.0),
        "output_base": gaussian(keys[9], (HEADS * HEAD_DIM, D), (HEADS * HEAD_DIM // 16) ** -0.5, 0.5, ((0, 4),)),
        "output_left": gaussian(keys[10], (HEADS * HEAD_DIM, RANK), (HEADS * HEAD_DIM) ** -0.5, 0.125, ((0, 4),), jnp.float32),
        "output_right": gaussian(keys[11], (RANK, D), RANK ** -0.5, 1.5, (), jnp.float32),
        "output_magnitude": jnp.clip(jnp.exp(jax.random.uniform(keys[12], (D,), jnp.float32, math.log(2.0), math.log(8.0))), 2.0, 8.0),
        "expand_base": gaussian(keys[13], (2, D, FF), D ** -0.5, 0.125, ((2, 4),)),
        "expand_left": gaussian(keys[14], (2, D, RANK), D ** -0.5, 0.125, (), jnp.float32),
        "expand_right": gaussian(keys[15], (2, RANK, FF), (16 * RANK) ** -0.5, 0.375, ((2, 4),), jnp.float32),
        "expand_magnitude": jnp.clip(jnp.exp(math.log(2.0) - 1.3862944 * jax.random.uniform(keys[16], (2, FF), jnp.float32) ** block_levels(keys[16], (2, FF), ((1, 4),), -0.2, 0.2)), 0.5, 2.0),
        "shrink_base": gaussian(keys[17], (FF, D), FF ** -0.5, 0.078125, ((0, 4),)),
        "shrink_left": gaussian(keys[18], (FF, RANK), FF ** -0.5, 0.078125, ((0, 4),), jnp.float32),
        "shrink_right": gaussian(keys[19], (RANK, D), (16 * RANK) ** -0.5, 0.375, (), jnp.float32),
        "shrink_magnitude": jnp.clip(jnp.exp(jax.random.uniform(keys[20], (D,), jnp.float32, math.log(0.7), math.log(3.0))), 0.7, 3.0),
    }


HIGH = lax.Precision.HIGHEST
ADAPT_SCALE = 2.0
NORM_EPS = 1e-05
ROPE_BASE = 10000.0
MASKED = -1e+30

@jax.custom_vjp
def low(v):
    return lax.optimization_barrier(v.astype(jnp.bfloat16)).astype(jnp.float32)

@jax.custom_vjp
def low_back(v):
    return v

def low_keep(v):
    return (low(v), None)

def low_pass(kept, grad):
    return (grad,)

def back_keep(v):
    return (v, None)

def back_low(kept, grad):
    return (low(grad),)
low.defvjp(low_keep, low_pass)
low_back.defvjp(back_keep, back_low)

def geometry(segment):
    length = segment.shape[0]
    places = lax.broadcasted_iota(jnp.int32, (length, length), 0)
    others = lax.broadcasted_iota(jnp.int32, (length, length), 1)
    visible = (segment[:, None] == segment[None, :]) & (others <= places)
    offset = lax.optimization_barrier(jnp.sum(visible.astype(jnp.float32), axis=1)) - 1.0
    half_dim = HEAD_DIM // 2
    frequency = jnp.exp(-jnp.log(ROPE_BASE) * 2.0 * jnp.arange(half_dim, dtype=jnp.float32) / HEAD_DIM)
    angles = offset[:, None] * frequency[None, :]
    angles = jnp.concatenate([angles, angles], axis=1)
    return (visible, jnp.cos(angles)[:, None, :], jnp.sin(angles)[:, None, :])

def rotate(values, cos_table, sine_table):
    half_dim = values.shape[-1] // 2
    turned = jnp.concatenate([-values[..., half_dim:], values[..., :half_dim]], axis=-1)
    return values * cos_table + turned * sine_table

def attend_row(pieces):
    queries, key_rows, values, segment = pieces
    visible, cos_table, sine_table = geometry(segment)
    queries = low(rotate(queries, cos_table, sine_table))
    key_rows = low(rotate(key_rows, cos_table, sine_table))
    values = low(values)
    scores = low_back(jnp.einsum('qhd,khd->hqk', queries, key_rows, precision=HIGH) * HEAD_DIM ** (-0.5))
    scores = jnp.where(visible[None], scores, MASKED)
    row_max = lax.optimization_barrier(jnp.max(scores, axis=-1, keepdims=True))
    exp_scores = jnp.exp(scores - row_max)
    probability = low(exp_scores / lax.optimization_barrier(jnp.sum(exp_scores, axis=-1, keepdims=True)))
    return jnp.einsum('hqk,khd->qhd', probability, values, precision=HIGH)

def direction(weight_base, left_map, right_map, magnitude):
    merged = weight_base + ADAPT_SCALE * jnp.dot(left_map, right_map, precision=HIGH)
    col_norm = jnp.sqrt(lax.optimization_barrier(jnp.sum(merged * merged, axis=0)))
    return (low(merged), magnitude / col_norm)

def project(inputs, merged, col_scale):
    return low_back(jnp.dot(inputs, merged, precision=HIGH)) * col_scale

def normalize(values, gain):
    factor = lax.rsqrt(lax.optimization_barrier(jnp.mean(values * values, axis=-1, keepdims=True)) + NORM_EPS)
    return low(values * factor * gain)

def reference(tokens, cotangent, segment_ids, attend_gain, expand_gain, heads_base, heads_left, heads_right, heads_magnitude, output_base, output_left, output_right, output_magnitude, expand_base, expand_left, expand_right, expand_magnitude, shrink_base, shrink_left, shrink_right, shrink_magnitude):
    heads_wide = heads_base.astype(jnp.float32)
    output_wide = output_base.astype(jnp.float32)
    expand_wide = expand_base.astype(jnp.float32)
    shrink_wide = shrink_base.astype(jnp.float32)

    def layer(inputs, attend_gain, expand_gain, heads_left, heads_right, heads_magnitude, output_left, output_right, output_magnitude, expand_left, expand_right, expand_magnitude, shrink_left, shrink_right, shrink_magnitude):
        normed = normalize(inputs, attend_gain)
        streams = []
        for member in range(3):
            merged, col_scale = direction(heads_wide[member], heads_left[member], heads_right[member], heads_magnitude[member])
            streams.append(project(normed, merged, col_scale).reshape(ROWS, SEQ, HEADS, HEAD_DIM))
        attended = lax.map(jax.checkpoint(attend_row), (streams[0], streams[1], streams[2], segment_ids))
        heads_out = low(low_back(attended.reshape(TOKENS, HEADS * HEAD_DIM)))
        merged, col_scale = direction(output_wide, output_left, output_right, output_magnitude)
        hidden = inputs + project(heads_out, merged, col_scale)
        normed_mid = normalize(hidden, expand_gain)
        merged, col_scale = direction(expand_wide[0], expand_left[0], expand_right[0], expand_magnitude[0])
        gate_act = project(normed_mid, merged, col_scale)
        merged, col_scale = direction(expand_wide[1], expand_left[1], expand_right[1], expand_magnitude[1])
        up_act = project(normed_mid, merged, col_scale)
        product = low(gate_act * jax.nn.sigmoid(gate_act) * up_act)
        merged, col_scale = direction(shrink_wide, shrink_left, shrink_right, shrink_magnitude)
        return hidden + project(product, merged, col_scale)
    output, pullback = jax.vjp(layer, tokens.astype(jnp.float32), attend_gain, expand_gain, heads_left, heads_right, heads_magnitude, output_left, output_right, output_magnitude, expand_left, expand_right, expand_magnitude, shrink_left, shrink_right, shrink_magnitude)
    gradients = pullback(cotangent.astype(jnp.float32))
    return (output.astype(jnp.bfloat16), gradients[0], gradients[1], gradients[2], gradients[3], gradients[4], gradients[5], gradients[6], gradients[7], gradients[8], gradients[9], gradients[10], gradients[11], gradients[12], gradients[13], gradients[14])
```

```python
import functools

import jax
import jax.numpy as jnp
from jax import lax
from jax.experimental import pallas as pl
from jax.experimental.pallas import tpu as pltpu
from jax.sharding import PartitionSpec as P

HEAD_DIM = 128
CORES = 2
LONGEST = 512
ATTEND_BLOCK = 256
ADAPT_SCALE = 2.0
NORM_EPS = 1e-05
ROPE_BASE = 10000.0
MASKED = -1e30

F32 = jnp.float32
LOW = jnp.bfloat16
NN = (((1,), (0,)), ((), ()))
NT = (((1,), (1,)), ((), ()))
TN = (((0,), (0,)), ((), ()))


def dot(left, right, dims=NN):
    return lax.dot_general(left, right, dims, preferred_element_type=F32)


def shape(dims, kind):
    return jax.ShapeDtypeStruct(tuple(dims), kind)


def call(kernel, operands, grid, in_specs, out_specs, out_shape, scratch=(), prefetch=(), flops=0, mib=48):
    moved = sum(v.size * v.dtype.itemsize for v in operands)
    moved += sum(v.size * v.dtype.itemsize for v in out_shape)
    return pl.pallas_call(
        kernel,
        out_shape=out_shape,
        grid_spec=pltpu.PrefetchScalarGridSpec(
            num_scalar_prefetch=len(prefetch),
            grid=grid,
            in_specs=in_specs,
            out_specs=out_specs,
            scratch_shapes=scratch,
        ),
        compiler_params=pltpu.CompilerParams(vmem_limit_bytes=mib * 2**20),
        cost_estimate=pl.CostEstimate(flops=flops, bytes_accessed=moved, transcendentals=0),
    )(*prefetch, *operands)


def tile_of(size, most):
    return most if size % most == 0 else size


def split_rows(values):
    top = values.astype(LOW)
    rest = (values - top.astype(F32)).astype(LOW)
    return jnp.concatenate([top, rest], axis=0)


def left_pairs(left_map):
    turned = jnp.swapaxes(left_map, -1, -2)
    top = lax.reduce_precision(turned, 8, 7)
    return jnp.concatenate([top, turned - top], axis=-2).astype(LOW)


def fold(values):
    half = values.shape[0] // 2
    return values[:half] + values[half:]


def merge_tile(base_at, low_put, left_rows, right, depth):
    rank = right.shape[0]
    doubled = ADAPT_SCALE * right
    top = doubled.astype(LOW)
    rest = (doubled - top.astype(F32)).astype(LOW)
    right_stack = jnp.concatenate([top, rest, top], axis=0)
    left_stack = jnp.concatenate([left_rows[:rank], left_rows[:rank], left_rows[rank:]], axis=0)
    squares = jnp.zeros((1, right.shape[1]), F32)
    step = 128 if depth % 128 == 0 else depth
    for start in range(0, depth, step):
        merged = base_at(start, step).astype(F32) + dot(
            left_stack[:, start : start + step], right_stack, TN
        )
        low_put(start, step, merged.astype(LOW))
        squares = squares + jnp.sum(merged * merged, axis=0, keepdims=True)
    return squares


def merge_kernel(base_ref, left_ref, right_ref, low_ref, squares_ref):
    depth = base_ref.shape[1]

    def put(start, step, tile):
        low_ref[0, start : start + step, :] = tile

    squares = merge_tile(
        lambda start, step: base_ref[0, start : start + step, :],
        put,
        left_ref[0],
        right_ref[0],
        depth,
    )

    @pl.when(pl.program_id(2) == 0)
    def _():
        squares_ref[0] = squares

    @pl.when(pl.program_id(2) > 0)
    def _():
        squares_ref[0] += squares


def merge(base, left_rows, right, deep, wide):
    members, depth, width = base.shape
    pairs, rank = left_rows.shape[1], right.shape[1]
    return call(
        merge_kernel,
        (base, left_rows, right),
        (members, width // wide, depth // deep),
        [
            pl.BlockSpec((1, deep, wide), lambda m, n, k: (m, k, n)),
            pl.BlockSpec((1, pairs, deep), lambda m, n, k: (m, 0, k)),
            pl.BlockSpec((1, rank, wide), lambda m, n, k: (m, 0, n)),
        ],
        [
            pl.BlockSpec((1, deep, wide), lambda m, n, k: (m, k, n)),
            pl.BlockSpec((1, 1, wide), lambda m, n, k: (m, 0, n)),
        ],
        [shape(base.shape, LOW), shape((members, 1, width), F32)],
        flops=2 * members * depth * width * 256,
    )


def rms_rows(values):
    return lax.rsqrt(jnp.mean(values * values, axis=1, keepdims=True) + NORM_EPS)


def heads_kernel(
    token_ref,
    gain_ref,
    base_ref,
    left_ref,
    right_ref,
    magnitude_ref,
    cos_ref,
    sine_ref,
    normed_ref,
    low_ref,
    post_ref,
    squares_ref,
):
    total_rows = token_ref.shape[0]
    depth, width = base_ref.shape[1:]

    @pl.when((pl.program_id(0) == 0) & (pl.program_id(1) == 0))
    def _():
        step = 128

        def some(i, carry):
            at = pl.ds(pl.multiple_of(i * step, step), step)
            values = token_ref[at, :].astype(F32)
            normed_ref[at, :] = (values * rms_rows(values) * gain_ref[...]).astype(LOW)
            return carry

        lax.fori_loop(0, total_rows // step, some, 0)

    def put(start, step, tile):
        low_ref[0, start : start + step, :] = tile

    squares = merge_tile(
        lambda start, step: base_ref[0, start : start + step, :],
        put,
        left_ref[0],
        right_ref[0],
        depth,
    )
    squares_ref[0] = squares
    scale = magnitude_ref[0] / jnp.sqrt(squares)
    low = low_ref[0]
    step = 256
    for start in range(0, total_rows, step):
        rows = slice(start, start + step)
        post = dot(normed_ref[rows, :], low) * scale
        cos_table, sine_table = cos_ref[0, rows, :], sine_ref[0, rows, :]
        for head in range(0, width, HEAD_DIM):
            piece = post[:, head : head + HEAD_DIM]
            turned = pltpu.roll(piece, HEAD_DIM // 2, 1)
            post_ref[0, rows, head : head + HEAD_DIM] = (
                piece * cos_table + turned * sine_table
            ).astype(LOW)


def project_heads(tokens, gain, base, left_rows, right, magnitude, cos_tables, sine_tables):
    members, depth, width = base.shape
    rows, pairs, rank = tokens.shape[0], left_rows.shape[1], right.shape[1]
    wide = 256
    whole = lambda m, n: (0, 0)
    return call(
        heads_kernel,
        (tokens, gain, base, left_rows, right, magnitude, cos_tables, sine_tables),
        (members, width // wide),
        [
            pl.BlockSpec((rows, depth), whole),
            pl.BlockSpec((1, depth), whole),
            pl.BlockSpec((1, depth, wide), lambda m, n: (m, 0, n)),
            pl.BlockSpec((1, pairs, depth), lambda m, n: (m, 0, 0)),
            pl.BlockSpec((1, rank, wide), lambda m, n: (m, 0, n)),
            pl.BlockSpec((1, 1, wide), lambda m, n: (m, 0, n)),
            pl.BlockSpec((1, rows, HEAD_DIM), lambda m, n: (m // 2, 0, 0)),
            pl.BlockSpec((1, rows, HEAD_DIM), lambda m, n: (m // 2, 0, 0)),
        ],
        [
            pl.BlockSpec((rows, depth), whole),
            pl.BlockSpec((1, depth, wide), lambda m, n: (m, 0, n)),
            pl.BlockSpec((1, rows, wide), lambda m, n: (m, 0, n)),
            pl.BlockSpec((1, 1, wide), lambda m, n: (m, 0, n)),
        ],
        [
            shape((rows, depth), LOW),
            shape(base.shape, LOW),
            shape((members, rows, width), LOW),
            shape((members, 1, width), F32),
        ],
        flops=2 * members * rows * depth * width,
    )


def key_start(block):
    return max(0, (block * ATTEND_BLOCK - (LONGEST - 1)) // ATTEND_BLOCK * ATTEND_BLOCK)


def masked_probs(queries, key_rows, first, row_at, key_at):
    scores = dot(queries, key_rows, NT) * HEAD_DIM ** (-0.5)
    places = row_at + lax.broadcasted_iota(jnp.int32, scores.shape, 0)
    others = key_at + lax.broadcasted_iota(jnp.int32, scores.shape, 1)
    scores = jnp.where((others >= first) & (others <= places), scores, MASKED)
    exp_scores = jnp.exp(scores - jnp.max(scores, axis=1, keepdims=True))
    return exp_scores / jnp.sum(exp_scores, axis=1, keepdims=True)


def attend_kernel(query_ref, key_ref, value_ref, first_ref, out_ref):
    for block in range(query_ref.shape[1] // ATTEND_BLOCK):
        row_at, key_at = block * ATTEND_BLOCK, key_start(block)
        rows = slice(row_at, row_at + ATTEND_BLOCK)
        keys = slice(key_at, row_at + ATTEND_BLOCK)
        probs = masked_probs(
            query_ref[0, rows, :], key_ref[0, keys, :], first_ref[rows, :], row_at, key_at
        )
        out_ref[rows, :] = dot(probs.astype(LOW), value_ref[0, keys, :]).astype(LOW)


def attend(post, first):
    rows, width = post.shape[1:]
    member = lambda m: pl.BlockSpec((1, rows, HEAD_DIM), lambda h: (m, 0, h))
    return call(
        attend_kernel,
        (post, post, post, first),
        (width // HEAD_DIM,),
        [member(0), member(1), member(2), pl.BlockSpec((rows, 1), lambda h: (0, 0))],
        [pl.BlockSpec((rows, HEAD_DIM), lambda h: (0, h))],
        [shape((rows, width), LOW)],
        flops=4 * rows * rows * width,
    )[0]


def attend_back_kernel(
    order_ref,
    query_ref,
    key_ref,
    value_ref,
    first_ref,
    cos_ref,
    sine_ref,
    magnitude_ref,
    squares_ref,
    *rest,
):
    pieces, (grad_ref, total_ref, heads_grad, key_grad, value_grad) = rest[:-5], rest[-5:]
    rows_all = query_ref.shape[1]
    share = pieces[0].shape[0]
    for place, piece in enumerate(pieces):
        at = pl.multiple_of(order_ref[place] * share, share)
        heads_grad[pl.ds(at, share), :] = piece[...]
    key_grad[...] = jnp.zeros_like(key_grad)
    value_grad[...] = jnp.zeros_like(value_grad)
    norm = [jnp.sqrt(squares_ref[m]) for m in range(3)]
    scale = [magnitude_ref[m] / norm[m] for m in range(3)]
    totals = [jnp.zeros((1, HEAD_DIM), F32) for _ in range(3)]

    def back(values, rows):
        return values * cos_ref[rows, :] - pltpu.roll(values, HEAD_DIM // 2, 1) * sine_ref[rows, :]

    for block in range(rows_all // ATTEND_BLOCK):
        row_at, key_at = block * ATTEND_BLOCK, key_start(block)
        rows = slice(row_at, row_at + ATTEND_BLOCK)
        keys = slice(key_at, row_at + ATTEND_BLOCK)
        queries, key_rows = query_ref[0, rows, :], key_ref[0, keys, :]
        probs = masked_probs(queries, key_rows, first_ref[rows, :], row_at, key_at)
        upper = heads_grad[rows, :]
        grad_weights = dot(upper, value_ref[0, keys, :], NT)
        inner = jnp.sum(probs * grad_weights, axis=1, keepdims=True)
        grad_scores = (probs * (grad_weights - inner)).astype(LOW)
        value_grad[keys, :] += dot(probs.astype(LOW), upper, TN)
        key_grad[keys, :] += dot(grad_scores, queries, TN)
        grad = back(dot(grad_scores, key_rows) * HEAD_DIM ** (-0.5), rows)
        totals[0] += jnp.sum(grad * back(queries.astype(F32), rows), axis=0, keepdims=True)
        grad_ref[0, rows, :] = (grad * scale[0]).astype(LOW)
    for block in range(rows_all // ATTEND_BLOCK):
        rows = slice(block * ATTEND_BLOCK, (block + 1) * ATTEND_BLOCK)
        grad = back(key_grad[rows, :] * HEAD_DIM ** (-0.5), rows)
        totals[1] += jnp.sum(
            grad * back(key_ref[0, rows, :].astype(F32), rows), axis=0, keepdims=True
        )
        grad_ref[1, rows, :] = (grad * scale[1]).astype(LOW)
        grad = value_grad[rows, :]
        totals[2] += jnp.sum(grad * value_ref[0, rows, :].astype(F32), axis=0, keepdims=True)
        grad_ref[2, rows, :] = (grad * scale[2]).astype(LOW)
    for m in range(3):
        total_ref[m] = totals[m] / scale[m]


def attend_back(order, post, first, cos_table, sine_table, magnitude, squares, pieces):
    rows, width = post.shape[1:]
    share = pieces[0].shape[0]
    member = lambda m: pl.BlockSpec((1, rows, HEAD_DIM), lambda h, o: (m, 0, h))
    table = pl.BlockSpec((rows, HEAD_DIM), lambda h, o: (0, 0))
    column = pl.BlockSpec((3, 1, HEAD_DIM), lambda h, o: (0, 0, h))
    return call(
        attend_back_kernel,
        (post, post, post, first, cos_table, sine_table, magnitude, squares, *pieces),
        (width // HEAD_DIM,),
        [
            member(0),
            member(1),
            member(2),
            pl.BlockSpec((rows, 1), lambda h, o: (0, 0)),
            table,
            table,
            column,
            column,
            *[pl.BlockSpec((share, HEAD_DIM), lambda h, o: (0, h)) for _ in pieces],
        ],
        [pl.BlockSpec((3, rows, HEAD_DIM), lambda h, o: (0, 0, h)), column],
        [shape((3, rows, width), LOW), shape((3, 1, width), F32)],
        scratch=[
            pltpu.VMEM((rows, HEAD_DIM), LOW),
            pltpu.VMEM((rows, HEAD_DIM), F32),
            pltpu.VMEM((rows, HEAD_DIM), F32),
        ],
        prefetch=(order,),
        flops=10 * rows * rows * width,
    )


def pair_kernel(dims, order_ref, other_ref, mine_ref, weight_ref, send_ref, keep_ref):
    for source, target in ((other_ref, send_ref), (mine_ref, keep_ref)):
        total = dot(source[0], weight_ref[0], dims)
        for m in range(1, weight_ref.shape[0]):
            total = total + dot(source[m], weight_ref[m], dims)
        target[...] = total.astype(target.dtype)


def pair_product(order, values, weights, dims, step, ordered):
    members, _, share, inner = values.shape
    width = weights.shape[2] if dims is NN else weights.shape[1]
    wide = tile_of(width, 512)
    if ordered:
        at = lambda place: lambda n, o: (0, o[place], 0, 0)
    else:
        at = lambda place: lambda n, o: (0, place, 0, 0)
    block = lambda place: pl.BlockSpec((members, None, share, inner), at(place))
    if dims is NN:
        weight_spec = pl.BlockSpec((members, inner, wide), lambda n, o: (0, 0, n))
    else:
        weight_spec = pl.BlockSpec((members, wide, inner), lambda n, o: (0, n, 0))
    out = pl.BlockSpec((share, wide), lambda n, o: (0, n))
    return call(
        functools.partial(pair_kernel, dims),
        (values, values, weights),
        (width // wide,),
        [block(CORES * step), block(CORES * step + 1), weight_spec],
        [out, out],
        [shape((share, width), LOW), shape((share, width), F32)],
        prefetch=(order,),
        flops=4 * members * share * inner * width,
    )


def row_call(kernel, order, given, whole, out_kinds, sums):
    share, width = given[-1][0].shape
    share = min(v.shape[0] for v, _ in given)
    step = tile_of(share, 64)
    blocks = share // step

    def spec(place):
        if place is None:
            return pl.BlockSpec((step, width), lambda i, o: (i, 0))
        return pl.BlockSpec((step, width), lambda i, o: (o[place] * blocks + i, 0))

    line = pl.BlockSpec((1, width), lambda i, o: (0, 0))
    return call(
        kernel,
        (*[v for v, _ in given], *whole),
        (blocks,),
        [spec(place) for _, place in given] + [line for _ in whole],
        [pl.BlockSpec((step, width), lambda i, o: (i, 0)) for _ in out_kinds]
        + [line for _ in range(sums)],
        [shape((share, width), kind) for kind in out_kinds]
        + [shape((1, width), F32) for _ in range(sums)],
        prefetch=(order,),
        flops=20 * share * width,
        mib=32,
    )


def sum_parts(refs):
    total = refs[0][...].astype(F32)
    for ref in refs[1:]:
        total = total + ref[...].astype(F32)
    return total


def add_column(ref, values):
    part = jnp.sum(values, axis=0, keepdims=True)

    @pl.when(pl.program_id(0) == 0)
    def _():
        ref[...] = part

    @pl.when(pl.program_id(0) > 0)
    def _():
        ref[...] += part


def hidden_kernel(parts, order_ref, *refs):
    token_ref, squares_ref, magnitude_ref, gain_ref, pre_ref, hidden_ref, normed_ref = refs[parts:]
    pre = sum_parts(refs[:parts])
    hidden = token_ref[...].astype(F32) + pre * (magnitude_ref[...] / jnp.sqrt(squares_ref[...]))
    pre_ref[...] = pre
    hidden_ref[...] = hidden
    normed_ref[...] = (hidden * rms_rows(hidden) * gain_ref[...]).astype(LOW)


def mixed_kernel(parts, order_ref, *refs):
    cot_ref, hidden_ref, squares_ref, magnitude_ref, mixed_ref, total_ref = refs[parts:]
    pre = sum_parts(refs[:parts])
    scale = magnitude_ref[...] / jnp.sqrt(squares_ref[...])
    mixed_ref[...] = (hidden_ref[...] + pre * scale).astype(LOW)
    add_column(total_ref, cot_ref[...].astype(F32) * pre)


def norm_back(grad_normed, values, gain):
    factor = rms_rows(values)
    scaled = grad_normed * gain
    inner = jnp.mean(scaled * values, axis=1, keepdims=True)
    back = factor * scaled - values * (factor * factor * factor * inner)
    return back, grad_normed * values * factor


def hidden_back_kernel(parts, order_ref, *refs):
    (
        cot_ref,
        hidden_ref,
        pre_ref,
        squares_ref,
        magnitude_ref,
        gain_ref,
        grad_ref,
        low_ref,
        total_ref,
        gain_grad_ref,
    ) = refs[parts:]
    back, gain_terms = norm_back(sum_parts(refs[:parts]), hidden_ref[...], gain_ref[...])
    grad = cot_ref[...].astype(F32) + back
    grad_ref[...] = grad
    scale = magnitude_ref[...] / jnp.sqrt(squares_ref[...])
    low_ref[...] = (grad * scale).astype(LOW)
    add_column(total_ref, grad * pre_ref[...])
    add_column(gain_grad_ref, gain_terms)


def token_back_kernel(parts, order_ref, *refs):
    token_ref, grad_ref, gain_ref, out_ref, gain_grad_ref = refs[parts:]
    back, gain_terms = norm_back(
        sum_parts(refs[:parts]), token_ref[...].astype(F32), gain_ref[...]
    )
    out_ref[...] = grad_ref[...] + back
    add_column(gain_grad_ref, gain_terms)


def shrink_back_kernel(order_ref, cot_ref, low_ref, squares_ref, magnitude_ref, product_ref, grad_ref):
    scale = magnitude_ref[0] / jnp.sqrt(squares_ref[0])
    grad = (cot_ref[...].astype(F32) * scale).astype(LOW)
    grad_ref[0] = grad
    product_ref[0] = dot(grad, low_ref[0], NT)


def shrink_back(order, cotangent, low, squares, magnitude, groups):
    rows, width = cotangent.shape
    share, inner = rows // groups, low.shape[1]
    line = pl.BlockSpec((1, 1, width), lambda j, o: (0, 0, 0))
    return call(
        shrink_back_kernel,
        (cotangent, low, squares, magnitude),
        (groups,),
        [
            pl.BlockSpec((share, width), lambda j, o: (o[j], 0)),
            pl.BlockSpec((1, inner, width), lambda j, o: (0, 0, 0)),
            line,
            line,
        ],
        [
            pl.BlockSpec((1, share, inner), lambda j, o: (j, 0, 0)),
            pl.BlockSpec((1, share, width), lambda j, o: (j, 0, 0)),
        ],
        [shape((groups, share, inner), F32), shape((groups, share, width), LOW)],
        prefetch=(order,),
        flops=2 * rows * width * inner,
    )


def expand_kernel(
    other_ref, mine_ref, low_ref, squares_ref, magnitude_ref, grad_ref, product_ref, back_ref, total_ref
):
    scale = [magnitude_ref[m] / jnp.sqrt(squares_ref[m]) for m in range(2)]
    width = low_ref.shape[2]
    totals = [jnp.zeros((1, width), F32) for _ in range(2)]
    if width % 128 == 0:
        weights = jnp.concatenate([low_ref[0], low_ref[1]], axis=1)
    for place, source in enumerate((other_ref, mine_ref)):
        if width % 128 == 0:
            pre = dot(source[...], weights)
            gate_pre, up_pre = pre[:, :width], pre[:, width:]
        else:
            gate_pre, up_pre = (dot(source[...], low_ref[m]) for m in range(2))
        gate, up = gate_pre * scale[0], up_pre * scale[1]
        sigmoid = jax.nn.sigmoid(gate)
        active = gate * sigmoid
        product_ref[0, place] = (active * up).astype(LOW)
        upper = grad_ref[place]
        grad_up = upper * active
        grad_gate = upper * up * sigmoid * (1.0 + gate * (1.0 - sigmoid))
        totals[0] += jnp.sum(grad_gate * gate_pre, axis=0, keepdims=True)
        totals[1] += jnp.sum(grad_up * up_pre, axis=0, keepdims=True)
        back_ref[0, place] = (grad_gate * scale[0]).astype(LOW)
        back_ref[1, place] = (grad_up * scale[1]).astype(LOW)
    for m in range(2):
        total_ref[m] = totals[m]


def expand(pieces, low, squares, magnitude, grad_product, step):
    share, depth = pieces[0].shape
    width = low.shape[2]
    wide = tile_of(width, 128)
    piece = pl.BlockSpec((share, depth), lambda n: (0, 0))
    column = pl.BlockSpec((2, 1, wide), lambda n: (0, 0, n))
    return call(
        expand_kernel,
        (*pieces, low, squares, magnitude, grad_product),
        (width // wide,),
        [
            piece,
            piece,
            pl.BlockSpec((2, depth, wide), lambda n: (0, 0, n)),
            column,
            column,
            pl.BlockSpec((2, share, wide), lambda n: (step, 0, n)),
        ],
        [
            pl.BlockSpec((1, 2, share, wide), lambda n: (0, 0, 0, n)),
            pl.BlockSpec((2, 2, share, wide), lambda n: (0, 0, 0, n)),
            column,
        ],
        [
            shape((1, 2, share, width), LOW),
            shape((2, 2, share, width), LOW),
            shape((2, 1, width), F32),
        ],
        flops=8 * share * depth * width,
    )


def heads_back_kernel(grad_ref, low_ref, out_ref):
    out_ref[...] = dot(grad_ref[...], low_ref[0], NT).astype(LOW)


def heads_back(grad, low):
    rows, width = grad.shape
    inner = low.shape[1]
    return call(
        heads_back_kernel,
        (grad, low),
        (1,),
        [
            pl.BlockSpec((rows, width), lambda i: (0, 0)),
            pl.BlockSpec((1, inner, width), lambda i: (0, 0, 0)),
        ],
        [pl.BlockSpec((rows, inner), lambda i: (0, 0))],
        [shape((rows, inner), LOW)],
        flops=2 * rows * width * inner,
    )[0]


def adapter_kernel(n_inputs, n_grads, order_ref, *refs):
    inputs, grads = refs[:n_inputs], refs[n_inputs : n_inputs + n_grads]
    (
        low_ref,
        left_ref,
        right_ref,
        total_ref,
        squares_ref,
        magnitude_ref,
        left_out,
        right_out,
        magnitude_out,
    ) = refs[n_inputs + n_grads :]
    left_rows = left_ref[0]
    right = right_ref[0]
    right_rows = split_rows(right)
    norm = jnp.sqrt(squares_ref[0])
    total = total_ref[0]
    weight = total * magnitude_ref[0] / (norm * norm * norm)
    low = low_ref[0]
    left_sum = -fold(dot(split_rows(right * weight), low, NT))
    right_sum = -(fold(dot(left_rows, low)) * weight)

    def flat(refs, lead):
        for ref in refs:
            view = ref[...].reshape((-1,) + ref.shape[-1:])
            yield view

    rows_in = [view for view in flat(inputs, 0)]
    rows_grad = [view for view in flat(grads, 0)]
    step = min(v.shape[0] for v in rows_in + rows_grad)

    def cut(views):
        return [v[at : at + step] for v in views for at in range(0, v.shape[0], step)]

    for taken, grad in zip(cut(rows_in), cut(rows_grad)):
        down = split_rows(fold(dot(right_rows, grad, NT)))
        left_sum = left_sum + fold(dot(down, taken))
        across = split_rows(fold(dot(left_rows, taken, NT)))
        right_sum = right_sum + fold(dot(across, grad))
    left_out[0] = ADAPT_SCALE * left_sum
    right_out[0] = ADAPT_SCALE * right_sum
    magnitude_out[0] = total / norm


def adapter(order, inputs, grads, low, left_rows, right, total, squares, magnitude):
    members, depth, width = low.shape
    pairs, rank = left_rows.shape[1], right.shape[1]
    column = pl.BlockSpec((1, 1, width), lambda m, o: (m, 0, 0))
    rows = sum(v.size // v.shape[-1] for v, _, _ in inputs)
    return call(
        functools.partial(adapter_kernel, len(inputs), len(grads)),
        (
            *[v for v, _, _ in inputs],
            *[v for v, _, _ in grads],
            low,
            left_rows,
            right,
            total,
            squares,
            magnitude,
        ),
        (members,),
        [pl.BlockSpec(block, at) for _, block, at in (*inputs, *grads)]
        + [
            pl.BlockSpec((1, depth, width), lambda m, o: (m, 0, 0)),
            pl.BlockSpec((1, pairs, depth), lambda m, o: (m, 0, 0)),
            pl.BlockSpec((1, rank, width), lambda m, o: (m, 0, 0)),
            column,
            column,
            column,
        ],
        [
            pl.BlockSpec((1, rank, depth), lambda m, o: (m, 0, 0)),
            pl.BlockSpec((1, rank, width), lambda m, o: (m, 0, 0)),
            column,
        ],
        [
            shape((members, rank, depth), F32),
            shape((members, rank, width), F32),
            shape((members, 1, width), F32),
        ],
        prefetch=(order,),
        flops=8 * members * (rows + depth) * width * 32,
        mib=56,
    )


def geometry(segment):
    length = segment.shape[0]
    places = lax.broadcasted_iota(jnp.int32, (length, length), 0)
    others = lax.broadcasted_iota(jnp.int32, (length, length), 1)
    visible = (segment[:, None] == segment[None, :]) & (others <= places)
    offset = jnp.sum(visible.astype(F32), axis=1) - 1.0
    half_dim = HEAD_DIM // 2
    frequency = jnp.exp(
        -jnp.log(ROPE_BASE) * 2.0 * jnp.arange(half_dim, dtype=F32) / HEAD_DIM
    )
    angles = offset[:, None] * frequency[None, :]
    cosine, sine = jnp.cos(angles), jnp.sin(angles)
    first = jnp.arange(length, dtype=jnp.int32) - offset.astype(jnp.int32)
    return (
        first[:, None],
        jnp.concatenate([cosine, cosine], axis=1),
        jnp.concatenate([-sine, sine], axis=1),
    )


def body(
    tokens,
    cotangent,
    segment_ids,
    attend_gain,
    expand_gain,
    heads_base,
    heads_left,
    heads_right,
    heads_magnitude,
    output_base,
    output_left,
    output_right,
    output_magnitude,
    expand_base,
    expand_left,
    expand_right,
    expand_magnitude,
    shrink_base,
    shrink_left,
    shrink_right,
    shrink_magnitude,
):
    groups = lax.axis_size("mp")
    chips = groups // CORES
    index = lax.axis_index("mp")
    chip, core = index // CORES, index % CORES
    rows, width = tokens.shape
    share = rows // groups
    local_heads = heads_base.shape[2]
    order = jnp.stack(
        [
            (chip + step) % chips * CORES + (core + 1 + place) % CORES
            for step in range(chips)
            for place in range(CORES)
        ]
    ).astype(jnp.int32)

    def sibling(values):
        return lax.ppermute(
            values, "mp", [(i, i // CORES * CORES + (i + 1) % CORES) for i in range(groups)]
        )

    def to_chip(values, step):
        return lax.ppermute(
            values,
            "mp",
            [((i, ((i // CORES + step) % chips) * CORES + i % CORES)) for i in range(groups)],
        )

    def mp_sum(values):
        values = values + sibling(values)
        total = values
        for step in range(1, chips):
            total = total + to_chip(values, step)
        return total

    def reduce_scatter(product):
        parts = []
        for step in range(1, chips):
            send, keep = product(step)
            joined = (keep + sibling(send).astype(F32)).astype(LOW)
            parts.append(to_chip(joined, step))
        send, keep = product(0)
        return [keep, sibling(send), *parts]

    def gather(own):
        pieces = [(sibling(own), own)]
        for step in range(1, chips):
            arrived = to_chip(own, chips - step)
            pieces.append((sibling(arrived), arrived))
        return pieces

    heads_rows, output_rows = left_pairs(heads_left), left_pairs(output_left[None])
    expand_rows, shrink_rows = left_pairs(expand_left), left_pairs(shrink_left[None])
    heads_mag, output_mag = heads_magnitude[:, None], output_magnitude[None, None]
    expand_mag, shrink_mag = expand_magnitude[:, None], shrink_magnitude[None, None]
    attend_line, expand_line = attend_gain[None], expand_gain[None]

    output_low, output_part = merge(
        output_base[None], output_rows, output_right[None], output_base.shape[0], 512
    )
    shrink_low, shrink_part = merge(
        shrink_base[None], shrink_rows, shrink_right[None], shrink_base.shape[0], 512
    )
    squares = mp_sum(jnp.concatenate([output_part, shrink_part], axis=1))
    output_sq, shrink_sq = squares[:, :1], squares[:, 1:]

    first, cos_table, sine_table = geometry(segment_ids.reshape(-1))
    normed, heads_low, post, heads_sq = project_heads(
        tokens,
        attend_line,
        heads_base,
        heads_rows,
        heads_right,
        heads_mag,
        jnp.stack([cos_table, jnp.ones_like(cos_table)]),
        jnp.stack([sine_table, jnp.zeros_like(sine_table)]),
    )
    heads_out = attend(post, first)
    heads_parts = heads_out.reshape(1, groups, share, local_heads)
    output_parts = reduce_scatter(
        lambda step: pair_product(order, heads_parts, output_low, NN, step, True)
    )
    expand_low, expand_sq = merge(expand_base, expand_rows, expand_right, 512, expand_base.shape[2])
    grad_product, shrink_grad = shrink_back(
        order, cotangent, shrink_low, shrink_sq, shrink_mag, groups
    )
    output_pre, hidden, normed_own = row_call(
        functools.partial(hidden_kernel, len(output_parts)),
        order,
        [(part, None) for part in output_parts] + [(tokens, 1)],
        (output_sq[0], output_mag[0], expand_line),
        (F32, F32, LOW),
        0,
    )
    normed_mid = gather(normed_own)
    forward = [
        expand(normed_mid[step], expand_low, expand_sq, expand_mag, grad_product, step)
        for step in range(chips)
    ]
    products, expand_grads = [f[0] for f in forward], [f[1] for f in forward]
    expand_total = functools.reduce(jnp.add, [f[2] for f in forward])
    mid_parts = reduce_scatter(
        lambda step: pair_product(order, expand_grads[step], expand_low, NT, 0, False)
    )
    shrink_parts = reduce_scatter(
        lambda step: pair_product(order, products[step], shrink_low, NN, 0, False)
    )
    grad_hidden, output_grad_own, output_total, expand_gain_part = row_call(
        functools.partial(hidden_back_kernel, len(mid_parts)),
        order,
        [(part, None) for part in mid_parts] + [(cotangent, 1), (hidden, None), (output_pre, None)],
        (output_sq[0], output_mag[0], expand_line),
        (F32, LOW),
        2,
    )
    mixed, shrink_total = row_call(
        functools.partial(mixed_kernel, len(shrink_parts)),
        order,
        [(part, None) for part in shrink_parts] + [(cotangent, 1), (hidden, None)],
        (shrink_sq[0], shrink_mag[0]),
        (LOW,),
        1,
    )
    output_grad = [piece for pair in gather(output_grad_own) for piece in pair]
    heads_grads, heads_total = attend_back(
        order,
        post,
        first,
        cos_table,
        sine_table,
        heads_mag,
        heads_sq,
        [heads_back(piece, output_low) for piece in output_grad],
    )
    grad_parts = heads_grads.reshape(3, groups, share, local_heads)
    token_parts = reduce_scatter(
        lambda step: pair_product(order, grad_parts, heads_low, NT, step, True)
    )
    grad_tokens, attend_gain_part = row_call(
        functools.partial(token_back_kernel, len(token_parts)),
        order,
        [(part, None) for part in token_parts] + [(tokens, 1), (grad_hidden, None)],
        (attend_line,),
        (F32,),
        1,
    )

    totals = mp_sum(jnp.concatenate([output_total, shrink_total], axis=0))

    def whole(values, lead):
        return (values, (None,) * lead + values.shape[lead:], lambda m, o: (0,) * values.ndim)

    def of_member(values):
        return (
            values,
            (None,) + values.shape[1:],
            lambda m, o: (m,) + (0,) * (values.ndim - 1),
        )

    expand_left_part, expand_right_part, expand_mag_part = adapter(
        order,
        [whole(piece, 0) for pair in normed_mid for piece in pair],
        [of_member(grad) for grad in expand_grads],
        expand_low,
        expand_rows,
        expand_right,
        expand_total,
        expand_sq,
        expand_mag,
    )
    shrink_left_part, shrink_right_part, shrink_mag_part = adapter(
        order,
        [whole(product, 1) for product in products],
        [whole(shrink_grad, 0)],
        shrink_low,
        shrink_rows,
        shrink_right[None],
        totals[1:, None],
        shrink_sq,
        shrink_mag,
    )
    output_left_part, output_right_part, output_mag_part = adapter(
        order,
        [
            (
                heads_parts,
                (None, None, share, local_heads),
                functools.partial(lambda place, m, o: (0, o[place], 0, 0), place),
            )
            for place in range(groups)
        ],
        [whole(piece, 0) for piece in output_grad],
        output_low,
        output_rows,
        output_right[None],
        totals[:1, None],
        output_sq,
        output_mag,
    )
    heads_left_part, heads_right_part, heads_mag_part = adapter(
        order,
        [whole(normed, 0)],
        [of_member(heads_grads)],
        heads_low,
        heads_rows,
        heads_right,
        heads_total,
        heads_sq,
        heads_mag,
    )

    rank = heads_right.shape[1]
    early = lax.psum(
        jnp.concatenate(
            [
                expand_left_part.reshape(2 * rank, width),
                output_right_part[0],
                shrink_right_part[0],
                expand_gain_part,
            ],
            axis=0,
        ),
        ("dp", "mp"),
    )
    late = lax.psum(
        jnp.concatenate([heads_left_part.reshape(3 * rank, width), attend_gain_part], axis=0),
        ("dp", "mp"),
    )
    (expand_right_grad, output_left_grad, shrink_left_grad, expand_mag_grad, output_mag_grad, shrink_mag_grad) = (
        lax.psum(
            (
                expand_right_part,
                output_left_part,
                shrink_left_part,
                expand_mag_part,
                output_mag_part,
                shrink_mag_part,
            ),
            "dp",
        )
    )
    heads_right_grad, heads_mag_grad = lax.psum((heads_right_part, heads_mag_part), "dp")
    return (
        mixed,
        grad_tokens,
        late[3 * rank],
        early[4 * rank],
        jnp.swapaxes(late[: 3 * rank].reshape(3, rank, width), 1, 2),
        heads_right_grad,
        heads_mag_grad[:, 0],
        output_left_grad[0].T,
        early[2 * rank : 3 * rank],
        output_mag_grad[0, 0],
        jnp.swapaxes(early[: 2 * rank].reshape(2, rank, width), 1, 2),
        expand_right_grad,
        expand_mag_grad[:, 0],
        shrink_left_grad[0].T,
        early[3 * rank : 4 * rank],
        shrink_mag_grad[0, 0],
    )


def solution(mesh):
    placed = (
        P("dp", None),
        P("dp", None),
        P("dp", None),
        P(),
        P(),
        P(None, None, "mp"),
        P(),
        P(None, None, "mp"),
        P(None, "mp"),
        P("mp", None),
        P("mp", None),
        P(),
        P(),
        P(None, None, "mp"),
        P(),
        P(None, None, "mp"),
        P(None, "mp"),
        P("mp", None),
        P("mp", None),
        P(),
        P(),
    )
    return jax.shard_map(
        body,
        mesh=mesh,
        in_specs=placed,
        out_specs=(
            P(("dp", "mp"), None),
            P(("dp", "mp"), None),
            P(),
            P(),
            P(),
            P(None, None, "mp"),
            P(None, "mp"),
            P("mp", None),
            P(),
            P(),
            P(),
            P(None, None, "mp"),
            P(None, "mp"),
            P("mp", None),
            P(),
            P(),
        ),
        check_vma=False,
    )
```

```python
import functools

import jax
import jax.numpy as jnp
from jax import lax
from jax.experimental import pallas as pl
from jax.experimental.pallas import tpu as pltpu
from jax.sharding import PartitionSpec as P

HEAD_DIM = 128
CORES = 2
LONGEST = 512
ATTEND_BLOCK = 256
ADAPT_SCALE = 2.0
NORM_EPS = 1e-05
ROPE_BASE = 10000.0
MASKED = -1e30

F32 = jnp.float32
LOW = jnp.bfloat16
NN = (((1,), (0,)), ((), ()))
NT = (((1,), (1,)), ((), ()))
TN = (((0,), (0,)), ((), ()))


def dot(left, right, dims=NN):
    return lax.dot_general(left, right, dims, preferred_element_type=F32)


def shape(dims, kind):
    return jax.ShapeDtypeStruct(tuple(dims), kind)


def call(name, kernel, operands, grid, in_specs, out_specs, out_shape, scratch=(), prefetch=(), flops=0, mib=60):
    moved = sum(v.size * v.dtype.itemsize for v in operands)
    moved += sum(v.size * v.dtype.itemsize for v in out_shape)
    return pl.pallas_call(
        kernel,
        name=name,
        out_shape=out_shape,
        grid_spec=pltpu.PrefetchScalarGridSpec(
            num_scalar_prefetch=len(prefetch),
            grid=grid,
            in_specs=in_specs,
            out_specs=out_specs,
            scratch_shapes=scratch,
        ),
        compiler_params=pltpu.CompilerParams(vmem_limit_bytes=mib * 2**20),
        cost_estimate=pl.CostEstimate(flops=flops, bytes_accessed=moved, transcendentals=0),
    )(*prefetch, *operands)


def tile_of(size, most):
    return most if size % most == 0 else size


def split_rows(values):
    top = values.astype(LOW)
    rest = (values - top.astype(F32)).astype(LOW)
    return jnp.concatenate([top, rest], axis=0)


def left_pairs(left_map):
    turned = jnp.swapaxes(left_map, -1, -2)
    top = lax.reduce_precision(turned, 8, 7)
    return jnp.concatenate([top, turned - top], axis=-2).astype(LOW)


def left_stack(left_map):
    top = lax.reduce_precision(left_map, 8, 7)
    return jnp.concatenate([top, top, left_map - top], axis=-1).astype(LOW)


def fold(values):
    half = values.shape[0] // 2
    return values[:half] + values[half:]


def merge_tile(base_at, low_put, left_at, right, depth):
    doubled = ADAPT_SCALE * right
    top = doubled.astype(LOW)
    rest = (doubled - top.astype(F32)).astype(LOW)
    right_stack = jnp.concatenate([top, rest, top], axis=0)
    squares = jnp.zeros((1, right.shape[1]), F32)
    step = 128 if depth % 128 == 0 else depth
    for start in range(0, depth, step):
        merged = base_at(start, step).astype(F32) + dot(left_at(start, step), right_stack)
        low_put(start, step, merged.astype(LOW))
        squares = squares + jnp.sum(merged * merged, axis=0, keepdims=True)
    return squares


def merge_kernel(base_ref, left_ref, right_ref, low_ref, squares_ref):
    depth = base_ref.shape[1]

    def put(start, step, tile):
        low_ref[0, start : start + step, :] = tile

    squares = merge_tile(
        lambda start, step: base_ref[0, start : start + step, :],
        put,
        lambda start, step: left_ref[0, start : start + step, :],
        right_ref[0],
        depth,
    )

    @pl.when(pl.program_id(2) == 0)
    def _():
        squares_ref[0] = squares

    @pl.when(pl.program_id(2) > 0)
    def _():
        squares_ref[0] += squares


def merge(base, left_map, right, deep, wide):
    members, depth, width = base.shape
    stack = left_stack(left_map)
    rank = right.shape[1]
    return call(
        "merge",
        merge_kernel,
        (base, stack, right),
        (members, width // wide, depth // deep),
        [
            pl.BlockSpec((1, deep, wide), lambda m, n, k: (m, k, n)),
            pl.BlockSpec((1, deep, stack.shape[2]), lambda m, n, k: (m, k, 0)),
            pl.BlockSpec((1, rank, wide), lambda m, n, k: (m, 0, n)),
        ],
        [
            pl.BlockSpec((1, deep, wide), lambda m, n, k: (m, k, n)),
            pl.BlockSpec((1, 1, wide), lambda m, n, k: (m, 0, n)),
        ],
        [shape(base.shape, LOW), shape((members, 1, width), F32)],
        flops=2 * members * depth * width * 256,
    )


def rms_rows(values):
    return lax.rsqrt(jnp.mean(values * values, axis=1, keepdims=True) + NORM_EPS)


def heads_kernel(
    token_ref,
    gain_ref,
    base_ref,
    left_ref,
    right_ref,
    magnitude_ref,
    cos_ref,
    sine_ref,
    normed_ref,
    low_ref,
    post_ref,
    squares_ref,
):
    total_rows = token_ref.shape[0]
    depth, width = base_ref.shape[1:]

    @pl.when((pl.program_id(0) == 0) & (pl.program_id(1) == 0))
    def _():
        step = 128

        def some(i, carry):
            at = pl.ds(pl.multiple_of(i * step, step), step)
            values = token_ref[at, :].astype(F32)
            normed_ref[at, :] = (values * rms_rows(values) * gain_ref[...]).astype(LOW)
            return carry

        lax.fori_loop(0, total_rows // step, some, 0)

    def put(start, step, tile):
        low_ref[0, start : start + step, :] = tile

    squares = merge_tile(
        lambda start, step: base_ref[0, start : start + step, :],
        put,
        lambda start, step: left_ref[0, start : start + step, :],
        right_ref[0],
        depth,
    )
    squares_ref[0] = squares
    scale = magnitude_ref[0] / jnp.sqrt(squares)
    low = low_ref[0]
    step = 256
    for start in range(0, total_rows, step):
        rows = slice(start, start + step)
        post = dot(normed_ref[rows, :], low) * scale
        cos_table, sine_table = cos_ref[0, rows, :], sine_ref[0, rows, :]
        for head in range(0, width, HEAD_DIM):
            piece = post[:, head : head + HEAD_DIM]
            turned = pltpu.roll(piece, HEAD_DIM // 2, 1)
            post_ref[0, rows, head : head + HEAD_DIM] = (
                piece * cos_table + turned * sine_table
            ).astype(LOW)


def project_heads(tokens, gain, base, left_map, right, magnitude, cos_tables, sine_tables):
    members, depth, width = base.shape
    stack = left_stack(left_map)
    rows, rank = tokens.shape[0], right.shape[1]
    wide = 256
    whole = lambda m, n: (0, 0)
    return call(
        "project_heads",
        heads_kernel,
        (tokens, gain, base, stack, right, magnitude, cos_tables, sine_tables),
        (members, width // wide),
        [
            pl.BlockSpec((rows, depth), whole),
            pl.BlockSpec((1, depth), whole),
            pl.BlockSpec((1, depth, wide), lambda m, n: (m, 0, n)),
            pl.BlockSpec((1, depth, stack.shape[2]), lambda m, n: (m, 0, 0)),
            pl.BlockSpec((1, rank, wide), lambda m, n: (m, 0, n)),
            pl.BlockSpec((1, 1, wide), lambda m, n: (m, 0, n)),
            pl.BlockSpec((1, rows, HEAD_DIM), lambda m, n: (m // 2, 0, 0)),
            pl.BlockSpec((1, rows, HEAD_DIM), lambda m, n: (m // 2, 0, 0)),
        ],
        [
            pl.BlockSpec((rows, depth), whole),
            pl.BlockSpec((1, depth, wide), lambda m, n: (m, 0, n)),
            pl.BlockSpec((1, rows, wide), lambda m, n: (m, 0, n)),
            pl.BlockSpec((1, 1, wide), lambda m, n: (m, 0, n)),
        ],
        [
            shape((rows, depth), LOW),
            shape(base.shape, LOW),
            shape((members, rows, width), LOW),
            shape((members, 1, width), F32),
        ],
        flops=2 * members * rows * depth * width,
    )


def key_start(block):
    return max(0, (block * ATTEND_BLOCK - (LONGEST - 1)) // ATTEND_BLOCK * ATTEND_BLOCK)


def masked_probs(queries, key_rows, first, row_at, key_at):
    scores = dot(queries, key_rows, NT) * HEAD_DIM ** (-0.5)
    places = row_at + lax.broadcasted_iota(jnp.int32, scores.shape, 0)
    others = key_at + lax.broadcasted_iota(jnp.int32, scores.shape, 1)
    scores = jnp.where((others >= first) & (others <= places), scores, MASKED)
    exp_scores = jnp.exp(scores - jnp.max(scores, axis=1, keepdims=True))
    return exp_scores * (1.0 / jnp.sum(exp_scores, axis=1, keepdims=True))


def attend_kernel(query_ref, key_ref, value_ref, first_ref, out_ref):
    for block in range(query_ref.shape[1] // ATTEND_BLOCK):
        row_at, key_at = block * ATTEND_BLOCK, key_start(block)
        rows = slice(row_at, row_at + ATTEND_BLOCK)
        keys = slice(key_at, row_at + ATTEND_BLOCK)
        probs = masked_probs(
            query_ref[0, rows, :], key_ref[0, keys, :], first_ref[rows, :], row_at, key_at
        )
        out_ref[rows, :] = dot(probs.astype(LOW), value_ref[0, keys, :]).astype(LOW)


def attend(post, first):
    rows, width = post.shape[1:]
    member = lambda m: pl.BlockSpec((1, rows, HEAD_DIM), lambda h: (m, 0, h))
    return call(
        "attend",
        attend_kernel,
        (post, post, post, first),
        (width // HEAD_DIM,),
        [member(0), member(1), member(2), pl.BlockSpec((rows, 1), lambda h: (0, 0))],
        [pl.BlockSpec((rows, HEAD_DIM), lambda h: (0, h))],
        [shape((rows, width), LOW)],
        flops=4 * rows * rows * width,
    )[0]


def attend_back_kernel(
    order_ref,
    query_ref,
    key_ref,
    value_ref,
    first_ref,
    cos_ref,
    sine_ref,
    magnitude_ref,
    squares_ref,
    *rest,
):
    pieces, (grad_ref, total_ref, heads_grad, key_grad, value_grad) = rest[:-5], rest[-5:]
    rows_all = query_ref.shape[1]
    share = pieces[0].shape[0]
    for place, piece in enumerate(pieces):
        at = pl.multiple_of(order_ref[place] * share, share)
        heads_grad[pl.ds(at, share), :] = piece[...]
    key_grad[...] = jnp.zeros_like(key_grad)
    value_grad[...] = jnp.zeros_like(value_grad)
    norm = [jnp.sqrt(squares_ref[m]) for m in range(3)]
    scale = [magnitude_ref[m] / norm[m] for m in range(3)]
    totals = [jnp.zeros((1, HEAD_DIM), F32) for _ in range(3)]

    def back(values, rows):
        return values * cos_ref[rows, :] - pltpu.roll(values, HEAD_DIM // 2, 1) * sine_ref[rows, :]

    for block in range(rows_all // ATTEND_BLOCK):
        row_at, key_at = block * ATTEND_BLOCK, key_start(block)
        rows = slice(row_at, row_at + ATTEND_BLOCK)
        keys = slice(key_at, row_at + ATTEND_BLOCK)
        queries, key_rows = query_ref[0, rows, :], key_ref[0, keys, :]
        probs = masked_probs(queries, key_rows, first_ref[rows, :], row_at, key_at)
        upper = heads_grad[rows, :]
        grad_weights = dot(upper, value_ref[0, keys, :], NT)
        inner = jnp.sum(probs * grad_weights, axis=1, keepdims=True)
        grad_scores = (probs * (grad_weights - inner)).astype(LOW)
        value_grad[keys, :] += dot(probs.astype(LOW), upper, TN)
        key_grad[keys, :] += dot(grad_scores, queries, TN)
        grad = back(dot(grad_scores, key_rows) * HEAD_DIM ** (-0.5), rows)
        totals[0] += jnp.sum(grad * back(queries.astype(F32), rows), axis=0, keepdims=True)
        grad_ref[0, rows, :] = (grad * scale[0]).astype(LOW)
    for block in range(rows_all // ATTEND_BLOCK):
        rows = slice(block * ATTEND_BLOCK, (block + 1) * ATTEND_BLOCK)
        grad = back(key_grad[rows, :] * HEAD_DIM ** (-0.5), rows)
        totals[1] += jnp.sum(
            grad * back(key_ref[0, rows, :].astype(F32), rows), axis=0, keepdims=True
        )
        grad_ref[1, rows, :] = (grad * scale[1]).astype(LOW)
        grad = value_grad[rows, :]
        totals[2] += jnp.sum(grad * value_ref[0, rows, :].astype(F32), axis=0, keepdims=True)
        grad_ref[2, rows, :] = (grad * scale[2]).astype(LOW)
    for m in range(3):
        total_ref[m] = totals[m] / scale[m]


def attend_back(order, post, first, cos_table, sine_table, magnitude, squares, pieces):
    rows, width = post.shape[1:]
    share = pieces[0].shape[0]
    member = lambda m: pl.BlockSpec((1, rows, HEAD_DIM), lambda h, o: (m, 0, h))
    table = pl.BlockSpec((rows, HEAD_DIM), lambda h, o: (0, 0))
    column = pl.BlockSpec((3, 1, HEAD_DIM), lambda h, o: (0, 0, h))
    return call(
        "attend_back",
        attend_back_kernel,
        (post, post, post, first, cos_table, sine_table, magnitude, squares, *pieces),
        (width // HEAD_DIM,),
        [
            member(0),
            member(1),
            member(2),
            pl.BlockSpec((rows, 1), lambda h, o: (0, 0)),
            table,
            table,
            column,
            column,
            *[pl.BlockSpec((share, HEAD_DIM), lambda h, o: (0, h)) for _ in pieces],
        ],
        [pl.BlockSpec((3, rows, HEAD_DIM), lambda h, o: (0, 0, h)), column],
        [shape((3, rows, width), LOW), shape((3, 1, width), F32)],
        scratch=[
            pltpu.VMEM((rows, HEAD_DIM), LOW),
            pltpu.VMEM((rows, HEAD_DIM), F32),
            pltpu.VMEM((rows, HEAD_DIM), F32),
        ],
        prefetch=(order,),
        flops=10 * rows * rows * width,
    )


def pair_kernel(dims, order_ref, other_ref, mine_ref, weight_ref, send_ref, keep_ref):
    for source, target in ((other_ref, send_ref), (mine_ref, keep_ref)):
        total = dot(source[0], weight_ref[0], dims)
        for m in range(1, weight_ref.shape[0]):
            total = total + dot(source[m], weight_ref[m], dims)
        target[...] = total.astype(target.dtype)


def pair_product(order, values, weights, dims, step, ordered):
    members, _, share, inner = values.shape
    width = weights.shape[2] if dims is NN else weights.shape[1]
    wide = tile_of(width, 512)
    if ordered:
        at = lambda place: lambda n, o: (0, o[place], 0, 0)
    else:
        at = lambda place: lambda n, o: (0, place, 0, 0)
    block = lambda place: pl.BlockSpec((members, None, share, inner), at(place))
    if dims is NN:
        weight_spec = pl.BlockSpec((members, inner, wide), lambda n, o: (0, 0, n))
    else:
        weight_spec = pl.BlockSpec((members, wide, inner), lambda n, o: (0, n, 0))
    out = pl.BlockSpec((share, wide), lambda n, o: (0, n))
    return call(
        "pair_product",
        functools.partial(pair_kernel, dims),
        (values, values, weights),
        (width // wide,),
        [block(CORES * step), block(CORES * step + 1), weight_spec],
        [out, out],
        [shape((share, width), LOW), shape((share, width), F32)],
        prefetch=(order,),
        flops=4 * members * share * inner * width,
    )


def shrink_kernel(order_ref, value_ref, weight_ref, other_ref, mine_ref, send_ref, keep_ref, total_ref):
    total = jnp.zeros((1, weight_ref.shape[2]), F32)
    for place, (cot_ref, target) in enumerate(((other_ref, send_ref), (mine_ref, keep_ref))):
        pre = dot(value_ref[0, place], weight_ref[0])
        target[...] = pre.astype(target.dtype)
        total = total + jnp.sum(pre * cot_ref[...].astype(F32), axis=0, keepdims=True)
    total_ref[...] = total


def shrink_product(order, values, weights, cotangent, step):
    _, _, share, inner = values.shape
    width = weights.shape[2]
    wide = tile_of(width, 512)
    out = pl.BlockSpec((share, wide), lambda n, o: (0, n))
    cot = lambda place: pl.BlockSpec((share, wide), lambda n, o: (o[place], n))
    return call(
        "shrink_product",
        shrink_kernel,
        (values, weights, cotangent, cotangent),
        (width // wide,),
        [
            pl.BlockSpec((1, CORES, share, inner), lambda n, o: (0, 0, 0, 0)),
            pl.BlockSpec((1, inner, wide), lambda n, o: (0, 0, n)),
            cot(CORES * step),
            cot(CORES * step + 1),
        ],
        [out, out, pl.BlockSpec((1, wide), lambda n, o: (0, n))],
        [shape((share, width), LOW), shape((share, width), F32), shape((1, width), F32)],
        prefetch=(order,),
        flops=4 * share * inner * width,
    )


def row_call(name, kernel, order, given, whole, out_kinds, sums):
    share, width = given[-1][0].shape
    share = min(v.shape[0] for v, _ in given)
    step = tile_of(share, 64)
    blocks = share // step

    def spec(place):
        if place is None:
            return pl.BlockSpec((step, width), lambda i, o: (i, 0))
        return pl.BlockSpec((step, width), lambda i, o: (o[place] * blocks + i, 0))

    line = pl.BlockSpec((1, width), lambda i, o: (0, 0))
    return call(
        name,
        kernel,
        (*[v for v, _ in given], *whole),
        (blocks,),
        [spec(place) for _, place in given] + [line for _ in whole],
        [pl.BlockSpec((step, width), lambda i, o: (i, 0)) for _ in out_kinds]
        + [line for _ in range(sums)],
        [shape((share, width), kind) for kind in out_kinds]
        + [shape((1, width), F32) for _ in range(sums)],
        prefetch=(order,),
        flops=20 * share * width,
    )


def sum_parts(refs):
    total = refs[0][...].astype(F32)
    for ref in refs[1:]:
        total = total + ref[...].astype(F32)
    return total


def add_column(ref, values):
    part = jnp.sum(values, axis=0, keepdims=True)

    @pl.when(pl.program_id(0) == 0)
    def _():
        ref[...] = part

    @pl.when(pl.program_id(0) > 0)
    def _():
        ref[...] += part


def hidden_kernel(parts, order_ref, *refs):
    token_ref, squares_ref, magnitude_ref, gain_ref, pre_ref, hidden_ref, normed_ref = refs[parts:]
    pre = sum_parts(refs[:parts])
    hidden = token_ref[...].astype(F32) + pre * (magnitude_ref[...] / jnp.sqrt(squares_ref[...]))
    pre_ref[...] = pre
    hidden_ref[...] = hidden
    normed_ref[...] = (hidden * rms_rows(hidden) * gain_ref[...]).astype(LOW)


def mixed_kernel(parts, order_ref, *refs):
    hidden_ref, squares_ref, magnitude_ref, mixed_ref = refs[parts:]
    scale = magnitude_ref[...] / jnp.sqrt(squares_ref[...])
    mixed_ref[...] = (hidden_ref[...] + sum_parts(refs[:parts]) * scale).astype(LOW)


def norm_back(grad_normed, values, gain):
    factor = rms_rows(values)
    scaled = grad_normed * gain
    inner = jnp.mean(scaled * values, axis=1, keepdims=True)
    back = factor * scaled - values * (factor * factor * factor * inner)
    return back, grad_normed * values * factor


def hidden_back_kernel(parts, order_ref, *refs):
    (
        cot_ref,
        hidden_ref,
        pre_ref,
        squares_ref,
        magnitude_ref,
        gain_ref,
        grad_ref,
        low_ref,
        total_ref,
        gain_grad_ref,
    ) = refs[parts:]
    back, gain_terms = norm_back(sum_parts(refs[:parts]), hidden_ref[...], gain_ref[...])
    grad = cot_ref[...].astype(F32) + back
    grad_ref[...] = grad
    scale = magnitude_ref[...] / jnp.sqrt(squares_ref[...])
    low_ref[...] = (grad * scale).astype(LOW)
    add_column(total_ref, grad * pre_ref[...])
    add_column(gain_grad_ref, gain_terms)


def token_back_kernel(parts, order_ref, *refs):
    token_ref, grad_ref, gain_ref, out_ref, gain_grad_ref = refs[parts:]
    back, gain_terms = norm_back(
        sum_parts(refs[:parts]), token_ref[...].astype(F32), gain_ref[...]
    )
    out_ref[...] = grad_ref[...] + back
    add_column(gain_grad_ref, gain_terms)


def shrink_back_kernel(order_ref, cot_ref, low_ref, squares_ref, magnitude_ref, product_ref, grad_ref):
    scale = magnitude_ref[0] / jnp.sqrt(squares_ref[0])
    grad = (cot_ref[...].astype(F32) * scale).astype(LOW)
    grad_ref[0] = grad
    product_ref[0] = dot(grad, low_ref[0], NT)


def shrink_back(order, cotangent, low, squares, magnitude, groups):
    rows, width = cotangent.shape
    share, inner = rows // groups, low.shape[1]
    line = pl.BlockSpec((1, 1, width), lambda j, o: (0, 0, 0))
    return call(
        "shrink_back",
        shrink_back_kernel,
        (cotangent, low, squares, magnitude),
        (groups,),
        [
            pl.BlockSpec((share, width), lambda j, o: (o[j], 0)),
            pl.BlockSpec((1, inner, width), lambda j, o: (0, 0, 0)),
            line,
            line,
        ],
        [
            pl.BlockSpec((1, share, inner), lambda j, o: (j, 0, 0)),
            pl.BlockSpec((1, share, width), lambda j, o: (j, 0, 0)),
        ],
        [shape((groups, share, inner), F32), shape((groups, share, width), LOW)],
        prefetch=(order,),
        flops=2 * rows * width * inner,
    )


def expand_kernel(
    other_ref, mine_ref, low_ref, squares_ref, magnitude_ref, grad_ref, product_ref, back_ref, total_ref
):
    scale = [magnitude_ref[m] / jnp.sqrt(squares_ref[m]) for m in range(2)]
    width = low_ref.shape[2]
    totals = [jnp.zeros((1, width), F32) for _ in range(2)]
    if width % 128 == 0:
        weights = jnp.concatenate([low_ref[0], low_ref[1]], axis=1)
    for place, source in enumerate((other_ref, mine_ref)):
        if width % 128 == 0:
            pre = dot(source[...], weights)
            gate_pre, up_pre = pre[:, :width], pre[:, width:]
        else:
            gate_pre, up_pre = (dot(source[...], low_ref[m]) for m in range(2))
        gate, up = gate_pre * scale[0], up_pre * scale[1]
        sigmoid = 0.5 + 0.5 * jnp.tanh(0.5 * gate)
        active = gate * sigmoid
        product_ref[0, place] = (active * up).astype(LOW)
        upper = grad_ref[place]
        grad_up = upper * active
        grad_gate = upper * up * sigmoid * (1.0 + gate * (1.0 - sigmoid))
        totals[0] += jnp.sum(grad_gate * gate_pre, axis=0, keepdims=True)
        totals[1] += jnp.sum(grad_up * up_pre, axis=0, keepdims=True)
        back_ref[0, place] = (grad_gate * scale[0]).astype(LOW)
        back_ref[1, place] = (grad_up * scale[1]).astype(LOW)
    for m in range(2):
        total_ref[m] = totals[m]


def expand(pieces, low, squares, magnitude, grad_product, step):
    share, depth = pieces[0].shape
    width = low.shape[2]
    wide = tile_of(width, 128)
    piece = pl.BlockSpec((share, depth), lambda n: (0, 0))
    column = pl.BlockSpec((2, 1, wide), lambda n: (0, 0, n))
    return call(
        "expand",
        expand_kernel,
        (*pieces, low, squares, magnitude, grad_product),
        (width // wide,),
        [
            piece,
            piece,
            pl.BlockSpec((2, depth, wide), lambda n: (0, 0, n)),
            column,
            column,
            pl.BlockSpec((2, share, wide), lambda n: (step, 0, n)),
        ],
        [
            pl.BlockSpec((1, 2, share, wide), lambda n: (0, 0, 0, n)),
            pl.BlockSpec((2, 2, share, wide), lambda n: (0, 0, 0, n)),
            column,
        ],
        [
            shape((1, 2, share, width), LOW),
            shape((2, 2, share, width), LOW),
            shape((2, 1, width), F32),
        ],
        flops=8 * share * depth * width,
    )


def heads_back_kernel(grad_ref, low_ref, out_ref):
    out_ref[...] = dot(grad_ref[...], low_ref[0], NT).astype(LOW)


def heads_back(grad, low):
    rows, width = grad.shape
    inner = low.shape[1]
    return call(
        "heads_back",
        heads_back_kernel,
        (grad, low),
        (1,),
        [
            pl.BlockSpec((rows, width), lambda i: (0, 0)),
            pl.BlockSpec((1, inner, width), lambda i: (0, 0, 0)),
        ],
        [pl.BlockSpec((rows, inner), lambda i: (0, 0))],
        [shape((rows, inner), LOW)],
        flops=2 * rows * width * inner,
    )[0]


def adapter_kernel(n_inputs, n_grads, order_ref, *refs):
    inputs, grads = refs[:n_inputs], refs[n_inputs : n_inputs + n_grads]
    (
        low_ref,
        left_ref,
        right_ref,
        total_ref,
        squares_ref,
        magnitude_ref,
        left_out,
        right_out,
        magnitude_out,
    ) = refs[n_inputs + n_grads :]
    left_rows = left_ref[0]
    right = right_ref[0]
    right_rows = split_rows(right)
    norm = jnp.sqrt(squares_ref[0])
    total = total_ref[0]
    weight = total * magnitude_ref[0] / (norm * norm * norm)
    low = low_ref[0]
    left_sum = -fold(dot(split_rows(right * weight), low, NT))
    right_sum = -(fold(dot(left_rows, low)) * weight)

    def flat(refs, lead):
        for ref in refs:
            view = ref[...].reshape((-1,) + ref.shape[-1:])
            yield view

    rows_in = [view for view in flat(inputs, 0)]
    rows_grad = [view for view in flat(grads, 0)]
    step = min(v.shape[0] for v in rows_in + rows_grad)

    def cut(views):
        return [v[at : at + step] for v in views for at in range(0, v.shape[0], step)]

    for taken, grad in zip(cut(rows_in), cut(rows_grad)):
        down = split_rows(fold(dot(right_rows, grad, NT)))
        left_sum = left_sum + fold(dot(down, taken))
        across = split_rows(fold(dot(left_rows, taken, NT)))
        right_sum = right_sum + fold(dot(across, grad))
    left_out[0] = ADAPT_SCALE * left_sum
    right_out[0] = ADAPT_SCALE * right_sum
    magnitude_out[0] = total / norm


def adapter(order, inputs, grads, low, left_rows, right, total, squares, magnitude):
    members, depth, width = low.shape
    pairs, rank = left_rows.shape[1], right.shape[1]
    column = pl.BlockSpec((1, 1, width), lambda m, o: (m, 0, 0))
    rows = sum(v.size // v.shape[-1] for v, _, _ in inputs)
    return call(
        "adapter",
        functools.partial(adapter_kernel, len(inputs), len(grads)),
        (
            *[v for v, _, _ in inputs],
            *[v for v, _, _ in grads],
            low,
            left_rows,
            right,
            total,
            squares,
            magnitude,
        ),
        (members,),
        [pl.BlockSpec(block, at) for _, block, at in (*inputs, *grads)]
        + [
            pl.BlockSpec((1, depth, width), lambda m, o: (m, 0, 0)),
            pl.BlockSpec((1, pairs, depth), lambda m, o: (m, 0, 0)),
            pl.BlockSpec((1, rank, width), lambda m, o: (m, 0, 0)),
            column,
            column,
            column,
        ],
        [
            pl.BlockSpec((1, rank, depth), lambda m, o: (m, 0, 0)),
            pl.BlockSpec((1, rank, width), lambda m, o: (m, 0, 0)),
            column,
        ],
        [
            shape((members, rank, depth), F32),
            shape((members, rank, width), F32),
            shape((members, 1, width), F32),
        ],
        prefetch=(order,),
        flops=8 * members * (rows + depth) * width * 32,
    )


MESH_IDS = pl.DeviceIdType.MESH
GRAIN = 16


def reduce_kernel(
    groups,
    lines,
    all_ref,
    line_ref,
    all_out,
    line_out,
    all_low,
    line_low,
    all_got,
    part,
    part_low,
    part_got,
    line_got,
    all_full,
    line_full,
    *sems,
):
    me, row = lax.axis_index("mp"), lax.axis_index("dp")
    piece, line_piece = part.shape[0] // lines, line_ref.shape[0] // lines
    mp_peer = [lax.rem(me + k, groups) for k in range(groups)]
    dp_peer = [lax.rem(row + k, lines) for k in range(lines)]
    barrier = pltpu.get_barrier_semaphore()
    for k in range(1, groups):
        pl.semaphore_signal(barrier, 1, device_id={"mp": mp_peer[k]}, device_id_type=MESH_IDS)
    for k in range(1, lines):
        pl.semaphore_signal(barrier, 1, device_id={"dp": dp_peer[k]}, device_id_type=MESH_IDS)
    all_low[...] = all_ref[...].astype(LOW)
    line_low[...] = line_ref[...].astype(LOW)
    pl.semaphore_wait(barrier, groups + lines - 2)

    def send(source, target, stage, k, axis, peer):
        copy = pltpu.make_async_remote_copy(
            src_ref=source,
            dst_ref=target,
            send_sem=sems[2 * stage].at[k],
            recv_sem=sems[2 * stage + 1].at[k],
            device_id={axis: peer},
            device_id_type=MESH_IDS,
        )
        copy.start()
        return copy

    over_mp = [
        send(all_low.at[mp_peer[k]], all_got.at[k], 0, k, "mp", mp_peer[k])
        for k in range(1, groups)
    ]
    over_dp = [
        send(
            line_low.at[pl.ds(dp_peer[k] * line_piece, line_piece)],
            line_got.at[k],
            1,
            k,
            "dp",
            dp_peer[k],
        )
        for k in range(1, lines)
    ]
    total = all_ref[me]
    for k, copy in enumerate(over_mp, 1):
        copy.wait_recv()
        total = total + all_got[k].astype(F32)
    part[...] = total
    part_low[...] = total.astype(LOW)
    part_dp = [
        send(part_low.at[pl.ds(dp_peer[k] * piece, piece)], part_got.at[k], 2, k, "dp", dp_peer[k])
        for k in range(1, lines)
    ]
    mine = pl.ds(row * line_piece, line_piece)
    total = line_ref[mine]
    for k, copy in enumerate(over_dp, 1):
        copy.wait_recv()
        total = total + line_got[k].astype(F32)
    line_full[mine] = total.astype(LOW)
    line_back = [
        send(line_full.at[mine], line_full.at[mine], 3, k, "dp", dp_peer[k])
        for k in range(1, lines)
    ]
    held = pl.ds(row * piece, piece)
    total = part[held]
    for k, copy in enumerate(part_dp, 1):
        copy.wait_recv()
        total = total + part_got[k].astype(F32)
    all_full[me, held] = total.astype(LOW)
    part_back = [
        send(all_full.at[me, held], all_full.at[me, held], 4, k, "dp", dp_peer[k])
        for k in range(1, lines)
    ]
    for copy in part_back:
        copy.wait_recv()
    all_back = [
        send(all_full.at[me], all_full.at[me], 5, k, "mp", mp_peer[k]) for k in range(1, groups)
    ]
    for copy in line_back:
        copy.wait_recv()
    line_out[...] = line_full[...].astype(F32)
    for copy in all_back:
        copy.wait_recv()
    all_out[...] = all_full[...].astype(F32)
    for copy in over_mp + over_dp + part_dp + line_back + part_back + all_back:
        copy.wait_send()


def pad_to(values, axis, size):
    spare = -values.shape[axis] % size
    if spare == 0:
        return values
    widths = [(0, spare if i == axis else 0) for i in range(values.ndim)]
    return jnp.pad(values, widths)


def reduce_devices(name, identity, over_all, over_all_lines, over_dp, over_dp_lines):
    groups, lines = lax.axis_size("mp"), lax.axis_size("dp")
    width = over_all[0].shape[-1]
    cells = width // groups // 128

    def cut(values, parts):
        values = pad_to(values, 2, 128 * parts)
        members, rank, wide = values.shape
        values = values.reshape(members, rank, parts, wide // parts // 128, 128)
        return values.transpose(2, 0, 3, 1, 4).reshape(parts, -1, rank, 128)

    def cut_lines(values, parts):
        flat = jnp.concatenate([v.reshape(parts, -1) for v in values], axis=1)
        return pad_to(flat, 1, GRAIN * 128).reshape(parts, -1, GRAIN, 128)

    def pile(blocks, values, parts):
        found = [cut(v, parts) for v in blocks] + [cut_lines(values, parts)]
        return pad_to(jnp.concatenate(found, axis=1), 1, lines), [v.shape[1] for v in found]

    every, every_sizes = pile(over_all, over_all_lines, groups)
    line, line_sizes = pile(over_dp, over_dp_lines, 1)
    line = line[0]
    count, line_count = every.shape[1], line.shape[0]
    vmem = pl.BlockSpec(memory_space=pltpu.VMEM)
    tail = (GRAIN, 128)
    sizes = (groups, lines, lines, lines, lines, groups)
    every_out, line_out = pl.pallas_call(
        functools.partial(reduce_kernel, groups, lines),
        name=name,
        out_shape=[shape(every.shape, F32), shape(line.shape, F32)],
        in_specs=[vmem, vmem],
        out_specs=[vmem, vmem],
        scratch_shapes=[
            pltpu.VMEM(every.shape, LOW),
            pltpu.VMEM(line.shape, LOW),
            pltpu.VMEM(every.shape, LOW),
            pltpu.VMEM((count,) + tail, F32),
            pltpu.VMEM((count,) + tail, LOW),
            pltpu.VMEM((lines, count // lines) + tail, LOW),
            pltpu.VMEM((lines, line_count // lines) + tail, LOW),
            pltpu.VMEM(every.shape, LOW),
            pltpu.VMEM(line.shape, LOW),
        ]
        + [pltpu.SemaphoreType.DMA((n,)) for n in sizes for _ in range(2)],
        compiler_params=pltpu.CompilerParams(
            collective_id=identity, has_side_effects=True, vmem_limit_bytes=32 * 2**20
        ),
        cost_estimate=pl.CostEstimate(
            flops=1000, bytes_accessed=40 * every.size + 40 * line.size, transcendentals=0
        ),
    )(every, line)

    def restore(values, sizes, blocks, flat, parts):
        at, found = 0, []
        for like, size in zip(blocks, sizes):
            members, rank, wide = like.shape
            view = values[:, at : at + size].reshape(parts, members, -1, rank, 128)
            view = view.transpose(1, 3, 0, 2, 4).reshape(members, rank, -1)
            found.append(view[:, :, :wide])
            at += size
        rest, at = values[:, at : at + sizes[-1]].reshape(parts, -1), 0
        for like in flat:
            size = like.size // parts
            found.append(rest[:, at : at + size].reshape(like.shape))
            at += size
        return found

    return (
        restore(every_out, every_sizes, over_all, over_all_lines, groups),
        restore(line_out[None], line_sizes, over_dp, over_dp_lines, 1),
    )


def geometry(segment):
    length = segment.shape[0]
    places = lax.broadcasted_iota(jnp.int32, (length, length), 0)
    others = lax.broadcasted_iota(jnp.int32, (length, length), 1)
    visible = (segment[:, None] == segment[None, :]) & (others <= places)
    offset = jnp.sum(visible.astype(F32), axis=1) - 1.0
    half_dim = HEAD_DIM // 2
    frequency = jnp.exp(
        -jnp.log(ROPE_BASE) * 2.0 * jnp.arange(half_dim, dtype=F32) / HEAD_DIM
    )
    angles = offset[:, None] * frequency[None, :]
    cosine, sine = jnp.cos(angles), jnp.sin(angles)
    first = jnp.arange(length, dtype=jnp.int32) - offset.astype(jnp.int32)
    return (
        first[:, None],
        jnp.concatenate([cosine, cosine], axis=1),
        jnp.concatenate([-sine, sine], axis=1),
    )


def body(
    tokens,
    cotangent,
    segment_ids,
    attend_gain,
    expand_gain,
    heads_base,
    heads_left,
    heads_right,
    heads_magnitude,
    output_base,
    output_left,
    output_right,
    output_magnitude,
    expand_base,
    expand_left,
    expand_right,
    expand_magnitude,
    shrink_base,
    shrink_left,
    shrink_right,
    shrink_magnitude,
):
    groups = lax.axis_size("mp")
    chips = groups // CORES
    index = lax.axis_index("mp")
    chip, core = index // CORES, index % CORES
    rows, width = tokens.shape
    share = rows // groups
    local_heads = heads_base.shape[2]
    order = jnp.stack(
        [
            (chip + step) % chips * CORES + (core + 1 + place) % CORES
            for step in range(chips)
            for place in range(CORES)
        ]
    ).astype(jnp.int32)

    def sibling(values):
        return lax.ppermute(
            values, "mp", [(i, i // CORES * CORES + (i + 1) % CORES) for i in range(groups)]
        )

    def to_chip(values, step):
        return lax.ppermute(
            values,
            "mp",
            [((i, ((i // CORES + step) % chips) * CORES + i % CORES)) for i in range(groups)],
        )

    def mp_sum(values):
        values = values + sibling(values)
        total = values
        for step in range(1, chips):
            total = total + to_chip(values, step)
        return total

    def reduce_scatter(product):
        parts = []
        for step in range(1, chips):
            send, keep = product(step)
            joined = (keep + sibling(send).astype(F32)).astype(LOW)
            parts.append(to_chip(joined, step))
        send, keep = product(0)
        return [keep, sibling(send), *parts]

    def gather(own):
        pieces = [(sibling(own), own)]
        for step in range(1, chips):
            arrived = to_chip(own, chips - step)
            pieces.append((sibling(arrived), arrived))
        return pieces

    heads_rows, output_rows = left_pairs(heads_left), left_pairs(output_left[None])
    expand_rows, shrink_rows = left_pairs(expand_left), left_pairs(shrink_left[None])
    heads_mag, output_mag = heads_magnitude[:, None], output_magnitude[None, None]
    expand_mag, shrink_mag = expand_magnitude[:, None], shrink_magnitude[None, None]
    attend_line, expand_line = attend_gain[None], expand_gain[None]

    output_low, output_part = merge(
        output_base[None], output_left[None], output_right[None], output_base.shape[0], 512
    )
    shrink_low, shrink_part = merge(
        shrink_base[None], shrink_left[None], shrink_right[None], shrink_base.shape[0], 512
    )
    tokens, output_part, shrink_part = lax.optimization_barrier((tokens, output_part, shrink_part))
    squares = mp_sum(jnp.concatenate([output_part, shrink_part], axis=1))
    output_sq, shrink_sq = squares[:, :1], squares[:, 1:]

    first, cos_table, sine_table = geometry(segment_ids.reshape(-1))
    normed, heads_low, post, heads_sq = project_heads(
        tokens,
        attend_line,
        heads_base,
        heads_left,
        heads_right,
        heads_mag,
        jnp.stack([cos_table, jnp.ones_like(cos_table)]),
        jnp.stack([sine_table, jnp.zeros_like(sine_table)]),
    )
    heads_out = attend(post, first)
    heads_parts = heads_out.reshape(1, groups, share, local_heads)
    output_parts = reduce_scatter(
        lambda step: pair_product(order, heads_parts, output_low, NN, step, True)
    )
    expand_low, expand_sq = merge(expand_base, expand_left, expand_right, 512, expand_base.shape[2])
    grad_product, shrink_grad = shrink_back(
        order, cotangent, shrink_low, shrink_sq, shrink_mag, groups
    )
    output_pre, hidden, normed_own = row_call(
        "hidden",
        functools.partial(hidden_kernel, len(output_parts)),
        order,
        [(part, None) for part in output_parts] + [(tokens, 1)],
        (output_sq[0], output_mag[0], expand_line),
        (F32, F32, LOW),
        0,
    )
    normed_mid = gather(normed_own)
    forward = [
        expand(normed_mid[step], expand_low, expand_sq, expand_mag, grad_product, step)
        for step in range(chips)
    ]
    products, expand_grads = [f[0] for f in forward], [f[1] for f in forward]
    expand_total = functools.reduce(jnp.add, [f[2] for f in forward])
    mid_parts = reduce_scatter(
        lambda step: pair_product(order, expand_grads[step], expand_low, NT, 0, False)
    )
    shrunk = [shrink_product(order, products[step], shrink_low, cotangent, step) for step in range(chips)]
    grad_hidden, output_grad_own, output_total, expand_gain_part = row_call(
        "hidden_back",
        functools.partial(hidden_back_kernel, len(mid_parts)),
        order,
        [(part, None) for part in mid_parts] + [(cotangent, 1), (hidden, None), (output_pre, None)],
        (output_sq[0], output_mag[0], expand_line),
        (F32, LOW),
        2,
    )
    shrink_total = functools.reduce(jnp.add, [piece[2] for piece in shrunk])
    output_grad = [piece for pair in gather(output_grad_own) for piece in pair]
    shrink_joined = [
        (keep + sibling(send).astype(F32)).astype(LOW) for send, keep, _ in shrunk[1:]
    ]
    shrink_joined, output_grad = lax.optimization_barrier((shrink_joined, output_grad))
    shrink_parts = [shrunk[0][1], sibling(shrunk[0][0])] + [
        to_chip(joined, step) for step, joined in enumerate(shrink_joined, 1)
    ]
    (mixed,) = row_call(
        "mixed",
        functools.partial(mixed_kernel, len(shrink_parts)),
        order,
        [(part, None) for part in shrink_parts] + [(hidden, None)],
        (shrink_sq[0], shrink_mag[0]),
        (LOW,),
        0,
    )
    heads_grads, heads_total = attend_back(
        order,
        post,
        first,
        cos_table,
        sine_table,
        heads_mag,
        heads_sq,
        [heads_back(piece, output_low) for piece in output_grad],
    )
    grad_parts = heads_grads.reshape(3, groups, share, local_heads)
    token_parts = reduce_scatter(
        lambda step: pair_product(order, grad_parts, heads_low, NT, step, True)
    )
    grad_tokens, attend_gain_part = row_call(
        "token_back",
        functools.partial(token_back_kernel, len(token_parts)),
        order,
        [(part, None) for part in token_parts] + [(tokens, 1), (grad_hidden, None)],
        (attend_line,),
        (F32,),
        1,
    )

    shrink_total, output_total = mp_sum(shrink_total), mp_sum(output_total)

    def whole(values, lead):
        return (values, (None,) * lead + values.shape[lead:], lambda m, o: (0,) * values.ndim)

    def of_member(values):
        return (
            values,
            (None,) + values.shape[1:],
            lambda m, o: (m,) + (0,) * (values.ndim - 1),
        )

    expand_left_part, expand_right_part, expand_mag_part = adapter(
        order,
        [whole(piece, 0) for pair in normed_mid for piece in pair],
        [of_member(grad) for grad in expand_grads],
        expand_low,
        expand_rows,
        expand_right,
        expand_total,
        expand_sq,
        expand_mag,
    )
    shrink_left_part, shrink_right_part, shrink_mag_part = adapter(
        order,
        [whole(product, 1) for product in products],
        [whole(shrink_grad, 0)],
        shrink_low,
        shrink_rows,
        shrink_right[None],
        shrink_total[None],
        shrink_sq,
        shrink_mag,
    )
    output_left_part, output_right_part, output_mag_part = adapter(
        order,
        [
            (
                heads_parts,
                (None, None, share, local_heads),
                functools.partial(lambda place, m, o: (0, o[place], 0, 0), place),
            )
            for place in range(groups)
        ],
        [whole(piece, 0) for piece in output_grad],
        output_low,
        output_rows,
        output_right[None],
        output_total[None],
        output_sq,
        output_mag,
    )
    heads_left_part, heads_right_part, heads_mag_part = adapter(
        order,
        [whole(normed, 0)],
        [of_member(heads_grads)],
        heads_low,
        heads_rows,
        heads_right,
        heads_total,
        heads_sq,
        heads_mag,
    )

    (
        (expand_left_grad, shrink_right_grad, expand_gain_grad),
        (expand_right_grad, shrink_left_grad, expand_mag_grad, shrink_mag_grad),
    ) = reduce_devices(
        "reduce_early",
        1,
        [expand_left_part, shrink_right_part],
        [expand_gain_part],
        [expand_right_part, shrink_left_part],
        [expand_mag_part, shrink_mag_part],
    )
    (
        (heads_left_grad, output_right_grad, attend_gain_grad),
        (heads_right_grad, output_left_grad, heads_mag_grad, output_mag_grad),
    ) = reduce_devices(
        "reduce_late",
        2,
        [heads_left_part, output_right_part],
        [attend_gain_part],
        [heads_right_part, output_left_part],
        [heads_mag_part, output_mag_part],
    )
    return (
        mixed,
        grad_tokens,
        attend_gain_grad[0],
        expand_gain_grad[0],
        jnp.swapaxes(heads_left_grad, 1, 2),
        heads_right_grad,
        heads_mag_grad[:, 0],
        output_left_grad[0].T,
        output_right_grad[0],
        output_mag_grad[0, 0],
        jnp.swapaxes(expand_left_grad, 1, 2),
        expand_right_grad,
        expand_mag_grad[:, 0],
        shrink_left_grad[0].T,
        shrink_right_grad[0],
        shrink_mag_grad[0, 0],
    )


def solution(mesh):
    placed = (
        P("dp", None),
        P("dp", None),
        P("dp", None),
        P(),
        P(),
        P(None, None, "mp"),
        P(),
        P(None, None, "mp"),
        P(None, "mp"),
        P("mp", None),
        P("mp", None),
        P(),
        P(),
        P(None, None, "mp"),
        P(),
        P(None, None, "mp"),
        P(None, "mp"),
        P("mp", None),
        P("mp", None),
        P(),
        P(),
    )
    return jax.shard_map(
        body,
        mesh=mesh,
        in_specs=placed,
        out_specs=(
            P(("dp", "mp"), None),
            P(("dp", "mp"), None),
            P(),
            P(),
            P(),
            P(None, None, "mp"),
            P(None, "mp"),
            P("mp", None),
            P(),
            P(),
            P(),
            P(None, None, "mp"),
            P(None, "mp"),
            P("mp", None),
            P(),
            P(),
        ),
        check_vma=False,
    )
```

```python
import functools

import jax
import jax.numpy as jnp
from jax import lax
from jax.experimental import pallas as pl
from jax.experimental.pallas import tpu as pltpu
from jax.sharding import PartitionSpec as P

HEAD_DIM = 128
CORES = 2
LONGEST = 512
ATTEND_BLOCK = 256
ADAPT_SCALE = 2.0
NORM_EPS = 1e-05
ROPE_BASE = 10000.0
MASKED = -1e30

F32 = jnp.float32
LOW = jnp.bfloat16
NN = (((1,), (0,)), ((), ()))
NT = (((1,), (1,)), ((), ()))
TN = (((0,), (0,)), ((), ()))


def dot(left, right, dims=NN):
    return lax.dot_general(left, right, dims, preferred_element_type=F32)


def shape(dims, kind):
    return jax.ShapeDtypeStruct(tuple(dims), kind)


def call(name, kernel, operands, grid, in_specs, out_specs, out_shape, scratch=(), prefetch=(), flops=0, mib=60):
    moved = sum(v.size * v.dtype.itemsize for v in operands)
    moved += sum(v.size * v.dtype.itemsize for v in out_shape)
    return pl.pallas_call(
        kernel,
        name=name,
        out_shape=out_shape,
        grid_spec=pltpu.PrefetchScalarGridSpec(
            num_scalar_prefetch=len(prefetch),
            grid=grid,
            in_specs=in_specs,
            out_specs=out_specs,
            scratch_shapes=scratch,
        ),
        compiler_params=pltpu.CompilerParams(vmem_limit_bytes=mib * 2**20),
        cost_estimate=pl.CostEstimate(flops=flops, bytes_accessed=moved, transcendentals=0),
    )(*prefetch, *operands)


def tile_of(size, most):
    return most if size % most == 0 else size


def split_rows(values):
    top = values.astype(LOW)
    rest = (values - top.astype(F32)).astype(LOW)
    return jnp.concatenate([top, rest], axis=0)


def left_pairs(left_map):
    turned = jnp.swapaxes(left_map, -1, -2)
    top = lax.reduce_precision(turned, 8, 7)
    return jnp.concatenate([top, turned - top], axis=-2).astype(LOW)


def fold(values):
    half = values.shape[0] // 2
    return values[:half] + values[half:]


def merge_tile(base_at, low_put, left_rows, right, depth):
    rank = right.shape[0]
    doubled = ADAPT_SCALE * right
    top = doubled.astype(LOW)
    rest = (doubled - top.astype(F32)).astype(LOW)
    right_stack = jnp.concatenate([top, rest, top], axis=0)
    left_stack = jnp.concatenate([left_rows[:rank], left_rows[:rank], left_rows[rank:]], axis=0)
    squares = jnp.zeros((1, right.shape[1]), F32)
    step = 128 if depth % 128 == 0 else depth
    for start in range(0, depth, step):
        merged = base_at(start, step).astype(F32) + dot(
            left_stack[:, start : start + step], right_stack, TN
        )
        low_put(start, step, merged.astype(LOW))
        squares = squares + jnp.sum(merged * merged, axis=0, keepdims=True)
    return squares


def merge_kernel(base_ref, left_ref, right_ref, low_ref, squares_ref):
    depth = base_ref.shape[1]

    def put(start, step, tile):
        low_ref[0, start : start + step, :] = tile

    squares = merge_tile(
        lambda start, step: base_ref[0, start : start + step, :],
        put,
        left_ref[0],
        right_ref[0],
        depth,
    )

    @pl.when(pl.program_id(2) == 0)
    def _():
        squares_ref[0] = squares

    @pl.when(pl.program_id(2) > 0)
    def _():
        squares_ref[0] += squares


def merge(base, left_rows, right, deep, wide):
    members, depth, width = base.shape
    pairs, rank = left_rows.shape[1], right.shape[1]
    return call(
        "merge",
        merge_kernel,
        (base, left_rows, right),
        (members, width // wide, depth // deep),
        [
            pl.BlockSpec((1, deep, wide), lambda m, n, k: (m, k, n)),
            pl.BlockSpec((1, pairs, deep), lambda m, n, k: (m, 0, k)),
            pl.BlockSpec((1, rank, wide), lambda m, n, k: (m, 0, n)),
        ],
        [
            pl.BlockSpec((1, deep, wide), lambda m, n, k: (m, k, n)),
            pl.BlockSpec((1, 1, wide), lambda m, n, k: (m, 0, n)),
        ],
        [shape(base.shape, LOW), shape((members, 1, width), F32)],
        flops=2 * members * depth * width * 256,
    )


def rms_rows(values):
    return lax.rsqrt(jnp.mean(values * values, axis=1, keepdims=True) + NORM_EPS)


def heads_kernel(
    token_ref,
    gain_ref,
    base_ref,
    left_ref,
    right_ref,
    magnitude_ref,
    cos_ref,
    sine_ref,
    normed_ref,
    low_ref,
    post_ref,
    squares_ref,
):
    total_rows = token_ref.shape[0]
    depth, width = base_ref.shape[1:]

    @pl.when((pl.program_id(0) == 0) & (pl.program_id(1) == 0))
    def _():
        step = 128

        def some(i, carry):
            at = pl.ds(pl.multiple_of(i * step, step), step)
            values = token_ref[at, :].astype(F32)
            normed_ref[at, :] = (values * rms_rows(values) * gain_ref[...]).astype(LOW)
            return carry

        lax.fori_loop(0, total_rows // step, some, 0)

    def put(start, step, tile):
        low_ref[0, start : start + step, :] = tile

    squares = merge_tile(
        lambda start, step: base_ref[0, start : start + step, :],
        put,
        left_ref[0],
        right_ref[0],
        depth,
    )
    squares_ref[0] = squares
    scale = magnitude_ref[0] / jnp.sqrt(squares)
    low = low_ref[0]
    turning = pl.program_id(0) < 2
    step = min(512, total_rows)
    for start in range(0, total_rows, step):
        rows = slice(start, start + step)
        post = dot(normed_ref[rows, :], low) * scale
        cos_table = jnp.where(turning, cos_ref[rows, :], 1.0)
        sine_table = jnp.where(turning, sine_ref[rows, :], 0.0)
        for head in range(0, width, HEAD_DIM):
            piece = post[:, head : head + HEAD_DIM]
            turned = pltpu.roll(piece, HEAD_DIM // 2, 1)
            post_ref[0, rows, head : head + HEAD_DIM] = (
                piece * cos_table + turned * sine_table
            ).astype(LOW)


def project_heads(tokens, gain, base, left_rows, right, magnitude, cos_table, sine_table):
    members, depth, width = base.shape
    rows, pairs, rank = tokens.shape[0], left_rows.shape[1], right.shape[1]
    wide = 256
    whole = lambda m, n: (0, 0)
    return call(
        "project_heads",
        heads_kernel,
        (tokens, gain, base, left_rows, right, magnitude, cos_table, sine_table),
        (members, width // wide),
        [
            pl.BlockSpec((rows, depth), whole),
            pl.BlockSpec((1, depth), whole),
            pl.BlockSpec((1, depth, wide), lambda m, n: (m, 0, n)),
            pl.BlockSpec((1, pairs, depth), lambda m, n: (m, 0, 0)),
            pl.BlockSpec((1, rank, wide), lambda m, n: (m, 0, n)),
            pl.BlockSpec((1, 1, wide), lambda m, n: (m, 0, n)),
            pl.BlockSpec((rows, HEAD_DIM), whole),
            pl.BlockSpec((rows, HEAD_DIM), whole),
        ],
        [
            pl.BlockSpec((rows, depth), whole),
            pl.BlockSpec((1, depth, wide), lambda m, n: (m, 0, n)),
            pl.BlockSpec((1, rows, wide), lambda m, n: (m, 0, n)),
            pl.BlockSpec((1, 1, wide), lambda m, n: (m, 0, n)),
        ],
        [
            shape((rows, depth), LOW),
            shape(base.shape, LOW),
            shape((members, rows, width), LOW),
            shape((members, 1, width), F32),
        ],
        flops=2 * members * rows * depth * width,
    )


def key_start(block):
    return max(0, (block * ATTEND_BLOCK - (LONGEST - 1)) // ATTEND_BLOCK * ATTEND_BLOCK)


def masked_probs(scores, first, row_at, key_at):
    scores = scores * HEAD_DIM ** (-0.5)
    places = row_at + lax.broadcasted_iota(jnp.int32, scores.shape, 0)
    others = key_at + lax.broadcasted_iota(jnp.int32, scores.shape, 1)
    scores = jnp.where((others >= first) & (others <= places), scores, MASKED)
    exp_scores = jnp.exp(scores - jnp.max(scores, axis=1, keepdims=True))
    return exp_scores * (1.0 / jnp.sum(exp_scores, axis=1, keepdims=True))


class Unit:
    def __init__(self, head, block):
        self.row_at, self.key_at = block * ATTEND_BLOCK, key_start(block)
        self.rows = slice(self.row_at, self.row_at + ATTEND_BLOCK)
        self.keys = slice(self.key_at, self.row_at + ATTEND_BLOCK)
        self.lanes = slice(head * HEAD_DIM, (head + 1) * HEAD_DIM)


def units_of(rows, width, most):
    units = [
        Unit(head, block)
        for block in range(rows // ATTEND_BLOCK)
        for head in range(width // HEAD_DIM)
    ]
    return [units[at : at + most] for at in range(0, len(units), most)]


def put_rows(ref, lead, row_at, lanes, values, order_ref, groups):
    share = ref.shape[len(lead)] // groups
    step = min(share, values.shape[0])
    for start in range(0, values.shape[0], step):
        group = (row_at + start) // share
        inside = (row_at + start) % share
        at = pl.multiple_of(order_ref[groups + group] * share + inside, step)
        ref[(*lead, pl.ds(at, step), lanes)] = values[start : start + step].astype(ref.dtype)


def attend_kernel(groups, order_ref, query_ref, key_ref, value_ref, first_ref, out_ref):
    for some in units_of(*query_ref.shape[1:], 4):
        scores = [
            dot(query_ref[0, u.rows, u.lanes], key_ref[0, u.keys, u.lanes], NT) for u in some
        ]
        probs = [
            masked_probs(s, first_ref[u.rows, :], u.row_at, u.key_at).astype(LOW)
            for u, s in zip(some, scores)
        ]
        for u, p in zip(some, probs):
            mixed = dot(p, value_ref[0, u.keys, u.lanes])
            put_rows(out_ref, (), u.row_at, u.lanes, mixed, order_ref, groups)


def attend(order, groups, post, first):
    rows, width = post.shape[1:]
    wide = 2 * HEAD_DIM
    member = lambda m: pl.BlockSpec((1, rows, wide), lambda h, o: (m, 0, h))
    return call(
        "attend",
        functools.partial(attend_kernel, groups),
        (post, post, post, first),
        (width // wide,),
        [member(0), member(1), member(2), pl.BlockSpec((rows, 1), lambda h, o: (0, 0))],
        [pl.BlockSpec((rows, wide), lambda h, o: (0, h))],
        [shape((rows, width), LOW)],
        prefetch=(order,),
        flops=4 * rows * rows * width,
        mib=32,
    )[0]


def attend_back_kernel(
    groups,
    order_ref,
    query_ref,
    key_ref,
    value_ref,
    first_ref,
    cos_ref,
    sine_ref,
    magnitude_ref,
    squares_ref,
    low_ref,
    *rest,
):
    pieces, (grad_ref, total_ref, upper_all, heads_grad, key_grad, value_grad, sems) = rest[:-7], rest[-7:]
    rows_all, width = query_ref.shape[1:]
    share = rows_all // groups

    @pl.when(pl.program_id(0) == 0)
    def _():
        copies = []
        for place, piece in enumerate(pieces):
            at = pl.multiple_of(order_ref[place] * share, share)
            copies.append(
                pltpu.make_async_copy(piece, upper_all.at[pl.ds(at, share), :], sems.at[place])
            )
            copies[-1].start()
        for copy in copies:
            copy.wait()

    step = min(512, rows_all)
    for start in range(0, rows_all, step):
        at = slice(start, start + step)
        heads_grad[at, :] = dot(upper_all[at, :], low_ref[0], NT).astype(LOW)
    norm = [jnp.sqrt(squares_ref[m]) for m in range(3)]
    scale = [magnitude_ref[m] / norm[m] for m in range(3)]
    heads = range(0, width, HEAD_DIM)
    totals = [jnp.zeros((1, width), F32) for _ in range(3)]
    filled = set()

    def back(values, rows):
        return values * cos_ref[rows, :] - pltpu.roll(values, HEAD_DIM // 2, 1) * sine_ref[rows, :]

    def add(ref, unit, values):
        for start in range(0, values.shape[0], ATTEND_BLOCK):
            at = unit.key_at + start
            rows = slice(at, at + ATTEND_BLOCK)
            name = (id(ref), at, unit.lanes.start)
            if name in filled:
                ref[rows, unit.lanes] += values[start : start + ATTEND_BLOCK]
            else:
                filled.add(name)
                ref[rows, unit.lanes] = values[start : start + ATTEND_BLOCK]

    def spread(per_head):
        return jnp.concatenate(per_head, axis=1)

    query_totals = [jnp.zeros((1, HEAD_DIM), F32) for _ in heads]
    for some in units_of(rows_all, width, 2):
        scores = [
            dot(query_ref[0, u.rows, u.lanes], key_ref[0, u.keys, u.lanes], NT) for u in some
        ]
        grad_weights = [
            dot(heads_grad[u.rows, u.lanes], value_ref[0, u.keys, u.lanes], NT) for u in some
        ]
        probs = [
            masked_probs(s, first_ref[u.rows, :], u.row_at, u.key_at)
            for u, s in zip(some, scores)
        ]
        grad_scores = [
            (p * (g - jnp.sum(p * g, axis=1, keepdims=True))).astype(LOW)
            for p, g in zip(probs, grad_weights)
        ]
        for u, p, g in zip(some, probs, grad_scores):
            add(value_grad, u, dot(p.astype(LOW), heads_grad[u.rows, u.lanes], TN))
            add(key_grad, u, dot(g, query_ref[0, u.rows, u.lanes], TN))
        for u, g in zip(some, grad_scores):
            grad = back(dot(g, key_ref[0, u.keys, u.lanes]) * HEAD_DIM ** (-0.5), u.rows)
            head = u.lanes.start // HEAD_DIM
            post = back(query_ref[0, u.rows, u.lanes].astype(F32), u.rows)
            query_totals[head] = query_totals[head] + jnp.sum(grad * post, axis=0, keepdims=True)
            put_rows(grad_ref, (0,), u.row_at, u.lanes, grad * scale[0][:, u.lanes], order_ref, groups)
    totals[0] = spread(query_totals)
    for row_at in range(0, rows_all, ATTEND_BLOCK):
        rows = slice(row_at, row_at + ATTEND_BLOCK)
        for head in heads:
            lanes = slice(head, head + HEAD_DIM)
            grad = back(key_grad[rows, lanes] * HEAD_DIM ** (-0.5), rows)
            post = back(key_ref[0, rows, lanes].astype(F32), rows)
            part = jnp.sum(grad * post, axis=0, keepdims=True)
            query_totals[head // HEAD_DIM] = part if row_at == 0 else query_totals[head // HEAD_DIM] + part
            put_rows(grad_ref, (1,), row_at, lanes, grad * scale[1][:, lanes], order_ref, groups)
        grad = value_grad[rows, :]
        totals[2] = totals[2] + jnp.sum(grad * value_ref[0, rows, :].astype(F32), axis=0, keepdims=True)
        put_rows(grad_ref, (2,), row_at, slice(0, width), grad * scale[2], order_ref, groups)
    totals[1] = spread(query_totals)
    for m in range(3):
        total_ref[m] = totals[m] / scale[m]


def attend_back(order, groups, post, first, cos_table, sine_table, magnitude, squares, low, pieces):
    rows, width = post.shape[1:]
    depth = low.shape[2]
    wide = 2 * HEAD_DIM
    member = lambda m: pl.BlockSpec((1, rows, wide), lambda h, o: (m, 0, h))
    table = pl.BlockSpec((rows, HEAD_DIM), lambda h, o: (0, 0))
    column = pl.BlockSpec((3, 1, wide), lambda h, o: (0, 0, h))
    return call(
        "attend_back",
        functools.partial(attend_back_kernel, groups),
        (post, post, post, first, cos_table, sine_table, magnitude, squares, low, *pieces),
        (width // wide,),
        [
            member(0),
            member(1),
            member(2),
            pl.BlockSpec((rows, 1), lambda h, o: (0, 0)),
            table,
            table,
            column,
            column,
            pl.BlockSpec((1, wide, depth), lambda h, o: (0, h, 0)),
            *[pl.BlockSpec(memory_space=pl.ANY) for _ in pieces],
        ],
        [pl.BlockSpec((3, rows, wide), lambda h, o: (0, 0, h)), column],
        [shape((3, rows, width), LOW), shape((3, 1, width), F32)],
        scratch=[
            pltpu.VMEM((rows, depth), LOW),
            pltpu.VMEM((rows, wide), LOW),
            pltpu.VMEM((rows, wide), F32),
            pltpu.VMEM((rows, wide), F32),
            pltpu.SemaphoreType.DMA((len(pieces),)),
        ],
        prefetch=(order,),
        flops=10 * rows * rows * width + 2 * rows * width * depth,
        mib=48,
    )


def pair_kernel(dims, value_ref, weight_ref, send_ref, keep_ref):
    members, _, share, inner = value_ref.shape
    total = None
    for m in range(members):
        part = dot(value_ref[m].reshape(CORES * share, inner), weight_ref[m], dims)
        total = part if total is None else total + part
    send_ref[...] = total[:share].astype(send_ref.dtype)
    keep_ref[...] = total[share:]


def pair_product(name, values, weights, dims, step):
    members, _, share, inner = values.shape
    width = weights.shape[2] if dims is NN else weights.shape[1]
    wide = tile_of(width, 512)
    if dims is NN:
        weight_spec = pl.BlockSpec((members, inner, wide), lambda n: (0, 0, n))
    else:
        weight_spec = pl.BlockSpec((members, wide, inner), lambda n: (0, n, 0))
    out = pl.BlockSpec((share, wide), lambda n: (0, n))
    return call(
        name,
        functools.partial(pair_kernel, dims),
        (values, weights),
        (width // wide,),
        [pl.BlockSpec((members, CORES, share, inner), lambda n: (0, step, 0, 0)), weight_spec],
        [out, out],
        [shape((share, width), LOW), shape((share, width), F32)],
        flops=4 * members * share * inner * width,
        mib=32,
    )


def shrink_kernel(order_ref, value_ref, weight_ref, other_ref, mine_ref, send_ref, keep_ref, total_ref):
    _, _, share, inner = value_ref.shape
    both = dot(value_ref[0].reshape(CORES * share, inner), weight_ref[0])
    total = jnp.zeros((1, weight_ref.shape[2]), F32)
    for pre, cot_ref, target in (
        (both[:share], other_ref, send_ref),
        (both[share:], mine_ref, keep_ref),
    ):
        target[...] = pre.astype(target.dtype)
        total = total + jnp.sum(pre * cot_ref[...].astype(F32), axis=0, keepdims=True)
    total_ref[...] = total


def shrink_product(order, values, weights, cotangent, step):
    _, _, share, inner = values.shape
    width = weights.shape[2]
    wide = tile_of(width, 512)
    out = pl.BlockSpec((share, wide), lambda n, o: (0, n))
    cot = lambda place: pl.BlockSpec((share, wide), lambda n, o: (o[place], n))
    return call(
        "shrink_product",
        shrink_kernel,
        (values, weights, cotangent, cotangent),
        (width // wide,),
        [
            pl.BlockSpec((1, CORES, share, inner), lambda n, o: (0, 0, 0, 0)),
            pl.BlockSpec((1, inner, wide), lambda n, o: (0, 0, n)),
            cot(CORES * step),
            cot(CORES * step + 1),
        ],
        [out, out, pl.BlockSpec((1, wide), lambda n, o: (0, n))],
        [shape((share, width), LOW), shape((share, width), F32), shape((1, width), F32)],
        prefetch=(order,),
        flops=4 * share * inner * width,
        mib=32,
    )


def row_call(name, kernel, given, whole, out_kinds, sums):
    share, width = given[0].shape
    step = tile_of(share, 64)
    line = pl.BlockSpec((1, width), lambda i: (0, 0))
    return call(
        name,
        functools.partial(kernel, len(given)),
        (*given, *whole),
        (share // step,),
        [pl.BlockSpec(memory_space=pltpu.VMEM) for _ in given] + [line for _ in whole],
        [pl.BlockSpec((step, width), lambda i: (i, 0)) for _ in out_kinds]
        + [line for _ in range(sums)],
        [shape((share, width), kind) for kind in out_kinds]
        + [shape((1, width), F32) for _ in range(sums)],
        flops=20 * share * width,
        mib=16,
    )


def now(ref):
    step = tile_of(ref.shape[0], 64)
    return ref[pl.ds(pl.multiple_of(pl.program_id(0) * step, step), step), :].astype(F32)


def sum_parts(refs):
    total = now(refs[0])
    for ref in refs[1:]:
        total = total + now(ref)
    return total


def add_column(ref, values):
    part = jnp.sum(values, axis=0, keepdims=True)

    @pl.when(pl.program_id(0) == 0)
    def _():
        ref[...] = part

    @pl.when(pl.program_id(0) > 0)
    def _():
        ref[...] += part


def hidden_kernel(count, *refs):
    given, (squares_ref, magnitude_ref, gain_ref, pre_ref, hidden_ref, normed_ref) = refs[:count], refs[count:]
    pre = sum_parts(given[1:])
    hidden = now(given[0]) + pre * (magnitude_ref[...] / jnp.sqrt(squares_ref[...]))
    pre_ref[...] = pre
    hidden_ref[...] = hidden
    normed_ref[...] = (hidden * rms_rows(hidden) * gain_ref[...]).astype(LOW)


def mixed_kernel(count, *refs):
    given, (squares_ref, magnitude_ref, mixed_ref) = refs[:count], refs[count:]
    scale = magnitude_ref[...] / jnp.sqrt(squares_ref[...])
    mixed_ref[...] = (now(given[0]) + sum_parts(given[1:]) * scale).astype(LOW)


def norm_back(grad_normed, values, gain):
    factor = rms_rows(values)
    scaled = grad_normed * gain
    inner = jnp.mean(scaled * values, axis=1, keepdims=True)
    back = factor * scaled - values * (factor * factor * factor * inner)
    return back, grad_normed * values * factor


def hidden_back_kernel(count, *refs):
    given, rest = refs[:count], refs[count:]
    squares_ref, magnitude_ref, gain_ref, grad_ref, low_ref, total_ref, gain_grad_ref = rest
    cot_ref, hidden_ref, pre_ref = given[:3]
    back, gain_terms = norm_back(sum_parts(given[3:]), now(hidden_ref), gain_ref[...])
    grad = now(cot_ref) + back
    grad_ref[...] = grad
    scale = magnitude_ref[...] / jnp.sqrt(squares_ref[...])
    low_ref[...] = (grad * scale).astype(LOW)
    add_column(total_ref, grad * now(pre_ref))
    add_column(gain_grad_ref, gain_terms)


def token_back_kernel(count, *refs):
    given, (gain_ref, out_ref, gain_grad_ref) = refs[:count], refs[count:]
    back, gain_terms = norm_back(sum_parts(given[2:]), now(given[0]), gain_ref[...])
    out_ref[...] = now(given[1]) + back
    add_column(gain_grad_ref, gain_terms)


def shrink_back_kernel(order_ref, cot_ref, low_ref, squares_ref, magnitude_ref, product_ref, grad_ref):
    scale = magnitude_ref[0] / jnp.sqrt(squares_ref[0])
    grad = (cot_ref[...].astype(F32) * scale).astype(LOW)
    grad_ref[0] = grad
    product_ref[0] = dot(grad, low_ref[0], NT)


def shrink_back(order, cotangent, low, squares, magnitude, groups):
    rows, width = cotangent.shape
    share, inner = rows // groups, low.shape[1]
    line = pl.BlockSpec((1, 1, width), lambda j, o: (0, 0, 0))
    return call(
        "shrink_back",
        shrink_back_kernel,
        (cotangent, low, squares, magnitude),
        (groups,),
        [
            pl.BlockSpec((share, width), lambda j, o: (o[j], 0)),
            pl.BlockSpec((1, inner, width), lambda j, o: (0, 0, 0)),
            line,
            line,
        ],
        [
            pl.BlockSpec((1, share, inner), lambda j, o: (j, 0, 0)),
            pl.BlockSpec((1, share, width), lambda j, o: (j, 0, 0)),
        ],
        [shape((groups, share, inner), F32), shape((groups, share, width), LOW)],
        prefetch=(order,),
        flops=2 * rows * width * inner,
        mib=32,
    )


def expand_kernel(
    other_ref,
    mine_ref,
    low_ref,
    squares_ref,
    magnitude_ref,
    grad_ref,
    product_ref,
    back_ref,
    total_ref,
    rows_both,
):
    share = other_ref.shape[0]

    @pl.when(pl.program_id(0) == 0)
    def _():
        rows_both[:share, :] = other_ref[...]
        rows_both[share:, :] = mine_ref[...]

    scale = [magnitude_ref[m] / jnp.sqrt(squares_ref[m]) for m in range(2)]
    width = low_ref.shape[2]
    totals = [jnp.zeros((1, width), F32) for _ in range(2)]
    if width % 128 == 0:
        pre = dot(rows_both[...], jnp.concatenate([low_ref[0], low_ref[1]], axis=1))
        gate_all, up_all = pre[:, :width], pre[:, width:]
    else:
        gate_all, up_all = (dot(rows_both[...], low_ref[m]) for m in range(2))
    for place in range(CORES):
        rows = slice(place * share, (place + 1) * share)
        gate_pre, up_pre = gate_all[rows], up_all[rows]
        gate, up = gate_pre * scale[0], up_pre * scale[1]
        sigmoid = 0.5 + 0.5 * jnp.tanh(0.5 * gate)
        active = gate * sigmoid
        product_ref[0, place] = (active * up).astype(LOW)
        upper = grad_ref[place]
        grad_up = upper * active
        grad_gate = upper * up * sigmoid * (1.0 + gate * (1.0 - sigmoid))
        totals[0] += jnp.sum(grad_gate * gate_pre, axis=0, keepdims=True)
        totals[1] += jnp.sum(grad_up * up_pre, axis=0, keepdims=True)
        back_ref[0, place] = (grad_gate * scale[0]).astype(LOW)
        back_ref[1, place] = (grad_up * scale[1]).astype(LOW)
    for m in range(2):
        total_ref[m] = totals[m]


def expand(pieces, low, squares, magnitude, grad_product, step):
    share, depth = pieces[0].shape
    width = low.shape[2]
    wide = tile_of(width, 128)
    piece = pl.BlockSpec((share, depth), lambda n: (0, 0))
    column = pl.BlockSpec((2, 1, wide), lambda n: (0, 0, n))
    return call(
        "expand",
        expand_kernel,
        (*pieces, low, squares, magnitude, grad_product),
        (width // wide,),
        [
            piece,
            piece,
            pl.BlockSpec((2, depth, wide), lambda n: (0, 0, n)),
            column,
            column,
            pl.BlockSpec((2, share, wide), lambda n: (step, 0, n)),
        ],
        [
            pl.BlockSpec((1, 2, share, wide), lambda n: (0, 0, 0, n)),
            pl.BlockSpec((2, 2, share, wide), lambda n: (0, 0, 0, n)),
            column,
        ],
        [
            shape((1, 2, share, width), LOW),
            shape((2, 2, share, width), LOW),
            shape((2, 1, width), F32),
        ],
        scratch=[pltpu.VMEM((CORES * share, depth), LOW)],
        flops=8 * share * depth * width,
        mib=32,
    )


def adapter_kernel(n_inputs, n_grads, order_ref, *refs):
    inputs, grads = refs[:n_inputs], refs[n_inputs : n_inputs + n_grads]
    (
        low_ref,
        left_ref,
        right_ref,
        total_ref,
        squares_ref,
        magnitude_ref,
        left_out,
        right_out,
        magnitude_out,
    ) = refs[n_inputs + n_grads :]
    left_rows = left_ref[0]
    right = right_ref[0]
    right_rows = split_rows(right)
    norm = jnp.sqrt(squares_ref[0])
    total = total_ref[0]
    weight = total * magnitude_ref[0] / (norm * norm * norm)
    low = low_ref[0]
    left_sum = -fold(dot(split_rows(right * weight), low, NT))
    right_sum = -(fold(dot(left_rows, low)) * weight)

    def flat(refs, lead):
        for ref in refs:
            view = ref[...].reshape((-1,) + ref.shape[-1:])
            yield view

    rows_in = [view for view in flat(inputs, 0)]
    rows_grad = [view for view in flat(grads, 0)]
    step = min(v.shape[0] for v in rows_in + rows_grad)

    def cut(views):
        return [v[at : at + step] for v in views for at in range(0, v.shape[0], step)]

    for taken, grad in zip(cut(rows_in), cut(rows_grad)):
        down = split_rows(fold(dot(right_rows, grad, NT)))
        left_sum = left_sum + fold(dot(down, taken))
        across = split_rows(fold(dot(left_rows, taken, NT)))
        right_sum = right_sum + fold(dot(across, grad))
    left_out[0] = ADAPT_SCALE * left_sum
    right_out[0] = ADAPT_SCALE * right_sum
    magnitude_out[0] = total / norm


def adapter(order, inputs, grads, low, left_rows, right, total, squares, magnitude):
    members, depth, width = low.shape
    pairs, rank = left_rows.shape[1], right.shape[1]
    column = pl.BlockSpec((1, 1, width), lambda m, o: (m, 0, 0))
    rows = sum(v.size // v.shape[-1] for v, _, _ in inputs)
    return call(
        "adapter",
        functools.partial(adapter_kernel, len(inputs), len(grads)),
        (
            *[v for v, _, _ in inputs],
            *[v for v, _, _ in grads],
            low,
            left_rows,
            right,
            total,
            squares,
            magnitude,
        ),
        (members,),
        [pl.BlockSpec(block, at) for _, block, at in (*inputs, *grads)]
        + [
            pl.BlockSpec((1, depth, width), lambda m, o: (m, 0, 0)),
            pl.BlockSpec((1, pairs, depth), lambda m, o: (m, 0, 0)),
            pl.BlockSpec((1, rank, width), lambda m, o: (m, 0, 0)),
            column,
            column,
            column,
        ],
        [
            pl.BlockSpec((1, rank, depth), lambda m, o: (m, 0, 0)),
            pl.BlockSpec((1, rank, width), lambda m, o: (m, 0, 0)),
            column,
        ],
        [
            shape((members, rank, depth), F32),
            shape((members, rank, width), F32),
            shape((members, 1, width), F32),
        ],
        prefetch=(order,),
        flops=8 * members * (rows + depth) * width * 32,
    )


MESH_IDS = pl.DeviceIdType.MESH
GRAIN = 16


def pieces_of(width):
    return [(at, min(128, width - at)) for at in range(0, width, 128)]


def cells_of(blocks, lines, parts):
    cells, rows = [], []
    for n, block in enumerate(blocks):
        for m in range(block.shape[0]):
            for at, size in pieces_of(block.shape[2] // parts):
                cells.append((n, m, at, size))
    for n, line in enumerate(lines):
        for m in range(line.shape[0]):
            for at, size in pieces_of(line.shape[2] // parts):
                rows.append((n, m, at, size))
    return cells, rows


def pack(blocks, lines, wide_ref, part, parts, cells, rows):
    for i, (n, m, at, size) in enumerate(cells):
        start = part * (blocks[n].shape[2] // parts) + at
        wide_ref[part, i, :, :size] = blocks[n][m, :, start : start + size]
    for i, (n, m, at, size) in enumerate(rows):
        start = part * (lines[n].shape[2] // parts) + at
        cell, row = len(cells) + i // GRAIN, i % GRAIN
        wide_ref[part, cell, row : row + 1, :size] = lines[n][m, :, start : start + size]


def unpack(full_ref, blocks, lines, part, parts, cells, rows):
    for i, (n, m, at, size) in enumerate(cells):
        start = part * (blocks[n].shape[2] // parts) + at
        blocks[n][m, :, start : start + size] = full_ref[part, i].astype(F32)[:, :size]
    for i, (n, m, at, size) in enumerate(rows):
        start = part * (lines[n].shape[2] // parts) + at
        cell, row = len(cells) + i // GRAIN, i % GRAIN
        values = full_ref[part, cell].astype(F32)
        lines[n][m, :, start : start + size] = values[row : row + 1, :size]


def reduce_kernel(groups, lines, counts, *refs):
    n_all, n_all_lines, n_dp, n_dp_lines = counts
    count = sum(counts)
    taken, given, scratch = refs[:count], refs[count : 2 * count], refs[2 * count :]
    ends = [n_all, n_all + n_all_lines, n_all + n_all_lines + n_dp]
    parted = lambda v: (v[: ends[0]], v[ends[0] : ends[1]], v[ends[1] : ends[2]], v[ends[2] :])
    all_in, all_lines_in, dp_in, dp_lines_in = parted(taken)
    all_out, all_lines_out, dp_out, dp_lines_out = parted(given)
    (
        all_ref,
        line_ref,
        all_low,
        line_low,
        all_got,
        part,
        part_low,
        part_got,
        line_got,
        all_full,
        line_full,
        *sems,
    ) = scratch
    me, row = lax.axis_index("mp"), lax.axis_index("dp")
    piece, line_piece = part.shape[0] // lines, line_ref.shape[1] // lines
    mp_peer = [lax.rem(me + k, groups) for k in range(groups)]
    dp_peer = [lax.rem(row + k, lines) for k in range(lines)]
    barrier = pltpu.get_barrier_semaphore()
    for k in range(1, groups):
        pl.semaphore_signal(barrier, 1, device_id={"mp": mp_peer[k]}, device_id_type=MESH_IDS)
    for k in range(1, lines):
        pl.semaphore_signal(barrier, 1, device_id={"dp": dp_peer[k]}, device_id_type=MESH_IDS)
    all_cells = cells_of(all_in, all_lines_in, groups)
    dp_cells = cells_of(dp_in, dp_lines_in, 1)
    all_ref[...] = jnp.zeros_like(all_ref)
    line_ref[...] = jnp.zeros_like(line_ref)
    for q in range(groups):
        pack(all_in, all_lines_in, all_ref, q, groups, *all_cells)
    pack(dp_in, dp_lines_in, line_ref, 0, 1, *dp_cells)
    all_low[...] = all_ref[...].astype(LOW)
    line_low[...] = line_ref[...].astype(LOW)
    pl.semaphore_wait(barrier, groups + lines - 2)

    def send(source, target, stage, k, axis, peer):
        copy = pltpu.make_async_remote_copy(
            src_ref=source,
            dst_ref=target,
            send_sem=sems[2 * stage].at[k],
            recv_sem=sems[2 * stage + 1].at[k],
            device_id={axis: peer},
            device_id_type=MESH_IDS,
        )
        copy.start()
        return copy

    over_mp = [
        send(all_low.at[mp_peer[k]], all_got.at[k], 0, k, "mp", mp_peer[k])
        for k in range(1, groups)
    ]
    over_dp = [
        send(
            line_low.at[0, pl.ds(dp_peer[k] * line_piece, line_piece)],
            line_got.at[k],
            1,
            k,
            "dp",
            dp_peer[k],
        )
        for k in range(1, lines)
    ]
    total = all_ref[me]
    for k, copy in enumerate(over_mp, 1):
        copy.wait_recv()
        total = total + all_got[k].astype(F32)
    part[...] = total
    part_low[...] = total.astype(LOW)
    part_dp = [
        send(part_low.at[pl.ds(dp_peer[k] * piece, piece)], part_got.at[k], 2, k, "dp", dp_peer[k])
        for k in range(1, lines)
    ]
    mine = pl.ds(row * line_piece, line_piece)
    total = line_ref[0, mine]
    for k, copy in enumerate(over_dp, 1):
        copy.wait_recv()
        total = total + line_got[k].astype(F32)
    line_full[0, mine] = total.astype(LOW)
    line_back = [
        send(line_full.at[0, mine], line_full.at[0, mine], 3, k, "dp", dp_peer[k])
        for k in range(1, lines)
    ]
    held = pl.ds(row * piece, piece)
    total = part[held]
    for k, copy in enumerate(part_dp, 1):
        copy.wait_recv()
        total = total + part_got[k].astype(F32)
    all_full[me, held] = total.astype(LOW)
    part_back = [
        send(all_full.at[me, held], all_full.at[me, held], 4, k, "dp", dp_peer[k])
        for k in range(1, lines)
    ]
    for copy in part_back:
        copy.wait_recv()
    all_back = [
        send(all_full.at[me], all_full.at[me], 5, k, "mp", mp_peer[k]) for k in range(1, groups)
    ]
    for copy in line_back:
        copy.wait_recv()
    unpack(line_full, dp_out, dp_lines_out, 0, 1, *dp_cells)
    for copy in all_back:
        copy.wait_recv()
    for q in range(groups):
        unpack(all_full, all_out, all_lines_out, q, groups, *all_cells)
    for copy in over_mp + over_dp + part_dp + line_back + part_back + all_back:
        copy.wait_send()


def reduce_devices(name, identity, over_all, over_all_lines, over_dp, over_dp_lines):
    groups, lines = lax.axis_size("mp"), lax.axis_size("dp")

    def size_of(blocks, rows, parts):
        cells, lines_in = cells_of(blocks, rows, parts)
        size = len(cells) + -(-len(lines_in) // GRAIN)
        return -(-size // lines) * lines

    count, line_count = size_of(over_all, over_all_lines, groups), size_of(over_dp, over_dp_lines, 1)
    operands = (*over_all, *over_all_lines, *over_dp, *over_dp_lines)
    counts = (len(over_all), len(over_all_lines), len(over_dp), len(over_dp_lines))
    vmem = pl.BlockSpec(memory_space=pltpu.VMEM)
    tail = (GRAIN, 128)
    sizes = (groups, lines, lines, lines, lines, groups)
    every, line = (groups, count) + tail, (1, line_count) + tail
    results = pl.pallas_call(
        functools.partial(reduce_kernel, groups, lines, counts),
        name=name,
        out_shape=[shape(v.shape, F32) for v in operands],
        in_specs=[vmem for _ in operands],
        out_specs=[vmem for _ in operands],
        scratch_shapes=[
            pltpu.VMEM(every, F32),
            pltpu.VMEM(line, F32),
            pltpu.VMEM(every, LOW),
            pltpu.VMEM(line, LOW),
            pltpu.VMEM(every, LOW),
            pltpu.VMEM((count,) + tail, F32),
            pltpu.VMEM((count,) + tail, LOW),
            pltpu.VMEM((lines, count // lines) + tail, LOW),
            pltpu.VMEM((lines, line_count // lines) + tail, LOW),
            pltpu.VMEM(every, LOW),
            pltpu.VMEM(line, LOW),
        ]
        + [pltpu.SemaphoreType.DMA((n,)) for n in sizes for _ in range(2)],
        compiler_params=pltpu.CompilerParams(
            collective_id=identity, has_side_effects=True, vmem_limit_bytes=32 * 2**20
        ),
        cost_estimate=pl.CostEstimate(flops=1000, bytes_accessed=50 * 2**20, transcendentals=0),
    )(*operands)
    return results


def geometry(segment):
    length = segment.shape[0]
    places = lax.broadcasted_iota(jnp.int32, (length, length), 0)
    others = lax.broadcasted_iota(jnp.int32, (length, length), 1)
    visible = (segment[:, None] == segment[None, :]) & (others <= places)
    offset = jnp.sum(visible.astype(F32), axis=1) - 1.0
    lane = jnp.arange(HEAD_DIM, dtype=jnp.int32)
    half = (lane % (HEAD_DIM // 2)).astype(F32)
    frequency = jnp.exp(-jnp.log(ROPE_BASE) * 2.0 * half / HEAD_DIM)
    sign = jnp.where(lane < HEAD_DIM // 2, -1.0, 1.0)
    angles = offset[:, None] * frequency[None, :]
    first = jnp.arange(length, dtype=jnp.int32) - offset.astype(jnp.int32)
    return first[:, None], jnp.cos(angles), jnp.sin(angles) * sign[None, :]


def body(
    tokens,
    cotangent,
    segment_ids,
    attend_gain,
    expand_gain,
    heads_base,
    heads_left,
    heads_right,
    heads_magnitude,
    output_base,
    output_left,
    output_right,
    output_magnitude,
    expand_base,
    expand_left,
    expand_right,
    expand_magnitude,
    shrink_base,
    shrink_left,
    shrink_right,
    shrink_magnitude,
):
    groups = lax.axis_size("mp")
    chips = groups // CORES
    index = lax.axis_index("mp")
    chip, core = index // CORES, index % CORES
    rows, width = tokens.shape
    share = rows // groups
    local_heads = heads_base.shape[2]
    device = jnp.arange(groups, dtype=jnp.int32)
    order = jnp.concatenate(
        [
            (chip + device // CORES) % chips * CORES + (core + 1 + device) % CORES,
            (device // CORES + chips - chip) % chips * CORES + (device + CORES - core + 1) % CORES,
        ]
    ).astype(jnp.int32)

    def own(values):
        return lax.dynamic_slice_in_dim(values, index * share, share, 0)

    def tie(*values):
        return lax.optimization_barrier(values)

    def whole(values, lead):
        return (values, (None,) * lead + values.shape[lead:], lambda m, o: (0,) * values.ndim)

    def of_member(values):
        return (
            values,
            (None,) + values.shape[1:],
            lambda m, o: (m,) + (0,) * (values.ndim - 1),
        )

    def sibling(values):
        return lax.ppermute(
            values, "mp", [(i, i // CORES * CORES + (i + 1) % CORES) for i in range(groups)]
        )

    def to_chip(values, step):
        return lax.ppermute(
            values,
            "mp",
            [((i, ((i // CORES + step) % chips) * CORES + i % CORES)) for i in range(groups)],
        )

    def mp_sum(values):
        values = values + sibling(values)
        total = values
        for step in range(1, chips):
            total = total + to_chip(values, step)
        return total

    def reduce_scatter(product):
        parts = []
        for step in range(1, chips):
            send, keep = product(step)
            joined = (keep + sibling(send).astype(F32)).astype(LOW)
            parts.append(to_chip(joined, step))
        send, keep = product(0)
        return [keep, sibling(send), *parts]

    def gather(own):
        pieces = [(sibling(own), own)]
        for step in range(1, chips):
            arrived = to_chip(own, chips - step)
            pieces.append((sibling(arrived), arrived))
        return pieces

    heads_rows, output_rows = left_pairs(heads_left), left_pairs(output_left[None])
    expand_rows, shrink_rows = left_pairs(expand_left), left_pairs(shrink_left[None])
    heads_mag, output_mag = heads_magnitude[:, None], output_magnitude[None, None]
    expand_mag, shrink_mag = expand_magnitude[:, None], shrink_magnitude[None, None]
    attend_line, expand_line = attend_gain[None], expand_gain[None]

    output_low, output_part = merge(
        output_base[None], output_rows, output_right[None], output_base.shape[0], 512
    )
    shrink_low, shrink_part = merge(
        shrink_base[None], shrink_rows, shrink_right[None], shrink_base.shape[0], 512
    )
    tokens, output_part, shrink_part = lax.optimization_barrier((tokens, output_part, shrink_part))
    squares = mp_sum(jnp.concatenate([output_part, shrink_part], axis=1))
    output_sq, shrink_sq = squares[:, :1], squares[:, 1:]

    first, cos_table, sine_table = geometry(segment_ids.reshape(-1))
    normed, heads_low, post, heads_sq = project_heads(
        tokens,
        attend_line,
        heads_base,
        heads_rows,
        heads_right,
        heads_mag,
        cos_table,
        sine_table,
    )
    heads_out = attend(order, groups, post, first)
    heads_parts = heads_out.reshape(1, groups, share, local_heads)
    output_parts = reduce_scatter(
        lambda step: pair_product("output_product", heads_parts, output_low, NN, step)
    )
    expand_low, expand_sq = merge(expand_base, expand_rows, expand_right, 512, expand_base.shape[2])
    grad_product, shrink_grad = shrink_back(
        order, cotangent, shrink_low, shrink_sq, shrink_mag, groups
    )
    own_tokens, own_cot = own(tokens), own(cotangent)
    output_parts, expand_low, grad_product, own_tokens, own_cot = tie(
        output_parts, expand_low, grad_product, own_tokens, own_cot
    )
    output_pre, hidden, normed_own = row_call(
        "hidden",
        hidden_kernel,
        [own_tokens, *output_parts],
        (output_sq[0], output_mag[0], expand_line),
        (F32, F32, LOW),
        0,
    )
    normed_mid = gather(normed_own)

    def feed(step):
        return expand(normed_mid[step], expand_low, expand_sq, expand_mag, grad_product, step)

    def mid_product(step):
        return pair_product("mid_product", forward[step][1], expand_low, NT, 0)

    forward = [feed(0)]
    mid_near = mid_product(0)
    normed_mid[1:], mid_near = tie(normed_mid[1:], mid_near)
    forward += [feed(step) for step in range(1, chips)]
    products, expand_grads = [f[0] for f in forward], [f[1] for f in forward]
    expand_total = functools.reduce(jnp.add, [f[2] for f in forward])
    mid_parts = reduce_scatter(lambda step: mid_product(step) if step else mid_near)
    shrunk = [shrink_product(order, products[step], shrink_low, cotangent, step) for step in range(chips)]
    shrink_total = mp_sum(functools.reduce(jnp.add, [piece[2] for piece in shrunk]))
    shrink_joined = [
        (keep + sibling(send).astype(F32)).astype(LOW) for send, keep, _ in shrunk[1:]
    ]
    expand_adapter = adapter(
        order,
        [whole(piece, 0) for pair in normed_mid for piece in pair],
        [of_member(grad) for grad in expand_grads],
        expand_low,
        expand_rows,
        expand_right,
        expand_total,
        expand_sq,
        expand_mag,
    )
    mid_parts, shrunk, expand_adapter = tie(mid_parts, shrunk, expand_adapter)
    grad_hidden, output_grad_own, output_total, expand_gain_part = row_call(
        "hidden_back",
        hidden_back_kernel,
        [own_cot, hidden, output_pre, *mid_parts],
        (output_sq[0], output_mag[0], expand_line),
        (F32, LOW),
        2,
    )
    output_grad = [piece for pair in gather(output_grad_own) for piece in pair]
    shrink_adapter = adapter(
        order,
        [whole(product, 1) for product in products],
        [whole(shrink_grad, 0)],
        shrink_low,
        shrink_rows,
        shrink_right[None],
        shrink_total[None],
        shrink_sq,
        shrink_mag,
    )
    early = reduce_devices(
        "reduce_early",
        1,
        [expand_adapter[0], shrink_adapter[1]],
        [expand_gain_part[None]],
        [expand_adapter[1], shrink_adapter[0]],
        [expand_adapter[2], shrink_adapter[2]],
    )
    output_grad, shrink_joined, early = tie(output_grad, shrink_joined, early)
    expand_left_grad, shrink_right_grad, expand_gain_grad = early[:3]
    expand_right_grad, shrink_left_grad, expand_mag_grad, shrink_mag_grad = early[3:]
    shrink_parts = [shrunk[0][1], sibling(shrunk[0][0])] + [
        to_chip(joined, step) for step, joined in enumerate(shrink_joined, 1)
    ]
    heads_grads, heads_total = attend_back(
        order,
        groups,
        post,
        first,
        cos_table,
        sine_table,
        heads_mag,
        heads_sq,
        output_low,
        output_grad,
    )
    grad_parts = heads_grads.reshape(3, groups, share, local_heads)
    token_parts = reduce_scatter(
        lambda step: pair_product("normed_product", grad_parts, heads_low, NT, step)
    )
    output_total = mp_sum(output_total)
    output_adapter = adapter(
        order,
        [whole(heads_out, 0)],
        [whole(piece, 0) for piece in output_grad],
        output_low,
        output_rows,
        output_right[None],
        output_total[None],
        output_sq,
        output_mag,
    )
    heads_adapter = adapter(
        order,
        [
            (normed, (share, width), functools.partial(lambda place, m, o: (o[place], 0), place))
            for place in range(groups)
        ],
        [of_member(heads_grads)],
        heads_low,
        heads_rows,
        heads_right,
        heads_total,
        heads_sq,
        heads_mag,
    )
    token_parts, output_adapter, heads_adapter = tie(token_parts, output_adapter, heads_adapter)
    (mixed,) = row_call(
        "mixed", mixed_kernel, [hidden, *shrink_parts], (shrink_sq[0], shrink_mag[0]), (LOW,), 0
    )
    grad_tokens, attend_gain_part = row_call(
        "token_back",
        token_back_kernel,
        [own_tokens, grad_hidden, *token_parts],
        (attend_line,),
        (F32,),
        1,
    )
    late = reduce_devices(
        "reduce_late",
        2,
        [heads_adapter[0], output_adapter[1]],
        [attend_gain_part[None]],
        [heads_adapter[1], output_adapter[0]],
        [heads_adapter[2], output_adapter[2]],
    )
    heads_left_grad, output_right_grad, attend_gain_grad = late[:3]
    heads_right_grad, output_left_grad, heads_mag_grad, output_mag_grad = late[3:]
    return (
        mixed,
        grad_tokens,
        attend_gain_grad[0, 0],
        expand_gain_grad[0, 0],
        jnp.swapaxes(heads_left_grad, 1, 2),
        heads_right_grad,
        heads_mag_grad[:, 0],
        output_left_grad[0].T,
        output_right_grad[0],
        output_mag_grad[0, 0],
        jnp.swapaxes(expand_left_grad, 1, 2),
        expand_right_grad,
        expand_mag_grad[:, 0],
        shrink_left_grad[0].T,
        shrink_right_grad[0],
        shrink_mag_grad[0, 0],
    )


def solution(mesh):
    placed = (
        P("dp", None),
        P("dp", None),
        P("dp", None),
        P(),
        P(),
        P(None, None, "mp"),
        P(),
        P(None, None, "mp"),
        P(None, "mp"),
        P("mp", None),
        P("mp", None),
        P(),
        P(),
        P(None, None, "mp"),
        P(),
        P(None, None, "mp"),
        P(None, "mp"),
        P("mp", None),
        P("mp", None),
        P(),
        P(),
    )
    return jax.shard_map(
        body,
        mesh=mesh,
        in_specs=placed,
        out_specs=(
            P(("dp", "mp"), None),
            P(("dp", "mp"), None),
            P(),
            P(),
            P(),
            P(None, None, "mp"),
            P(None, "mp"),
            P("mp", None),
            P(),
            P(),
            P(),
            P(None, None, "mp"),
            P(None, "mp"),
            P("mp", None),
            P(),
            P(),
        ),
        check_vma=False,
    )
```

```python
import functools

import jax
import jax.numpy as jnp
from jax import lax
from jax.experimental import pallas as pl
from jax.experimental.pallas import tpu as pltpu
from jax.sharding import PartitionSpec as P

HEAD_DIM = 128
CORES = 2
LONGEST = 512
ATTEND_BLOCK = 256
ADAPT_SCALE = 2.0
NORM_EPS = 1e-05
ROPE_BASE = 10000.0
MASKED = -1e30

F32 = jnp.float32
LOW = jnp.bfloat16
NN = (((1,), (0,)), ((), ()))
NT = (((1,), (1,)), ((), ()))
TN = (((0,), (0,)), ((), ()))


def dot(left, right, dims=NN):
    return lax.dot_general(left, right, dims, preferred_element_type=F32)


def shape(dims, kind):
    return jax.ShapeDtypeStruct(tuple(dims), kind)


def call(name, kernel, operands, grid, in_specs, out_specs, out_shape, scratch=(), prefetch=(), flops=0, mib=60):
    moved = sum(v.size * v.dtype.itemsize for v in operands)
    moved += sum(v.size * v.dtype.itemsize for v in out_shape)
    return pl.pallas_call(
        kernel,
        name=name,
        out_shape=out_shape,
        grid_spec=pltpu.PrefetchScalarGridSpec(
            num_scalar_prefetch=len(prefetch),
            grid=grid,
            in_specs=in_specs,
            out_specs=out_specs,
            scratch_shapes=scratch,
        ),
        compiler_params=pltpu.CompilerParams(vmem_limit_bytes=mib * 2**20),
        cost_estimate=pl.CostEstimate(flops=flops, bytes_accessed=moved, transcendentals=0),
    )(*prefetch, *operands)


def tile_of(size, most):
    return most if size % most == 0 else size


def split_rows(values):
    top = values.astype(LOW)
    rest = (values - top.astype(F32)).astype(LOW)
    return jnp.concatenate([top, rest], axis=0)


def left_pairs(left_map):
    turned = jnp.swapaxes(left_map, -1, -2)
    top = lax.reduce_precision(turned, 8, 7)
    return jnp.concatenate([top, turned - top], axis=-2).astype(LOW)


def norm_weight(total, squares, magnitude):
    norm = jnp.sqrt(squares)
    return total * magnitude / (norm * norm * norm)


def sum_refs(refs):
    total = refs[0][...]
    for ref in refs[1:]:
        total = total + ref[...]
    return total


def fold(values):
    half = values.shape[0] // 2
    return values[:half] + values[half:]


def merge_tile(base_at, low_put, left_rows, right, depth):
    rank = right.shape[0]
    doubled = ADAPT_SCALE * right
    top = doubled.astype(LOW)
    rest = (doubled - top.astype(F32)).astype(LOW)
    right_stack = jnp.concatenate([top, rest, top], axis=0)
    left_stack = jnp.concatenate([left_rows[:rank], left_rows[:rank], left_rows[rank:]], axis=0)
    squares = jnp.zeros((1, right.shape[1]), F32)
    step = tile_of(depth, 1024)
    for start in range(0, depth, step):
        merged = base_at(start, step).astype(F32) + dot(
            left_stack[:, start : start + step], right_stack, TN
        )
        low_put(start, step, merged.astype(LOW))
        squares = squares + jnp.sum(merged * merged, axis=0, keepdims=True)
    return squares


def merge_kernel(base_ref, left_ref, right_ref, low_ref, squares_ref):
    depth = base_ref.shape[1]

    def put(start, step, tile):
        low_ref[0, start : start + step, :] = tile

    squares = merge_tile(
        lambda start, step: base_ref[0, start : start + step, :],
        put,
        left_ref[0],
        right_ref[0],
        depth,
    )

    @pl.when(pl.program_id(2) == 0)
    def _():
        squares_ref[0] = squares

    @pl.when(pl.program_id(2) > 0)
    def _():
        squares_ref[0] += squares


def merge(base, left_rows, right, deep, wide):
    members, depth, width = base.shape
    pairs, rank = left_rows.shape[1], right.shape[1]
    return call(
        "merge",
        merge_kernel,
        (base, left_rows, right),
        (members, width // wide, depth // deep),
        [
            pl.BlockSpec((1, deep, wide), lambda m, n, k: (m, k, n)),
            pl.BlockSpec((1, pairs, deep), lambda m, n, k: (m, 0, k)),
            pl.BlockSpec((1, rank, wide), lambda m, n, k: (m, 0, n)),
        ],
        [
            pl.BlockSpec((1, deep, wide), lambda m, n, k: (m, k, n)),
            pl.BlockSpec((1, 1, wide), lambda m, n, k: (m, 0, n)),
        ],
        [shape(base.shape, LOW), shape((members, 1, width), F32)],
        flops=2 * members * depth * width * 256,
    )


def rms_rows(values):
    return lax.rsqrt(jnp.mean(values * values, axis=1, keepdims=True) + NORM_EPS)


def heads_kernel(
    token_ref,
    gain_ref,
    base_ref,
    left_ref,
    right_ref,
    magnitude_ref,
    cos_ref,
    sine_ref,
    normed_ref,
    low_ref,
    post_ref,
    squares_ref,
    across_ref,
    rows_all,
):
    total_rows = token_ref.shape[0]
    depth, width = base_ref.shape[1:]
    rank = right_ref.shape[1]

    @pl.when((pl.program_id(0) == 0) & (pl.program_id(1) == 0))
    def _():
        step = 128

        def some(i, carry):
            at = pl.ds(pl.multiple_of(i * step, step), step)
            values = token_ref[at, :].astype(F32)
            low = (values * rms_rows(values) * gain_ref[...]).astype(LOW)
            normed_ref[at, :] = low
            rows_all[at, :] = low
            return carry

        lax.fori_loop(0, total_rows // step, some, 0)

    rows_all[total_rows:, :] = left_ref[0, :rank, :]

    def put(start, step, tile):
        low_ref[0, start : start + step, :] = tile

    squares = merge_tile(
        lambda start, step: base_ref[0, start : start + step, :],
        put,
        left_ref[0],
        right_ref[0],
        depth,
    )
    squares_ref[0] = squares
    scale = magnitude_ref[0] / jnp.sqrt(squares)
    low = low_ref[0]
    turning = pl.program_id(0) < 2
    step = min(512, total_rows)
    for start in range(0, total_rows, step):
        last = start + step == total_rows
        rows = slice(start, start + step)
        pre = dot(rows_all[start : start + step + (rank if last else 0), :], low)
        if last:
            across_ref[0] = pre[step:]
        post = pre[:step] * scale
        cos_table = jnp.where(turning, cos_ref[rows, :], 1.0)
        sine_table = jnp.where(turning, sine_ref[rows, :], 0.0)
        for head in range(0, width, HEAD_DIM):
            piece = post[:, head : head + HEAD_DIM]
            turned = pltpu.roll(piece, HEAD_DIM // 2, 1)
            post_ref[0, rows, head : head + HEAD_DIM] = (
                piece * cos_table + turned * sine_table
            ).astype(LOW)


def project_heads(tokens, gain, base, left_rows, right, magnitude, cos_table, sine_table):
    members, depth, width = base.shape
    rows, pairs, rank = tokens.shape[0], left_rows.shape[1], right.shape[1]
    wide = 256
    whole = lambda m, n: (0, 0)
    return call(
        "project_heads",
        heads_kernel,
        (tokens, gain, base, left_rows, right, magnitude, cos_table, sine_table),
        (members, width // wide),
        [
            pl.BlockSpec((rows, depth), whole),
            pl.BlockSpec((1, depth), whole),
            pl.BlockSpec((1, depth, wide), lambda m, n: (m, 0, n)),
            pl.BlockSpec((1, pairs, depth), lambda m, n: (m, 0, 0)),
            pl.BlockSpec((1, rank, wide), lambda m, n: (m, 0, n)),
            pl.BlockSpec((1, 1, wide), lambda m, n: (m, 0, n)),
            pl.BlockSpec((rows, HEAD_DIM), whole),
            pl.BlockSpec((rows, HEAD_DIM), whole),
        ],
        [
            pl.BlockSpec((rows, depth), whole),
            pl.BlockSpec((1, depth, wide), lambda m, n: (m, 0, n)),
            pl.BlockSpec((1, rows, wide), lambda m, n: (m, 0, n)),
            pl.BlockSpec((1, 1, wide), lambda m, n: (m, 0, n)),
            pl.BlockSpec((1, rank, wide), lambda m, n: (m, 0, n)),
        ],
        [
            shape((rows, depth), LOW),
            shape(base.shape, LOW),
            shape((members, rows, width), LOW),
            shape((members, 1, width), F32),
            shape((members, rank, width), F32),
        ],
        scratch=[pltpu.VMEM((rows + rank, depth), LOW)],
        flops=2 * members * rows * depth * width,
    )


def key_start(block):
    return max(0, (block * ATTEND_BLOCK - (LONGEST - 1)) // ATTEND_BLOCK * ATTEND_BLOCK)


def masked_probs(scores, first, row_at, key_at):
    scores = scores * HEAD_DIM ** (-0.5)
    places = row_at + lax.broadcasted_iota(jnp.int32, scores.shape, 0)
    others = key_at + lax.broadcasted_iota(jnp.int32, scores.shape, 1)
    scores = jnp.where((others >= first) & (others <= places), scores, MASKED)
    exp_scores = jnp.exp(scores - jnp.max(scores, axis=1, keepdims=True))
    return exp_scores * (1.0 / jnp.sum(exp_scores, axis=1, keepdims=True))


class Unit:
    def __init__(self, head, block):
        self.row_at, self.key_at = block * ATTEND_BLOCK, key_start(block)
        self.rows = slice(self.row_at, self.row_at + ATTEND_BLOCK)
        self.keys = slice(self.key_at, self.row_at + ATTEND_BLOCK)
        self.lanes = slice(head * HEAD_DIM, (head + 1) * HEAD_DIM)


def units_of(rows, width, most):
    units = [
        Unit(head, block)
        for block in range(rows // ATTEND_BLOCK)
        for head in range(width // HEAD_DIM)
    ]
    return [units[at : at + most] for at in range(0, len(units), most)]


def put_rows(ref, lead, row_at, lanes, values, order_ref, groups):
    share = ref.shape[len(lead)] // groups
    step = min(share, values.shape[0])
    for start in range(0, values.shape[0], step):
        group = (row_at + start) // share
        inside = (row_at + start) % share
        at = pl.multiple_of(order_ref[groups + group] * share + inside, step)
        ref[(*lead, pl.ds(at, step), lanes)] = values[start : start + step].astype(ref.dtype)


def attend_kernel(groups, order_ref, query_ref, key_ref, value_ref, first_ref, out_ref):
    for some in units_of(*query_ref.shape[1:], 4):
        scores = [
            dot(query_ref[0, u.rows, u.lanes], key_ref[0, u.keys, u.lanes], NT) for u in some
        ]
        probs = [
            masked_probs(s, first_ref[u.rows, :], u.row_at, u.key_at).astype(LOW)
            for u, s in zip(some, scores)
        ]
        for u, p in zip(some, probs):
            mixed = dot(p, value_ref[0, u.keys, u.lanes])
            put_rows(out_ref, (), u.row_at, u.lanes, mixed, order_ref, groups)


def attend(order, groups, post, first):
    rows, width = post.shape[1:]
    wide = 2 * HEAD_DIM
    member = lambda m: pl.BlockSpec((1, rows, wide), lambda h, o: (m, 0, h))
    return call(
        "attend",
        functools.partial(attend_kernel, groups),
        (post, post, post, first),
        (width // wide,),
        [member(0), member(1), member(2), pl.BlockSpec((rows, 1), lambda h, o: (0, 0))],
        [pl.BlockSpec((rows, wide), lambda h, o: (0, h))],
        [shape((rows, width), LOW)],
        prefetch=(order,),
        flops=4 * rows * rows * width,
        mib=32,
    )[0]


def attend_back_kernel(
    groups,
    order_ref,
    query_ref,
    key_ref,
    value_ref,
    first_ref,
    cos_ref,
    sine_ref,
    magnitude_ref,
    squares_ref,
    low_ref,
    *rest,
):
    pieces, (grad_ref, total_ref, upper_all, heads_grad, key_grad, value_grad, sems) = rest[:-7], rest[-7:]
    rows_all, width = query_ref.shape[1:]
    share = rows_all // groups

    @pl.when(pl.program_id(0) == 0)
    def _():
        copies = []
        for place, piece in enumerate(pieces):
            at = pl.multiple_of(order_ref[place] * share, share)
            copies.append(
                pltpu.make_async_copy(piece, upper_all.at[pl.ds(at, share), :], sems.at[place])
            )
            copies[-1].start()
        for copy in copies:
            copy.wait()

    step = min(512, rows_all)
    for start in range(0, rows_all, step):
        at = slice(start, start + step)
        heads_grad[at, :] = dot(upper_all[at, :], low_ref[0], NT).astype(LOW)
    norm = [jnp.sqrt(squares_ref[m]) for m in range(3)]
    scale = [magnitude_ref[m] / norm[m] for m in range(3)]
    heads = range(0, width, HEAD_DIM)
    totals = [jnp.zeros((1, width), F32) for _ in range(3)]
    filled = set()

    def back(values, rows):
        return values * cos_ref[rows, :] - pltpu.roll(values, HEAD_DIM // 2, 1) * sine_ref[rows, :]

    def add(ref, unit, values):
        for start in range(0, values.shape[0], ATTEND_BLOCK):
            at = unit.key_at + start
            rows = slice(at, at + ATTEND_BLOCK)
            name = (id(ref), at, unit.lanes.start)
            if name in filled:
                ref[rows, unit.lanes] += values[start : start + ATTEND_BLOCK]
            else:
                filled.add(name)
                ref[rows, unit.lanes] = values[start : start + ATTEND_BLOCK]

    def spread(per_head):
        return jnp.concatenate(per_head, axis=1)

    query_totals = [jnp.zeros((1, HEAD_DIM), F32) for _ in heads]
    for some in units_of(rows_all, width, 2):
        scores = [
            dot(query_ref[0, u.rows, u.lanes], key_ref[0, u.keys, u.lanes], NT) for u in some
        ]
        grad_weights = [
            dot(heads_grad[u.rows, u.lanes], value_ref[0, u.keys, u.lanes], NT) for u in some
        ]
        probs = [
            masked_probs(s, first_ref[u.rows, :], u.row_at, u.key_at)
            for u, s in zip(some, scores)
        ]
        grad_scores = [
            (p * (g - jnp.sum(p * g, axis=1, keepdims=True))).astype(LOW)
            for p, g in zip(probs, grad_weights)
        ]
        for u, p, g in zip(some, probs, grad_scores):
            add(value_grad, u, dot(p.astype(LOW), heads_grad[u.rows, u.lanes], TN))
            add(key_grad, u, dot(g, query_ref[0, u.rows, u.lanes], TN))
        for u, g in zip(some, grad_scores):
            grad = back(dot(g, key_ref[0, u.keys, u.lanes]) * HEAD_DIM ** (-0.5), u.rows)
            head = u.lanes.start // HEAD_DIM
            post = back(query_ref[0, u.rows, u.lanes].astype(F32), u.rows)
            query_totals[head] = query_totals[head] + jnp.sum(grad * post, axis=0, keepdims=True)
            put_rows(grad_ref, (0,), u.row_at, u.lanes, grad * scale[0][:, u.lanes], order_ref, groups)
    totals[0] = spread(query_totals)
    for row_at in range(0, rows_all, ATTEND_BLOCK):
        rows = slice(row_at, row_at + ATTEND_BLOCK)
        for head in heads:
            lanes = slice(head, head + HEAD_DIM)
            grad = back(key_grad[rows, lanes] * HEAD_DIM ** (-0.5), rows)
            post = back(key_ref[0, rows, lanes].astype(F32), rows)
            part = jnp.sum(grad * post, axis=0, keepdims=True)
            query_totals[head // HEAD_DIM] = part if row_at == 0 else query_totals[head // HEAD_DIM] + part
            put_rows(grad_ref, (1,), row_at, lanes, grad * scale[1][:, lanes], order_ref, groups)
        grad = value_grad[rows, :]
        totals[2] = totals[2] + jnp.sum(grad * value_ref[0, rows, :].astype(F32), axis=0, keepdims=True)
        put_rows(grad_ref, (2,), row_at, slice(0, width), grad * scale[2], order_ref, groups)
    totals[1] = spread(query_totals)
    for m in range(3):
        total_ref[m] = totals[m] / scale[m]


def attend_back(order, groups, post, first, cos_table, sine_table, magnitude, squares, low, pieces):
    rows, width = post.shape[1:]
    depth = low.shape[2]
    wide = 2 * HEAD_DIM
    member = lambda m: pl.BlockSpec((1, rows, wide), lambda h, o: (m, 0, h))
    table = pl.BlockSpec((rows, HEAD_DIM), lambda h, o: (0, 0))
    column = pl.BlockSpec((3, 1, wide), lambda h, o: (0, 0, h))
    return call(
        "attend_back",
        functools.partial(attend_back_kernel, groups),
        (post, post, post, first, cos_table, sine_table, magnitude, squares, low, *pieces),
        (width // wide,),
        [
            member(0),
            member(1),
            member(2),
            pl.BlockSpec((rows, 1), lambda h, o: (0, 0)),
            table,
            table,
            column,
            column,
            pl.BlockSpec((1, wide, depth), lambda h, o: (0, h, 0)),
            *[pl.BlockSpec(memory_space=pl.ANY) for _ in pieces],
        ],
        [pl.BlockSpec((3, rows, wide), lambda h, o: (0, 0, h)), column],
        [shape((3, rows, width), LOW), shape((3, 1, width), F32)],
        scratch=[
            pltpu.VMEM((rows, depth), LOW),
            pltpu.VMEM((rows, wide), LOW),
            pltpu.VMEM((rows, wide), F32),
            pltpu.VMEM((rows, wide), F32),
            pltpu.SemaphoreType.DMA((len(pieces),)),
        ],
        prefetch=(order,),
        flops=10 * rows * rows * width + 2 * rows * width * depth,
        mib=48,
    )


def pair_kernel(dims, n_totals, *refs):
    if n_totals is None:
        value_ref, weight_ref, send_ref, keep_ref = refs
    elif n_totals == 0:
        value_ref, weight_ref, left_ref, send_ref, keep_ref, extra_ref, rows_all = refs
    else:
        value_ref, weight_ref, right_ref, squares_ref, magnitude_ref = refs[:5]
        totals = refs[5 : 5 + n_totals]
        send_ref, keep_ref, extra_ref, rows_all = refs[5 + n_totals :]
    members, _, share, inner = value_ref.shape
    both = CORES * share
    if n_totals is not None:

        @pl.when(pl.program_id(0) == 0)
        def _():
            if n_totals > 0:
                weight = norm_weight(sum_refs(totals), squares_ref[...], magnitude_ref[...])
            for m in range(members):
                rows_all[m, :both, :] = value_ref[m].reshape(both, inner)
                if n_totals == 0:
                    rows_all[m, both:, :] = left_ref[m, : rows_all.shape[1] - both, :]
                else:
                    rows_all[m, both:, :] = (right_ref[m] * weight[m]).astype(LOW)

    total = None
    for m in range(members):
        rows = value_ref[m].reshape(both, inner) if n_totals is None else rows_all[m]
        part = dot(rows, weight_ref[m], dims)
        if n_totals is not None:
            extra_ref[m] = part[both:]
            part = part[:both]
        total = part if total is None else total + part
    send_ref[...] = total[:share].astype(send_ref.dtype)
    keep_ref[...] = total[share:]


def pair_product(name, values, weights, dims, step, left_rows=None, correction=None):
    members, _, share, inner = values.shape
    width = weights.shape[2] if dims is NN else weights.shape[1]
    wide = tile_of(width, 512)
    if dims is NN:
        weight_spec = pl.BlockSpec((members, inner, wide), lambda n: (0, 0, n))
    else:
        weight_spec = pl.BlockSpec((members, wide, inner), lambda n: (0, n, 0))
    out = pl.BlockSpec((share, wide), lambda n: (0, n))
    out_specs, out_shape = [out, out], [shape((share, width), LOW), shape((share, width), F32)]
    extra, n_totals, rank, scratch = (), None, 0, []
    if left_rows is not None:
        extra, n_totals, rank = (left_rows,), 0, left_rows.shape[1] // 2
    if correction is not None:
        right, squares, magnitude, totals = correction
        extra, n_totals, rank = (right, squares, magnitude, *totals), len(totals), right.shape[1]
    if n_totals is not None:
        out_specs.append(pl.BlockSpec((members, rank, wide), lambda n: (0, 0, n)))
        out_shape.append(shape((members, rank, width), F32))
        scratch = [pltpu.VMEM((members, CORES * share + rank, inner), LOW)]
    return call(
        name,
        functools.partial(pair_kernel, dims, n_totals),
        (values, weights, *extra),
        (width // wide,),
        [pl.BlockSpec((members, CORES, share, inner), lambda n: (0, step, 0, 0)), weight_spec]
        + [pl.BlockSpec(v.shape, lambda n: (0, 0, 0)) for v in extra],
        out_specs,
        out_shape,
        scratch=scratch,
        flops=4 * members * share * inner * width,
    )


def shrink_kernel(order_ref, value_ref, weight_ref, left_ref, other_ref, mine_ref, *rest):
    send_ref, keep_ref, total_ref, across_ref, rows_all = rest
    _, _, share, inner = value_ref.shape
    both = CORES * share

    @pl.when(pl.program_id(0) == 0)
    def _():
        rows_all[:both, :] = value_ref[0].reshape(both, inner)
        rows_all[both:, :] = left_ref[0, : rows_all.shape[0] - both, :]

    result = dot(rows_all[...], weight_ref[0])
    across_ref[0] = result[both:]
    total = jnp.zeros((1, weight_ref.shape[2]), F32)
    for pre, cot_ref, target in (
        (result[:share], other_ref, send_ref),
        (result[share:both], mine_ref, keep_ref),
    ):
        target[...] = pre.astype(target.dtype)
        total = total + jnp.sum(pre * cot_ref[...].astype(F32), axis=0, keepdims=True)
    total_ref[...] = total


def shrink_product(order, values, weights, left_rows, cotangent, step):
    _, _, share, inner = values.shape
    width = weights.shape[2]
    rank = left_rows.shape[1] // 2
    wide = tile_of(width, 512)
    out = pl.BlockSpec((share, wide), lambda n, o: (0, n))
    cot = lambda place: pl.BlockSpec((share, wide), lambda n, o: (o[place], n))
    return call(
        "shrink_product",
        shrink_kernel,
        (values, weights, left_rows, cotangent, cotangent),
        (width // wide,),
        [
            pl.BlockSpec((1, CORES, share, inner), lambda n, o: (0, 0, 0, 0)),
            pl.BlockSpec((1, inner, wide), lambda n, o: (0, 0, n)),
            pl.BlockSpec(left_rows.shape, lambda n, o: (0, 0, 0)),
            cot(CORES * step),
            cot(CORES * step + 1),
        ],
        [
            out,
            out,
            pl.BlockSpec((1, wide), lambda n, o: (0, n)),
            pl.BlockSpec((1, rank, wide), lambda n, o: (0, 0, n)),
        ],
        [
            shape((share, width), LOW),
            shape((share, width), F32),
            shape((1, width), F32),
            shape((1, rank, width), F32),
        ],
        scratch=[pltpu.VMEM((CORES * share + rank, inner), LOW)],
        prefetch=(order,),
        flops=4 * share * inner * width,
    )


def row_call(name, kernel, given, whole, out_kinds, sums):
    share, width = given[0].shape
    step = tile_of(share, 64)
    line = pl.BlockSpec((1, width), lambda i: (0, 0))
    return call(
        name,
        functools.partial(kernel, len(given)),
        (*given, *whole),
        (share // step,),
        [pl.BlockSpec(memory_space=pltpu.VMEM) for _ in given] + [line for _ in whole],
        [pl.BlockSpec((step, width), lambda i: (i, 0)) for _ in out_kinds]
        + [line for _ in range(sums)],
        [shape((share, width), kind) for kind in out_kinds]
        + [shape((1, width), F32) for _ in range(sums)],
        flops=20 * share * width,
        mib=16,
    )


def now(ref):
    step = tile_of(ref.shape[0], 64)
    return ref[pl.ds(pl.multiple_of(pl.program_id(0) * step, step), step), :].astype(F32)


def sum_parts(refs):
    total = now(refs[0])
    for ref in refs[1:]:
        total = total + now(ref)
    return total


def add_column(ref, values):
    part = jnp.sum(values, axis=0, keepdims=True)

    @pl.when(pl.program_id(0) == 0)
    def _():
        ref[...] = part

    @pl.when(pl.program_id(0) > 0)
    def _():
        ref[...] += part


def hidden_kernel(count, *refs):
    given, (squares_ref, magnitude_ref, gain_ref, pre_ref, hidden_ref, normed_ref) = refs[:count], refs[count:]
    pre = sum_parts(given[1:])
    hidden = now(given[0]) + pre * (magnitude_ref[...] / jnp.sqrt(squares_ref[...]))
    pre_ref[...] = pre
    hidden_ref[...] = hidden
    normed_ref[...] = (hidden * rms_rows(hidden) * gain_ref[...]).astype(LOW)


def mixed_kernel(count, *refs):
    given, (squares_ref, magnitude_ref, mixed_ref) = refs[:count], refs[count:]
    scale = magnitude_ref[...] / jnp.sqrt(squares_ref[...])
    mixed_ref[...] = (now(given[0]) + sum_parts(given[1:]) * scale).astype(LOW)


def norm_back(grad_normed, values, gain):
    factor = rms_rows(values)
    scaled = grad_normed * gain
    inner = jnp.mean(scaled * values, axis=1, keepdims=True)
    back = factor * scaled - values * (factor * factor * factor * inner)
    return back, grad_normed * values * factor


def hidden_back_kernel(count, *refs):
    given, rest = refs[:count], refs[count:]
    squares_ref, magnitude_ref, gain_ref, grad_ref, low_ref, total_ref, gain_grad_ref = rest
    cot_ref, hidden_ref, pre_ref = given[:3]
    back, gain_terms = norm_back(sum_parts(given[3:]), now(hidden_ref), gain_ref[...])
    grad = now(cot_ref) + back
    grad_ref[...] = grad
    scale = magnitude_ref[...] / jnp.sqrt(squares_ref[...])
    low_ref[...] = (grad * scale).astype(LOW)
    add_column(total_ref, grad * now(pre_ref))
    add_column(gain_grad_ref, gain_terms)


def token_back_kernel(count, *refs):
    given, (gain_ref, out_ref, gain_grad_ref) = refs[:count], refs[count:]
    back, gain_terms = norm_back(sum_parts(given[2:]), now(given[0]), gain_ref[...])
    out_ref[...] = now(given[1]) + back
    add_column(gain_grad_ref, gain_terms)


def shrink_back_kernel(order_ref, cot_ref, low_ref, squares_ref, magnitude_ref, product_ref, grad_ref):
    scale = magnitude_ref[0] / jnp.sqrt(squares_ref[0])
    grad = (cot_ref[...].astype(F32) * scale).astype(LOW)
    grad_ref[0] = grad
    product_ref[0] = dot(grad, low_ref[0], NT)


def shrink_back(order, cotangent, low, squares, magnitude, groups):
    rows, width = cotangent.shape
    share, inner = rows // groups, low.shape[1]
    line = pl.BlockSpec((1, 1, width), lambda j, o: (0, 0, 0))
    return call(
        "shrink_back",
        shrink_back_kernel,
        (cotangent, low, squares, magnitude),
        (groups,),
        [
            pl.BlockSpec((share, width), lambda j, o: (o[j], 0)),
            pl.BlockSpec((1, inner, width), lambda j, o: (0, 0, 0)),
            line,
            line,
        ],
        [
            pl.BlockSpec((1, share, inner), lambda j, o: (j, 0, 0)),
            pl.BlockSpec((1, share, width), lambda j, o: (j, 0, 0)),
        ],
        [shape((groups, share, inner), F32), shape((groups, share, width), LOW)],
        prefetch=(order,),
        flops=2 * rows * width * inner,
        mib=32,
    )


def expand_kernel(
    other_ref,
    mine_ref,
    low_ref,
    squares_ref,
    magnitude_ref,
    grad_ref,
    left_ref,
    product_ref,
    back_ref,
    total_ref,
    rows_ref,
    across_ref,
    rows_all,
):
    share = other_ref.shape[0]
    both, rank = CORES * share, across_ref.shape[1]

    @pl.when(pl.program_id(0) == 0)
    def _():
        for at, ref in ((0, other_ref), (share, mine_ref)):
            rows_ref[at : at + share, :] = ref[...]
            rows_all[at : at + share, :] = ref[...]
        for m in range(2):
            rows_all[both + m * rank : both + (m + 1) * rank, :] = left_ref[m, :rank, :]

    scale = [magnitude_ref[m] / jnp.sqrt(squares_ref[m]) for m in range(2)]
    width = low_ref.shape[2]
    totals = [jnp.zeros((1, width), F32) for _ in range(2)]
    if width % 128 == 0:
        pre = dot(rows_all[...], jnp.concatenate([low_ref[0], low_ref[1]], axis=1))
        gate_all, up_all = pre[:, :width], pre[:, width:]
    else:
        gate_all, up_all = (dot(rows_all[...], low_ref[m]) for m in range(2))
    across_ref[0] = gate_all[both : both + rank]
    across_ref[1] = up_all[both + rank :]
    for place in range(CORES):
        rows = slice(place * share, (place + 1) * share)
        gate_pre, up_pre = gate_all[rows], up_all[rows]
        gate, up = gate_pre * scale[0], up_pre * scale[1]
        sigmoid = 0.5 + 0.5 * jnp.tanh(0.5 * gate)
        active = gate * sigmoid
        product_ref[0, place] = (active * up).astype(LOW)
        upper = grad_ref[place]
        grad_up = upper * active
        grad_gate = upper * up * sigmoid * (1.0 + gate * (1.0 - sigmoid))
        totals[0] += jnp.sum(grad_gate * gate_pre, axis=0, keepdims=True)
        totals[1] += jnp.sum(grad_up * up_pre, axis=0, keepdims=True)
        back_ref[0, place] = (grad_gate * scale[0]).astype(LOW)
        back_ref[1, place] = (grad_up * scale[1]).astype(LOW)
    for m in range(2):
        total_ref[m] = totals[m]


def expand(pieces, low, squares, magnitude, grad_product, left_rows, step):
    share, depth = pieces[0].shape
    width = low.shape[2]
    rank = left_rows.shape[1] // 2
    wide = tile_of(width, 128)
    piece = pl.BlockSpec((share, depth), lambda n: (0, 0))
    column = pl.BlockSpec((2, 1, wide), lambda n: (0, 0, n))
    return call(
        "expand",
        expand_kernel,
        (*pieces, low, squares, magnitude, grad_product, left_rows),
        (width // wide,),
        [
            piece,
            piece,
            pl.BlockSpec((2, depth, wide), lambda n: (0, 0, n)),
            column,
            column,
            pl.BlockSpec((2, share, wide), lambda n: (step, 0, n)),
            pl.BlockSpec(left_rows.shape, lambda n: (0, 0, 0)),
        ],
        [
            pl.BlockSpec((1, 2, share, wide), lambda n: (0, 0, 0, n)),
            pl.BlockSpec((2, 2, share, wide), lambda n: (0, 0, 0, n)),
            column,
            pl.BlockSpec((CORES * share, depth), lambda n: (0, 0)),
            pl.BlockSpec((2, rank, wide), lambda n: (0, 0, n)),
        ],
        [
            shape((1, 2, share, width), LOW),
            shape((2, 2, share, width), LOW),
            shape((2, 1, width), F32),
            shape((CORES * share, depth), LOW),
            shape((2, rank, width), F32),
        ],
        scratch=[pltpu.VMEM((CORES * share + 2 * rank, depth), LOW)],
        flops=8 * share * depth * width,
    )


def adapter_kernel(views, n_inputs, n_grads, n_totals, has_low, order_ref, *refs):
    inputs, grads = refs[:n_inputs], refs[n_inputs : n_inputs + n_grads]
    rest = refs[n_inputs + n_grads :]
    back_ref, across_ref, left_ref, right_ref, squares_ref, magnitude_ref = rest[:6]
    totals, (left_out, right_out, magnitude_out) = rest[6 : 6 + n_totals], rest[6 + n_totals :]
    members, rank, _ = right_ref.shape
    total = sum_refs(totals)
    weight = norm_weight(total, squares_ref[...], magnitude_ref[...])
    magnitude_out[...] = total / jnp.sqrt(squares_ref[...])
    left_rows = left_ref[...].reshape(members * 2 * rank, -1)
    right_rows = [split_rows(right_ref[m]) for m in range(members)]
    for m in range(members):
        if has_low:
            left_out[m] = -fold(dot(split_rows(right_ref[m] * weight[m]), back_ref[m], NT))
        else:
            left_out[m] = -back_ref[m]
        right_out[m] = -(across_ref[m] * weight[m])
    for taken, grads_of in views(order_ref, inputs, grads):
        across = dot(left_rows, taken, NT)
        downs = []
        for m in range(members):
            grad = grads_of(m)
            mine = split_rows(fold(across[2 * rank * m : 2 * rank * (m + 1)]))
            right_out[m] += fold(dot(mine, grad))
            downs.append(split_rows(fold(dot(right_rows[m], grad, NT))))
        left = dot(jnp.concatenate(downs, axis=0), taken)
        for m in range(members):
            left_out[m] += fold(left[2 * rank * m : 2 * rank * (m + 1)])
    for m in range(members):
        left_out[m] = ADAPT_SCALE * left_out[m]
        right_out[m] = ADAPT_SCALE * right_out[m]


def adapter(name, order, views, inputs, grads, back, across, left_rows, right, totals, squares, magnitude):
    members, rank, width = right.shape
    depth = left_rows.shape[2]
    operands = (*inputs, *grads, back, across, left_rows, right, squares, magnitude, *totals)
    full = lambda dims: pl.BlockSpec(tuple(dims), lambda i, o: (0,) * len(dims))
    outs = [(members, rank, depth), (members, rank, width), (members, 1, width)]
    rows = sum(v.size // v.shape[-1] for v in inputs)
    return call(
        name,
        functools.partial(
            adapter_kernel, views, len(inputs), len(grads), len(totals), back.dtype == LOW
        ),
        operands,
        (1,),
        [full(v.shape) for v in operands],
        [full(dims) for dims in outs],
        [shape(dims, F32) for dims in outs],
        prefetch=(order,),
        flops=8 * members * rows * width * 32,
        mib=40,
    )


MESH_IDS = pl.DeviceIdType.MESH


def copy_kernel(count, *refs):
    for source, target in zip(refs[:count], refs[count:]):
        target[...] = source[...]


def copy_out(arrays):
    vmem = pl.BlockSpec(memory_space=pltpu.VMEM)
    full = lambda v: pl.BlockSpec(v.shape, lambda i: (0,) * v.ndim)
    return call(
        "copy_out",
        functools.partial(copy_kernel, len(arrays)),
        tuple(arrays),
        (1,),
        [vmem for _ in arrays],
        [full(v) for v in arrays],
        [shape(v.shape, F32) for v in arrays],
        mib=16,
    )


GRAIN = 16


def pieces_of(width):
    return [(at, min(128, width - at)) for at in range(0, width, 128)]


def cells_of(blocks, lines, parts):
    cells, rows = [], []
    for n, block in enumerate(blocks):
        for m in range(block.shape[0]):
            for at, size in pieces_of(block.shape[2] // parts):
                cells.append((n, m, at, size))
    for n, line in enumerate(lines):
        for m in range(line.shape[0]):
            for at, size in pieces_of(line.shape[2] // parts):
                rows.append((n, m, at, size))
    return cells, rows


def pack(blocks, lines, wide_ref, part, parts, cells, rows):
    for i, (n, m, at, size) in enumerate(cells):
        start = part * (blocks[n].shape[2] // parts) + at
        wide_ref[part, i, :, :size] = blocks[n][m, :, start : start + size]
    for i, (n, m, at, size) in enumerate(rows):
        start = part * (lines[n].shape[2] // parts) + at
        cell, row = len(cells) + i // GRAIN, i % GRAIN
        wide_ref[part, cell, row : row + 1, :size] = lines[n][m, :, start : start + size]


def unpack(full_ref, blocks, lines, part, parts, cells, rows):
    for i, (n, m, at, size) in enumerate(cells):
        start = part * (blocks[n].shape[2] // parts) + at
        blocks[n][m, :, start : start + size] = full_ref[part, i].astype(F32)[:, :size]
    for i, (n, m, at, size) in enumerate(rows):
        start = part * (lines[n].shape[2] // parts) + at
        cell, row = len(cells) + i // GRAIN, i % GRAIN
        values = full_ref[part, cell].astype(F32)
        lines[n][m, :, start : start + size] = values[row : row + 1, :size]


def reduce_kernel(groups, lines, counts, *refs):
    n_all, n_all_lines, n_dp, n_dp_lines = counts
    count = sum(counts)
    taken, given, scratch = refs[:count], refs[count : 2 * count], refs[2 * count :]
    ends = [n_all, n_all + n_all_lines, n_all + n_all_lines + n_dp]
    parted = lambda v: (v[: ends[0]], v[ends[0] : ends[1]], v[ends[1] : ends[2]], v[ends[2] :])
    all_in, all_lines_in, dp_in, dp_lines_in = parted(taken)
    all_out, all_lines_out, dp_out, dp_lines_out = parted(given)
    (
        all_ref,
        line_ref,
        all_low,
        line_low,
        all_got,
        part,
        part_low,
        part_got,
        line_got,
        all_full,
        line_full,
        *sems,
    ) = scratch
    me, row = lax.axis_index("mp"), lax.axis_index("dp")
    piece, line_piece = part.shape[0] // lines, line_ref.shape[1] // lines
    mp_peer = [lax.rem(me + k, groups) for k in range(groups)]
    dp_peer = [lax.rem(row + k, lines) for k in range(lines)]
    barrier = pltpu.get_barrier_semaphore()
    for k in range(1, groups):
        pl.semaphore_signal(barrier, 1, device_id={"mp": mp_peer[k]}, device_id_type=MESH_IDS)
    for k in range(1, lines):
        pl.semaphore_signal(barrier, 1, device_id={"dp": dp_peer[k]}, device_id_type=MESH_IDS)
    all_cells = cells_of(all_in, all_lines_in, groups)
    dp_cells = cells_of(dp_in, dp_lines_in, 1)
    all_ref[...] = jnp.zeros_like(all_ref)
    line_ref[...] = jnp.zeros_like(line_ref)
    for q in range(groups):
        pack(all_in, all_lines_in, all_ref, q, groups, *all_cells)
    pack(dp_in, dp_lines_in, line_ref, 0, 1, *dp_cells)
    all_low[...] = all_ref[...].astype(LOW)
    line_low[...] = line_ref[...].astype(LOW)
    pl.semaphore_wait(barrier, groups + lines - 2)

    def send(source, target, stage, k, axis, peer):
        copy = pltpu.make_async_remote_copy(
            src_ref=source,
            dst_ref=target,
            send_sem=sems[2 * stage].at[k],
            recv_sem=sems[2 * stage + 1].at[k],
            device_id={axis: peer},
            device_id_type=MESH_IDS,
        )
        copy.start()
        return copy

    over_mp = [
        send(all_low.at[mp_peer[k]], all_got.at[k], 0, k, "mp", mp_peer[k])
        for k in range(1, groups)
    ]
    over_dp = [
        send(
            line_low.at[0, pl.ds(dp_peer[k] * line_piece, line_piece)],
            line_got.at[k],
            1,
            k,
            "dp",
            dp_peer[k],
        )
        for k in range(1, lines)
    ]
    total = all_ref[me]
    for k, copy in enumerate(over_mp, 1):
        copy.wait_recv()
        total = total + all_got[k].astype(F32)
    part[...] = total
    part_low[...] = total.astype(LOW)
    part_dp = [
        send(part_low.at[pl.ds(dp_peer[k] * piece, piece)], part_got.at[k], 2, k, "dp", dp_peer[k])
        for k in range(1, lines)
    ]
    mine = pl.ds(row * line_piece, line_piece)
    total = line_ref[0, mine]
    for k, copy in enumerate(over_dp, 1):
        copy.wait_recv()
        total = total + line_got[k].astype(F32)
    line_full[0, mine] = total.astype(LOW)
    line_back = [
        send(line_full.at[0, mine], line_full.at[0, mine], 3, k, "dp", dp_peer[k])
        for k in range(1, lines)
    ]
    held = pl.ds(row * piece, piece)
    total = part[held]
    for k, copy in enumerate(part_dp, 1):
        copy.wait_recv()
        total = total + part_got[k].astype(F32)
    all_full[me, held] = total.astype(LOW)
    part_back = [
        send(all_full.at[me, held], all_full.at[me, held], 4, k, "dp", dp_peer[k])
        for k in range(1, lines)
    ]
    for copy in part_back:
        copy.wait_recv()
    all_back = [
        send(all_full.at[me], all_full.at[me], 5, k, "mp", mp_peer[k]) for k in range(1, groups)
    ]
    for copy in line_back:
        copy.wait_recv()
    unpack(line_full, dp_out, dp_lines_out, 0, 1, *dp_cells)
    for copy in all_back:
        copy.wait_recv()
    for q in range(groups):
        unpack(all_full, all_out, all_lines_out, q, groups, *all_cells)
    for copy in over_mp + over_dp + part_dp + line_back + part_back + all_back:
        copy.wait_send()


def reduce_devices(name, identity, over_all, over_all_lines, over_dp, over_dp_lines):
    groups, lines = lax.axis_size("mp"), lax.axis_size("dp")

    def size_of(blocks, rows, parts):
        cells, lines_in = cells_of(blocks, rows, parts)
        size = len(cells) + -(-len(lines_in) // GRAIN)
        return -(-size // lines) * lines

    count, line_count = size_of(over_all, over_all_lines, groups), size_of(over_dp, over_dp_lines, 1)
    operands = (*over_all, *over_all_lines, *over_dp, *over_dp_lines)
    counts = (len(over_all), len(over_all_lines), len(over_dp), len(over_dp_lines))
    vmem = pl.BlockSpec(memory_space=pltpu.VMEM)
    tail = (GRAIN, 128)
    sizes = (groups, lines, lines, lines, lines, groups)
    every, line = (groups, count) + tail, (1, line_count) + tail
    results = pl.pallas_call(
        functools.partial(reduce_kernel, groups, lines, counts),
        name=name,
        out_shape=[shape(v.shape, F32) for v in operands],
        in_specs=[vmem for _ in operands],
        out_specs=[vmem for _ in operands],
        scratch_shapes=[
            pltpu.VMEM(every, F32),
            pltpu.VMEM(line, F32),
            pltpu.VMEM(every, LOW),
            pltpu.VMEM(line, LOW),
            pltpu.VMEM(every, LOW),
            pltpu.VMEM((count,) + tail, F32),
            pltpu.VMEM((count,) + tail, LOW),
            pltpu.VMEM((lines, count // lines) + tail, LOW),
            pltpu.VMEM((lines, line_count // lines) + tail, LOW),
            pltpu.VMEM(every, LOW),
            pltpu.VMEM(line, LOW),
        ]
        + [pltpu.SemaphoreType.DMA((n,)) for n in sizes for _ in range(2)],
        compiler_params=pltpu.CompilerParams(
            collective_id=identity, has_side_effects=True, vmem_limit_bytes=32 * 2**20
        ),
        cost_estimate=pl.CostEstimate(flops=1000, bytes_accessed=50 * 2**20, transcendentals=0),
    )(*operands)
    return copy_out(results)


def geometry(segment):
    length = segment.shape[0]
    places = lax.broadcasted_iota(jnp.int32, (length, length), 0)
    others = lax.broadcasted_iota(jnp.int32, (length, length), 1)
    visible = (segment[:, None] == segment[None, :]) & (others <= places)
    offset = jnp.sum(visible.astype(F32), axis=1) - 1.0
    lane = jnp.arange(HEAD_DIM, dtype=jnp.int32)
    half = (lane % (HEAD_DIM // 2)).astype(F32)
    frequency = jnp.exp(-jnp.log(ROPE_BASE) * 2.0 * half / HEAD_DIM)
    sign = jnp.where(lane < HEAD_DIM // 2, -1.0, 1.0)
    angles = offset[:, None] * frequency[None, :]
    first = jnp.arange(length, dtype=jnp.int32) - offset.astype(jnp.int32)
    return first[:, None], jnp.cos(angles), jnp.sin(angles) * sign[None, :]


def body(
    tokens,
    cotangent,
    segment_ids,
    attend_gain,
    expand_gain,
    heads_base,
    heads_left,
    heads_right,
    heads_magnitude,
    output_base,
    output_left,
    output_right,
    output_magnitude,
    expand_base,
    expand_left,
    expand_right,
    expand_magnitude,
    shrink_base,
    shrink_left,
    shrink_right,
    shrink_magnitude,
):
    groups = lax.axis_size("mp")
    chips = groups // CORES
    index = lax.axis_index("mp")
    chip, core = index // CORES, index % CORES
    rows, width = tokens.shape
    share = rows // groups
    local_heads = heads_base.shape[2]
    device = jnp.arange(groups, dtype=jnp.int32)
    order = jnp.concatenate(
        [
            (chip + device // CORES) % chips * CORES + (core + 1 + device) % CORES,
            (device // CORES + chips - chip) % chips * CORES + (device + CORES - core + 1) % CORES,
        ]
    ).astype(jnp.int32)

    def own(values):
        return lax.dynamic_slice_in_dim(values, index * share, share, 0)

    def tie(*values):
        return lax.optimization_barrier(values)

    def sibling(values):
        return lax.ppermute(
            values, "mp", [(i, i // CORES * CORES + (i + 1) % CORES) for i in range(groups)]
        )

    def to_chip(values, step):
        return lax.ppermute(
            values,
            "mp",
            [((i, ((i // CORES + step) % chips) * CORES + i % CORES)) for i in range(groups)],
        )

    def mp_sum(values):
        values = values + sibling(values)
        total = values
        for step in range(1, chips):
            total = total + to_chip(values, step)
        return total

    def join(product):
        return (product[1] + sibling(product[0]).astype(F32)).astype(LOW)

    def arrive(own):
        return [to_chip(own, chips - step) for step in range(1, chips)]

    def pairs_of(own, near_sibling, arrived):
        return [(near_sibling, own)] + [(sibling(piece), piece) for piece in arrived]

    def in_pairs(order_ref, inputs, grads):
        for taken, grad in zip(inputs, grads):
            yield taken[...], lambda m, grad=grad: grad[m].reshape(-1, grad.shape[-1])

    def in_shrink(order_ref, inputs, grads):
        for step, taken in enumerate(inputs):
            at = slice(CORES * step, CORES * (step + 1))
            yield (
                taken[0].reshape(-1, taken.shape[-1]),
                lambda m, at=at: grads[0][at].reshape(-1, grads[0].shape[-1]),
            )

    def in_output(order_ref, inputs, grads):
        for place, grad in enumerate(grads):
            yield inputs[0][0, place], lambda m, grad=grad: grad[...]

    def in_heads(order_ref, inputs, grads):
        for place in range(groups):
            at = pl.multiple_of(order_ref[place] * share, share)
            rows = slice(place * share, (place + 1) * share)
            yield inputs[0][pl.ds(at, share), :], lambda m, rows=rows: grads[0][m, rows, :]

    heads_rows, output_rows = left_pairs(heads_left), left_pairs(output_left[None])
    expand_rows, shrink_rows = left_pairs(expand_left), left_pairs(shrink_left[None])
    heads_mag, output_mag = heads_magnitude[:, None], output_magnitude[None, None]
    expand_mag, shrink_mag = expand_magnitude[:, None], shrink_magnitude[None, None]
    attend_line, expand_line = attend_gain[None], expand_gain[None]

    output_low, output_part = merge(
        output_base[None], output_rows, output_right[None], output_base.shape[0], 512
    )
    shrink_low, shrink_part = merge(
        shrink_base[None], shrink_rows, shrink_right[None], shrink_base.shape[0], 512
    )
    tokens, output_part, shrink_part = lax.optimization_barrier((tokens, output_part, shrink_part))
    squares = mp_sum(jnp.concatenate([output_part, shrink_part], axis=1))
    output_sq, shrink_sq = squares[:, :1], squares[:, 1:]

    first, cos_table, sine_table = geometry(segment_ids.reshape(-1))
    normed, heads_low, post, heads_sq, heads_across = project_heads(
        tokens,
        attend_line,
        heads_base,
        heads_rows,
        heads_right,
        heads_mag,
        cos_table,
        sine_table,
    )
    heads_out = attend(order, groups, post, first)
    heads_parts = heads_out.reshape(1, groups, share, local_heads)
    output_far = [
        pair_product("output_product", heads_parts, output_low, NN, step)
        for step in range(1, chips)
    ]
    output_near = pair_product("output_product", heads_parts, output_low, NN, 0, output_rows)
    joined = [join(product) for product in output_far]
    joined, expand_rows = tie(joined, expand_rows)
    output_arrived = [to_chip(values, step) for step, values in enumerate(joined, 1)]
    expand_low, expand_sq = merge(expand_base, expand_rows, expand_right, 512, expand_base.shape[2])
    grad_product, shrink_grad = shrink_back(
        order, cotangent, shrink_low, shrink_sq, shrink_mag, groups
    )
    own_tokens, own_cot = own(tokens), own(cotangent)
    output_parts = [output_near[1], sibling(output_near[0]), *output_arrived]
    output_parts, expand_low, grad_product, own_tokens, own_cot = tie(
        output_parts, expand_low, grad_product, own_tokens, own_cot
    )
    output_pre, hidden, normed_own = row_call(
        "hidden",
        hidden_kernel,
        [own_tokens, *output_parts],
        (output_sq[0], output_mag[0], expand_line),
        (F32, F32, LOW),
        0,
    )

    def feed(pieces, step):
        return expand(pieces, expand_low, expand_sq, expand_mag, grad_product, expand_rows, step)

    def mid_product(fed, correction=None):
        return pair_product("mid_product", fed[1], expand_low, NT, 0, correction=correction)

    def shrink_of(fed, step):
        return shrink_product(order, fed[0], shrink_low, shrink_rows, cotangent, step)

    arrived, near_sibling = arrive(normed_own), sibling(normed_own)
    fed = [feed((near_sibling, normed_own), 0)]
    mid_near = mid_product(fed[0])
    arrived, mid_near = tie(arrived, mid_near)
    mid_sibling = sibling(mid_near[0])
    normed_mid = pairs_of(normed_own, near_sibling, arrived)
    fed += [feed(normed_mid[step], step) for step in range(1, chips)]
    expand_totals = [f[2] for f in fed]
    mid_far = [mid_product(f) for f in fed[1:-1]]
    mid_far.append(mid_product(fed[-1], (expand_right, expand_sq, expand_mag, expand_totals)))
    joined = [join(product) for product in mid_far]
    shrink_inputs = [f[0] for f in fed]
    joined, shrink_rows = tie(joined, shrink_rows)
    mid_arrived = [to_chip(values, step) for step, values in enumerate(joined, 1)]
    shrunk = [shrink_of(f, step) for step, f in enumerate(fed)]
    shrink_total = mp_sum(functools.reduce(jnp.add, [piece[2] for piece in shrunk]))
    shrink_joined = [join(product) for product in shrunk[1:]]
    expand_adapter = adapter(
        "expand_adapter",
        order,
        in_pairs,
        [f[3] for f in fed],
        [f[1] for f in fed],
        mid_far[-1][2],
        fed[0][4],
        expand_rows,
        expand_right,
        expand_totals,
        expand_sq,
        expand_mag,
    )
    mid_parts = [mid_near[1], mid_sibling, *mid_arrived]
    mid_parts, shrunk, shrink_joined, expand_adapter = tie(
        mid_parts, shrunk, shrink_joined, expand_adapter
    )
    grad_hidden, output_grad_own, output_total, expand_gain_part = row_call(
        "hidden_back",
        hidden_back_kernel,
        [own_cot, hidden, output_pre, *mid_parts],
        (output_sq[0], output_mag[0], expand_line),
        (F32, LOW),
        2,
    )
    arrived, near_sibling = arrive(output_grad_own), sibling(output_grad_own)
    output_total = mp_sum(output_total)
    shrink_adapter = adapter(
        "shrink_adapter",
        order,
        in_shrink,
        shrink_inputs,
        [shrink_grad],
        shrink_low,
        shrunk[0][3],
        shrink_rows,
        shrink_right[None],
        [shrink_total[None]],
        shrink_sq,
        shrink_mag,
    )
    early = reduce_devices(
        "reduce_early",
        1,
        [expand_adapter[0], shrink_adapter[1]],
        [expand_gain_part[None]],
        [expand_adapter[1], shrink_adapter[0]],
        [expand_adapter[2], shrink_adapter[2]],
    )
    arrived, near_sibling, output_total, shrink_joined, early = tie(
        arrived, near_sibling, output_total, shrink_joined, early
    )
    expand_left_grad, shrink_right_grad, expand_gain_grad = early[:3]
    expand_right_grad, shrink_left_grad, expand_mag_grad, shrink_mag_grad = early[3:]
    output_grad = [
        piece for pair in pairs_of(output_grad_own, near_sibling, arrived) for piece in pair
    ]
    shrink_parts = [shrunk[0][1], sibling(shrunk[0][0])] + [
        to_chip(values, step) for step, values in enumerate(shrink_joined, 1)
    ]
    heads_grads, heads_total = attend_back(
        order,
        groups,
        post,
        first,
        cos_table,
        sine_table,
        heads_mag,
        heads_sq,
        output_low,
        output_grad,
    )
    grad_parts = heads_grads.reshape(3, groups, share, local_heads)
    token_far = [
        pair_product("normed_product", grad_parts, heads_low, NT, step)
        for step in range(1, chips)
    ]
    joined = [join(product) for product in token_far]
    token_near = pair_product(
        "normed_product",
        grad_parts,
        heads_low,
        NT,
        0,
        correction=(heads_right, heads_sq, heads_mag, [heads_total]),
    )
    joined, heads_rows, output_rows = tie(joined, heads_rows, output_rows)
    token_arrived = [to_chip(values, step) for step, values in enumerate(joined, 1)]
    output_adapter = adapter(
        "output_adapter",
        order,
        in_output,
        [heads_parts],
        output_grad,
        output_low,
        output_near[2],
        output_rows,
        output_right[None],
        [output_total[None]],
        output_sq,
        output_mag,
    )
    heads_adapter = adapter(
        "heads_adapter",
        order,
        in_heads,
        [normed],
        [heads_grads],
        token_near[2],
        heads_across,
        heads_rows,
        heads_right,
        [heads_total],
        heads_sq,
        heads_mag,
    )
    (mixed,) = row_call(
        "mixed", mixed_kernel, [hidden, *shrink_parts], (shrink_sq[0], shrink_mag[0]), (LOW,), 0
    )
    token_parts = [token_near[1], sibling(token_near[0]), *token_arrived]
    token_parts, output_adapter, heads_adapter, mixed = tie(
        token_parts, output_adapter, heads_adapter, mixed
    )
    grad_tokens, attend_gain_part = row_call(
        "token_back",
        token_back_kernel,
        [own_tokens, grad_hidden, *token_parts],
        (attend_line,),
        (F32,),
        1,
    )
    late = reduce_devices(
        "reduce_late",
        2,
        [heads_adapter[0], output_adapter[1]],
        [attend_gain_part[None]],
        [heads_adapter[1], output_adapter[0]],
        [heads_adapter[2], output_adapter[2]],
    )
    heads_left_grad, output_right_grad, attend_gain_grad = late[:3]
    heads_right_grad, output_left_grad, heads_mag_grad, output_mag_grad = late[3:]
    return (
        mixed,
        grad_tokens,
        attend_gain_grad[0, 0],
        expand_gain_grad[0, 0],
        jnp.swapaxes(heads_left_grad, 1, 2),
        heads_right_grad,
        heads_mag_grad[:, 0],
        output_left_grad[0].T,
        output_right_grad[0],
        output_mag_grad[0, 0],
        jnp.swapaxes(expand_left_grad, 1, 2),
        expand_right_grad,
        expand_mag_grad[:, 0],
        shrink_left_grad[0].T,
        shrink_right_grad[0],
        shrink_mag_grad[0, 0],
    )


def solution(mesh):
    placed = (
        P("dp", None),
        P("dp", None),
        P("dp", None),
        P(),
        P(),
        P(None, None, "mp"),
        P(),
        P(None, None, "mp"),
        P(None, "mp"),
        P("mp", None),
        P("mp", None),
        P(),
        P(),
        P(None, None, "mp"),
        P(),
        P(None, None, "mp"),
        P(None, "mp"),
        P("mp", None),
        P("mp", None),
        P(),
        P(),
    )
    return jax.shard_map(
        body,
        mesh=mesh,
        in_specs=placed,
        out_specs=(
            P(("dp", "mp"), None),
            P(("dp", "mp"), None),
            P(),
            P(),
            P(),
            P(None, None, "mp"),
            P(None, "mp"),
            P("mp", None),
            P(),
            P(),
            P(),
            P(None, None, "mp"),
            P(None, "mp"),
            P("mp", None),
            P(),
            P(),
        ),
        check_vma=False,
    )
```

```python
import functools

import jax
import jax.numpy as jnp
from jax import lax
from jax.experimental import pallas as pl
from jax.experimental.pallas import tpu as pltpu
from jax.sharding import PartitionSpec as P

HEAD_DIM = 128
CORES = 2
LONGEST = 512
ATTEND_BLOCK = 256
ADAPT_SCALE = 2.0
NORM_EPS = 1e-05
ROPE_BASE = 10000.0
MASKED = -1e30

F32 = jnp.float32
LOW = jnp.bfloat16
NN = (((1,), (0,)), ((), ()))
NT = (((1,), (1,)), ((), ()))
TN = (((0,), (0,)), ((), ()))


def dot(left, right, dims=NN):
    return lax.dot_general(left, right, dims, preferred_element_type=F32)


def shape(dims, kind):
    return jax.ShapeDtypeStruct(tuple(dims), kind)


def call(name, kernel, operands, grid, in_specs, out_specs, out_shape, scratch=(), prefetch=(), flops=0, mib=60):
    moved = sum(v.size * v.dtype.itemsize for v in operands)
    moved += sum(v.size * v.dtype.itemsize for v in out_shape)
    return pl.pallas_call(
        kernel,
        name=name,
        out_shape=out_shape,
        grid_spec=pltpu.PrefetchScalarGridSpec(
            num_scalar_prefetch=len(prefetch),
            grid=grid,
            in_specs=in_specs,
            out_specs=out_specs,
            scratch_shapes=scratch,
        ),
        compiler_params=pltpu.CompilerParams(vmem_limit_bytes=mib * 2**20),
        cost_estimate=pl.CostEstimate(flops=flops // 16, bytes_accessed=moved // 16, transcendentals=0),
    )(*prefetch, *operands)


def tile_of(size, most):
    return most if size % most == 0 else size


def split_rows(values):
    top = values.astype(LOW)
    rest = (values - top.astype(F32)).astype(LOW)
    return jnp.concatenate([top, rest], axis=0)


def left_pairs(left_map):
    turned = jnp.swapaxes(left_map, -1, -2)
    top = lax.reduce_precision(turned, 8, 7)
    return jnp.concatenate([top, turned - top], axis=-2).astype(LOW)


def norm_weight(total, squares, magnitude):
    norm = jnp.sqrt(squares)
    return total * magnitude / (norm * norm * norm)


def sum_refs(refs):
    total = refs[0][...]
    for ref in refs[1:]:
        total = total + ref[...]
    return total


def fold(values):
    half = values.shape[0] // 2
    return values[:half] + values[half:]


def merge_tile(base_at, low_put, left_rows, right, depth):
    rank = right.shape[0]
    doubled = ADAPT_SCALE * right
    top = doubled.astype(LOW)
    rest = (doubled - top.astype(F32)).astype(LOW)
    right_stack = jnp.concatenate([top, rest, top], axis=0)
    left_stack = jnp.concatenate([left_rows[:rank], left_rows[:rank], left_rows[rank:]], axis=0)
    squares = jnp.zeros((1, right.shape[1]), F32)
    step = tile_of(depth, 1024)
    for start in range(0, depth, step):
        merged = base_at(start, step).astype(F32) + dot(
            left_stack[:, start : start + step], right_stack, TN
        )
        low_put(start, step, merged.astype(LOW))
        squares = squares + jnp.sum(merged * merged, axis=0, keepdims=True)
    return squares


def merge_kernel(base_ref, left_ref, right_ref, low_ref, squares_ref):
    depth, width = base_ref.shape[1:]
    if low_ref.shape[1] > depth:
        low_ref[0, depth:, :] = jnp.zeros((low_ref.shape[1] - depth, low_ref.shape[2]), LOW)
    if low_ref.shape[2] > width:
        spare = low_ref.shape[2] - width
        low_ref[0, :, width:] = jnp.zeros((low_ref.shape[1], spare), LOW)
        squares_ref[0, :, width:] = jnp.ones((1, spare), F32)

    def put(start, step, tile):
        low_ref[0, start : start + step, :width] = tile

    squares = merge_tile(
        lambda start, step: base_ref[0, start : start + step, :],
        put,
        left_ref[0],
        right_ref[0],
        depth,
    )

    @pl.when(pl.program_id(2) == 0)
    def _():
        squares_ref[0, :, :width] = squares

    @pl.when(pl.program_id(2) > 0)
    def _():
        squares_ref[0, :, :width] += squares


def padded(size):
    return -(-size // 256) * 256


def pad_last(values, size):
    return jnp.pad(values, [(0, 0)] * (values.ndim - 1) + [(0, size - values.shape[-1])])


def merge(base, left_rows, right, deep, wide):
    members, depth, width = base.shape
    low_deep = padded(deep) if deep == depth else deep
    low_wide = padded(wide) if wide == width else wide
    low_shape = (members, depth // deep * low_deep, width // wide * low_wide)
    pairs, rank = left_rows.shape[1], right.shape[1]
    return call(
        "merge",
        merge_kernel,
        (base, left_rows, right),
        (members, width // wide, depth // deep),
        [
            pl.BlockSpec((1, deep, wide), lambda m, n, k: (m, k, n)),
            pl.BlockSpec((1, pairs, deep), lambda m, n, k: (m, 0, k)),
            pl.BlockSpec((1, rank, wide), lambda m, n, k: (m, 0, n)),
        ],
        [
            pl.BlockSpec((1, low_deep, low_wide), lambda m, n, k: (m, k, n)),
            pl.BlockSpec((1, 1, low_wide), lambda m, n, k: (m, 0, n)),
        ],
        [shape(low_shape, LOW), shape((members, 1, low_shape[2]), F32)],
        flops=2 * members * depth * width * 256,
    )


def rms_rows(values):
    return lax.rsqrt(jnp.mean(values * values, axis=1, keepdims=True) + NORM_EPS)


def heads_kernel(
    token_ref,
    gain_ref,
    base_ref,
    left_ref,
    right_ref,
    magnitude_ref,
    cos_ref,
    sine_ref,
    normed_ref,
    low_ref,
    post_ref,
    squares_ref,
    across_ref,
    rows_all,
):
    total_rows = token_ref.shape[0]
    depth, width = base_ref.shape[1:]
    rank = right_ref.shape[1]

    @pl.when((pl.program_id(0) == 0) & (pl.program_id(1) == 0))
    def _():
        step = 128

        def some(i, carry):
            at = pl.ds(pl.multiple_of(i * step, step), step)
            values = token_ref[at, :].astype(F32)
            low = (values * rms_rows(values) * gain_ref[...]).astype(LOW)
            normed_ref[at, :] = low
            rows_all[at, :] = low
            return carry

        lax.fori_loop(0, total_rows // step, some, 0)

    rows_all[total_rows:, :] = left_ref[0, :rank, :]

    def put(start, step, tile):
        low_ref[0, start : start + step, :] = tile

    squares = merge_tile(
        lambda start, step: base_ref[0, start : start + step, :],
        put,
        left_ref[0],
        right_ref[0],
        depth,
    )
    squares_ref[0] = squares
    scale = magnitude_ref[0] / jnp.sqrt(squares)
    low = low_ref[0]
    turning = pl.program_id(0) < 2
    step = min(512, total_rows)
    for start in range(0, total_rows, step):
        last = start + step == total_rows
        rows = slice(start, start + step)
        pre = dot(rows_all[start : start + step + (rank if last else 0), :], low)
        if last:
            across_ref[0] = pre[step:]
        post = pre[:step] * scale
        cos_table = jnp.where(turning, cos_ref[rows, :], 1.0)
        sine_table = jnp.where(turning, sine_ref[rows, :], 0.0)
        for head in range(0, width, HEAD_DIM):
            piece = post[:, head : head + HEAD_DIM]
            turned = pltpu.roll(piece, HEAD_DIM // 2, 1)
            post_ref[0, rows, head : head + HEAD_DIM] = (
                piece * cos_table + turned * sine_table
            ).astype(LOW)


def project_heads(tokens, gain, base, left_rows, right, magnitude, cos_table, sine_table):
    members, depth, width = base.shape
    rows, pairs, rank = tokens.shape[0], left_rows.shape[1], right.shape[1]
    wide = 256
    whole = lambda m, n: (0, 0)
    return call(
        "project_heads",
        heads_kernel,
        (tokens, gain, base, left_rows, right, magnitude, cos_table, sine_table),
        (members, width // wide),
        [
            pl.BlockSpec((rows, depth), whole),
            pl.BlockSpec((1, depth), whole),
            pl.BlockSpec((1, depth, wide), lambda m, n: (m, 0, n)),
            pl.BlockSpec((1, pairs, depth), lambda m, n: (m, 0, 0)),
            pl.BlockSpec((1, rank, wide), lambda m, n: (m, 0, n)),
            pl.BlockSpec((1, 1, wide), lambda m, n: (m, 0, n)),
            pl.BlockSpec((rows, HEAD_DIM), whole),
            pl.BlockSpec((rows, HEAD_DIM), whole),
        ],
        [
            pl.BlockSpec((rows, depth), whole),
            pl.BlockSpec((1, depth, wide), lambda m, n: (m, 0, n)),
            pl.BlockSpec((1, rows, wide), lambda m, n: (m, 0, n)),
            pl.BlockSpec((1, 1, wide), lambda m, n: (m, 0, n)),
            pl.BlockSpec((1, rank, wide), lambda m, n: (m, 0, n)),
        ],
        [
            shape((rows, depth), LOW),
            shape(base.shape, LOW),
            shape((members, rows, width), LOW),
            shape((members, 1, width), F32),
            shape((members, rank, width), F32),
        ],
        scratch=[pltpu.VMEM((rows + rank, depth), LOW)],
        flops=2 * members * rows * depth * width,
    )


def key_start(block):
    return max(0, (block * ATTEND_BLOCK - (LONGEST - 1)) // ATTEND_BLOCK * ATTEND_BLOCK)


def masked_probs(scores, first, row_at, key_at):
    scores = scores * HEAD_DIM ** (-0.5)
    places = row_at + lax.broadcasted_iota(jnp.int32, scores.shape, 0)
    others = key_at + lax.broadcasted_iota(jnp.int32, scores.shape, 1)
    scores = jnp.where((others >= first) & (others <= places), scores, MASKED)
    exp_scores = jnp.exp(scores - jnp.max(scores, axis=1, keepdims=True))
    return exp_scores * (1.0 / jnp.sum(exp_scores, axis=1, keepdims=True))


class Unit:
    def __init__(self, head, block):
        self.row_at, self.key_at = block * ATTEND_BLOCK, key_start(block)
        self.rows = slice(self.row_at, self.row_at + ATTEND_BLOCK)
        self.keys = slice(self.key_at, self.row_at + ATTEND_BLOCK)
        self.lanes = slice(head * HEAD_DIM, (head + 1) * HEAD_DIM)


def units_of(rows, width, most):
    units = [
        Unit(head, block)
        for block in range(rows // ATTEND_BLOCK)
        for head in range(width // HEAD_DIM)
    ]
    return [units[at : at + most] for at in range(0, len(units), most)]


def put_rows(ref, lead, row_at, lanes, values, order_ref, groups):
    share = ref.shape[len(lead)] // groups
    step = min(share, values.shape[0])
    for start in range(0, values.shape[0], step):
        group = (row_at + start) // share
        inside = (row_at + start) % share
        at = pl.multiple_of(order_ref[groups + group] * share + inside, step)
        ref[(*lead, pl.ds(at, step), lanes)] = values[start : start + step].astype(ref.dtype)


def attend_kernel(groups, order_ref, query_ref, key_ref, value_ref, first_ref, out_ref):
    for some in units_of(*query_ref.shape[1:], 4):
        scores = [
            dot(query_ref[0, u.rows, u.lanes], key_ref[0, u.keys, u.lanes], NT) for u in some
        ]
        probs = [
            masked_probs(s, first_ref[u.rows, :], u.row_at, u.key_at).astype(LOW)
            for u, s in zip(some, scores)
        ]
        for u, p in zip(some, probs):
            mixed = dot(p, value_ref[0, u.keys, u.lanes])
            put_rows(out_ref, (), u.row_at, u.lanes, mixed, order_ref, groups)


def attend(order, groups, post, first):
    rows, width = post.shape[1:]
    wide = 2 * HEAD_DIM
    member = lambda m: pl.BlockSpec((1, rows, wide), lambda h, o: (m, 0, h))
    return call(
        "attend",
        functools.partial(attend_kernel, groups),
        (post, post, post, first),
        (width // wide,),
        [member(0), member(1), member(2), pl.BlockSpec((rows, 1), lambda h, o: (0, 0))],
        [pl.BlockSpec((rows, wide), lambda h, o: (0, h))],
        [shape((rows, width), LOW)],
        prefetch=(order,),
        flops=4 * rows * rows * width,
        mib=32,
    )[0]


def attend_back_kernel(
    groups,
    order_ref,
    query_ref,
    key_ref,
    value_ref,
    first_ref,
    cos_ref,
    sine_ref,
    magnitude_ref,
    squares_ref,
    low_ref,
    *rest,
):
    pieces, (grad_ref, total_ref, upper_all, heads_grad, key_grad, value_grad, sems) = rest[:-7], rest[-7:]
    rows_all, width = query_ref.shape[1:]
    share = rows_all // groups

    @pl.when(pl.program_id(0) == 0)
    def _():
        copies = []
        for place, piece in enumerate(pieces):
            at = pl.multiple_of(order_ref[place] * share, share)
            copies.append(
                pltpu.make_async_copy(piece, upper_all.at[pl.ds(at, share), :], sems.at[place])
            )
            copies[-1].start()
        for copy in copies:
            copy.wait()

    step = min(512, rows_all)
    for start in range(0, rows_all, step):
        at = slice(start, start + step)
        heads_grad[at, :] = dot(upper_all[at, :], low_ref[0], NT).astype(LOW)
    norm = [jnp.sqrt(squares_ref[m]) for m in range(3)]
    scale = [magnitude_ref[m] / norm[m] for m in range(3)]
    heads = range(0, width, HEAD_DIM)
    totals = [jnp.zeros((1, width), F32) for _ in range(3)]
    filled = set()

    def back(values, rows):
        return values * cos_ref[rows, :] - pltpu.roll(values, HEAD_DIM // 2, 1) * sine_ref[rows, :]

    def add(ref, unit, values):
        for start in range(0, values.shape[0], ATTEND_BLOCK):
            at = unit.key_at + start
            rows = slice(at, at + ATTEND_BLOCK)
            name = (id(ref), at, unit.lanes.start)
            if name in filled:
                ref[rows, unit.lanes] += values[start : start + ATTEND_BLOCK]
            else:
                filled.add(name)
                ref[rows, unit.lanes] = values[start : start + ATTEND_BLOCK]

    def spread(per_head):
        return jnp.concatenate(per_head, axis=1)

    query_totals = [jnp.zeros((1, HEAD_DIM), F32) for _ in heads]
    for some in units_of(rows_all, width, 2):
        scores = [
            dot(query_ref[0, u.rows, u.lanes], key_ref[0, u.keys, u.lanes], NT) for u in some
        ]
        grad_weights = [
            dot(heads_grad[u.rows, u.lanes], value_ref[0, u.keys, u.lanes], NT) for u in some
        ]
        probs = [
            masked_probs(s, first_ref[u.rows, :], u.row_at, u.key_at)
            for u, s in zip(some, scores)
        ]
        grad_scores = [
            (p * (g - jnp.sum(p * g, axis=1, keepdims=True))).astype(LOW)
            for p, g in zip(probs, grad_weights)
        ]
        for u, p, g in zip(some, probs, grad_scores):
            add(value_grad, u, dot(p.astype(LOW), heads_grad[u.rows, u.lanes], TN))
            add(key_grad, u, dot(g, query_ref[0, u.rows, u.lanes], TN))
        for u, g in zip(some, grad_scores):
            grad = back(dot(g, key_ref[0, u.keys, u.lanes]) * HEAD_DIM ** (-0.5), u.rows)
            head = u.lanes.start // HEAD_DIM
            post = back(query_ref[0, u.rows, u.lanes].astype(F32), u.rows)
            query_totals[head] = query_totals[head] + jnp.sum(grad * post, axis=0, keepdims=True)
            put_rows(grad_ref, (0,), u.row_at, u.lanes, grad * scale[0][:, u.lanes], order_ref, groups)
    totals[0] = spread(query_totals)
    for row_at in range(0, rows_all, ATTEND_BLOCK):
        rows = slice(row_at, row_at + ATTEND_BLOCK)
        for head in heads:
            lanes = slice(head, head + HEAD_DIM)
            grad = back(key_grad[rows, lanes] * HEAD_DIM ** (-0.5), rows)
            post = back(key_ref[0, rows, lanes].astype(F32), rows)
            part = jnp.sum(grad * post, axis=0, keepdims=True)
            query_totals[head // HEAD_DIM] = part if row_at == 0 else query_totals[head // HEAD_DIM] + part
            put_rows(grad_ref, (1,), row_at, lanes, grad * scale[1][:, lanes], order_ref, groups)
        grad = value_grad[rows, :]
        totals[2] = totals[2] + jnp.sum(grad * value_ref[0, rows, :].astype(F32), axis=0, keepdims=True)
        put_rows(grad_ref, (2,), row_at, slice(0, width), grad * scale[2], order_ref, groups)
    totals[1] = spread(query_totals)
    for m in range(3):
        total_ref[m] = totals[m] / scale[m]


def attend_back(order, groups, post, first, cos_table, sine_table, magnitude, squares, low, pieces):
    rows, width = post.shape[1:]
    depth = low.shape[2]
    wide = 2 * HEAD_DIM
    member = lambda m: pl.BlockSpec((1, rows, wide), lambda h, o: (m, 0, h))
    table = pl.BlockSpec((rows, HEAD_DIM), lambda h, o: (0, 0))
    column = pl.BlockSpec((3, 1, wide), lambda h, o: (0, 0, h))
    return call(
        "attend_back",
        functools.partial(attend_back_kernel, groups),
        (post, post, post, first, cos_table, sine_table, magnitude, squares, low, *pieces),
        (width // wide,),
        [
            member(0),
            member(1),
            member(2),
            pl.BlockSpec((rows, 1), lambda h, o: (0, 0)),
            table,
            table,
            column,
            column,
            pl.BlockSpec((1, wide, depth), lambda h, o: (0, h, 0)),
            *[pl.BlockSpec(memory_space=pl.ANY) for _ in pieces],
        ],
        [pl.BlockSpec((3, rows, wide), lambda h, o: (0, 0, h)), column],
        [shape((3, rows, width), LOW), shape((3, 1, width), F32)],
        scratch=[
            pltpu.VMEM((rows, depth), LOW),
            pltpu.VMEM((rows, wide), LOW),
            pltpu.VMEM((rows, wide), F32),
            pltpu.VMEM((rows, wide), F32),
            pltpu.SemaphoreType.DMA((len(pieces),)),
        ],
        prefetch=(order,),
        flops=10 * rows * rows * width + 2 * rows * width * depth,
        mib=48,
    )


def pair_kernel(dims, n_totals, *refs):
    if n_totals is None:
        value_ref, weight_ref, send_ref, keep_ref = refs
    elif n_totals == 0:
        value_ref, weight_ref, left_ref, send_ref, keep_ref, extra_ref, rows_all = refs
    else:
        value_ref, weight_ref, right_ref, squares_ref, magnitude_ref = refs[:5]
        totals = refs[5 : 5 + n_totals]
        send_ref, keep_ref, extra_ref, rows_all = refs[5 + n_totals :]
    members, _, share, inner = value_ref.shape
    both = CORES * share
    if n_totals is not None:

        @pl.when(pl.program_id(0) == 0)
        def _():
            if n_totals > 0:
                weight = norm_weight(sum_refs(totals), squares_ref[...], magnitude_ref[...])
            for m in range(members):
                rows_all[m, :both, :] = value_ref[m].reshape(both, inner)
                if n_totals == 0:
                    rows_all[m, both:, :] = left_ref[m, : rows_all.shape[1] - both, :]
                else:
                    rows_all[m, both:, :] = (right_ref[m] * weight[m]).astype(LOW)

    total = None
    for m in range(members):
        rows = value_ref[m].reshape(both, inner) if n_totals is None else rows_all[m]
        part = dot(rows, weight_ref[m], dims)
        if n_totals is not None:
            extra_ref[m] = part[both:]
            part = part[:both]
        total = part if total is None else total + part
    send_ref[...] = total[:share].astype(LOW)
    keep_ref[...] = total[share:].astype(LOW)


def pair_product(name, values, weights, dims, step, left_rows=None, correction=None):
    members, _, share, inner = values.shape
    width = weights.shape[2] if dims is NN else weights.shape[1]
    wide = tile_of(width, 512)
    if dims is NN:
        weight_spec = pl.BlockSpec((members, inner, wide), lambda n: (0, 0, n))
    else:
        weight_spec = pl.BlockSpec((members, wide, inner), lambda n: (0, n, 0))
    out = pl.BlockSpec((share, wide), lambda n: (0, n))
    out_specs, out_shape = [out, out], [shape((share, width), LOW) for _ in range(2)]
    extra, n_totals, rank, scratch = (), None, 0, []
    if left_rows is not None:
        extra, n_totals, rank = (left_rows,), 0, left_rows.shape[1] // 2
    if correction is not None:
        right, squares, magnitude, totals = correction
        extra, n_totals, rank = (right, squares, magnitude, *totals), len(totals), right.shape[1]
    if n_totals is not None:
        out_specs.append(pl.BlockSpec((members, rank, wide), lambda n: (0, 0, n)))
        out_shape.append(shape((members, rank, width), F32))
        scratch = [pltpu.VMEM((members, CORES * share + rank, inner), LOW)]
    return call(
        name,
        functools.partial(pair_kernel, dims, n_totals),
        (values, weights, *extra),
        (width // wide,),
        [pl.BlockSpec((members, CORES, share, inner), lambda n: (0, step, 0, 0)), weight_spec]
        + [pl.BlockSpec(v.shape, lambda n: (0, 0, 0)) for v in extra],
        out_specs,
        out_shape,
        scratch=scratch,
        flops=4 * members * share * inner * width,
    )


def shrink_kernel(order_ref, value_ref, weight_ref, left_ref, other_ref, mine_ref, *rest):
    send_ref, keep_ref, total_ref, across_ref, rows_all = rest
    _, _, share, inner = value_ref.shape
    both = CORES * share

    @pl.when(pl.program_id(0) == 0)
    def _():
        rows_all[:both, :] = value_ref[0].reshape(both, inner)
        rows_all[both:, :] = left_ref[0, : rows_all.shape[0] - both, :]

    result = dot(rows_all[...], weight_ref[0])
    across_ref[0] = result[both:]
    total = jnp.zeros((1, weight_ref.shape[2]), F32)
    for pre, cot_ref, target in (
        (result[:share], other_ref, send_ref),
        (result[share:both], mine_ref, keep_ref),
    ):
        target[...] = pre.astype(target.dtype)
        total = total + jnp.sum(pre * cot_ref[...].astype(F32), axis=0, keepdims=True)
    total_ref[...] = total


def shrink_product(order, values, weights, left_rows, cotangent, step):
    _, _, share, inner = values.shape
    width = weights.shape[2]
    rank = left_rows.shape[1] // 2
    wide = tile_of(width, 512)
    out = pl.BlockSpec((share, wide), lambda n, o: (0, n))
    cot = lambda place: pl.BlockSpec((share, wide), lambda n, o: (o[place], n))
    return call(
        "shrink_product",
        shrink_kernel,
        (values, weights, left_rows, cotangent, cotangent),
        (width // wide,),
        [
            pl.BlockSpec((1, CORES, share, inner), lambda n, o: (0, 0, 0, 0)),
            pl.BlockSpec((1, inner, wide), lambda n, o: (0, 0, n)),
            pl.BlockSpec(left_rows.shape, lambda n, o: (0, 0, 0)),
            cot(CORES * step),
            cot(CORES * step + 1),
        ],
        [
            out,
            out,
            pl.BlockSpec((1, wide), lambda n, o: (0, n)),
            pl.BlockSpec((1, rank, wide), lambda n, o: (0, 0, n)),
        ],
        [
            shape((share, width), LOW),
            shape((share, width), LOW),
            shape((1, width), F32),
            shape((1, rank, width), F32),
        ],
        scratch=[pltpu.VMEM((CORES * share + rank, inner), LOW)],
        prefetch=(order,),
        flops=4 * share * inner * width,
    )


def row_call(name, kernel, given, whole, out_kinds, sums):
    share, width = given[0].shape
    step = tile_of(share, 64)
    line = pl.BlockSpec((1, width), lambda i: (0, 0))
    return call(
        name,
        functools.partial(kernel, len(given)),
        (*given, *whole),
        (share // step,),
        [pl.BlockSpec(memory_space=pltpu.VMEM) for _ in given] + [line for _ in whole],
        [pl.BlockSpec((step, width), lambda i: (i, 0)) for _ in out_kinds]
        + [line for _ in range(sums)],
        [shape((share, width), kind) for kind in out_kinds]
        + [shape((1, width), F32) for _ in range(sums)],
        flops=20 * share * width,
        mib=16,
    )


def now(ref):
    step = tile_of(ref.shape[0], 64)
    return ref[pl.ds(pl.multiple_of(pl.program_id(0) * step, step), step), :].astype(F32)


def sum_parts(refs):
    total = now(refs[0])
    for ref in refs[1:]:
        total = total + now(ref)
    return total


def add_column(ref, values):
    part = jnp.sum(values, axis=0, keepdims=True)

    @pl.when(pl.program_id(0) == 0)
    def _():
        ref[...] = part

    @pl.when(pl.program_id(0) > 0)
    def _():
        ref[...] += part


def hidden_kernel(count, *refs):
    given, (squares_ref, magnitude_ref, gain_ref, hidden_ref, normed_ref) = refs[:count], refs[count:]
    pre = sum_parts(given[1:])
    hidden = now(given[0]) + pre * (magnitude_ref[...] / jnp.sqrt(squares_ref[...]))
    hidden_ref[...] = hidden
    normed_ref[...] = (hidden * rms_rows(hidden) * gain_ref[...]).astype(LOW)


def mixed_kernel(count, *refs):
    given, (squares_ref, magnitude_ref, mixed_ref) = refs[:count], refs[count:]
    scale = magnitude_ref[...] / jnp.sqrt(squares_ref[...])
    mixed_ref[...] = (now(given[0]) + sum_parts(given[1:]) * scale).astype(LOW)


def norm_back(grad_normed, values, gain):
    factor = rms_rows(values)
    scaled = grad_normed * gain
    inner = jnp.mean(scaled * values, axis=1, keepdims=True)
    back = factor * scaled - values * (factor * factor * factor * inner)
    return back, grad_normed * values * factor


def hidden_back_kernel(count, *refs):
    given, rest = refs[:count], refs[count:]
    squares_ref, magnitude_ref, gain_ref, grad_ref, low_ref, total_ref, gain_grad_ref = rest
    cot_ref, token_ref, hidden_ref = given[:3]
    hidden = now(hidden_ref)
    back, gain_terms = norm_back(sum_parts(given[3:]), hidden, gain_ref[...])
    grad = now(cot_ref) + back
    grad_ref[...] = grad
    scale = magnitude_ref[...] / jnp.sqrt(squares_ref[...])
    low_ref[...] = (grad * scale).astype(LOW)
    add_column(total_ref, grad * ((hidden - now(token_ref)) / scale))
    add_column(gain_grad_ref, gain_terms)


def token_back_kernel(count, *refs):
    given, (gain_ref, out_ref, gain_grad_ref) = refs[:count], refs[count:]
    back, gain_terms = norm_back(sum_parts(given[2:]), now(given[0]), gain_ref[...])
    out_ref[...] = now(given[1]) + back
    add_column(gain_grad_ref, gain_terms)


def shrink_back_kernel(order_ref, cot_ref, low_ref, squares_ref, magnitude_ref, product_ref, grad_ref):
    scale = magnitude_ref[0] / jnp.sqrt(squares_ref[0])
    grad = (cot_ref[...].astype(F32) * scale).astype(LOW)
    grad_ref[0] = grad
    product_ref[0] = dot(grad, low_ref[0], NT)


def shrink_back(order, cotangent, low, squares, magnitude, groups):
    rows, width = cotangent.shape
    share, inner = rows // groups, low.shape[1]
    line = pl.BlockSpec((1, 1, width), lambda j, o: (0, 0, 0))
    return call(
        "shrink_back",
        shrink_back_kernel,
        (cotangent, low, squares, magnitude),
        (groups,),
        [
            pl.BlockSpec((share, width), lambda j, o: (o[j], 0)),
            pl.BlockSpec((1, inner, width), lambda j, o: (0, 0, 0)),
            line,
            line,
        ],
        [
            pl.BlockSpec((1, share, inner), lambda j, o: (j, 0, 0)),
            pl.BlockSpec((1, share, width), lambda j, o: (j, 0, 0)),
        ],
        [shape((groups, share, inner), F32), shape((groups, share, width), LOW)],
        prefetch=(order,),
        flops=2 * rows * width * inner,
        mib=32,
    )


def expand_kernel(first, last, n_totals, *refs):
    other_ref, mine_ref, low_ref, squares_ref, magnitude_ref, grad_ref = refs[:6]
    refs = list(refs[6:])
    left_ref = refs.pop(0) if first else None
    right_ref = refs.pop(0) if last else None
    before = [refs.pop(0) for _ in range(n_totals)]
    product_ref, back_ref, total_ref, rows_ref, send_ref, keep_ref = refs[:6]
    refs = refs[6:]
    across_ref = refs.pop(0) if first else None
    extra_ref = refs.pop(0) if last else None
    rows_all, back_all, mid_sum = refs
    share, depth = other_ref.shape
    wide = low_ref.shape[2]
    both = CORES * share

    @pl.when(pl.program_id(0) == 0)
    def _():
        for at, ref in ((0, other_ref), (share, mine_ref)):
            rows_ref[at : at + share, :] = ref[...]
            rows_all[at : at + share, :] = ref[...]
        if first:
            rank = across_ref.shape[1]
            for m in range(2):
                rows_all[both + m * rank : both + (m + 1) * rank, :] = left_ref[m, :rank, :]
        mid_sum[...] = jnp.zeros_like(mid_sum)

    scale = [magnitude_ref[m] / jnp.sqrt(squares_ref[m]) for m in range(2)]
    totals = [jnp.zeros((1, wide), F32) for _ in range(2)]
    pre = [dot(rows_all[...], low_ref[m]) for m in range(2)]
    if first:
        across_ref[0] = pre[0][both : both + rank_of(across_ref)]
        across_ref[1] = pre[1][both + rank_of(across_ref) :]
    for place in range(CORES):
        rows = slice(place * share, (place + 1) * share)
        gate_pre, up_pre = pre[0][rows], pre[1][rows]
        gate, up = gate_pre * scale[0], up_pre * scale[1]
        sigmoid = 0.5 + 0.5 * jnp.tanh(0.5 * gate)
        active = gate * sigmoid
        product_ref[0, place] = (active * up).astype(LOW)
        upper = grad_ref[place]
        grad_up = upper * active
        grad_gate = upper * up * sigmoid * (1.0 + gate * (1.0 - sigmoid))
        totals[0] += jnp.sum(grad_gate * gate_pre, axis=0, keepdims=True)
        totals[1] += jnp.sum(grad_up * up_pre, axis=0, keepdims=True)
        for m, grad in enumerate((grad_gate, grad_up)):
            low = (grad * scale[m]).astype(LOW)
            back_ref[m, place] = low
            back_all[rows, m * wide : (m + 1) * wide] = low
    for m in range(2):
        total_ref[m] = totals[m]
    if last:
        rank = rank_of(extra_ref)
        for m in range(2):
            total = totals[m]
            for ref in before:
                total = total + ref[m]
            weighted = right_ref[m] * norm_weight(total, squares_ref[m], magnitude_ref[m])
            rows = slice(both + m * rank, both + (m + 1) * rank)
            back_all[rows, m * wide : (m + 1) * wide] = weighted.astype(LOW)
            back_all[rows, (1 - m) * wide : (2 - m) * wide] = jnp.zeros((rank, wide), LOW)
    step = tile_of(depth, 512)
    for at in range(0, depth, step):
        columns = slice(at, at + step)
        weights = jnp.concatenate([low_ref[0, columns, :], low_ref[1, columns, :]], axis=1)
        mid_sum[:, columns] += dot(back_all[...], weights, NT)

    @pl.when(pl.program_id(0) == pl.num_programs(0) - 1)
    def _():
        send_ref[...] = mid_sum[:share, :].astype(LOW)
        keep_ref[...] = mid_sum[share:both, :].astype(LOW)
        if last:
            for m in range(2):
                extra_ref[m] = mid_sum[both + m * rank_of(extra_ref) : both + (m + 1) * rank_of(extra_ref), :]


def rank_of(ref):
    return ref.shape[1]


def expand(pieces, low, squares, magnitude, grad_product, step, left_rows=None, right=None, before=()):
    share, depth = pieces[0].shape
    width = low.shape[2]
    first, last = left_rows is not None, right is not None
    wide = 256
    rows = CORES * share
    fixed = lambda dims: pl.BlockSpec(tuple(dims), lambda n: (0,) * len(dims))
    column = pl.BlockSpec((2, 1, wide), lambda n: (0, 0, n))
    operands = [*pieces, low, squares, magnitude, grad_product]
    in_specs = [
        fixed((share, depth)),
        fixed((share, depth)),
        pl.BlockSpec((2, depth, wide), lambda n: (0, 0, n)),
        column,
        column,
        pl.BlockSpec((2, share, wide), lambda n: (step, 0, n)),
    ]
    out_specs = [
        pl.BlockSpec((1, 2, share, wide), lambda n: (0, 0, 0, n)),
        pl.BlockSpec((2, 2, share, wide), lambda n: (0, 0, 0, n)),
        column,
        fixed((rows, depth)),
        fixed((share, depth)),
        fixed((share, depth)),
    ]
    out_shape = [
        shape((1, 2, share, width), LOW),
        shape((2, 2, share, width), LOW),
        shape((2, 1, width), F32),
        shape((rows, depth), LOW),
        shape((share, depth), LOW),
        shape((share, depth), LOW),
    ]
    extra_in = extra_out = 0
    if first:
        rank = left_rows.shape[1] // 2
        extra_in = 2 * rank
        operands.append(left_rows)
        in_specs.append(fixed(left_rows.shape))
        out_specs.append(pl.BlockSpec((2, rank, wide), lambda n: (0, 0, n)))
        out_shape.append(shape((2, rank, width), F32))
    if last:
        rank = right.shape[1]
        extra_out = 2 * rank
        operands += [right, *before]
        in_specs.append(pl.BlockSpec((2, rank, wide), lambda n: (0, 0, n)))
        in_specs += [column for _ in before]
        out_specs.append(fixed((2, rank, depth)))
        out_shape.append(shape((2, rank, depth), F32))
    return call(
        "expand",
        functools.partial(expand_kernel, first, last, len(before)),
        tuple(operands),
        (width // wide,),
        in_specs,
        out_specs,
        out_shape,
        scratch=[
            pltpu.VMEM((rows + extra_in, depth), LOW),
            pltpu.VMEM((rows + extra_out, 2 * wide), LOW),
            pltpu.VMEM((rows + extra_out, depth), F32),
        ],
        flops=8 * rows * depth * width,
    )


def adapter_kernel(views, n_inputs, n_grads, n_totals, has_low, order_ref, *refs):
    inputs, grads = refs[:n_inputs], refs[n_inputs : n_inputs + n_grads]
    rest = refs[n_inputs + n_grads :]
    back_ref, across_ref, left_ref, right_ref, squares_ref, magnitude_ref = rest[:6]
    totals, (left_out, right_out, magnitude_out) = rest[6 : 6 + n_totals], rest[6 + n_totals :]
    members, rank, _ = right_ref.shape
    width = right_ref.shape[2]
    total = sum_refs(totals)[:, :, :width]
    squares = squares_ref[:, :, :width]
    weight = norm_weight(total, squares, magnitude_ref[...])
    magnitude_out[...] = total / jnp.sqrt(squares)
    left_rows = left_ref[...].reshape(members * 2 * rank, -1)
    right_rows = [split_rows(right_ref[m]) for m in range(members)]
    for m in range(members):
        if has_low:
            low = back_ref[m, : left_ref.shape[2], :]
            left_out[m] = -fold(dot(split_rows(right_ref[m] * weight[m]), low, NT))
        else:
            left_out[m] = -back_ref[m]
        right_out[m] = -(across_ref[m][:, :width] * weight[m])
    for taken, grads_of in views(order_ref, inputs, grads):
        across = dot(left_rows, taken, NT)
        downs = []
        for m in range(members):
            grad = grads_of(m)
            mine = split_rows(fold(across[2 * rank * m : 2 * rank * (m + 1)]))
            right_out[m] += fold(dot(mine, grad))
            downs.append(split_rows(fold(dot(right_rows[m], grad, NT))))
        left = dot(jnp.concatenate(downs, axis=0), taken)
        for m in range(members):
            left_out[m] += fold(left[2 * rank * m : 2 * rank * (m + 1)])
    for m in range(members):
        left_out[m] = ADAPT_SCALE * left_out[m]
        right_out[m] = ADAPT_SCALE * right_out[m]


def adapter(name, order, views, inputs, grads, back, across, left_rows, right, totals, squares, magnitude):
    members, rank, width = right.shape
    depth = left_rows.shape[2]
    operands = (*inputs, *grads, back, across, left_rows, right, squares, magnitude, *totals)
    full = lambda dims: pl.BlockSpec(tuple(dims), lambda i, o: (0,) * len(dims))
    outs = [(members, rank, depth), (members, rank, width), (members, 1, width)]
    rows = sum(v.size // v.shape[-1] for v in inputs)
    return call(
        name,
        functools.partial(
            adapter_kernel, views, len(inputs), len(grads), len(totals), back.dtype == LOW
        ),
        operands,
        (1,),
        [full(v.shape) for v in operands],
        [full(dims) for dims in outs],
        [shape(dims, F32) for dims in outs],
        prefetch=(order,),
        flops=8 * members * rows * width * 32,
    )


MESH_IDS = pl.DeviceIdType.MESH


def copy_kernel(count, *refs):
    for source, target in zip(refs[:count], refs[count:]):
        target[...] = source[...]


def copy_out(arrays):
    vmem = pl.BlockSpec(memory_space=pltpu.VMEM)
    full = lambda v: pl.BlockSpec(v.shape, lambda i: (0,) * v.ndim)
    return call(
        "copy_out",
        functools.partial(copy_kernel, len(arrays)),
        tuple(arrays),
        (1,),
        [vmem for _ in arrays],
        [full(v) for v in arrays],
        [shape(v.shape, F32) for v in arrays],
        mib=16,
    )


GRAIN = 16


def pieces_of(width):
    return [(at, min(128, width - at)) for at in range(0, width, 128)]


def cells_of(blocks, lines, parts):
    cells, rows = [], []
    for n, block in enumerate(blocks):
        for m in range(block.shape[0]):
            for at, size in pieces_of(block.shape[2] // parts):
                cells.append((n, m, at, size))
    for n, line in enumerate(lines):
        for m in range(line.shape[0]):
            for at, size in pieces_of(line.shape[2] // parts):
                rows.append((n, m, at, size))
    return cells, rows


def pack(blocks, lines, wide_ref, part, parts, cells, rows):
    for i, (n, m, at, size) in enumerate(cells):
        start = part * (blocks[n].shape[2] // parts) + at
        wide_ref[part, i, :, :size] = blocks[n][m, :, start : start + size]
    for i, (n, m, at, size) in enumerate(rows):
        start = part * (lines[n].shape[2] // parts) + at
        cell, row = len(cells) + i // GRAIN, i % GRAIN
        wide_ref[part, cell, row : row + 1, :size] = lines[n][m, :, start : start + size]


def unpack(full_ref, blocks, lines, part, parts, cells, rows):
    for i, (n, m, at, size) in enumerate(cells):
        start = part * (blocks[n].shape[2] // parts) + at
        blocks[n][m, :, start : start + size] = full_ref[part, i].astype(F32)[:, :size]
    for i, (n, m, at, size) in enumerate(rows):
        start = part * (lines[n].shape[2] // parts) + at
        cell, row = len(cells) + i // GRAIN, i % GRAIN
        values = full_ref[part, cell].astype(F32)
        lines[n][m, :, start : start + size] = values[row : row + 1, :size]


def reduce_kernel(groups, lines, counts, *refs):
    n_all, n_all_lines, n_dp, n_dp_lines = counts
    count = sum(counts)
    taken, given, scratch = refs[:count], refs[count : 2 * count], refs[2 * count :]
    ends = [n_all, n_all + n_all_lines, n_all + n_all_lines + n_dp]
    parted = lambda v: (v[: ends[0]], v[ends[0] : ends[1]], v[ends[1] : ends[2]], v[ends[2] :])
    all_in, all_lines_in, dp_in, dp_lines_in = parted(taken)
    all_out, all_lines_out, dp_out, dp_lines_out = parted(given)
    (
        all_ref,
        line_ref,
        all_low,
        line_low,
        all_got,
        part,
        part_low,
        part_got,
        line_got,
        all_full,
        line_full,
        *sems,
    ) = scratch
    me, row = lax.axis_index("mp"), lax.axis_index("dp")
    piece, line_piece = part.shape[0] // lines, line_ref.shape[1] // lines
    mp_peer = [lax.rem(me + k, groups) for k in range(groups)]
    dp_peer = [lax.rem(row + k, lines) for k in range(lines)]
    barrier = pltpu.get_barrier_semaphore()
    for k in range(1, groups):
        pl.semaphore_signal(barrier, 1, device_id={"mp": mp_peer[k]}, device_id_type=MESH_IDS)
    for k in range(1, lines):
        pl.semaphore_signal(barrier, 1, device_id={"dp": dp_peer[k]}, device_id_type=MESH_IDS)
    all_cells = cells_of(all_in, all_lines_in, groups)
    dp_cells = cells_of(dp_in, dp_lines_in, 1)
    all_ref[...] = jnp.zeros_like(all_ref)
    line_ref[...] = jnp.zeros_like(line_ref)
    for q in range(groups):
        pack(all_in, all_lines_in, all_ref, q, groups, *all_cells)
    pack(dp_in, dp_lines_in, line_ref, 0, 1, *dp_cells)
    all_low[...] = all_ref[...].astype(LOW)
    line_low[...] = line_ref[...].astype(LOW)
    pl.semaphore_wait(barrier, groups + lines - 2)

    def send(source, target, stage, k, axis, peer):
        copy = pltpu.make_async_remote_copy(
            src_ref=source,
            dst_ref=target,
            send_sem=sems[2 * stage].at[k],
            recv_sem=sems[2 * stage + 1].at[k],
            device_id={axis: peer},
            device_id_type=MESH_IDS,
        )
        copy.start()
        return copy

    over_mp = [
        send(all_low.at[mp_peer[k]], all_got.at[k], 0, k, "mp", mp_peer[k])
        for k in range(1, groups)
    ]
    over_dp = [
        send(
            line_low.at[0, pl.ds(dp_peer[k] * line_piece, line_piece)],
            line_got.at[k],
            1,
            k,
            "dp",
            dp_peer[k],
        )
        for k in range(1, lines)
    ]
    total = all_ref[me]
    for k, copy in enumerate(over_mp, 1):
        copy.wait_recv()
        total = total + all_got[k].astype(F32)
    part[...] = total
    part_low[...] = total.astype(LOW)
    part_dp = [
        send(part_low.at[pl.ds(dp_peer[k] * piece, piece)], part_got.at[k], 2, k, "dp", dp_peer[k])
        for k in range(1, lines)
    ]
    mine = pl.ds(row * line_piece, line_piece)
    total = line_ref[0, mine]
    for k, copy in enumerate(over_dp, 1):
        copy.wait_recv()
        total = total + line_got[k].astype(F32)
    line_full[0, mine] = total.astype(LOW)
    line_back = [
        send(line_full.at[0, mine], line_full.at[0, mine], 3, k, "dp", dp_peer[k])
        for k in range(1, lines)
    ]
    held = pl.ds(row * piece, piece)
    total = part[held]
    for k, copy in enumerate(part_dp, 1):
        copy.wait_recv()
        total = total + part_got[k].astype(F32)
    all_full[me, held] = total.astype(LOW)
    part_back = [
        send(all_full.at[me, held], all_full.at[me, held], 4, k, "dp", dp_peer[k])
        for k in range(1, lines)
    ]
    for copy in part_back:
        copy.wait_recv()
    all_back = [
        send(all_full.at[me], all_full.at[me], 5, k, "mp", mp_peer[k]) for k in range(1, groups)
    ]
    for copy in line_back:
        copy.wait_recv()
    unpack(line_full, dp_out, dp_lines_out, 0, 1, *dp_cells)
    for copy in all_back:
        copy.wait_recv()
    for q in range(groups):
        unpack(all_full, all_out, all_lines_out, q, groups, *all_cells)
    for copy in over_mp + over_dp + part_dp + line_back + part_back + all_back:
        copy.wait_send()


def reduce_devices(name, identity, over_all, over_all_lines, over_dp, over_dp_lines):
    groups, lines = lax.axis_size("mp"), lax.axis_size("dp")

    def size_of(blocks, rows, parts):
        cells, lines_in = cells_of(blocks, rows, parts)
        size = len(cells) + -(-len(lines_in) // GRAIN)
        return -(-size // lines) * lines

    count, line_count = size_of(over_all, over_all_lines, groups), size_of(over_dp, over_dp_lines, 1)
    operands = (*over_all, *over_all_lines, *over_dp, *over_dp_lines)
    counts = (len(over_all), len(over_all_lines), len(over_dp), len(over_dp_lines))
    vmem = pl.BlockSpec(memory_space=pltpu.VMEM)
    tail = (GRAIN, 128)
    sizes = (groups, lines, lines, lines, lines, groups)
    every, line = (groups, count) + tail, (1, line_count) + tail
    results = pl.pallas_call(
        functools.partial(reduce_kernel, groups, lines, counts),
        name=name,
        out_shape=[shape(v.shape, F32) for v in operands],
        in_specs=[vmem for _ in operands],
        out_specs=[vmem for _ in operands],
        scratch_shapes=[
            pltpu.VMEM(every, F32),
            pltpu.VMEM(line, F32),
            pltpu.VMEM(every, LOW),
            pltpu.VMEM(line, LOW),
            pltpu.VMEM(every, LOW),
            pltpu.VMEM((count,) + tail, F32),
            pltpu.VMEM((count,) + tail, LOW),
            pltpu.VMEM((lines, count // lines) + tail, LOW),
            pltpu.VMEM((lines, line_count // lines) + tail, LOW),
            pltpu.VMEM(every, LOW),
            pltpu.VMEM(line, LOW),
        ]
        + [pltpu.SemaphoreType.DMA((n,)) for n in sizes for _ in range(2)],
        compiler_params=pltpu.CompilerParams(
            collective_id=identity, has_side_effects=True, vmem_limit_bytes=32 * 2**20
        ),
        cost_estimate=pl.CostEstimate(flops=1000, bytes_accessed=2**20, transcendentals=0),
    )(*operands)
    return copy_out(results)


def geometry(segment):
    length = segment.shape[0]
    places = lax.broadcasted_iota(jnp.int32, (length, length), 0)
    others = lax.broadcasted_iota(jnp.int32, (length, length), 1)
    visible = (segment[:, None] == segment[None, :]) & (others <= places)
    offset = jnp.sum(visible.astype(F32), axis=1) - 1.0
    lane = jnp.arange(HEAD_DIM, dtype=jnp.int32)
    half = (lane % (HEAD_DIM // 2)).astype(F32)
    frequency = jnp.exp(-jnp.log(ROPE_BASE) * 2.0 * half / HEAD_DIM)
    sign = jnp.where(lane < HEAD_DIM // 2, -1.0, 1.0)
    angles = offset[:, None] * frequency[None, :]
    first = jnp.arange(length, dtype=jnp.int32) - offset.astype(jnp.int32)
    return first[:, None], jnp.cos(angles), jnp.sin(angles) * sign[None, :]


def body(
    tokens,
    cotangent,
    segment_ids,
    attend_gain,
    expand_gain,
    heads_base,
    heads_left,
    heads_right,
    heads_magnitude,
    output_base,
    output_left,
    output_right,
    output_magnitude,
    expand_base,
    expand_left,
    expand_right,
    expand_magnitude,
    shrink_base,
    shrink_left,
    shrink_right,
    shrink_magnitude,
):
    groups = lax.axis_size("mp")
    chips = groups // CORES
    index = lax.axis_index("mp")
    chip, core = index // CORES, index % CORES
    rows, width = tokens.shape
    share = rows // groups
    local_heads, ff = heads_base.shape[2], expand_base.shape[2]
    ff_wide = padded(ff)
    device = jnp.arange(groups, dtype=jnp.int32)
    order = jnp.concatenate(
        [
            (chip + device // CORES) % chips * CORES + (core + 1 + device) % CORES,
            (device // CORES + chips - chip) % chips * CORES + (device + CORES - core + 1) % CORES,
        ]
    ).astype(jnp.int32)

    def own(values):
        return lax.dynamic_slice_in_dim(values, index * share, share, 0)

    def tie(*values):
        return lax.optimization_barrier(values)

    def sibling(values):
        return lax.ppermute(
            values, "mp", [(i, i // CORES * CORES + (i + 1) % CORES) for i in range(groups)]
        )

    def to_chip(values, step):
        return lax.ppermute(
            values,
            "mp",
            [((i, ((i // CORES + step) % chips) * CORES + i % CORES)) for i in range(groups)],
        )

    def mp_sum(values):
        values = values + sibling(values)
        total = values
        for step in range(1, chips):
            total = total + to_chip(values, step)
        return total

    def join(product):
        return (product[1].astype(F32) + sibling(product[0]).astype(F32)).astype(LOW)

    def arrive(own):
        return [to_chip(own, chips - step) for step in range(1, chips)]

    def pairs_of(own, near_sibling, arrived):
        return [(near_sibling, own)] + [(sibling(piece), piece) for piece in arrived]

    def in_pairs(order_ref, inputs, grads):
        for taken, grad in zip(inputs, grads):
            yield taken[...], lambda m, grad=grad: grad[m].reshape(-1, grad.shape[-1])[:, :ff]

    def in_shrink(order_ref, inputs, grads):
        for step, taken in enumerate(inputs):
            at = slice(CORES * step, CORES * (step + 1))
            yield (
                taken[0].reshape(-1, taken.shape[-1])[:, :ff],
                lambda m, at=at: grads[0][at].reshape(-1, grads[0].shape[-1]),
            )

    def in_output(order_ref, inputs, grads):
        for place, grad in enumerate(grads):
            yield inputs[0][0, place], lambda m, grad=grad: grad[...]

    def in_heads(order_ref, inputs, grads):
        for place in range(groups):
            at = pl.multiple_of(order_ref[place] * share, share)
            rows = slice(place * share, (place + 1) * share)
            yield inputs[0][pl.ds(at, share), :], lambda m, rows=rows: grads[0][m, rows, :]

    heads_rows, output_rows = left_pairs(heads_left), left_pairs(output_left[None])
    expand_rows, shrink_rows = left_pairs(expand_left), left_pairs(shrink_left[None])
    heads_mag, output_mag = heads_magnitude[:, None], output_magnitude[None, None]
    expand_mag, shrink_mag = expand_magnitude[:, None], shrink_magnitude[None, None]
    attend_line, expand_line = attend_gain[None], expand_gain[None]

    output_low, output_part = merge(
        output_base[None], output_rows, output_right[None], output_base.shape[0], 512
    )
    shrink_low, shrink_part = merge(
        shrink_base[None], shrink_rows, shrink_right[None], shrink_base.shape[0], 512
    )
    tokens, output_part, shrink_part = lax.optimization_barrier((tokens, output_part, shrink_part))
    squares = mp_sum(jnp.concatenate([output_part, shrink_part], axis=1))
    output_sq, shrink_sq = squares[:, :1], squares[:, 1:]

    first, cos_table, sine_table = geometry(segment_ids.reshape(-1))
    normed, heads_low, post, heads_sq, heads_across = project_heads(
        tokens,
        attend_line,
        heads_base,
        heads_rows,
        heads_right,
        heads_mag,
        cos_table,
        sine_table,
    )
    heads_out = attend(order, groups, post, first)
    heads_parts = heads_out.reshape(1, groups, share, local_heads)
    output_far = [
        pair_product("output_product", heads_parts, output_low, NN, step)
        for step in range(1, chips)
    ]
    output_near = pair_product("output_product", heads_parts, output_low, NN, 0, output_rows)
    joined = [join(product) for product in output_far]
    joined, expand_rows = tie(joined, expand_rows)
    output_arrived = [to_chip(values, step) for step, values in enumerate(joined, 1)]
    expand_low, expand_sq = merge(expand_base, expand_rows, expand_right, 512, expand_base.shape[2])
    grad_product, shrink_grad = shrink_back(
        order, cotangent, shrink_low, shrink_sq, shrink_mag, groups
    )
    own_tokens, own_cot = own(tokens), own(cotangent)
    output_parts = [output_near[1], sibling(output_near[0]), *output_arrived]
    output_parts, expand_low, grad_product, own_tokens, own_cot = tie(
        output_parts, expand_low, grad_product, own_tokens, own_cot
    )
    hidden, normed_own = row_call(
        "hidden",
        hidden_kernel,
        [own_tokens, *output_parts],
        (output_sq[0], output_mag[0], expand_line),
        (F32, LOW),
        0,
    )

    expand_mag_wide = pad_last(expand_mag, ff_wide)
    expand_right_wide = pad_last(expand_right, ff_wide)
    shrink_rows_wide = pad_last(shrink_rows, ff_wide)

    def feed(pieces, step, **extra):
        return expand(
            pieces, expand_low, expand_sq, expand_mag_wide, grad_product, step, **extra
        )

    def shrink_of(fed, step):
        return shrink_product(order, fed[0], shrink_low, shrink_rows_wide, cotangent, step)

    arrived, near_sibling = arrive(normed_own), sibling(normed_own)
    fed = [feed((near_sibling, normed_own), 0, left_rows=expand_rows)]
    shrunk = [shrink_of(fed[0], 0)]
    arrived, fed, shrunk = tie(arrived, fed, shrunk)
    fed, shrunk = list(fed), list(shrunk)
    mid_sibling = sibling(fed[0][4])
    normed_mid = pairs_of(normed_own, near_sibling, arrived)
    for step in range(1, chips):
        extra = {}
        if step == chips - 1:
            extra = {"right": expand_right_wide, "before": [f[2] for f in fed]}
        fed.append(feed(normed_mid[step], step, **extra))
    expand_totals = [f[2] for f in fed]
    joined = [join(f[4:6]) for f in fed[1:]]
    joined, shrink_rows_wide = tie(joined, shrink_rows_wide)
    mid_arrived = [to_chip(values, step) for step, values in enumerate(joined, 1)]
    shrunk += [shrink_of(f, step) for step, f in enumerate(fed) if step]
    shrink_total = mp_sum(functools.reduce(jnp.add, [piece[2] for piece in shrunk]))
    shrink_joined = [join(product) for product in shrunk[1:]]
    expand_adapter = adapter(
        "expand_adapter",
        order,
        in_pairs,
        [f[3] for f in fed],
        [f[1] for f in fed],
        fed[-1][6],
        fed[0][6],
        expand_rows,
        expand_right,
        expand_totals,
        expand_sq,
        expand_mag,
    )
    mid_parts = [fed[0][5], mid_sibling, *mid_arrived]
    mid_parts, shrunk, shrink_joined, shrink_total, expand_adapter = tie(
        mid_parts, shrunk, shrink_joined, shrink_total, expand_adapter
    )
    grad_hidden, output_grad_own, output_total, expand_gain_part = row_call(
        "hidden_back",
        hidden_back_kernel,
        [own_cot, own_tokens, hidden, *mid_parts],
        (output_sq[0], output_mag[0], expand_line),
        (F32, LOW),
        2,
    )
    arrived, near_sibling = arrive(output_grad_own), sibling(output_grad_own)
    output_total = mp_sum(output_total)
    shrink_adapter = adapter(
        "shrink_adapter",
        order,
        in_shrink,
        [f[0] for f in fed],
        [shrink_grad],
        shrink_low,
        shrunk[0][3],
        shrink_rows,
        shrink_right[None],
        [shrink_total[None]],
        shrink_sq,
        shrink_mag,
    )
    early = reduce_devices(
        "reduce_early",
        1,
        [expand_adapter[0], shrink_adapter[1]],
        [expand_gain_part[None]],
        [expand_adapter[1], shrink_adapter[0]],
        [expand_adapter[2], shrink_adapter[2]],
    )
    arrived, near_sibling, output_total, shrink_joined, early = tie(
        arrived, near_sibling, output_total, shrink_joined, early
    )
    expand_left_grad, shrink_right_grad, expand_gain_grad = early[:3]
    expand_right_grad, shrink_left_grad, expand_mag_grad, shrink_mag_grad = early[3:]
    output_grad = [
        piece for pair in pairs_of(output_grad_own, near_sibling, arrived) for piece in pair
    ]
    shrink_parts = [shrunk[0][1], sibling(shrunk[0][0])] + [
        to_chip(values, step) for step, values in enumerate(shrink_joined, 1)
    ]
    heads_grads, heads_total = attend_back(
        order,
        groups,
        post,
        first,
        cos_table,
        sine_table,
        heads_mag,
        heads_sq,
        output_low,
        output_grad,
    )
    heads_grads, shrink_parts = tie(heads_grads, shrink_parts)
    grad_parts = heads_grads.reshape(3, groups, share, local_heads)
    token_far = [
        pair_product("normed_product", grad_parts, heads_low, NT, step)
        for step in range(1, chips)
    ]
    joined = [join(product) for product in token_far]
    token_near = pair_product(
        "normed_product",
        grad_parts,
        heads_low,
        NT,
        0,
        correction=(heads_right, heads_sq, heads_mag, [heads_total]),
    )
    joined, heads_rows, output_rows = tie(joined, heads_rows, output_rows)
    token_arrived = [to_chip(values, step) for step, values in enumerate(joined, 1)]
    output_adapter = adapter(
        "output_adapter",
        order,
        in_output,
        [heads_parts],
        output_grad,
        output_low,
        output_near[2],
        output_rows,
        output_right[None],
        [output_total[None]],
        output_sq,
        output_mag,
    )
    heads_adapter = adapter(
        "heads_adapter",
        order,
        in_heads,
        [normed],
        [heads_grads],
        token_near[2],
        heads_across,
        heads_rows,
        heads_right,
        [heads_total],
        heads_sq,
        heads_mag,
    )
    (mixed,) = row_call(
        "mixed", mixed_kernel, [hidden, *shrink_parts], (shrink_sq[0], shrink_mag[0]), (LOW,), 0
    )
    token_parts = [token_near[1], sibling(token_near[0]), *token_arrived]
    token_parts, output_adapter, heads_adapter, mixed = tie(
        token_parts, output_adapter, heads_adapter, mixed
    )
    grad_tokens, attend_gain_part = row_call(
        "token_back",
        token_back_kernel,
        [own_tokens, grad_hidden, *token_parts],
        (attend_line,),
        (F32,),
        1,
    )
    late = reduce_devices(
        "reduce_late",
        2,
        [heads_adapter[0], output_adapter[1]],
        [attend_gain_part[None]],
        [heads_adapter[1], output_adapter[0]],
        [heads_adapter[2], output_adapter[2]],
    )
    heads_left_grad, output_right_grad, attend_gain_grad = late[:3]
    heads_right_grad, output_left_grad, heads_mag_grad, output_mag_grad = late[3:]
    return (
        mixed,
        grad_tokens,
        attend_gain_grad[0, 0],
        expand_gain_grad[0, 0],
        jnp.swapaxes(heads_left_grad, 1, 2),
        heads_right_grad,
        heads_mag_grad[:, 0],
        output_left_grad[0].T,
        output_right_grad[0],
        output_mag_grad[0, 0],
        jnp.swapaxes(expand_left_grad, 1, 2),
        expand_right_grad,
        expand_mag_grad[:, 0],
        shrink_left_grad[0].T,
        shrink_right_grad[0],
        shrink_mag_grad[0, 0],
    )


def solution(mesh):
    placed = (
        P("dp", None),
        P("dp", None),
        P("dp", None),
        P(),
        P(),
        P(None, None, "mp"),
        P(),
        P(None, None, "mp"),
        P(None, "mp"),
        P("mp", None),
        P("mp", None),
        P(),
        P(),
        P(None, None, "mp"),
        P(),
        P(None, None, "mp"),
        P(None, "mp"),
        P("mp", None),
        P("mp", None),
        P(),
        P(),
    )
    return jax.shard_map(
        body,
        mesh=mesh,
        in_specs=placed,
        out_specs=(
            P(("dp", "mp"), None),
            P(("dp", "mp"), None),
            P(),
            P(),
            P(),
            P(None, None, "mp"),
            P(None, "mp"),
            P("mp", None),
            P(),
            P(),
            P(),
            P(None, None, "mp"),
            P(None, "mp"),
            P("mp", None),
            P(),
            P(),
        ),
        check_vma=False,
    )
```

```python
import functools

import jax
import jax.numpy as jnp
from jax import lax
from jax.experimental import pallas as pl
from jax.experimental.pallas import tpu as pltpu
from jax.sharding import PartitionSpec as P

HEAD_DIM = 128
CORES = 2
LONGEST = 512
ATTEND_BLOCK = 256
ADAPT_SCALE = 2.0
NORM_EPS = 1e-05
ROPE_BASE = 10000.0
MASKED = -1e30

F32 = jnp.float32
LOW = jnp.bfloat16
NN = (((1,), (0,)), ((), ()))
NT = (((1,), (1,)), ((), ()))
TN = (((0,), (0,)), ((), ()))


def dot(left, right, dims=NN):
    return lax.dot_general(left, right, dims, preferred_element_type=F32)


def shape(dims, kind):
    return jax.ShapeDtypeStruct(tuple(dims), kind)


def call(name, kernel, operands, grid, in_specs, out_specs, out_shape, scratch=(), prefetch=(), flops=0, mib=60):
    moved = sum(v.size * v.dtype.itemsize for v in operands)
    moved += sum(v.size * v.dtype.itemsize for v in out_shape)
    return pl.pallas_call(
        kernel,
        name=name,
        out_shape=out_shape,
        grid_spec=pltpu.PrefetchScalarGridSpec(
            num_scalar_prefetch=len(prefetch),
            grid=grid,
            in_specs=in_specs,
            out_specs=out_specs,
            scratch_shapes=scratch,
        ),
        compiler_params=pltpu.CompilerParams(vmem_limit_bytes=mib * 2**20),
        cost_estimate=pl.CostEstimate(flops=flops // 16, bytes_accessed=moved // 16, transcendentals=0),
    )(*prefetch, *operands)


def tile_of(size, most):
    return most if size % most == 0 else size


def split_rows(values):
    top = values.astype(LOW)
    rest = (values - top.astype(F32)).astype(LOW)
    return jnp.concatenate([top, rest], axis=0)


def turned(left_map):
    return jnp.swapaxes(left_map, -1, -2)


def norm_weight(total, squares, magnitude):
    norm = jnp.sqrt(squares)
    return total * magnitude / (norm * norm * norm)


def sum_refs(refs):
    total = refs[0][...]
    for ref in refs[1:]:
        total = total + ref[...]
    return total


def fold(values):
    half = values.shape[0] // 2
    return values[:half] + values[half:]


def merge_tile(base_at, low_put, left, right, depth):
    rank = right.shape[0]
    doubled = ADAPT_SCALE * right
    top = doubled.astype(LOW)
    rest = (doubled - top.astype(F32)).astype(LOW)
    right_stack = jnp.concatenate([top, rest, top], axis=0)
    left_pair = split_rows(left)
    left_stack = jnp.concatenate([left_pair[:rank], left_pair[:rank], left_pair[rank:]], axis=0)
    squares = jnp.zeros((1, right.shape[1]), F32)
    step = tile_of(depth, 1024)
    for start in range(0, depth, step):
        merged = base_at(start, step).astype(F32) + dot(
            left_stack[:, start : start + step], right_stack, TN
        )
        low_put(start, step, merged.astype(LOW))
        squares = squares + jnp.sum(merged * merged, axis=0, keepdims=True)
    return squares


def merge_kernel(base_ref, left_ref, right_ref, low_ref, squares_ref):
    depth, width = base_ref.shape[1:]
    if low_ref.shape[1] > depth:
        low_ref[0, depth:, :] = jnp.zeros((low_ref.shape[1] - depth, low_ref.shape[2]), LOW)
    if low_ref.shape[2] > width:
        spare = low_ref.shape[2] - width
        low_ref[0, :, width:] = jnp.zeros((low_ref.shape[1], spare), LOW)
        squares_ref[0, :, width:] = jnp.ones((1, spare), F32)

    def put(start, step, tile):
        low_ref[0, start : start + step, :width] = tile

    squares = merge_tile(
        lambda start, step: base_ref[0, start : start + step, :],
        put,
        left_ref[0],
        right_ref[0],
        depth,
    )

    @pl.when(pl.program_id(2) == 0)
    def _():
        squares_ref[0, :, :width] = squares

    @pl.when(pl.program_id(2) > 0)
    def _():
        squares_ref[0, :, :width] += squares


def padded(size):
    return -(-size // 256) * 256


def pad_last(values, size):
    return jnp.pad(values, [(0, 0)] * (values.ndim - 1) + [(0, size - values.shape[-1])])


def merge(base, left, right, deep, wide):
    members, depth, width = base.shape
    low_deep = padded(deep) if deep == depth else deep
    low_wide = padded(wide) if wide == width else wide
    low_shape = (members, depth // deep * low_deep, width // wide * low_wide)
    rank = right.shape[1]
    return call(
        "merge",
        merge_kernel,
        (base, left, right),
        (members, width // wide, depth // deep),
        [
            pl.BlockSpec((1, deep, wide), lambda m, n, k: (m, k, n)),
            pl.BlockSpec((1, rank, deep), lambda m, n, k: (m, 0, k)),
            pl.BlockSpec((1, rank, wide), lambda m, n, k: (m, 0, n)),
        ],
        [
            pl.BlockSpec((1, low_deep, low_wide), lambda m, n, k: (m, k, n)),
            pl.BlockSpec((1, 1, low_wide), lambda m, n, k: (m, 0, n)),
        ],
        [shape(low_shape, LOW), shape((members, 1, low_shape[2]), F32)],
        flops=2 * members * depth * width * 256,
    )


def rms_rows(values):
    return lax.rsqrt(jnp.mean(values * values, axis=1, keepdims=True) + NORM_EPS)


def heads_kernel(
    token_ref,
    gain_ref,
    base_ref,
    left_ref,
    right_ref,
    magnitude_ref,
    cos_ref,
    sine_ref,
    normed_ref,
    low_ref,
    post_ref,
    squares_ref,
    across_ref,
    rows_all,
):
    total_rows = token_ref.shape[0]
    depth, width = base_ref.shape[1:]
    rank = right_ref.shape[1]

    @pl.when((pl.program_id(0) == 0) & (pl.program_id(1) == 0))
    def _():
        step = 128

        def some(i, carry):
            at = pl.ds(pl.multiple_of(i * step, step), step)
            values = token_ref[at, :].astype(F32)
            low = (values * rms_rows(values) * gain_ref[...]).astype(LOW)
            normed_ref[at, :] = low
            rows_all[at, :] = low
            return carry

        lax.fori_loop(0, total_rows // step, some, 0)

    rows_all[total_rows:, :] = left_ref[0].astype(LOW)

    def put(start, step, tile):
        low_ref[0, start : start + step, :] = tile

    squares = merge_tile(
        lambda start, step: base_ref[0, start : start + step, :],
        put,
        left_ref[0],
        right_ref[0],
        depth,
    )
    squares_ref[0] = squares
    scale = magnitude_ref[pl.ds(pl.program_id(0), 1), :] / jnp.sqrt(squares)
    low = low_ref[0]
    turning = pl.program_id(0) < 2
    step = min(512, total_rows)
    for start in range(0, total_rows, step):
        last = start + step == total_rows
        rows = slice(start, start + step)
        pre = dot(rows_all[start : start + step + (rank if last else 0), :], low)
        if last:
            across_ref[0] = pre[step:]
        post = pre[:step] * scale
        cos_table = jnp.where(turning, cos_ref[rows, :], 1.0)
        sine_table = jnp.where(turning, sine_ref[rows, :], 0.0)
        for head in range(0, width, HEAD_DIM):
            piece = post[:, head : head + HEAD_DIM]
            turned = pltpu.roll(piece, HEAD_DIM // 2, 1)
            post_ref[0, rows, head : head + HEAD_DIM] = (
                piece * cos_table + turned * sine_table
            ).astype(LOW)


def project_heads(tokens, gain, base, left, right, magnitude, cos_table, sine_table):
    members, depth, width = base.shape
    rows, rank = tokens.shape[0], right.shape[1]
    wide = 256
    whole = lambda m, n: (0, 0)
    return call(
        "project_heads",
        heads_kernel,
        (tokens, gain, base, left, right, magnitude, cos_table, sine_table),
        (members, width // wide),
        [
            pl.BlockSpec((rows, depth), whole),
            pl.BlockSpec((1, depth), whole),
            pl.BlockSpec((1, depth, wide), lambda m, n: (m, 0, n)),
            pl.BlockSpec((1, rank, depth), lambda m, n: (m, 0, 0)),
            pl.BlockSpec((1, rank, wide), lambda m, n: (m, 0, n)),
            pl.BlockSpec((members, wide), lambda m, n: (0, n)),
            pl.BlockSpec((rows, HEAD_DIM), whole),
            pl.BlockSpec((rows, HEAD_DIM), whole),
        ],
        [
            pl.BlockSpec((rows, depth), whole),
            pl.BlockSpec((1, depth, wide), lambda m, n: (m, 0, n)),
            pl.BlockSpec((1, rows, wide), lambda m, n: (m, 0, n)),
            pl.BlockSpec((1, 1, wide), lambda m, n: (m, 0, n)),
            pl.BlockSpec((1, rank, wide), lambda m, n: (m, 0, n)),
        ],
        [
            shape((rows, depth), LOW),
            shape(base.shape, LOW),
            shape((members, rows, width), LOW),
            shape((members, 1, width), F32),
            shape((members, rank, width), F32),
        ],
        scratch=[pltpu.VMEM((rows + rank, depth), LOW)],
        flops=2 * members * rows * depth * width,
    )


def key_start(block):
    return max(0, (block * ATTEND_BLOCK - (LONGEST - 1)) // ATTEND_BLOCK * ATTEND_BLOCK)


def masked_probs(scores, first, row_at, key_at):
    scores = scores * HEAD_DIM ** (-0.5)
    places = row_at + lax.broadcasted_iota(jnp.int32, scores.shape, 0)
    others = key_at + lax.broadcasted_iota(jnp.int32, scores.shape, 1)
    scores = jnp.where((others >= first) & (others <= places), scores, MASKED)
    exp_scores = jnp.exp(scores - jnp.max(scores, axis=1, keepdims=True))
    return exp_scores * (1.0 / jnp.sum(exp_scores, axis=1, keepdims=True))


class Unit:
    def __init__(self, head, block):
        self.row_at, self.key_at = block * ATTEND_BLOCK, key_start(block)
        self.rows = slice(self.row_at, self.row_at + ATTEND_BLOCK)
        self.keys = slice(self.key_at, self.row_at + ATTEND_BLOCK)
        self.lanes = slice(head * HEAD_DIM, (head + 1) * HEAD_DIM)


def units_of(rows, width, most):
    units = [
        Unit(head, block)
        for block in range(rows // ATTEND_BLOCK)
        for head in range(width // HEAD_DIM)
    ]
    return [units[at : at + most] for at in range(0, len(units), most)]


def put_rows(ref, lead, row_at, lanes, values, order_ref, groups):
    share = ref.shape[len(lead)] // groups
    step = min(share, values.shape[0])
    for start in range(0, values.shape[0], step):
        group = (row_at + start) // share
        inside = (row_at + start) % share
        at = pl.multiple_of(order_ref[groups + group] * share + inside, step)
        ref[(*lead, pl.ds(at, step), lanes)] = values[start : start + step].astype(ref.dtype)


def attend_kernel(groups, order_ref, query_ref, key_ref, value_ref, first_ref, out_ref):
    for some in units_of(*query_ref.shape[1:], 4):
        scores = [
            dot(query_ref[0, u.rows, u.lanes], key_ref[0, u.keys, u.lanes], NT) for u in some
        ]
        probs = [
            masked_probs(s, first_ref[u.rows, :], u.row_at, u.key_at).astype(LOW)
            for u, s in zip(some, scores)
        ]
        for u, p in zip(some, probs):
            mixed = dot(p, value_ref[0, u.keys, u.lanes])
            put_rows(out_ref, (), u.row_at, u.lanes, mixed, order_ref, groups)


def attend(order, groups, post, first):
    rows, width = post.shape[1:]
    wide = 2 * HEAD_DIM
    member = lambda m: pl.BlockSpec((1, rows, wide), lambda h, o: (m, 0, h))
    return call(
        "attend",
        functools.partial(attend_kernel, groups),
        (post, post, post, first),
        (width // wide,),
        [member(0), member(1), member(2), pl.BlockSpec((rows, 1), lambda h, o: (0, 0))],
        [pl.BlockSpec((rows, wide), lambda h, o: (0, h))],
        [shape((rows, width), LOW)],
        prefetch=(order,),
        flops=4 * rows * rows * width,
        mib=32,
    )[0]


def attend_back_kernel(
    groups,
    order_ref,
    query_ref,
    key_ref,
    value_ref,
    first_ref,
    cos_ref,
    sine_ref,
    magnitude_ref,
    squares_ref,
    low_ref,
    *rest,
):
    pieces, (grad_ref, total_ref, upper_all, heads_grad, key_grad, value_grad, sems) = rest[:-7], rest[-7:]
    rows_all, width = query_ref.shape[1:]
    share = rows_all // groups

    @pl.when(pl.program_id(0) == 0)
    def _():
        copies = []
        for place, piece in enumerate(pieces):
            at = pl.multiple_of(order_ref[place] * share, share)
            copies.append(
                pltpu.make_async_copy(piece, upper_all.at[pl.ds(at, share), :], sems.at[place])
            )
            copies[-1].start()
        for copy in copies:
            copy.wait()

    step = min(512, rows_all)
    for start in range(0, rows_all, step):
        at = slice(start, start + step)
        heads_grad[at, :] = dot(upper_all[at, :], low_ref[0], NT).astype(LOW)
    norm = [jnp.sqrt(squares_ref[m]) for m in range(3)]
    scale = [magnitude_ref[m : m + 1] / norm[m] for m in range(3)]
    heads = range(0, width, HEAD_DIM)
    totals = [jnp.zeros((1, width), F32) for _ in range(3)]
    filled = set()

    def back(values, rows):
        return values * cos_ref[rows, :] - pltpu.roll(values, HEAD_DIM // 2, 1) * sine_ref[rows, :]

    def add(ref, unit, values):
        for start in range(0, values.shape[0], ATTEND_BLOCK):
            at = unit.key_at + start
            rows = slice(at, at + ATTEND_BLOCK)
            name = (id(ref), at, unit.lanes.start)
            if name in filled:
                ref[rows, unit.lanes] += values[start : start + ATTEND_BLOCK]
            else:
                filled.add(name)
                ref[rows, unit.lanes] = values[start : start + ATTEND_BLOCK]

    def spread(per_head):
        return jnp.concatenate(per_head, axis=1)

    query_totals = [jnp.zeros((1, HEAD_DIM), F32) for _ in heads]
    for some in units_of(rows_all, width, 2):
        scores = [
            dot(query_ref[0, u.rows, u.lanes], key_ref[0, u.keys, u.lanes], NT) for u in some
        ]
        grad_weights = [
            dot(heads_grad[u.rows, u.lanes], value_ref[0, u.keys, u.lanes], NT) for u in some
        ]
        probs = [
            masked_probs(s, first_ref[u.rows, :], u.row_at, u.key_at)
            for u, s in zip(some, scores)
        ]
        grad_scores = [
            (p * (g - jnp.sum(p * g, axis=1, keepdims=True))).astype(LOW)
            for p, g in zip(probs, grad_weights)
        ]
        for u, p, g in zip(some, probs, grad_scores):
            add(value_grad, u, dot(p.astype(LOW), heads_grad[u.rows, u.lanes], TN))
            add(key_grad, u, dot(g, query_ref[0, u.rows, u.lanes], TN))
        for u, g in zip(some, grad_scores):
            grad = back(dot(g, key_ref[0, u.keys, u.lanes]) * HEAD_DIM ** (-0.5), u.rows)
            head = u.lanes.start // HEAD_DIM
            post = back(query_ref[0, u.rows, u.lanes].astype(F32), u.rows)
            query_totals[head] = query_totals[head] + jnp.sum(grad * post, axis=0, keepdims=True)
            put_rows(grad_ref, (0,), u.row_at, u.lanes, grad * scale[0][:, u.lanes], order_ref, groups)
    totals[0] = spread(query_totals)
    for row_at in range(0, rows_all, ATTEND_BLOCK):
        rows = slice(row_at, row_at + ATTEND_BLOCK)
        for head in heads:
            lanes = slice(head, head + HEAD_DIM)
            grad = back(key_grad[rows, lanes] * HEAD_DIM ** (-0.5), rows)
            post = back(key_ref[0, rows, lanes].astype(F32), rows)
            part = jnp.sum(grad * post, axis=0, keepdims=True)
            query_totals[head // HEAD_DIM] = part if row_at == 0 else query_totals[head // HEAD_DIM] + part
            put_rows(grad_ref, (1,), row_at, lanes, grad * scale[1][:, lanes], order_ref, groups)
        grad = value_grad[rows, :]
        totals[2] = totals[2] + jnp.sum(grad * value_ref[0, rows, :].astype(F32), axis=0, keepdims=True)
        put_rows(grad_ref, (2,), row_at, slice(0, width), grad * scale[2], order_ref, groups)
    totals[1] = spread(query_totals)
    for m in range(3):
        total_ref[m] = totals[m] / scale[m]


def attend_back(order, groups, post, first, cos_table, sine_table, magnitude, squares, low, pieces):
    rows, width = post.shape[1:]
    depth = low.shape[2]
    wide = 2 * HEAD_DIM
    member = lambda m: pl.BlockSpec((1, rows, wide), lambda h, o: (m, 0, h))
    table = pl.BlockSpec((rows, HEAD_DIM), lambda h, o: (0, 0))
    column = pl.BlockSpec((3, 1, wide), lambda h, o: (0, 0, h))
    return call(
        "attend_back",
        functools.partial(attend_back_kernel, groups),
        (post, post, post, first, cos_table, sine_table, magnitude, squares, low, *pieces),
        (width // wide,),
        [
            member(0),
            member(1),
            member(2),
            pl.BlockSpec((rows, 1), lambda h, o: (0, 0)),
            table,
            table,
            pl.BlockSpec((3, wide), lambda h, o: (0, h)),
            column,
            pl.BlockSpec((1, wide, depth), lambda h, o: (0, h, 0)),
            *[pl.BlockSpec(memory_space=pl.ANY) for _ in pieces],
        ],
        [pl.BlockSpec((3, rows, wide), lambda h, o: (0, 0, h)), column],
        [shape((3, rows, width), LOW), shape((3, 1, width), F32)],
        scratch=[
            pltpu.VMEM((rows, depth), LOW),
            pltpu.VMEM((rows, wide), LOW),
            pltpu.VMEM((rows, wide), F32),
            pltpu.VMEM((rows, wide), F32),
            pltpu.SemaphoreType.DMA((len(pieces),)),
        ],
        prefetch=(order,),
        flops=10 * rows * rows * width + 2 * rows * width * depth,
        mib=48,
    )


def product_kernel(dims, n_totals, *refs):
    value_ref, weight_ref = refs[:2]
    groups = value_ref.shape[1]
    if n_totals == 0:
        left_ref, *refs = refs[2:]
    else:
        right_ref, squares_ref, magnitude_ref = refs[2:5]
        totals, refs = refs[5 : 5 + n_totals], refs[5 + n_totals :]
    outs, extra_ref, rows_all = refs[:groups], refs[groups], refs[groups + 1]
    members, _, share, inner = value_ref.shape
    count = groups * share

    @pl.when(pl.program_id(0) == 0)
    def _():
        if n_totals > 0:
            total = sum_refs(totals)
        for m in range(members):
            rows_all[m, :count, :] = value_ref[m].reshape(count, inner)
            if n_totals == 0:
                rows_all[m, count:, :] = left_ref[m].astype(LOW)
            else:
                weight = norm_weight(total[m], squares_ref[m], magnitude_ref[m : m + 1])
                rows_all[m, count:, :] = (right_ref[m] * weight).astype(LOW)

    result = None
    for m in range(members):
        part = dot(rows_all[m], weight_ref[m], dims)
        extra_ref[m] = part[count:]
        result = part[:count] if result is None else result + part[:count]
    for place, ref in enumerate(outs):
        ref[...] = result[place * share : (place + 1) * share].astype(LOW)


def product(name, values, weights, dims, left=None, correction=None):
    members, groups, share, inner = values.shape
    width = weights.shape[2] if dims is NN else weights.shape[1]
    wide = tile_of(width, 512)
    if dims is NN:
        weight_spec = pl.BlockSpec((members, inner, wide), lambda n: (0, 0, n))
    else:
        weight_spec = pl.BlockSpec((members, wide, inner), lambda n: (0, n, 0))
    if correction is None:
        extra, n_totals, rank = (left,), 0, left.shape[1]
    else:
        right, squares, magnitude, totals = correction
        extra, n_totals, rank = (right, squares, magnitude, *totals), len(totals), right.shape[1]
    fixed = lambda v: pl.BlockSpec(v.shape, lambda n: (0,) * v.ndim)
    out = pl.BlockSpec((share, wide), lambda n: (0, n))
    results = call(
        name,
        functools.partial(product_kernel, dims, n_totals),
        (values, weights, *extra),
        (width // wide,),
        [fixed(values), weight_spec] + [fixed(v) for v in extra],
        [out] * groups + [pl.BlockSpec((members, rank, wide), lambda n: (0, 0, n))],
        [shape((share, width), LOW)] * groups + [shape((members, rank, width), F32)],
        scratch=[pltpu.VMEM((members, groups * share + rank, inner), LOW)],
        flops=2 * members * groups * share * inner * width,
    )
    return results[:groups], results[groups]


def shrink_kernel(chips, order_ref, *refs):
    values, (weight_ref, left_ref, cot_ref), outs = refs[:chips], refs[chips : chips + 3], refs[chips + 3 :]
    total_ref, across_ref, rows_all = outs[-3:]
    _, _, share, inner = values[0].shape
    depth = left_ref.shape[2]
    count = chips * CORES * share

    @pl.when(pl.program_id(0) == 0)
    def _():
        for step, ref in enumerate(values):
            at = step * CORES * share
            rows_all[at : at + CORES * share, :] = ref[0].reshape(CORES * share, inner)
        if inner > depth:
            rows_all[count:, depth:] = jnp.zeros((rows_all.shape[0] - count, inner - depth), LOW)
        rows_all[count:, :depth] = left_ref[0].astype(LOW)

    result = dot(rows_all[...], weight_ref[0])
    across_ref[0] = result[count:]
    total = jnp.zeros((1, weight_ref.shape[2]), F32)
    for place in range(chips * CORES):
        pre = result[place * share : (place + 1) * share]
        outs[place][...] = pre.astype(LOW)
        at = pl.multiple_of(order_ref[place] * share, share)
        cot = cot_ref[pl.ds(at, share), :].astype(F32)
        total = total + jnp.sum(pre * cot, axis=0, keepdims=True)
    total_ref[...] = total


def shrink_product(order, values, weights, left, cotangent):
    chips = len(values)
    _, _, share, inner = values[0].shape
    width, rank = weights.shape[2], left.shape[1]
    rows = chips * CORES * share
    wide = tile_of(width, 512)
    fixed = lambda v: pl.BlockSpec(v.shape, lambda n, o: (0,) * v.ndim)
    results = call(
        "shrink_product",
        functools.partial(shrink_kernel, chips),
        (*values, weights, left, cotangent),
        (width // wide,),
        [fixed(v) for v in values]
        + [
            pl.BlockSpec((1, inner, wide), lambda n, o: (0, 0, n)),
            fixed(left),
            pl.BlockSpec((rows, wide), lambda n, o: (0, n)),
        ],
        [pl.BlockSpec((share, wide), lambda n, o: (0, n))] * (chips * CORES)
        + [
            pl.BlockSpec((1, wide), lambda n, o: (0, n)),
            pl.BlockSpec((1, rank, wide), lambda n, o: (0, 0, n)),
        ],
        [shape((share, width), LOW)] * (chips * CORES)
        + [shape((1, width), F32), shape((1, rank, width), F32)],
        scratch=[pltpu.VMEM((rows + rank, inner), LOW)],
        prefetch=(order,),
        flops=2 * rows * inner * width,
    )
    return results[: chips * CORES], results[-2], results[-1]


def row_call(name, kernel, order, given, whole, out_kinds, sums):
    share = min(v.shape[0] for v, _ in given)
    width = given[0][0].shape[1]
    halves = 2
    half = share // halves
    count = len(given)

    def run(order_ref, *refs):
        sources, rest = refs[:count], refs[count : -count - 1]
        held, sems = refs[-count - 1 : -1], refs[-1]

        def copies(part):
            for i, ((_, cut), source, target) in enumerate(zip(given, sources, held)):
                at = part * half
                if cut:
                    at = pl.multiple_of(order_ref[1] * share + at, half)
                yield pltpu.make_async_copy(
                    source.at[pl.ds(at, half), :],
                    target.at[pl.ds(part * half, half), :],
                    sems.at[part, i],
                )

        for part in range(halves):

            @pl.when(pl.program_id(0) == part)
            def _(part=part):
                if part == 0:
                    for each in range(halves):
                        for copy in copies(each):
                            copy.start()
                for copy in copies(part):
                    copy.wait()

        at = pl.ds(pl.multiple_of(pl.program_id(0) * half, half), half)
        kernel([ref[at, :].astype(F32) for ref in held], *rest)

    line = pl.BlockSpec((1, width), lambda i, o: (0, 0))
    return call(
        name,
        run,
        (*[v for v, _ in given], *whole),
        (halves,),
        [pl.BlockSpec(memory_space=pl.ANY) for _ in given] + [line for _ in whole],
        [pl.BlockSpec((half, width), lambda i, o: (i, 0)) for _ in out_kinds]
        + [line for _ in range(sums)],
        [shape((share, width), kind) for kind in out_kinds]
        + [shape((1, width), F32) for _ in range(sums)],
        scratch=[pltpu.VMEM((share, width), v.dtype) for v, _ in given]
        + [pltpu.SemaphoreType.DMA((halves, count))],
        prefetch=(order,),
        flops=20 * share * width,
    )


def sum_of(values):
    total = values[0]
    for value in values[1:]:
        total = total + value
    return total


def add_column(ref, values):
    part = jnp.sum(values, axis=0, keepdims=True)

    @pl.when(pl.program_id(0) == 0)
    def _():
        ref[...] = part

    @pl.when(pl.program_id(0) > 0)
    def _():
        ref[...] += part


def hidden_kernel(given, squares_ref, magnitude_ref, gain_ref, hidden_ref, normed_ref):
    hidden = given[0] + sum_of(given[1:]) * (magnitude_ref[...] / jnp.sqrt(squares_ref[...]))
    hidden_ref[...] = hidden
    normed_ref[...] = (hidden * rms_rows(hidden) * gain_ref[...]).astype(LOW)


def mixed_kernel(given, squares_ref, magnitude_ref, mixed_ref):
    scale = magnitude_ref[...] / jnp.sqrt(squares_ref[...])
    mixed_ref[...] = (given[0] + sum_of(given[1:]) * scale).astype(LOW)


def norm_back(grad_normed, values, gain):
    factor = rms_rows(values)
    scaled = grad_normed * gain
    inner = jnp.mean(scaled * values, axis=1, keepdims=True)
    back = factor * scaled - values * (factor * factor * factor * inner)
    return back, grad_normed * values * factor


def hidden_back_kernel(
    given, squares_ref, magnitude_ref, gain_ref, grad_ref, low_ref, total_ref, gain_grad_ref
):
    cot, token, hidden = given[:3]
    back, gain_terms = norm_back(sum_of(given[3:]), hidden, gain_ref[...])
    grad = cot + back
    grad_ref[...] = grad
    scale = magnitude_ref[...] / jnp.sqrt(squares_ref[...])
    low_ref[...] = (grad * scale).astype(LOW)
    add_column(total_ref, grad * ((hidden - token) / scale))
    add_column(gain_grad_ref, gain_terms)


def token_back_kernel(given, gain_ref, out_ref, gain_grad_ref):
    back, gain_terms = norm_back(sum_of(given[2:]), given[0], gain_ref[...])
    out_ref[...] = given[1] + back
    add_column(gain_grad_ref, gain_terms)


def shrink_back_kernel(order_ref, cot_ref, low_ref, squares_ref, magnitude_ref, product_ref, grad_ref):
    scale = magnitude_ref[0] / jnp.sqrt(squares_ref[0])
    grad = (cot_ref[...].astype(F32) * scale).astype(LOW)
    grad_ref[0] = grad
    product_ref[0] = dot(grad, low_ref[0], NT)


def shrink_back(order, cotangent, low, squares, magnitude, groups):
    rows, width = cotangent.shape
    share, inner = rows // groups, low.shape[1]
    line = pl.BlockSpec((1, 1, width), lambda j, o: (0, 0, 0))
    return call(
        "shrink_back",
        shrink_back_kernel,
        (cotangent, low, squares, magnitude),
        (groups,),
        [
            pl.BlockSpec((share, width), lambda j, o: (o[j], 0)),
            pl.BlockSpec((1, inner, width), lambda j, o: (0, 0, 0)),
            line,
            line,
        ],
        [
            pl.BlockSpec((1, share, inner), lambda j, o: (j, 0, 0)),
            pl.BlockSpec((1, share, width), lambda j, o: (j, 0, 0)),
        ],
        [shape((groups, share, inner), F32), shape((groups, share, width), LOW)],
        prefetch=(order,),
        flops=2 * rows * width * inner,
    )


def expand_kernel(first, last, n_totals, ff, *refs):
    other_ref, mine_ref, low_ref, squares_ref, magnitude_ref, grad_ref = refs[:6]
    refs = list(refs[6:])
    left_ref = refs.pop(0) if first else None
    right_ref = refs.pop(0) if last else None
    before = [refs.pop(0) for _ in range(n_totals)]
    product_ref, back_ref, total_ref, rows_ref, send_ref, keep_ref = refs[:6]
    refs = refs[6:]
    across_ref = refs.pop(0) if first else None
    extra_ref = refs.pop(0) if last else None
    rows_all, back_all, mid_sum = refs
    share, depth = other_ref.shape
    wide = low_ref.shape[2]
    both = CORES * share

    @pl.when(pl.program_id(0) == 0)
    def _():
        for at, ref in ((0, other_ref), (share, mine_ref)):
            rows_ref[at : at + share, :] = ref[...]
            rows_all[at : at + share, :] = ref[...]
        if first:
            rank = across_ref.shape[1]
            for m in range(2):
                rows_all[both + m * rank : both + (m + 1) * rank, :] = left_ref[m].astype(LOW)
        mid_sum[...] = jnp.zeros_like(mid_sum)

    lane = pl.program_id(0) * wide + lax.broadcasted_iota(jnp.int32, (1, wide), 1)
    magnitude = [jnp.where(lane < ff, magnitude_ref[m : m + 1], 0.0) for m in range(2)]
    scale = [magnitude[m] / jnp.sqrt(squares_ref[m]) for m in range(2)]
    totals = [jnp.zeros((1, wide), F32) for _ in range(2)]
    pre = [dot(rows_all[...], low_ref[m]) for m in range(2)]
    if first:
        across_ref[0] = pre[0][both : both + rank_of(across_ref)]
        across_ref[1] = pre[1][both + rank_of(across_ref) :]
    for place in range(CORES):
        rows = slice(place * share, (place + 1) * share)
        gate_pre, up_pre = pre[0][rows], pre[1][rows]
        gate, up = gate_pre * scale[0], up_pre * scale[1]
        sigmoid = 0.5 + 0.5 * jnp.tanh(0.5 * gate)
        active = gate * sigmoid
        product_ref[0, place] = (active * up).astype(LOW)
        upper = grad_ref[place]
        grad_up = upper * active
        grad_gate = upper * up * sigmoid * (1.0 + gate * (1.0 - sigmoid))
        totals[0] += jnp.sum(grad_gate * gate_pre, axis=0, keepdims=True)
        totals[1] += jnp.sum(grad_up * up_pre, axis=0, keepdims=True)
        for m, grad in enumerate((grad_gate, grad_up)):
            low = (grad * scale[m]).astype(LOW)
            back_ref[m, place] = low
            back_all[rows, m * wide : (m + 1) * wide] = low
    for m in range(2):
        total_ref[m] = totals[m]
    if last:
        rank = rank_of(extra_ref)
        for m in range(2):
            total = totals[m]
            for ref in before:
                total = total + ref[m]
            right = jnp.where(lane < ff, right_ref[m], 0.0)
            weighted = right * norm_weight(total, squares_ref[m], magnitude[m])
            rows = slice(both + m * rank, both + (m + 1) * rank)
            back_all[rows, m * wide : (m + 1) * wide] = weighted.astype(LOW)
            back_all[rows, (1 - m) * wide : (2 - m) * wide] = jnp.zeros((rank, wide), LOW)
    step = tile_of(depth, 512)
    for at in range(0, depth, step):
        columns = slice(at, at + step)
        weights = jnp.concatenate([low_ref[0, columns, :], low_ref[1, columns, :]], axis=1)
        mid_sum[:, columns] += dot(back_all[...], weights, NT)

    @pl.when(pl.program_id(0) == pl.num_programs(0) - 1)
    def _():
        send_ref[...] = mid_sum[:share, :].astype(LOW)
        keep_ref[...] = mid_sum[share:both, :].astype(LOW)
        if last:
            for m in range(2):
                extra_ref[m] = mid_sum[both + m * rank_of(extra_ref) : both + (m + 1) * rank_of(extra_ref), :]


def rank_of(ref):
    return ref.shape[1]


def expand(pieces, low, squares, magnitude, grad_product, step, left=None, right=None, before=()):
    share, depth = pieces[0].shape
    width = low.shape[2]
    first, last = left is not None, right is not None
    wide = 256
    rows = CORES * share
    fixed = lambda dims: pl.BlockSpec(tuple(dims), lambda n: (0,) * len(dims))
    column = pl.BlockSpec((2, 1, wide), lambda n: (0, 0, n))
    operands = [*pieces, low, squares, magnitude, grad_product]
    in_specs = [
        fixed((share, depth)),
        fixed((share, depth)),
        pl.BlockSpec((2, depth, wide), lambda n: (0, 0, n)),
        column,
        pl.BlockSpec((2, wide), lambda n: (0, n)),
        pl.BlockSpec((2, share, wide), lambda n: (step, 0, n)),
    ]
    out_specs = [
        pl.BlockSpec((1, 2, share, wide), lambda n: (0, 0, 0, n)),
        pl.BlockSpec((2, 2, share, wide), lambda n: (0, 0, 0, n)),
        column,
        fixed((rows, depth)),
        fixed((share, depth)),
        fixed((share, depth)),
    ]
    out_shape = [
        shape((1, 2, share, width), LOW),
        shape((2, 2, share, width), LOW),
        shape((2, 1, width), F32),
        shape((rows, depth), LOW),
        shape((share, depth), LOW),
        shape((share, depth), LOW),
    ]
    extra_in = extra_out = 0
    if first:
        rank = left.shape[1]
        extra_in = 2 * rank
        operands.append(left)
        in_specs.append(fixed(left.shape))
        out_specs.append(pl.BlockSpec((2, rank, wide), lambda n: (0, 0, n)))
        out_shape.append(shape((2, rank, width), F32))
    if last:
        rank = right.shape[1]
        extra_out = 2 * rank
        operands += [right, *before]
        in_specs.append(pl.BlockSpec((2, rank, wide), lambda n: (0, 0, n)))
        in_specs += [column for _ in before]
        out_specs.append(fixed((2, rank, depth)))
        out_shape.append(shape((2, rank, depth), F32))
    return call(
        "expand",
        functools.partial(expand_kernel, first, last, len(before), magnitude.shape[1]),
        tuple(operands),
        (width // wide,),
        in_specs,
        out_specs,
        out_shape,
        scratch=[
            pltpu.VMEM((rows + extra_in, depth), LOW),
            pltpu.VMEM((rows + extra_out, 2 * wide), LOW),
            pltpu.VMEM((rows + extra_out, depth), F32),
        ],
        flops=8 * rows * depth * width,
    )


def adapter_kernel(views, n_inputs, n_grads, n_totals, has_low, order_ref, *refs):
    inputs, grads = refs[:n_inputs], refs[n_inputs : n_inputs + n_grads]
    rest = refs[n_inputs + n_grads :]
    back_ref, across_ref, left_ref, right_ref, squares_ref, magnitude_ref = rest[:6]
    totals, (left_out, right_out, magnitude_out) = rest[6 : 6 + n_totals], rest[6 + n_totals :]
    members, rank, _ = right_ref.shape
    width = right_ref.shape[2]
    total = sum_refs(totals)[:, :, :width]
    squares = squares_ref[:, :, :width]
    weight = [
        norm_weight(total[m], squares[m], magnitude_ref[m : m + 1]) for m in range(members)
    ]
    magnitude_out[...] = total / jnp.sqrt(squares)
    left_rows = jnp.concatenate([split_rows(left_ref[m]) for m in range(members)], axis=0)
    right_rows = [split_rows(right_ref[m]) for m in range(members)]
    for m in range(members):
        if has_low:
            low = back_ref[m, : left_ref.shape[2], :]
            left_out[m] = -fold(dot(split_rows(right_ref[m] * weight[m]), low, NT))
        else:
            left_out[m] = -back_ref[m]
        right_out[m] = -(across_ref[m][:, :width] * weight[m])
    for taken, grads_of in views(order_ref, inputs, grads):
        across = dot(left_rows, taken, NT)
        downs = []
        for m in range(members):
            grad = grads_of(m)
            mine = split_rows(fold(across[2 * rank * m : 2 * rank * (m + 1)]))
            right_out[m] += fold(dot(mine, grad))
            downs.append(split_rows(fold(dot(right_rows[m], grad, NT))))
        left = dot(jnp.concatenate(downs, axis=0), taken)
        for m in range(members):
            left_out[m] += fold(left[2 * rank * m : 2 * rank * (m + 1)])
    for m in range(members):
        left_out[m] = ADAPT_SCALE * left_out[m]
        right_out[m] = ADAPT_SCALE * right_out[m]


def adapter(name, order, views, inputs, grads, back, across, left, right, totals, squares, magnitude):
    members, rank, width = right.shape
    depth = left.shape[2]
    operands = (*inputs, *grads, back, across, left, right, squares, magnitude, *totals)
    full = lambda dims: pl.BlockSpec(tuple(dims), lambda i, o: (0,) * len(dims))
    outs = [(members, rank, depth), (members, rank, width), (members, 1, width)]
    rows = sum(v.size // v.shape[-1] for v in inputs)
    return call(
        name,
        functools.partial(
            adapter_kernel, views, len(inputs), len(grads), len(totals), back.dtype == LOW
        ),
        operands,
        (1,),
        [full(v.shape) for v in operands],
        [full(dims) for dims in outs],
        [shape(dims, F32) for dims in outs],
        prefetch=(order,),
        flops=8 * members * rows * width * 32,
    )


MESH_IDS = pl.DeviceIdType.MESH


def copy_kernel(count, *refs):
    for source, target in zip(refs[:count], refs[count:]):
        target[...] = source[...]


def copy_out(arrays):
    vmem = pl.BlockSpec(memory_space=pltpu.VMEM)
    full = lambda v: pl.BlockSpec(v.shape, lambda i: (0,) * v.ndim)
    return call(
        "copy_out",
        functools.partial(copy_kernel, len(arrays)),
        tuple(arrays),
        (1,),
        [vmem for _ in arrays],
        [full(v) for v in arrays],
        [shape(v.shape, F32) for v in arrays],
        mib=16,
    )


GRAIN = 16


def pieces_of(width):
    return [(at, min(128, width - at)) for at in range(0, width, 128)]


def cells_of(blocks, lines, parts):
    cells, rows = [], []
    for n, block in enumerate(blocks):
        for m in range(block.shape[0]):
            for at, size in pieces_of(block.shape[2] // parts):
                cells.append((n, m, at, size))
    for n, line in enumerate(lines):
        for m in range(line.shape[0]):
            for at, size in pieces_of(line.shape[2] // parts):
                rows.append((n, m, at, size))
    return cells, rows


def pack(blocks, lines, wide_ref, part, parts, cells, rows):
    for i, (n, m, at, size) in enumerate(cells):
        start = part * (blocks[n].shape[2] // parts) + at
        wide_ref[part, i, :, :size] = blocks[n][m, :, start : start + size]
    for i, (n, m, at, size) in enumerate(rows):
        start = part * (lines[n].shape[2] // parts) + at
        cell, row = len(cells) + i // GRAIN, i % GRAIN
        wide_ref[part, cell, row : row + 1, :size] = lines[n][m, :, start : start + size]


def unpack(full_ref, blocks, lines, part, parts, cells, rows):
    for i, (n, m, at, size) in enumerate(cells):
        start = part * (blocks[n].shape[2] // parts) + at
        blocks[n][m, :, start : start + size] = full_ref[part, i].astype(F32)[:, :size]
    for i, (n, m, at, size) in enumerate(rows):
        start = part * (lines[n].shape[2] // parts) + at
        cell, row = len(cells) + i // GRAIN, i % GRAIN
        values = full_ref[part, cell].astype(F32)
        lines[n][m, :, start : start + size] = values[row : row + 1, :size]


def reduce_kernel(groups, lines, counts, *refs):
    n_all, n_all_lines, n_dp, n_dp_lines = counts
    count = sum(counts)
    taken, given, scratch = refs[:count], refs[count : 2 * count], refs[2 * count :]
    ends = [n_all, n_all + n_all_lines, n_all + n_all_lines + n_dp]
    parted = lambda v: (v[: ends[0]], v[ends[0] : ends[1]], v[ends[1] : ends[2]], v[ends[2] :])
    all_in, all_lines_in, dp_in, dp_lines_in = parted(taken)
    all_out, all_lines_out, dp_out, dp_lines_out = parted(given)
    (
        all_ref,
        line_ref,
        all_low,
        line_low,
        all_got,
        part,
        part_low,
        part_got,
        line_got,
        all_full,
        line_full,
        *sems,
    ) = scratch
    me, row = lax.axis_index("mp"), lax.axis_index("dp")
    piece, line_piece = part.shape[0] // lines, line_ref.shape[1] // lines
    mp_peer = [lax.rem(me + k, groups) for k in range(groups)]
    dp_peer = [lax.rem(row + k, lines) for k in range(lines)]
    barrier = pltpu.get_barrier_semaphore()
    for k in range(1, groups):
        pl.semaphore_signal(barrier, 1, device_id={"mp": mp_peer[k]}, device_id_type=MESH_IDS)
    for k in range(1, lines):
        pl.semaphore_signal(barrier, 1, device_id={"dp": dp_peer[k]}, device_id_type=MESH_IDS)
    all_cells = cells_of(all_in, all_lines_in, groups)
    dp_cells = cells_of(dp_in, dp_lines_in, 1)
    all_ref[...] = jnp.zeros_like(all_ref)
    line_ref[...] = jnp.zeros_like(line_ref)
    for q in range(groups):
        pack(all_in, all_lines_in, all_ref, q, groups, *all_cells)
    pack(dp_in, dp_lines_in, line_ref, 0, 1, *dp_cells)
    all_low[...] = all_ref[...].astype(LOW)
    line_low[...] = line_ref[...].astype(LOW)
    pl.semaphore_wait(barrier, groups + lines - 2)

    def send(source, target, stage, k, axis, peer):
        copy = pltpu.make_async_remote_copy(
            src_ref=source,
            dst_ref=target,
            send_sem=sems[2 * stage].at[k],
            recv_sem=sems[2 * stage + 1].at[k],
            device_id={axis: peer},
            device_id_type=MESH_IDS,
        )
        copy.start()
        return copy

    over_mp = [
        send(all_low.at[mp_peer[k]], all_got.at[k], 0, k, "mp", mp_peer[k])
        for k in range(1, groups)
    ]
    over_dp = [
        send(
            line_low.at[0, pl.ds(dp_peer[k] * line_piece, line_piece)],
            line_got.at[k],
            1,
            k,
            "dp",
            dp_peer[k],
        )
        for k in range(1, lines)
    ]
    total = all_ref[me]
    for k, copy in enumerate(over_mp, 1):
        copy.wait_recv()
        total = total + all_got[k].astype(F32)
    part[...] = total
    part_low[...] = total.astype(LOW)
    part_dp = [
        send(part_low.at[pl.ds(dp_peer[k] * piece, piece)], part_got.at[k], 2, k, "dp", dp_peer[k])
        for k in range(1, lines)
    ]
    mine = pl.ds(row * line_piece, line_piece)
    total = line_ref[0, mine]
    for k, copy in enumerate(over_dp, 1):
        copy.wait_recv()
        total = total + line_got[k].astype(F32)
    line_full[0, mine] = total.astype(LOW)
    line_back = [
        send(line_full.at[0, mine], line_full.at[0, mine], 3, k, "dp", dp_peer[k])
        for k in range(1, lines)
    ]
    held = pl.ds(row * piece, piece)
    total = part[held]
    for k, copy in enumerate(part_dp, 1):
        copy.wait_recv()
        total = total + part_got[k].astype(F32)
    all_full[me, held] = total.astype(LOW)
    part_back = [
        send(all_full.at[me, held], all_full.at[me, held], 4, k, "dp", dp_peer[k])
        for k in range(1, lines)
    ]
    for copy in part_back:
        copy.wait_recv()
    all_back = [
        send(all_full.at[me], all_full.at[me], 5, k, "mp", mp_peer[k]) for k in range(1, groups)
    ]
    for copy in line_back:
        copy.wait_recv()
    unpack(line_full, dp_out, dp_lines_out, 0, 1, *dp_cells)
    for copy in all_back:
        copy.wait_recv()
    for q in range(groups):
        unpack(all_full, all_out, all_lines_out, q, groups, *all_cells)
    for copy in over_mp + over_dp + part_dp + line_back + part_back + all_back:
        copy.wait_send()


def reduce_devices(name, identity, over_all, over_all_lines, over_dp, over_dp_lines):
    groups, lines = lax.axis_size("mp"), lax.axis_size("dp")

    def size_of(blocks, rows, parts):
        cells, lines_in = cells_of(blocks, rows, parts)
        size = len(cells) + -(-len(lines_in) // GRAIN)
        return -(-size // lines) * lines

    count, line_count = size_of(over_all, over_all_lines, groups), size_of(over_dp, over_dp_lines, 1)
    operands = (*over_all, *over_all_lines, *over_dp, *over_dp_lines)
    counts = (len(over_all), len(over_all_lines), len(over_dp), len(over_dp_lines))
    vmem = pl.BlockSpec(memory_space=pltpu.VMEM)
    tail = (GRAIN, 128)
    sizes = (groups, lines, lines, lines, lines, groups)
    every, line = (groups, count) + tail, (1, line_count) + tail
    results = pl.pallas_call(
        functools.partial(reduce_kernel, groups, lines, counts),
        name=name,
        out_shape=[shape(v.shape, F32) for v in operands],
        in_specs=[vmem for _ in operands],
        out_specs=[vmem for _ in operands],
        scratch_shapes=[
            pltpu.VMEM(every, F32),
            pltpu.VMEM(line, F32),
            pltpu.VMEM(every, LOW),
            pltpu.VMEM(line, LOW),
            pltpu.VMEM(every, LOW),
            pltpu.VMEM((count,) + tail, F32),
            pltpu.VMEM((count,) + tail, LOW),
            pltpu.VMEM((lines, count // lines) + tail, LOW),
            pltpu.VMEM((lines, line_count // lines) + tail, LOW),
            pltpu.VMEM(every, LOW),
            pltpu.VMEM(line, LOW),
        ]
        + [pltpu.SemaphoreType.DMA((n,)) for n in sizes for _ in range(2)],
        compiler_params=pltpu.CompilerParams(
            collective_id=identity, has_side_effects=True, vmem_limit_bytes=32 * 2**20
        ),
        cost_estimate=pl.CostEstimate(flops=1000, bytes_accessed=2**20, transcendentals=0),
    )(*operands)
    return copy_out(results)


def geometry(segment):
    length = segment.shape[0]
    places = lax.broadcasted_iota(jnp.int32, (length, length), 0)
    others = lax.broadcasted_iota(jnp.int32, (length, length), 1)
    visible = (segment[:, None] == segment[None, :]) & (others <= places)
    offset = jnp.sum(visible.astype(F32), axis=1) - 1.0
    lane = jnp.arange(HEAD_DIM, dtype=jnp.int32)
    half = (lane % (HEAD_DIM // 2)).astype(F32)
    frequency = jnp.exp(-jnp.log(ROPE_BASE) * 2.0 * half / HEAD_DIM)
    sign = jnp.where(lane < HEAD_DIM // 2, -1.0, 1.0)
    angles = offset[:, None] * frequency[None, :]
    first = jnp.arange(length, dtype=jnp.int32) - offset.astype(jnp.int32)
    return first[:, None], jnp.cos(angles), jnp.sin(angles) * sign[None, :]


def body(
    tokens,
    cotangent,
    segment_ids,
    attend_gain,
    expand_gain,
    heads_base,
    heads_left,
    heads_right,
    heads_magnitude,
    output_base,
    output_left,
    output_right,
    output_magnitude,
    expand_base,
    expand_left,
    expand_right,
    expand_magnitude,
    shrink_base,
    shrink_left,
    shrink_right,
    shrink_magnitude,
):
    groups = lax.axis_size("mp")
    chips = groups // CORES
    index = lax.axis_index("mp")
    chip, core = index // CORES, index % CORES
    rows, width = tokens.shape
    share = rows // groups
    local_heads, ff = heads_base.shape[2], expand_base.shape[2]
    ff_wide = padded(ff)
    device = jnp.arange(groups, dtype=jnp.int32)
    order = jnp.concatenate(
        [
            (chip + device // CORES) % chips * CORES + (core + 1 + device) % CORES,
            (device // CORES + chips - chip) % chips * CORES + (device + CORES - core + 1) % CORES,
        ]
    ).astype(jnp.int32)

    def tie(*values):
        return lax.optimization_barrier(values)

    def sibling(values):
        return lax.ppermute(
            values, "mp", [(i, i // CORES * CORES + (i + 1) % CORES) for i in range(groups)]
        )

    def to_chip(values, step):
        return lax.ppermute(
            values,
            "mp",
            [((i, ((i // CORES + step) % chips) * CORES + i % CORES)) for i in range(groups)],
        )

    def mp_sum(values):
        values = values + sibling(values)
        total = values
        for step in range(1, chips):
            total = total + to_chip(values, step)
        return total

    def join(pair):
        return (pair[1].astype(F32) + sibling(pair[0]).astype(F32)).astype(LOW)

    def chip_pairs(places):
        return [places[CORES * step : CORES * (step + 1)] for step in range(chips)]

    def arrive(own):
        return [to_chip(own, chips - step) for step in range(1, chips)]

    def pairs_of(own, near_sibling, arrived):
        return [(near_sibling, own)] + [(sibling(piece), piece) for piece in arrived]

    def in_pairs(order_ref, inputs, grads):
        for taken, grad in zip(inputs, grads):
            yield taken[...], lambda m, grad=grad: grad[m].reshape(-1, grad.shape[-1])[:, :ff]

    def in_shrink(order_ref, inputs, grads):
        for step, taken in enumerate(inputs):
            at = slice(CORES * step, CORES * (step + 1))
            yield (
                taken[0].reshape(-1, taken.shape[-1])[:, :ff],
                lambda m, at=at: grads[0][at].reshape(-1, grads[0].shape[-1]),
            )

    def in_output(order_ref, inputs, grads):
        for place, grad in enumerate(grads):
            yield inputs[0][0, place], lambda m, grad=grad: grad[...]

    def in_heads(order_ref, inputs, grads):
        for place in range(groups):
            at = pl.multiple_of(order_ref[place] * share, share)
            rows = slice(place * share, (place + 1) * share)
            yield inputs[0][pl.ds(at, share), :], lambda m, rows=rows: grads[0][m, rows, :]

    heads_rows, output_rows = turned(heads_left), turned(output_left[None])
    expand_rows, shrink_rows = turned(expand_left), turned(shrink_left[None])
    heads_mag, output_mag = heads_magnitude, output_magnitude[None]
    expand_mag, shrink_mag = expand_magnitude, shrink_magnitude[None]
    attend_line, expand_line = attend_gain[None], expand_gain[None]

    output_low, output_part = merge(
        output_base[None], output_rows, output_right[None], output_base.shape[0], 512
    )
    shrink_low, shrink_part = merge(
        shrink_base[None], shrink_rows, shrink_right[None], shrink_base.shape[0], 512
    )
    tokens, output_part, shrink_part = lax.optimization_barrier((tokens, output_part, shrink_part))
    squares = mp_sum(jnp.concatenate([output_part, shrink_part], axis=1))
    output_sq, shrink_sq = squares[:, :1], squares[:, 1:]

    first, cos_table, sine_table = geometry(segment_ids.reshape(-1))
    normed, heads_low, post, heads_sq, heads_across = project_heads(
        tokens,
        attend_line,
        heads_base,
        heads_rows,
        heads_right,
        heads_mag,
        cos_table,
        sine_table,
    )
    heads_out = attend(order, groups, post, first)
    heads_parts = heads_out.reshape(1, groups, share, local_heads)
    output_places, output_across = product(
        "output_product", heads_parts, output_low, NN, left=output_rows
    )
    output_pairs = chip_pairs(output_places)
    joined = [join(pair) for pair in output_pairs[1:]]
    joined, expand_right_tied = tie(joined, expand_right)
    output_arrived = [to_chip(values, step) for step, values in enumerate(joined, 1)]
    expand_low, expand_sq = merge(
        expand_base, expand_rows, expand_right_tied, 512, expand_base.shape[2]
    )
    grad_product, shrink_grad = shrink_back(
        order, cotangent, shrink_low, shrink_sq, shrink_mag[None], groups
    )
    output_parts = [output_pairs[0][1], sibling(output_pairs[0][0]), *output_arrived]
    output_parts, expand_low, grad_product = tie(output_parts, expand_low, grad_product)
    hidden, normed_own = row_call(
        "hidden",
        hidden_kernel,
        order,
        [(tokens, True)] + [(part, False) for part in output_parts],
        (output_sq[0], output_mag, expand_line),
        (F32, LOW),
        0,
    )

    def feed(pieces, step, **extra):
        return expand(pieces, expand_low, expand_sq, expand_mag, grad_product, step, **extra)

    arrived, near_sibling = arrive(normed_own), sibling(normed_own)
    fed = [feed((near_sibling, normed_own), 0, left=expand_rows)]
    arrived, fed = tie(arrived, fed)
    fed = list(fed)
    mid_sibling = sibling(fed[0][4])
    normed_mid = pairs_of(normed_own, near_sibling, arrived)
    for step in range(1, chips):
        extra = {}
        if step == chips - 1:
            extra = {"right": expand_right, "before": [f[2] for f in fed]}
        fed.append(feed(normed_mid[step], step, **extra))
    expand_totals = [f[2] for f in fed]
    joined = [join(f[4:6]) for f in fed[1:]]
    joined, shrink_rows_tied = tie(joined, shrink_rows)
    mid_arrived = [to_chip(values, step) for step, values in enumerate(joined, 1)]
    shrink_places, shrink_total, shrink_across = shrink_product(
        order, [f[0] for f in fed], shrink_low, shrink_rows_tied, cotangent
    )
    shrink_pairs = chip_pairs(shrink_places)
    shrink_total = mp_sum(shrink_total)
    shrink_joined = [join(pair) for pair in shrink_pairs[1:]]
    mid_parts = [fed[0][5], mid_sibling, *mid_arrived]
    mid_parts, shrink_pairs, shrink_joined, shrink_total = tie(
        mid_parts, shrink_pairs, shrink_joined, shrink_total
    )
    grad_hidden, output_grad_own, output_total, expand_gain_part = row_call(
        "hidden_back",
        hidden_back_kernel,
        order,
        [(cotangent, True), (tokens, True), (hidden, False)]
        + [(part, False) for part in mid_parts],
        (output_sq[0], output_mag, expand_line),
        (F32, LOW),
        2,
    )
    arrived, near_sibling = arrive(output_grad_own), sibling(output_grad_own)
    output_total = mp_sum(output_total)
    expand_adapter = adapter(
        "expand_adapter",
        order,
        in_pairs,
        [f[3] for f in fed],
        [f[1] for f in fed],
        fed[-1][6],
        fed[0][6],
        expand_rows,
        expand_right,
        expand_totals,
        expand_sq,
        expand_mag,
    )
    shrink_adapter = adapter(
        "shrink_adapter",
        order,
        in_shrink,
        [f[0] for f in fed],
        [shrink_grad],
        shrink_low,
        shrink_across,
        shrink_rows,
        shrink_right[None],
        [shrink_total[None]],
        shrink_sq,
        shrink_mag,
    )
    arrived, near_sibling, output_total, shrink_joined, expand_adapter, shrink_adapter = tie(
        arrived, near_sibling, output_total, shrink_joined, expand_adapter, shrink_adapter
    )
    output_grad = [
        piece for pair in pairs_of(output_grad_own, near_sibling, arrived) for piece in pair
    ]
    shrink_parts = [shrink_pairs[0][1], sibling(shrink_pairs[0][0])] + [
        to_chip(values, step) for step, values in enumerate(shrink_joined, 1)
    ]
    heads_grads, heads_total = attend_back(
        order,
        groups,
        post,
        first,
        cos_table,
        sine_table,
        heads_mag,
        heads_sq,
        output_low,
        output_grad,
    )
    heads_grads, shrink_parts = tie(heads_grads, shrink_parts)
    grad_parts = heads_grads.reshape(3, groups, share, local_heads)
    token_places, token_extra = product(
        "normed_product",
        grad_parts,
        heads_low,
        NT,
        correction=(heads_right, heads_sq, heads_mag, [heads_total]),
    )
    token_pairs = chip_pairs(token_places)
    joined = [join(pair) for pair in token_pairs[1:]]
    joined, heads_rows_tied, output_rows_tied = tie(joined, heads_rows, output_rows)
    token_arrived = [to_chip(values, step) for step, values in enumerate(joined, 1)]
    output_adapter = adapter(
        "output_adapter",
        order,
        in_output,
        [heads_parts],
        output_grad,
        output_low,
        output_across,
        output_rows_tied,
        output_right[None],
        [output_total[None]],
        output_sq,
        output_mag,
    )
    heads_adapter = adapter(
        "heads_adapter",
        order,
        in_heads,
        [normed],
        [heads_grads],
        token_extra,
        heads_across,
        heads_rows_tied,
        heads_right,
        [heads_total],
        heads_sq,
        heads_mag,
    )
    (mixed,) = row_call(
        "mixed",
        mixed_kernel,
        order,
        [(hidden, False)] + [(part, False) for part in shrink_parts],
        (shrink_sq[0], shrink_mag),
        (LOW,),
        0,
    )
    token_parts = [token_pairs[0][1], sibling(token_pairs[0][0]), *token_arrived]
    token_parts, output_adapter, heads_adapter, mixed = tie(
        token_parts, output_adapter, heads_adapter, mixed
    )
    grad_tokens, attend_gain_part = row_call(
        "token_back",
        token_back_kernel,
        order,
        [(tokens, True), (grad_hidden, False)] + [(part, False) for part in token_parts],
        (attend_line,),
        (F32,),
        1,
    )
    (
        expand_left_grad,
        shrink_right_grad,
        heads_left_grad,
        output_right_grad,
        expand_gain_grad,
        attend_gain_grad,
        expand_right_grad,
        shrink_left_grad,
        heads_right_grad,
        output_left_grad,
        expand_mag_grad,
        shrink_mag_grad,
        heads_mag_grad,
        output_mag_grad,
    ) = reduce_devices(
        "reduce_gradients",
        1,
        [expand_adapter[0], shrink_adapter[1], heads_adapter[0], output_adapter[1]],
        [expand_gain_part[None], attend_gain_part[None]],
        [expand_adapter[1], shrink_adapter[0], heads_adapter[1], output_adapter[0]],
        [expand_adapter[2], shrink_adapter[2], heads_adapter[2], output_adapter[2]],
    )
    return (
        mixed,
        grad_tokens,
        attend_gain_grad[0, 0],
        expand_gain_grad[0, 0],
        jnp.swapaxes(heads_left_grad, 1, 2),
        heads_right_grad,
        heads_mag_grad[:, 0],
        output_left_grad[0].T,
        output_right_grad[0],
        output_mag_grad[0, 0],
        jnp.swapaxes(expand_left_grad, 1, 2),
        expand_right_grad,
        expand_mag_grad[:, 0],
        shrink_left_grad[0].T,
        shrink_right_grad[0],
        shrink_mag_grad[0, 0],
    )


def solution(mesh):
    placed = (
        P("dp", None),
        P("dp", None),
        P("dp", None),
        P(),
        P(),
        P(None, None, "mp"),
        P(),
        P(None, None, "mp"),
        P(None, "mp"),
        P("mp", None),
        P("mp", None),
        P(),
        P(),
        P(None, None, "mp"),
        P(),
        P(None, None, "mp"),
        P(None, "mp"),
        P("mp", None),
        P("mp", None),
        P(),
        P(),
    )
    return jax.shard_map(
        body,
        mesh=mesh,
        in_specs=placed,
        out_specs=(
            P(("dp", "mp"), None),
            P(("dp", "mp"), None),
            P(),
            P(),
            P(),
            P(None, None, "mp"),
            P(None, "mp"),
            P("mp", None),
            P(),
            P(),
            P(),
            P(None, None, "mp"),
            P(None, "mp"),
            P("mp", None),
            P(),
            P(),
        ),
        check_vma=False,
    )
```

```python
import functools

import jax
import jax.numpy as jnp
import ml_dtypes
import numpy as np
from jax import lax
from jax.experimental import pallas as pl
from jax.experimental.pallas import tpu as pltpu
from jax.sharding import PartitionSpec as P

HEAD_DIM = 128
CORES = 2
LONGEST = 512
ATTEND_BLOCK = 256
ADAPT_SCALE = 2.0
NORM_EPS = 1e-05
ROPE_BASE = 10000.0
MASKED = -1e30

F32 = jnp.float32
LOW = jnp.bfloat16
NN = (((1,), (0,)), ((), ()))
NT = (((1,), (1,)), ((), ()))
TN = (((0,), (0,)), ((), ()))


def dot(left, right, dims=NN):
    return lax.dot_general(left, right, dims, preferred_element_type=F32)


def shape(dims, kind):
    return jax.ShapeDtypeStruct(tuple(dims), kind)


def call(name, kernel, operands, grid, in_specs, out_specs, out_shape, scratch=(), prefetch=(), flops=0, mib=60):
    moved = sum(v.size * v.dtype.itemsize for v in operands)
    moved += sum(v.size * v.dtype.itemsize for v in out_shape)
    return pl.pallas_call(
        kernel,
        name=name,
        out_shape=out_shape,
        grid_spec=pltpu.PrefetchScalarGridSpec(
            num_scalar_prefetch=len(prefetch),
            grid=grid,
            in_specs=in_specs,
            out_specs=out_specs,
            scratch_shapes=scratch,
        ),
        compiler_params=pltpu.CompilerParams(vmem_limit_bytes=mib * 2**20),
        cost_estimate=pl.CostEstimate(flops=flops // 16, bytes_accessed=moved // 16, transcendentals=0),
    )(*prefetch, *operands)


def tile_of(size, most):
    return most if size % most == 0 else size


def split_rows(values):
    top = values.astype(LOW)
    rest = (values - top.astype(F32)).astype(LOW)
    return jnp.concatenate([top, rest], axis=0)


def turned(left_map):
    return jnp.swapaxes(left_map, -1, -2)


def norm_weight(total, squares, magnitude):
    norm = jnp.sqrt(squares)
    return total * magnitude / (norm * norm * norm)


def sum_refs(refs):
    total = refs[0][...]
    for ref in refs[1:]:
        total = total + ref[...]
    return total


def fold(values):
    half = values.shape[0] // 2
    return values[:half] + values[half:]


def merge_tile(base_at, low_put, left, right, depth):
    rank = right.shape[0]
    doubled = ADAPT_SCALE * right
    top = doubled.astype(LOW)
    rest = (doubled - top.astype(F32)).astype(LOW)
    right_stack = jnp.concatenate([top, rest, top], axis=0)
    left_pair = split_rows(left)
    left_stack = jnp.concatenate([left_pair[:rank], left_pair[:rank], left_pair[rank:]], axis=0)
    squares = jnp.zeros((1, right.shape[1]), F32)
    step = tile_of(depth, 1024)
    for start in range(0, depth, step):
        merged = base_at(start, step).astype(F32) + dot(
            left_stack[:, start : start + step], right_stack, TN
        )
        low_put(start, step, merged.astype(LOW))
        squares = squares + jnp.sum(merged * merged, axis=0, keepdims=True)
    return squares


def merge_kernel(base_ref, left_ref, right_ref, low_ref, squares_ref):
    depth, width = base_ref.shape[1:]
    if low_ref.shape[1] > depth:
        low_ref[0, depth:, :] = jnp.zeros((low_ref.shape[1] - depth, low_ref.shape[2]), LOW)
    if low_ref.shape[2] > width:
        spare = low_ref.shape[2] - width
        low_ref[0, :, width:] = jnp.zeros((low_ref.shape[1], spare), LOW)
        squares_ref[0, :, width:] = jnp.ones((1, spare), F32)

    def put(start, step, tile):
        low_ref[0, start : start + step, :width] = tile

    squares = merge_tile(
        lambda start, step: base_ref[0, start : start + step, :],
        put,
        left_ref[0],
        right_ref[0],
        depth,
    )

    @pl.when(pl.program_id(2) == 0)
    def _():
        squares_ref[0, :, :width] = squares

    @pl.when(pl.program_id(2) > 0)
    def _():
        squares_ref[0, :, :width] += squares


def padded(size):
    return -(-size // 256) * 256


def pad_last(values, size):
    return jnp.pad(values, [(0, 0)] * (values.ndim - 1) + [(0, size - values.shape[-1])])


def merge(base, left, right, deep, wide):
    members, depth, width = base.shape
    low_deep = padded(deep) if deep == depth else deep
    low_wide = padded(wide) if wide == width else wide
    low_shape = (members, depth // deep * low_deep, width // wide * low_wide)
    rank = right.shape[1]
    return call(
        "merge",
        merge_kernel,
        (base, left, right),
        (members, width // wide, depth // deep),
        [
            pl.BlockSpec((1, deep, wide), lambda m, n, k: (m, k, n)),
            pl.BlockSpec((1, rank, deep), lambda m, n, k: (m, 0, k)),
            pl.BlockSpec((1, rank, wide), lambda m, n, k: (m, 0, n)),
        ],
        [
            pl.BlockSpec((1, low_deep, low_wide), lambda m, n, k: (m, k, n)),
            pl.BlockSpec((1, 1, low_wide), lambda m, n, k: (m, 0, n)),
        ],
        [shape(low_shape, LOW), shape((members, 1, low_shape[2]), F32)],
        flops=2 * members * depth * width * 256,
    )


def rms_rows(values):
    return lax.rsqrt(jnp.mean(values * values, axis=1, keepdims=True) + NORM_EPS)


TABLE_STEP = 32


def table_pieces(places):
    half = np.arange(HEAD_DIM) % (HEAD_DIM // 2)
    angles = np.asarray(places)[:, None] * ROPE_BASE ** (-2.0 * half / HEAD_DIM)[None, :]
    rest = np.concatenate([np.cos(angles), np.sin(angles)], axis=1)
    pieces = []
    for _ in range(3):
        pieces.append(rest.astype(ml_dtypes.bfloat16))
        rest = rest - pieces[-1].astype(np.float64)
    return jnp.asarray(np.concatenate(pieces, axis=0))


def rotation(first, coarse, fine):
    rows = first.shape[0]
    position = lax.broadcasted_iota(jnp.int32, (rows, 1), 0) - first
    lane = lax.broadcasted_iota(jnp.int32, (rows, 3 * TABLE_STEP), 1) % TABLE_STEP
    pick = lambda place, table: dot((lane == place).astype(F32).astype(LOW), table)
    high = pick(position // TABLE_STEP, coarse)
    small = pick(position % TABLE_STEP, fine)
    cos_a, sin_a = high[:, :HEAD_DIM], high[:, HEAD_DIM:]
    cos_b, sin_b = small[:, :HEAD_DIM], small[:, HEAD_DIM:]
    sine = sin_a * cos_b + cos_a * sin_b
    left_half = lax.broadcasted_iota(jnp.int32, sine.shape, 1) < HEAD_DIM // 2
    return cos_a * cos_b - sin_a * sin_b, jnp.where(left_half, -sine, sine)


def heads_kernel(
    token_ref,
    gain_ref,
    base_ref,
    left_ref,
    right_ref,
    magnitude_ref,
    first_ref,
    coarse_ref,
    fine_ref,
    normed_ref,
    low_ref,
    post_ref,
    squares_ref,
    across_ref,
    cos_ref,
    sine_ref,
    rows_all,
):
    total_rows = token_ref.shape[0]
    depth, width = base_ref.shape[1:]
    rank = right_ref.shape[1]

    @pl.when(pl.program_id(0) == 0)
    def _():
        step = 16

        def some(i, carry):
            at = pl.ds(pl.multiple_of(i * step, step), step)
            values = token_ref[at, :].astype(F32)
            low = (values * rms_rows(values) * gain_ref[...]).astype(LOW)
            normed_ref[at, :] = low
            rows_all[at, :] = low
            return carry

        lax.fori_loop(0, total_rows // step, some, 0)
        for start in range(0, total_rows, 256):
            rows = slice(start, start + 256)
            cosine, sine = rotation(first_ref[rows, :] - start, coarse_ref[...], fine_ref[...])
            cos_ref[rows, :] = cosine
            sine_ref[rows, :] = sine

    rows_all[total_rows:, :] = left_ref[0].astype(LOW)
    turning = pl.program_id(0) < 2
    wide = 256
    for column in range(0, width, wide):
        columns = slice(column, column + wide)

        def put(start, step, tile, columns=columns):
            low_ref[0, start : start + step, columns] = tile

        squares_ref[0, :, columns] = merge_tile(
            lambda start, step, columns=columns: base_ref[0, start : start + step, columns],
            put,
            left_ref[0],
            right_ref[0, :, columns],
            depth,
        )
    for column in range(0, width, wide):
        columns = slice(column, column + wide)
        magnitude = magnitude_ref[pl.ds(pl.program_id(0), 1), columns]
        scale = magnitude / jnp.sqrt(squares_ref[0, :, columns])
        low = low_ref[0, :, columns]
        step = min(512, total_rows)
        for start in range(0, total_rows, step):
            last = start + step == total_rows
            rows = slice(start, start + step)
            pre = dot(rows_all[start : start + step + (rank if last else 0), :], low)
            if last:
                across_ref[0, :, columns] = pre[step:]
            post = pre[:step] * scale
            cos_table = jnp.where(turning, cos_ref[rows, :], 1.0)
            sine_table = jnp.where(turning, sine_ref[rows, :], 0.0)
            for head in range(0, wide, HEAD_DIM):
                piece = post[:, head : head + HEAD_DIM]
                other = pltpu.roll(piece, HEAD_DIM // 2, 1)
                post_ref[0, rows, column + head : column + head + HEAD_DIM] = (
                    piece * cos_table + other * sine_table
                ).astype(LOW)


def project_heads(tokens, gain, base, left, right, magnitude, first):
    members, depth, width = base.shape
    rows, rank = tokens.shape[0], right.shape[1]
    coarse = table_pieces(np.arange(TABLE_STEP) * TABLE_STEP)
    fine = table_pieces(np.arange(TABLE_STEP))
    whole = lambda v: pl.BlockSpec(v.shape, lambda m: (0,) * v.ndim)
    of_member = lambda *dims: pl.BlockSpec((1,) + dims, lambda m: (m, 0, 0))
    table = pl.BlockSpec((rows, HEAD_DIM), lambda m: (0, 0))
    return call(
        "project_heads",
        heads_kernel,
        (tokens, gain, base, left, right, magnitude, first, coarse, fine),
        (members,),
        [
            whole(tokens),
            whole(gain),
            of_member(depth, width),
            of_member(rank, depth),
            of_member(rank, width),
            whole(magnitude),
            whole(first),
            whole(coarse),
            whole(fine),
        ],
        [
            whole(tokens),
            of_member(depth, width),
            of_member(rows, width),
            of_member(1, width),
            of_member(rank, width),
            table,
            table,
        ],
        [
            shape((rows, depth), LOW),
            shape(base.shape, LOW),
            shape((members, rows, width), LOW),
            shape((members, 1, width), F32),
            shape((members, rank, width), F32),
            shape((rows, HEAD_DIM), F32),
            shape((rows, HEAD_DIM), F32),
        ],
        scratch=[pltpu.VMEM((rows + rank, depth), LOW)],
        flops=2 * members * rows * depth * width,
    )


def key_start(block):
    return max(0, (block * ATTEND_BLOCK - (LONGEST - 1)) // ATTEND_BLOCK * ATTEND_BLOCK)


def masked_probs(scores, first, row_at, key_at):
    scores = scores * HEAD_DIM ** (-0.5)
    places = row_at + lax.broadcasted_iota(jnp.int32, scores.shape, 0)
    others = key_at + lax.broadcasted_iota(jnp.int32, scores.shape, 1)
    scores = jnp.where((others >= first) & (others <= places), scores, MASKED)
    exp_scores = jnp.exp(scores - jnp.max(scores, axis=1, keepdims=True))
    return exp_scores * (1.0 / jnp.sum(exp_scores, axis=1, keepdims=True))


class Unit:
    def __init__(self, head, block):
        self.row_at, self.key_at = block * ATTEND_BLOCK, key_start(block)
        self.rows = slice(self.row_at, self.row_at + ATTEND_BLOCK)
        self.keys = slice(self.key_at, self.row_at + ATTEND_BLOCK)
        self.lanes = slice(head * HEAD_DIM, (head + 1) * HEAD_DIM)


def units_of(rows, width, most):
    units = [
        Unit(head, block)
        for block in range(rows // ATTEND_BLOCK)
        for head in range(width // HEAD_DIM)
    ]
    return [units[at : at + most] for at in range(0, len(units), most)]


def put_rows(ref, lead, row_at, lanes, values, order_ref, groups):
    share = ref.shape[len(lead)] // groups
    step = min(share, values.shape[0])
    for start in range(0, values.shape[0], step):
        group = (row_at + start) // share
        inside = (row_at + start) % share
        at = pl.multiple_of(order_ref[groups + group] * share + inside, step)
        ref[(*lead, pl.ds(at, step), lanes)] = values[start : start + step].astype(ref.dtype)


def attend_kernel(groups, order_ref, query_ref, key_ref, value_ref, first_ref, out_ref):
    for some in units_of(*query_ref.shape[1:], 4):
        scores = [
            dot(query_ref[0, u.rows, u.lanes], key_ref[0, u.keys, u.lanes], NT) for u in some
        ]
        probs = [
            masked_probs(s, first_ref[u.rows, :], u.row_at, u.key_at).astype(LOW)
            for u, s in zip(some, scores)
        ]
        for u, p in zip(some, probs):
            mixed = dot(p, value_ref[0, u.keys, u.lanes])
            put_rows(out_ref, (), u.row_at, u.lanes, mixed, order_ref, groups)


def attend(order, groups, post, first):
    rows, width = post.shape[1:]
    wide = 2 * HEAD_DIM
    member = lambda m: pl.BlockSpec((1, rows, wide), lambda h, o: (m, 0, h))
    return call(
        "attend",
        functools.partial(attend_kernel, groups),
        (post, post, post, first),
        (width // wide,),
        [member(0), member(1), member(2), pl.BlockSpec((rows, 1), lambda h, o: (0, 0))],
        [pl.BlockSpec((rows, wide), lambda h, o: (0, h))],
        [shape((rows, width), LOW)],
        prefetch=(order,),
        flops=4 * rows * rows * width,
        mib=32,
    )[0]


def attend_back_kernel(
    groups,
    order_ref,
    query_ref,
    key_ref,
    value_ref,
    first_ref,
    cos_ref,
    sine_ref,
    magnitude_ref,
    squares_ref,
    low_ref,
    *rest,
):
    pieces, (grad_ref, total_ref, upper_all, heads_grad, key_grad, value_grad, sems) = rest[:-7], rest[-7:]
    rows_all, width = query_ref.shape[1:]
    share = rows_all // groups

    @pl.when(pl.program_id(0) == 0)
    def _():
        copies = []
        for place, piece in enumerate(pieces):
            at = pl.multiple_of(order_ref[place] * share, share)
            copies.append(
                pltpu.make_async_copy(piece, upper_all.at[pl.ds(at, share), :], sems.at[place])
            )
            copies[-1].start()
        for copy in copies:
            copy.wait()

    step = min(512, rows_all)
    for start in range(0, rows_all, step):
        at = slice(start, start + step)
        heads_grad[at, :] = dot(upper_all[at, :], low_ref[0], NT).astype(LOW)
    norm = [jnp.sqrt(squares_ref[m]) for m in range(3)]
    scale = [magnitude_ref[m : m + 1] / norm[m] for m in range(3)]
    heads = range(0, width, HEAD_DIM)
    totals = [jnp.zeros((1, width), F32) for _ in range(3)]
    filled = set()

    def back(values, rows):
        return values * cos_ref[rows, :] - pltpu.roll(values, HEAD_DIM // 2, 1) * sine_ref[rows, :]

    def add(ref, unit, values):
        for start in range(0, values.shape[0], ATTEND_BLOCK):
            at = unit.key_at + start
            rows = slice(at, at + ATTEND_BLOCK)
            name = (id(ref), at, unit.lanes.start)
            if name in filled:
                ref[rows, unit.lanes] += values[start : start + ATTEND_BLOCK]
            else:
                filled.add(name)
                ref[rows, unit.lanes] = values[start : start + ATTEND_BLOCK]

    def spread(per_head):
        return jnp.concatenate(per_head, axis=1)

    query_totals = [jnp.zeros((1, HEAD_DIM), F32) for _ in heads]
    for some in units_of(rows_all, width, 2):
        scores = [
            dot(query_ref[0, u.rows, u.lanes], key_ref[0, u.keys, u.lanes], NT) for u in some
        ]
        grad_weights = [
            dot(heads_grad[u.rows, u.lanes], value_ref[0, u.keys, u.lanes], NT) for u in some
        ]
        probs = [
            masked_probs(s, first_ref[u.rows, :], u.row_at, u.key_at)
            for u, s in zip(some, scores)
        ]
        grad_scores = [
            (p * (g - jnp.sum(p * g, axis=1, keepdims=True))).astype(LOW)
            for p, g in zip(probs, grad_weights)
        ]
        for u, p, g in zip(some, probs, grad_scores):
            add(value_grad, u, dot(p.astype(LOW), heads_grad[u.rows, u.lanes], TN))
            add(key_grad, u, dot(g, query_ref[0, u.rows, u.lanes], TN))
        for u, g in zip(some, grad_scores):
            grad = back(dot(g, key_ref[0, u.keys, u.lanes]) * HEAD_DIM ** (-0.5), u.rows)
            head = u.lanes.start // HEAD_DIM
            post = back(query_ref[0, u.rows, u.lanes].astype(F32), u.rows)
            query_totals[head] = query_totals[head] + jnp.sum(grad * post, axis=0, keepdims=True)
            put_rows(grad_ref, (0,), u.row_at, u.lanes, grad * scale[0][:, u.lanes], order_ref, groups)
    totals[0] = spread(query_totals)
    for row_at in range(0, rows_all, ATTEND_BLOCK):
        rows = slice(row_at, row_at + ATTEND_BLOCK)
        for head in heads:
            lanes = slice(head, head + HEAD_DIM)
            grad = back(key_grad[rows, lanes] * HEAD_DIM ** (-0.5), rows)
            post = back(key_ref[0, rows, lanes].astype(F32), rows)
            part = jnp.sum(grad * post, axis=0, keepdims=True)
            query_totals[head // HEAD_DIM] = part if row_at == 0 else query_totals[head // HEAD_DIM] + part
            put_rows(grad_ref, (1,), row_at, lanes, grad * scale[1][:, lanes], order_ref, groups)
        grad = value_grad[rows, :]
        totals[2] = totals[2] + jnp.sum(grad * value_ref[0, rows, :].astype(F32), axis=0, keepdims=True)
        put_rows(grad_ref, (2,), row_at, slice(0, width), grad * scale[2], order_ref, groups)
    totals[1] = spread(query_totals)
    for m in range(3):
        total_ref[m] = totals[m] / scale[m]


def attend_back(order, groups, post, first, cos_table, sine_table, magnitude, squares, low, pieces):
    rows, width = post.shape[1:]
    depth = low.shape[2]
    wide = 2 * HEAD_DIM
    member = lambda m: pl.BlockSpec((1, rows, wide), lambda h, o: (m, 0, h))
    table = pl.BlockSpec((rows, HEAD_DIM), lambda h, o: (0, 0))
    column = pl.BlockSpec((3, 1, wide), lambda h, o: (0, 0, h))
    return call(
        "attend_back",
        functools.partial(attend_back_kernel, groups),
        (post, post, post, first, cos_table, sine_table, magnitude, squares, low, *pieces),
        (width // wide,),
        [
            member(0),
            member(1),
            member(2),
            pl.BlockSpec((rows, 1), lambda h, o: (0, 0)),
            table,
            table,
            pl.BlockSpec((3, wide), lambda h, o: (0, h)),
            column,
            pl.BlockSpec((1, wide, depth), lambda h, o: (0, h, 0)),
            *[pl.BlockSpec(memory_space=pl.ANY) for _ in pieces],
        ],
        [pl.BlockSpec((3, rows, wide), lambda h, o: (0, 0, h)), column],
        [shape((3, rows, width), LOW), shape((3, 1, width), F32)],
        scratch=[
            pltpu.VMEM((rows, depth), LOW),
            pltpu.VMEM((rows, wide), LOW),
            pltpu.VMEM((rows, wide), F32),
            pltpu.VMEM((rows, wide), F32),
            pltpu.SemaphoreType.DMA((len(pieces),)),
        ],
        prefetch=(order,),
        flops=10 * rows * rows * width + 2 * rows * width * depth,
        mib=48,
    )


def product_kernel(dims, n_totals, *refs):
    value_ref, weight_ref = refs[:2]
    groups = value_ref.shape[1]
    if n_totals == 0:
        left_ref, *refs = refs[2:]
    else:
        right_ref, squares_ref, magnitude_ref = refs[2:5]
        totals, refs = refs[5 : 5 + n_totals], refs[5 + n_totals :]
    outs, extra_ref, rows_all = refs[:groups], refs[groups], refs[groups + 1]
    members, _, share, inner = value_ref.shape
    count = groups * share

    @pl.when(pl.program_id(0) == 0)
    def _():
        if n_totals > 0:
            total = sum_refs(totals)
        for m in range(members):
            rows_all[m, :count, :] = value_ref[m].reshape(count, inner)
            if n_totals == 0:
                rows_all[m, count:, :] = left_ref[m].astype(LOW)
            else:
                weight = norm_weight(total[m], squares_ref[m], magnitude_ref[m : m + 1])
                rows_all[m, count:, :] = (right_ref[m] * weight).astype(LOW)

    result = None
    for m in range(members):
        part = dot(rows_all[m], weight_ref[m], dims)
        extra_ref[m] = part[count:]
        result = part[:count] if result is None else result + part[:count]
    for place, ref in enumerate(outs):
        ref[...] = result[place * share : (place + 1) * share].astype(LOW)


def product(name, values, weights, dims, left=None, correction=None):
    members, groups, share, inner = values.shape
    width = weights.shape[2] if dims is NN else weights.shape[1]
    wide = tile_of(width, 512)
    if dims is NN:
        weight_spec = pl.BlockSpec((members, inner, wide), lambda n: (0, 0, n))
    else:
        weight_spec = pl.BlockSpec((members, wide, inner), lambda n: (0, n, 0))
    if correction is None:
        extra, n_totals, rank = (left,), 0, left.shape[1]
    else:
        right, squares, magnitude, totals = correction
        extra, n_totals, rank = (right, squares, magnitude, *totals), len(totals), right.shape[1]
    fixed = lambda v: pl.BlockSpec(v.shape, lambda n: (0,) * v.ndim)
    out = pl.BlockSpec((share, wide), lambda n: (0, n))
    results = call(
        name,
        functools.partial(product_kernel, dims, n_totals),
        (values, weights, *extra),
        (width // wide,),
        [fixed(values), weight_spec] + [fixed(v) for v in extra],
        [out] * groups + [pl.BlockSpec((members, rank, wide), lambda n: (0, 0, n))],
        [shape((share, width), LOW)] * groups + [shape((members, rank, width), F32)],
        scratch=[pltpu.VMEM((members, groups * share + rank, inner), LOW)],
        flops=2 * members * groups * share * inner * width,
    )
    return results[:groups], results[groups]


def shrink_kernel(chips, order_ref, *refs):
    values, (weight_ref, left_ref, cot_ref), outs = refs[:chips], refs[chips : chips + 3], refs[chips + 3 :]
    total_ref, across_ref, rows_all = outs[-3:]
    _, _, share, inner = values[0].shape
    depth = left_ref.shape[2]
    count = chips * CORES * share

    @pl.when(pl.program_id(0) == 0)
    def _():
        for step, ref in enumerate(values):
            at = step * CORES * share
            rows_all[at : at + CORES * share, :] = ref[0].reshape(CORES * share, inner)
        if inner > depth:
            rows_all[count:, depth:] = jnp.zeros((rows_all.shape[0] - count, inner - depth), LOW)
        rows_all[count:, :depth] = left_ref[0].astype(LOW)

    result = dot(rows_all[...], weight_ref[0])
    across_ref[0] = result[count:]
    total = jnp.zeros((1, weight_ref.shape[2]), F32)
    for place in range(chips * CORES):
        pre = result[place * share : (place + 1) * share]
        outs[place][...] = pre.astype(LOW)
        at = pl.multiple_of(order_ref[place] * share, share)
        cot = cot_ref[pl.ds(at, share), :].astype(F32)
        total = total + jnp.sum(pre * cot, axis=0, keepdims=True)
    total_ref[...] = total


def shrink_product(order, values, weights, left, cotangent):
    chips = len(values)
    _, _, share, inner = values[0].shape
    width, rank = weights.shape[2], left.shape[1]
    rows = chips * CORES * share
    wide = tile_of(width, 512)
    fixed = lambda v: pl.BlockSpec(v.shape, lambda n, o: (0,) * v.ndim)
    results = call(
        "shrink_product",
        functools.partial(shrink_kernel, chips),
        (*values, weights, left, cotangent),
        (width // wide,),
        [fixed(v) for v in values]
        + [
            pl.BlockSpec((1, inner, wide), lambda n, o: (0, 0, n)),
            fixed(left),
            pl.BlockSpec((rows, wide), lambda n, o: (0, n)),
        ],
        [pl.BlockSpec((share, wide), lambda n, o: (0, n))] * (chips * CORES)
        + [
            pl.BlockSpec((1, wide), lambda n, o: (0, n)),
            pl.BlockSpec((1, rank, wide), lambda n, o: (0, 0, n)),
        ],
        [shape((share, width), LOW)] * (chips * CORES)
        + [shape((1, width), F32), shape((1, rank, width), F32)],
        scratch=[pltpu.VMEM((rows + rank, inner), LOW)],
        prefetch=(order,),
        flops=2 * rows * inner * width,
    )
    return results[: chips * CORES], results[-2], results[-1]


def row_call(name, kernel, order, given, whole, out_kinds, sums):
    share = min(v.shape[0] for v, _ in given)
    width = given[0][0].shape[1]
    halves = 2
    half = share // halves
    count = len(given)

    def run(order_ref, *refs):
        sources, rest = refs[:count], refs[count : -count - 1]
        held, sems = refs[-count - 1 : -1], refs[-1]

        def copies(part):
            for i, ((_, cut), source, target) in enumerate(zip(given, sources, held)):
                at = part * half
                if cut:
                    at = pl.multiple_of(order_ref[1] * share + at, half)
                yield pltpu.make_async_copy(
                    source.at[pl.ds(at, half), :],
                    target.at[pl.ds(part * half, half), :],
                    sems.at[part, i],
                )

        for part in range(halves):

            @pl.when(pl.program_id(0) == part)
            def _(part=part):
                if part == 0:
                    for each in range(halves):
                        for copy in copies(each):
                            copy.start()
                for copy in copies(part):
                    copy.wait()

        outs = rest[len(whole) : len(whole) + len(out_kinds)]
        totals, sums_held = rest[len(whole) + len(out_kinds) :][:sums], rest[len(rest) - sums :]
        tile = 16
        for ref in sums_held:
            ref[...] = jnp.zeros_like(ref)

        def some(i, carry):
            inside = pl.ds(pl.multiple_of(i * tile, tile), tile)
            at = pl.ds(pl.multiple_of(pl.program_id(0) * half + i * tile, tile), tile)
            values = kernel([ref[at, :].astype(F32) for ref in held], *[ref[...] for ref in rest[: len(whole)]])
            for ref, value in zip(outs, values):
                ref[inside, :] = value.astype(ref.dtype)
            for ref, value in zip(sums_held, values[len(outs) :]):
                ref[...] += value[:8] + value[8:]
            return carry

        lax.fori_loop(0, half // tile, some, 0)
        for ref, held_ref in zip(totals, sums_held):
            add_column(ref, held_ref[...])

    line = pl.BlockSpec((1, width), lambda i, o: (0, 0))
    return call(
        name,
        run,
        (*[v for v, _ in given], *whole),
        (halves,),
        [pl.BlockSpec(memory_space=pl.ANY) for _ in given] + [line for _ in whole],
        [pl.BlockSpec((half, width), lambda i, o: (i, 0)) for _ in out_kinds]
        + [line for _ in range(sums)],
        [shape((share, width), kind) for kind in out_kinds]
        + [shape((1, width), F32) for _ in range(sums)],
        scratch=[pltpu.VMEM((8, width), F32) for _ in range(sums)]
        + [pltpu.VMEM((share, width), v.dtype) for v, _ in given]
        + [pltpu.SemaphoreType.DMA((halves, count))],
        prefetch=(order,),
        flops=20 * share * width,
    )


def sum_of(values):
    total = values[0]
    for value in values[1:]:
        total = total + value
    return total


def add_column(ref, values):
    part = jnp.sum(values, axis=0, keepdims=True)

    @pl.when(pl.program_id(0) == 0)
    def _():
        ref[...] = part

    @pl.when(pl.program_id(0) > 0)
    def _():
        ref[...] += part


def hidden_kernel(given, squares, magnitude, gain):
    hidden = given[0] + sum_of(given[1:]) * (magnitude / jnp.sqrt(squares))
    return hidden, hidden * rms_rows(hidden) * gain


def mixed_kernel(given, squares, magnitude):
    return (given[0] + sum_of(given[1:]) * (magnitude / jnp.sqrt(squares)),)


def norm_back(grad_normed, values, gain):
    factor = rms_rows(values)
    scaled = grad_normed * gain
    inner = jnp.mean(scaled * values, axis=1, keepdims=True)
    back = factor * scaled - values * (factor * factor * factor * inner)
    return back, grad_normed * values * factor


def hidden_back_kernel(given, squares, magnitude, gain):
    cot, token, hidden = given[:3]
    back, gain_terms = norm_back(sum_of(given[3:]), hidden, gain)
    grad = cot + back
    norm = jnp.sqrt(squares)
    return grad, grad * (magnitude / norm), grad * ((hidden - token) * (norm / magnitude)), gain_terms


def token_back_kernel(given, gain):
    back, gain_terms = norm_back(sum_of(given[2:]), given[0], gain)
    return given[1] + back, gain_terms


def shrink_back_kernel(order_ref, cot_ref, low_ref, squares_ref, magnitude_ref, product_ref, grad_ref):
    scale = magnitude_ref[0] / jnp.sqrt(squares_ref[0])
    grad = (cot_ref[...].astype(F32) * scale).astype(LOW)
    grad_ref[0] = grad
    product_ref[0] = dot(grad, low_ref[0], NT)


def shrink_back(order, cotangent, low, squares, magnitude, groups):
    rows, width = cotangent.shape
    share, inner = rows // groups, low.shape[1]
    line = pl.BlockSpec((1, 1, width), lambda j, o: (0, 0, 0))
    return call(
        "shrink_back",
        shrink_back_kernel,
        (cotangent, low, squares, magnitude),
        (groups,),
        [
            pl.BlockSpec((share, width), lambda j, o: (o[j], 0)),
            pl.BlockSpec((1, inner, width), lambda j, o: (0, 0, 0)),
            line,
            line,
        ],
        [
            pl.BlockSpec((1, share, inner), lambda j, o: (j, 0, 0)),
            pl.BlockSpec((1, share, width), lambda j, o: (j, 0, 0)),
        ],
        [shape((groups, share, inner), F32), shape((groups, share, width), LOW)],
        prefetch=(order,),
        flops=2 * rows * width * inner,
    )


def expand_kernel(first, last, n_totals, ff, *refs):
    other_ref, mine_ref, low_ref, squares_ref, magnitude_ref, grad_ref = refs[:6]
    refs = list(refs[6:])
    left_ref = refs.pop(0) if first else None
    right_ref = refs.pop(0) if last else None
    before = [refs.pop(0) for _ in range(n_totals)]
    product_ref, back_ref, total_ref, rows_ref, send_ref, keep_ref = refs[:6]
    refs = refs[6:]
    across_ref = refs.pop(0) if first else None
    extra_ref = refs.pop(0) if last else None
    rows_all, back_all, mid_sum = refs
    share, depth = other_ref.shape
    wide = low_ref.shape[2]
    both = CORES * share

    @pl.when(pl.program_id(0) == 0)
    def _():
        for at, ref in ((0, other_ref), (share, mine_ref)):
            rows_ref[at : at + share, :] = ref[...]
            rows_all[at : at + share, :] = ref[...]
        if first:
            rank = across_ref.shape[1]
            for m in range(2):
                rows_all[both + m * rank : both + (m + 1) * rank, :] = left_ref[m].astype(LOW)
        mid_sum[...] = jnp.zeros_like(mid_sum)

    lane = pl.program_id(0) * wide + lax.broadcasted_iota(jnp.int32, (1, wide), 1)
    magnitude = [jnp.where(lane < ff, magnitude_ref[m : m + 1], 0.0) for m in range(2)]
    scale = [magnitude[m] / jnp.sqrt(squares_ref[m]) for m in range(2)]
    totals = [[], []]
    tile = 256
    cuts = [slice(at, at + tile) for at in range(0, wide, tile)]
    pre = [[dot(rows_all[...], low_ref[m, :, cut]) for m in range(2)] for cut in cuts]
    for cut, (gate_all, up_all) in zip(cuts, pre):
        if first:
            across_ref[0, :, cut] = gate_all[both : both + rank_of(across_ref)]
            across_ref[1, :, cut] = up_all[both + rank_of(across_ref) :]
        sums = [jnp.zeros((1, tile), F32) for _ in range(2)]
        gate_scale, up_scale = scale[0][:, cut], scale[1][:, cut]
        for place in range(CORES):
            rows = slice(place * share, (place + 1) * share)
            gate_pre, up_pre = gate_all[rows], up_all[rows]
            gate, up = gate_pre * gate_scale, up_pre * up_scale
            sigmoid = 0.5 + 0.5 * jnp.tanh(0.5 * gate)
            active = gate * sigmoid
            product_ref[0, place, :, cut] = (active * up).astype(LOW)
            upper = grad_ref[place, :, cut]
            grad_up = upper * active
            grad_gate = upper * up * sigmoid * (1.0 + gate * (1.0 - sigmoid))
            sums[0] += jnp.sum(grad_gate * gate_pre, axis=0, keepdims=True)
            sums[1] += jnp.sum(grad_up * up_pre, axis=0, keepdims=True)
            for m, low in enumerate((grad_gate * gate_scale, grad_up * up_scale)):
                low = low.astype(LOW)
                back_ref[m, place, :, cut] = low
                back_all[rows, m * wide + cut.start : m * wide + cut.stop] = low
        for m in range(2):
            totals[m].append(sums[m])
    totals = [jnp.concatenate(total, axis=1) for total in totals]
    for m in range(2):
        total_ref[m] = totals[m]
    if last:
        rank = rank_of(extra_ref)
        for m in range(2):
            total = totals[m]
            for ref in before:
                total = total + ref[m]
            right = jnp.where(lane < ff, right_ref[m], 0.0)
            weighted = right * norm_weight(total, squares_ref[m], magnitude[m])
            rows = slice(both + m * rank, both + (m + 1) * rank)
            back_all[rows, m * wide : (m + 1) * wide] = weighted.astype(LOW)
            back_all[rows, (1 - m) * wide : (2 - m) * wide] = jnp.zeros((rank, wide), LOW)
    step = tile_of(depth, 512)
    for at in range(0, depth, step):
        columns = slice(at, at + step)
        weights = jnp.concatenate([low_ref[0, columns, :], low_ref[1, columns, :]], axis=1)
        mid_sum[:, columns] += dot(back_all[...], weights, NT)

    @pl.when(pl.program_id(0) == pl.num_programs(0) - 1)
    def _():
        send_ref[...] = mid_sum[:share, :].astype(LOW)
        keep_ref[...] = mid_sum[share:both, :].astype(LOW)
        if last:
            for m in range(2):
                extra_ref[m] = mid_sum[both + m * rank_of(extra_ref) : both + (m + 1) * rank_of(extra_ref), :]


def rank_of(ref):
    return ref.shape[1]


def expand(pieces, low, squares, magnitude, grad_product, step, left=None, right=None, before=()):
    share, depth = pieces[0].shape
    width = low.shape[2]
    first, last = left is not None, right is not None
    wide = 512 if width % 512 == 0 else 256
    rows = CORES * share
    fixed = lambda dims: pl.BlockSpec(tuple(dims), lambda n: (0,) * len(dims))
    column = pl.BlockSpec((2, 1, wide), lambda n: (0, 0, n))
    operands = [*pieces, low, squares, magnitude, grad_product]
    in_specs = [
        fixed((share, depth)),
        fixed((share, depth)),
        pl.BlockSpec((2, depth, wide), lambda n: (0, 0, n)),
        column,
        pl.BlockSpec((2, wide), lambda n: (0, n)),
        pl.BlockSpec((2, share, wide), lambda n: (step, 0, n)),
    ]
    out_specs = [
        pl.BlockSpec((1, 2, share, wide), lambda n: (0, 0, 0, n)),
        pl.BlockSpec((2, 2, share, wide), lambda n: (0, 0, 0, n)),
        column,
        fixed((rows, depth)),
        fixed((share, depth)),
        fixed((share, depth)),
    ]
    out_shape = [
        shape((1, 2, share, width), LOW),
        shape((2, 2, share, width), LOW),
        shape((2, 1, width), F32),
        shape((rows, depth), LOW),
        shape((share, depth), LOW),
        shape((share, depth), LOW),
    ]
    extra_in = extra_out = 0
    if first:
        rank = left.shape[1]
        extra_in = 2 * rank
        operands.append(left)
        in_specs.append(fixed(left.shape))
        out_specs.append(pl.BlockSpec((2, rank, wide), lambda n: (0, 0, n)))
        out_shape.append(shape((2, rank, width), F32))
    if last:
        rank = right.shape[1]
        extra_out = 2 * rank
        operands += [right, *before]
        in_specs.append(pl.BlockSpec((2, rank, wide), lambda n: (0, 0, n)))
        in_specs += [column for _ in before]
        out_specs.append(fixed((2, rank, depth)))
        out_shape.append(shape((2, rank, depth), F32))
    return call(
        "expand",
        functools.partial(expand_kernel, first, last, len(before), magnitude.shape[1]),
        tuple(operands),
        (width // wide,),
        in_specs,
        out_specs,
        out_shape,
        scratch=[
            pltpu.VMEM((rows + extra_in, depth), LOW),
            pltpu.VMEM((rows + extra_out, 2 * wide), LOW),
            pltpu.VMEM((rows + extra_out, depth), F32),
        ],
        flops=8 * rows * depth * width,
    )


def adapter_kernel(views, n_inputs, n_grads, corrections, order_ref, *refs):
    inputs, grads = refs[:n_inputs], refs[n_inputs : n_inputs + n_grads]
    left_ref, right_ref = refs[n_inputs + n_grads : n_inputs + n_grads + 2]
    *corrected, left_out, right_out = refs[n_inputs + n_grads + 2 :]
    members, rank, width = right_ref.shape
    left_rows = jnp.concatenate([split_rows(left_ref[m]) for m in range(members)], axis=0)
    right_rows = [split_rows(right_ref[m]) for m in range(members)]
    left_out[...] = jnp.zeros_like(left_out)
    right_out[...] = jnp.zeros_like(right_out)
    for taken, grads_of in views(order_ref, inputs, grads):
        across = dot(left_rows, taken, NT)
        downs = []
        for m in range(members):
            grad = grads_of(m)
            mine = split_rows(fold(across[2 * rank * m : 2 * rank * (m + 1)]))
            right_out[m] += fold(dot(mine, grad))
            downs.append(split_rows(fold(dot(right_rows[m], grad, NT))))
        left = dot(jnp.concatenate(downs, axis=0), taken)
        for m in range(members):
            left_out[m] += fold(left[2 * rank * m : 2 * rank * (m + 1)])
    if corrections:
        correct(corrections, right_ref, left_out, right_out, left_out, right_out, *corrected)


def correct(n_totals, right_ref, left_in, right_in, left_out, right_out, *refs):
    back_ref, across_ref, squares_ref, magnitude_ref = refs[:4]
    totals, magnitude_out = refs[4 : 4 + n_totals], refs[4 + n_totals]
    members, rank, width = right_ref.shape
    total = sum_refs(totals)[:, :, :width]
    squares = squares_ref[:, :, :width]
    magnitude_out[...] = total / jnp.sqrt(squares)
    for m in range(members):
        weight = norm_weight(total[m], squares[m], magnitude_ref[m : m + 1])
        if back_ref.dtype == LOW:
            low = back_ref[m, : left_in.shape[2], :]
            back = fold(dot(split_rows(right_ref[m] * weight), low, NT))
        else:
            back = back_ref[m]
        left_out[m] = ADAPT_SCALE * (left_in[m] - back)
        right_out[m] = ADAPT_SCALE * (right_in[m] - across_ref[m][:, :width] * weight)


def correct_kernel(n_totals, order_ref, right_ref, left_in, right_in, *refs):
    *rest, left_out, right_out = refs
    correct(n_totals, right_ref, left_in, right_in, left_out, right_out, *rest)


def adapter_call(name, kernel, order, operands, right, outs):
    full = lambda dims: pl.BlockSpec(tuple(dims), lambda i, o: (0,) * len(dims))
    return call(
        name,
        kernel,
        operands,
        (1,),
        [full(v.shape) for v in operands],
        [full(dims) for dims in outs],
        [shape(dims, F32) for dims in outs],
        prefetch=(order,),
        flops=sum(v.size for v in operands) * 64,
    )


def adapter(name, order, views, inputs, grads, left, right, correction=None):
    members, rank, width = right.shape
    operands = [*inputs, *grads, left, right]
    outs = [(members, rank, left.shape[2]), (members, rank, width)]
    n_totals = 0
    if correction is not None:
        *given, totals = correction
        n_totals = len(totals)
        operands += [*given, *totals]
        outs = [(members, 1, width)] + outs
    kernel = functools.partial(adapter_kernel, views, len(inputs), len(grads), n_totals)
    return adapter_call(name, kernel, order, tuple(operands), right, outs)


def corrected(name, order, sums, right, correction):
    members, rank, width = right.shape
    *given, totals = correction
    operands = (right, *sums, *given, *totals)
    outs = [(members, 1, width), sums[0].shape, sums[1].shape]
    return adapter_call(name, functools.partial(correct_kernel, len(totals)), order, operands, right, outs)


MESH_IDS = pl.DeviceIdType.MESH


def copy_kernel(count, *refs):
    for source, target in zip(refs[:count], refs[count:]):
        target[...] = source[...]


def copy_out(arrays):
    vmem = pl.BlockSpec(memory_space=pltpu.VMEM)
    full = lambda v: pl.BlockSpec(v.shape, lambda i: (0,) * v.ndim)
    return call(
        "copy_out",
        functools.partial(copy_kernel, len(arrays)),
        tuple(arrays),
        (1,),
        [vmem for _ in arrays],
        [full(v) for v in arrays],
        [shape(v.shape, F32) for v in arrays],
        mib=16,
    )


GRAIN = 16


def pieces_of(width):
    return [(at, min(128, width - at)) for at in range(0, width, 128)]


def cells_of(blocks, lines, parts):
    cells, rows = [], []
    for n, block in enumerate(blocks):
        for m in range(block.shape[0]):
            for at, size in pieces_of(block.shape[2] // parts):
                cells.append((n, m, at, size))
    for n, line in enumerate(lines):
        for m in range(line.shape[0]):
            for at, size in pieces_of(line.shape[2] // parts):
                rows.append((n, m, at, size))
    return cells, rows


def pack(blocks, lines, wide_ref, part, parts, cells, rows):
    for i, (n, m, at, size) in enumerate(cells):
        start = part * (blocks[n].shape[2] // parts) + at
        wide_ref[part, i, :, :size] = blocks[n][m, :, start : start + size]
    for i, (n, m, at, size) in enumerate(rows):
        start = part * (lines[n].shape[2] // parts) + at
        cell, row = len(cells) + i // GRAIN, i % GRAIN
        wide_ref[part, cell, row : row + 1, :size] = lines[n][m, :, start : start + size]


def unpack(full_ref, blocks, lines, part, parts, cells, rows):
    for i, (n, m, at, size) in enumerate(cells):
        start = part * (blocks[n].shape[2] // parts) + at
        blocks[n][m, :, start : start + size] = full_ref[part, i].astype(F32)[:, :size]
    for i, (n, m, at, size) in enumerate(rows):
        start = part * (lines[n].shape[2] // parts) + at
        cell, row = len(cells) + i // GRAIN, i % GRAIN
        values = full_ref[part, cell].astype(F32)
        lines[n][m, :, start : start + size] = values[row : row + 1, :size]


def reduce_kernel(groups, lines, counts, *refs):
    n_all, n_all_lines, n_dp, n_dp_lines = counts
    count = sum(counts)
    taken, given, scratch = refs[:count], refs[count : 2 * count], refs[2 * count :]
    ends = [n_all, n_all + n_all_lines, n_all + n_all_lines + n_dp]
    parted = lambda v: (v[: ends[0]], v[ends[0] : ends[1]], v[ends[1] : ends[2]], v[ends[2] :])
    all_in, all_lines_in, dp_in, dp_lines_in = parted(taken)
    all_out, all_lines_out, dp_out, dp_lines_out = parted(given)
    (
        all_ref,
        line_ref,
        all_low,
        line_low,
        all_got,
        part,
        part_low,
        part_got,
        line_got,
        all_full,
        line_full,
        *sems,
    ) = scratch
    me, row = lax.axis_index("mp"), lax.axis_index("dp")
    piece, line_piece = part.shape[0] // lines, line_ref.shape[1] // lines
    mp_peer = [lax.rem(me + k, groups) for k in range(groups)]
    dp_peer = [lax.rem(row + k, lines) for k in range(lines)]
    barrier = pltpu.get_barrier_semaphore()
    for k in range(1, groups):
        pl.semaphore_signal(barrier, 1, device_id={"mp": mp_peer[k]}, device_id_type=MESH_IDS)
    for k in range(1, lines):
        pl.semaphore_signal(barrier, 1, device_id={"dp": dp_peer[k]}, device_id_type=MESH_IDS)
    all_cells = cells_of(all_in, all_lines_in, groups)
    dp_cells = cells_of(dp_in, dp_lines_in, 1)
    all_ref[...] = jnp.zeros_like(all_ref)
    line_ref[...] = jnp.zeros_like(line_ref)
    for q in range(groups):
        pack(all_in, all_lines_in, all_ref, q, groups, *all_cells)
    pack(dp_in, dp_lines_in, line_ref, 0, 1, *dp_cells)
    all_low[...] = all_ref[...].astype(LOW)
    line_low[...] = line_ref[...].astype(LOW)
    pl.semaphore_wait(barrier, groups + lines - 2)

    def send(source, target, stage, k, axis, peer):
        copy = pltpu.make_async_remote_copy(
            src_ref=source,
            dst_ref=target,
            send_sem=sems[2 * stage].at[k],
            recv_sem=sems[2 * stage + 1].at[k],
            device_id={axis: peer},
            device_id_type=MESH_IDS,
        )
        copy.start()
        return copy

    over_mp = [
        send(all_low.at[mp_peer[k]], all_got.at[k], 0, k, "mp", mp_peer[k])
        for k in range(1, groups)
    ]
    over_dp = [
        send(
            line_low.at[0, pl.ds(dp_peer[k] * line_piece, line_piece)],
            line_got.at[k],
            1,
            k,
            "dp",
            dp_peer[k],
        )
        for k in range(1, lines)
    ]
    total = all_ref[me]
    for k, copy in enumerate(over_mp, 1):
        copy.wait_recv()
        total = total + all_got[k].astype(F32)
    part[...] = total
    part_low[...] = total.astype(LOW)
    part_dp = [
        send(part_low.at[pl.ds(dp_peer[k] * piece, piece)], part_got.at[k], 2, k, "dp", dp_peer[k])
        for k in range(1, lines)
    ]
    held = pl.ds(row * piece, piece)
    total = part[held]
    for k, copy in enumerate(part_dp, 1):
        copy.wait_recv()
        total = total + part_got[k].astype(F32)
    all_full[me, held] = total.astype(LOW)
    part_back = [
        send(all_full.at[me, held], all_full.at[me, held], 4, k, "dp", dp_peer[k])
        for k in range(1, lines)
    ]
    mine = pl.ds(row * line_piece, line_piece)
    total = line_ref[0, mine]
    for k, copy in enumerate(over_dp, 1):
        copy.wait_recv()
        total = total + line_got[k].astype(F32)
    line_full[0, mine] = total.astype(LOW)
    line_back = [
        send(line_full.at[0, mine], line_full.at[0, mine], 3, k, "dp", dp_peer[k])
        for k in range(1, lines)
    ]
    for copy in part_back:
        copy.wait_recv()
    all_back = [
        send(all_full.at[me], all_full.at[me], 5, k, "mp", mp_peer[k]) for k in range(1, groups)
    ]
    for copy in line_back:
        copy.wait_recv()
    unpack(line_full, dp_out, dp_lines_out, 0, 1, *dp_cells)
    for copy in all_back:
        copy.wait_recv()
    for q in range(groups):
        unpack(all_full, all_out, all_lines_out, q, groups, *all_cells)
    for copy in over_mp + over_dp + part_dp + line_back + part_back + all_back:
        copy.wait_send()


def reduce_devices(name, identity, over_all, over_all_lines, over_dp, over_dp_lines):
    groups, lines = lax.axis_size("mp"), lax.axis_size("dp")

    def size_of(blocks, rows, parts):
        cells, lines_in = cells_of(blocks, rows, parts)
        size = len(cells) + -(-len(lines_in) // GRAIN)
        return -(-size // lines) * lines

    count, line_count = size_of(over_all, over_all_lines, groups), size_of(over_dp, over_dp_lines, 1)
    operands = (*over_all, *over_all_lines, *over_dp, *over_dp_lines)
    counts = (len(over_all), len(over_all_lines), len(over_dp), len(over_dp_lines))
    vmem = pl.BlockSpec(memory_space=pltpu.VMEM)
    tail = (GRAIN, 128)
    sizes = (groups, lines, lines, lines, lines, groups)
    every, line = (groups, count) + tail, (1, line_count) + tail
    results = pl.pallas_call(
        functools.partial(reduce_kernel, groups, lines, counts),
        name=name,
        out_shape=[shape(v.shape, F32) for v in operands],
        in_specs=[vmem for _ in operands],
        out_specs=[vmem for _ in operands],
        scratch_shapes=[
            pltpu.VMEM(every, F32),
            pltpu.VMEM(line, F32),
            pltpu.VMEM(every, LOW),
            pltpu.VMEM(line, LOW),
            pltpu.VMEM(every, LOW),
            pltpu.VMEM((count,) + tail, F32),
            pltpu.VMEM((count,) + tail, LOW),
            pltpu.VMEM((lines, count // lines) + tail, LOW),
            pltpu.VMEM((lines, line_count // lines) + tail, LOW),
            pltpu.VMEM(every, LOW),
            pltpu.VMEM(line, LOW),
        ]
        + [pltpu.SemaphoreType.DMA((n,)) for n in sizes for _ in range(2)],
        compiler_params=pltpu.CompilerParams(
            collective_id=identity, has_side_effects=True, vmem_limit_bytes=32 * 2**20
        ),
        cost_estimate=pl.CostEstimate(flops=1000, bytes_accessed=2**20, transcendentals=0),
    )(*operands)
    return copy_out(results)


def first_places(segment):
    length = segment.shape[0]
    places = lax.broadcasted_iota(jnp.int32, (length, length), 0)
    others = lax.broadcasted_iota(jnp.int32, (length, length), 1)
    visible = (segment[:, None] == segment[None, :]) & (others <= places)
    offset = jnp.sum(visible.astype(F32), axis=1) - 1.0
    return (jnp.arange(length, dtype=jnp.int32) - offset.astype(jnp.int32))[:, None]


def body(
    tokens,
    cotangent,
    segment_ids,
    attend_gain,
    expand_gain,
    heads_base,
    heads_left,
    heads_right,
    heads_magnitude,
    output_base,
    output_left,
    output_right,
    output_magnitude,
    expand_base,
    expand_left,
    expand_right,
    expand_magnitude,
    shrink_base,
    shrink_left,
    shrink_right,
    shrink_magnitude,
):
    groups = lax.axis_size("mp")
    chips = groups // CORES
    index = lax.axis_index("mp")
    chip, core = index // CORES, index % CORES
    rows, width = tokens.shape
    share = rows // groups
    local_heads, ff = heads_base.shape[2], expand_base.shape[2]
    ff_wide = padded(ff)
    device = jnp.arange(groups, dtype=jnp.int32)
    order = jnp.concatenate(
        [
            (chip + device // CORES) % chips * CORES + (core + 1 + device) % CORES,
            (device // CORES + chips - chip) % chips * CORES + (device + CORES - core + 1) % CORES,
        ]
    ).astype(jnp.int32)

    def tie(*values):
        return lax.optimization_barrier(values)

    def sibling(values):
        return lax.ppermute(
            values, "mp", [(i, i // CORES * CORES + (i + 1) % CORES) for i in range(groups)]
        )

    def to_chip(values, step):
        return lax.ppermute(
            values,
            "mp",
            [((i, ((i // CORES + step) % chips) * CORES + i % CORES)) for i in range(groups)],
        )

    def mp_sum(values):
        values = values + sibling(values)
        total = values
        for step in range(1, chips):
            total = total + to_chip(values, step)
        return total

    def join(pair):
        return (pair[1].astype(F32) + sibling(pair[0]).astype(F32)).astype(LOW)

    def chip_pairs(places):
        return [places[CORES * step : CORES * (step + 1)] for step in range(chips)]

    def arrive(own):
        return [to_chip(own, chips - step) for step in range(1, chips)]

    def pairs_of(own, near_sibling, arrived):
        return [(near_sibling, own)] + [(sibling(piece), piece) for piece in arrived]

    def in_pairs(order_ref, inputs, grads):
        for taken, grad in zip(inputs, grads):
            yield taken[...], lambda m, grad=grad: grad[m].reshape(-1, grad.shape[-1])[:, :ff]

    def in_shrink(order_ref, inputs, grads):
        for step, taken in enumerate(inputs):
            at = slice(CORES * step, CORES * (step + 1))
            yield (
                taken[0].reshape(-1, taken.shape[-1])[:, :ff],
                lambda m, at=at: grads[0][at].reshape(-1, grads[0].shape[-1]),
            )

    def in_output(order_ref, inputs, grads):
        for place, grad in enumerate(grads):
            yield inputs[0][0, place], lambda m, grad=grad: grad[...]

    def in_heads(order_ref, inputs, grads):
        for place in range(groups):
            at = pl.multiple_of(order_ref[place] * share, share)
            rows = slice(place * share, (place + 1) * share)
            yield inputs[0][pl.ds(at, share), :], lambda m, rows=rows: grads[0][m, rows, :]

    heads_rows, output_rows = turned(heads_left), turned(output_left[None])
    expand_rows, shrink_rows = turned(expand_left), turned(shrink_left[None])
    heads_mag, output_mag = heads_magnitude, output_magnitude[None]
    expand_mag, shrink_mag = expand_magnitude, shrink_magnitude[None]
    attend_line, expand_line = attend_gain[None], expand_gain[None]

    output_low, output_part = merge(
        output_base[None], output_rows, output_right[None], output_base.shape[0], 512
    )
    shrink_low, shrink_part = merge(
        shrink_base[None], shrink_rows, shrink_right[None], shrink_base.shape[0], 512
    )
    tokens, output_part, shrink_part = lax.optimization_barrier((tokens, output_part, shrink_part))
    squares = mp_sum(jnp.concatenate([output_part, shrink_part], axis=1))

    first = first_places(segment_ids.reshape(-1))
    normed, heads_low, post, heads_sq, heads_across, cos_table, sine_table = project_heads(
        tokens, attend_line, heads_base, heads_rows, heads_right, heads_mag, first
    )
    heads_out = attend(order, groups, post, first)
    heads_out, squares = tie(heads_out, squares)
    output_sq, shrink_sq = squares[:, :1], squares[:, 1:]
    heads_parts = heads_out.reshape(1, groups, share, local_heads)
    output_places, output_across = product(
        "output_product", heads_parts, output_low, NN, left=output_rows
    )
    output_pairs = chip_pairs(output_places)
    joined = [join(pair) for pair in output_pairs[1:]]
    joined, expand_right_tied = tie(joined, expand_right)
    output_arrived = [to_chip(values, step) for step, values in enumerate(joined, 1)]
    expand_low, expand_sq = merge(
        expand_base, expand_rows, expand_right_tied, 512, expand_base.shape[2]
    )
    grad_product, shrink_grad = shrink_back(
        order, cotangent, shrink_low, shrink_sq, shrink_mag[None], groups
    )
    output_parts = [output_pairs[0][1], sibling(output_pairs[0][0]), *output_arrived]
    output_parts, expand_low, grad_product = tie(output_parts, expand_low, grad_product)
    hidden, normed_own = row_call(
        "hidden",
        hidden_kernel,
        order,
        [(tokens, True)] + [(part, False) for part in output_parts],
        (output_sq[0], output_mag, expand_line),
        (F32, LOW),
        0,
    )

    def feed(pieces, step, **extra):
        return expand(pieces, expand_low, expand_sq, expand_mag, grad_product, step, **extra)

    arrived, near_sibling = arrive(normed_own), sibling(normed_own)
    fed = [feed((near_sibling, normed_own), 0, left=expand_rows)]
    arrived, fed = tie(arrived, fed)
    fed = list(fed)
    mid_sibling = sibling(fed[0][4])
    normed_mid = pairs_of(normed_own, near_sibling, arrived)
    for step in range(1, chips):
        extra = {}
        if step == chips - 1:
            extra = {"right": expand_right, "before": [f[2] for f in fed]}
        fed.append(feed(normed_mid[step], step, **extra))
    expand_totals = [f[2] for f in fed]
    joined = [join(f[4:6]) for f in fed[1:]]
    joined, shrink_rows_tied = tie(joined, shrink_rows)
    mid_arrived = [to_chip(values, step) for step, values in enumerate(joined, 1)]
    shrink_places, shrink_total, shrink_across = shrink_product(
        order, [f[0] for f in fed], shrink_low, shrink_rows_tied, cotangent
    )
    shrink_pairs = chip_pairs(shrink_places)
    mid_parts = [fed[0][5], mid_sibling, *mid_arrived]
    mid_parts, shrink_pairs, shrink_total = tie(mid_parts, shrink_pairs, shrink_total)
    grad_hidden, output_grad_own, output_total, expand_gain_part = row_call(
        "hidden_back",
        hidden_back_kernel,
        order,
        [(cotangent, True), (tokens, True), (hidden, False)]
        + [(part, False) for part in mid_parts],
        (output_sq[0], output_mag, expand_line),
        (F32, LOW),
        2,
    )
    arrived, near_sibling = arrive(output_grad_own), sibling(output_grad_own)
    both_totals = mp_sum(jnp.concatenate([output_total, shrink_total], axis=0))
    shrink_joined = [join(pair) for pair in shrink_pairs[1:]]
    expand_adapter = adapter(
        "expand_adapter",
        order,
        in_pairs,
        [f[3] for f in fed],
        [f[1] for f in fed],
        expand_rows,
        expand_right,
        (fed[-1][6], fed[0][6], expand_sq, expand_mag, expand_totals),
    )
    shrink_sums = adapter(
        "shrink_adapter",
        order,
        in_shrink,
        [f[0] for f in fed],
        [shrink_grad],
        shrink_rows,
        shrink_right[None],
    )
    arrived, near_sibling, both_totals, shrink_joined, expand_adapter, shrink_sums = tie(
        arrived, near_sibling, both_totals, shrink_joined, expand_adapter, shrink_sums
    )
    output_total, shrink_total = both_totals[:1], both_totals[1:]
    output_grad = [
        piece for pair in pairs_of(output_grad_own, near_sibling, arrived) for piece in pair
    ]
    shrink_parts = [shrink_pairs[0][1], sibling(shrink_pairs[0][0])] + [
        to_chip(values, step) for step, values in enumerate(shrink_joined, 1)
    ]
    heads_grads, heads_total = attend_back(
        order,
        groups,
        post,
        first,
        cos_table,
        sine_table,
        heads_mag,
        heads_sq,
        output_low,
        output_grad,
    )
    heads_grads, shrink_parts = tie(heads_grads, shrink_parts)
    grad_parts = heads_grads.reshape(3, groups, share, local_heads)
    token_places, token_extra = product(
        "normed_product",
        grad_parts,
        heads_low,
        NT,
        correction=(heads_right, heads_sq, heads_mag, [heads_total]),
    )
    token_pairs = chip_pairs(token_places)
    joined = [join(pair) for pair in token_pairs[1:]]
    joined, heads_rows_tied, output_rows_tied = tie(joined, heads_rows, output_rows)
    token_arrived = [to_chip(values, step) for step, values in enumerate(joined, 1)]
    output_adapter = adapter(
        "output_adapter",
        order,
        in_output,
        [heads_parts],
        output_grad,
        output_rows_tied,
        output_right[None],
        (output_low, output_across, output_sq, output_mag, [output_total[None]]),
    )
    shrink_adapter = corrected(
        "shrink_correct",
        order,
        shrink_sums,
        shrink_right[None],
        (shrink_low, shrink_across, shrink_sq, shrink_mag, [shrink_total[None]]),
    )
    heads_adapter = adapter(
        "heads_adapter",
        order,
        in_heads,
        [normed],
        [heads_grads],
        heads_rows_tied,
        heads_right,
        (token_extra, heads_across, heads_sq, heads_mag, [heads_total]),
    )
    (mixed,) = row_call(
        "mixed",
        mixed_kernel,
        order,
        [(hidden, False)] + [(part, False) for part in shrink_parts],
        (shrink_sq[0], shrink_mag),
        (LOW,),
        0,
    )
    token_parts = [token_pairs[0][1], sibling(token_pairs[0][0]), *token_arrived]
    token_parts, output_adapter, shrink_adapter, heads_adapter, mixed = tie(
        token_parts, output_adapter, shrink_adapter, heads_adapter, mixed
    )
    grad_tokens, attend_gain_part = row_call(
        "token_back",
        token_back_kernel,
        order,
        [(tokens, True), (grad_hidden, False)] + [(part, False) for part in token_parts],
        (attend_line,),
        (F32,),
        1,
    )
    (
        expand_left_grad,
        shrink_right_grad,
        heads_left_grad,
        output_right_grad,
        expand_gain_grad,
        attend_gain_grad,
        expand_right_grad,
        shrink_left_grad,
        heads_right_grad,
        output_left_grad,
        expand_mag_grad,
        shrink_mag_grad,
        heads_mag_grad,
        output_mag_grad,
    ) = reduce_devices(
        "reduce_gradients",
        1,
        [expand_adapter[1], shrink_adapter[2], heads_adapter[1], output_adapter[2]],
        [expand_gain_part[None], attend_gain_part[None]],
        [expand_adapter[2], shrink_adapter[1], heads_adapter[2], output_adapter[1]],
        [expand_adapter[0], shrink_adapter[0], heads_adapter[0], output_adapter[0]],
    )
    return (
        mixed,
        grad_tokens,
        attend_gain_grad[0, 0],
        expand_gain_grad[0, 0],
        jnp.swapaxes(heads_left_grad, 1, 2),
        heads_right_grad,
        heads_mag_grad[:, 0],
        output_left_grad[0].T,
        output_right_grad[0],
        output_mag_grad[0, 0],
        jnp.swapaxes(expand_left_grad, 1, 2),
        expand_right_grad,
        expand_mag_grad[:, 0],
        shrink_left_grad[0].T,
        shrink_right_grad[0],
        shrink_mag_grad[0, 0],
    )


def solution(mesh):
    placed = (
        P("dp", None),
        P("dp", None),
        P("dp", None),
        P(),
        P(),
        P(None, None, "mp"),
        P(),
        P(None, None, "mp"),
        P(None, "mp"),
        P("mp", None),
        P("mp", None),
        P(),
        P(),
        P(None, None, "mp"),
        P(),
        P(None, None, "mp"),
        P(None, "mp"),
        P("mp", None),
        P("mp", None),
        P(),
        P(),
    )
    return jax.shard_map(
        body,
        mesh=mesh,
        in_specs=placed,
        out_specs=(
            P(("dp", "mp"), None),
            P(("dp", "mp"), None),
            P(),
            P(),
            P(),
            P(None, None, "mp"),
            P(None, "mp"),
            P("mp", None),
            P(),
            P(),
            P(),
            P(None, None, "mp"),
            P(None, "mp"),
            P("mp", None),
            P(),
            P(),
        ),
        check_vma=False,
    )
```

```python
import functools

import jax
import jax.numpy as jnp
import ml_dtypes
import numpy as np
from jax import lax
from jax.experimental import pallas as pl
from jax.experimental.pallas import tpu as pltpu
from jax.sharding import PartitionSpec as P

HEAD_DIM = 128
CORES = 2
LONGEST = 512
ATTEND_BLOCK = 256
ADAPT_SCALE = 2.0
NORM_EPS = 1e-05
ROPE_BASE = 10000.0
MASKED = -1e30

F32 = jnp.float32
LOW = jnp.bfloat16
NN = (((1,), (0,)), ((), ()))
NT = (((1,), (1,)), ((), ()))
TN = (((0,), (0,)), ((), ()))


def dot(left, right, dims=NN):
    return lax.dot_general(left, right, dims, preferred_element_type=F32)


def shape(dims, kind):
    return jax.ShapeDtypeStruct(tuple(dims), kind)


def call(name, kernel, operands, grid, in_specs, out_specs, out_shape, scratch=(), prefetch=(), flops=0, mib=60):
    moved = sum(v.size * v.dtype.itemsize for v in operands)
    moved += sum(v.size * v.dtype.itemsize for v in out_shape)
    return pl.pallas_call(
        kernel,
        name=name,
        out_shape=out_shape,
        grid_spec=pltpu.PrefetchScalarGridSpec(
            num_scalar_prefetch=len(prefetch),
            grid=grid,
            in_specs=in_specs,
            out_specs=out_specs,
            scratch_shapes=scratch,
        ),
        compiler_params=pltpu.CompilerParams(vmem_limit_bytes=mib * 2**20),
        cost_estimate=pl.CostEstimate(flops=flops // 16, bytes_accessed=moved // 16, transcendentals=0),
    )(*prefetch, *operands)


def tile_of(size, most):
    return most if size % most == 0 else size


def split_rows(values):
    top = values.astype(LOW)
    rest = (values - top.astype(F32)).astype(LOW)
    return jnp.concatenate([top, rest], axis=0)


def turned(left_map):
    return jnp.swapaxes(left_map, -1, -2)


def norm_weight(total, squares, magnitude):
    norm = jnp.sqrt(squares)
    return total * magnitude / (norm * norm * norm)


def sum_refs(refs):
    total = refs[0][...]
    for ref in refs[1:]:
        total = total + ref[...]
    return total


def fold(values):
    half = values.shape[0] // 2
    return values[:half] + values[half:]


def merge_tile(base_at, low_put, left, right, depth):
    rank = right.shape[0]
    doubled = ADAPT_SCALE * right
    top = doubled.astype(LOW)
    rest = (doubled - top.astype(F32)).astype(LOW)
    right_stack = jnp.concatenate([top, rest, top], axis=0)
    left_pair = split_rows(left)
    left_stack = jnp.concatenate([left_pair[:rank], left_pair[:rank], left_pair[rank:]], axis=0)
    squares = jnp.zeros((1, right.shape[1]), F32)
    step = tile_of(depth, 1024)
    for start in range(0, depth, step):
        merged = base_at(start, step).astype(F32) + dot(
            left_stack[:, start : start + step], right_stack, TN
        )
        low_put(start, step, merged.astype(LOW))
        squares = squares + jnp.sum(merged * merged, axis=0, keepdims=True)
    return squares


def merge_pair_kernel(*refs):
    for n in range(2):
        base_ref, left_ref, right_ref = refs[3 * n : 3 * n + 3]
        low_ref, squares_ref = refs[6 + n], refs[8]
        depth = base_ref.shape[0]
        if low_ref.shape[0] > depth:
            low_ref[depth:, :] = jnp.zeros((low_ref.shape[0] - depth, low_ref.shape[1]), LOW)

        def put(start, step, tile, low_ref=low_ref):
            low_ref[start : start + step, :] = tile

        squares_ref[n : n + 1, :] = merge_tile(
            lambda start, step, base_ref=base_ref: base_ref[start : start + step, :],
            put,
            left_ref[...],
            right_ref[...],
            depth,
        )


def merge_pair(triples):
    operands, in_specs, low_specs, low_shapes = [], [], [], []
    width = triples[0][0].shape[1]
    wide = tile_of(width, 512)
    for base, left, right in triples:
        depth, rank = base.shape[0], right.shape[0]
        operands += [base, left, right]
        in_specs += [
            pl.BlockSpec((depth, wide), lambda n: (0, n)),
            pl.BlockSpec((rank, depth), lambda n: (0, 0)),
            pl.BlockSpec((rank, wide), lambda n: (0, n)),
        ]
        low_specs.append(pl.BlockSpec((padded(depth), wide), lambda n: (0, n)))
        low_shapes.append(shape((padded(depth), width), LOW))
    return call(
        "merge_pair",
        merge_pair_kernel,
        tuple(operands),
        (width // wide,),
        in_specs,
        low_specs + [pl.BlockSpec((2, wide), lambda n: (0, n))],
        low_shapes + [shape((2, width), F32)],
        flops=2 * sum(v.size for v in operands) * 256,
    )


def merge_kernel(base_ref, left_ref, right_ref, low_ref, squares_ref):
    depth, width = base_ref.shape[1:]
    if low_ref.shape[1] > depth:
        low_ref[0, depth:, :] = jnp.zeros((low_ref.shape[1] - depth, low_ref.shape[2]), LOW)
    if low_ref.shape[2] > width:
        spare = low_ref.shape[2] - width
        low_ref[0, :, width:] = jnp.zeros((low_ref.shape[1], spare), LOW)
        squares_ref[0, :, width:] = jnp.ones((1, spare), F32)

    def put(start, step, tile):
        low_ref[0, start : start + step, :width] = tile

    squares = merge_tile(
        lambda start, step: base_ref[0, start : start + step, :],
        put,
        left_ref[0],
        right_ref[0],
        depth,
    )

    @pl.when(pl.program_id(2) == 0)
    def _():
        squares_ref[0, :, :width] = squares

    @pl.when(pl.program_id(2) > 0)
    def _():
        squares_ref[0, :, :width] += squares


def padded(size):
    return -(-size // 256) * 256


def pad_last(values, size):
    return jnp.pad(values, [(0, 0)] * (values.ndim - 1) + [(0, size - values.shape[-1])])


def merge(base, left, right, deep, wide):
    members, depth, width = base.shape
    low_deep = padded(deep) if deep == depth else deep
    low_wide = padded(wide) if wide == width else wide
    low_shape = (members, depth // deep * low_deep, width // wide * low_wide)
    rank = right.shape[1]
    return call(
        "merge",
        merge_kernel,
        (base, left, right),
        (members, width // wide, depth // deep),
        [
            pl.BlockSpec((1, deep, wide), lambda m, n, k: (m, k, n)),
            pl.BlockSpec((1, rank, deep), lambda m, n, k: (m, 0, k)),
            pl.BlockSpec((1, rank, wide), lambda m, n, k: (m, 0, n)),
        ],
        [
            pl.BlockSpec((1, low_deep, low_wide), lambda m, n, k: (m, k, n)),
            pl.BlockSpec((1, 1, low_wide), lambda m, n, k: (m, 0, n)),
        ],
        [shape(low_shape, LOW), shape((members, 1, low_shape[2]), F32)],
        flops=2 * members * depth * width * 256,
    )


def rms_rows(values):
    return lax.rsqrt(jnp.mean(values * values, axis=1, keepdims=True) + NORM_EPS)


TABLE_STEP = 32


def table_pieces(places):
    half = np.arange(HEAD_DIM) % (HEAD_DIM // 2)
    angles = np.asarray(places)[:, None] * ROPE_BASE ** (-2.0 * half / HEAD_DIM)[None, :]
    rest = np.concatenate([np.cos(angles), np.sin(angles)], axis=1)
    pieces = []
    for _ in range(3):
        pieces.append(rest.astype(ml_dtypes.bfloat16))
        rest = rest - pieces[-1].astype(np.float64)
    return jnp.asarray(np.concatenate(pieces, axis=0))


def rotation(first, coarse, fine):
    rows = first.shape[0]
    position = lax.broadcasted_iota(jnp.int32, (rows, 1), 0) - first
    lane = lax.broadcasted_iota(jnp.int32, (rows, 3 * TABLE_STEP), 1) % TABLE_STEP
    pick = lambda place, table: dot((lane == place).astype(F32).astype(LOW), table)
    high = pick(position // TABLE_STEP, coarse)
    small = pick(position % TABLE_STEP, fine)
    cos_a, sin_a = high[:, :HEAD_DIM], high[:, HEAD_DIM:]
    cos_b, sin_b = small[:, :HEAD_DIM], small[:, HEAD_DIM:]
    sine = sin_a * cos_b + cos_a * sin_b
    left_half = lax.broadcasted_iota(jnp.int32, sine.shape, 1) < HEAD_DIM // 2
    return cos_a * cos_b - sin_a * sin_b, jnp.where(left_half, -sine, sine)


def heads_kernel(
    token_ref,
    gain_ref,
    base_ref,
    left_ref,
    right_ref,
    magnitude_ref,
    first_ref,
    coarse_ref,
    fine_ref,
    normed_ref,
    low_ref,
    post_ref,
    squares_ref,
    across_ref,
    cos_ref,
    sine_ref,
    rows_all,
):
    total_rows = token_ref.shape[0]
    depth, width = base_ref.shape[1:]
    rank = right_ref.shape[1]

    @pl.when(pl.program_id(0) == 0)
    def _():
        step = 128

        def some(i, carry):
            at = pl.ds(pl.multiple_of(i * step, step), step)
            values = token_ref[at, :].astype(F32)
            low = (values * rms_rows(values) * gain_ref[...]).astype(LOW)
            normed_ref[at, :] = low
            rows_all[at, :] = low
            return carry

        lax.fori_loop(0, total_rows // step, some, 0)
        for start in range(0, total_rows, 256):
            rows = slice(start, start + 256)
            cosine, sine = rotation(first_ref[rows, :] - start, coarse_ref[...], fine_ref[...])
            cos_ref[rows, :] = cosine
            sine_ref[rows, :] = sine

    rows_all[total_rows:, :] = left_ref[0].astype(LOW)
    turning = pl.program_id(0) < 2
    wide = 256
    for column in range(0, width, wide):
        columns = slice(column, column + wide)

        def put(start, step, tile, columns=columns):
            low_ref[0, start : start + step, columns] = tile

        squares_ref[0, :, columns] = merge_tile(
            lambda start, step, columns=columns: base_ref[0, start : start + step, columns],
            put,
            left_ref[0],
            right_ref[0, :, columns],
            depth,
        )
    for column in range(0, width, wide):
        columns = slice(column, column + wide)
        magnitude = magnitude_ref[pl.ds(pl.program_id(0), 1), columns]
        scale = magnitude / jnp.sqrt(squares_ref[0, :, columns])
        low = low_ref[0, :, columns]
        step = min(512, total_rows)
        for start in range(0, total_rows, step):
            last = start + step == total_rows
            rows = slice(start, start + step)
            pre = dot(rows_all[start : start + step + (rank if last else 0), :], low)
            if last:
                across_ref[0, :, columns] = pre[step:]
            post = pre[:step] * scale
            cos_table = jnp.where(turning, cos_ref[rows, :], 1.0)
            sine_table = jnp.where(turning, sine_ref[rows, :], 0.0)
            for head in range(0, wide, HEAD_DIM):
                piece = post[:, head : head + HEAD_DIM]
                other = pltpu.roll(piece, HEAD_DIM // 2, 1)
                post_ref[0, rows, column + head : column + head + HEAD_DIM] = (
                    piece * cos_table + other * sine_table
                ).astype(LOW)


def project_heads(tokens, gain, base, left, right, magnitude, first):
    members, depth, width = base.shape
    rows, rank = tokens.shape[0], right.shape[1]
    coarse = table_pieces(np.arange(TABLE_STEP) * TABLE_STEP)
    fine = table_pieces(np.arange(TABLE_STEP))
    whole = lambda v: pl.BlockSpec(v.shape, lambda m: (0,) * v.ndim)
    of_member = lambda *dims: pl.BlockSpec((1,) + dims, lambda m: (m, 0, 0))
    table = pl.BlockSpec((rows, HEAD_DIM), lambda m: (0, 0))
    return call(
        "project_heads",
        heads_kernel,
        (tokens, gain, base, left, right, magnitude, first, coarse, fine),
        (members,),
        [
            whole(tokens),
            whole(gain),
            of_member(depth, width),
            of_member(rank, depth),
            of_member(rank, width),
            whole(magnitude),
            whole(first),
            whole(coarse),
            whole(fine),
        ],
        [
            whole(tokens),
            of_member(depth, width),
            of_member(rows, width),
            of_member(1, width),
            of_member(rank, width),
            table,
            table,
        ],
        [
            shape((rows, depth), LOW),
            shape(base.shape, LOW),
            shape((members, rows, width), LOW),
            shape((members, 1, width), F32),
            shape((members, rank, width), F32),
            shape((rows, HEAD_DIM), F32),
            shape((rows, HEAD_DIM), F32),
        ],
        scratch=[pltpu.VMEM((rows + rank, depth), LOW)],
        flops=2 * members * rows * depth * width,
    )


def key_start(block):
    return max(0, (block * ATTEND_BLOCK - (LONGEST - 1)) // ATTEND_BLOCK * ATTEND_BLOCK)


def masked_probs(scores, first, row_at, key_at):
    scores = scores * HEAD_DIM ** (-0.5)
    places = row_at + lax.broadcasted_iota(jnp.int32, scores.shape, 0)
    others = key_at + lax.broadcasted_iota(jnp.int32, scores.shape, 1)
    scores = jnp.where((others >= first) & (others <= places), scores, MASKED)
    exp_scores = jnp.exp(scores - jnp.max(scores, axis=1, keepdims=True))
    return exp_scores * (1.0 / jnp.sum(exp_scores, axis=1, keepdims=True))


class Unit:
    def __init__(self, head, block):
        self.row_at, self.key_at = block * ATTEND_BLOCK, key_start(block)
        self.rows = slice(self.row_at, self.row_at + ATTEND_BLOCK)
        self.keys = slice(self.key_at, self.row_at + ATTEND_BLOCK)
        self.lanes = slice(head * HEAD_DIM, (head + 1) * HEAD_DIM)


def units_of(rows, width, most):
    units = [
        Unit(head, block)
        for block in range(rows // ATTEND_BLOCK)
        for head in range(width // HEAD_DIM)
    ]
    return [units[at : at + most] for at in range(0, len(units), most)]


def put_rows(ref, lead, row_at, lanes, values, order_ref, groups):
    share = ref.shape[len(lead)] // groups
    step = min(share, values.shape[0])
    for start in range(0, values.shape[0], step):
        group = (row_at + start) // share
        inside = (row_at + start) % share
        at = pl.multiple_of(order_ref[groups + group] * share + inside, step)
        ref[(*lead, pl.ds(at, step), lanes)] = values[start : start + step].astype(ref.dtype)


def attend_kernel(groups, order_ref, query_ref, key_ref, value_ref, first_ref, out_ref):
    for some in units_of(*query_ref.shape[1:], 4):
        scores = [
            dot(query_ref[0, u.rows, u.lanes], key_ref[0, u.keys, u.lanes], NT) for u in some
        ]
        probs = [
            masked_probs(s, first_ref[u.rows, :], u.row_at, u.key_at).astype(LOW)
            for u, s in zip(some, scores)
        ]
        for u, p in zip(some, probs):
            mixed = dot(p, value_ref[0, u.keys, u.lanes])
            put_rows(out_ref, (), u.row_at, u.lanes, mixed, order_ref, groups)


def attend(order, groups, post, first):
    rows, width = post.shape[1:]
    wide = 2 * HEAD_DIM
    member = lambda m: pl.BlockSpec((1, rows, wide), lambda h, o: (m, 0, h))
    return call(
        "attend",
        functools.partial(attend_kernel, groups),
        (post, post, post, first),
        (width // wide,),
        [member(0), member(1), member(2), pl.BlockSpec((rows, 1), lambda h, o: (0, 0))],
        [pl.BlockSpec((rows, wide), lambda h, o: (0, h))],
        [shape((rows, width), LOW)],
        prefetch=(order,),
        flops=4 * rows * rows * width,
        mib=32,
    )[0]


def attend_back_kernel(
    groups,
    order_ref,
    query_ref,
    key_ref,
    value_ref,
    first_ref,
    cos_ref,
    sine_ref,
    magnitude_ref,
    squares_ref,
    low_ref,
    *rest,
):
    pieces, (grad_ref, total_ref, upper_all, heads_grad, key_grad, value_grad, sems) = rest[:-7], rest[-7:]
    rows_all, width = query_ref.shape[1:]
    share = rows_all // groups

    @pl.when(pl.program_id(0) == 0)
    def _():
        copies = []
        for place, piece in enumerate(pieces):
            at = pl.multiple_of(order_ref[place] * share, share)
            copies.append(
                pltpu.make_async_copy(piece, upper_all.at[pl.ds(at, share), :], sems.at[place])
            )
            copies[-1].start()
        for copy in copies:
            copy.wait()

    step = min(512, rows_all)
    for start in range(0, rows_all, step):
        at = slice(start, start + step)
        heads_grad[at, :] = dot(upper_all[at, :], low_ref[0], NT).astype(LOW)
    norm = [jnp.sqrt(squares_ref[m]) for m in range(3)]
    scale = [magnitude_ref[m : m + 1] / norm[m] for m in range(3)]
    heads = range(0, width, HEAD_DIM)
    totals = [jnp.zeros((1, width), F32) for _ in range(3)]
    filled = set()

    def back(values, rows):
        return values * cos_ref[rows, :] - pltpu.roll(values, HEAD_DIM // 2, 1) * sine_ref[rows, :]

    def add(ref, unit, values):
        for start in range(0, values.shape[0], ATTEND_BLOCK):
            at = unit.key_at + start
            rows = slice(at, at + ATTEND_BLOCK)
            name = (id(ref), at, unit.lanes.start)
            if name in filled:
                ref[rows, unit.lanes] += values[start : start + ATTEND_BLOCK]
            else:
                filled.add(name)
                ref[rows, unit.lanes] = values[start : start + ATTEND_BLOCK]

    def spread(per_head):
        return jnp.concatenate(per_head, axis=1)

    query_totals = [jnp.zeros((1, HEAD_DIM), F32) for _ in heads]
    for some in units_of(rows_all, width, 2):
        scores = [
            dot(query_ref[0, u.rows, u.lanes], key_ref[0, u.keys, u.lanes], NT) for u in some
        ]
        grad_weights = [
            dot(heads_grad[u.rows, u.lanes], value_ref[0, u.keys, u.lanes], NT) for u in some
        ]
        probs = [
            masked_probs(s, first_ref[u.rows, :], u.row_at, u.key_at)
            for u, s in zip(some, scores)
        ]
        grad_scores = [
            (p * (g - jnp.sum(p * g, axis=1, keepdims=True))).astype(LOW)
            for p, g in zip(probs, grad_weights)
        ]
        for u, p, g in zip(some, probs, grad_scores):
            add(value_grad, u, dot(p.astype(LOW), heads_grad[u.rows, u.lanes], TN))
            add(key_grad, u, dot(g, query_ref[0, u.rows, u.lanes], TN))
        for u, g in zip(some, grad_scores):
            grad = back(dot(g, key_ref[0, u.keys, u.lanes]) * HEAD_DIM ** (-0.5), u.rows)
            head = u.lanes.start // HEAD_DIM
            post = back(query_ref[0, u.rows, u.lanes].astype(F32), u.rows)
            query_totals[head] = query_totals[head] + jnp.sum(grad * post, axis=0, keepdims=True)
            put_rows(grad_ref, (0,), u.row_at, u.lanes, grad * scale[0][:, u.lanes], order_ref, groups)
    totals[0] = spread(query_totals)
    for row_at in range(0, rows_all, ATTEND_BLOCK):
        rows = slice(row_at, row_at + ATTEND_BLOCK)
        for head in heads:
            lanes = slice(head, head + HEAD_DIM)
            grad = back(key_grad[rows, lanes] * HEAD_DIM ** (-0.5), rows)
            post = back(key_ref[0, rows, lanes].astype(F32), rows)
            part = jnp.sum(grad * post, axis=0, keepdims=True)
            query_totals[head // HEAD_DIM] = part if row_at == 0 else query_totals[head // HEAD_DIM] + part
            put_rows(grad_ref, (1,), row_at, lanes, grad * scale[1][:, lanes], order_ref, groups)
        grad = value_grad[rows, :]
        totals[2] = totals[2] + jnp.sum(grad * value_ref[0, rows, :].astype(F32), axis=0, keepdims=True)
        put_rows(grad_ref, (2,), row_at, slice(0, width), grad * scale[2], order_ref, groups)
    totals[1] = spread(query_totals)
    for m in range(3):
        total_ref[m] = totals[m] / scale[m]


def attend_back(order, groups, post, first, cos_table, sine_table, magnitude, squares, low, pieces):
    rows, width = post.shape[1:]
    depth = low.shape[2]
    wide = 2 * HEAD_DIM
    member = lambda m: pl.BlockSpec((1, rows, wide), lambda h, o: (m, 0, h))
    table = pl.BlockSpec((rows, HEAD_DIM), lambda h, o: (0, 0))
    column = pl.BlockSpec((3, 1, wide), lambda h, o: (0, 0, h))
    return call(
        "attend_back",
        functools.partial(attend_back_kernel, groups),
        (post, post, post, first, cos_table, sine_table, magnitude, squares, low, *pieces),
        (width // wide,),
        [
            member(0),
            member(1),
            member(2),
            pl.BlockSpec((rows, 1), lambda h, o: (0, 0)),
            table,
            table,
            pl.BlockSpec((3, wide), lambda h, o: (0, h)),
            column,
            pl.BlockSpec((1, wide, depth), lambda h, o: (0, h, 0)),
            *[pl.BlockSpec(memory_space=pl.ANY) for _ in pieces],
        ],
        [pl.BlockSpec((3, rows, wide), lambda h, o: (0, 0, h)), column],
        [shape((3, rows, width), LOW), shape((3, 1, width), F32)],
        scratch=[
            pltpu.VMEM((rows, depth), LOW),
            pltpu.VMEM((rows, wide), LOW),
            pltpu.VMEM((rows, wide), F32),
            pltpu.VMEM((rows, wide), F32),
            pltpu.SemaphoreType.DMA((len(pieces),)),
        ],
        prefetch=(order,),
        flops=10 * rows * rows * width + 2 * rows * width * depth,
        mib=48,
    )


def product_kernel(dims, n_totals, *refs):
    value_ref, weight_ref = refs[:2]
    groups = value_ref.shape[1]
    if n_totals == 0:
        left_ref, *refs = refs[2:]
    else:
        right_ref, squares_ref, magnitude_ref = refs[2:5]
        totals, refs = refs[5 : 5 + n_totals], refs[5 + n_totals :]
    outs, extra_ref, rows_all = refs[:groups], refs[groups], refs[groups + 1]
    members, _, share, inner = value_ref.shape
    count = groups * share

    @pl.when(pl.program_id(0) == 0)
    def _():
        if n_totals > 0:
            total = sum_refs(totals)
        for m in range(members):
            rows_all[m, :count, :] = value_ref[m].reshape(count, inner)
            if n_totals == 0:
                rows_all[m, count:, :] = left_ref[m].astype(LOW)
            else:
                weight = norm_weight(total[m], squares_ref[m], magnitude_ref[m : m + 1])
                rows_all[m, count:, :] = (right_ref[m] * weight).astype(LOW)

    result = None
    for m in range(members):
        part = dot(rows_all[m], weight_ref[m], dims)
        extra_ref[m] = part[count:]
        result = part[:count] if result is None else result + part[:count]
    for place, ref in enumerate(outs):
        ref[...] = result[place * share : (place + 1) * share].astype(LOW)


def product(name, values, weights, dims, left=None, correction=None):
    members, groups, share, inner = values.shape
    width = weights.shape[2] if dims is NN else weights.shape[1]
    wide = tile_of(width, 512)
    if dims is NN:
        weight_spec = pl.BlockSpec((members, inner, wide), lambda n: (0, 0, n))
    else:
        weight_spec = pl.BlockSpec((members, wide, inner), lambda n: (0, n, 0))
    if correction is None:
        extra, n_totals, rank = (left,), 0, left.shape[1]
    else:
        right, squares, magnitude, totals = correction
        extra, n_totals, rank = (right, squares, magnitude, *totals), len(totals), right.shape[1]
    fixed = lambda v: pl.BlockSpec(v.shape, lambda n: (0,) * v.ndim)
    out = pl.BlockSpec((share, wide), lambda n: (0, n))
    results = call(
        name,
        functools.partial(product_kernel, dims, n_totals),
        (values, weights, *extra),
        (width // wide,),
        [fixed(values), weight_spec] + [fixed(v) for v in extra],
        [out] * groups + [pl.BlockSpec((members, rank, wide), lambda n: (0, 0, n))],
        [shape((share, width), LOW)] * groups + [shape((members, rank, width), F32)],
        scratch=[pltpu.VMEM((members, groups * share + rank, inner), LOW)],
        flops=2 * members * groups * share * inner * width,
    )
    return results[:groups], results[groups]


def shrink_kernel(chips, order_ref, *refs):
    values, (weight_ref, left_ref, cot_ref), outs = refs[:chips], refs[chips : chips + 3], refs[chips + 3 :]
    total_ref, across_ref, rows_all = outs[-3:]
    _, _, share, inner = values[0].shape
    depth = left_ref.shape[2]
    count = chips * CORES * share

    @pl.when(pl.program_id(0) == 0)
    def _():
        for step, ref in enumerate(values):
            at = step * CORES * share
            rows_all[at : at + CORES * share, :] = ref[0].reshape(CORES * share, inner)
        if inner > depth:
            rows_all[count:, depth:] = jnp.zeros((rows_all.shape[0] - count, inner - depth), LOW)
        rows_all[count:, :depth] = left_ref[0].astype(LOW)

    result = dot(rows_all[...], weight_ref[0])
    across_ref[0] = result[count:]
    total = jnp.zeros((1, weight_ref.shape[2]), F32)
    for place in range(chips * CORES):
        pre = result[place * share : (place + 1) * share]
        outs[place][...] = pre.astype(LOW)
        at = pl.multiple_of(order_ref[place] * share, share)
        cot = cot_ref[pl.ds(at, share), :].astype(F32)
        total = total + jnp.sum(pre * cot, axis=0, keepdims=True)
    total_ref[...] = total


def shrink_product(order, values, weights, left, cotangent):
    chips = len(values)
    _, _, share, inner = values[0].shape
    width, rank = weights.shape[2], left.shape[1]
    rows = chips * CORES * share
    wide = tile_of(width, 512)
    fixed = lambda v: pl.BlockSpec(v.shape, lambda n, o: (0,) * v.ndim)
    results = call(
        "shrink_product",
        functools.partial(shrink_kernel, chips),
        (*values, weights, left, cotangent),
        (width // wide,),
        [fixed(v) for v in values]
        + [
            pl.BlockSpec((1, inner, wide), lambda n, o: (0, 0, n)),
            fixed(left),
            pl.BlockSpec((rows, wide), lambda n, o: (0, n)),
        ],
        [pl.BlockSpec((share, wide), lambda n, o: (0, n))] * (chips * CORES)
        + [
            pl.BlockSpec((1, wide), lambda n, o: (0, n)),
            pl.BlockSpec((1, rank, wide), lambda n, o: (0, 0, n)),
        ],
        [shape((share, width), LOW)] * (chips * CORES)
        + [shape((1, width), F32), shape((1, rank, width), F32)],
        scratch=[pltpu.VMEM((rows + rank, inner), LOW)],
        prefetch=(order,),
        flops=2 * rows * inner * width,
    )
    return results[: chips * CORES], results[-2], results[-1]


def row_call(name, kernel, order, given, whole, out_kinds, sums, prepare):
    share = min(v.shape[0] for v, _ in given)
    width = given[0][0].shape[1]
    halves = 2
    half = share // halves
    count = len(given)

    def run(order_ref, *refs):
        sources, rest = refs[:count], refs[count : -count - 1]
        held, sems = refs[-count - 1 : -1], refs[-1]

        def copies(part):
            for i, ((_, cut), source, target) in enumerate(zip(given, sources, held)):
                at = part * half
                if cut:
                    at = pl.multiple_of(order_ref[1] * share + at, half)
                yield pltpu.make_async_copy(
                    source.at[pl.ds(at, half), :],
                    target.at[pl.ds(part * half, half), :],
                    sems.at[part, i],
                )

        for part in range(halves):

            @pl.when(pl.program_id(0) == part)
            def _(part=part):
                if part == 0:
                    for each in range(halves):
                        for copy in copies(each):
                            copy.start()
                for copy in copies(part):
                    copy.wait()

        outs = rest[len(whole) : len(whole) + len(out_kinds)]
        totals, sums_held = rest[len(whole) + len(out_kinds) :][:sums], rest[len(rest) - sums :]
        tile = 32
        lines = prepare(*[ref[...] for ref in rest[: len(whole)]])
        for ref in sums_held:
            ref[...] = jnp.zeros_like(ref)

        def some(i, carry):
            inside = pl.ds(pl.multiple_of(i * tile, tile), tile)
            at = pl.ds(pl.multiple_of(pl.program_id(0) * half + i * tile, tile), tile)
            values = kernel([ref[at, :].astype(F32) for ref in held], *lines)
            for ref, value in zip(outs, values):
                ref[inside, :] = value.astype(ref.dtype)
            for ref, value in zip(sums_held, values[len(outs) :]):
                ref[...] += jnp.sum(value.reshape(tile // 8, 8, width), axis=0)
            return carry

        lax.fori_loop(0, half // tile, some, 0, unroll=2)
        for ref, held_ref in zip(totals, sums_held):
            add_column(ref, held_ref[...])

    line = pl.BlockSpec((1, width), lambda i, o: (0, 0))
    return call(
        name,
        run,
        (*[v for v, _ in given], *whole),
        (halves,),
        [pl.BlockSpec(memory_space=pl.ANY) for _ in given] + [line for _ in whole],
        [pl.BlockSpec((half, width), lambda i, o: (i, 0)) for _ in out_kinds]
        + [line for _ in range(sums)],
        [shape((share, width), kind) for kind in out_kinds]
        + [shape((1, width), F32) for _ in range(sums)],
        scratch=[pltpu.VMEM((8, width), F32) for _ in range(sums)]
        + [pltpu.VMEM((share, width), v.dtype) for v, _ in given]
        + [pltpu.SemaphoreType.DMA((halves, count))],
        prefetch=(order,),
        flops=20 * share * width,
    )


def sum_of(values):
    total = values[0]
    for value in values[1:]:
        total = total + value
    return total


def add_column(ref, values):
    part = jnp.sum(values, axis=0, keepdims=True)

    @pl.when(pl.program_id(0) == 0)
    def _():
        ref[...] = part

    @pl.when(pl.program_id(0) > 0)
    def _():
        ref[...] += part


def scale_first(squares, magnitude, *rest):
    norm = jnp.sqrt(squares)
    return (magnitude / norm, norm / magnitude, *rest)


def hidden_kernel(given, scale, inverse, gain):
    hidden = given[0] + sum_of(given[1:]) * scale
    return hidden, hidden * rms_rows(hidden) * gain


def mixed_kernel(given, scale, inverse):
    return (given[0] + sum_of(given[1:]) * scale,)


def norm_back(grad_normed, values, gain):
    factor = rms_rows(values)
    scaled = grad_normed * gain
    inner = jnp.mean(scaled * values, axis=1, keepdims=True)
    back = factor * scaled - values * (factor * factor * factor * inner)
    return back, grad_normed * values * factor


def hidden_back_kernel(given, scale, inverse, gain):
    cot, token, hidden = given[:3]
    back, gain_terms = norm_back(sum_of(given[3:]), hidden, gain)
    grad = cot + back
    return grad, grad * scale, grad * ((hidden - token) * inverse), gain_terms


def token_back_kernel(given, gain):
    back, gain_terms = norm_back(sum_of(given[2:]), given[0], gain)
    return given[1] + back, gain_terms


def shrink_back_kernel(order_ref, cot_ref, low_ref, squares_ref, magnitude_ref, product_ref, grad_ref):
    scale = magnitude_ref[0] / jnp.sqrt(squares_ref[0])
    grad = (cot_ref[...].astype(F32) * scale).astype(LOW)
    grad_ref[0] = grad
    product_ref[0] = dot(grad, low_ref[0], NT)


def shrink_back(order, cotangent, low, squares, magnitude, groups):
    rows, width = cotangent.shape
    share, inner = rows // groups, low.shape[1]
    line = pl.BlockSpec((1, 1, width), lambda j, o: (0, 0, 0))
    return call(
        "shrink_back",
        shrink_back_kernel,
        (cotangent, low, squares, magnitude),
        (groups,),
        [
            pl.BlockSpec((share, width), lambda j, o: (o[j], 0)),
            pl.BlockSpec((1, inner, width), lambda j, o: (0, 0, 0)),
            line,
            line,
        ],
        [
            pl.BlockSpec((1, share, inner), lambda j, o: (j, 0, 0)),
            pl.BlockSpec((1, share, width), lambda j, o: (j, 0, 0)),
        ],
        [shape((groups, share, inner), F32), shape((groups, share, width), LOW)],
        prefetch=(order,),
        flops=2 * rows * width * inner,
    )


def expand_kernel(first, last, n_totals, ff, *refs):
    other_ref, mine_ref, low_ref, squares_ref, magnitude_ref, grad_ref = refs[:6]
    refs = list(refs[6:])
    left_ref = refs.pop(0) if first else None
    right_ref = refs.pop(0) if last else None
    before = [refs.pop(0) for _ in range(n_totals)]
    product_ref, back_ref, total_ref, rows_ref, send_ref, keep_ref = refs[:6]
    refs = refs[6:]
    across_ref = refs.pop(0) if first else None
    extra_ref = refs.pop(0) if last else None
    rows_all, back_all, mid_sum = refs
    share, depth = other_ref.shape
    wide = low_ref.shape[2]
    both = CORES * share

    @pl.when(pl.program_id(0) == 0)
    def _():
        for at, ref in ((0, other_ref), (share, mine_ref)):
            rows_ref[at : at + share, :] = ref[...]
            rows_all[at : at + share, :] = ref[...]
        if first:
            rank = across_ref.shape[1]
            for m in range(2):
                rows_all[both + m * rank : both + (m + 1) * rank, :] = left_ref[m].astype(LOW)
        mid_sum[...] = jnp.zeros_like(mid_sum)

    lane = pl.program_id(0) * wide + lax.broadcasted_iota(jnp.int32, (1, wide), 1)
    magnitude = [jnp.where(lane < ff, magnitude_ref[m : m + 1], 0.0) for m in range(2)]
    scale = [magnitude[m] / jnp.sqrt(squares_ref[m]) for m in range(2)]
    tile = 256
    cuts = [slice(at, at + tile) for at in range(0, wide, tile)]
    pre = [[dot(rows_all[...], low_ref[m, :, cut]) for m in range(2)] for cut in cuts]
    for cut, (gate_all, up_all) in zip(cuts, pre):
        if first:
            across_ref[0, :, cut] = gate_all[both : both + rank_of(across_ref)]
            across_ref[1, :, cut] = up_all[both + rank_of(across_ref) :]
        sums = [jnp.zeros((1, tile), F32) for _ in range(2)]
        scales = [scale[m][:, cut] for m in range(2)]
        at = [slice(2 * cut.start + m * tile, 2 * cut.start + (m + 1) * tile) for m in range(2)]
        for place in range(CORES):
            rows = slice(place * share, (place + 1) * share)
            gate_pre, up_pre = gate_all[rows], up_all[rows]
            gate, up = gate_pre * scales[0], up_pre * scales[1]
            sigmoid = 0.5 + 0.5 * jnp.tanh(0.5 * gate)
            active = gate * sigmoid
            product_ref[0, place, :, cut] = (active * up).astype(LOW)
            upper = grad_ref[place, :, cut]
            grad_up = upper * active
            grad_gate = upper * up * sigmoid * (1.0 + gate * (1.0 - sigmoid))
            sums[0] += jnp.sum(grad_gate * gate_pre, axis=0, keepdims=True)
            sums[1] += jnp.sum(grad_up * up_pre, axis=0, keepdims=True)
            for m, low in enumerate((grad_gate * scales[0], grad_up * scales[1])):
                low = low.astype(LOW)
                back_ref[m, place, :, cut] = low
                back_all[rows, at[m]] = low
        for m in range(2):
            total_ref[m, :, cut] = sums[m]
        if last:
            rank = rank_of(extra_ref)
            for m in range(2):
                total = sums[m]
                for ref in before:
                    total = total + ref[m, :, cut]
                right = jnp.where(lane[:, cut] < ff, right_ref[m, :, cut], 0.0)
                weight = norm_weight(total, squares_ref[m, :, cut], magnitude[m][:, cut])
                rows = slice(both + m * rank, both + (m + 1) * rank)
                back_all[rows, at[m]] = (right * weight).astype(LOW)
                back_all[rows, at[1 - m]] = jnp.zeros((rank, tile), LOW)
        step = tile_of(depth, 512)
        now = slice(2 * cut.start, 2 * cut.stop)
        for start in range(0, depth, step):
            columns = slice(start, start + step)
            weights = jnp.concatenate(
                [low_ref[0, columns, cut], low_ref[1, columns, cut]], axis=1
            )
            mid_sum[:, columns] += dot(back_all[:, now], weights, NT)

    @pl.when(pl.program_id(0) == pl.num_programs(0) - 1)
    def _():
        send_ref[...] = mid_sum[:share, :].astype(LOW)
        keep_ref[...] = mid_sum[share:both, :].astype(LOW)
        if last:
            for m in range(2):
                extra_ref[m] = mid_sum[both + m * rank_of(extra_ref) : both + (m + 1) * rank_of(extra_ref), :]


def rank_of(ref):
    return ref.shape[1]


def expand(pieces, low, squares, magnitude, grad_product, step, left=None, right=None, before=()):
    share, depth = pieces[0].shape
    width = low.shape[2]
    first, last = left is not None, right is not None
    wide = 512 if width % 512 == 0 else 256
    rows = CORES * share
    fixed = lambda dims: pl.BlockSpec(tuple(dims), lambda n: (0,) * len(dims))
    column = pl.BlockSpec((2, 1, wide), lambda n: (0, 0, n))
    operands = [*pieces, low, squares, magnitude, grad_product]
    in_specs = [
        fixed((share, depth)),
        fixed((share, depth)),
        pl.BlockSpec((2, depth, wide), lambda n: (0, 0, n)),
        column,
        pl.BlockSpec((2, wide), lambda n: (0, n)),
        pl.BlockSpec((2, share, wide), lambda n: (step, 0, n)),
    ]
    out_specs = [
        pl.BlockSpec((1, 2, share, wide), lambda n: (0, 0, 0, n)),
        pl.BlockSpec((2, 2, share, wide), lambda n: (0, 0, 0, n)),
        column,
        fixed((rows, depth)),
        fixed((share, depth)),
        fixed((share, depth)),
    ]
    out_shape = [
        shape((1, 2, share, width), LOW),
        shape((2, 2, share, width), LOW),
        shape((2, 1, width), F32),
        shape((rows, depth), LOW),
        shape((share, depth), LOW),
        shape((share, depth), LOW),
    ]
    extra_in = extra_out = 0
    if first:
        rank = left.shape[1]
        extra_in = 2 * rank
        operands.append(left)
        in_specs.append(fixed(left.shape))
        out_specs.append(pl.BlockSpec((2, rank, wide), lambda n: (0, 0, n)))
        out_shape.append(shape((2, rank, width), F32))
    if last:
        rank = right.shape[1]
        extra_out = 2 * rank
        operands += [right, *before]
        in_specs.append(pl.BlockSpec((2, rank, wide), lambda n: (0, 0, n)))
        in_specs += [column for _ in before]
        out_specs.append(fixed((2, rank, depth)))
        out_shape.append(shape((2, rank, depth), F32))
    return call(
        "expand",
        functools.partial(expand_kernel, first, last, len(before), magnitude.shape[1]),
        tuple(operands),
        (width // wide,),
        in_specs,
        out_specs,
        out_shape,
        scratch=[
            pltpu.VMEM((rows + extra_in, depth), LOW),
            pltpu.VMEM((rows + extra_out, 2 * wide), LOW),
            pltpu.VMEM((rows + extra_out, depth), F32),
        ],
        flops=8 * rows * depth * width,
    )


def adapter_kernel(plan, n_inputs, n_grads, corrections, order_ref, *refs):
    count = n_inputs + n_grads
    sources, held, sems = refs[:count], refs[-count - 1 : -1], refs[-1]
    left_ref, right_ref = refs[count : count + 2]
    *corrected, left_out, right_out = refs[count + 2 : -count - 1]
    members, rank, width = right_ref.shape
    chunks = list(plan(order_ref, held[:n_inputs], held[n_inputs:]))
    copies = []
    for parts, _, _ in chunks:
        copies.append([])
        for which, index in parts:
            copy = pltpu.make_async_copy(
                sources[which].at[index],
                held[which].at[index],
                sems.at[sum(len(c) for c in copies)],
            )
            copy.start()
            copies[-1].append(copy)
    left_rows = jnp.concatenate([split_rows(left_ref[m]) for m in range(members)], axis=0)
    right_rows = [split_rows(right_ref[m]) for m in range(members)]
    left_out[...] = jnp.zeros_like(left_out)
    right_out[...] = jnp.zeros_like(right_out)
    for waits, (_, taken_of, grads_of) in zip(copies, chunks):
        for copy in waits:
            copy.wait()
        taken = taken_of()
        across = dot(left_rows, taken, NT)
        downs = []
        for m in range(members):
            grad = grads_of(m)
            mine = split_rows(fold(across[2 * rank * m : 2 * rank * (m + 1)]))
            right_out[m] += fold(dot(mine, grad))
            downs.append(split_rows(fold(dot(right_rows[m], grad, NT))))
        left = dot(jnp.concatenate(downs, axis=0), taken)
        for m in range(members):
            left_out[m] += fold(left[2 * rank * m : 2 * rank * (m + 1)])
    if corrections:
        correct(corrections, right_ref, left_out, right_out, left_out, right_out, *corrected)


def correct(n_totals, right_ref, left_in, right_in, left_out, right_out, *refs):
    back_ref, across_ref, squares_ref, magnitude_ref = refs[:4]
    totals, magnitude_out = refs[4 : 4 + n_totals], refs[4 + n_totals]
    members, rank, width = right_ref.shape
    total = sum_refs(totals)[:, :, :width]
    squares = squares_ref[:, :, :width]
    magnitude_out[...] = total / jnp.sqrt(squares)
    for m in range(members):
        weight = norm_weight(total[m], squares[m], magnitude_ref[m : m + 1])
        if back_ref.dtype == LOW:
            low = back_ref[m, : left_in.shape[2], :]
            back = fold(dot(split_rows(right_ref[m] * weight), low, NT))
        else:
            back = back_ref[m]
        left_out[m] = ADAPT_SCALE * (left_in[m] - back)
        right_out[m] = ADAPT_SCALE * (right_in[m] - across_ref[m][:, :width] * weight)


def correct_kernel(n_totals, order_ref, right_ref, left_in, right_in, *refs):
    *rest, left_out, right_out = refs
    correct(n_totals, right_ref, left_in, right_in, left_out, right_out, *rest)


def adapter(name, order, plan, inputs, grads, left, right, correction):
    members, rank, width = right.shape
    *given, totals = correction
    moved, fixed = [*inputs, *grads], [left, right, *given, *totals]
    full = lambda dims: pl.BlockSpec(tuple(dims), lambda i, o: (0,) * len(dims))
    outs = [(members, 1, width), (members, rank, left.shape[2]), (members, rank, width)]
    kernel = functools.partial(adapter_kernel, plan, len(inputs), len(grads), len(totals))
    return call(
        name,
        kernel,
        (*moved, *fixed),
        (1,),
        [pl.BlockSpec(memory_space=pl.ANY) for _ in moved] + [full(v.shape) for v in fixed],
        [full(dims) for dims in outs],
        [shape(dims, F32) for dims in outs],
        scratch=[pltpu.VMEM(v.shape, v.dtype) for v in moved] + [pltpu.SemaphoreType.DMA((32,))],
        prefetch=(order,),
        flops=sum(v.size for v in moved) * 64,
    )


MESH_IDS = pl.DeviceIdType.MESH


def copy_kernel(count, *refs):
    for source, target in zip(refs[:count], refs[count:]):
        target[...] = source[...]


def copy_out(arrays):
    vmem = pl.BlockSpec(memory_space=pltpu.VMEM)
    full = lambda v: pl.BlockSpec(v.shape, lambda i: (0,) * v.ndim)
    return call(
        "copy_out",
        functools.partial(copy_kernel, len(arrays)),
        tuple(arrays),
        (1,),
        [vmem for _ in arrays],
        [full(v) for v in arrays],
        [shape(v.shape, F32) for v in arrays],
        mib=16,
    )


GRAIN = 16


def pieces_of(width):
    return [(at, min(128, width - at)) for at in range(0, width, 128)]


def cells_of(blocks, lines, parts):
    cells, rows = [], []
    for n, block in enumerate(blocks):
        for m in range(block.shape[0]):
            for at, size in pieces_of(block.shape[2] // parts):
                cells.append((n, m, at, size))
    for n, line in enumerate(lines):
        for m in range(line.shape[0]):
            for at, size in pieces_of(line.shape[2] // parts):
                rows.append((n, m, at, size))
    return cells, rows


def pack(blocks, lines, wide_ref, part, parts, cells, rows):
    for i, (n, m, at, size) in enumerate(cells):
        start = part * (blocks[n].shape[2] // parts) + at
        wide_ref[part, i, :, :size] = blocks[n][m, :, start : start + size]
    for i, (n, m, at, size) in enumerate(rows):
        start = part * (lines[n].shape[2] // parts) + at
        cell, row = len(cells) + i // GRAIN, i % GRAIN
        wide_ref[part, cell, row : row + 1, :size] = lines[n][m, :, start : start + size]


def unpack(full_ref, blocks, lines, part, parts, cells, rows):
    for i, (n, m, at, size) in enumerate(cells):
        start = part * (blocks[n].shape[2] // parts) + at
        blocks[n][m, :, start : start + size] = full_ref[part, i].astype(F32)[:, :size]
    for i, (n, m, at, size) in enumerate(rows):
        start = part * (lines[n].shape[2] // parts) + at
        cell, row = len(cells) + i // GRAIN, i % GRAIN
        values = full_ref[part, cell].astype(F32)
        lines[n][m, :, start : start + size] = values[row : row + 1, :size]


def reduce_kernel(groups, lines, counts, *refs):
    n_all, n_all_lines, n_dp, n_dp_lines = counts
    count = sum(counts)
    taken, given, scratch = refs[:count], refs[count : 2 * count], refs[2 * count :]
    ends = [n_all, n_all + n_all_lines, n_all + n_all_lines + n_dp]
    parted = lambda v: (v[: ends[0]], v[ends[0] : ends[1]], v[ends[1] : ends[2]], v[ends[2] :])
    all_in, all_lines_in, dp_in, dp_lines_in = parted(taken)
    all_out, all_lines_out, dp_out, dp_lines_out = parted(given)
    (
        all_ref,
        line_ref,
        all_low,
        line_low,
        all_got,
        part,
        part_low,
        part_got,
        line_got,
        all_full,
        line_full,
        *sems,
    ) = scratch
    me, row = lax.axis_index("mp"), lax.axis_index("dp")
    piece, line_piece = part.shape[0] // lines, line_ref.shape[1] // lines
    mp_peer = [lax.rem(me + k, groups) for k in range(groups)]
    dp_peer = [lax.rem(row + k, lines) for k in range(lines)]
    barrier = pltpu.get_barrier_semaphore()
    for k in range(1, groups):
        pl.semaphore_signal(barrier, 1, device_id={"mp": mp_peer[k]}, device_id_type=MESH_IDS)
    for k in range(1, lines):
        pl.semaphore_signal(barrier, 1, device_id={"dp": dp_peer[k]}, device_id_type=MESH_IDS)
    all_cells = cells_of(all_in, all_lines_in, groups)
    dp_cells = cells_of(dp_in, dp_lines_in, 1)
    all_ref[...] = jnp.zeros_like(all_ref)
    line_ref[...] = jnp.zeros_like(line_ref)
    for q in range(groups):
        pack(all_in, all_lines_in, all_ref, q, groups, *all_cells)
    pack(dp_in, dp_lines_in, line_ref, 0, 1, *dp_cells)
    all_low[...] = all_ref[...].astype(LOW)
    line_low[...] = line_ref[...].astype(LOW)
    pl.semaphore_wait(barrier, groups + lines - 2)

    def send(source, target, stage, k, axis, peer):
        copy = pltpu.make_async_remote_copy(
            src_ref=source,
            dst_ref=target,
            send_sem=sems[2 * stage].at[k],
            recv_sem=sems[2 * stage + 1].at[k],
            device_id={axis: peer},
            device_id_type=MESH_IDS,
        )
        copy.start()
        return copy

    over_mp = [
        send(all_low.at[mp_peer[k]], all_got.at[k], 0, k, "mp", mp_peer[k])
        for k in range(1, groups)
    ]
    over_dp = [
        send(
            line_low.at[0, pl.ds(dp_peer[k] * line_piece, line_piece)],
            line_got.at[k],
            1,
            k,
            "dp",
            dp_peer[k],
        )
        for k in range(1, lines)
    ]
    total = all_ref[me]
    for k, copy in enumerate(over_mp, 1):
        copy.wait_recv()
        total = total + all_got[k].astype(F32)
    part[...] = total
    part_low[...] = total.astype(LOW)
    part_dp = [
        send(part_low.at[pl.ds(dp_peer[k] * piece, piece)], part_got.at[k], 2, k, "dp", dp_peer[k])
        for k in range(1, lines)
    ]
    held = pl.ds(row * piece, piece)
    total = part[held]
    for k, copy in enumerate(part_dp, 1):
        copy.wait_recv()
        total = total + part_got[k].astype(F32)
    all_full[me, held] = total.astype(LOW)
    part_back = [
        send(all_full.at[me, held], all_full.at[me, held], 4, k, "dp", dp_peer[k])
        for k in range(1, lines)
    ]
    mine = pl.ds(row * line_piece, line_piece)
    total = line_ref[0, mine]
    for k, copy in enumerate(over_dp, 1):
        copy.wait_recv()
        total = total + line_got[k].astype(F32)
    line_full[0, mine] = total.astype(LOW)
    line_back = [
        send(line_full.at[0, mine], line_full.at[0, mine], 3, k, "dp", dp_peer[k])
        for k in range(1, lines)
    ]
    for copy in part_back:
        copy.wait_recv()
    all_back = [
        send(all_full.at[me], all_full.at[me], 5, k, "mp", mp_peer[k]) for k in range(1, groups)
    ]
    for copy in line_back:
        copy.wait_recv()
    unpack(line_full, dp_out, dp_lines_out, 0, 1, *dp_cells)
    for copy in all_back:
        copy.wait_recv()
    for q in range(groups):
        unpack(all_full, all_out, all_lines_out, q, groups, *all_cells)
    for copy in over_mp + over_dp + part_dp + line_back + part_back + all_back:
        copy.wait_send()


def reduce_devices(name, identity, over_all, over_all_lines, over_dp, over_dp_lines):
    groups, lines = lax.axis_size("mp"), lax.axis_size("dp")

    def size_of(blocks, rows, parts):
        cells, lines_in = cells_of(blocks, rows, parts)
        size = len(cells) + -(-len(lines_in) // GRAIN)
        return -(-size // lines) * lines

    count, line_count = size_of(over_all, over_all_lines, groups), size_of(over_dp, over_dp_lines, 1)
    operands = (*over_all, *over_all_lines, *over_dp, *over_dp_lines)
    counts = (len(over_all), len(over_all_lines), len(over_dp), len(over_dp_lines))
    vmem = pl.BlockSpec(memory_space=pltpu.VMEM)
    tail = (GRAIN, 128)
    sizes = (groups, lines, lines, lines, lines, groups)
    every, line = (groups, count) + tail, (1, line_count) + tail
    results = pl.pallas_call(
        functools.partial(reduce_kernel, groups, lines, counts),
        name=name,
        out_shape=[shape(v.shape, F32) for v in operands],
        in_specs=[vmem for _ in operands],
        out_specs=[vmem for _ in operands],
        scratch_shapes=[
            pltpu.VMEM(every, F32),
            pltpu.VMEM(line, F32),
            pltpu.VMEM(every, LOW),
            pltpu.VMEM(line, LOW),
            pltpu.VMEM(every, LOW),
            pltpu.VMEM((count,) + tail, F32),
            pltpu.VMEM((count,) + tail, LOW),
            pltpu.VMEM((lines, count // lines) + tail, LOW),
            pltpu.VMEM((lines, line_count // lines) + tail, LOW),
            pltpu.VMEM(every, LOW),
            pltpu.VMEM(line, LOW),
        ]
        + [pltpu.SemaphoreType.DMA((n,)) for n in sizes for _ in range(2)],
        compiler_params=pltpu.CompilerParams(
            collective_id=identity, has_side_effects=True, vmem_limit_bytes=32 * 2**20
        ),
        cost_estimate=pl.CostEstimate(flops=1000, bytes_accessed=2**20, transcendentals=0),
    )(*operands)
    return copy_out(results)


def first_places(segment):
    length = segment.shape[0]
    places = lax.broadcasted_iota(jnp.int32, (length, length), 0)
    others = lax.broadcasted_iota(jnp.int32, (length, length), 1)
    visible = (segment[:, None] == segment[None, :]) & (others <= places)
    offset = jnp.sum(visible.astype(F32), axis=1) - 1.0
    return (jnp.arange(length, dtype=jnp.int32) - offset.astype(jnp.int32))[:, None]


def body(
    tokens,
    cotangent,
    segment_ids,
    attend_gain,
    expand_gain,
    heads_base,
    heads_left,
    heads_right,
    heads_magnitude,
    output_base,
    output_left,
    output_right,
    output_magnitude,
    expand_base,
    expand_left,
    expand_right,
    expand_magnitude,
    shrink_base,
    shrink_left,
    shrink_right,
    shrink_magnitude,
):
    groups = lax.axis_size("mp")
    chips = groups // CORES
    index = lax.axis_index("mp")
    chip, core = index // CORES, index % CORES
    rows, width = tokens.shape
    share = rows // groups
    local_heads, ff = heads_base.shape[2], expand_base.shape[2]
    ff_wide = padded(ff)
    device = jnp.arange(groups, dtype=jnp.int32)
    order = jnp.concatenate(
        [
            (chip + device // CORES) % chips * CORES + (core + 1 + device) % CORES,
            (device // CORES + chips - chip) % chips * CORES + (device + CORES - core + 1) % CORES,
        ]
    ).astype(jnp.int32)

    def tie(*values):
        return lax.optimization_barrier(values)

    def sibling(values):
        return lax.ppermute(
            values, "mp", [(i, i // CORES * CORES + (i + 1) % CORES) for i in range(groups)]
        )

    def to_chip(values, step):
        return lax.ppermute(
            values,
            "mp",
            [((i, ((i // CORES + step) % chips) * CORES + i % CORES)) for i in range(groups)],
        )

    def mp_sum(values):
        values = values + sibling(values)
        total = values
        for step in range(1, chips):
            total = total + to_chip(values, step)
        return total

    def join(pair):
        return (pair[1].astype(F32) + sibling(pair[0]).astype(F32)).astype(LOW)

    def chip_pairs(places):
        return [places[CORES * step : CORES * (step + 1)] for step in range(chips)]

    def arrive(own):
        return [to_chip(own, chips - step) for step in range(1, chips)]

    def pairs_of(own, near_sibling, arrived):
        return [(near_sibling, own)] + [(sibling(piece), piece) for piece in arrived]

    def in_pairs(order_ref, inputs, grads):
        for step, (taken, grad) in enumerate(zip(inputs, grads)):
            yield (
                [(step, ...), (chips + step, ...)],
                lambda taken=taken: taken[...],
                lambda m, grad=grad: grad[m].reshape(-1, grad.shape[-1])[:, :ff],
            )

    def in_shrink(order_ref, inputs, grads):
        for step, taken in enumerate(inputs):
            at = slice(CORES * step, CORES * (step + 1))
            yield (
                [(step, ...), (chips, pl.ds(CORES * step, CORES))],
                lambda taken=taken: taken[0].reshape(-1, taken.shape[-1])[:, :ff],
                lambda m, at=at: grads[0][at].reshape(-1, grads[0].shape[-1]),
            )

    def in_output(order_ref, inputs, grads):
        for place, grad in enumerate(grads):
            yield (
                [(0, (0, place)), (1 + place, ...)],
                lambda place=place: inputs[0][0, place],
                lambda m, grad=grad: grad[...],
            )

    def in_heads(order_ref, inputs, grads):
        for place in range(groups):
            at = pl.multiple_of(order_ref[place] * share, share)
            rows = pl.ds(place * share, share)
            yield (
                [(0, pl.ds(at, share)), (1, (slice(None), rows))],
                lambda at=at: inputs[0][pl.ds(at, share), :],
                lambda m, rows=rows: grads[0][m, rows, :],
            )

    heads_rows, output_rows = turned(heads_left), turned(output_left[None])
    expand_rows, shrink_rows = turned(expand_left), turned(shrink_left[None])
    heads_mag, output_mag = heads_magnitude, output_magnitude[None]
    expand_mag, shrink_mag = expand_magnitude, shrink_magnitude[None]
    attend_line, expand_line = attend_gain[None], expand_gain[None]

    output_low, shrink_low, squares_part = merge_pair(
        [(output_base, output_rows[0], output_right), (shrink_base, shrink_rows[0], shrink_right)]
    )
    output_low, shrink_low = output_low[None], shrink_low[None]
    tokens, squares_part = tie(tokens, squares_part)
    squares = mp_sum(squares_part)
    first = first_places(segment_ids.reshape(-1))
    normed, heads_low, post, heads_sq, heads_across, cos_table, sine_table = project_heads(
        tokens, attend_line, heads_base, heads_rows, heads_right, heads_mag, first
    )
    heads_out = attend(order, groups, post, first)
    heads_out, squares = tie(heads_out, squares)
    output_sq, shrink_sq = squares[None, :1], squares[None, 1:]
    heads_parts = heads_out.reshape(1, groups, share, local_heads)
    output_places, output_across = product(
        "output_product", heads_parts, output_low, NN, left=output_rows
    )
    output_pairs = chip_pairs(output_places)
    joined = [join(pair) for pair in output_pairs[1:]]
    joined, expand_right_tied = tie(joined, expand_right)
    output_arrived = [to_chip(values, step) for step, values in enumerate(joined, 1)]
    expand_low, expand_sq = merge(
        expand_base, expand_rows, expand_right_tied, 512, expand_base.shape[2]
    )
    grad_product, shrink_grad = shrink_back(
        order, cotangent, shrink_low, shrink_sq, shrink_mag[None], groups
    )
    output_parts = [output_pairs[0][1], sibling(output_pairs[0][0]), *output_arrived]
    output_parts, expand_low, grad_product = tie(output_parts, expand_low, grad_product)
    hidden, normed_own = row_call(
        "hidden",
        hidden_kernel,
        order,
        [(tokens, True)] + [(part, False) for part in output_parts],
        (output_sq[0], output_mag, expand_line),
        (F32, LOW),
        0,
        scale_first,
    )

    def feed(pieces, step, **extra):
        return expand(pieces, expand_low, expand_sq, expand_mag, grad_product, step, **extra)

    arrived, near_sibling = arrive(normed_own), sibling(normed_own)
    fed = [feed((near_sibling, normed_own), 0, left=expand_rows)]
    arrived, fed = tie(arrived, fed)
    fed = list(fed)
    mid_sibling = sibling(fed[0][4])
    normed_mid = pairs_of(normed_own, near_sibling, arrived)
    for step in range(1, chips):
        extra = {}
        if step == chips - 1:
            extra = {"right": expand_right, "before": [f[2] for f in fed]}
        fed.append(feed(normed_mid[step], step, **extra))
    expand_totals = [f[2] for f in fed]
    joined = [join(f[4:6]) for f in fed[1:]]
    joined, shrink_rows_tied = tie(joined, shrink_rows)
    mid_arrived = [to_chip(values, step) for step, values in enumerate(joined, 1)]
    shrink_places, shrink_total, shrink_across = shrink_product(
        order, [f[0] for f in fed], shrink_low, shrink_rows_tied, cotangent
    )
    shrink_pairs = chip_pairs(shrink_places)
    shrink_total = mp_sum(shrink_total)
    expand_adapter = adapter(
        "expand_adapter",
        order,
        in_pairs,
        [f[3] for f in fed],
        [f[1] for f in fed],
        expand_rows,
        expand_right,
        (fed[-1][6], fed[0][6], expand_sq, expand_mag, expand_totals),
    )
    mid_parts = [fed[0][5], mid_sibling, *mid_arrived]
    mid_parts, shrink_pairs, expand_adapter = tie(mid_parts, shrink_pairs, expand_adapter)
    grad_hidden, output_grad_own, output_total, expand_gain_part = row_call(
        "hidden_back",
        hidden_back_kernel,
        order,
        [(cotangent, True), (tokens, True), (hidden, False)]
        + [(part, False) for part in mid_parts],
        (output_sq[0], output_mag, expand_line),
        (F32, LOW),
        2,
        scale_first,
    )
    output_grad_own, shrink_total = tie(output_grad_own, shrink_total)
    arrived, near_sibling = arrive(output_grad_own), sibling(output_grad_own)
    output_total = mp_sum(output_total)
    shrink_joined = [join(pair) for pair in shrink_pairs[1:]]
    shrink_joined, shrink_rows_tied = tie(shrink_joined, shrink_rows)
    shrink_adapter = adapter(
        "shrink_adapter",
        order,
        in_shrink,
        [f[0] for f in fed],
        [shrink_grad],
        shrink_rows_tied,
        shrink_right[None],
        (shrink_low, shrink_across, shrink_sq, shrink_mag, [shrink_total[None]]),
    )
    arrived, near_sibling, output_total, shrink_joined, shrink_adapter = tie(
        arrived, near_sibling, output_total, shrink_joined, shrink_adapter
    )
    output_grad = [
        piece for pair in pairs_of(output_grad_own, near_sibling, arrived) for piece in pair
    ]
    shrink_parts = [shrink_pairs[0][1], sibling(shrink_pairs[0][0])] + [
        to_chip(values, step) for step, values in enumerate(shrink_joined, 1)
    ]
    heads_grads, heads_total = attend_back(
        order,
        groups,
        post,
        first,
        cos_table,
        sine_table,
        heads_mag,
        heads_sq,
        output_low,
        output_grad,
    )
    grad_parts = heads_grads.reshape(3, groups, share, local_heads)
    token_places, token_extra = product(
        "normed_product",
        grad_parts,
        heads_low,
        NT,
        correction=(heads_right, heads_sq, heads_mag, [heads_total]),
    )
    token_places, shrink_parts = tie(token_places, shrink_parts)
    token_pairs = chip_pairs(token_places)
    joined = [join(pair) for pair in token_pairs[1:]]
    joined, heads_rows_tied, output_rows_tied = tie(joined, heads_rows, output_rows)
    token_arrived = [to_chip(values, step) for step, values in enumerate(joined, 1)]
    output_adapter = adapter(
        "output_adapter",
        order,
        in_output,
        [heads_parts],
        output_grad,
        output_rows_tied,
        output_right[None],
        (output_low, output_across, output_sq, output_mag, [output_total[None]]),
    )
    heads_adapter = adapter(
        "heads_adapter",
        order,
        in_heads,
        [normed],
        [heads_grads],
        heads_rows_tied,
        heads_right,
        (token_extra, heads_across, heads_sq, heads_mag, [heads_total]),
    )
    (mixed,) = row_call(
        "mixed",
        mixed_kernel,
        order,
        [(hidden, False)] + [(part, False) for part in shrink_parts],
        (shrink_sq[0], shrink_mag),
        (LOW,),
        0,
        scale_first,
    )
    token_parts = [token_pairs[0][1], sibling(token_pairs[0][0]), *token_arrived]
    token_parts, output_adapter, heads_adapter, mixed = tie(
        token_parts, output_adapter, heads_adapter, mixed
    )
    grad_tokens, attend_gain_part = row_call(
        "token_back",
        token_back_kernel,
        order,
        [(tokens, True), (grad_hidden, False)] + [(part, False) for part in token_parts],
        (attend_line,),
        (F32,),
        1,
        lambda gain: (gain,),
    )
    (
        expand_left_grad,
        shrink_right_grad,
        heads_left_grad,
        output_right_grad,
        expand_gain_grad,
        attend_gain_grad,
        expand_right_grad,
        shrink_left_grad,
        heads_right_grad,
        output_left_grad,
        expand_mag_grad,
        shrink_mag_grad,
        heads_mag_grad,
        output_mag_grad,
    ) = reduce_devices(
        "reduce_gradients",
        1,
        [expand_adapter[1], shrink_adapter[2], heads_adapter[1], output_adapter[2]],
        [expand_gain_part[None], attend_gain_part[None]],
        [expand_adapter[2], shrink_adapter[1], heads_adapter[2], output_adapter[1]],
        [expand_adapter[0], shrink_adapter[0], heads_adapter[0], output_adapter[0]],
    )
    return (
        mixed,
        grad_tokens,
        attend_gain_grad[0, 0],
        expand_gain_grad[0, 0],
        jnp.swapaxes(heads_left_grad, 1, 2),
        heads_right_grad,
        heads_mag_grad[:, 0],
        output_left_grad[0].T,
        output_right_grad[0],
        output_mag_grad[0, 0],
        jnp.swapaxes(expand_left_grad, 1, 2),
        expand_right_grad,
        expand_mag_grad[:, 0],
        shrink_left_grad[0].T,
        shrink_right_grad[0],
        shrink_mag_grad[0, 0],
    )


def solution(mesh):
    placed = (
        P("dp", None),
        P("dp", None),
        P("dp", None),
        P(),
        P(),
        P(None, None, "mp"),
        P(),
        P(None, None, "mp"),
        P(None, "mp"),
        P("mp", None),
        P("mp", None),
        P(),
        P(),
        P(None, None, "mp"),
        P(),
        P(None, None, "mp"),
        P(None, "mp"),
        P("mp", None),
        P("mp", None),
        P(),
        P(),
    )
    return jax.shard_map(
        body,
        mesh=mesh,
        in_specs=placed,
        out_specs=(
            P(("dp", "mp"), None),
            P(("dp", "mp"), None),
            P(),
            P(),
            P(),
            P(None, None, "mp"),
            P(None, "mp"),
            P("mp", None),
            P(),
            P(),
            P(),
            P(None, None, "mp"),
            P(None, "mp"),
            P("mp", None),
            P(),
            P(),
        ),
        check_vma=False,
    )
```

```python
import functools

import jax
import jax.numpy as jnp
import ml_dtypes
import numpy as np
from jax import lax
from jax.experimental import pallas as pl
from jax.experimental.pallas import tpu as pltpu
from jax.sharding import PartitionSpec as P

HEAD_DIM = 128
CORES = 2
LONGEST = 512
ATTEND_BLOCK = 256
ADAPT_SCALE = 2.0
NORM_EPS = 1e-05
ROPE_BASE = 10000.0
MASKED = -1e30

F32 = jnp.float32
LOW = jnp.bfloat16
NN = (((1,), (0,)), ((), ()))
NT = (((1,), (1,)), ((), ()))
TN = (((0,), (0,)), ((), ()))


def dot(left, right, dims=NN):
    return lax.dot_general(left, right, dims, preferred_element_type=F32)


def shape(dims, kind):
    return jax.ShapeDtypeStruct(tuple(dims), kind)


def call(name, kernel, operands, grid, in_specs, out_specs, out_shape, scratch=(), prefetch=(), flops=0, mib=60):
    moved = sum(v.size * v.dtype.itemsize for v in operands)
    moved += sum(v.size * v.dtype.itemsize for v in out_shape)
    return pl.pallas_call(
        kernel,
        name=name,
        out_shape=out_shape,
        grid_spec=pltpu.PrefetchScalarGridSpec(
            num_scalar_prefetch=len(prefetch),
            grid=grid,
            in_specs=in_specs,
            out_specs=out_specs,
            scratch_shapes=scratch,
        ),
        compiler_params=pltpu.CompilerParams(vmem_limit_bytes=mib * 2**20),
        cost_estimate=pl.CostEstimate(flops=flops // 16, bytes_accessed=moved // 16, transcendentals=0),
    )(*prefetch, *operands)


def tile_of(size, most):
    return most if size % most == 0 else size


def split_rows(values):
    top = values.astype(LOW)
    rest = (values - top.astype(F32)).astype(LOW)
    return jnp.concatenate([top, rest], axis=0)


def turned(left_map):
    return jnp.swapaxes(left_map, -1, -2)


def norm_weight(total, squares, magnitude):
    norm = jnp.sqrt(squares)
    return total * magnitude / (norm * norm * norm)


def sum_refs(refs):
    total = refs[0][...]
    for ref in refs[1:]:
        total = total + ref[...]
    return total


def fold(values):
    half = values.shape[0] // 2
    return values[:half] + values[half:]


def merge_tile(base_at, low_put, left, right, depth):
    rank = right.shape[0]
    doubled = ADAPT_SCALE * right
    top = doubled.astype(LOW)
    rest = (doubled - top.astype(F32)).astype(LOW)
    right_stack = jnp.concatenate([top, rest, top], axis=0)
    left_pair = split_rows(left)
    left_stack = jnp.concatenate([left_pair[:rank], left_pair[:rank], left_pair[rank:]], axis=0)
    squares = jnp.zeros((1, right.shape[1]), F32)
    step = tile_of(depth, 1024)
    for start in range(0, depth, step):
        merged = base_at(start, step).astype(F32) + dot(
            left_stack[:, start : start + step], right_stack, TN
        )
        low_put(start, step, merged.astype(LOW))
        squares = squares + jnp.sum(merged * merged, axis=0, keepdims=True)
    return squares


def merge_pair_kernel(*refs):
    for n in range(2):
        base_ref, left_ref, right_ref = refs[3 * n : 3 * n + 3]
        low_ref, squares_ref = refs[6 + n], refs[8]
        depth = base_ref.shape[0]
        if low_ref.shape[0] > depth:
            low_ref[depth:, :] = jnp.zeros((low_ref.shape[0] - depth, low_ref.shape[1]), LOW)

        def put(start, step, tile, low_ref=low_ref):
            low_ref[start : start + step, :] = tile

        squares_ref[n : n + 1, :] = merge_tile(
            lambda start, step, base_ref=base_ref: base_ref[start : start + step, :],
            put,
            left_ref[...],
            right_ref[...],
            depth,
        )


def merge_pair(triples):
    operands, in_specs, low_specs, low_shapes = [], [], [], []
    width = triples[0][0].shape[1]
    wide = tile_of(width, 512)
    for base, left, right in triples:
        depth, rank = base.shape[0], right.shape[0]
        operands += [base, left, right]
        in_specs += [
            pl.BlockSpec((depth, wide), lambda n: (0, n)),
            pl.BlockSpec((rank, depth), lambda n: (0, 0)),
            pl.BlockSpec((rank, wide), lambda n: (0, n)),
        ]
        low_specs.append(pl.BlockSpec((padded(depth), wide), lambda n: (0, n)))
        low_shapes.append(shape((padded(depth), width), LOW))
    return call(
        "merge_pair",
        merge_pair_kernel,
        tuple(operands),
        (width // wide,),
        in_specs,
        low_specs + [pl.BlockSpec((2, wide), lambda n: (0, n))],
        low_shapes + [shape((2, width), F32)],
        flops=2 * sum(v.size for v in operands) * 256,
    )


def merge_kernel(base_ref, left_ref, right_ref, low_ref, squares_ref):
    depth, width = base_ref.shape[1:]
    if low_ref.shape[1] > depth:
        low_ref[0, depth:, :] = jnp.zeros((low_ref.shape[1] - depth, low_ref.shape[2]), LOW)
    if low_ref.shape[2] > width:
        spare = low_ref.shape[2] - width
        low_ref[0, :, width:] = jnp.zeros((low_ref.shape[1], spare), LOW)
        squares_ref[0, :, width:] = jnp.ones((1, spare), F32)

    def put(start, step, tile):
        low_ref[0, start : start + step, :width] = tile

    squares = merge_tile(
        lambda start, step: base_ref[0, start : start + step, :],
        put,
        left_ref[0],
        right_ref[0],
        depth,
    )

    @pl.when(pl.program_id(2) == 0)
    def _():
        squares_ref[0, :, :width] = squares

    @pl.when(pl.program_id(2) > 0)
    def _():
        squares_ref[0, :, :width] += squares


def padded(size):
    return -(-size // 256) * 256


def pad_last(values, size):
    return jnp.pad(values, [(0, 0)] * (values.ndim - 1) + [(0, size - values.shape[-1])])


def merge(base, left, right, deep, wide):
    members, depth, width = base.shape
    low_deep = padded(deep) if deep == depth else deep
    low_wide = padded(wide) if wide == width else wide
    low_shape = (members, depth // deep * low_deep, width // wide * low_wide)
    rank = right.shape[1]
    return call(
        "merge",
        merge_kernel,
        (base, left, right),
        (members, width // wide, depth // deep),
        [
            pl.BlockSpec((1, deep, wide), lambda m, n, k: (m, k, n)),
            pl.BlockSpec((1, rank, deep), lambda m, n, k: (m, 0, k)),
            pl.BlockSpec((1, rank, wide), lambda m, n, k: (m, 0, n)),
        ],
        [
            pl.BlockSpec((1, low_deep, low_wide), lambda m, n, k: (m, k, n)),
            pl.BlockSpec((1, 1, low_wide), lambda m, n, k: (m, 0, n)),
        ],
        [shape(low_shape, LOW), shape((members, 1, low_shape[2]), F32)],
        flops=2 * members * depth * width * 256,
    )


def rms_rows(values):
    return lax.rsqrt(jnp.mean(values * values, axis=1, keepdims=True) + NORM_EPS)


TABLE_STEP = 32


def table_pieces(places):
    half = np.arange(HEAD_DIM) % (HEAD_DIM // 2)
    angles = np.asarray(places)[:, None] * ROPE_BASE ** (-2.0 * half / HEAD_DIM)[None, :]
    rest = np.concatenate([np.cos(angles), np.sin(angles)], axis=1)
    pieces = []
    for _ in range(3):
        pieces.append(rest.astype(ml_dtypes.bfloat16))
        rest = rest - pieces[-1].astype(np.float64)
    return jnp.asarray(np.concatenate(pieces, axis=0))


def rotation(first, coarse, fine):
    rows = first.shape[0]
    position = lax.broadcasted_iota(jnp.int32, (rows, 1), 0) - first
    lane = lax.broadcasted_iota(jnp.int32, (rows, 3 * TABLE_STEP), 1) % TABLE_STEP
    pick = lambda place, table: dot((lane == place).astype(F32).astype(LOW), table)
    high = pick(position // TABLE_STEP, coarse)
    small = pick(position % TABLE_STEP, fine)
    cos_a, sin_a = high[:, :HEAD_DIM], high[:, HEAD_DIM:]
    cos_b, sin_b = small[:, :HEAD_DIM], small[:, HEAD_DIM:]
    sine = sin_a * cos_b + cos_a * sin_b
    left_half = lax.broadcasted_iota(jnp.int32, sine.shape, 1) < HEAD_DIM // 2
    return cos_a * cos_b - sin_a * sin_b, jnp.where(left_half, -sine, sine)


def heads_kernel(
    token_ref,
    gain_ref,
    base_ref,
    left_ref,
    right_ref,
    magnitude_ref,
    first_ref,
    coarse_ref,
    fine_ref,
    normed_ref,
    low_ref,
    post_ref,
    squares_ref,
    across_ref,
    cos_ref,
    sine_ref,
    rows_all,
):
    total_rows = token_ref.shape[0]
    depth, width = base_ref.shape[1:]
    rank = right_ref.shape[1]

    @pl.when(pl.program_id(0) == 0)
    def _():
        step = 128

        def some(i, carry):
            at = pl.ds(pl.multiple_of(i * step, step), step)
            values = token_ref[at, :].astype(F32)
            low = (values * rms_rows(values) * gain_ref[...]).astype(LOW)
            normed_ref[at, :] = low
            rows_all[at, :] = low
            return carry

        lax.fori_loop(0, total_rows // step, some, 0)
        for start in range(0, total_rows, 256):
            rows = slice(start, start + 256)
            cosine, sine = rotation(first_ref[rows, :] - start, coarse_ref[...], fine_ref[...])
            cos_ref[rows, :] = cosine
            sine_ref[rows, :] = sine

    rows_all[total_rows:, :] = left_ref[0].astype(LOW)
    turning = pl.program_id(0) < 2
    wide = 256
    for column in range(0, width, wide):
        columns = slice(column, column + wide)

        def put(start, step, tile, columns=columns):
            low_ref[0, start : start + step, columns] = tile

        squares_ref[0, :, columns] = merge_tile(
            lambda start, step, columns=columns: base_ref[0, start : start + step, columns],
            put,
            left_ref[0],
            right_ref[0, :, columns],
            depth,
        )
    for column in range(0, width, wide):
        columns = slice(column, column + wide)
        magnitude = magnitude_ref[pl.ds(pl.program_id(0), 1), columns]
        scale = magnitude / jnp.sqrt(squares_ref[0, :, columns])
        low = low_ref[0, :, columns]
        step = min(512, total_rows)
        for start in range(0, total_rows, step):
            last = start + step == total_rows
            rows = slice(start, start + step)
            pre = dot(rows_all[start : start + step + (rank if last else 0), :], low)
            if last:
                across_ref[0, :, columns] = pre[step:]
            post = pre[:step] * scale
            cos_table = jnp.where(turning, cos_ref[rows, :], 1.0)
            sine_table = jnp.where(turning, sine_ref[rows, :], 0.0)
            for head in range(0, wide, HEAD_DIM):
                piece = post[:, head : head + HEAD_DIM]
                other = pltpu.roll(piece, HEAD_DIM // 2, 1)
                post_ref[0, rows, column + head : column + head + HEAD_DIM] = (
                    piece * cos_table + other * sine_table
                ).astype(LOW)


def project_heads(tokens, gain, base, left, right, magnitude, first):
    members, depth, width = base.shape
    rows, rank = tokens.shape[0], right.shape[1]
    coarse = table_pieces(np.arange(TABLE_STEP) * TABLE_STEP)
    fine = table_pieces(np.arange(TABLE_STEP))
    whole = lambda v: pl.BlockSpec(v.shape, lambda m: (0,) * v.ndim)
    of_member = lambda *dims: pl.BlockSpec((1,) + dims, lambda m: (m, 0, 0))
    table = pl.BlockSpec((rows, HEAD_DIM), lambda m: (0, 0))
    return call(
        "project_heads",
        heads_kernel,
        (tokens, gain, base, left, right, magnitude, first, coarse, fine),
        (members,),
        [
            whole(tokens),
            whole(gain),
            of_member(depth, width),
            of_member(rank, depth),
            of_member(rank, width),
            whole(magnitude),
            whole(first),
            whole(coarse),
            whole(fine),
        ],
        [
            whole(tokens),
            of_member(depth, width),
            of_member(rows, width),
            of_member(1, width),
            of_member(rank, width),
            table,
            table,
        ],
        [
            shape((rows, depth), LOW),
            shape(base.shape, LOW),
            shape((members, rows, width), LOW),
            shape((members, 1, width), F32),
            shape((members, rank, width), F32),
            shape((rows, HEAD_DIM), F32),
            shape((rows, HEAD_DIM), F32),
        ],
        scratch=[pltpu.VMEM((rows + rank, depth), LOW)],
        flops=2 * members * rows * depth * width,
    )


def key_start(block):
    return max(0, (block * ATTEND_BLOCK - (LONGEST - 1)) // ATTEND_BLOCK * ATTEND_BLOCK)


def masked_probs(scores, first, row_at, key_at):
    scores = scores * HEAD_DIM ** (-0.5)
    places = row_at + lax.broadcasted_iota(jnp.int32, scores.shape, 0)
    others = key_at + lax.broadcasted_iota(jnp.int32, scores.shape, 1)
    scores = jnp.where((others >= first) & (others <= places), scores, MASKED)
    exp_scores = jnp.exp(scores - jnp.max(scores, axis=1, keepdims=True))
    return exp_scores * (1.0 / jnp.sum(exp_scores, axis=1, keepdims=True))


class Unit:
    def __init__(self, head, block):
        self.row_at, self.key_at = block * ATTEND_BLOCK, key_start(block)
        self.rows = slice(self.row_at, self.row_at + ATTEND_BLOCK)
        self.keys = slice(self.key_at, self.row_at + ATTEND_BLOCK)
        self.lanes = slice(head * HEAD_DIM, (head + 1) * HEAD_DIM)


def units_of(rows, width, most):
    units = [
        Unit(head, block)
        for block in range(rows // ATTEND_BLOCK)
        for head in range(width // HEAD_DIM)
    ]
    return [units[at : at + most] for at in range(0, len(units), most)]


def put_rows(ref, lead, row_at, lanes, values, order_ref, groups):
    share = ref.shape[len(lead)] // groups
    step = min(share, values.shape[0])
    for start in range(0, values.shape[0], step):
        group = (row_at + start) // share
        inside = (row_at + start) % share
        at = pl.multiple_of(order_ref[groups + group] * share + inside, step)
        ref[(*lead, pl.ds(at, step), lanes)] = values[start : start + step].astype(ref.dtype)


def attend_kernel(groups, order_ref, query_ref, key_ref, value_ref, first_ref, out_ref):
    for some in units_of(*query_ref.shape[1:], 4):
        scores = [
            dot(query_ref[0, u.rows, u.lanes], key_ref[0, u.keys, u.lanes], NT) for u in some
        ]
        probs = [
            masked_probs(s, first_ref[u.rows, :], u.row_at, u.key_at).astype(LOW)
            for u, s in zip(some, scores)
        ]
        for u, p in zip(some, probs):
            mixed = dot(p, value_ref[0, u.keys, u.lanes])
            put_rows(out_ref, (), u.row_at, u.lanes, mixed, order_ref, groups)


def attend(order, groups, post, first):
    rows, width = post.shape[1:]
    wide = 2 * HEAD_DIM
    member = lambda m: pl.BlockSpec((1, rows, wide), lambda h, o: (m, 0, h))
    return call(
        "attend",
        functools.partial(attend_kernel, groups),
        (post, post, post, first),
        (width // wide,),
        [member(0), member(1), member(2), pl.BlockSpec((rows, 1), lambda h, o: (0, 0))],
        [pl.BlockSpec((rows, wide), lambda h, o: (0, h))],
        [shape((rows, width), LOW)],
        prefetch=(order,),
        flops=4 * rows * rows * width,
        mib=32,
    )[0]


def attend_back_kernel(
    groups,
    order_ref,
    query_ref,
    key_ref,
    value_ref,
    first_ref,
    cos_ref,
    sine_ref,
    magnitude_ref,
    squares_ref,
    low_ref,
    *rest,
):
    pieces, (grad_ref, total_ref, upper_all, heads_grad, key_grad, value_grad, sems) = rest[:-7], rest[-7:]
    rows_all, width = query_ref.shape[1:]
    share = rows_all // groups

    @pl.when(pl.program_id(0) == 0)
    def _():
        copies = []
        for place, piece in enumerate(pieces):
            at = pl.multiple_of(order_ref[place] * share, share)
            copies.append(
                pltpu.make_async_copy(piece, upper_all.at[pl.ds(at, share), :], sems.at[place])
            )
            copies[-1].start()
        for copy in copies:
            copy.wait()

    step = min(512, rows_all)
    for start in range(0, rows_all, step):
        at = slice(start, start + step)
        heads_grad[at, :] = dot(upper_all[at, :], low_ref[0], NT).astype(LOW)
    norm = [jnp.sqrt(squares_ref[m]) for m in range(3)]
    scale = [magnitude_ref[m : m + 1] / norm[m] for m in range(3)]
    heads = range(0, width, HEAD_DIM)
    totals = [jnp.zeros((1, width), F32) for _ in range(3)]
    filled = set()

    def back(values, rows):
        return values * cos_ref[rows, :] - pltpu.roll(values, HEAD_DIM // 2, 1) * sine_ref[rows, :]

    def add(ref, unit, values):
        for start in range(0, values.shape[0], ATTEND_BLOCK):
            at = unit.key_at + start
            rows = slice(at, at + ATTEND_BLOCK)
            name = (id(ref), at, unit.lanes.start)
            if name in filled:
                ref[rows, unit.lanes] += values[start : start + ATTEND_BLOCK]
            else:
                filled.add(name)
                ref[rows, unit.lanes] = values[start : start + ATTEND_BLOCK]

    def spread(per_head):
        return jnp.concatenate(per_head, axis=1)

    query_totals = [jnp.zeros((1, HEAD_DIM), F32) for _ in heads]
    for some in units_of(rows_all, width, 2):
        scores = [
            dot(query_ref[0, u.rows, u.lanes], key_ref[0, u.keys, u.lanes], NT) for u in some
        ]
        grad_weights = [
            dot(heads_grad[u.rows, u.lanes], value_ref[0, u.keys, u.lanes], NT) for u in some
        ]
        probs = [
            masked_probs(s, first_ref[u.rows, :], u.row_at, u.key_at)
            for u, s in zip(some, scores)
        ]
        grad_scores = [
            (p * (g - jnp.sum(p * g, axis=1, keepdims=True))).astype(LOW)
            for p, g in zip(probs, grad_weights)
        ]
        for u, p, g in zip(some, probs, grad_scores):
            add(value_grad, u, dot(p.astype(LOW), heads_grad[u.rows, u.lanes], TN))
            add(key_grad, u, dot(g, query_ref[0, u.rows, u.lanes], TN))
        for u, g in zip(some, grad_scores):
            grad = back(dot(g, key_ref[0, u.keys, u.lanes]) * HEAD_DIM ** (-0.5), u.rows)
            head = u.lanes.start // HEAD_DIM
            post = back(query_ref[0, u.rows, u.lanes].astype(F32), u.rows)
            query_totals[head] = query_totals[head] + jnp.sum(grad * post, axis=0, keepdims=True)
            put_rows(grad_ref, (0,), u.row_at, u.lanes, grad * scale[0][:, u.lanes], order_ref, groups)
    totals[0] = spread(query_totals)
    for row_at in range(0, rows_all, ATTEND_BLOCK):
        rows = slice(row_at, row_at + ATTEND_BLOCK)
        for head in heads:
            lanes = slice(head, head + HEAD_DIM)
            grad = back(key_grad[rows, lanes] * HEAD_DIM ** (-0.5), rows)
            post = back(key_ref[0, rows, lanes].astype(F32), rows)
            part = jnp.sum(grad * post, axis=0, keepdims=True)
            query_totals[head // HEAD_DIM] = part if row_at == 0 else query_totals[head // HEAD_DIM] + part
            put_rows(grad_ref, (1,), row_at, lanes, grad * scale[1][:, lanes], order_ref, groups)
        grad = value_grad[rows, :]
        totals[2] = totals[2] + jnp.sum(grad * value_ref[0, rows, :].astype(F32), axis=0, keepdims=True)
        put_rows(grad_ref, (2,), row_at, slice(0, width), grad * scale[2], order_ref, groups)
    totals[1] = spread(query_totals)
    for m in range(3):
        total_ref[m] = totals[m] / scale[m]


def attend_back(order, groups, post, first, cos_table, sine_table, magnitude, squares, low, pieces):
    rows, width = post.shape[1:]
    depth = low.shape[2]
    wide = 2 * HEAD_DIM
    member = lambda m: pl.BlockSpec((1, rows, wide), lambda h, o: (m, 0, h))
    table = pl.BlockSpec((rows, HEAD_DIM), lambda h, o: (0, 0))
    column = pl.BlockSpec((3, 1, wide), lambda h, o: (0, 0, h))
    return call(
        "attend_back",
        functools.partial(attend_back_kernel, groups),
        (post, post, post, first, cos_table, sine_table, magnitude, squares, low, *pieces),
        (width // wide,),
        [
            member(0),
            member(1),
            member(2),
            pl.BlockSpec((rows, 1), lambda h, o: (0, 0)),
            table,
            table,
            pl.BlockSpec((3, wide), lambda h, o: (0, h)),
            column,
            pl.BlockSpec((1, wide, depth), lambda h, o: (0, h, 0)),
            *[pl.BlockSpec(memory_space=pl.ANY) for _ in pieces],
        ],
        [pl.BlockSpec((3, rows, wide), lambda h, o: (0, 0, h)), column],
        [shape((3, rows, width), LOW), shape((3, 1, width), F32)],
        scratch=[
            pltpu.VMEM((rows, depth), LOW),
            pltpu.VMEM((rows, wide), LOW),
            pltpu.VMEM((rows, wide), F32),
            pltpu.VMEM((rows, wide), F32),
            pltpu.SemaphoreType.DMA((len(pieces),)),
        ],
        prefetch=(order,),
        flops=10 * rows * rows * width + 2 * rows * width * depth,
        mib=48,
    )


def product_kernel(dims, n_totals, *refs):
    value_ref, weight_ref = refs[:2]
    groups = value_ref.shape[1]
    if n_totals == 0:
        left_ref, *refs = refs[2:]
    else:
        right_ref, squares_ref, magnitude_ref = refs[2:5]
        totals, refs = refs[5 : 5 + n_totals], refs[5 + n_totals :]
    outs, extra_ref, rows_all = refs[:groups], refs[groups], refs[groups + 1]
    members, _, share, inner = value_ref.shape
    count = groups * share

    @pl.when(pl.program_id(0) == 0)
    def _():
        if n_totals > 0:
            total = sum_refs(totals)
        for m in range(members):
            rows_all[m, :count, :] = value_ref[m].reshape(count, inner)
            if n_totals == 0:
                rows_all[m, count:, :] = left_ref[m].astype(LOW)
            else:
                weight = norm_weight(total[m], squares_ref[m], magnitude_ref[m : m + 1])
                rows_all[m, count:, :] = (right_ref[m] * weight).astype(LOW)

    result = None
    for m in range(members):
        part = dot(rows_all[m], weight_ref[m], dims)
        extra_ref[m] = part[count:]
        result = part[:count] if result is None else result + part[:count]
    for place, ref in enumerate(outs):
        ref[...] = result[place * share : (place + 1) * share].astype(LOW)


def product(name, values, weights, dims, left=None, correction=None):
    members, groups, share, inner = values.shape
    width = weights.shape[2] if dims is NN else weights.shape[1]
    wide = tile_of(width, 512)
    if dims is NN:
        weight_spec = pl.BlockSpec((members, inner, wide), lambda n: (0, 0, n))
    else:
        weight_spec = pl.BlockSpec((members, wide, inner), lambda n: (0, n, 0))
    if correction is None:
        extra, n_totals, rank = (left,), 0, left.shape[1]
    else:
        right, squares, magnitude, totals = correction
        extra, n_totals, rank = (right, squares, magnitude, *totals), len(totals), right.shape[1]
    fixed = lambda v: pl.BlockSpec(v.shape, lambda n: (0,) * v.ndim)
    out = pl.BlockSpec((share, wide), lambda n: (0, n))
    results = call(
        name,
        functools.partial(product_kernel, dims, n_totals),
        (values, weights, *extra),
        (width // wide,),
        [fixed(values), weight_spec] + [fixed(v) for v in extra],
        [out] * groups + [pl.BlockSpec((members, rank, wide), lambda n: (0, 0, n))],
        [shape((share, width), LOW)] * groups + [shape((members, rank, width), F32)],
        scratch=[pltpu.VMEM((members, groups * share + rank, inner), LOW)],
        flops=2 * members * groups * share * inner * width,
    )
    return results[:groups], results[groups]


def shrink_kernel(chips, order_ref, *refs):
    values, (weight_ref, left_ref, cot_ref), outs = refs[:chips], refs[chips : chips + 3], refs[chips + 3 :]
    total_ref, across_ref, rows_all = outs[-3:]
    both, inner = values[0].shape
    share, depth = both // CORES, left_ref.shape[2]
    count = chips * both

    @pl.when(pl.program_id(0) == 0)
    def _():
        for step, ref in enumerate(values):
            rows_all[step * both : (step + 1) * both, :] = ref[...]
        if inner > depth:
            rows_all[count:, depth:] = jnp.zeros((rows_all.shape[0] - count, inner - depth), LOW)
        rows_all[count:, :depth] = left_ref[0].astype(LOW)

    result = dot(rows_all[...], weight_ref[0])
    across_ref[0] = result[count:]
    total = jnp.zeros((1, weight_ref.shape[2]), F32)
    for place in range(chips * CORES):
        pre = result[place * share : (place + 1) * share]
        outs[place][...] = pre.astype(LOW)
        at = pl.multiple_of(order_ref[place] * share, share)
        cot = cot_ref[pl.ds(at, share), :].astype(F32)
        total = total + jnp.sum(pre * cot, axis=0, keepdims=True)
    total_ref[...] = total


def shrink_product(order, values, weights, left, cotangent):
    chips = len(values)
    share, inner = values[0].shape[0] // CORES, values[0].shape[1]
    width, rank = weights.shape[2], left.shape[1]
    rows = chips * CORES * share
    wide = tile_of(width, 512)
    fixed = lambda v: pl.BlockSpec(v.shape, lambda n, o: (0,) * v.ndim)
    results = call(
        "shrink_product",
        functools.partial(shrink_kernel, chips),
        (*values, weights, left, cotangent),
        (width // wide,),
        [fixed(v) for v in values]
        + [
            pl.BlockSpec((1, inner, wide), lambda n, o: (0, 0, n)),
            fixed(left),
            pl.BlockSpec((rows, wide), lambda n, o: (0, n)),
        ],
        [pl.BlockSpec((share, wide), lambda n, o: (0, n))] * (chips * CORES)
        + [
            pl.BlockSpec((1, wide), lambda n, o: (0, n)),
            pl.BlockSpec((1, rank, wide), lambda n, o: (0, 0, n)),
        ],
        [shape((share, width), LOW)] * (chips * CORES)
        + [shape((1, width), F32), shape((1, rank, width), F32)],
        scratch=[pltpu.VMEM((rows + rank, inner), LOW)],
        prefetch=(order,),
        flops=2 * rows * inner * width,
    )
    return results[: chips * CORES], results[-2], results[-1]


def row_call(name, kernel, order, given, whole, out_kinds, sums, prepare):
    share = min(v.shape[0] for v, _ in given)
    width = given[0][0].shape[1]
    halves = 2
    half = share // halves
    count = len(given)

    def run(order_ref, *refs):
        sources, rest = refs[:count], refs[count : -count - 1]
        held, sems = refs[-count - 1 : -1], refs[-1]

        def copies(part):
            for i, ((_, cut), source, target) in enumerate(zip(given, sources, held)):
                at = part * half
                if cut:
                    at = pl.multiple_of(order_ref[1] * share + at, half)
                yield pltpu.make_async_copy(
                    source.at[pl.ds(at, half), :],
                    target.at[pl.ds(part * half, half), :],
                    sems.at[part, i],
                )

        for part in range(halves):

            @pl.when(pl.program_id(0) == part)
            def _(part=part):
                if part == 0:
                    for each in range(halves):
                        for copy in copies(each):
                            copy.start()
                for copy in copies(part):
                    copy.wait()

        outs = rest[len(whole) : len(whole) + len(out_kinds)]
        totals, sums_held = rest[len(whole) + len(out_kinds) :][:sums], rest[len(rest) - sums :]
        tile = 32
        lines = prepare(*[ref[...] for ref in rest[: len(whole)]])
        for ref in sums_held:
            ref[...] = jnp.zeros_like(ref)

        def some(i, carry):
            inside = pl.ds(pl.multiple_of(i * tile, tile), tile)
            at = pl.ds(pl.multiple_of(pl.program_id(0) * half + i * tile, tile), tile)
            values = kernel([ref[at, :].astype(F32) for ref in held], *lines)
            for ref, value in zip(outs, values):
                ref[inside, :] = value.astype(ref.dtype)
            for ref, value in zip(sums_held, values[len(outs) :]):
                ref[...] += jnp.sum(value.reshape(tile // 8, 8, width), axis=0)
            return carry

        lax.fori_loop(0, half // tile, some, 0, unroll=2)
        for ref, held_ref in zip(totals, sums_held):
            add_column(ref, held_ref[...])

    line = pl.BlockSpec((1, width), lambda i, o: (0, 0))
    return call(
        name,
        run,
        (*[v for v, _ in given], *whole),
        (halves,),
        [pl.BlockSpec(memory_space=pl.ANY) for _ in given] + [line for _ in whole],
        [pl.BlockSpec((half, width), lambda i, o: (i, 0)) for _ in out_kinds]
        + [line for _ in range(sums)],
        [shape((share, width), kind) for kind in out_kinds]
        + [shape((1, width), F32) for _ in range(sums)],
        scratch=[pltpu.VMEM((8, width), F32) for _ in range(sums)]
        + [pltpu.VMEM((share, width), v.dtype) for v, _ in given]
        + [pltpu.SemaphoreType.DMA((halves, count))],
        prefetch=(order,),
        flops=20 * share * width,
    )


def sum_of(values):
    total = values[0]
    for value in values[1:]:
        total = total + value
    return total


def add_column(ref, values):
    part = jnp.sum(values, axis=0, keepdims=True)

    @pl.when(pl.program_id(0) == 0)
    def _():
        ref[...] = part

    @pl.when(pl.program_id(0) > 0)
    def _():
        ref[...] += part


def scale_first(squares, magnitude, *rest):
    norm = jnp.sqrt(squares)
    return (magnitude / norm, norm / magnitude, *rest)


def hidden_kernel(given, scale, inverse, gain):
    hidden = given[0] + sum_of(given[1:]) * scale
    return hidden, hidden * rms_rows(hidden) * gain


def mixed_kernel(given, scale, inverse):
    return (given[0] + sum_of(given[1:]) * scale,)


def norm_back(grad_normed, values, gain):
    factor = rms_rows(values)
    scaled = grad_normed * gain
    inner = jnp.mean(scaled * values, axis=1, keepdims=True)
    back = factor * scaled - values * (factor * factor * factor * inner)
    return back, grad_normed * values * factor


def hidden_back_kernel(given, scale, inverse, gain):
    cot, token, hidden = given[:3]
    back, gain_terms = norm_back(sum_of(given[3:]), hidden, gain)
    grad = cot + back
    return grad, grad * scale, grad * ((hidden - token) * inverse), gain_terms


def token_back_kernel(given, gain):
    back, gain_terms = norm_back(sum_of(given[2:]), given[0], gain)
    return given[1] + back, gain_terms


def shrink_back_kernel(order_ref, cot_ref, low_ref, squares_ref, magnitude_ref, product_ref, grad_ref):
    scale = magnitude_ref[0] / jnp.sqrt(squares_ref[0])
    grad = (cot_ref[...].astype(F32) * scale).astype(LOW)
    grad_ref[0] = grad
    product_ref[0] = dot(grad, low_ref[0], NT)


def shrink_back(order, cotangent, low, squares, magnitude, groups):
    rows, width = cotangent.shape
    share, inner = rows // groups, low.shape[1]
    line = pl.BlockSpec((1, 1, width), lambda j, o: (0, 0, 0))
    return call(
        "shrink_back",
        shrink_back_kernel,
        (cotangent, low, squares, magnitude),
        (groups,),
        [
            pl.BlockSpec((share, width), lambda j, o: (o[j], 0)),
            pl.BlockSpec((1, inner, width), lambda j, o: (0, 0, 0)),
            line,
            line,
        ],
        [
            pl.BlockSpec((1, share, inner), lambda j, o: (j, 0, 0)),
            pl.BlockSpec((1, share, width), lambda j, o: (j, 0, 0)),
        ],
        [shape((groups, share, inner), F32), shape((groups, share, width), LOW)],
        prefetch=(order,),
        flops=2 * rows * width * inner,
    )


def expand_kernel(step, first, last, n_totals, *refs):
    other_ref, mine_ref, low_ref, grad_ref, squares_ref, magnitude_ref = refs[:6]
    refs = list(refs[6:])
    left_ref = refs.pop(0) if first else None
    right_ref = refs.pop(0) if last else None
    before = [refs.pop(0) for _ in range(n_totals)]
    product_ref, back_ref, rows_ref, total_ref, send_ref, keep_ref = refs[:6]
    refs = refs[6:]
    across_ref = refs.pop(0) if first else None
    extra_ref = refs.pop(0) if last else None
    rows_all, low_all, grad_all, product_all, back_all, in_sems, out_sems = refs
    share, depth = other_ref.shape
    both = CORES * share
    width, ff = low_ref.shape[2], magnitude_ref.shape[1]
    tile = 256
    cuts = [slice(at, at + tile) for at in range(0, width, tile)]

    row_copies = [
        pltpu.make_async_copy(ref, rows_all.at[pl.ds(at, share), :], in_sems.at[i])
        for i, (at, ref) in enumerate(((0, other_ref), (share, mine_ref)))
    ]
    tile_copies = []
    for n, cut in enumerate(cuts):
        lanes = pl.ds(cut.start, tile)
        tile_copies.append(
            [
                pltpu.make_async_copy(
                    low_ref.at[:, :, lanes], low_all.at[:, :, lanes], in_sems.at[2 + 2 * n]
                ),
                pltpu.make_async_copy(
                    grad_ref.at[pl.ds(CORES * step, CORES), :, lanes],
                    grad_all.at[:, :, lanes],
                    in_sems.at[3 + 2 * n],
                ),
            ]
        )
    for copy in row_copies:
        copy.start()
    for copies in tile_copies:
        for copy in copies:
            copy.start()
    if first:
        rank = across_ref.shape[1]
        for m in range(2):
            rows_all[both + m * rank : both + (m + 1) * rank, :] = left_ref[m].astype(LOW)
    for copy in row_copies:
        copy.wait()
    out_copies = [
        pltpu.make_async_copy(rows_all.at[pl.ds(0, both), :], rows_ref, out_sems.at[2 * len(cuts)])
    ]
    out_copies[0].start()
    lane = lax.broadcasted_iota(jnp.int32, (1, tile), 1)
    for n, cut in enumerate(cuts):
        for copy in tile_copies[n]:
            copy.wait()
        size = min(tile, ff - cut.start)
        pre = [dot(rows_all[...], low_all[m, :, cut]) for m in range(2)]
        if first:
            for m in range(2):
                rows = slice(both + m * rank, both + (m + 1) * rank)
                across_ref[m, :, cut.start : cut.start + size] = pre[m][rows, :size]
        magnitude, squares, scale = [], [], []
        for m in range(2):
            given = magnitude_ref[m : m + 1, cut.start : cut.start + size]
            if size < tile:
                given = jnp.concatenate([given, jnp.zeros((1, tile - size), F32)], axis=1)
            magnitude.append(given)
            squares.append(squares_ref[m, :, cut])
            scale.append(given / jnp.sqrt(squares[m]))
        sums = [jnp.zeros((1, tile), F32) for _ in range(2)]
        at = [slice(m * width + cut.start, m * width + cut.stop) for m in range(2)]
        for place in range(CORES):
            rows = slice(place * share, (place + 1) * share)
            gate_pre, up_pre = pre[0][rows], pre[1][rows]
            gate, up = gate_pre * scale[0], up_pre * scale[1]
            sigmoid = 0.5 + 0.5 * jnp.tanh(0.5 * gate)
            active = gate * sigmoid
            product_all[rows, cut] = (active * up).astype(LOW)
            upper = grad_all[place, :, cut]
            grad_up = upper * active
            grad_gate = upper * up * sigmoid * (1.0 + gate * (1.0 - sigmoid))
            sums[0] += jnp.sum(grad_gate * gate_pre, axis=0, keepdims=True)
            sums[1] += jnp.sum(grad_up * up_pre, axis=0, keepdims=True)
            back_all[rows, at[0]] = (grad_gate * scale[0]).astype(LOW)
            back_all[rows, at[1]] = (grad_up * scale[1]).astype(LOW)
        for m in range(2):
            total_ref[m, :, cut] = sums[m]
        if last:
            rank = extra_ref.shape[1]
            for m in range(2):
                total = sums[m]
                for ref in before:
                    total = total + ref[m, :, cut]
                right = right_ref[m, :, cut.start : cut.start + size]
                if size < tile:
                    spare = jnp.zeros((rank, tile - size), F32)
                    right = jnp.concatenate([right, spare], axis=1)
                weighted = right * norm_weight(total, squares[m], magnitude[m])
                rows = slice(both + m * rank, both + (m + 1) * rank)
                back_all[rows, at[m]] = weighted.astype(LOW)
                back_all[rows, at[1 - m]] = jnp.zeros((rank, tile), LOW)
    for m in range(2):
        lanes = pl.ds(m * width, width)
        copy = pltpu.make_async_copy(
            back_all.at[pl.ds(0, both), lanes], back_ref.at[m], out_sems.at[m]
        )
        copy.start()
        out_copies.append(copy)
    copy = pltpu.make_async_copy(product_all, product_ref, out_sems.at[2])
    copy.start()
    out_copies.append(copy)
    chunk = tile_of(depth, 512)
    for start in range(0, depth, chunk):
        columns = slice(start, start + chunk)
        result = dot(back_all[:, :width], low_all[0, columns, :], NT)
        result = result + dot(back_all[:, width:], low_all[1, columns, :], NT)
        send_ref[:, columns] = result[:share].astype(LOW)
        keep_ref[:, columns] = result[share:both].astype(LOW)
        if last:
            for m in range(2):
                extra_ref[m, :, columns] = result[both + m * rank : both + (m + 1) * rank]
    for copy in out_copies:
        copy.wait()


def expand(pieces, low, squares, magnitude, grad_product, step, left=None, right=None, before=()):
    share, depth = pieces[0].shape
    width = low.shape[2]
    first, last = left is not None, right is not None
    rows = CORES * share
    hbm = pl.BlockSpec(memory_space=pl.ANY)
    fixed = lambda dims: pl.BlockSpec(tuple(dims), lambda i: (0,) * len(dims))
    operands = [*pieces, low, grad_product, squares, magnitude]
    in_specs = [hbm, hbm, hbm, hbm, fixed(squares.shape), fixed(magnitude.shape)]
    out_shape = [
        shape((rows, width), LOW),
        shape((2, rows, width), LOW),
        shape((rows, depth), LOW),
        shape((2, 1, width), F32),
        shape((share, depth), LOW),
        shape((share, depth), LOW),
    ]
    out_specs = [hbm, hbm, hbm] + [fixed(v.shape) for v in out_shape[3:]]
    extra_in = extra_out = 0
    if first:
        rank = left.shape[1]
        extra_in = 2 * rank
        operands.append(left)
        in_specs.append(fixed(left.shape))
        out_shape.append(shape((2, rank, magnitude.shape[1]), F32))
        out_specs.append(fixed(out_shape[-1].shape))
    if last:
        rank = right.shape[1]
        extra_out = 2 * rank
        operands += [right, *before]
        in_specs += [fixed(v.shape) for v in (right, *before)]
        out_shape.append(shape((2, rank, depth), F32))
        out_specs.append(fixed(out_shape[-1].shape))
    tiles = width // 256
    return call(
        "expand",
        functools.partial(expand_kernel, step, first, last, len(before)),
        tuple(operands),
        (1,),
        in_specs,
        out_specs,
        out_shape,
        scratch=[
            pltpu.VMEM((rows + extra_in, depth), LOW),
            pltpu.VMEM(low.shape, LOW),
            pltpu.VMEM((CORES, share, width), F32),
            pltpu.VMEM((rows, width), LOW),
            pltpu.VMEM((rows + extra_out, 2 * width), LOW),
            pltpu.SemaphoreType.DMA((2 + 2 * tiles,)),
            pltpu.SemaphoreType.DMA((2 * tiles + 1,)),
        ],
        flops=8 * rows * depth * width,
    )


def adapter_kernel(plan, n_inputs, n_grads, corrections, n_before, order_ref, *refs):
    count = n_inputs + n_grads
    sources, held, sems = refs[:count], refs[-count - 1 : -1], refs[-1]
    left_ref, right_ref = refs[count : count + 2]
    *corrected, left_out, right_out = refs[count + 2 : -count - 1]
    members, rank, width = right_ref.shape
    chunks = list(plan(order_ref, held[:n_inputs], held[n_inputs:]))
    copies = []
    for parts, _, _ in chunks:
        copies.append([])
        for which, index in parts:
            copy = pltpu.make_async_copy(
                sources[which].at[index],
                held[which].at[index],
                sems.at[sum(len(c) for c in copies)],
            )
            copy.start()
            copies[-1].append(copy)
    left_rows = jnp.concatenate([split_rows(left_ref[m]) for m in range(members)], axis=0)
    right_rows = [split_rows(right_ref[m]) for m in range(members)]
    before, corrected = corrected[:n_before], corrected[n_before:]
    for out, ref in zip((left_out, right_out), before or (None, None)):
        out[...] = jnp.zeros_like(out) if ref is None else ref[...]
    for waits, (_, taken_of, grads_of) in zip(copies, chunks):
        for copy in waits:
            copy.wait()
        taken = taken_of()
        across = dot(left_rows, taken, NT)
        downs = []
        for m in range(members):
            grad = grads_of(m)
            mine = split_rows(fold(across[2 * rank * m : 2 * rank * (m + 1)]))
            right_out[m] += fold(dot(mine, grad))
            downs.append(split_rows(fold(dot(right_rows[m], grad, NT))))
        left = dot(jnp.concatenate(downs, axis=0), taken)
        for m in range(members):
            left_out[m] += fold(left[2 * rank * m : 2 * rank * (m + 1)])
    if corrections:
        correct(corrections, right_ref, left_out, right_out, left_out, right_out, *corrected)


def correct(n_totals, right_ref, left_in, right_in, left_out, right_out, *refs):
    back_ref, across_ref, squares_ref, magnitude_ref = refs[:4]
    totals, magnitude_out = refs[4 : 4 + n_totals], refs[4 + n_totals]
    members, rank, width = right_ref.shape
    total = sum_refs(totals)[:, :, :width]
    squares = squares_ref[:, :, :width]
    magnitude_out[...] = total / jnp.sqrt(squares)
    for m in range(members):
        weight = norm_weight(total[m], squares[m], magnitude_ref[m : m + 1])
        if back_ref.dtype == LOW:
            low = back_ref[m, : left_in.shape[2], :]
            back = fold(dot(split_rows(right_ref[m] * weight), low, NT))
        else:
            back = back_ref[m]
        left_out[m] = ADAPT_SCALE * (left_in[m] - back)
        right_out[m] = ADAPT_SCALE * (right_in[m] - across_ref[m][:, :width] * weight)


def correct_kernel(n_totals, order_ref, right_ref, left_in, right_in, *refs):
    *rest, left_out, right_out = refs
    correct(n_totals, right_ref, left_in, right_in, left_out, right_out, *rest)


def correct_kernel(n_totals, right_ref, left_in, right_in, *refs):
    *rest, left_out, right_out = refs
    correct(n_totals, right_ref, left_in, right_in, left_out, right_out, *rest)


def corrected(name, sums, right, correction):
    members, rank, width = right.shape
    *given, totals = correction
    operands = (right, *sums, *given, *totals)
    outs = [(members, 1, width), sums[0].shape, sums[1].shape]
    full = lambda dims: pl.BlockSpec(tuple(dims), lambda i: (0,) * len(dims))
    return call(
        name,
        functools.partial(correct_kernel, len(totals)),
        operands,
        (1,),
        [full(v.shape) for v in operands],
        [full(dims) for dims in outs],
        [shape(dims, F32) for dims in outs],
        flops=sum(v.size for v in operands) * 64,
    )


def adapter(name, order, plan, inputs, grads, left, right, correction=None, before=()):
    members, rank, width = right.shape
    moved, fixed, n_totals = [*inputs, *grads], [left, right, *before], 0
    outs = [(members, rank, left.shape[2]), (members, rank, width)]
    if correction is not None:
        *given, totals = correction
        n_totals = len(totals)
        fixed += [*given, *totals]
        outs = [(members, 1, width)] + outs
    full = lambda dims: pl.BlockSpec(tuple(dims), lambda i, o: (0,) * len(dims))
    kernel = functools.partial(
        adapter_kernel, plan, len(inputs), len(grads), n_totals, len(before)
    )
    return call(
        name,
        kernel,
        (*moved, *fixed),
        (1,),
        [pl.BlockSpec(memory_space=pl.ANY) for _ in moved] + [full(v.shape) for v in fixed],
        [full(dims) for dims in outs],
        [shape(dims, F32) for dims in outs],
        scratch=[pltpu.VMEM(v.shape, v.dtype) for v in moved] + [pltpu.SemaphoreType.DMA((32,))],
        prefetch=(order,),
        flops=sum(v.size for v in moved) * 64,
    )


MESH_IDS = pl.DeviceIdType.MESH


def copy_kernel(count, *refs):
    for source, target in zip(refs[:count], refs[count:]):
        target[...] = source[...]


def copy_out(arrays):
    vmem = pl.BlockSpec(memory_space=pltpu.VMEM)
    full = lambda v: pl.BlockSpec(v.shape, lambda i: (0,) * v.ndim)
    return call(
        "copy_out",
        functools.partial(copy_kernel, len(arrays)),
        tuple(arrays),
        (1,),
        [vmem for _ in arrays],
        [full(v) for v in arrays],
        [shape(v.shape, F32) for v in arrays],
        mib=16,
    )


GRAIN = 16


def pieces_of(width):
    return [(at, min(128, width - at)) for at in range(0, width, 128)]


def cells_of(blocks, lines, parts):
    cells, rows = [], []
    for n, block in enumerate(blocks):
        for m in range(block.shape[0]):
            for at, size in pieces_of(block.shape[2] // parts):
                cells.append((n, m, at, size))
    for n, line in enumerate(lines):
        for m in range(line.shape[0]):
            for at, size in pieces_of(line.shape[2] // parts):
                rows.append((n, m, at, size))
    return cells, rows


def pack(blocks, lines, wide_ref, part, parts, cells, rows):
    for i, (n, m, at, size) in enumerate(cells):
        start = part * (blocks[n].shape[2] // parts) + at
        wide_ref[part, i, :, :size] = blocks[n][m, :, start : start + size]
    for i, (n, m, at, size) in enumerate(rows):
        start = part * (lines[n].shape[2] // parts) + at
        cell, row = len(cells) + i // GRAIN, i % GRAIN
        wide_ref[part, cell, row : row + 1, :size] = lines[n][m, :, start : start + size]


def unpack(full_ref, blocks, lines, part, parts, cells, rows):
    for i, (n, m, at, size) in enumerate(cells):
        start = part * (blocks[n].shape[2] // parts) + at
        blocks[n][m, :, start : start + size] = full_ref[part, i].astype(F32)[:, :size]
    for i, (n, m, at, size) in enumerate(rows):
        start = part * (lines[n].shape[2] // parts) + at
        cell, row = len(cells) + i // GRAIN, i % GRAIN
        values = full_ref[part, cell].astype(F32)
        lines[n][m, :, start : start + size] = values[row : row + 1, :size]


def reduce_kernel(groups, lines, counts, *refs):
    n_all, n_all_lines, n_dp, n_dp_lines = counts
    count = sum(counts)
    taken, given, scratch = refs[:count], refs[count : 2 * count], refs[2 * count :]
    ends = [n_all, n_all + n_all_lines, n_all + n_all_lines + n_dp]
    parted = lambda v: (v[: ends[0]], v[ends[0] : ends[1]], v[ends[1] : ends[2]], v[ends[2] :])
    all_in, all_lines_in, dp_in, dp_lines_in = parted(taken)
    all_out, all_lines_out, dp_out, dp_lines_out = parted(given)
    (
        all_ref,
        line_ref,
        all_low,
        line_low,
        all_got,
        part,
        part_low,
        part_got,
        line_got,
        all_full,
        line_full,
        *sems,
    ) = scratch
    me, row = lax.axis_index("mp"), lax.axis_index("dp")
    piece, line_piece = part.shape[0] // lines, line_ref.shape[1] // lines
    mp_peer = [lax.rem(me + k, groups) for k in range(groups)]
    dp_peer = [lax.rem(row + k, lines) for k in range(lines)]
    barrier = pltpu.get_barrier_semaphore()
    for k in range(1, groups):
        pl.semaphore_signal(barrier, 1, device_id={"mp": mp_peer[k]}, device_id_type=MESH_IDS)
    for k in range(1, lines):
        pl.semaphore_signal(barrier, 1, device_id={"dp": dp_peer[k]}, device_id_type=MESH_IDS)
    all_cells = cells_of(all_in, all_lines_in, groups)
    dp_cells = cells_of(dp_in, dp_lines_in, 1)
    all_ref[...] = jnp.zeros_like(all_ref)
    line_ref[...] = jnp.zeros_like(line_ref)
    for q in range(groups):
        pack(all_in, all_lines_in, all_ref, q, groups, *all_cells)
    pack(dp_in, dp_lines_in, line_ref, 0, 1, *dp_cells)
    all_low[...] = all_ref[...].astype(LOW)
    line_low[...] = line_ref[...].astype(LOW)
    pl.semaphore_wait(barrier, groups + lines - 2)

    def send(source, target, stage, k, axis, peer):
        copy = pltpu.make_async_remote_copy(
            src_ref=source,
            dst_ref=target,
            send_sem=sems[2 * stage].at[k],
            recv_sem=sems[2 * stage + 1].at[k],
            device_id={axis: peer},
            device_id_type=MESH_IDS,
        )
        copy.start()
        return copy

    over_mp = [
        send(all_low.at[mp_peer[k]], all_got.at[k], 0, k, "mp", mp_peer[k])
        for k in range(1, groups)
    ]
    over_dp = [
        send(
            line_low.at[0, pl.ds(dp_peer[k] * line_piece, line_piece)],
            line_got.at[k],
            1,
            k,
            "dp",
            dp_peer[k],
        )
        for k in range(1, lines)
    ]
    total = all_ref[me]
    for k, copy in enumerate(over_mp, 1):
        copy.wait_recv()
        total = total + all_got[k].astype(F32)
    part[...] = total
    part_low[...] = total.astype(LOW)
    part_dp = [
        send(part_low.at[pl.ds(dp_peer[k] * piece, piece)], part_got.at[k], 2, k, "dp", dp_peer[k])
        for k in range(1, lines)
    ]
    held = pl.ds(row * piece, piece)
    total = part[held]
    for k, copy in enumerate(part_dp, 1):
        copy.wait_recv()
        total = total + part_got[k].astype(F32)
    all_full[me, held] = total.astype(LOW)
    part_back = [
        send(all_full.at[me, held], all_full.at[me, held], 4, k, "dp", dp_peer[k])
        for k in range(1, lines)
    ]
    mine = pl.ds(row * line_piece, line_piece)
    total = line_ref[0, mine]
    for k, copy in enumerate(over_dp, 1):
        copy.wait_recv()
        total = total + line_got[k].astype(F32)
    line_full[0, mine] = total.astype(LOW)
    line_back = [
        send(line_full.at[0, mine], line_full.at[0, mine], 3, k, "dp", dp_peer[k])
        for k in range(1, lines)
    ]
    for copy in part_back:
        copy.wait_recv()
    all_back = [
        send(all_full.at[me], all_full.at[me], 5, k, "mp", mp_peer[k]) for k in range(1, groups)
    ]
    for copy in line_back:
        copy.wait_recv()
    unpack(line_full, dp_out, dp_lines_out, 0, 1, *dp_cells)
    for copy in all_back:
        copy.wait_recv()
    for q in range(groups):
        unpack(all_full, all_out, all_lines_out, q, groups, *all_cells)
    for copy in over_mp + over_dp + part_dp + line_back + part_back + all_back:
        copy.wait_send()


def reduce_devices(name, identity, over_all, over_all_lines, over_dp, over_dp_lines):
    groups, lines = lax.axis_size("mp"), lax.axis_size("dp")

    def size_of(blocks, rows, parts):
        cells, lines_in = cells_of(blocks, rows, parts)
        size = len(cells) + -(-len(lines_in) // GRAIN)
        return -(-size // lines) * lines

    count, line_count = size_of(over_all, over_all_lines, groups), size_of(over_dp, over_dp_lines, 1)
    operands = (*over_all, *over_all_lines, *over_dp, *over_dp_lines)
    counts = (len(over_all), len(over_all_lines), len(over_dp), len(over_dp_lines))
    vmem = pl.BlockSpec(memory_space=pltpu.VMEM)
    tail = (GRAIN, 128)
    sizes = (groups, lines, lines, lines, lines, groups)
    every, line = (groups, count) + tail, (1, line_count) + tail
    results = pl.pallas_call(
        functools.partial(reduce_kernel, groups, lines, counts),
        name=name,
        out_shape=[shape(v.shape, F32) for v in operands],
        in_specs=[vmem for _ in operands],
        out_specs=[vmem for _ in operands],
        scratch_shapes=[
            pltpu.VMEM(every, F32),
            pltpu.VMEM(line, F32),
            pltpu.VMEM(every, LOW),
            pltpu.VMEM(line, LOW),
            pltpu.VMEM(every, LOW),
            pltpu.VMEM((count,) + tail, F32),
            pltpu.VMEM((count,) + tail, LOW),
            pltpu.VMEM((lines, count // lines) + tail, LOW),
            pltpu.VMEM((lines, line_count // lines) + tail, LOW),
            pltpu.VMEM(every, LOW),
            pltpu.VMEM(line, LOW),
        ]
        + [pltpu.SemaphoreType.DMA((n,)) for n in sizes for _ in range(2)],
        compiler_params=pltpu.CompilerParams(
            collective_id=identity, has_side_effects=True, vmem_limit_bytes=32 * 2**20
        ),
        cost_estimate=pl.CostEstimate(flops=1000, bytes_accessed=2**20, transcendentals=0),
    )(*operands)
    return copy_out(results)


def first_places(segment):
    length = segment.shape[0]
    places = lax.broadcasted_iota(jnp.int32, (length, length), 0)
    others = lax.broadcasted_iota(jnp.int32, (length, length), 1)
    visible = (segment[:, None] == segment[None, :]) & (others <= places)
    offset = jnp.sum(visible.astype(F32), axis=1) - 1.0
    return (jnp.arange(length, dtype=jnp.int32) - offset.astype(jnp.int32))[:, None]


def body(
    tokens,
    cotangent,
    segment_ids,
    attend_gain,
    expand_gain,
    heads_base,
    heads_left,
    heads_right,
    heads_magnitude,
    output_base,
    output_left,
    output_right,
    output_magnitude,
    expand_base,
    expand_left,
    expand_right,
    expand_magnitude,
    shrink_base,
    shrink_left,
    shrink_right,
    shrink_magnitude,
):
    groups = lax.axis_size("mp")
    chips = groups // CORES
    index = lax.axis_index("mp")
    chip, core = index // CORES, index % CORES
    rows, width = tokens.shape
    share = rows // groups
    local_heads, ff = heads_base.shape[2], expand_base.shape[2]
    ff_wide = padded(ff)
    device = jnp.arange(groups, dtype=jnp.int32)
    order = jnp.concatenate(
        [
            (chip + device // CORES) % chips * CORES + (core + 1 + device) % CORES,
            (device // CORES + chips - chip) % chips * CORES + (device + CORES - core + 1) % CORES,
        ]
    ).astype(jnp.int32)

    def tie(*values):
        return lax.optimization_barrier(values)

    def sibling(values):
        return lax.ppermute(
            values, "mp", [(i, i // CORES * CORES + (i + 1) % CORES) for i in range(groups)]
        )

    def to_chip(values, step):
        return lax.ppermute(
            values,
            "mp",
            [((i, ((i // CORES + step) % chips) * CORES + i % CORES)) for i in range(groups)],
        )

    def mp_sum(values):
        values = values + sibling(values)
        total = values
        for step in range(1, chips):
            total = total + to_chip(values, step)
        return total

    def join(pair):
        return (pair[1].astype(F32) + sibling(pair[0]).astype(F32)).astype(LOW)

    def chip_pairs(places):
        return [places[CORES * step : CORES * (step + 1)] for step in range(chips)]

    def arrive(own):
        return [to_chip(own, chips - step) for step in range(1, chips)]

    def pairs_of(own, near_sibling, arrived):
        return [(near_sibling, own)] + [(sibling(piece), piece) for piece in arrived]

    def in_pairs(order_ref, inputs, grads):
        for step, (taken, grad) in enumerate(zip(inputs, grads)):
            yield (
                [(step, ...), (chips + step, ...)],
                lambda taken=taken: taken[...],
                lambda m, grad=grad: grad[m, :, :ff],
            )

    def in_shrink(order_ref, inputs, grads):
        for step, taken in enumerate(inputs):
            at = slice(CORES * step, CORES * (step + 1))
            yield (
                [(step, ...), (chips, pl.ds(CORES * step, CORES))],
                lambda taken=taken: taken[:, :ff],
                lambda m, at=at: grads[0][at].reshape(-1, grads[0].shape[-1]),
            )

    def in_output(start):
        def plan(order_ref, inputs, grads):
            for n, grad in enumerate(grads):
                yield (
                    [(0, (0, start + n)), (1 + n, ...)],
                    lambda place=start + n: inputs[0][0, place],
                    lambda m, grad=grad: grad[...],
                )

        return plan

    def in_heads(order_ref, inputs, grads):
        for place in range(groups):
            at = pl.multiple_of(order_ref[place] * share, share)
            rows = pl.ds(place * share, share)
            yield (
                [(0, pl.ds(at, share)), (1, (slice(None), rows))],
                lambda at=at: inputs[0][pl.ds(at, share), :],
                lambda m, rows=rows: grads[0][m, rows, :],
            )

    heads_rows, output_rows = turned(heads_left), turned(output_left[None])
    expand_rows, shrink_rows = turned(expand_left), turned(shrink_left[None])
    heads_mag, output_mag = heads_magnitude, output_magnitude[None]
    expand_mag, shrink_mag = expand_magnitude, shrink_magnitude[None]
    attend_line, expand_line = attend_gain[None], expand_gain[None]

    output_low, shrink_low, squares_part = merge_pair(
        [(output_base, output_rows[0], output_right), (shrink_base, shrink_rows[0], shrink_right)]
    )
    output_low, shrink_low = output_low[None], shrink_low[None]
    tokens, squares_part = tie(tokens, squares_part)
    squares = mp_sum(squares_part)
    first = first_places(segment_ids.reshape(-1))
    normed, heads_low, post, heads_sq, heads_across, cos_table, sine_table = project_heads(
        tokens, attend_line, heads_base, heads_rows, heads_right, heads_mag, first
    )
    heads_out = attend(order, groups, post, first)
    heads_out, squares = tie(heads_out, squares)
    output_sq, shrink_sq = squares[None, :1], squares[None, 1:]
    heads_parts = heads_out.reshape(1, groups, share, local_heads)
    output_places, output_across = product(
        "output_product", heads_parts, output_low, NN, left=output_rows
    )
    output_pairs = chip_pairs(output_places)
    joined = [join(pair) for pair in output_pairs[1:]]
    joined, expand_right_tied = tie(joined, expand_right)
    output_arrived = [to_chip(values, step) for step, values in enumerate(joined, 1)]
    expand_low, expand_sq = merge(
        expand_base, expand_rows, expand_right_tied, 1024, expand_base.shape[2]
    )
    grad_product, shrink_grad = shrink_back(
        order, cotangent, shrink_low, shrink_sq, shrink_mag[None], groups
    )
    output_parts = [output_pairs[0][1], sibling(output_pairs[0][0]), *output_arrived]
    output_parts, expand_low, grad_product = tie(output_parts, expand_low, grad_product)
    hidden, normed_own = row_call(
        "hidden",
        hidden_kernel,
        order,
        [(tokens, True)] + [(part, False) for part in output_parts],
        (output_sq[0], output_mag, expand_line),
        (F32, LOW),
        0,
        scale_first,
    )

    def feed(pieces, step, **extra):
        return expand(pieces, expand_low, expand_sq, expand_mag, grad_product, step, **extra)

    arrived, near_sibling = arrive(normed_own), sibling(normed_own)
    fed = [feed((near_sibling, normed_own), 0, left=expand_rows)]
    arrived, fed = tie(arrived, fed)
    fed = list(fed)
    mid_sibling = sibling(fed[0][4])
    normed_mid = pairs_of(normed_own, near_sibling, arrived)
    for step in range(1, chips):
        extra = {}
        if step == chips - 1:
            extra = {"right": expand_right, "before": [f[3] for f in fed]}
        fed.append(feed(normed_mid[step], step, **extra))
    expand_totals = [f[3] for f in fed]
    joined = [join(f[4:6]) for f in fed[1:]]
    joined, shrink_rows_tied = tie(joined, shrink_rows)
    mid_arrived = [to_chip(values, step) for step, values in enumerate(joined, 1)]
    shrink_places, shrink_total, shrink_across = shrink_product(
        order, [f[0] for f in fed], shrink_low, shrink_rows_tied, cotangent
    )
    shrink_pairs = chip_pairs(shrink_places)
    expand_adapter = adapter(
        "expand_adapter",
        order,
        in_pairs,
        [f[2] for f in fed],
        [f[1] for f in fed],
        expand_rows,
        expand_right,
        (fed[-1][6], fed[0][6], expand_sq, expand_mag, expand_totals),
    )
    mid_parts = [fed[0][5], mid_sibling, *mid_arrived]
    mid_parts, shrink_pairs, expand_adapter = tie(mid_parts, shrink_pairs, expand_adapter)
    grad_hidden, output_grad_own, output_total, expand_gain_part = row_call(
        "hidden_back",
        hidden_back_kernel,
        order,
        [(cotangent, True), (tokens, True), (hidden, False)]
        + [(part, False) for part in mid_parts],
        (output_sq[0], output_mag, expand_line),
        (F32, LOW),
        2,
        scale_first,
    )
    arrived, near_sibling = arrive(output_grad_own), sibling(output_grad_own)
    both_totals = jnp.concatenate([output_total, shrink_total], axis=0)
    both_totals = both_totals + sibling(both_totals)
    shrink_joined = [join(pair) for pair in shrink_pairs[1:]]
    shrink_joined, both_totals, shrink_rows_tied = tie(shrink_joined, both_totals, shrink_rows)
    shrink_sums = adapter(
        "shrink_adapter",
        order,
        in_shrink,
        [f[0] for f in fed],
        [shrink_grad],
        shrink_rows_tied,
        shrink_right[None],
    )
    output_sums = adapter(
        "output_near_adapter",
        order,
        in_output(0),
        [heads_parts],
        [near_sibling, output_grad_own],
        output_rows,
        output_right[None],
    )
    arrived, near_sibling, both_totals, shrink_joined, shrink_sums, output_sums = tie(
        arrived, near_sibling, both_totals, shrink_joined, shrink_sums, output_sums
    )
    both_totals = functools.reduce(
        jnp.add, [both_totals] + [to_chip(both_totals, step) for step in range(1, chips)]
    )
    output_total, shrink_total = both_totals[:1], both_totals[1:]
    output_grad = [
        piece for pair in pairs_of(output_grad_own, near_sibling, arrived) for piece in pair
    ]
    shrink_parts = [shrink_pairs[0][1], sibling(shrink_pairs[0][0])] + [
        to_chip(values, step) for step, values in enumerate(shrink_joined, 1)
    ]
    heads_grads, heads_total = attend_back(
        order,
        groups,
        post,
        first,
        cos_table,
        sine_table,
        heads_mag,
        heads_sq,
        output_low,
        output_grad,
    )
    grad_parts = heads_grads.reshape(3, groups, share, local_heads)
    token_places, token_extra = product(
        "normed_product",
        grad_parts,
        heads_low,
        NT,
        correction=(heads_right, heads_sq, heads_mag, [heads_total]),
    )
    token_places, shrink_parts = tie(token_places, shrink_parts)
    token_pairs = chip_pairs(token_places)
    joined = [join(pair) for pair in token_pairs[1:]]
    joined, heads_rows_tied, output_rows_tied = tie(joined, heads_rows, output_rows)
    token_arrived = [to_chip(values, step) for step, values in enumerate(joined, 1)]
    output_adapter = adapter(
        "output_far_adapter",
        order,
        in_output(CORES),
        [heads_parts],
        output_grad[CORES:],
        output_rows_tied,
        output_right[None],
        (output_low, output_across, output_sq, output_mag, [output_total[None]]),
        output_sums,
    )
    shrink_adapter = corrected(
        "shrink_correct",
        shrink_sums,
        shrink_right[None],
        (shrink_low, shrink_across, shrink_sq, shrink_mag, [shrink_total[None]]),
    )
    heads_adapter = adapter(
        "heads_adapter",
        order,
        in_heads,
        [normed],
        [heads_grads],
        heads_rows_tied,
        heads_right,
        (token_extra, heads_across, heads_sq, heads_mag, [heads_total]),
    )
    (mixed,) = row_call(
        "mixed",
        mixed_kernel,
        order,
        [(hidden, False)] + [(part, False) for part in shrink_parts],
        (shrink_sq[0], shrink_mag),
        (LOW,),
        0,
        scale_first,
    )
    token_parts = [token_pairs[0][1], sibling(token_pairs[0][0]), *token_arrived]
    token_parts, output_adapter, shrink_adapter, heads_adapter, mixed = tie(
        token_parts, output_adapter, shrink_adapter, heads_adapter, mixed
    )
    grad_tokens, attend_gain_part = row_call(
        "token_back",
        token_back_kernel,
        order,
        [(tokens, True), (grad_hidden, False)] + [(part, False) for part in token_parts],
        (attend_line,),
        (F32,),
        1,
        lambda gain: (gain,),
    )
    (
        expand_left_grad,
        shrink_right_grad,
        heads_left_grad,
        output_right_grad,
        expand_gain_grad,
        attend_gain_grad,
        expand_right_grad,
        shrink_left_grad,
        heads_right_grad,
        output_left_grad,
        expand_mag_grad,
        shrink_mag_grad,
        heads_mag_grad,
        output_mag_grad,
    ) = reduce_devices(
        "reduce_gradients",
        1,
        [expand_adapter[1], shrink_adapter[2], heads_adapter[1], output_adapter[2]],
        [expand_gain_part[None], attend_gain_part[None]],
        [expand_adapter[2], shrink_adapter[1], heads_adapter[2], output_adapter[1]],
        [expand_adapter[0], shrink_adapter[0], heads_adapter[0], output_adapter[0]],
    )
    return (
        mixed,
        grad_tokens,
        attend_gain_grad[0, 0],
        expand_gain_grad[0, 0],
        jnp.swapaxes(heads_left_grad, 1, 2),
        heads_right_grad,
        heads_mag_grad[:, 0],
        output_left_grad[0].T,
        output_right_grad[0],
        output_mag_grad[0, 0],
        jnp.swapaxes(expand_left_grad, 1, 2),
        expand_right_grad,
        expand_mag_grad[:, 0],
        shrink_left_grad[0].T,
        shrink_right_grad[0],
        shrink_mag_grad[0, 0],
    )


def solution(mesh):
    placed = (
        P("dp", None),
        P("dp", None),
        P("dp", None),
        P(),
        P(),
        P(None, None, "mp"),
        P(),
        P(None, None, "mp"),
        P(None, "mp"),
        P("mp", None),
        P("mp", None),
        P(),
        P(),
        P(None, None, "mp"),
        P(),
        P(None, None, "mp"),
        P(None, "mp"),
        P("mp", None),
        P("mp", None),
        P(),
        P(),
    )
    return jax.shard_map(
        body,
        mesh=mesh,
        in_specs=placed,
        out_specs=(
            P(("dp", "mp"), None),
            P(("dp", "mp"), None),
            P(),
            P(),
            P(),
            P(None, None, "mp"),
            P(None, "mp"),
            P("mp", None),
            P(),
            P(),
            P(),
            P(None, None, "mp"),
            P(None, "mp"),
            P("mp", None),
            P(),
            P(),
        ),
        check_vma=False,
    )
```

```python
import functools

import jax
import jax.numpy as jnp
import ml_dtypes
import numpy as np
from jax import lax
from jax.experimental import pallas as pl
from jax.experimental.pallas import tpu as pltpu
from jax.sharding import PartitionSpec as P

HEAD_DIM = 128
CORES = 2
LONGEST = 512
ATTEND_BLOCK = 256
ADAPT_SCALE = 2.0
NORM_EPS = 1e-05
ROPE_BASE = 10000.0
MASKED = -1e30

F32 = jnp.float32
LOW = jnp.bfloat16
NN = (((1,), (0,)), ((), ()))
NT = (((1,), (1,)), ((), ()))
TN = (((0,), (0,)), ((), ()))


MESH_IDS = pl.DeviceIdType.MESH


def sibling_id():
    me = lax.axis_index("mp")
    return me // CORES * CORES + lax.rem(me + 1, CORES)


def greet(peers):
    for peer in peers:
        pl.semaphore_signal(
            pltpu.get_barrier_semaphore(), 1, device_id={"mp": peer}, device_id_type=MESH_IDS
        )


def greeted(count):
    pl.semaphore_wait(pltpu.get_barrier_semaphore(), count)


def remote(source, target, send_sem, recv_sem, peer):
    return pltpu.make_async_remote_copy(
        src_ref=source,
        dst_ref=target,
        send_sem=send_sem,
        recv_sem=recv_sem,
        device_id={"mp": peer},
        device_id_type=MESH_IDS,
    )


def dot(left, right, dims=NN):
    return lax.dot_general(left, right, dims, preferred_element_type=F32)


def shape(dims, kind):
    return jax.ShapeDtypeStruct(tuple(dims), kind)


def call(name, kernel, operands, grid, in_specs, out_specs, out_shape, scratch=(), prefetch=(), flops=0, mib=60, identity=None):
    moved = sum(v.size * v.dtype.itemsize for v in operands)
    moved += sum(v.size * v.dtype.itemsize for v in out_shape)
    return pl.pallas_call(
        kernel,
        name=name,
        out_shape=out_shape,
        grid_spec=pltpu.PrefetchScalarGridSpec(
            num_scalar_prefetch=len(prefetch),
            grid=grid,
            in_specs=in_specs,
            out_specs=out_specs,
            scratch_shapes=scratch,
        ),
        compiler_params=pltpu.CompilerParams(
            vmem_limit_bytes=mib * 2**20, collective_id=identity, has_side_effects=identity is not None
        ),
        cost_estimate=pl.CostEstimate(flops=flops // 16, bytes_accessed=moved // 16, transcendentals=0),
    )(*prefetch, *operands)


def tile_of(size, most):
    return most if size % most == 0 else size


def split_rows(values):
    top = values.astype(LOW)
    rest = (values - top.astype(F32)).astype(LOW)
    return jnp.concatenate([top, rest], axis=0)


def turned(left_map):
    return jnp.swapaxes(left_map, -1, -2)


def norm_weight(total, squares, magnitude):
    norm = jnp.sqrt(squares)
    return total * magnitude / (norm * norm * norm)


def sum_refs(refs):
    total = refs[0][...]
    for ref in refs[1:]:
        total = total + ref[...]
    return total


def fold(values):
    half = values.shape[0] // 2
    return values[:half] + values[half:]


def merge_tile(base_at, low_put, left, right, depth):
    rank = right.shape[0]
    doubled = ADAPT_SCALE * right
    top = doubled.astype(LOW)
    rest = (doubled - top.astype(F32)).astype(LOW)
    right_stack = jnp.concatenate([top, rest, top], axis=0)
    left_pair = split_rows(left)
    left_stack = jnp.concatenate([left_pair[:rank], left_pair[:rank], left_pair[rank:]], axis=0)
    squares = jnp.zeros((1, right.shape[1]), F32)
    step = tile_of(depth, 1024)
    for start in range(0, depth, step):
        merged = base_at(start, step).astype(F32) + dot(
            left_stack[:, start : start + step], right_stack, TN
        )
        low_put(start, step, merged.astype(LOW))
        squares = squares + jnp.sum(merged * merged, axis=0, keepdims=True)
    return squares


def merge_pair_kernel(*refs):
    for n in range(2):
        base_ref, left_ref, right_ref = refs[3 * n : 3 * n + 3]
        low_ref, squares_ref = refs[6 + n], refs[8]
        depth = base_ref.shape[0]
        if low_ref.shape[0] > depth:
            low_ref[depth:, :] = jnp.zeros((low_ref.shape[0] - depth, low_ref.shape[1]), LOW)

        def put(start, step, tile, low_ref=low_ref):
            low_ref[start : start + step, :] = tile

        squares_ref[n : n + 1, :] = merge_tile(
            lambda start, step, base_ref=base_ref: base_ref[start : start + step, :],
            put,
            left_ref[...],
            right_ref[...],
            depth,
        )


def merge_pair(triples):
    operands, in_specs, low_specs, low_shapes = [], [], [], []
    width = triples[0][0].shape[1]
    wide = tile_of(width, 512)
    for base, left, right in triples:
        depth, rank = base.shape[0], right.shape[0]
        operands += [base, left, right]
        in_specs += [
            pl.BlockSpec((depth, wide), lambda n: (0, n)),
            pl.BlockSpec((rank, depth), lambda n: (0, 0)),
            pl.BlockSpec((rank, wide), lambda n: (0, n)),
        ]
        low_specs.append(pl.BlockSpec((padded(depth), wide), lambda n: (0, n)))
        low_shapes.append(shape((padded(depth), width), LOW))
    return call(
        "merge_pair",
        merge_pair_kernel,
        tuple(operands),
        (width // wide,),
        in_specs,
        low_specs + [pl.BlockSpec((2, wide), lambda n: (0, n))],
        low_shapes + [shape((2, width), F32)],
        flops=2 * sum(v.size for v in operands) * 256,
    )


def merge_kernel(base_ref, left_ref, right_ref, low_ref, squares_ref):
    depth, width = base_ref.shape[1:]
    if low_ref.shape[1] > depth:
        low_ref[0, depth:, :] = jnp.zeros((low_ref.shape[1] - depth, low_ref.shape[2]), LOW)
    if low_ref.shape[2] > width:
        spare = low_ref.shape[2] - width
        low_ref[0, :, width:] = jnp.zeros((low_ref.shape[1], spare), LOW)
        squares_ref[0, :, width:] = jnp.ones((1, spare), F32)

    def put(start, step, tile):
        low_ref[0, start : start + step, :width] = tile

    squares = merge_tile(
        lambda start, step: base_ref[0, start : start + step, :],
        put,
        left_ref[0],
        right_ref[0],
        depth,
    )

    @pl.when(pl.program_id(2) == 0)
    def _():
        squares_ref[0, :, :width] = squares

    @pl.when(pl.program_id(2) > 0)
    def _():
        squares_ref[0, :, :width] += squares


def padded(size):
    return -(-size // 256) * 256


def pad_last(values, size):
    return jnp.pad(values, [(0, 0)] * (values.ndim - 1) + [(0, size - values.shape[-1])])


def merge(base, left, right, deep, wide):
    members, depth, width = base.shape
    low_deep = padded(deep) if deep == depth else deep
    low_wide = padded(wide) if wide == width else wide
    low_shape = (members, depth // deep * low_deep, width // wide * low_wide)
    rank = right.shape[1]
    return call(
        "merge",
        merge_kernel,
        (base, left, right),
        (members, width // wide, depth // deep),
        [
            pl.BlockSpec((1, deep, wide), lambda m, n, k: (m, k, n)),
            pl.BlockSpec((1, rank, deep), lambda m, n, k: (m, 0, k)),
            pl.BlockSpec((1, rank, wide), lambda m, n, k: (m, 0, n)),
        ],
        [
            pl.BlockSpec((1, low_deep, low_wide), lambda m, n, k: (m, k, n)),
            pl.BlockSpec((1, 1, low_wide), lambda m, n, k: (m, 0, n)),
        ],
        [shape(low_shape, LOW), shape((members, 1, low_shape[2]), F32)],
        flops=2 * members * depth * width * 256,
    )


def rms_rows(values):
    return lax.rsqrt(jnp.mean(values * values, axis=1, keepdims=True) + NORM_EPS)


TABLE_STEP = 32


def table_pieces(places):
    half = np.arange(HEAD_DIM) % (HEAD_DIM // 2)
    angles = np.asarray(places)[:, None] * ROPE_BASE ** (-2.0 * half / HEAD_DIM)[None, :]
    rest = np.concatenate([np.cos(angles), np.sin(angles)], axis=1)
    pieces = []
    for _ in range(3):
        pieces.append(rest.astype(ml_dtypes.bfloat16))
        rest = rest - pieces[-1].astype(np.float64)
    return jnp.asarray(np.concatenate(pieces, axis=0))


def rotation(first, coarse, fine):
    rows = first.shape[0]
    position = lax.broadcasted_iota(jnp.int32, (rows, 1), 0) - first
    lane = lax.broadcasted_iota(jnp.int32, (rows, 3 * TABLE_STEP), 1) % TABLE_STEP
    pick = lambda place, table: dot((lane == place).astype(F32).astype(LOW), table)
    high = pick(position // TABLE_STEP, coarse)
    small = pick(position % TABLE_STEP, fine)
    cos_a, sin_a = high[:, :HEAD_DIM], high[:, HEAD_DIM:]
    cos_b, sin_b = small[:, :HEAD_DIM], small[:, HEAD_DIM:]
    sine = sin_a * cos_b + cos_a * sin_b
    left_half = lax.broadcasted_iota(jnp.int32, sine.shape, 1) < HEAD_DIM // 2
    return cos_a * cos_b - sin_a * sin_b, jnp.where(left_half, -sine, sine)


def heads_kernel(
    token_ref,
    gain_ref,
    base_ref,
    left_ref,
    right_ref,
    magnitude_ref,
    first_ref,
    coarse_ref,
    fine_ref,
    part_ref,
    normed_ref,
    low_ref,
    post_ref,
    squares_ref,
    across_ref,
    cos_ref,
    sine_ref,
    sum_ref,
    rows_all,
    part_mine,
    part_got,
    send_sems,
    recv_sems,
):
    total_rows = token_ref.shape[0]
    depth, width = base_ref.shape[1:]
    rank = right_ref.shape[1]
    groups = part_got.shape[0]
    me = lax.axis_index("mp")
    peers = [lax.rem(me + k, groups) for k in range(groups)]
    part_copies = [
        remote(part_mine, part_got.at[k], send_sems.at[k], recv_sems.at[k], peers[k])
        for k in range(1, groups)
    ]

    @pl.when(pl.program_id(0) == 0)
    def _():
        greet(peers[1:])
        part_mine[...] = part_ref[...]
        step = 128

        def some(i, carry):
            at = pl.ds(pl.multiple_of(i * step, step), step)
            values = token_ref[at, :].astype(F32)
            low = (values * rms_rows(values) * gain_ref[...]).astype(LOW)
            normed_ref[at, :] = low
            rows_all[at, :] = low
            return carry

        lax.fori_loop(0, total_rows // step, some, 0)
        for start in range(0, total_rows, 256):
            rows = slice(start, start + 256)
            cosine, sine = rotation(first_ref[rows, :] - start, coarse_ref[...], fine_ref[...])
            cos_ref[rows, :] = cosine
            sine_ref[rows, :] = sine
        greeted(groups - 1)
        for copy in part_copies:
            copy.start()

    @pl.when(pl.program_id(0) == pl.num_programs(0) - 1)
    def _():
        total = part_mine[...]
        for k, copy in enumerate(part_copies, 1):
            copy.wait_recv()
            total = total + part_got[k]
        sum_ref[...] = total
        for copy in part_copies:
            copy.wait_send()

    rows_all[total_rows:, :] = left_ref[0].astype(LOW)
    turning = pl.program_id(0) < 2
    wide = 256
    for column in range(0, width, wide):
        columns = slice(column, column + wide)

        def put(start, step, tile, columns=columns):
            low_ref[0, start : start + step, columns] = tile

        squares_ref[0, :, columns] = merge_tile(
            lambda start, step, columns=columns: base_ref[0, start : start + step, columns],
            put,
            left_ref[0],
            right_ref[0, :, columns],
            depth,
        )
    for column in range(0, width, wide):
        columns = slice(column, column + wide)
        magnitude = magnitude_ref[pl.ds(pl.program_id(0), 1), columns]
        scale = magnitude / jnp.sqrt(squares_ref[0, :, columns])
        low = low_ref[0, :, columns]
        step = min(512, total_rows)
        for start in range(0, total_rows, step):
            last = start + step == total_rows
            rows = slice(start, start + step)
            pre = dot(rows_all[start : start + step + (rank if last else 0), :], low)
            if last:
                across_ref[0, :, columns] = pre[step:]
            post = pre[:step] * scale
            cos_table = jnp.where(turning, cos_ref[rows, :], 1.0)
            sine_table = jnp.where(turning, sine_ref[rows, :], 0.0)
            for head in range(0, wide, HEAD_DIM):
                piece = post[:, head : head + HEAD_DIM]
                other = pltpu.roll(piece, HEAD_DIM // 2, 1)
                post_ref[0, rows, column + head : column + head + HEAD_DIM] = (
                    piece * cos_table + other * sine_table
                ).astype(LOW)


def project_heads(tokens, gain, base, left, right, magnitude, first, part, groups):
    members, depth, width = base.shape
    rows, rank = tokens.shape[0], right.shape[1]
    coarse = table_pieces(np.arange(TABLE_STEP) * TABLE_STEP)
    fine = table_pieces(np.arange(TABLE_STEP))
    whole = lambda v: pl.BlockSpec(v.shape, lambda m: (0,) * v.ndim)
    of_member = lambda *dims: pl.BlockSpec((1,) + dims, lambda m: (m, 0, 0))
    table = pl.BlockSpec((rows, HEAD_DIM), lambda m: (0, 0))
    return call(
        "project_heads",
        heads_kernel,
        (tokens, gain, base, left, right, magnitude, first, coarse, fine, part),
        (members,),
        [
            whole(tokens),
            whole(gain),
            of_member(depth, width),
            of_member(rank, depth),
            of_member(rank, width),
            whole(magnitude),
            whole(first),
            whole(coarse),
            whole(fine),
            whole(part),
        ],
        [
            whole(tokens),
            of_member(depth, width),
            of_member(rows, width),
            of_member(1, width),
            of_member(rank, width),
            table,
            table,
            whole(part),
        ],
        [
            shape((rows, depth), LOW),
            shape(base.shape, LOW),
            shape((members, rows, width), LOW),
            shape((members, 1, width), F32),
            shape((members, rank, width), F32),
            shape((rows, HEAD_DIM), F32),
            shape((rows, HEAD_DIM), F32),
            shape(part.shape, F32),
        ],
        scratch=[
            pltpu.VMEM((rows + rank, depth), LOW),
            pltpu.VMEM(part.shape, F32),
            pltpu.VMEM((groups,) + part.shape, F32),
            pltpu.SemaphoreType.DMA((groups,)),
            pltpu.SemaphoreType.DMA((groups,)),
        ],
        identity=2,
        flops=2 * members * rows * depth * width,
    )


def key_start(block):
    return max(0, (block * ATTEND_BLOCK - (LONGEST - 1)) // ATTEND_BLOCK * ATTEND_BLOCK)


def masked_probs(scores, first, row_at, key_at):
    scores = scores * HEAD_DIM ** (-0.5)
    places = row_at + lax.broadcasted_iota(jnp.int32, scores.shape, 0)
    others = key_at + lax.broadcasted_iota(jnp.int32, scores.shape, 1)
    scores = jnp.where((others >= first) & (others <= places), scores, MASKED)
    exp_scores = jnp.exp(scores - jnp.max(scores, axis=1, keepdims=True))
    return exp_scores * (1.0 / jnp.sum(exp_scores, axis=1, keepdims=True))


class Unit:
    def __init__(self, head, block):
        self.row_at, self.key_at = block * ATTEND_BLOCK, key_start(block)
        self.rows = slice(self.row_at, self.row_at + ATTEND_BLOCK)
        self.keys = slice(self.key_at, self.row_at + ATTEND_BLOCK)
        self.lanes = slice(head * HEAD_DIM, (head + 1) * HEAD_DIM)


def units_of(rows, width, most):
    units = [
        Unit(head, block)
        for block in range(rows // ATTEND_BLOCK)
        for head in range(width // HEAD_DIM)
    ]
    return [units[at : at + most] for at in range(0, len(units), most)]


def put_rows(ref, lead, row_at, lanes, values, order_ref, groups):
    share = ref.shape[len(lead)] // groups
    step = min(share, values.shape[0])
    for start in range(0, values.shape[0], step):
        group = (row_at + start) // share
        inside = (row_at + start) % share
        at = pl.multiple_of(order_ref[groups + group] * share + inside, step)
        ref[(*lead, pl.ds(at, step), lanes)] = values[start : start + step].astype(ref.dtype)


def attend_kernel(groups, order_ref, query_ref, key_ref, value_ref, first_ref, out_ref):
    for some in units_of(*query_ref.shape[1:], 4):
        scores = [
            dot(query_ref[0, u.rows, u.lanes], key_ref[0, u.keys, u.lanes], NT) for u in some
        ]
        probs = [
            masked_probs(s, first_ref[u.rows, :], u.row_at, u.key_at).astype(LOW)
            for u, s in zip(some, scores)
        ]
        for u, p in zip(some, probs):
            mixed = dot(p, value_ref[0, u.keys, u.lanes])
            put_rows(out_ref, (), u.row_at, u.lanes, mixed, order_ref, groups)


def attend(order, groups, post, first):
    rows, width = post.shape[1:]
    wide = 2 * HEAD_DIM
    member = lambda m: pl.BlockSpec((1, rows, wide), lambda h, o: (m, 0, h))
    return call(
        "attend",
        functools.partial(attend_kernel, groups),
        (post, post, post, first),
        (width // wide,),
        [member(0), member(1), member(2), pl.BlockSpec((rows, 1), lambda h, o: (0, 0))],
        [pl.BlockSpec((rows, wide), lambda h, o: (0, h))],
        [shape((rows, width), LOW)],
        prefetch=(order,),
        flops=4 * rows * rows * width,
        mib=32,
    )[0]


def attend_back_kernel(
    groups,
    order_ref,
    query_ref,
    key_ref,
    value_ref,
    first_ref,
    cos_ref,
    sine_ref,
    magnitude_ref,
    squares_ref,
    low_ref,
    *rest,
):
    pieces, (grad_ref, total_ref, upper_all, heads_grad, key_grad, value_grad, sems) = rest[:-7], rest[-7:]
    rows_all, width = query_ref.shape[1:]
    share = rows_all // groups

    @pl.when(pl.program_id(0) == 0)
    def _():
        copies = []
        for place, piece in enumerate(pieces):
            at = pl.multiple_of(order_ref[place] * share, share)
            copies.append(
                pltpu.make_async_copy(piece, upper_all.at[pl.ds(at, share), :], sems.at[place])
            )
            copies[-1].start()
        for copy in copies:
            copy.wait()

    step = min(512, rows_all)
    for start in range(0, rows_all, step):
        at = slice(start, start + step)
        heads_grad[at, :] = dot(upper_all[at, :], low_ref[0], NT).astype(LOW)
    norm = [jnp.sqrt(squares_ref[m]) for m in range(3)]
    scale = [magnitude_ref[m : m + 1] / norm[m] for m in range(3)]
    heads = range(0, width, HEAD_DIM)
    totals = [jnp.zeros((1, width), F32) for _ in range(3)]
    filled = set()

    def back(values, rows):
        return values * cos_ref[rows, :] - pltpu.roll(values, HEAD_DIM // 2, 1) * sine_ref[rows, :]

    def add(ref, unit, values):
        for start in range(0, values.shape[0], ATTEND_BLOCK):
            at = unit.key_at + start
            rows = slice(at, at + ATTEND_BLOCK)
            name = (id(ref), at, unit.lanes.start)
            if name in filled:
                ref[rows, unit.lanes] += values[start : start + ATTEND_BLOCK]
            else:
                filled.add(name)
                ref[rows, unit.lanes] = values[start : start + ATTEND_BLOCK]

    def spread(per_head):
        return jnp.concatenate(per_head, axis=1)

    query_totals = [jnp.zeros((1, HEAD_DIM), F32) for _ in heads]
    for some in units_of(rows_all, width, 2):
        scores = [
            dot(query_ref[0, u.rows, u.lanes], key_ref[0, u.keys, u.lanes], NT) for u in some
        ]
        grad_weights = [
            dot(heads_grad[u.rows, u.lanes], value_ref[0, u.keys, u.lanes], NT) for u in some
        ]
        probs = [
            masked_probs(s, first_ref[u.rows, :], u.row_at, u.key_at)
            for u, s in zip(some, scores)
        ]
        grad_scores = [
            (p * (g - jnp.sum(p * g, axis=1, keepdims=True))).astype(LOW)
            for p, g in zip(probs, grad_weights)
        ]
        for u, p, g in zip(some, probs, grad_scores):
            add(value_grad, u, dot(p.astype(LOW), heads_grad[u.rows, u.lanes], TN))
            add(key_grad, u, dot(g, query_ref[0, u.rows, u.lanes], TN))
        for u, g in zip(some, grad_scores):
            grad = back(dot(g, key_ref[0, u.keys, u.lanes]) * HEAD_DIM ** (-0.5), u.rows)
            head = u.lanes.start // HEAD_DIM
            post = back(query_ref[0, u.rows, u.lanes].astype(F32), u.rows)
            query_totals[head] = query_totals[head] + jnp.sum(grad * post, axis=0, keepdims=True)
            put_rows(grad_ref, (0,), u.row_at, u.lanes, grad * scale[0][:, u.lanes], order_ref, groups)
    totals[0] = spread(query_totals)
    for row_at in range(0, rows_all, ATTEND_BLOCK):
        rows = slice(row_at, row_at + ATTEND_BLOCK)
        for head in heads:
            lanes = slice(head, head + HEAD_DIM)
            grad = back(key_grad[rows, lanes] * HEAD_DIM ** (-0.5), rows)
            post = back(key_ref[0, rows, lanes].astype(F32), rows)
            part = jnp.sum(grad * post, axis=0, keepdims=True)
            query_totals[head // HEAD_DIM] = part if row_at == 0 else query_totals[head // HEAD_DIM] + part
            put_rows(grad_ref, (1,), row_at, lanes, grad * scale[1][:, lanes], order_ref, groups)
        grad = value_grad[rows, :]
        totals[2] = totals[2] + jnp.sum(grad * value_ref[0, rows, :].astype(F32), axis=0, keepdims=True)
        put_rows(grad_ref, (2,), row_at, slice(0, width), grad * scale[2], order_ref, groups)
    totals[1] = spread(query_totals)
    for m in range(3):
        total_ref[m] = totals[m] / scale[m]


def attend_back(order, groups, post, first, cos_table, sine_table, magnitude, squares, low, pieces):
    rows, width = post.shape[1:]
    depth = low.shape[2]
    wide = 2 * HEAD_DIM
    member = lambda m: pl.BlockSpec((1, rows, wide), lambda h, o: (m, 0, h))
    table = pl.BlockSpec((rows, HEAD_DIM), lambda h, o: (0, 0))
    column = pl.BlockSpec((3, 1, wide), lambda h, o: (0, 0, h))
    return call(
        "attend_back",
        functools.partial(attend_back_kernel, groups),
        (post, post, post, first, cos_table, sine_table, magnitude, squares, low, *pieces),
        (width // wide,),
        [
            member(0),
            member(1),
            member(2),
            pl.BlockSpec((rows, 1), lambda h, o: (0, 0)),
            table,
            table,
            pl.BlockSpec((3, wide), lambda h, o: (0, h)),
            column,
            pl.BlockSpec((1, wide, depth), lambda h, o: (0, h, 0)),
            *[pl.BlockSpec(memory_space=pl.ANY) for _ in pieces],
        ],
        [pl.BlockSpec((3, rows, wide), lambda h, o: (0, 0, h)), column],
        [shape((3, rows, width), LOW), shape((3, 1, width), F32)],
        scratch=[
            pltpu.VMEM((rows, depth), LOW),
            pltpu.VMEM((rows, wide), LOW),
            pltpu.VMEM((rows, wide), F32),
            pltpu.VMEM((rows, wide), F32),
            pltpu.SemaphoreType.DMA((len(pieces),)),
        ],
        prefetch=(order,),
        flops=10 * rows * rows * width + 2 * rows * width * depth,
        mib=48,
    )


def product_kernel(dims, n_totals, steps, *refs):
    value_ref, weight_ref = refs[:2]
    if n_totals == 0:
        left_ref, *refs = refs[2:]
    else:
        right_ref, squares_ref, magnitude_ref = refs[2:5]
        totals, refs = refs[5 : 5 + n_totals], refs[5 + n_totals :]
    *outs, extra_ref, rows_all, sent, got, send_sems, recv_sems = refs
    members, groups, share, inner = value_ref.shape
    count, wide = groups * share, extra_ref.shape[2]
    now = pl.program_id(0)
    sibling = sibling_id()

    @pl.when(now == 0)
    def _():
        greet([sibling])
        if n_totals > 0:
            total = sum_refs(totals)
        for m in range(members):
            rows_all[m, :count, :] = value_ref[m].reshape(count, inner)
            if n_totals == 0:
                rows_all[m, count:, :] = left_ref[m].astype(LOW)
            else:
                weight = norm_weight(total[m], squares_ref[m], magnitude_ref[m : m + 1])
                rows_all[m, count:, :] = (right_ref[m] * weight).astype(LOW)

    result = None
    for m in range(members):
        part = dot(rows_all[m], weight_ref[m], dims)
        extra_ref[m] = part[count:]
        result = part[:count] if result is None else result + part[:count]

    def columns(step):
        return pl.ds(pl.multiple_of(step * wide, wide), wide)

    def copy(step):
        return remote(sent.at[step], got.at[step], send_sems.at[step], recv_sems.at[step], sibling)

    def add(step):
        copy(step).wait_recv()
        for n, ref in enumerate(outs):
            total = ref[:, columns(step)].astype(F32) + got[step, n].astype(F32)
            ref[:, columns(step)] = total.astype(LOW)

    for n, ref in enumerate(outs):
        at = CORES * n * share
        sent[now, n] = result[at : at + share].astype(LOW)
        ref[:, columns(now)] = result[at + share : at + CORES * share].astype(LOW)

    @pl.when(now == 0)
    def _():
        greeted(1)

    copy(now).start()

    @pl.when(now > 0)
    def _():
        add(now - 1)

    @pl.when(now == steps - 1)
    def _():
        add(now)
        for step in range(steps):
            copy(step).wait_send()


def product(name, identity, values, weights, dims, left=None, correction=None):
    members, groups, share, inner = values.shape
    chips = groups // CORES
    width = weights.shape[2] if dims is NN else weights.shape[1]
    wide = tile_of(width, 512)
    steps = width // wide
    if dims is NN:
        weight_spec = pl.BlockSpec((members, inner, wide), lambda n: (0, 0, n))
    else:
        weight_spec = pl.BlockSpec((members, wide, inner), lambda n: (0, n, 0))
    if correction is None:
        extra, n_totals, rank = (left,), 0, left.shape[1]
    else:
        right, squares, magnitude, totals = correction
        extra, n_totals, rank = (right, squares, magnitude, *totals), len(totals), right.shape[1]
    fixed = lambda v: pl.BlockSpec(v.shape, lambda n: (0,) * v.ndim)
    out = pl.BlockSpec((share, width), lambda n: (0, 0))
    results = call(
        name,
        functools.partial(product_kernel, dims, n_totals, steps),
        (values, weights, *extra),
        (steps,),
        [fixed(values), weight_spec] + [fixed(v) for v in extra],
        [out] * chips + [pl.BlockSpec((members, rank, wide), lambda n: (0, 0, n))],
        [shape((share, width), LOW)] * chips + [shape((members, rank, width), F32)],
        scratch=[
            pltpu.VMEM((members, groups * share + rank, inner), LOW),
            pltpu.VMEM((steps, chips, share, wide), LOW),
            pltpu.VMEM((steps, chips, share, wide), LOW),
            pltpu.SemaphoreType.DMA((steps,)),
            pltpu.SemaphoreType.DMA((steps,)),
        ],
        flops=2 * members * groups * share * inner * width,
        identity=identity,
    )
    return results[:chips], results[chips]


def shrink_kernel(chips, order_ref, *refs):
    values, (weight_ref, left_ref, cot_ref), outs = refs[:chips], refs[chips : chips + 3], refs[chips + 3 :]
    total_ref, across_ref, rows_all = outs[-3:]
    both, inner = values[0].shape
    share, depth = both // CORES, left_ref.shape[2]
    count = chips * both

    @pl.when(pl.program_id(0) == 0)
    def _():
        for step, ref in enumerate(values):
            rows_all[step * both : (step + 1) * both, :] = ref[...]
        if inner > depth:
            rows_all[count:, depth:] = jnp.zeros((rows_all.shape[0] - count, inner - depth), LOW)
        rows_all[count:, :depth] = left_ref[0].astype(LOW)

    result = dot(rows_all[...], weight_ref[0])
    across_ref[0] = result[count:]
    total = jnp.zeros((1, weight_ref.shape[2]), F32)
    for place in range(chips * CORES):
        pre = result[place * share : (place + 1) * share]
        outs[place][...] = pre.astype(LOW)
        at = pl.multiple_of(order_ref[place] * share, share)
        cot = cot_ref[pl.ds(at, share), :].astype(F32)
        total = total + jnp.sum(pre * cot, axis=0, keepdims=True)
    total_ref[...] = total


def shrink_product(order, values, weights, left, cotangent):
    chips = len(values)
    share, inner = values[0].shape[0] // CORES, values[0].shape[1]
    width, rank = weights.shape[2], left.shape[1]
    rows = chips * CORES * share
    wide = tile_of(width, 512)
    fixed = lambda v: pl.BlockSpec(v.shape, lambda n, o: (0,) * v.ndim)
    results = call(
        "shrink_product",
        functools.partial(shrink_kernel, chips),
        (*values, weights, left, cotangent),
        (width // wide,),
        [fixed(v) for v in values]
        + [
            pl.BlockSpec((1, inner, wide), lambda n, o: (0, 0, n)),
            fixed(left),
            pl.BlockSpec((rows, wide), lambda n, o: (0, n)),
        ],
        [pl.BlockSpec((share, wide), lambda n, o: (0, n))] * (chips * CORES)
        + [
            pl.BlockSpec((1, wide), lambda n, o: (0, n)),
            pl.BlockSpec((1, rank, wide), lambda n, o: (0, 0, n)),
        ],
        [shape((share, width), LOW)] * (chips * CORES)
        + [shape((1, width), F32), shape((1, rank, width), F32)],
        scratch=[pltpu.VMEM((rows + rank, inner), LOW)],
        prefetch=(order,),
        flops=2 * rows * inner * width,
    )
    return results[: chips * CORES], results[-2], results[-1]


def row_call(name, kernel, order, given, whole, out_kinds, sums, prepare):
    share = min(v.shape[0] for v, _ in given)
    width = given[0][0].shape[1]
    halves = 2
    half = share // halves
    count = len(given)

    def run(order_ref, *refs):
        sources, rest = refs[:count], refs[count : -count - 1]
        held, sems = refs[-count - 1 : -1], refs[-1]

        def copies(part):
            for i, ((_, cut), source, target) in enumerate(zip(given, sources, held)):
                at = part * half
                if cut:
                    at = pl.multiple_of(order_ref[1] * share + at, half)
                yield pltpu.make_async_copy(
                    source.at[pl.ds(at, half), :],
                    target.at[pl.ds(part * half, half), :],
                    sems.at[part, i],
                )

        for part in range(halves):

            @pl.when(pl.program_id(0) == part)
            def _(part=part):
                if part == 0:
                    for each in range(halves):
                        for copy in copies(each):
                            copy.start()
                for copy in copies(part):
                    copy.wait()

        outs = rest[len(whole) : len(whole) + len(out_kinds)]
        totals, sums_held = rest[len(whole) + len(out_kinds) :][:sums], rest[len(rest) - sums :]
        tile = 32
        lines = prepare(*[ref[...] for ref in rest[: len(whole)]])
        for ref in sums_held:
            ref[...] = jnp.zeros_like(ref)

        def some(i, carry):
            inside = pl.ds(pl.multiple_of(i * tile, tile), tile)
            at = pl.ds(pl.multiple_of(pl.program_id(0) * half + i * tile, tile), tile)
            values = kernel([ref[at, :].astype(F32) for ref in held], *lines)
            for ref, value in zip(outs, values):
                ref[inside, :] = value.astype(ref.dtype)
            for ref, value in zip(sums_held, values[len(outs) :]):
                ref[...] += jnp.sum(value.reshape(tile // 8, 8, width), axis=0)
            return carry

        lax.fori_loop(0, half // tile, some, 0, unroll=2)
        for ref, held_ref in zip(totals, sums_held):
            add_column(ref, held_ref[...])

    line = pl.BlockSpec((1, width), lambda i, o: (0, 0))
    return call(
        name,
        run,
        (*[v for v, _ in given], *whole),
        (halves,),
        [pl.BlockSpec(memory_space=pl.ANY) for _ in given] + [line for _ in whole],
        [pl.BlockSpec((half, width), lambda i, o: (i, 0)) for _ in out_kinds]
        + [line for _ in range(sums)],
        [shape((share, width), kind) for kind in out_kinds]
        + [shape((1, width), F32) for _ in range(sums)],
        scratch=[pltpu.VMEM((8, width), F32) for _ in range(sums)]
        + [pltpu.VMEM((share, width), v.dtype) for v, _ in given]
        + [pltpu.SemaphoreType.DMA((halves, count))],
        prefetch=(order,),
        flops=20 * share * width,
    )


def sum_of(values):
    total = values[0]
    for value in values[1:]:
        total = total + value
    return total


def add_column(ref, values):
    part = jnp.sum(values, axis=0, keepdims=True)

    @pl.when(pl.program_id(0) == 0)
    def _():
        ref[...] = part

    @pl.when(pl.program_id(0) > 0)
    def _():
        ref[...] += part


def scale_first(squares, magnitude, *rest):
    norm = jnp.sqrt(squares)
    return (magnitude / norm, norm / magnitude, *rest)


def hidden_kernel(given, scale, inverse, gain):
    hidden = given[0] + sum_of(given[1:]) * scale
    return hidden, hidden * rms_rows(hidden) * gain


def mixed_kernel(given, scale, inverse):
    return (given[0] + sum_of(given[1:]) * scale,)


def norm_back(grad_normed, values, gain):
    factor = rms_rows(values)
    scaled = grad_normed * gain
    inner = jnp.mean(scaled * values, axis=1, keepdims=True)
    back = factor * scaled - values * (factor * factor * factor * inner)
    return back, grad_normed * values * factor


def hidden_back_kernel(given, scale, inverse, gain):
    cot, token, hidden = given[:3]
    back, gain_terms = norm_back(sum_of(given[3:]), hidden, gain)
    grad = cot + back
    return grad, grad * scale, grad * ((hidden - token) * inverse), gain_terms


def token_back_kernel(given, gain):
    back, gain_terms = norm_back(sum_of(given[2:]), given[0], gain)
    return given[1] + back, gain_terms


def shrink_back_kernel(order_ref, cot_ref, low_ref, squares_ref, magnitude_ref, product_ref, grad_ref):
    scale = magnitude_ref[0] / jnp.sqrt(squares_ref[0])
    grad = (cot_ref[...].astype(F32) * scale).astype(LOW)
    grad_ref[0] = grad
    product_ref[0] = dot(grad, low_ref[0], NT)


def shrink_back(order, cotangent, low, squares, magnitude, groups):
    rows, width = cotangent.shape
    share, inner = rows // groups, low.shape[1]
    line = pl.BlockSpec((1, 1, width), lambda j, o: (0, 0, 0))
    return call(
        "shrink_back",
        shrink_back_kernel,
        (cotangent, low, squares, magnitude),
        (groups,),
        [
            pl.BlockSpec((share, width), lambda j, o: (o[j], 0)),
            pl.BlockSpec((1, inner, width), lambda j, o: (0, 0, 0)),
            line,
            line,
        ],
        [
            pl.BlockSpec((1, share, inner), lambda j, o: (j, 0, 0)),
            pl.BlockSpec((1, share, width), lambda j, o: (j, 0, 0)),
        ],
        [shape((groups, share, inner), F32), shape((groups, share, width), LOW)],
        prefetch=(order,),
        flops=2 * rows * width * inner,
    )


def expand_kernel(step, first, last, n_totals, *refs):
    mine_ref, low_ref, grad_ref, squares_ref, magnitude_ref = refs[:5]
    refs = list(refs[5:])
    left_ref = refs.pop(0) if first else None
    right_ref = refs.pop(0) if last else None
    before = [refs.pop(0) for _ in range(n_totals)]
    product_ref, back_ref, rows_ref, total_ref, joined_ref = refs[:5]
    refs = refs[5:]
    across_ref = refs.pop(0) if first else None
    extra_ref = refs.pop(0) if last else None
    rows_all, low_all, grad_all, product_all, back_all, sent, got, in_sems, out_sems, send_sems, recv_sems = refs
    share, depth = mine_ref.shape
    sibling = sibling_id()
    greet([sibling])
    both = CORES * share
    width, ff = low_ref.shape[2], magnitude_ref.shape[1]
    tile = 256
    cuts = [slice(at, at + tile) for at in range(0, width, tile)]

    mine_copy = pltpu.make_async_copy(mine_ref, rows_all.at[pl.ds(share, share), :], in_sems.at[0])
    other_copy = remote(
        rows_all.at[pl.ds(share, share), :],
        rows_all.at[pl.ds(0, share), :],
        send_sems.at[sent.shape[0]],
        recv_sems.at[sent.shape[0]],
        sibling,
    )
    tile_copies = []
    for n, cut in enumerate(cuts):
        lanes = pl.ds(cut.start, tile)
        tile_copies.append(
            [
                pltpu.make_async_copy(
                    low_ref.at[:, :, lanes], low_all.at[:, :, lanes], in_sems.at[2 + 2 * n]
                ),
                pltpu.make_async_copy(
                    grad_ref.at[pl.ds(CORES * step, CORES), :, lanes],
                    grad_all.at[:, :, lanes],
                    in_sems.at[3 + 2 * n],
                ),
            ]
        )
    mine_copy.start()
    for copies in tile_copies:
        for copy in copies:
            copy.start()
    if first:
        rank = across_ref.shape[1]
        for m in range(2):
            rows_all[both + m * rank : both + (m + 1) * rank, :] = left_ref[m].astype(LOW)
    mine_copy.wait()
    greeted(1)
    other_copy.start()
    other_copy.wait_recv()
    out_copies = [
        pltpu.make_async_copy(rows_all.at[pl.ds(0, both), :], rows_ref, out_sems.at[2 * len(cuts)])
    ]
    out_copies[0].start()
    lane = lax.broadcasted_iota(jnp.int32, (1, tile), 1)
    for n, cut in enumerate(cuts):
        for copy in tile_copies[n]:
            copy.wait()
        size = min(tile, ff - cut.start)
        pre = [dot(rows_all[...], low_all[m, :, cut]) for m in range(2)]
        if first:
            for m in range(2):
                rows = slice(both + m * rank, both + (m + 1) * rank)
                across_ref[m, :, cut.start : cut.start + size] = pre[m][rows, :size]
        magnitude, squares, scale = [], [], []
        for m in range(2):
            given = magnitude_ref[m : m + 1, cut.start : cut.start + size]
            if size < tile:
                given = jnp.concatenate([given, jnp.zeros((1, tile - size), F32)], axis=1)
            magnitude.append(given)
            squares.append(squares_ref[m, :, cut])
            scale.append(given / jnp.sqrt(squares[m]))
        sums = [jnp.zeros((1, tile), F32) for _ in range(2)]
        at = [slice(m * width + cut.start, m * width + cut.stop) for m in range(2)]
        for place in range(CORES):
            rows = slice(place * share, (place + 1) * share)
            gate_pre, up_pre = pre[0][rows], pre[1][rows]
            gate, up = gate_pre * scale[0], up_pre * scale[1]
            sigmoid = 0.5 + 0.5 * jnp.tanh(0.5 * gate)
            active = gate * sigmoid
            product_all[rows, cut] = (active * up).astype(LOW)
            upper = grad_all[place, :, cut]
            grad_up = upper * active
            grad_gate = upper * up * sigmoid * (1.0 + gate * (1.0 - sigmoid))
            sums[0] += jnp.sum(grad_gate * gate_pre, axis=0, keepdims=True)
            sums[1] += jnp.sum(grad_up * up_pre, axis=0, keepdims=True)
            back_all[rows, at[0]] = (grad_gate * scale[0]).astype(LOW)
            back_all[rows, at[1]] = (grad_up * scale[1]).astype(LOW)
        for m in range(2):
            total_ref[m, :, cut] = sums[m]
        if last:
            rank = extra_ref.shape[1]
            for m in range(2):
                total = sums[m]
                for ref in before:
                    total = total + ref[m, :, cut]
                right = right_ref[m, :, cut.start : cut.start + size]
                if size < tile:
                    spare = jnp.zeros((rank, tile - size), F32)
                    right = jnp.concatenate([right, spare], axis=1)
                weighted = right * norm_weight(total, squares[m], magnitude[m])
                rows = slice(both + m * rank, both + (m + 1) * rank)
                back_all[rows, at[m]] = weighted.astype(LOW)
                back_all[rows, at[1 - m]] = jnp.zeros((rank, tile), LOW)
    for m in range(2):
        lanes = pl.ds(m * width, width)
        copy = pltpu.make_async_copy(
            back_all.at[pl.ds(0, both), lanes], back_ref.at[m], out_sems.at[m]
        )
        copy.start()
        out_copies.append(copy)
    copy = pltpu.make_async_copy(product_all, product_ref, out_sems.at[2])
    copy.start()
    out_copies.append(copy)
    chunk = sent.shape[2]
    copies = [
        remote(sent.at[n], got.at[n], send_sems.at[n], recv_sems.at[n], sibling)
        for n in range(depth // chunk)
    ]

    def add(n):
        columns = slice(n * chunk, (n + 1) * chunk)
        copies[n].wait_recv()
        total = joined_ref[:, columns].astype(F32) + got[n].astype(F32)
        joined_ref[:, columns] = total.astype(LOW)

    for n in range(depth // chunk):
        columns = slice(n * chunk, (n + 1) * chunk)
        result = dot(back_all[:, :width], low_all[0, columns, :], NT)
        result = result + dot(back_all[:, width:], low_all[1, columns, :], NT)
        sent[n] = result[:share].astype(LOW)
        joined_ref[:, columns] = result[share:both].astype(LOW)
        copies[n].start()
        if n > 0:
            add(n - 1)
        if last:
            for m in range(2):
                extra_ref[m, :, columns] = result[both + m * rank : both + (m + 1) * rank]
    add(len(copies) - 1)
    for copy in out_copies:
        copy.wait()
    for copy in [other_copy, *copies]:
        copy.wait_send()


def expand(identity, mine, low, squares, magnitude, grad_product, step, left=None, right=None, before=()):
    share, depth = mine.shape
    width = low.shape[2]
    first, last = left is not None, right is not None
    rows = CORES * share
    hbm = pl.BlockSpec(memory_space=pl.ANY)
    fixed = lambda dims: pl.BlockSpec(tuple(dims), lambda i: (0,) * len(dims))
    operands = [mine, low, grad_product, squares, magnitude]
    in_specs = [hbm, hbm, hbm, fixed(squares.shape), fixed(magnitude.shape)]
    out_shape = [
        shape((rows, width), LOW),
        shape((2, rows, width), LOW),
        shape((rows, depth), LOW),
        shape((2, 1, width), F32),
        shape((share, depth), LOW),
    ]
    out_specs = [hbm, hbm, hbm] + [fixed(v.shape) for v in out_shape[3:]]
    extra_in = extra_out = 0
    if first:
        rank = left.shape[1]
        extra_in = 2 * rank
        operands.append(left)
        in_specs.append(fixed(left.shape))
        out_shape.append(shape((2, rank, magnitude.shape[1]), F32))
        out_specs.append(fixed(out_shape[-1].shape))
    if last:
        rank = right.shape[1]
        extra_out = 2 * rank
        operands += [right, *before]
        in_specs += [fixed(v.shape) for v in (right, *before)]
        out_shape.append(shape((2, rank, depth), F32))
        out_specs.append(fixed(out_shape[-1].shape))
    tiles, chunk = width // 256, tile_of(depth, 512)
    return call(
        "expand",
        functools.partial(expand_kernel, step, first, last, len(before)),
        tuple(operands),
        (1,),
        in_specs,
        out_specs,
        out_shape,
        scratch=[
            pltpu.VMEM((rows + extra_in, depth), LOW),
            pltpu.VMEM(low.shape, LOW),
            pltpu.VMEM((CORES, share, width), F32),
            pltpu.VMEM((rows, width), LOW),
            pltpu.VMEM((rows + extra_out, 2 * width), LOW),
            pltpu.VMEM((depth // chunk, share, chunk), LOW),
            pltpu.VMEM((depth // chunk, share, chunk), LOW),
            pltpu.SemaphoreType.DMA((2 + 2 * tiles,)),
            pltpu.SemaphoreType.DMA((2 * tiles + 1,)),
            pltpu.SemaphoreType.DMA((depth // chunk + 1,)),
            pltpu.SemaphoreType.DMA((depth // chunk + 1,)),
        ],
        flops=8 * rows * depth * width,
        identity=identity,
    )


def adapter_kernel(plan, n_inputs, n_grads, corrections, n_before, order_ref, *refs):
    count = n_inputs + n_grads
    sources, held, sems = refs[:count], refs[-count - 1 : -1], refs[-1]
    left_ref, right_ref = refs[count : count + 2]
    *corrected, left_out, right_out = refs[count + 2 : -count - 1]
    members, rank, width = right_ref.shape
    chunks = list(plan(order_ref, held[:n_inputs], held[n_inputs:]))
    copies = []
    for parts, _, _ in chunks:
        copies.append([])
        for which, index in parts:
            copy = pltpu.make_async_copy(
                sources[which].at[index],
                held[which].at[index],
                sems.at[sum(len(c) for c in copies)],
            )
            copy.start()
            copies[-1].append(copy)
    left_rows = jnp.concatenate([split_rows(left_ref[m]) for m in range(members)], axis=0)
    right_rows = [split_rows(right_ref[m]) for m in range(members)]
    before, corrected = corrected[:n_before], corrected[n_before:]
    for out, ref in zip((left_out, right_out), before or (None, None)):
        out[...] = jnp.zeros_like(out) if ref is None else ref[...]
    for waits, (_, taken_of, grads_of) in zip(copies, chunks):
        for copy in waits:
            copy.wait()
        taken = taken_of()
        across = dot(left_rows, taken, NT)
        downs = []
        for m in range(members):
            grad = grads_of(m)
            mine = split_rows(fold(across[2 * rank * m : 2 * rank * (m + 1)]))
            right_out[m] += fold(dot(mine, grad))
            downs.append(split_rows(fold(dot(right_rows[m], grad, NT))))
        left = dot(jnp.concatenate(downs, axis=0), taken)
        for m in range(members):
            left_out[m] += fold(left[2 * rank * m : 2 * rank * (m + 1)])
    if corrections:
        correct(corrections, right_ref, left_out, right_out, left_out, right_out, *corrected)


def correct(n_totals, right_ref, left_in, right_in, left_out, right_out, *refs):
    back_ref, across_ref, squares_ref, magnitude_ref = refs[:4]
    totals, magnitude_out = refs[4 : 4 + n_totals], refs[4 + n_totals]
    members, rank, width = right_ref.shape
    total = sum_refs(totals)[:, :, :width]
    squares = squares_ref[:, :, :width]
    magnitude_out[...] = total / jnp.sqrt(squares)
    for m in range(members):
        weight = norm_weight(total[m], squares[m], magnitude_ref[m : m + 1])
        if back_ref.dtype == LOW:
            low = back_ref[m, : left_in.shape[2], :]
            back = fold(dot(split_rows(right_ref[m] * weight), low, NT))
        else:
            back = back_ref[m]
        left_out[m] = ADAPT_SCALE * (left_in[m] - back)
        right_out[m] = ADAPT_SCALE * (right_in[m] - across_ref[m][:, :width] * weight)


def correct_kernel(n_totals, order_ref, right_ref, left_in, right_in, *refs):
    *rest, left_out, right_out = refs
    correct(n_totals, right_ref, left_in, right_in, left_out, right_out, *rest)


def correct_kernel(n_totals, right_ref, left_in, right_in, *refs):
    *rest, left_out, right_out = refs
    correct(n_totals, right_ref, left_in, right_in, left_out, right_out, *rest)


def corrected(name, sums, right, correction):
    members, rank, width = right.shape
    *given, totals = correction
    operands = (right, *sums, *given, *totals)
    outs = [(members, 1, width), sums[0].shape, sums[1].shape]
    full = lambda dims: pl.BlockSpec(tuple(dims), lambda i: (0,) * len(dims))
    return call(
        name,
        functools.partial(correct_kernel, len(totals)),
        operands,
        (1,),
        [full(v.shape) for v in operands],
        [full(dims) for dims in outs],
        [shape(dims, F32) for dims in outs],
        flops=sum(v.size for v in operands) * 64,
    )


def adapter(name, order, plan, inputs, grads, left, right, correction=None, before=()):
    members, rank, width = right.shape
    moved, fixed, n_totals = [*inputs, *grads], [left, right, *before], 0
    outs = [(members, rank, left.shape[2]), (members, rank, width)]
    if correction is not None:
        *given, totals = correction
        n_totals = len(totals)
        fixed += [*given, *totals]
        outs = [(members, 1, width)] + outs
    full = lambda dims: pl.BlockSpec(tuple(dims), lambda i, o: (0,) * len(dims))
    kernel = functools.partial(
        adapter_kernel, plan, len(inputs), len(grads), n_totals, len(before)
    )
    return call(
        name,
        kernel,
        (*moved, *fixed),
        (1,),
        [pl.BlockSpec(memory_space=pl.ANY) for _ in moved] + [full(v.shape) for v in fixed],
        [full(dims) for dims in outs],
        [shape(dims, F32) for dims in outs],
        scratch=[pltpu.VMEM(v.shape, v.dtype) for v in moved] + [pltpu.SemaphoreType.DMA((32,))],
        prefetch=(order,),
        flops=sum(v.size for v in moved) * 64,
    )


def copy_kernel(count, *refs):
    for source, target in zip(refs[:count], refs[count:]):
        target[...] = source[...]


def copy_out(arrays):
    vmem = pl.BlockSpec(memory_space=pltpu.VMEM)
    full = lambda v: pl.BlockSpec(v.shape, lambda i: (0,) * v.ndim)
    return call(
        "copy_out",
        functools.partial(copy_kernel, len(arrays)),
        tuple(arrays),
        (1,),
        [vmem for _ in arrays],
        [full(v) for v in arrays],
        [shape(v.shape, F32) for v in arrays],
        mib=16,
    )


GRAIN = 16


def pieces_of(width):
    return [(at, min(128, width - at)) for at in range(0, width, 128)]


def cells_of(blocks, lines, parts):
    cells, rows = [], []
    for n, block in enumerate(blocks):
        for m in range(block.shape[0]):
            for at, size in pieces_of(block.shape[2] // parts):
                cells.append((n, m, at, size))
    for n, line in enumerate(lines):
        for m in range(line.shape[0]):
            for at, size in pieces_of(line.shape[2] // parts):
                rows.append((n, m, at, size))
    return cells, rows


def pack(blocks, lines, wide_ref, part, parts, cells, rows):
    for i, (n, m, at, size) in enumerate(cells):
        start = part * (blocks[n].shape[2] // parts) + at
        wide_ref[part, i, :, :size] = blocks[n][m, :, start : start + size]
    for i, (n, m, at, size) in enumerate(rows):
        start = part * (lines[n].shape[2] // parts) + at
        cell, row = len(cells) + i // GRAIN, i % GRAIN
        wide_ref[part, cell, row : row + 1, :size] = lines[n][m, :, start : start + size]


def unpack(full_ref, blocks, lines, part, parts, cells, rows):
    for i, (n, m, at, size) in enumerate(cells):
        start = part * (blocks[n].shape[2] // parts) + at
        blocks[n][m, :, start : start + size] = full_ref[part, i].astype(F32)[:, :size]
    for i, (n, m, at, size) in enumerate(rows):
        start = part * (lines[n].shape[2] // parts) + at
        cell, row = len(cells) + i // GRAIN, i % GRAIN
        values = full_ref[part, cell].astype(F32)
        lines[n][m, :, start : start + size] = values[row : row + 1, :size]


def reduce_kernel(groups, lines, counts, *refs):
    n_all, n_all_lines, n_dp, n_dp_lines = counts
    count = sum(counts)
    taken, given, scratch = refs[:count], refs[count : 2 * count], refs[2 * count :]
    ends = [n_all, n_all + n_all_lines, n_all + n_all_lines + n_dp]
    parted = lambda v: (v[: ends[0]], v[ends[0] : ends[1]], v[ends[1] : ends[2]], v[ends[2] :])
    all_in, all_lines_in, dp_in, dp_lines_in = parted(taken)
    all_out, all_lines_out, dp_out, dp_lines_out = parted(given)
    (
        all_ref,
        line_ref,
        all_low,
        line_low,
        all_got,
        part,
        part_low,
        part_got,
        line_got,
        all_full,
        line_full,
        *sems,
    ) = scratch
    me, row = lax.axis_index("mp"), lax.axis_index("dp")
    piece, line_piece = part.shape[0] // lines, line_ref.shape[1] // lines
    mp_peer = [lax.rem(me + k, groups) for k in range(groups)]
    dp_peer = [lax.rem(row + k, lines) for k in range(lines)]
    barrier = pltpu.get_barrier_semaphore()
    for k in range(1, groups):
        pl.semaphore_signal(barrier, 1, device_id={"mp": mp_peer[k]}, device_id_type=MESH_IDS)
    for k in range(1, lines):
        pl.semaphore_signal(barrier, 1, device_id={"dp": dp_peer[k]}, device_id_type=MESH_IDS)
    all_cells = cells_of(all_in, all_lines_in, groups)
    dp_cells = cells_of(dp_in, dp_lines_in, 1)
    all_ref[...] = jnp.zeros_like(all_ref)
    line_ref[...] = jnp.zeros_like(line_ref)
    for q in range(groups):
        pack(all_in, all_lines_in, all_ref, q, groups, *all_cells)
    pack(dp_in, dp_lines_in, line_ref, 0, 1, *dp_cells)
    all_low[...] = all_ref[...].astype(LOW)
    line_low[...] = line_ref[...].astype(LOW)
    pl.semaphore_wait(barrier, groups + lines - 2)

    def send(source, target, stage, k, axis, peer):
        copy = pltpu.make_async_remote_copy(
            src_ref=source,
            dst_ref=target,
            send_sem=sems[2 * stage].at[k],
            recv_sem=sems[2 * stage + 1].at[k],
            device_id={axis: peer},
            device_id_type=MESH_IDS,
        )
        copy.start()
        return copy

    over_mp = [
        send(all_low.at[mp_peer[k]], all_got.at[k], 0, k, "mp", mp_peer[k])
        for k in range(1, groups)
    ]
    over_dp = [
        send(
            line_low.at[0, pl.ds(dp_peer[k] * line_piece, line_piece)],
            line_got.at[k],
            1,
            k,
            "dp",
            dp_peer[k],
        )
        for k in range(1, lines)
    ]
    total = all_ref[me]
    for k, copy in enumerate(over_mp, 1):
        copy.wait_recv()
        total = total + all_got[k].astype(F32)
    part[...] = total
    part_low[...] = total.astype(LOW)
    part_dp = [
        send(part_low.at[pl.ds(dp_peer[k] * piece, piece)], part_got.at[k], 2, k, "dp", dp_peer[k])
        for k in range(1, lines)
    ]
    held = pl.ds(row * piece, piece)
    total = part[held]
    for k, copy in enumerate(part_dp, 1):
        copy.wait_recv()
        total = total + part_got[k].astype(F32)
    all_full[me, held] = total.astype(LOW)
    part_back = [
        send(all_full.at[me, held], all_full.at[me, held], 4, k, "dp", dp_peer[k])
        for k in range(1, lines)
    ]
    mine = pl.ds(row * line_piece, line_piece)
    total = line_ref[0, mine]
    for k, copy in enumerate(over_dp, 1):
        copy.wait_recv()
        total = total + line_got[k].astype(F32)
    line_full[0, mine] = total.astype(LOW)
    line_back = [
        send(line_full.at[0, mine], line_full.at[0, mine], 3, k, "dp", dp_peer[k])
        for k in range(1, lines)
    ]
    for copy in part_back:
        copy.wait_recv()
    all_back = [
        send(all_full.at[me], all_full.at[me], 5, k, "mp", mp_peer[k]) for k in range(1, groups)
    ]
    for copy in line_back:
        copy.wait_recv()
    unpack(line_full, dp_out, dp_lines_out, 0, 1, *dp_cells)
    for copy in all_back:
        copy.wait_recv()
    for q in range(groups):
        unpack(all_full, all_out, all_lines_out, q, groups, *all_cells)
    for copy in over_mp + over_dp + part_dp + line_back + part_back + all_back:
        copy.wait_send()


def reduce_devices(name, identity, over_all, over_all_lines, over_dp, over_dp_lines):
    groups, lines = lax.axis_size("mp"), lax.axis_size("dp")

    def size_of(blocks, rows, parts):
        cells, lines_in = cells_of(blocks, rows, parts)
        size = len(cells) + -(-len(lines_in) // GRAIN)
        return -(-size // lines) * lines

    count, line_count = size_of(over_all, over_all_lines, groups), size_of(over_dp, over_dp_lines, 1)
    operands = (*over_all, *over_all_lines, *over_dp, *over_dp_lines)
    counts = (len(over_all), len(over_all_lines), len(over_dp), len(over_dp_lines))
    vmem = pl.BlockSpec(memory_space=pltpu.VMEM)
    tail = (GRAIN, 128)
    sizes = (groups, lines, lines, lines, lines, groups)
    every, line = (groups, count) + tail, (1, line_count) + tail
    results = pl.pallas_call(
        functools.partial(reduce_kernel, groups, lines, counts),
        name=name,
        out_shape=[shape(v.shape, F32) for v in operands],
        in_specs=[vmem for _ in operands],
        out_specs=[vmem for _ in operands],
        scratch_shapes=[
            pltpu.VMEM(every, F32),
            pltpu.VMEM(line, F32),
            pltpu.VMEM(every, LOW),
            pltpu.VMEM(line, LOW),
            pltpu.VMEM(every, LOW),
            pltpu.VMEM((count,) + tail, F32),
            pltpu.VMEM((count,) + tail, LOW),
            pltpu.VMEM((lines, count // lines) + tail, LOW),
            pltpu.VMEM((lines, line_count // lines) + tail, LOW),
            pltpu.VMEM(every, LOW),
            pltpu.VMEM(line, LOW),
        ]
        + [pltpu.SemaphoreType.DMA((n,)) for n in sizes for _ in range(2)],
        compiler_params=pltpu.CompilerParams(
            collective_id=identity, has_side_effects=True, vmem_limit_bytes=32 * 2**20
        ),
        cost_estimate=pl.CostEstimate(flops=1000, bytes_accessed=2**20, transcendentals=0),
    )(*operands)
    return copy_out(results)


def first_places(segment):
    length = segment.shape[0]
    places = lax.broadcasted_iota(jnp.int32, (length, length), 0)
    others = lax.broadcasted_iota(jnp.int32, (length, length), 1)
    visible = (segment[:, None] == segment[None, :]) & (others <= places)
    offset = jnp.sum(visible.astype(F32), axis=1) - 1.0
    return (jnp.arange(length, dtype=jnp.int32) - offset.astype(jnp.int32))[:, None]


def body(
    tokens,
    cotangent,
    segment_ids,
    attend_gain,
    expand_gain,
    heads_base,
    heads_left,
    heads_right,
    heads_magnitude,
    output_base,
    output_left,
    output_right,
    output_magnitude,
    expand_base,
    expand_left,
    expand_right,
    expand_magnitude,
    shrink_base,
    shrink_left,
    shrink_right,
    shrink_magnitude,
):
    groups = lax.axis_size("mp")
    chips = groups // CORES
    index = lax.axis_index("mp")
    chip, core = index // CORES, index % CORES
    rows, width = tokens.shape
    share = rows // groups
    local_heads, ff = heads_base.shape[2], expand_base.shape[2]
    ff_wide = padded(ff)
    device = jnp.arange(groups, dtype=jnp.int32)
    order = jnp.concatenate(
        [
            (chip + device // CORES) % chips * CORES + (core + 1 + device) % CORES,
            (device // CORES + chips - chip) % chips * CORES + (device + CORES - core + 1) % CORES,
        ]
    ).astype(jnp.int32)

    def tie(*values):
        return lax.optimization_barrier(values)

    def sibling(values):
        return lax.ppermute(
            values, "mp", [(i, i // CORES * CORES + (i + 1) % CORES) for i in range(groups)]
        )

    def to_chip(values, step):
        return lax.ppermute(
            values,
            "mp",
            [((i, ((i // CORES + step) % chips) * CORES + i % CORES)) for i in range(groups)],
        )

    def mp_sum(values):
        values = values + sibling(values)
        total = values
        for step in range(1, chips):
            total = total + to_chip(values, step)
        return total

    def join(pair):
        return (pair[1].astype(F32) + sibling(pair[0]).astype(F32)).astype(LOW)

    def chip_pairs(places):
        return [places[CORES * step : CORES * (step + 1)] for step in range(chips)]

    def arrive(own):
        return [to_chip(own, chips - step) for step in range(1, chips)]

    def pairs_of(own, near_sibling, arrived):
        return [(near_sibling, own)] + [(sibling(piece), piece) for piece in arrived]

    def in_pairs(order_ref, inputs, grads):
        for step, (taken, grad) in enumerate(zip(inputs, grads)):
            yield (
                [(step, ...), (chips + step, ...)],
                lambda taken=taken: taken[...],
                lambda m, grad=grad: grad[m, :, :ff],
            )

    def in_shrink(order_ref, inputs, grads):
        for step, taken in enumerate(inputs):
            at = slice(CORES * step, CORES * (step + 1))
            yield (
                [(step, ...), (chips, pl.ds(CORES * step, CORES))],
                lambda taken=taken: taken[:, :ff],
                lambda m, at=at: grads[0][at].reshape(-1, grads[0].shape[-1]),
            )

    def in_output(start):
        def plan(order_ref, inputs, grads):
            for n, grad in enumerate(grads):
                yield (
                    [(0, (0, start + n)), (1 + n, ...)],
                    lambda place=start + n: inputs[0][0, place],
                    lambda m, grad=grad: grad[...],
                )

        return plan

    def in_heads(order_ref, inputs, grads):
        for place in range(groups):
            at = pl.multiple_of(order_ref[place] * share, share)
            rows = pl.ds(place * share, share)
            yield (
                [(0, pl.ds(at, share)), (1, (slice(None), rows))],
                lambda at=at: inputs[0][pl.ds(at, share), :],
                lambda m, rows=rows: grads[0][m, rows, :],
            )

    heads_rows, output_rows = turned(heads_left), turned(output_left[None])
    expand_rows, shrink_rows = turned(expand_left), turned(shrink_left[None])
    heads_mag, output_mag = heads_magnitude, output_magnitude[None]
    expand_mag, shrink_mag = expand_magnitude, shrink_magnitude[None]
    attend_line, expand_line = attend_gain[None], expand_gain[None]

    output_low, shrink_low, squares_part = merge_pair(
        [(output_base, output_rows[0], output_right), (shrink_base, shrink_rows[0], shrink_right)]
    )
    output_low, shrink_low = output_low[None], shrink_low[None]
    first = first_places(segment_ids.reshape(-1))
    normed, heads_low, post, heads_sq, heads_across, cos_table, sine_table, squares = project_heads(
        tokens, attend_line, heads_base, heads_rows, heads_right, heads_mag, first, squares_part, groups
    )
    heads_out = attend(order, groups, post, first)
    output_sq, shrink_sq = squares[None, :1], squares[None, 1:]
    heads_parts = heads_out.reshape(1, groups, share, local_heads)
    joined, output_across = product(
        "output_product", 3, heads_parts, output_low, NN, left=output_rows
    )
    joined, expand_right_tied = tie(joined, expand_right)
    output_parts = [joined[0]] + [to_chip(joined[step], step) for step in range(1, chips)]
    expand_low, expand_sq = merge(
        expand_base, expand_rows, expand_right_tied, 1024, expand_base.shape[2]
    )
    grad_product, shrink_grad = shrink_back(
        order, cotangent, shrink_low, shrink_sq, shrink_mag[None], groups
    )
    output_parts, expand_low, grad_product = tie(output_parts, expand_low, grad_product)
    hidden, normed_own = row_call(
        "hidden",
        hidden_kernel,
        order,
        [(tokens, True)] + [(part, False) for part in output_parts],
        (output_sq[0], output_mag, expand_line),
        (F32, LOW),
        0,
        scale_first,
    )

    def feed(mine, step, **extra):
        return expand(
            4 + step, mine, expand_low, expand_sq, expand_mag, grad_product, step, **extra
        )

    arrived = arrive(normed_own)
    fed = [feed(normed_own, 0, left=expand_rows)]
    arrived, fed = tie(arrived, fed)
    fed = list(fed)
    for step in range(1, chips):
        extra = {}
        if step == chips - 1:
            extra = {"right": expand_right, "before": [f[3] for f in fed]}
        fed.append(feed(arrived[step - 1], step, **extra))
    expand_totals = [f[3] for f in fed]
    joined, shrink_rows_tied = tie([f[4] for f in fed], shrink_rows)
    mid_parts = [joined[0]] + [to_chip(joined[step], step) for step in range(1, chips)]
    shrink_places, shrink_total, shrink_across = shrink_product(
        order, [f[0] for f in fed], shrink_low, shrink_rows_tied, cotangent
    )
    shrink_pairs = chip_pairs(shrink_places)
    expand_adapter = adapter(
        "expand_adapter",
        order,
        in_pairs,
        [f[2] for f in fed],
        [f[1] for f in fed],
        expand_rows,
        expand_right,
        (fed[-1][5], fed[0][5], expand_sq, expand_mag, expand_totals),
    )
    mid_parts, shrink_pairs, expand_adapter = tie(mid_parts, shrink_pairs, expand_adapter)
    grad_hidden, output_grad_own, output_total, expand_gain_part = row_call(
        "hidden_back",
        hidden_back_kernel,
        order,
        [(cotangent, True), (tokens, True), (hidden, False)]
        + [(part, False) for part in mid_parts],
        (output_sq[0], output_mag, expand_line),
        (F32, LOW),
        2,
        scale_first,
    )
    arrived, near_sibling = arrive(output_grad_own), sibling(output_grad_own)
    both_totals = jnp.concatenate([output_total, shrink_total], axis=0)
    both_totals = both_totals + sibling(both_totals)
    shrink_joined = [join(pair) for pair in shrink_pairs[1:]]
    shrink_joined, both_totals, shrink_rows_tied = tie(shrink_joined, both_totals, shrink_rows)
    shrink_sums = adapter(
        "shrink_adapter",
        order,
        in_shrink,
        [f[0] for f in fed],
        [shrink_grad],
        shrink_rows_tied,
        shrink_right[None],
    )
    output_sums = adapter(
        "output_near_adapter",
        order,
        in_output(0),
        [heads_parts],
        [near_sibling, output_grad_own],
        output_rows,
        output_right[None],
    )
    arrived, near_sibling, both_totals, shrink_joined, shrink_sums, output_sums = tie(
        arrived, near_sibling, both_totals, shrink_joined, shrink_sums, output_sums
    )
    both_totals = functools.reduce(
        jnp.add, [both_totals] + [to_chip(both_totals, step) for step in range(1, chips)]
    )
    output_grad = [
        piece for pair in pairs_of(output_grad_own, near_sibling, arrived) for piece in pair
    ]
    shrink_parts = [shrink_pairs[0][1], sibling(shrink_pairs[0][0])] + [
        to_chip(values, step) for step, values in enumerate(shrink_joined, 1)
    ]
    heads_grads, heads_total = attend_back(
        order,
        groups,
        post,
        first,
        cos_table,
        sine_table,
        heads_mag,
        heads_sq,
        output_low,
        output_grad,
    )
    grad_parts = heads_grads.reshape(3, groups, share, local_heads)
    joined, token_extra = product(
        "normed_product",
        20,
        grad_parts,
        heads_low,
        NT,
        correction=(heads_right, heads_sq, heads_mag, [heads_total]),
    )
    joined, shrink_parts, both_totals, heads_rows_tied, output_rows_tied = tie(
        joined, shrink_parts, both_totals, heads_rows, output_rows
    )
    output_total, shrink_total = both_totals[:1], both_totals[1:]
    token_parts = [joined[0]] + [to_chip(joined[step], step) for step in range(1, chips)]
    output_adapter = adapter(
        "output_far_adapter",
        order,
        in_output(CORES),
        [heads_parts],
        output_grad[CORES:],
        output_rows_tied,
        output_right[None],
        (output_low, output_across, output_sq, output_mag, [output_total[None]]),
        output_sums,
    )
    shrink_adapter = corrected(
        "shrink_correct",
        shrink_sums,
        shrink_right[None],
        (shrink_low, shrink_across, shrink_sq, shrink_mag, [shrink_total[None]]),
    )
    heads_adapter = adapter(
        "heads_adapter",
        order,
        in_heads,
        [normed],
        [heads_grads],
        heads_rows_tied,
        heads_right,
        (token_extra, heads_across, heads_sq, heads_mag, [heads_total]),
    )
    (mixed,) = row_call(
        "mixed",
        mixed_kernel,
        order,
        [(hidden, False)] + [(part, False) for part in shrink_parts],
        (shrink_sq[0], shrink_mag),
        (LOW,),
        0,
        scale_first,
    )
    token_parts, output_adapter, shrink_adapter, heads_adapter, mixed = tie(
        token_parts, output_adapter, shrink_adapter, heads_adapter, mixed
    )
    grad_tokens, attend_gain_part = row_call(
        "token_back",
        token_back_kernel,
        order,
        [(tokens, True), (grad_hidden, False)] + [(part, False) for part in token_parts],
        (attend_line,),
        (F32,),
        1,
        lambda gain: (gain,),
    )
    (
        expand_left_grad,
        shrink_right_grad,
        heads_left_grad,
        output_right_grad,
        expand_gain_grad,
        attend_gain_grad,
        expand_right_grad,
        shrink_left_grad,
        heads_right_grad,
        output_left_grad,
        expand_mag_grad,
        shrink_mag_grad,
        heads_mag_grad,
        output_mag_grad,
    ) = reduce_devices(
        "reduce_gradients",
        1,
        [expand_adapter[1], shrink_adapter[2], heads_adapter[1], output_adapter[2]],
        [expand_gain_part[None], attend_gain_part[None]],
        [expand_adapter[2], shrink_adapter[1], heads_adapter[2], output_adapter[1]],
        [expand_adapter[0], shrink_adapter[0], heads_adapter[0], output_adapter[0]],
    )
    return (
        mixed,
        grad_tokens,
        attend_gain_grad[0, 0],
        expand_gain_grad[0, 0],
        jnp.swapaxes(heads_left_grad, 1, 2),
        heads_right_grad,
        heads_mag_grad[:, 0],
        output_left_grad[0].T,
        output_right_grad[0],
        output_mag_grad[0, 0],
        jnp.swapaxes(expand_left_grad, 1, 2),
        expand_right_grad,
        expand_mag_grad[:, 0],
        shrink_left_grad[0].T,
        shrink_right_grad[0],
        shrink_mag_grad[0, 0],
    )


def solution(mesh):
    placed = (
        P("dp", None),
        P("dp", None),
        P("dp", None),
        P(),
        P(),
        P(None, None, "mp"),
        P(),
        P(None, None, "mp"),
        P(None, "mp"),
        P("mp", None),
        P("mp", None),
        P(),
        P(),
        P(None, None, "mp"),
        P(),
        P(None, None, "mp"),
        P(None, "mp"),
        P("mp", None),
        P("mp", None),
        P(),
        P(),
    )
    return jax.shard_map(
        body,
        mesh=mesh,
        in_specs=placed,
        out_specs=(
            P(("dp", "mp"), None),
            P(("dp", "mp"), None),
            P(),
            P(),
            P(),
            P(None, None, "mp"),
            P(None, "mp"),
            P("mp", None),
            P(),
            P(),
            P(),
            P(None, None, "mp"),
            P(None, "mp"),
            P("mp", None),
            P(),
            P(),
        ),
        check_vma=False,
    )
```

```python
import functools

import jax
import jax.numpy as jnp
import ml_dtypes
import numpy as np
from jax import lax
from jax.experimental import pallas as pl
from jax.experimental.pallas import tpu as pltpu
from jax.sharding import PartitionSpec as P

HEAD_DIM = 128
CORES = 2
LONGEST = 512
ATTEND_BLOCK = 256
ADAPT_SCALE = 2.0
NORM_EPS = 1e-05
ROPE_BASE = 10000.0
MASKED = -1e30

F32 = jnp.float32
LOW = jnp.bfloat16
NN = (((1,), (0,)), ((), ()))
NT = (((1,), (1,)), ((), ()))
TN = (((0,), (0,)), ((), ()))


MESH_IDS = pl.DeviceIdType.MESH


def sibling_id():
    me = lax.axis_index("mp")
    return me // CORES * CORES + lax.rem(me + 1, CORES)


def greet(peers):
    for peer in peers:
        pl.semaphore_signal(
            pltpu.get_barrier_semaphore(), 1, device_id={"mp": peer}, device_id_type=MESH_IDS
        )


def greeted(count):
    pl.semaphore_wait(pltpu.get_barrier_semaphore(), count)


def remote(source, target, send_sem, recv_sem, peer):
    return pltpu.make_async_remote_copy(
        src_ref=source,
        dst_ref=target,
        send_sem=send_sem,
        recv_sem=recv_sem,
        device_id={"mp": peer},
        device_id_type=MESH_IDS,
    )


def dot(left, right, dims=NN):
    return lax.dot_general(left, right, dims, preferred_element_type=F32)


def shape(dims, kind):
    return jax.ShapeDtypeStruct(tuple(dims), kind)


def call(name, kernel, operands, grid, in_specs, out_specs, out_shape, scratch=(), prefetch=(), flops=0, mib=63, identity=None):
    moved = sum(v.size * v.dtype.itemsize for v in operands)
    moved += sum(v.size * v.dtype.itemsize for v in out_shape)
    return pl.pallas_call(
        kernel,
        name=name,
        out_shape=out_shape,
        grid_spec=pltpu.PrefetchScalarGridSpec(
            num_scalar_prefetch=len(prefetch),
            grid=grid,
            in_specs=in_specs,
            out_specs=out_specs,
            scratch_shapes=scratch,
        ),
        compiler_params=pltpu.CompilerParams(
            vmem_limit_bytes=mib * 2**20, collective_id=identity, has_side_effects=identity is not None
        ),
        cost_estimate=pl.CostEstimate(flops=flops // 16, bytes_accessed=moved // 16, transcendentals=0),
    )(*prefetch, *operands)


def tile_of(size, most):
    return most if size % most == 0 else size


def split_rows(values):
    top = values.astype(LOW)
    rest = (values - top.astype(F32)).astype(LOW)
    return jnp.concatenate([top, rest], axis=0)


def turned(left_map):
    return jnp.swapaxes(left_map, -1, -2)


def norm_weight(total, squares, magnitude):
    norm = jnp.sqrt(squares)
    return total * magnitude / (norm * norm * norm)


def sum_refs(refs):
    total = refs[0][...]
    for ref in refs[1:]:
        total = total + ref[...]
    return total


def fold(values):
    half = values.shape[0] // 2
    return values[:half] + values[half:]


def merge_tile(base_at, low_put, left, right, depth):
    doubled = ADAPT_SCALE * right
    top = doubled.astype(LOW)
    rest = (doubled - top.astype(F32)).astype(LOW)
    right_stack = jnp.concatenate([top, rest, top], axis=0)
    high = left.astype(LOW).astype(F32)
    left_stack = jnp.transpose(jnp.concatenate([high, high, left - high], axis=0)).astype(LOW)
    width = right.shape[1]
    step = tile_of(depth, 1024)
    squares = []
    for at in range(0, width, 256):
        size = min(256, width - at)
        columns = slice(at, at + size)
        same = lax.broadcasted_iota(jnp.int32, (size, size), 0) == lax.broadcasted_iota(
            jnp.int32, (size, size), 1
        )
        weights = jnp.concatenate(
            [same.astype(F32).astype(LOW), right_stack[:, columns]], axis=0
        )
        total = jnp.zeros((1, size), F32)
        for start in range(0, depth, step):
            rows = jnp.concatenate(
                [base_at(start, step, columns), left_stack[start : start + step]], axis=1
            )
            merged = dot(rows, weights)
            low_put(start, step, columns, merged.astype(LOW))
            total = total + jnp.sum(merged * merged, axis=0, keepdims=True)
        squares.append(total)
    return jnp.concatenate(squares, axis=1)


def merge_pair_kernel(*refs):
    for n in range(2):
        base_ref, left_ref, right_ref = refs[3 * n : 3 * n + 3]
        low_ref, squares_ref = refs[6 + n], refs[8]
        depth = base_ref.shape[0]
        if low_ref.shape[0] > depth:
            low_ref[depth:, :] = jnp.zeros((low_ref.shape[0] - depth, low_ref.shape[1]), LOW)

        def put(start, step, columns, tile, low_ref=low_ref):
            low_ref[start : start + step, columns] = tile

        squares_ref[n : n + 1, :] = merge_tile(
            lambda start, step, columns, base_ref=base_ref: base_ref[start : start + step, columns],
            put,
            left_ref[...],
            right_ref[...],
            depth,
        )


def merge_pair(triples):
    operands, in_specs, low_specs, low_shapes = [], [], [], []
    width = triples[0][0].shape[1]
    wide = tile_of(width, 512)
    for base, left, right in triples:
        depth, rank = base.shape[0], right.shape[0]
        operands += [base, left, right]
        in_specs += [
            pl.BlockSpec((depth, wide), lambda n: (0, n)),
            pl.BlockSpec((rank, depth), lambda n: (0, 0)),
            pl.BlockSpec((rank, wide), lambda n: (0, n)),
        ]
        low_specs.append(pl.BlockSpec((padded(depth), wide), lambda n: (0, n)))
        low_shapes.append(shape((padded(depth), width), LOW))
    return call(
        "merge_pair",
        merge_pair_kernel,
        tuple(operands),
        (width // wide,),
        in_specs,
        low_specs + [pl.BlockSpec((2, wide), lambda n: (0, n))],
        low_shapes + [shape((2, width), F32)],
        flops=2 * sum(v.size for v in operands) * 256,
    )


def merge_kernel(base_ref, left_ref, right_ref, low_ref, squares_ref):
    depth, width = base_ref.shape[1:]
    if low_ref.shape[1] > depth:
        low_ref[0, depth:, :] = jnp.zeros((low_ref.shape[1] - depth, low_ref.shape[2]), LOW)
    if low_ref.shape[2] > width:
        spare = low_ref.shape[2] - width
        low_ref[0, :, width:] = jnp.zeros((low_ref.shape[1], spare), LOW)
        squares_ref[0, :, width:] = jnp.ones((1, spare), F32)

    def put(start, step, columns, tile):
        low_ref[0, start : start + step, columns] = tile

    squares = merge_tile(
        lambda start, step, columns: base_ref[0, start : start + step, columns],
        put,
        left_ref[0],
        right_ref[0],
        depth,
    )

    @pl.when(pl.program_id(2) == 0)
    def _():
        squares_ref[0, :, :width] = squares

    @pl.when(pl.program_id(2) > 0)
    def _():
        squares_ref[0, :, :width] += squares


def padded(size):
    return -(-size // 256) * 256


def pad_last(values, size):
    return jnp.pad(values, [(0, 0)] * (values.ndim - 1) + [(0, size - values.shape[-1])])


def merge(base, left, right, deep, wide):
    members, depth, width = base.shape
    low_deep = padded(deep) if deep == depth else deep
    low_wide = padded(wide) if wide == width else wide
    low_shape = (members, depth // deep * low_deep, width // wide * low_wide)
    rank = right.shape[1]
    return call(
        "merge",
        merge_kernel,
        (base, left, right),
        (members, width // wide, depth // deep),
        [
            pl.BlockSpec((1, deep, wide), lambda m, n, k: (m, k, n)),
            pl.BlockSpec((1, rank, deep), lambda m, n, k: (m, 0, k)),
            pl.BlockSpec((1, rank, wide), lambda m, n, k: (m, 0, n)),
        ],
        [
            pl.BlockSpec((1, low_deep, low_wide), lambda m, n, k: (m, k, n)),
            pl.BlockSpec((1, 1, low_wide), lambda m, n, k: (m, 0, n)),
        ],
        [shape(low_shape, LOW), shape((members, 1, low_shape[2]), F32)],
        flops=2 * members * depth * width * 256,
    )


def rms_rows(values):
    return lax.rsqrt(jnp.mean(values * values, axis=1, keepdims=True) + NORM_EPS)


TABLE_STEP = 32


def table_pieces(places):
    half = np.arange(HEAD_DIM) % (HEAD_DIM // 2)
    angles = np.asarray(places)[:, None] * ROPE_BASE ** (-2.0 * half / HEAD_DIM)[None, :]
    rest = np.concatenate([np.cos(angles), np.sin(angles)], axis=1)
    pieces = []
    for _ in range(3):
        pieces.append(rest.astype(ml_dtypes.bfloat16))
        rest = rest - pieces[-1].astype(np.float64)
    return jnp.asarray(np.concatenate(pieces, axis=0))


def rotation(first, coarse, fine):
    rows = first.shape[0]
    position = lax.broadcasted_iota(jnp.int32, (rows, 1), 0) - first
    lane = lax.broadcasted_iota(jnp.int32, (rows, 3 * TABLE_STEP), 1) % TABLE_STEP
    pick = lambda place, table: dot((lane == place).astype(F32).astype(LOW), table)
    high = pick(position // TABLE_STEP, coarse)
    small = pick(position % TABLE_STEP, fine)
    cos_a, sin_a = high[:, :HEAD_DIM], high[:, HEAD_DIM:]
    cos_b, sin_b = small[:, :HEAD_DIM], small[:, HEAD_DIM:]
    sine = sin_a * cos_b + cos_a * sin_b
    left_half = lax.broadcasted_iota(jnp.int32, sine.shape, 1) < HEAD_DIM // 2
    return cos_a * cos_b - sin_a * sin_b, jnp.where(left_half, -sine, sine)


def heads_kernel(
    token_ref,
    gain_ref,
    base_ref,
    left_ref,
    right_ref,
    magnitude_ref,
    first_ref,
    coarse_ref,
    fine_ref,
    part_ref,
    normed_ref,
    low_ref,
    post_ref,
    squares_ref,
    across_ref,
    cos_ref,
    sine_ref,
    sum_ref,
    rows_all,
    part_mine,
    part_got,
    send_sems,
    recv_sems,
):
    total_rows = token_ref.shape[0]
    depth, width = base_ref.shape[1:]
    rank = right_ref.shape[1]
    groups = part_got.shape[0]
    me = lax.axis_index("mp")
    peers = [lax.rem(me + k, groups) for k in range(groups)]
    part_copies = [
        remote(part_mine, part_got.at[k], send_sems.at[k], recv_sems.at[k], peers[k])
        for k in range(1, groups)
    ]

    @pl.when(pl.program_id(0) == 0)
    def _():
        greet(peers[1:])
        part_mine[...] = part_ref[...]
        step = 128

        def some(i, carry):
            at = pl.ds(pl.multiple_of(i * step, step), step)
            values = token_ref[at, :].astype(F32)
            low = (values * rms_rows(values) * gain_ref[...]).astype(LOW)
            normed_ref[at, :] = low
            rows_all[at, :] = low
            return carry

        lax.fori_loop(0, total_rows // step, some, 0)
        for start in range(0, total_rows, 256):
            rows = slice(start, start + 256)
            cosine, sine = rotation(first_ref[rows, :] - start, coarse_ref[...], fine_ref[...])
            cos_ref[rows, :] = cosine
            sine_ref[rows, :] = sine
        greeted(groups - 1)
        for copy in part_copies:
            copy.start()

    @pl.when(pl.program_id(0) == pl.num_programs(0) - 1)
    def _():
        total = part_mine[...]
        for k, copy in enumerate(part_copies, 1):
            copy.wait_recv()
            total = total + part_got[k]
        sum_ref[...] = total
        for copy in part_copies:
            copy.wait_send()

    rows_all[total_rows:, :] = left_ref[0].astype(LOW)
    turning = pl.program_id(0) < 2
    wide = 256

    def put(start, step, columns, tile):
        low_ref[0, start : start + step, columns] = tile

    squares_ref[0] = merge_tile(
        lambda start, step, columns: base_ref[0, start : start + step, columns],
        put,
        left_ref[0],
        right_ref[0],
        depth,
    )
    for column in range(0, width, wide):
        columns = slice(column, column + wide)
        magnitude = magnitude_ref[pl.ds(pl.program_id(0), 1), columns]
        scale = magnitude / jnp.sqrt(squares_ref[0, :, columns])
        low = low_ref[0, :, columns]
        step = min(512, total_rows)
        for start in range(0, total_rows, step):
            last = start + step == total_rows
            rows = slice(start, start + step)
            pre = dot(rows_all[start : start + step + (rank if last else 0), :], low)
            if last:
                across_ref[0, :, columns] = pre[step:]
            post = pre[:step] * scale
            cos_table = jnp.where(turning, cos_ref[rows, :], 1.0)
            sine_table = jnp.where(turning, sine_ref[rows, :], 0.0)
            for head in range(0, wide, HEAD_DIM):
                piece = post[:, head : head + HEAD_DIM]
                other = pltpu.roll(piece, HEAD_DIM // 2, 1)
                post_ref[0, rows, column + head : column + head + HEAD_DIM] = (
                    piece * cos_table + other * sine_table
                ).astype(LOW)


def project_heads(tokens, gain, base, left, right, magnitude, first, part, groups):
    members, depth, width = base.shape
    rows, rank = tokens.shape[0], right.shape[1]
    coarse = table_pieces(np.arange(TABLE_STEP) * TABLE_STEP)
    fine = table_pieces(np.arange(TABLE_STEP))
    whole = lambda v: pl.BlockSpec(v.shape, lambda m: (0,) * v.ndim)
    of_member = lambda *dims: pl.BlockSpec((1,) + dims, lambda m: (m, 0, 0))
    table = pl.BlockSpec((rows, HEAD_DIM), lambda m: (0, 0))
    return call(
        "project_heads",
        heads_kernel,
        (tokens, gain, base, left, right, magnitude, first, coarse, fine, part),
        (members,),
        [
            whole(tokens),
            whole(gain),
            of_member(depth, width),
            of_member(rank, depth),
            of_member(rank, width),
            whole(magnitude),
            whole(first),
            whole(coarse),
            whole(fine),
            whole(part),
        ],
        [
            whole(tokens),
            of_member(depth, width),
            of_member(rows, width),
            of_member(1, width),
            of_member(rank, width),
            table,
            table,
            whole(part),
        ],
        [
            shape((rows, depth), LOW),
            shape(base.shape, LOW),
            shape((members, rows, width), LOW),
            shape((members, 1, width), F32),
            shape((members, rank, width), F32),
            shape((rows, HEAD_DIM), F32),
            shape((rows, HEAD_DIM), F32),
            shape(part.shape, F32),
        ],
        scratch=[
            pltpu.VMEM((rows + rank, depth), LOW),
            pltpu.VMEM(part.shape, F32),
            pltpu.VMEM((groups,) + part.shape, F32),
            pltpu.SemaphoreType.DMA((groups,)),
            pltpu.SemaphoreType.DMA((groups,)),
        ],
        identity=2,
        flops=2 * members * rows * depth * width,
    )


def key_start(block):
    return max(0, (block * ATTEND_BLOCK - (LONGEST - 1)) // ATTEND_BLOCK * ATTEND_BLOCK)


def masked_probs(scores, first, row_at, key_at):
    scores = scores * HEAD_DIM ** (-0.5)
    places = row_at + lax.broadcasted_iota(jnp.int32, scores.shape, 0)
    others = key_at + lax.broadcasted_iota(jnp.int32, scores.shape, 1)
    scores = jnp.where((others >= first) & (others <= places), scores, MASKED)
    exp_scores = jnp.exp(scores - jnp.max(scores, axis=1, keepdims=True))
    return exp_scores * (1.0 / jnp.sum(exp_scores, axis=1, keepdims=True))


class Unit:
    def __init__(self, head, block):
        self.row_at, self.key_at = block * ATTEND_BLOCK, key_start(block)
        self.rows = slice(self.row_at, self.row_at + ATTEND_BLOCK)
        self.keys = slice(self.key_at, self.row_at + ATTEND_BLOCK)
        self.lanes = slice(head * HEAD_DIM, (head + 1) * HEAD_DIM)


def units_of(rows, width, most):
    units = [
        Unit(head, block)
        for block in range(rows // ATTEND_BLOCK)
        for head in range(width // HEAD_DIM)
    ]
    return [units[at : at + most] for at in range(0, len(units), most)]


def put_rows(ref, lead, row_at, lanes, values, order_ref, groups):
    share = ref.shape[len(lead)] // groups
    step = min(share, values.shape[0])
    for start in range(0, values.shape[0], step):
        group = (row_at + start) // share
        inside = (row_at + start) % share
        at = pl.multiple_of(order_ref[groups + group] * share + inside, step)
        ref[(*lead, pl.ds(at, step), lanes)] = values[start : start + step].astype(ref.dtype)


def attend_kernel(groups, order_ref, query_ref, key_ref, value_ref, first_ref, out_ref):
    for some in units_of(*query_ref.shape[1:], 4):
        scores = [
            dot(query_ref[0, u.rows, u.lanes], key_ref[0, u.keys, u.lanes], NT) for u in some
        ]
        probs = [
            masked_probs(s, first_ref[u.rows, :], u.row_at, u.key_at).astype(LOW)
            for u, s in zip(some, scores)
        ]
        for u, p in zip(some, probs):
            mixed = dot(p, value_ref[0, u.keys, u.lanes])
            put_rows(out_ref, (), u.row_at, u.lanes, mixed, order_ref, groups)


def attend(order, groups, post, first):
    rows, width = post.shape[1:]
    wide = 2 * HEAD_DIM
    member = lambda m: pl.BlockSpec((1, rows, wide), lambda h, o: (m, 0, h))
    return call(
        "attend",
        functools.partial(attend_kernel, groups),
        (post, post, post, first),
        (width // wide,),
        [member(0), member(1), member(2), pl.BlockSpec((rows, 1), lambda h, o: (0, 0))],
        [pl.BlockSpec((rows, wide), lambda h, o: (0, h))],
        [shape((rows, width), LOW)],
        prefetch=(order,),
        flops=4 * rows * rows * width,
        mib=32,
    )[0]


def attend_back_kernel(
    groups,
    order_ref,
    query_ref,
    key_ref,
    value_ref,
    first_ref,
    cos_ref,
    sine_ref,
    magnitude_ref,
    squares_ref,
    low_ref,
    *rest,
):
    pieces, (grad_ref, total_ref, upper_all, heads_grad, key_grad, value_grad, sems) = rest[:-7], rest[-7:]
    rows_all, width = query_ref.shape[1:]
    share = rows_all // groups

    @pl.when(pl.program_id(0) == 0)
    def _():
        copies = []
        for place, piece in enumerate(pieces):
            at = pl.multiple_of(order_ref[place] * share, share)
            copies.append(
                pltpu.make_async_copy(piece, upper_all.at[pl.ds(at, share), :], sems.at[place])
            )
            copies[-1].start()
        for copy in copies:
            copy.wait()

    step = min(512, rows_all)
    for start in range(0, rows_all, step):
        at = slice(start, start + step)
        heads_grad[at, :] = dot(upper_all[at, :], low_ref[0], NT).astype(LOW)
    norm = [jnp.sqrt(squares_ref[m]) for m in range(3)]
    scale = [magnitude_ref[m : m + 1] / norm[m] for m in range(3)]
    heads = range(0, width, HEAD_DIM)
    totals = [jnp.zeros((1, width), F32) for _ in range(3)]
    filled = set()

    def back(values, rows):
        return values * cos_ref[rows, :] - pltpu.roll(values, HEAD_DIM // 2, 1) * sine_ref[rows, :]

    def add(ref, unit, values):
        for start in range(0, values.shape[0], ATTEND_BLOCK):
            at = unit.key_at + start
            rows = slice(at, at + ATTEND_BLOCK)
            name = (id(ref), at, unit.lanes.start)
            if name in filled:
                ref[rows, unit.lanes] += values[start : start + ATTEND_BLOCK]
            else:
                filled.add(name)
                ref[rows, unit.lanes] = values[start : start + ATTEND_BLOCK]

    def spread(per_head):
        return jnp.concatenate(per_head, axis=1)

    query_totals = [jnp.zeros((1, HEAD_DIM), F32) for _ in heads]
    for some in units_of(rows_all, width, 2):
        scores = [
            dot(query_ref[0, u.rows, u.lanes], key_ref[0, u.keys, u.lanes], NT) for u in some
        ]
        grad_weights = [
            dot(heads_grad[u.rows, u.lanes], value_ref[0, u.keys, u.lanes], NT) for u in some
        ]
        probs = [
            masked_probs(s, first_ref[u.rows, :], u.row_at, u.key_at)
            for u, s in zip(some, scores)
        ]
        grad_scores = [
            (p * (g - jnp.sum(p * g, axis=1, keepdims=True))).astype(LOW)
            for p, g in zip(probs, grad_weights)
        ]
        for u, p, g in zip(some, probs, grad_scores):
            add(value_grad, u, dot(p.astype(LOW), heads_grad[u.rows, u.lanes], TN))
            add(key_grad, u, dot(g, query_ref[0, u.rows, u.lanes], TN))
        for u, g in zip(some, grad_scores):
            grad = back(dot(g, key_ref[0, u.keys, u.lanes]) * HEAD_DIM ** (-0.5), u.rows)
            head = u.lanes.start // HEAD_DIM
            post = back(query_ref[0, u.rows, u.lanes].astype(F32), u.rows)
            query_totals[head] = query_totals[head] + jnp.sum(grad * post, axis=0, keepdims=True)
            put_rows(grad_ref, (0,), u.row_at, u.lanes, grad * scale[0][:, u.lanes], order_ref, groups)
    totals[0] = spread(query_totals)
    for row_at in range(0, rows_all, ATTEND_BLOCK):
        rows = slice(row_at, row_at + ATTEND_BLOCK)
        for head in heads:
            lanes = slice(head, head + HEAD_DIM)
            grad = back(key_grad[rows, lanes] * HEAD_DIM ** (-0.5), rows)
            post = back(key_ref[0, rows, lanes].astype(F32), rows)
            part = jnp.sum(grad * post, axis=0, keepdims=True)
            query_totals[head // HEAD_DIM] = part if row_at == 0 else query_totals[head // HEAD_DIM] + part
            put_rows(grad_ref, (1,), row_at, lanes, grad * scale[1][:, lanes], order_ref, groups)
        grad = value_grad[rows, :]
        totals[2] = totals[2] + jnp.sum(grad * value_ref[0, rows, :].astype(F32), axis=0, keepdims=True)
        put_rows(grad_ref, (2,), row_at, slice(0, width), grad * scale[2], order_ref, groups)
    totals[1] = spread(query_totals)
    for m in range(3):
        total_ref[m] = totals[m] / scale[m]


def attend_back(order, groups, post, first, cos_table, sine_table, magnitude, squares, low, pieces):
    rows, width = post.shape[1:]
    depth = low.shape[2]
    wide = 2 * HEAD_DIM
    member = lambda m: pl.BlockSpec((1, rows, wide), lambda h, o: (m, 0, h))
    table = pl.BlockSpec((rows, HEAD_DIM), lambda h, o: (0, 0))
    column = pl.BlockSpec((3, 1, wide), lambda h, o: (0, 0, h))
    return call(
        "attend_back",
        functools.partial(attend_back_kernel, groups),
        (post, post, post, first, cos_table, sine_table, magnitude, squares, low, *pieces),
        (width // wide,),
        [
            member(0),
            member(1),
            member(2),
            pl.BlockSpec((rows, 1), lambda h, o: (0, 0)),
            table,
            table,
            pl.BlockSpec((3, wide), lambda h, o: (0, h)),
            column,
            pl.BlockSpec((1, wide, depth), lambda h, o: (0, h, 0)),
            *[pl.BlockSpec(memory_space=pl.ANY) for _ in pieces],
        ],
        [pl.BlockSpec((3, rows, wide), lambda h, o: (0, 0, h)), column],
        [shape((3, rows, width), LOW), shape((3, 1, width), F32)],
        scratch=[
            pltpu.VMEM((rows, depth), LOW),
            pltpu.VMEM((rows, wide), LOW),
            pltpu.VMEM((rows, wide), F32),
            pltpu.VMEM((rows, wide), F32),
            pltpu.SemaphoreType.DMA((len(pieces),)),
        ],
        prefetch=(order,),
        flops=10 * rows * rows * width + 2 * rows * width * depth,
        mib=48,
    )


def product_kernel(dims, n_totals, n_lines, steps, *refs):
    value_ref, weight_ref = refs[:2]
    if n_totals == 0:
        left_ref, *refs = refs[2:]
    else:
        right_ref, squares_ref, magnitude_ref = refs[2:5]
        totals, refs = refs[5 : 5 + n_totals], refs[5 + n_totals :]
    lines = []
    if n_lines > 0:
        lines, refs = refs[:n_lines], refs[n_lines:]
        *refs, line_mine, line_got, line_send_sems, line_recv_sems = refs
    *outs, extra_ref, rows_all, sent, got, send_sems, recv_sems = refs
    if n_lines > 0:
        *outs, line_out = outs
    members, groups, share, inner = value_ref.shape
    count, wide = groups * share, extra_ref.shape[2]
    now = pl.program_id(0)
    sibling = sibling_id()
    me = lax.axis_index("mp")
    peers = [lax.rem(me + k, groups) for k in range(1, groups)] if n_lines > 0 else [sibling]
    line_copies = [
        remote(line_mine, line_got.at[k], line_send_sems.at[k], line_recv_sems.at[k], peer)
        for k, peer in enumerate(peers if n_lines > 0 else [], 1)
    ]

    @pl.when(now == 0)
    def _():
        greet(peers)
        for n, ref in enumerate(lines):
            line_mine[n : n + 1, :] = ref[...]
        if n_totals > 0:
            total = sum_refs(totals)
        for m in range(members):
            rows_all[m, :count, :] = value_ref[m].reshape(count, inner)
            if n_totals == 0:
                rows_all[m, count:, :] = left_ref[m].astype(LOW)
            else:
                weight = norm_weight(total[m], squares_ref[m], magnitude_ref[m : m + 1])
                rows_all[m, count:, :] = (right_ref[m] * weight).astype(LOW)

    result = None
    for m in range(members):
        part = dot(rows_all[m], weight_ref[m], dims)
        extra_ref[m] = part[count:]
        result = part[:count] if result is None else result + part[:count]

    def columns(step):
        return pl.ds(pl.multiple_of(step * wide, wide), wide)

    def copy(step):
        return remote(sent.at[step], got.at[step], send_sems.at[step], recv_sems.at[step], sibling)

    def add(step):
        copy(step).wait_recv()
        for n, ref in enumerate(outs):
            total = ref[:, columns(step)].astype(F32) + got[step, n].astype(F32)
            ref[:, columns(step)] = total.astype(LOW)

    for n, ref in enumerate(outs):
        at = CORES * n * share
        sent[now, n] = result[at : at + share].astype(LOW)
        ref[:, columns(now)] = result[at + share : at + CORES * share].astype(LOW)

    @pl.when(now == 0)
    def _():
        greeted(len(peers))
        for each in line_copies:
            each.start()

    copy(now).start()

    @pl.when(now > 0)
    def _():
        add(now - 1)

    @pl.when(now == steps - 1)
    def _():
        add(now)
        for step in range(steps):
            copy(step).wait_send()
        if n_lines > 0:
            line_sum = line_mine[...]
            for k, each in enumerate(line_copies, 1):
                each.wait_recv()
                line_sum = line_sum + line_got[k]
            line_out[...] = line_sum
            for each in line_copies:
                each.wait_send()


def product(name, identity, values, weights, dims, left=None, correction=None, lines=()):
    members, groups, share, inner = values.shape
    chips = groups // CORES
    width = weights.shape[2] if dims is NN else weights.shape[1]
    wide = tile_of(width, 512)
    steps = width // wide
    if dims is NN:
        weight_spec = pl.BlockSpec((members, inner, wide), lambda n: (0, 0, n))
    else:
        weight_spec = pl.BlockSpec((members, wide, inner), lambda n: (0, n, 0))
    if correction is None:
        extra, n_totals, rank = (left,), 0, left.shape[1]
    else:
        right, squares, magnitude, totals = correction
        extra, n_totals, rank = (right, squares, magnitude, *totals), len(totals), right.shape[1]
    fixed = lambda v: pl.BlockSpec(v.shape, lambda n: (0,) * v.ndim)
    out = pl.BlockSpec((share, width), lambda n: (0, 0))
    line_specs, line_shapes, line_scratch = [], [], []
    if lines:
        line = (len(lines), width)
        line_specs = [pl.BlockSpec(line, lambda n: (0, 0))]
        line_shapes = [shape(line, F32)]
        line_scratch = [
            pltpu.VMEM(line, F32),
            pltpu.VMEM((groups,) + line, F32),
            pltpu.SemaphoreType.DMA((groups,)),
            pltpu.SemaphoreType.DMA((groups,)),
        ]
    results = call(
        name,
        functools.partial(product_kernel, dims, n_totals, len(lines), steps),
        (values, weights, *extra, *lines),
        (steps,),
        [fixed(values), weight_spec] + [fixed(v) for v in (*extra, *lines)],
        [out] * chips + line_specs + [pl.BlockSpec((members, rank, wide), lambda n: (0, 0, n))],
        [shape((share, width), LOW)] * chips
        + line_shapes
        + [shape((members, rank, width), F32)],
        scratch=[
            pltpu.VMEM((members, groups * share + rank, inner), LOW),
            pltpu.VMEM((steps, chips, share, wide), LOW),
            pltpu.VMEM((steps, chips, share, wide), LOW),
            pltpu.SemaphoreType.DMA((steps,)),
            pltpu.SemaphoreType.DMA((steps,)),
        ]
        + line_scratch,
        flops=2 * members * groups * share * inner * width,
        identity=identity,
    )
    return results[:chips], *results[chips:]


def shrink_kernel(chips, order_ref, *refs):
    values, (weight_ref, left_ref, cot_ref), outs = refs[:chips], refs[chips : chips + 3], refs[chips + 3 :]
    total_ref, across_ref, rows_all = outs[-3:]
    both, inner = values[0].shape
    share, depth = both // CORES, left_ref.shape[2]
    count = chips * both

    @pl.when(pl.program_id(0) == 0)
    def _():
        for step, ref in enumerate(values):
            rows_all[step * both : (step + 1) * both, :] = ref[...]
        if inner > depth:
            rows_all[count:, depth:] = jnp.zeros((rows_all.shape[0] - count, inner - depth), LOW)
        rows_all[count:, :depth] = left_ref[0].astype(LOW)

    result = dot(rows_all[...], weight_ref[0])
    across_ref[0] = result[count:]
    total = jnp.zeros((1, weight_ref.shape[2]), F32)
    for place in range(chips * CORES):
        pre = result[place * share : (place + 1) * share]
        outs[place][...] = pre.astype(LOW)
        at = pl.multiple_of(order_ref[place] * share, share)
        cot = cot_ref[pl.ds(at, share), :].astype(F32)
        total = total + jnp.sum(pre * cot, axis=0, keepdims=True)
    total_ref[...] = total


def shrink_product(order, values, weights, left, cotangent):
    chips = len(values)
    share, inner = values[0].shape[0] // CORES, values[0].shape[1]
    width, rank = weights.shape[2], left.shape[1]
    rows = chips * CORES * share
    wide = tile_of(width, 512)
    fixed = lambda v: pl.BlockSpec(v.shape, lambda n, o: (0,) * v.ndim)
    results = call(
        "shrink_product",
        functools.partial(shrink_kernel, chips),
        (*values, weights, left, cotangent),
        (width // wide,),
        [fixed(v) for v in values]
        + [
            pl.BlockSpec((1, inner, wide), lambda n, o: (0, 0, n)),
            fixed(left),
            pl.BlockSpec((rows, wide), lambda n, o: (0, n)),
        ],
        [pl.BlockSpec((share, wide), lambda n, o: (0, n))] * (chips * CORES)
        + [
            pl.BlockSpec((1, wide), lambda n, o: (0, n)),
            pl.BlockSpec((1, rank, wide), lambda n, o: (0, 0, n)),
        ],
        [shape((share, width), LOW)] * (chips * CORES)
        + [shape((1, width), F32), shape((1, rank, width), F32)],
        scratch=[pltpu.VMEM((rows + rank, inner), LOW)],
        prefetch=(order,),
        flops=2 * rows * inner * width,
    )
    return results[: chips * CORES], results[-2], results[-1]


def row_call(name, kernel, order, given, whole, out_kinds, sums, prepare):
    share = min(v.shape[0] for v, _ in given)
    width = given[0][0].shape[1]
    halves = 2
    half = share // halves
    count = len(given)

    def run(order_ref, *refs):
        sources, rest = refs[:count], refs[count : -count - 1]
        held, sems = refs[-count - 1 : -1], refs[-1]

        def copies(part):
            for i, ((_, cut), source, target) in enumerate(zip(given, sources, held)):
                at = part * half
                if cut:
                    at = pl.multiple_of(order_ref[1] * share + at, half)
                yield pltpu.make_async_copy(
                    source.at[pl.ds(at, half), :],
                    target.at[pl.ds(part * half, half), :],
                    sems.at[part, i],
                )

        for part in range(halves):

            @pl.when(pl.program_id(0) == part)
            def _(part=part):
                if part == 0:
                    for each in range(halves):
                        for copy in copies(each):
                            copy.start()
                for copy in copies(part):
                    copy.wait()

        outs = rest[len(whole) : len(whole) + len(out_kinds)]
        totals, sums_held = rest[len(whole) + len(out_kinds) :][:sums], rest[len(rest) - sums :]
        tile = 32
        lines = prepare(*[ref[...] for ref in rest[: len(whole)]])
        for ref in sums_held:
            ref[...] = jnp.zeros_like(ref)

        def some(i, carry):
            inside = pl.ds(pl.multiple_of(i * tile, tile), tile)
            at = pl.ds(pl.multiple_of(pl.program_id(0) * half + i * tile, tile), tile)
            values = kernel([ref[at, :].astype(F32) for ref in held], *lines)
            for ref, value in zip(outs, values):
                ref[inside, :] = value.astype(ref.dtype)
            for ref, value in zip(sums_held, values[len(outs) :]):
                ref[...] += jnp.sum(value.reshape(tile // 8, 8, width), axis=0)
            return carry

        lax.fori_loop(0, half // tile, some, 0, unroll=2)
        for ref, held_ref in zip(totals, sums_held):
            add_column(ref, held_ref[...])

    line = pl.BlockSpec((1, width), lambda i, o: (0, 0))
    return call(
        name,
        run,
        (*[v for v, _ in given], *whole),
        (halves,),
        [pl.BlockSpec(memory_space=pl.ANY) for _ in given] + [line for _ in whole],
        [pl.BlockSpec((half, width), lambda i, o: (i, 0)) for _ in out_kinds]
        + [line for _ in range(sums)],
        [shape((share, width), kind) for kind in out_kinds]
        + [shape((1, width), F32) for _ in range(sums)],
        scratch=[pltpu.VMEM((8, width), F32) for _ in range(sums)]
        + [pltpu.VMEM((share, width), v.dtype) for v, _ in given]
        + [pltpu.SemaphoreType.DMA((halves, count))],
        prefetch=(order,),
        flops=20 * share * width,
    )


def sum_of(values):
    total = values[0]
    for value in values[1:]:
        total = total + value
    return total


def add_column(ref, values):
    part = jnp.sum(values, axis=0, keepdims=True)

    @pl.when(pl.program_id(0) == 0)
    def _():
        ref[...] = part

    @pl.when(pl.program_id(0) > 0)
    def _():
        ref[...] += part


def scale_first(squares, magnitude, *rest):
    norm = jnp.sqrt(squares)
    return (magnitude / norm, norm / magnitude, *rest)


def hidden_kernel(given, scale, inverse, gain):
    hidden = given[0] + sum_of(given[1:]) * scale
    return hidden, hidden * rms_rows(hidden) * gain


def mixed_kernel(given, scale, inverse):
    return (given[0] + sum_of(given[1:]) * scale,)


def norm_back(grad_normed, values, gain):
    factor = rms_rows(values)
    scaled = grad_normed * gain
    inner = jnp.mean(scaled * values, axis=1, keepdims=True)
    back = factor * scaled - values * (factor * factor * factor * inner)
    return back, grad_normed * values * factor


def hidden_back_kernel(given, scale, inverse, gain):
    cot, token, hidden = given[:3]
    back, gain_terms = norm_back(sum_of(given[3:]), hidden, gain)
    grad = cot + back
    return grad, grad * scale, grad * ((hidden - token) * inverse), gain_terms


def token_back_kernel(given, gain):
    back, gain_terms = norm_back(sum_of(given[2:]), given[0], gain)
    return given[1] + back, gain_terms


def shrink_back_kernel(places, order_ref, *refs):
    cots, (low_ref, squares_ref, magnitude_ref, product_ref, grad_ref, rows_all) = refs[:places], refs[places:]
    scale = magnitude_ref[0] / jnp.sqrt(squares_ref[0])
    share = cots[0].shape[0]
    for place, cot_ref in enumerate(cots):
        grad = (cot_ref[...].astype(F32) * scale).astype(LOW)
        grad_ref[place] = grad
        rows_all[place * share : (place + 1) * share, :] = grad
    result = dot(rows_all[...], low_ref[0], NT).astype(LOW)
    for place in range(places):
        product_ref[place] = result[place * share : (place + 1) * share]


def shrink_back(order, cotangent, low, squares, magnitude, groups):
    rows, width = cotangent.shape
    share, inner = rows // groups, low.shape[1]
    places = CORES
    line = pl.BlockSpec((1, 1, width), lambda j, o: (0, 0, 0))
    cot = lambda place: pl.BlockSpec((share, width), lambda j, o: (o[places * j + place], 0))
    return call(
        "shrink_back",
        functools.partial(shrink_back_kernel, places),
        (*[cotangent] * places, low, squares, magnitude),
        (groups // places,),
        [cot(place) for place in range(places)]
        + [pl.BlockSpec((1, inner, width), lambda j, o: (0, 0, 0)), line, line],
        [
            pl.BlockSpec((places, share, inner), lambda j, o: (j, 0, 0)),
            pl.BlockSpec((places, share, width), lambda j, o: (j, 0, 0)),
        ],
        [shape((groups, share, inner), LOW), shape((groups, share, width), LOW)],
        scratch=[pltpu.VMEM((places * share, width), LOW)],
        prefetch=(order,),
        flops=2 * rows * width * inner,
    )


def expand_kernel(step, first, last, n_totals, *refs):
    mine_ref, low_ref, grad_ref, squares_ref, magnitude_ref = refs[:5]
    refs = list(refs[5:])
    left_ref = refs.pop(0) if first else None
    right_ref = refs.pop(0) if last else None
    before = [refs.pop(0) for _ in range(n_totals)]
    product_ref, back_ref, rows_ref, total_ref, joined_ref = refs[:5]
    refs = refs[5:]
    across_ref = refs.pop(0) if first else None
    extra_ref = refs.pop(0) if last else None
    rows_all, low_all, grad_all, product_all, back_all, sent, got, in_sems, out_sems, send_sems, recv_sems = refs
    share, depth = mine_ref.shape
    sibling = sibling_id()
    greet([sibling])
    both = CORES * share
    width, ff = low_ref.shape[2], magnitude_ref.shape[1]
    tile = 256
    cuts = [slice(at, at + tile) for at in range(0, width, tile)]

    mine_copy = pltpu.make_async_copy(mine_ref, rows_all.at[pl.ds(share, share), :], in_sems.at[0])
    other_copy = remote(
        mine_ref,
        rows_all.at[pl.ds(0, share), :],
        send_sems.at[sent.shape[0]],
        recv_sems.at[sent.shape[0]],
        sibling,
    )
    tile_copies = []
    for n, cut in enumerate(cuts):
        lanes = pl.ds(cut.start, tile)
        tile_copies.append(
            [
                pltpu.make_async_copy(
                    low_ref.at[:, :, lanes], low_all.at[:, :, lanes], in_sems.at[2 + 2 * n]
                ),
                pltpu.make_async_copy(
                    grad_ref.at[pl.ds(CORES * step, CORES), :, lanes],
                    grad_all.at[:, :, lanes],
                    in_sems.at[3 + 2 * n],
                ),
            ]
        )
    mine_copy.start()
    for copy in tile_copies[0]:
        copy.start()
    greeted(1)
    other_copy.start()
    for copies in tile_copies[1:]:
        for copy in copies:
            copy.start()
    if first:
        rank = across_ref.shape[1]
        for m in range(2):
            rows_all[both + m * rank : both + (m + 1) * rank, :] = left_ref[m].astype(LOW)
    mine_copy.wait()
    other_copy.wait_recv()
    out_copies = [
        pltpu.make_async_copy(rows_all.at[pl.ds(0, both), :], rows_ref, out_sems.at[2 * len(cuts)])
    ]
    out_copies[0].start()
    lane = lax.broadcasted_iota(jnp.int32, (1, tile), 1)
    for n, cut in enumerate(cuts):
        for copy in tile_copies[n]:
            copy.wait()
        size = min(tile, ff - cut.start)
        pre = [dot(rows_all[...], low_all[m, :, cut]) for m in range(2)]
        if first:
            for m in range(2):
                rows = slice(both + m * rank, both + (m + 1) * rank)
                across_ref[m, :, cut.start : cut.start + size] = pre[m][rows, :size]
        magnitude, squares, scale = [], [], []
        for m in range(2):
            given = magnitude_ref[m : m + 1, cut.start : cut.start + size]
            if size < tile:
                given = jnp.concatenate([given, jnp.zeros((1, tile - size), F32)], axis=1)
            magnitude.append(given)
            squares.append(squares_ref[m, :, cut])
            scale.append(given / jnp.sqrt(squares[m]))
        sums = [jnp.zeros((1, tile), F32) for _ in range(2)]
        at = [slice(m * width + cut.start, m * width + cut.stop) for m in range(2)]
        for place in range(CORES):
            rows = slice(place * share, (place + 1) * share)
            gate_pre, up_pre = pre[0][rows], pre[1][rows]
            gate, up = gate_pre * scale[0], up_pre * scale[1]
            sigmoid = 0.5 + 0.5 * jnp.tanh(0.5 * gate)
            active = gate * sigmoid
            product_all[rows, cut] = (active * up).astype(LOW)
            upper = grad_all[place, :, cut].astype(F32)
            grad_up = upper * active
            grad_gate = upper * up * sigmoid * (1.0 + gate * (1.0 - sigmoid))
            sums[0] += jnp.sum(grad_gate * gate_pre, axis=0, keepdims=True)
            sums[1] += jnp.sum(grad_up * up_pre, axis=0, keepdims=True)
            back_all[rows, at[0]] = (grad_gate * scale[0]).astype(LOW)
            back_all[rows, at[1]] = (grad_up * scale[1]).astype(LOW)
        for m in range(2):
            total_ref[m, :, cut] = sums[m]
        if last:
            rank = extra_ref.shape[1]
            for m in range(2):
                total = sums[m]
                for ref in before:
                    total = total + ref[m, :, cut]
                right = right_ref[m, :, cut.start : cut.start + size]
                if size < tile:
                    spare = jnp.zeros((rank, tile - size), F32)
                    right = jnp.concatenate([right, spare], axis=1)
                weighted = right * norm_weight(total, squares[m], magnitude[m])
                rows = slice(both + m * rank, both + (m + 1) * rank)
                back_all[rows, at[m]] = weighted.astype(LOW)
                back_all[rows, at[1 - m]] = jnp.zeros((rank, tile), LOW)
    for m in range(2):
        lanes = pl.ds(m * width, width)
        copy = pltpu.make_async_copy(
            back_all.at[pl.ds(0, both), lanes], back_ref.at[m], out_sems.at[m]
        )
        copy.start()
        out_copies.append(copy)
    copy = pltpu.make_async_copy(product_all, product_ref, out_sems.at[2])
    copy.start()
    out_copies.append(copy)
    chunk = sent.shape[2]
    copies = [
        remote(sent.at[n], got.at[n], send_sems.at[n], recv_sems.at[n], sibling)
        for n in range(depth // chunk)
    ]

    def add(n):
        columns = slice(n * chunk, (n + 1) * chunk)
        copies[n].wait_recv()
        total = joined_ref[:, columns].astype(F32) + got[n].astype(F32)
        joined_ref[:, columns] = total.astype(LOW)

    for n in range(depth // chunk):
        columns = slice(n * chunk, (n + 1) * chunk)
        result = dot(back_all[:, :width], low_all[0, columns, :], NT)
        result = result + dot(back_all[:, width:], low_all[1, columns, :], NT)
        sent[n] = result[:share].astype(LOW)
        joined_ref[:, columns] = result[share:both].astype(LOW)
        copies[n].start()
        if n > 0:
            add(n - 1)
        if last:
            for m in range(2):
                extra_ref[m, :, columns] = result[both + m * rank : both + (m + 1) * rank]
    add(len(copies) - 1)
    for copy in out_copies:
        copy.wait()
    for copy in [other_copy, *copies]:
        copy.wait_send()


def expand(identity, mine, low, squares, magnitude, grad_product, step, left=None, right=None, before=()):
    share, depth = mine.shape
    width = low.shape[2]
    first, last = left is not None, right is not None
    rows = CORES * share
    hbm = pl.BlockSpec(memory_space=pl.ANY)
    fixed = lambda dims: pl.BlockSpec(tuple(dims), lambda i: (0,) * len(dims))
    operands = [mine, low, grad_product, squares, magnitude]
    in_specs = [hbm, hbm, hbm, fixed(squares.shape), fixed(magnitude.shape)]
    out_shape = [
        shape((rows, width), LOW),
        shape((2, rows, width), LOW),
        shape((rows, depth), LOW),
        shape((2, 1, width), F32),
        shape((share, depth), LOW),
    ]
    out_specs = [hbm, hbm, hbm] + [fixed(v.shape) for v in out_shape[3:]]
    extra_in = extra_out = 0
    if first:
        rank = left.shape[1]
        extra_in = 2 * rank
        operands.append(left)
        in_specs.append(fixed(left.shape))
        out_shape.append(shape((2, rank, magnitude.shape[1]), F32))
        out_specs.append(fixed(out_shape[-1].shape))
    if last:
        rank = right.shape[1]
        extra_out = 2 * rank
        operands += [right, *before]
        in_specs += [fixed(v.shape) for v in (right, *before)]
        out_shape.append(shape((2, rank, depth), F32))
        out_specs.append(fixed(out_shape[-1].shape))
    tiles, chunk = width // 256, tile_of(depth, 512)
    return call(
        "expand",
        functools.partial(expand_kernel, step, first, last, len(before)),
        tuple(operands),
        (1,),
        in_specs,
        out_specs,
        out_shape,
        scratch=[
            pltpu.VMEM((rows + extra_in, depth), LOW),
            pltpu.VMEM(low.shape, LOW),
            pltpu.VMEM((CORES, share, width), LOW),
            pltpu.VMEM((rows, width), LOW),
            pltpu.VMEM((rows + extra_out, 2 * width), LOW),
            pltpu.VMEM((depth // chunk, share, chunk), LOW),
            pltpu.VMEM((depth // chunk, share, chunk), LOW),
            pltpu.SemaphoreType.DMA((2 + 2 * tiles,)),
            pltpu.SemaphoreType.DMA((2 * tiles + 1,)),
            pltpu.SemaphoreType.DMA((depth // chunk + 1,)),
            pltpu.SemaphoreType.DMA((depth // chunk + 1,)),
        ],
        flops=8 * rows * depth * width,
        identity=identity,
    )


def adapter_kernel(plan, n_inputs, n_grads, corrections, n_before, order_ref, *refs):
    count = n_inputs + n_grads
    sources, held, sems = refs[:count], refs[-count - 1 : -1], refs[-1]
    left_ref, right_ref = refs[count : count + 2]
    *corrected, left_out, right_out = refs[count + 2 : -count - 1]
    members, rank, width = right_ref.shape
    chunks = list(plan(order_ref, held[:n_inputs], held[n_inputs:]))
    copies = []
    for parts, _, _ in chunks:
        copies.append([])
        for which, index in parts:
            copy = pltpu.make_async_copy(
                sources[which].at[index],
                held[which].at[index],
                sems.at[sum(len(c) for c in copies)],
            )
            copy.start()
            copies[-1].append(copy)
    left_rows = jnp.concatenate([split_rows(left_ref[m]) for m in range(members)], axis=0)
    right_rows = [split_rows(right_ref[m]) for m in range(members)]
    before, corrected = corrected[:n_before], corrected[n_before:]
    for out, ref in zip((left_out, right_out), before or (None, None)):
        out[...] = jnp.zeros_like(out) if ref is None else ref[...]
    for waits, (_, taken_of, grads_of) in zip(copies, chunks):
        for copy in waits:
            copy.wait()
        taken = taken_of()
        across = dot(left_rows, taken, NT)
        downs = []
        for m in range(members):
            grad = grads_of(m)
            mine = split_rows(fold(across[2 * rank * m : 2 * rank * (m + 1)]))
            right_out[m] += fold(dot(mine, grad))
            downs.append(split_rows(fold(dot(right_rows[m], grad, NT))))
        left = dot(jnp.concatenate(downs, axis=0), taken)
        for m in range(members):
            left_out[m] += fold(left[2 * rank * m : 2 * rank * (m + 1)])
    if corrections:
        correct(corrections, right_ref, left_out, right_out, left_out, right_out, *corrected)


def correct(n_totals, right_ref, left_in, right_in, left_out, right_out, *refs):
    back_ref, across_ref, squares_ref, magnitude_ref = refs[:4]
    totals, magnitude_out = refs[4 : 4 + n_totals], refs[4 + n_totals]
    members, rank, width = right_ref.shape
    total = sum_refs(totals)[:, :, :width]
    squares = squares_ref[:, :, :width]
    magnitude_out[...] = total / jnp.sqrt(squares)
    for m in range(members):
        weight = norm_weight(total[m], squares[m], magnitude_ref[m : m + 1])
        if back_ref.dtype == LOW:
            low = back_ref[m, : left_in.shape[2], :]
            back = fold(dot(split_rows(right_ref[m] * weight), low, NT))
        else:
            back = back_ref[m]
        left_out[m] = ADAPT_SCALE * (left_in[m] - back)
        right_out[m] = ADAPT_SCALE * (right_in[m] - across_ref[m][:, :width] * weight)


def correct_kernel(n_totals, order_ref, right_ref, left_in, right_in, *refs):
    *rest, left_out, right_out = refs
    correct(n_totals, right_ref, left_in, right_in, left_out, right_out, *rest)


def correct_kernel(n_totals, right_ref, left_in, right_in, *refs):
    *rest, left_out, right_out = refs
    correct(n_totals, right_ref, left_in, right_in, left_out, right_out, *rest)


def corrected(name, sums, right, correction):
    members, rank, width = right.shape
    *given, totals = correction
    operands = (right, *sums, *given, *totals)
    outs = [(members, 1, width), sums[0].shape, sums[1].shape]
    full = lambda dims: pl.BlockSpec(tuple(dims), lambda i: (0,) * len(dims))
    return call(
        name,
        functools.partial(correct_kernel, len(totals)),
        operands,
        (1,),
        [full(v.shape) for v in operands],
        [full(dims) for dims in outs],
        [shape(dims, F32) for dims in outs],
        flops=sum(v.size for v in operands) * 64,
    )


def adapter(name, order, plan, inputs, grads, left, right, correction=None, before=()):
    members, rank, width = right.shape
    moved, fixed, n_totals = [*inputs, *grads], [left, right, *before], 0
    outs = [(members, rank, left.shape[2]), (members, rank, width)]
    if correction is not None:
        *given, totals = correction
        n_totals = len(totals)
        fixed += [*given, *totals]
        outs = [(members, 1, width)] + outs
    full = lambda dims: pl.BlockSpec(tuple(dims), lambda i, o: (0,) * len(dims))
    kernel = functools.partial(
        adapter_kernel, plan, len(inputs), len(grads), n_totals, len(before)
    )
    return call(
        name,
        kernel,
        (*moved, *fixed),
        (1,),
        [pl.BlockSpec(memory_space=pl.ANY) for _ in moved] + [full(v.shape) for v in fixed],
        [full(dims) for dims in outs],
        [shape(dims, F32) for dims in outs],
        scratch=[pltpu.VMEM(v.shape, v.dtype) for v in moved] + [pltpu.SemaphoreType.DMA((32,))],
        prefetch=(order,),
        flops=sum(v.size for v in moved) * 64,
    )


def copy_kernel(count, *refs):
    for source, target in zip(refs[:count], refs[count:]):
        target[...] = source[...]


def copy_out(arrays):
    vmem = pl.BlockSpec(memory_space=pltpu.VMEM)
    full = lambda v: pl.BlockSpec(v.shape, lambda i: (0,) * v.ndim)
    return call(
        "copy_out",
        functools.partial(copy_kernel, len(arrays)),
        tuple(arrays),
        (1,),
        [vmem for _ in arrays],
        [full(v) for v in arrays],
        [shape(v.shape, F32) for v in arrays],
        mib=16,
    )


GRAIN = 16


def pieces_of(width):
    return [(at, min(128, width - at)) for at in range(0, width, 128)]


def cells_of(blocks, lines, parts):
    cells, rows = [], []
    for n, block in enumerate(blocks):
        for m in range(block.shape[0]):
            for at, size in pieces_of(block.shape[2] // parts):
                cells.append((n, m, at, size))
    for n, line in enumerate(lines):
        for m in range(line.shape[0]):
            for at, size in pieces_of(line.shape[2] // parts):
                rows.append((n, m, at, size))
    return cells, rows


def pack(blocks, lines, wide_ref, part, parts, cells, rows):
    for i, (n, m, at, size) in enumerate(cells):
        start = part * (blocks[n].shape[2] // parts) + at
        wide_ref[part, i, :, :size] = blocks[n][m, :, start : start + size]
    for i, (n, m, at, size) in enumerate(rows):
        start = part * (lines[n].shape[2] // parts) + at
        cell, row = len(cells) + i // GRAIN, i % GRAIN
        wide_ref[part, cell, row : row + 1, :size] = lines[n][m, :, start : start + size]


def unpack(full_ref, blocks, lines, part, parts, cells, rows):
    for i, (n, m, at, size) in enumerate(cells):
        start = part * (blocks[n].shape[2] // parts) + at
        blocks[n][m, :, start : start + size] = full_ref[part, i].astype(F32)[:, :size]
    for i, (n, m, at, size) in enumerate(rows):
        start = part * (lines[n].shape[2] // parts) + at
        cell, row = len(cells) + i // GRAIN, i % GRAIN
        values = full_ref[part, cell].astype(F32)
        lines[n][m, :, start : start + size] = values[row : row + 1, :size]


def reduce_kernel(groups, lines, counts, *refs):
    n_all, n_all_lines, n_dp, n_dp_lines = counts
    count = sum(counts)
    taken, given, scratch = refs[:count], refs[count : 2 * count], refs[2 * count :]
    ends = [n_all, n_all + n_all_lines, n_all + n_all_lines + n_dp]
    parted = lambda v: (v[: ends[0]], v[ends[0] : ends[1]], v[ends[1] : ends[2]], v[ends[2] :])
    all_in, all_lines_in, dp_in, dp_lines_in = parted(taken)
    all_out, all_lines_out, dp_out, dp_lines_out = parted(given)
    (
        all_ref,
        line_ref,
        all_low,
        line_low,
        all_got,
        part,
        part_low,
        part_got,
        line_got,
        all_full,
        line_full,
        *sems,
    ) = scratch
    me, row = lax.axis_index("mp"), lax.axis_index("dp")
    piece, line_piece = part.shape[0] // lines, line_ref.shape[1] // lines
    mp_peer = [lax.rem(me + k, groups) for k in range(groups)]
    dp_peer = [lax.rem(row + k, lines) for k in range(lines)]
    barrier = pltpu.get_barrier_semaphore()
    for k in range(1, groups):
        pl.semaphore_signal(barrier, 1, device_id={"mp": mp_peer[k]}, device_id_type=MESH_IDS)
    for k in range(1, lines):
        pl.semaphore_signal(barrier, 1, device_id={"dp": dp_peer[k]}, device_id_type=MESH_IDS)
    all_cells = cells_of(all_in, all_lines_in, groups)
    dp_cells = cells_of(dp_in, dp_lines_in, 1)
    all_ref[...] = jnp.zeros_like(all_ref)
    line_ref[...] = jnp.zeros_like(line_ref)
    for q in range(groups):
        pack(all_in, all_lines_in, all_ref, q, groups, *all_cells)
    pack(dp_in, dp_lines_in, line_ref, 0, 1, *dp_cells)
    all_low[...] = all_ref[...].astype(LOW)
    line_low[...] = line_ref[...].astype(LOW)
    pl.semaphore_wait(barrier, groups + lines - 2)

    def send(source, target, stage, k, axis, peer):
        copy = pltpu.make_async_remote_copy(
            src_ref=source,
            dst_ref=target,
            send_sem=sems[2 * stage].at[k],
            recv_sem=sems[2 * stage + 1].at[k],
            device_id={axis: peer},
            device_id_type=MESH_IDS,
        )
        copy.start()
        return copy

    over_mp = [
        send(all_low.at[mp_peer[k]], all_got.at[k], 0, k, "mp", mp_peer[k])
        for k in range(1, groups)
    ]
    over_dp = [
        send(
            line_low.at[0, pl.ds(dp_peer[k] * line_piece, line_piece)],
            line_got.at[k],
            1,
            k,
            "dp",
            dp_peer[k],
        )
        for k in range(1, lines)
    ]
    total = all_ref[me]
    for k, copy in enumerate(over_mp, 1):
        copy.wait_recv()
        total = total + all_got[k].astype(F32)
    part[...] = total
    part_low[...] = total.astype(LOW)
    part_dp = [
        send(part_low.at[pl.ds(dp_peer[k] * piece, piece)], part_got.at[k], 2, k, "dp", dp_peer[k])
        for k in range(1, lines)
    ]
    held = pl.ds(row * piece, piece)
    total = part[held]
    for k, copy in enumerate(part_dp, 1):
        copy.wait_recv()
        total = total + part_got[k].astype(F32)
    all_full[me, held] = total.astype(LOW)
    part_back = [
        send(all_full.at[me, held], all_full.at[me, held], 4, k, "dp", dp_peer[k])
        for k in range(1, lines)
    ]
    mine = pl.ds(row * line_piece, line_piece)
    total = line_ref[0, mine]
    for k, copy in enumerate(over_dp, 1):
        copy.wait_recv()
        total = total + line_got[k].astype(F32)
    line_full[0, mine] = total.astype(LOW)
    line_back = [
        send(line_full.at[0, mine], line_full.at[0, mine], 3, k, "dp", dp_peer[k])
        for k in range(1, lines)
    ]
    for copy in part_back:
        copy.wait_recv()
    all_back = [
        send(all_full.at[me], all_full.at[me], 5, k, "mp", mp_peer[k]) for k in range(1, groups)
    ]
    for copy in line_back:
        copy.wait_recv()
    unpack(line_full, dp_out, dp_lines_out, 0, 1, *dp_cells)
    for copy in all_back:
        copy.wait_recv()
    for q in range(groups):
        unpack(all_full, all_out, all_lines_out, q, groups, *all_cells)
    for copy in over_mp + over_dp + part_dp + line_back + part_back + all_back:
        copy.wait_send()


def reduce_devices(name, identity, over_all, over_all_lines, over_dp, over_dp_lines):
    groups, lines = lax.axis_size("mp"), lax.axis_size("dp")

    def size_of(blocks, rows, parts):
        cells, lines_in = cells_of(blocks, rows, parts)
        size = len(cells) + -(-len(lines_in) // GRAIN)
        return -(-size // lines) * lines

    count, line_count = size_of(over_all, over_all_lines, groups), size_of(over_dp, over_dp_lines, 1)
    operands = (*over_all, *over_all_lines, *over_dp, *over_dp_lines)
    counts = (len(over_all), len(over_all_lines), len(over_dp), len(over_dp_lines))
    vmem = pl.BlockSpec(memory_space=pltpu.VMEM)
    tail = (GRAIN, 128)
    sizes = (groups, lines, lines, lines, lines, groups)
    every, line = (groups, count) + tail, (1, line_count) + tail
    results = pl.pallas_call(
        functools.partial(reduce_kernel, groups, lines, counts),
        name=name,
        out_shape=[shape(v.shape, F32) for v in operands],
        in_specs=[vmem for _ in operands],
        out_specs=[vmem for _ in operands],
        scratch_shapes=[
            pltpu.VMEM(every, F32),
            pltpu.VMEM(line, F32),
            pltpu.VMEM(every, LOW),
            pltpu.VMEM(line, LOW),
            pltpu.VMEM(every, LOW),
            pltpu.VMEM((count,) + tail, F32),
            pltpu.VMEM((count,) + tail, LOW),
            pltpu.VMEM((lines, count // lines) + tail, LOW),
            pltpu.VMEM((lines, line_count // lines) + tail, LOW),
            pltpu.VMEM(every, LOW),
            pltpu.VMEM(line, LOW),
        ]
        + [pltpu.SemaphoreType.DMA((n,)) for n in sizes for _ in range(2)],
        compiler_params=pltpu.CompilerParams(
            collective_id=identity, has_side_effects=True, vmem_limit_bytes=32 * 2**20
        ),
        cost_estimate=pl.CostEstimate(flops=1000, bytes_accessed=2**20, transcendentals=0),
    )(*operands)
    return copy_out(results)


def first_places(segment):
    length = segment.shape[0]
    places = lax.broadcasted_iota(jnp.int32, (length, length), 0)
    others = lax.broadcasted_iota(jnp.int32, (length, length), 1)
    visible = (segment[:, None] == segment[None, :]) & (others <= places)
    offset = jnp.sum(visible.astype(F32), axis=1) - 1.0
    return (jnp.arange(length, dtype=jnp.int32) - offset.astype(jnp.int32))[:, None]


def body(
    tokens,
    cotangent,
    segment_ids,
    attend_gain,
    expand_gain,
    heads_base,
    heads_left,
    heads_right,
    heads_magnitude,
    output_base,
    output_left,
    output_right,
    output_magnitude,
    expand_base,
    expand_left,
    expand_right,
    expand_magnitude,
    shrink_base,
    shrink_left,
    shrink_right,
    shrink_magnitude,
):
    groups = lax.axis_size("mp")
    chips = groups // CORES
    index = lax.axis_index("mp")
    chip, core = index // CORES, index % CORES
    rows, width = tokens.shape
    share = rows // groups
    local_heads, ff = heads_base.shape[2], expand_base.shape[2]
    ff_wide = padded(ff)
    device = jnp.arange(groups, dtype=jnp.int32)
    order = jnp.concatenate(
        [
            (chip + device // CORES) % chips * CORES + (core + 1 + device) % CORES,
            (device // CORES + chips - chip) % chips * CORES + (device + CORES - core + 1) % CORES,
        ]
    ).astype(jnp.int32)

    def tie(*values):
        return lax.optimization_barrier(values)

    def sibling(values):
        return lax.ppermute(
            values, "mp", [(i, i // CORES * CORES + (i + 1) % CORES) for i in range(groups)]
        )

    def to_chip(values, step):
        return lax.ppermute(
            values,
            "mp",
            [((i, ((i // CORES + step) % chips) * CORES + i % CORES)) for i in range(groups)],
        )

    def mp_sum(values):
        values = values + sibling(values)
        total = values
        for step in range(1, chips):
            total = total + to_chip(values, step)
        return total

    def join(pair):
        return (pair[1].astype(F32) + sibling(pair[0]).astype(F32)).astype(LOW)

    def chip_pairs(places):
        return [places[CORES * step : CORES * (step + 1)] for step in range(chips)]

    def arrive(own):
        return [to_chip(own, chips - step) for step in range(1, chips)]

    def pairs_of(own, near_sibling, arrived):
        return [(near_sibling, own)] + [(sibling(piece), piece) for piece in arrived]

    def in_pairs(order_ref, inputs, grads):
        for step, (taken, grad) in enumerate(zip(inputs, grads)):
            yield (
                [(step, ...), (chips + step, ...)],
                lambda taken=taken: taken[...],
                lambda m, grad=grad: grad[m, :, :ff],
            )

    def in_shrink(order_ref, inputs, grads):
        for step, taken in enumerate(inputs):
            at = slice(CORES * step, CORES * (step + 1))
            yield (
                [(step, ...), (chips, pl.ds(CORES * step, CORES))],
                lambda taken=taken: taken[:, :ff],
                lambda m, at=at: grads[0][at].reshape(-1, grads[0].shape[-1]),
            )

    def in_output(start):
        def plan(order_ref, inputs, grads):
            for n, grad in enumerate(grads):
                yield (
                    [(0, (0, start + n)), (1 + n, ...)],
                    lambda place=start + n: inputs[0][0, place],
                    lambda m, grad=grad: grad[...],
                )

        return plan

    def in_heads(order_ref, inputs, grads):
        for place in range(groups):
            at = pl.multiple_of(order_ref[place] * share, share)
            rows = pl.ds(place * share, share)
            yield (
                [(0, pl.ds(at, share)), (1, (slice(None), rows))],
                lambda at=at: inputs[0][pl.ds(at, share), :],
                lambda m, rows=rows: grads[0][m, rows, :],
            )

    heads_rows, output_rows = turned(heads_left), turned(output_left[None])
    expand_rows, shrink_rows = turned(expand_left), turned(shrink_left[None])
    heads_mag, output_mag = heads_magnitude, output_magnitude[None]
    expand_mag, shrink_mag = expand_magnitude, shrink_magnitude[None]
    attend_line, expand_line = attend_gain[None], expand_gain[None]

    output_low, shrink_low, squares_part = merge_pair(
        [(output_base, output_rows[0], output_right), (shrink_base, shrink_rows[0], shrink_right)]
    )
    output_low, shrink_low = output_low[None], shrink_low[None]
    first = first_places(segment_ids.reshape(-1))
    normed, heads_low, post, heads_sq, heads_across, cos_table, sine_table, squares = project_heads(
        tokens, attend_line, heads_base, heads_rows, heads_right, heads_mag, first, squares_part, groups
    )
    heads_out = attend(order, groups, post, first)
    output_sq, shrink_sq = squares[None, :1], squares[None, 1:]
    heads_parts = heads_out.reshape(1, groups, share, local_heads)
    joined, output_across = product(
        "output_product", 3, heads_parts, output_low, NN, left=output_rows
    )
    joined, expand_right_tied = tie(joined, expand_right)
    output_parts = [joined[0]] + [to_chip(joined[step], step) for step in range(1, chips)]
    expand_low, expand_sq = merge(
        expand_base, expand_rows, expand_right_tied, 1024, expand_base.shape[2]
    )
    grad_product, shrink_grad = shrink_back(
        order, cotangent, shrink_low, shrink_sq, shrink_mag[None], groups
    )
    output_parts, expand_low, grad_product = tie(output_parts, expand_low, grad_product)
    hidden, normed_own = row_call(
        "hidden",
        hidden_kernel,
        order,
        [(tokens, True)] + [(part, False) for part in output_parts],
        (output_sq[0], output_mag, expand_line),
        (F32, LOW),
        0,
        scale_first,
    )

    def feed(mine, step, **extra):
        return expand(
            4 + step, mine, expand_low, expand_sq, expand_mag, grad_product, step, **extra
        )

    arrived = arrive(normed_own)
    fed = [feed(normed_own, 0, left=expand_rows)]
    arrived, fed = tie(arrived, fed)
    fed = list(fed)
    for step in range(1, chips):
        extra = {}
        if step == chips - 1:
            extra = {"right": expand_right, "before": [f[3] for f in fed]}
        fed.append(feed(arrived[step - 1], step, **extra))
    expand_totals = [f[3] for f in fed]
    joined, shrink_rows_tied = tie([f[4] for f in fed], shrink_rows)
    mid_parts = [joined[0]] + [to_chip(joined[step], step) for step in range(1, chips)]
    shrink_places, shrink_total, shrink_across = shrink_product(
        order, [f[0] for f in fed], shrink_low, shrink_rows_tied, cotangent
    )
    shrink_pairs = chip_pairs(shrink_places)
    expand_adapter = adapter(
        "expand_adapter",
        order,
        in_pairs,
        [f[2] for f in fed],
        [f[1] for f in fed],
        expand_rows,
        expand_right,
        (fed[-1][5], fed[0][5], expand_sq, expand_mag, expand_totals),
    )
    mid_parts, shrink_pairs, expand_adapter = tie(mid_parts, shrink_pairs, expand_adapter)
    grad_hidden, output_grad_own, output_total, expand_gain_part = row_call(
        "hidden_back",
        hidden_back_kernel,
        order,
        [(cotangent, True), (tokens, True), (hidden, False)]
        + [(part, False) for part in mid_parts],
        (output_sq[0], output_mag, expand_line),
        (F32, LOW),
        2,
        scale_first,
    )
    arrived, near_sibling = arrive(output_grad_own), sibling(output_grad_own)
    shrink_joined = [join(pair) for pair in shrink_pairs[1:]]
    shrink_joined, shrink_rows_tied = tie(shrink_joined, shrink_rows)
    shrink_sums = adapter(
        "shrink_adapter",
        order,
        in_shrink,
        [f[0] for f in fed],
        [shrink_grad],
        shrink_rows_tied,
        shrink_right[None],
    )
    output_sums = adapter(
        "output_near_adapter",
        order,
        in_output(0),
        [heads_parts],
        [near_sibling, output_grad_own],
        output_rows,
        output_right[None],
    )
    arrived, near_sibling, shrink_joined, shrink_sums, output_sums = tie(
        arrived, near_sibling, shrink_joined, shrink_sums, output_sums
    )
    output_grad = [
        piece for pair in pairs_of(output_grad_own, near_sibling, arrived) for piece in pair
    ]
    shrink_parts = [shrink_pairs[0][1], sibling(shrink_pairs[0][0])] + [
        to_chip(values, step) for step, values in enumerate(shrink_joined, 1)
    ]
    heads_grads, heads_total = attend_back(
        order,
        groups,
        post,
        first,
        cos_table,
        sine_table,
        heads_mag,
        heads_sq,
        output_low,
        output_grad,
    )
    grad_parts = heads_grads.reshape(3, groups, share, local_heads)
    joined, both_totals, token_extra = product(
        "normed_product",
        20,
        grad_parts,
        heads_low,
        NT,
        correction=(heads_right, heads_sq, heads_mag, [heads_total]),
        lines=(output_total, shrink_total),
    )
    joined, shrink_parts, heads_rows_tied, output_rows_tied = tie(
        joined, shrink_parts, heads_rows, output_rows
    )
    output_total, shrink_total = both_totals[:1], both_totals[1:]
    token_parts = [joined[0]] + [to_chip(joined[step], step) for step in range(1, chips)]
    output_adapter = adapter(
        "output_far_adapter",
        order,
        in_output(CORES),
        [heads_parts],
        output_grad[CORES:],
        output_rows_tied,
        output_right[None],
        (output_low, output_across, output_sq, output_mag, [output_total[None]]),
        output_sums,
    )
    shrink_adapter = corrected(
        "shrink_correct",
        shrink_sums,
        shrink_right[None],
        (shrink_low, shrink_across, shrink_sq, shrink_mag, [shrink_total[None]]),
    )
    heads_adapter = adapter(
        "heads_adapter",
        order,
        in_heads,
        [normed],
        [heads_grads],
        heads_rows_tied,
        heads_right,
        (token_extra, heads_across, heads_sq, heads_mag, [heads_total]),
    )
    (mixed,) = row_call(
        "mixed",
        mixed_kernel,
        order,
        [(hidden, False)] + [(part, False) for part in shrink_parts],
        (shrink_sq[0], shrink_mag),
        (LOW,),
        0,
        scale_first,
    )
    token_parts, output_adapter, shrink_adapter, heads_adapter, mixed = tie(
        token_parts, output_adapter, shrink_adapter, heads_adapter, mixed
    )
    grad_tokens, attend_gain_part = row_call(
        "token_back",
        token_back_kernel,
        order,
        [(tokens, True), (grad_hidden, False)] + [(part, False) for part in token_parts],
        (attend_line,),
        (F32,),
        1,
        lambda gain: (gain,),
    )
    (
        expand_left_grad,
        shrink_right_grad,
        heads_left_grad,
        output_right_grad,
        expand_gain_grad,
        attend_gain_grad,
        expand_right_grad,
        shrink_left_grad,
        heads_right_grad,
        output_left_grad,
        expand_mag_grad,
        shrink_mag_grad,
        heads_mag_grad,
        output_mag_grad,
    ) = reduce_devices(
        "reduce_gradients",
        1,
        [expand_adapter[1], shrink_adapter[2], heads_adapter[1], output_adapter[2]],
        [expand_gain_part[None], attend_gain_part[None]],
        [expand_adapter[2], shrink_adapter[1], heads_adapter[2], output_adapter[1]],
        [expand_adapter[0], shrink_adapter[0], heads_adapter[0], output_adapter[0]],
    )
    return (
        mixed,
        grad_tokens,
        attend_gain_grad[0, 0],
        expand_gain_grad[0, 0],
        jnp.swapaxes(heads_left_grad, 1, 2),
        heads_right_grad,
        heads_mag_grad[:, 0],
        output_left_grad[0].T,
        output_right_grad[0],
        output_mag_grad[0, 0],
        jnp.swapaxes(expand_left_grad, 1, 2),
        expand_right_grad,
        expand_mag_grad[:, 0],
        shrink_left_grad[0].T,
        shrink_right_grad[0],
        shrink_mag_grad[0, 0],
    )


def solution(mesh):
    placed = (
        P("dp", None),
        P("dp", None),
        P("dp", None),
        P(),
        P(),
        P(None, None, "mp"),
        P(),
        P(None, None, "mp"),
        P(None, "mp"),
        P("mp", None),
        P("mp", None),
        P(),
        P(),
        P(None, None, "mp"),
        P(),
        P(None, None, "mp"),
        P(None, "mp"),
        P("mp", None),
        P("mp", None),
        P(),
        P(),
    )
    return jax.shard_map(
        body,
        mesh=mesh,
        in_specs=placed,
        out_specs=(
            P(("dp", "mp"), None),
            P(("dp", "mp"), None),
            P(),
            P(),
            P(),
            P(None, None, "mp"),
            P(None, "mp"),
            P("mp", None),
            P(),
            P(),
            P(),
            P(None, None, "mp"),
            P(None, "mp"),
            P("mp", None),
            P(),
            P(),
        ),
        check_vma=False,
    )
```

```python
import functools

import jax
import jax.numpy as jnp
import ml_dtypes
import numpy as np
from jax import lax
from jax.experimental import pallas as pl
from jax.experimental.pallas import tpu as pltpu
from jax.sharding import PartitionSpec as P

HEAD_DIM = 128
CORES = 2
LONGEST = 512
ATTEND_BLOCK = 256
ADAPT_SCALE = 2.0
NORM_EPS = 1e-05
ROPE_BASE = 10000.0
MASKED = -1e30

F32 = jnp.float32
LOW = jnp.bfloat16
NN = (((1,), (0,)), ((), ()))
NT = (((1,), (1,)), ((), ()))
TN = (((0,), (0,)), ((), ()))


MESH_IDS = pl.DeviceIdType.MESH


def sibling_id():
    me = lax.axis_index("mp")
    return me // CORES * CORES + lax.rem(me + 1, CORES)


def greet(peers):
    for peer in peers:
        pl.semaphore_signal(
            pltpu.get_barrier_semaphore(), 1, device_id={"mp": peer}, device_id_type=MESH_IDS
        )


def greeted(count):
    pl.semaphore_wait(pltpu.get_barrier_semaphore(), count)


def remote(source, target, send_sem, recv_sem, peer):
    return pltpu.make_async_remote_copy(
        src_ref=source,
        dst_ref=target,
        send_sem=send_sem,
        recv_sem=recv_sem,
        device_id={"mp": peer},
        device_id_type=MESH_IDS,
    )


def dot(left, right, dims=NN):
    return lax.dot_general(left, right, dims, preferred_element_type=F32)


def shape(dims, kind):
    return jax.ShapeDtypeStruct(tuple(dims), kind)


def call(name, kernel, operands, grid, in_specs, out_specs, out_shape, scratch=(), prefetch=(), flops=0, mib=63.5, identity=None):
    moved = sum(v.size * v.dtype.itemsize for v in operands)
    moved += sum(v.size * v.dtype.itemsize for v in out_shape)
    return pl.pallas_call(
        kernel,
        name=name,
        out_shape=out_shape,
        grid_spec=pltpu.PrefetchScalarGridSpec(
            num_scalar_prefetch=len(prefetch),
            grid=grid,
            in_specs=in_specs,
            out_specs=out_specs,
            scratch_shapes=scratch,
        ),
        compiler_params=pltpu.CompilerParams(
            vmem_limit_bytes=int(mib * 2**20), collective_id=identity, has_side_effects=identity is not None
        ),
        cost_estimate=pl.CostEstimate(flops=flops // 16, bytes_accessed=moved // 16, transcendentals=0),
    )(*prefetch, *operands)


def tile_of(size, most):
    return most if size % most == 0 else size


def split_rows(values):
    top = values.astype(LOW)
    rest = (values - top.astype(F32)).astype(LOW)
    return jnp.concatenate([top, rest], axis=0)


def turned(left_map):
    return jnp.swapaxes(left_map, -1, -2)


def norm_weight(total, squares, magnitude):
    norm = jnp.sqrt(squares)
    return total * magnitude / (norm * norm * norm)


def sum_refs(refs):
    total = refs[0][...]
    for ref in refs[1:]:
        total = total + ref[...]
    return total


def fold(values):
    half = values.shape[0] // 2
    return values[:half] + values[half:]


def merge_tile(base_at, low_put, left, right, depth):
    rank = right.shape[0]
    doubled = ADAPT_SCALE * right
    top = doubled.astype(LOW)
    rest = (doubled - top.astype(F32)).astype(LOW)
    right_stack = jnp.concatenate([top, rest, top], axis=0)
    left_pair = split_rows(left)
    left_stack = jnp.concatenate([left_pair[:rank], left_pair[:rank], left_pair[rank:]], axis=0)
    width = right.shape[1]
    wide = 256 if width == 512 else width
    step = tile_of(depth, 1024)
    squares = []
    for at in range(0, width, wide):
        columns = slice(at, at + wide)
        total = jnp.zeros((1, wide), F32)
        for start in range(0, depth, step):
            merged = base_at(start, step, columns).astype(F32) + dot(
                left_stack[:, start : start + step], right_stack[:, columns], TN
            )
            low_put(start, step, columns, merged.astype(LOW))
            total = total + jnp.sum(merged * merged, axis=0, keepdims=True)
        squares.append(total)
    return jnp.concatenate(squares, axis=1)


def merge_pair_kernel(*refs):
    for n in range(2):
        base_ref, left_ref, right_ref = refs[3 * n : 3 * n + 3]
        low_ref, squares_ref = refs[6 + n], refs[8]
        depth = base_ref.shape[0]
        if low_ref.shape[0] > depth:
            low_ref[depth:, :] = jnp.zeros((low_ref.shape[0] - depth, low_ref.shape[1]), LOW)

        def put(start, step, columns, tile, low_ref=low_ref):
            low_ref[start : start + step, columns] = tile

        squares_ref[n : n + 1, :] = merge_tile(
            lambda start, step, columns, base_ref=base_ref: base_ref[start : start + step, columns],
            put,
            left_ref[...],
            right_ref[...],
            depth,
        )


def merge_pair(triples):
    operands, in_specs, low_specs, low_shapes = [], [], [], []
    width = triples[0][0].shape[1]
    wide = tile_of(width, 512)
    for base, left, right in triples:
        depth, rank = base.shape[0], right.shape[0]
        operands += [base, left, right]
        in_specs += [
            pl.BlockSpec((depth, wide), lambda n: (0, n)),
            pl.BlockSpec((rank, depth), lambda n: (0, 0)),
            pl.BlockSpec((rank, wide), lambda n: (0, n)),
        ]
        low_specs.append(pl.BlockSpec((padded(depth), wide), lambda n: (0, n)))
        low_shapes.append(shape((padded(depth), width), LOW))
    return call(
        "merge_pair",
        merge_pair_kernel,
        tuple(operands),
        (width // wide,),
        in_specs,
        low_specs + [pl.BlockSpec((2, wide), lambda n: (0, n))],
        low_shapes + [shape((2, width), F32)],
        flops=2 * sum(v.size for v in operands) * 256,
    )


def merge_kernel(base_ref, left_ref, right_ref, low_ref, squares_ref):
    depth, width = base_ref.shape[1:]
    if low_ref.shape[1] > depth:
        low_ref[0, depth:, :] = jnp.zeros((low_ref.shape[1] - depth, low_ref.shape[2]), LOW)
    if low_ref.shape[2] > width:
        spare = low_ref.shape[2] - width
        low_ref[0, :, width:] = jnp.zeros((low_ref.shape[1], spare), LOW)
        squares_ref[0, :, width:] = jnp.ones((1, spare), F32)

    def put(start, step, columns, tile):
        low_ref[0, start : start + step, columns] = tile

    squares = merge_tile(
        lambda start, step, columns: base_ref[0, start : start + step, columns],
        put,
        left_ref[0],
        right_ref[0],
        depth,
    )

    @pl.when(pl.program_id(2) == 0)
    def _():
        squares_ref[0, :, :width] = squares

    @pl.when(pl.program_id(2) > 0)
    def _():
        squares_ref[0, :, :width] += squares


def padded(size):
    return -(-size // 256) * 256


def pad_last(values, size):
    return jnp.pad(values, [(0, 0)] * (values.ndim - 1) + [(0, size - values.shape[-1])])


def merge(base, left, right, deep, wide):
    members, depth, width = base.shape
    low_deep = padded(deep) if deep == depth else deep
    low_wide = padded(wide) if wide == width else wide
    low_shape = (members, depth // deep * low_deep, width // wide * low_wide)
    rank = right.shape[1]
    return call(
        "merge",
        merge_kernel,
        (base, left, right),
        (members, width // wide, depth // deep),
        [
            pl.BlockSpec((1, deep, wide), lambda m, n, k: (m, k, n)),
            pl.BlockSpec((1, rank, deep), lambda m, n, k: (m, 0, k)),
            pl.BlockSpec((1, rank, wide), lambda m, n, k: (m, 0, n)),
        ],
        [
            pl.BlockSpec((1, low_deep, low_wide), lambda m, n, k: (m, k, n)),
            pl.BlockSpec((1, 1, low_wide), lambda m, n, k: (m, 0, n)),
        ],
        [shape(low_shape, LOW), shape((members, 1, low_shape[2]), F32)],
        flops=2 * members * depth * width * 256,
    )


def rms_rows(values):
    return lax.rsqrt(jnp.mean(values * values, axis=1, keepdims=True) + NORM_EPS)


TABLE_STEP = 32


def table_pieces(places):
    half = np.arange(HEAD_DIM) % (HEAD_DIM // 2)
    angles = np.asarray(places)[:, None] * ROPE_BASE ** (-2.0 * half / HEAD_DIM)[None, :]
    rest = np.concatenate([np.cos(angles), np.sin(angles)], axis=1)
    pieces = []
    for _ in range(3):
        pieces.append(rest.astype(ml_dtypes.bfloat16))
        rest = rest - pieces[-1].astype(np.float64)
    return jnp.asarray(np.concatenate(pieces, axis=0))


def rotation(first, coarse, fine):
    rows = first.shape[0]
    position = lax.broadcasted_iota(jnp.int32, (rows, 1), 0) - first
    lane = lax.broadcasted_iota(jnp.int32, (rows, 3 * TABLE_STEP), 1) % TABLE_STEP
    pick = lambda place, table: dot((lane == place).astype(F32).astype(LOW), table)
    high = pick(position // TABLE_STEP, coarse)
    small = pick(position % TABLE_STEP, fine)
    cos_a, sin_a = high[:, :HEAD_DIM], high[:, HEAD_DIM:]
    cos_b, sin_b = small[:, :HEAD_DIM], small[:, HEAD_DIM:]
    sine = sin_a * cos_b + cos_a * sin_b
    left_half = lax.broadcasted_iota(jnp.int32, sine.shape, 1) < HEAD_DIM // 2
    return cos_a * cos_b - sin_a * sin_b, jnp.where(left_half, -sine, sine)


def heads_kernel(
    token_ref,
    gain_ref,
    base_ref,
    left_ref,
    right_ref,
    magnitude_ref,
    segment_ref,
    coarse_ref,
    fine_ref,
    part_ref,
    normed_ref,
    low_ref,
    post_ref,
    squares_ref,
    across_ref,
    cos_ref,
    sine_ref,
    sum_ref,
    first_ref,
    rows_all,
    part_mine,
    part_got,
    send_sems,
    recv_sems,
):
    total_rows = token_ref.shape[0]
    depth, width = base_ref.shape[1:]
    rank = right_ref.shape[1]
    groups = part_got.shape[0]
    me = lax.axis_index("mp")
    peers = [lax.rem(me + k, groups) for k in range(groups)]
    part_copies = [
        remote(part_mine, part_got.at[k], send_sems.at[k], recv_sems.at[k], peers[k])
        for k in range(1, groups)
    ]

    @pl.when(pl.program_id(0) == 0)
    def _():
        greet(peers[1:])
        part_mine[...] = part_ref[...]
        step = 128

        def some(i, carry):
            at = pl.ds(pl.multiple_of(i * step, step), step)
            values = token_ref[at, :].astype(F32)
            low = (values * rms_rows(values) * gain_ref[...]).astype(LOW)
            normed_ref[at, :] = low
            rows_all[at, :] = low
            return carry

        lax.fori_loop(0, total_rows // step, some, 0)
        ids = segment_ref[...].astype(F32)
        ids_down = jnp.transpose(jnp.broadcast_to(ids, (8, total_rows)))[:, :1]
        for start in range(0, total_rows, 256):
            rows = slice(start, start + 256)
            smaller = jnp.where(ids < ids_down[rows], 1.0, 0.0)
            first = jnp.sum(smaller, axis=1, keepdims=True).astype(jnp.int32)
            first_ref[rows, :] = first
            cosine, sine = rotation(first - start, coarse_ref[...], fine_ref[...])
            cos_ref[rows, :] = cosine
            sine_ref[rows, :] = sine
        greeted(groups - 1)
        for copy in part_copies:
            copy.start()

    @pl.when(pl.program_id(0) == pl.num_programs(0) - 1)
    def _():
        total = part_mine[...]
        for k, copy in enumerate(part_copies, 1):
            copy.wait_recv()
            total = total + part_got[k]
        sum_ref[...] = total
        for copy in part_copies:
            copy.wait_send()

    rows_all[total_rows:, :] = left_ref[0].astype(LOW)
    turning = pl.program_id(0) < 2
    wide = 256

    def put(start, step, columns, tile):
        low_ref[0, start : start + step, columns] = tile

    squares_ref[0] = merge_tile(
        lambda start, step, columns: base_ref[0, start : start + step, columns],
        put,
        left_ref[0],
        right_ref[0],
        depth,
    )
    for column in range(0, width, wide):
        columns = slice(column, column + wide)
        magnitude = magnitude_ref[pl.ds(pl.program_id(0), 1), columns]
        scale = magnitude / jnp.sqrt(squares_ref[0, :, columns])
        low = low_ref[0, :, columns]
        step = min(512, total_rows)
        for start in range(0, total_rows, step):
            last = start + step == total_rows
            rows = slice(start, start + step)
            pre = dot(rows_all[start : start + step + (rank if last else 0), :], low)
            if last:
                across_ref[0, :, columns] = pre[step:]
            post = pre[:step] * scale
            cos_table = jnp.where(turning, cos_ref[rows, :], 1.0)
            sine_table = jnp.where(turning, sine_ref[rows, :], 0.0)
            for head in range(0, wide, HEAD_DIM):
                piece = post[:, head : head + HEAD_DIM]
                other = pltpu.roll(piece, HEAD_DIM // 2, 1)
                post_ref[0, rows, column + head : column + head + HEAD_DIM] = (
                    piece * cos_table + other * sine_table
                ).astype(LOW)


def project_heads(tokens, gain, base, left, right, magnitude, segments, part, groups):
    members, depth, width = base.shape
    rows, rank = tokens.shape[0], right.shape[1]
    coarse = table_pieces(np.arange(TABLE_STEP) * TABLE_STEP)
    fine = table_pieces(np.arange(TABLE_STEP))
    whole = lambda v: pl.BlockSpec(v.shape, lambda m: (0,) * v.ndim)
    of_member = lambda *dims: pl.BlockSpec((1,) + dims, lambda m: (m, 0, 0))
    table = pl.BlockSpec((rows, HEAD_DIM), lambda m: (0, 0))
    return call(
        "project_heads",
        heads_kernel,
        (tokens, gain, base, left, right, magnitude, segments, coarse, fine, part),
        (members,),
        [
            whole(tokens),
            whole(gain),
            of_member(depth, width),
            of_member(rank, depth),
            of_member(rank, width),
            whole(magnitude),
            whole(segments),
            whole(coarse),
            whole(fine),
            whole(part),
        ],
        [
            whole(tokens),
            of_member(depth, width),
            of_member(rows, width),
            of_member(1, width),
            of_member(rank, width),
            table,
            table,
            whole(part),
            pl.BlockSpec((rows, 1), lambda m: (0, 0)),
        ],
        [
            shape((rows, depth), LOW),
            shape(base.shape, LOW),
            shape((members, rows, width), LOW),
            shape((members, 1, width), F32),
            shape((members, rank, width), F32),
            shape((rows, HEAD_DIM), F32),
            shape((rows, HEAD_DIM), F32),
            shape(part.shape, F32),
            shape((rows, 1), jnp.int32),
        ],
        scratch=[
            pltpu.VMEM((rows + rank, depth), LOW),
            pltpu.VMEM(part.shape, F32),
            pltpu.VMEM((groups,) + part.shape, F32),
            pltpu.SemaphoreType.DMA((groups,)),
            pltpu.SemaphoreType.DMA((groups,)),
        ],
        identity=2,
        flops=2 * members * rows * depth * width,
    )


def key_start(block):
    return max(0, (block * ATTEND_BLOCK - (LONGEST - 1)) // ATTEND_BLOCK * ATTEND_BLOCK)


def masked_probs(scores, first, row_at, key_at):
    scores = scores * HEAD_DIM ** (-0.5)
    places = row_at + lax.broadcasted_iota(jnp.int32, scores.shape, 0)
    others = key_at + lax.broadcasted_iota(jnp.int32, scores.shape, 1)
    scores = jnp.where((others >= first) & (others <= places), scores, MASKED)
    exp_scores = jnp.exp(scores - jnp.max(scores, axis=1, keepdims=True))
    return exp_scores * (1.0 / jnp.sum(exp_scores, axis=1, keepdims=True))


class Unit:
    def __init__(self, head, block):
        self.row_at, self.key_at = block * ATTEND_BLOCK, key_start(block)
        self.rows = slice(self.row_at, self.row_at + ATTEND_BLOCK)
        self.keys = slice(self.key_at, self.row_at + ATTEND_BLOCK)
        self.lanes = slice(head * HEAD_DIM, (head + 1) * HEAD_DIM)


def units_of(rows, width, most):
    units = [
        Unit(head, block)
        for block in range(rows // ATTEND_BLOCK)
        for head in range(width // HEAD_DIM)
    ]
    return [units[at : at + most] for at in range(0, len(units), most)]


def put_rows(ref, lead, row_at, lanes, values, order_ref, groups):
    share = ref.shape[len(lead)] // groups
    step = min(share, values.shape[0])
    for start in range(0, values.shape[0], step):
        group = (row_at + start) // share
        inside = (row_at + start) % share
        at = pl.multiple_of(order_ref[groups + group] * share + inside, step)
        ref[(*lead, pl.ds(at, step), lanes)] = values[start : start + step].astype(ref.dtype)


def attend_kernel(groups, order_ref, query_ref, key_ref, value_ref, first_ref, out_ref):
    for some in units_of(*query_ref.shape[1:], 4):
        scores = [
            dot(query_ref[0, u.rows, u.lanes], key_ref[0, u.keys, u.lanes], NT) for u in some
        ]
        probs = [
            masked_probs(s, first_ref[u.rows, :], u.row_at, u.key_at).astype(LOW)
            for u, s in zip(some, scores)
        ]
        for u, p in zip(some, probs):
            mixed = dot(p, value_ref[0, u.keys, u.lanes])
            put_rows(out_ref, (), u.row_at, u.lanes, mixed, order_ref, groups)


def attend(order, groups, post, first):
    rows, width = post.shape[1:]
    wide = 2 * HEAD_DIM
    member = lambda m: pl.BlockSpec((1, rows, wide), lambda h, o: (m, 0, h))
    return call(
        "attend",
        functools.partial(attend_kernel, groups),
        (post, post, post, first),
        (width // wide,),
        [member(0), member(1), member(2), pl.BlockSpec((rows, 1), lambda h, o: (0, 0))],
        [pl.BlockSpec((rows, wide), lambda h, o: (0, h))],
        [shape((rows, width), LOW)],
        prefetch=(order,),
        flops=4 * rows * rows * width,
    )[0]


def attend_back_kernel(
    groups,
    order_ref,
    query_ref,
    key_ref,
    value_ref,
    first_ref,
    cos_ref,
    sine_ref,
    magnitude_ref,
    squares_ref,
    low_ref,
    *rest,
):
    pieces, (grad_ref, total_ref, upper_all, heads_grad, key_grad, value_grad, sems) = rest[:-7], rest[-7:]
    rows_all, width = query_ref.shape[1:]
    share = rows_all // groups

    @pl.when(pl.program_id(0) == 0)
    def _():
        copies = []
        for place, piece in enumerate(pieces):
            at = pl.multiple_of(order_ref[place] * share, share)
            copies.append(
                pltpu.make_async_copy(piece, upper_all.at[pl.ds(at, share), :], sems.at[place])
            )
            copies[-1].start()
        for copy in copies:
            copy.wait()

    step = min(512, rows_all)
    for start in range(0, rows_all, step):
        at = slice(start, start + step)
        heads_grad[at, :] = dot(upper_all[at, :], low_ref[0], NT).astype(LOW)
    norm = [jnp.sqrt(squares_ref[m]) for m in range(3)]
    scale = [magnitude_ref[m : m + 1] / norm[m] for m in range(3)]
    heads = range(0, width, HEAD_DIM)
    totals = [jnp.zeros((1, width), F32) for _ in range(3)]
    filled = set()

    def back(values, rows):
        return values * cos_ref[rows, :] - pltpu.roll(values, HEAD_DIM // 2, 1) * sine_ref[rows, :]

    def add(ref, unit, values):
        for start in range(0, values.shape[0], ATTEND_BLOCK):
            at = unit.key_at + start
            rows = slice(at, at + ATTEND_BLOCK)
            name = (id(ref), at, unit.lanes.start)
            if name in filled:
                ref[rows, unit.lanes] += values[start : start + ATTEND_BLOCK]
            else:
                filled.add(name)
                ref[rows, unit.lanes] = values[start : start + ATTEND_BLOCK]

    def spread(per_head):
        return jnp.concatenate(per_head, axis=1)

    query_totals = [jnp.zeros((1, HEAD_DIM), F32) for _ in heads]
    for some in units_of(rows_all, width, 2):
        scores = [
            dot(query_ref[0, u.rows, u.lanes], key_ref[0, u.keys, u.lanes], NT) for u in some
        ]
        grad_weights = [
            dot(heads_grad[u.rows, u.lanes], value_ref[0, u.keys, u.lanes], NT) for u in some
        ]
        probs = [
            masked_probs(s, first_ref[u.rows, :], u.row_at, u.key_at)
            for u, s in zip(some, scores)
        ]
        grad_scores = [
            (p * (g - jnp.sum(p * g, axis=1, keepdims=True))).astype(LOW)
            for p, g in zip(probs, grad_weights)
        ]
        for u, p, g in zip(some, probs, grad_scores):
            add(value_grad, u, dot(p.astype(LOW), heads_grad[u.rows, u.lanes], TN))
            add(key_grad, u, dot(g, query_ref[0, u.rows, u.lanes], TN))
        for u, g in zip(some, grad_scores):
            grad = back(dot(g, key_ref[0, u.keys, u.lanes]) * HEAD_DIM ** (-0.5), u.rows)
            head = u.lanes.start // HEAD_DIM
            post = back(query_ref[0, u.rows, u.lanes].astype(F32), u.rows)
            query_totals[head] = query_totals[head] + jnp.sum(grad * post, axis=0, keepdims=True)
            put_rows(grad_ref, (0,), u.row_at, u.lanes, grad * scale[0][:, u.lanes], order_ref, groups)
    totals[0] = spread(query_totals)
    for row_at in range(0, rows_all, ATTEND_BLOCK):
        rows = slice(row_at, row_at + ATTEND_BLOCK)
        for head in heads:
            lanes = slice(head, head + HEAD_DIM)
            grad = back(key_grad[rows, lanes] * HEAD_DIM ** (-0.5), rows)
            post = back(key_ref[0, rows, lanes].astype(F32), rows)
            part = jnp.sum(grad * post, axis=0, keepdims=True)
            query_totals[head // HEAD_DIM] = part if row_at == 0 else query_totals[head // HEAD_DIM] + part
            put_rows(grad_ref, (1,), row_at, lanes, grad * scale[1][:, lanes], order_ref, groups)
        grad = value_grad[rows, :]
        totals[2] = totals[2] + jnp.sum(grad * value_ref[0, rows, :].astype(F32), axis=0, keepdims=True)
        put_rows(grad_ref, (2,), row_at, slice(0, width), grad * scale[2], order_ref, groups)
    totals[1] = spread(query_totals)
    for m in range(3):
        total_ref[m] = totals[m] / scale[m]


def attend_back(order, groups, post, first, cos_table, sine_table, magnitude, squares, low, pieces):
    rows, width = post.shape[1:]
    depth = low.shape[2]
    wide = 2 * HEAD_DIM
    member = lambda m: pl.BlockSpec((1, rows, wide), lambda h, o: (m, 0, h))
    table = pl.BlockSpec((rows, HEAD_DIM), lambda h, o: (0, 0))
    column = pl.BlockSpec((3, 1, wide), lambda h, o: (0, 0, h))
    return call(
        "attend_back",
        functools.partial(attend_back_kernel, groups),
        (post, post, post, first, cos_table, sine_table, magnitude, squares, low, *pieces),
        (width // wide,),
        [
            member(0),
            member(1),
            member(2),
            pl.BlockSpec((rows, 1), lambda h, o: (0, 0)),
            table,
            table,
            pl.BlockSpec((3, wide), lambda h, o: (0, h)),
            column,
            pl.BlockSpec((1, wide, depth), lambda h, o: (0, h, 0)),
            *[pl.BlockSpec(memory_space=pl.ANY) for _ in pieces],
        ],
        [pl.BlockSpec((3, rows, wide), lambda h, o: (0, 0, h)), column],
        [shape((3, rows, width), LOW), shape((3, 1, width), F32)],
        scratch=[
            pltpu.VMEM((rows, depth), LOW),
            pltpu.VMEM((rows, wide), LOW),
            pltpu.VMEM((rows, wide), F32),
            pltpu.VMEM((rows, wide), F32),
            pltpu.SemaphoreType.DMA((len(pieces),)),
        ],
        prefetch=(order,),
        flops=10 * rows * rows * width + 2 * rows * width * depth,
    )


def product_kernel(dims, n_totals, n_lines, steps, *refs):
    value_ref, weight_ref = refs[:2]
    if n_totals == 0:
        left_ref, *refs = refs[2:]
    else:
        right_ref, squares_ref, magnitude_ref = refs[2:5]
        totals, refs = refs[5 : 5 + n_totals], refs[5 + n_totals :]
    lines = []
    if n_lines > 0:
        lines, refs = refs[:n_lines], refs[n_lines:]
        *refs, line_mine, line_got, line_send_sems, line_recv_sems = refs
    *outs, extra_ref, rows_all, sent, got, send_sems, recv_sems = refs
    if n_lines > 0:
        *outs, line_out = outs
    members, groups, share, inner = value_ref.shape
    count, wide = groups * share, extra_ref.shape[2]
    now = pl.program_id(0)
    sibling = sibling_id()
    me = lax.axis_index("mp")
    peers = [lax.rem(me + k, groups) for k in range(1, groups)] if n_lines > 0 else [sibling]
    line_copies = [
        remote(line_mine, line_got.at[k], line_send_sems.at[k], line_recv_sems.at[k], peer)
        for k, peer in enumerate(peers if n_lines > 0 else [], 1)
    ]

    @pl.when(now == 0)
    def _():
        greet(peers)
        for n, ref in enumerate(lines):
            line_mine[n : n + 1, :] = ref[...]
        if n_totals > 0:
            total = sum_refs(totals)
        for m in range(members):
            rows_all[m, :count, :] = value_ref[m].reshape(count, inner)
            if n_totals == 0:
                rows_all[m, count:, :] = left_ref[m].astype(LOW)
            else:
                weight = norm_weight(total[m], squares_ref[m], magnitude_ref[m : m + 1])
                rows_all[m, count:, :] = (right_ref[m] * weight).astype(LOW)

    result = None
    for m in range(members):
        part = dot(rows_all[m], weight_ref[m], dims)
        extra_ref[m] = part[count:]
        result = part[:count] if result is None else result + part[:count]

    def columns(step):
        return pl.ds(pl.multiple_of(step * wide, wide), wide)

    def copy(step):
        return remote(sent.at[step], got.at[step], send_sems.at[step], recv_sems.at[step], sibling)

    def add(step):
        copy(step).wait_recv()
        for n, ref in enumerate(outs):
            total = ref[:, columns(step)].astype(F32) + got[step, n].astype(F32)
            ref[:, columns(step)] = total.astype(LOW)

    for n, ref in enumerate(outs):
        at = CORES * n * share
        sent[now, n] = result[at : at + share].astype(LOW)
        ref[:, columns(now)] = result[at + share : at + CORES * share].astype(LOW)

    @pl.when(now == 0)
    def _():
        greeted(len(peers))
        for each in line_copies:
            each.start()

    copy(now).start()

    @pl.when(now > 0)
    def _():
        add(now - 1)

    @pl.when(now == steps - 1)
    def _():
        add(now)
        for step in range(steps):
            copy(step).wait_send()
        if n_lines > 0:
            line_sum = line_mine[...]
            for k, each in enumerate(line_copies, 1):
                each.wait_recv()
                line_sum = line_sum + line_got[k]
            line_out[...] = line_sum
            for each in line_copies:
                each.wait_send()


def product(name, identity, values, weights, dims, left=None, correction=None, lines=()):
    members, groups, share, inner = values.shape
    chips = groups // CORES
    width = weights.shape[2] if dims is NN else weights.shape[1]
    wide = tile_of(width, 512)
    steps = width // wide
    if dims is NN:
        weight_spec = pl.BlockSpec((members, inner, wide), lambda n: (0, 0, n))
    else:
        weight_spec = pl.BlockSpec((members, wide, inner), lambda n: (0, n, 0))
    if correction is None:
        extra, n_totals, rank = (left,), 0, left.shape[1]
    else:
        right, squares, magnitude, totals = correction
        extra, n_totals, rank = (right, squares, magnitude, *totals), len(totals), right.shape[1]
    fixed = lambda v: pl.BlockSpec(v.shape, lambda n: (0,) * v.ndim)
    out = pl.BlockSpec((share, width), lambda n: (0, 0))
    line_specs, line_shapes, line_scratch = [], [], []
    if lines:
        line = (len(lines), width)
        line_specs = [pl.BlockSpec(line, lambda n: (0, 0))]
        line_shapes = [shape(line, F32)]
        line_scratch = [
            pltpu.VMEM(line, F32),
            pltpu.VMEM((groups,) + line, F32),
            pltpu.SemaphoreType.DMA((groups,)),
            pltpu.SemaphoreType.DMA((groups,)),
        ]
    results = call(
        name,
        functools.partial(product_kernel, dims, n_totals, len(lines), steps),
        (values, weights, *extra, *lines),
        (steps,),
        [fixed(values), weight_spec] + [fixed(v) for v in (*extra, *lines)],
        [out] * chips + line_specs + [pl.BlockSpec((members, rank, wide), lambda n: (0, 0, n))],
        [shape((share, width), LOW)] * chips
        + line_shapes
        + [shape((members, rank, width), F32)],
        scratch=[
            pltpu.VMEM((members, groups * share + rank, inner), LOW),
            pltpu.VMEM((steps, chips, share, wide), LOW),
            pltpu.VMEM((steps, chips, share, wide), LOW),
            pltpu.SemaphoreType.DMA((steps,)),
            pltpu.SemaphoreType.DMA((steps,)),
        ]
        + line_scratch,
        flops=2 * members * groups * share * inner * width,
        identity=identity,
    )
    return results[:chips], *results[chips:]


def shrink_kernel(chips, order_ref, *refs):
    values, (weight_ref, left_ref, cot_ref), outs = refs[:chips], refs[chips : chips + 3], refs[chips + 3 :]
    total_ref, across_ref, rows_all = outs[-3:]
    both, inner = values[0].shape
    share, depth = both // CORES, left_ref.shape[2]
    count = chips * both

    @pl.when(pl.program_id(0) == 0)
    def _():
        for step, ref in enumerate(values):
            rows_all[step * both : (step + 1) * both, :] = ref[...]
        if inner > depth:
            rows_all[count:, depth:] = jnp.zeros((rows_all.shape[0] - count, inner - depth), LOW)
        rows_all[count:, :depth] = left_ref[0].astype(LOW)

    result = dot(rows_all[...], weight_ref[0])
    across_ref[0] = result[count:]
    total = jnp.zeros((1, weight_ref.shape[2]), F32)
    for place in range(chips * CORES):
        pre = result[place * share : (place + 1) * share]
        outs[place][...] = pre.astype(LOW)
        at = pl.multiple_of(order_ref[place] * share, share)
        cot = cot_ref[pl.ds(at, share), :].astype(F32)
        total = total + jnp.sum(pre * cot, axis=0, keepdims=True)
    total_ref[...] = total


def shrink_product(order, values, weights, left, cotangent):
    chips = len(values)
    share, inner = values[0].shape[0] // CORES, values[0].shape[1]
    width, rank = weights.shape[2], left.shape[1]
    rows = chips * CORES * share
    wide = tile_of(width, 512)
    fixed = lambda v: pl.BlockSpec(v.shape, lambda n, o: (0,) * v.ndim)
    results = call(
        "shrink_product",
        functools.partial(shrink_kernel, chips),
        (*values, weights, left, cotangent),
        (width // wide,),
        [fixed(v) for v in values]
        + [
            pl.BlockSpec((1, inner, wide), lambda n, o: (0, 0, n)),
            fixed(left),
            pl.BlockSpec((rows, wide), lambda n, o: (0, n)),
        ],
        [pl.BlockSpec((share, wide), lambda n, o: (0, n))] * (chips * CORES)
        + [
            pl.BlockSpec((1, wide), lambda n, o: (0, n)),
            pl.BlockSpec((1, rank, wide), lambda n, o: (0, 0, n)),
        ],
        [shape((share, width), LOW)] * (chips * CORES)
        + [shape((1, width), F32), shape((1, rank, width), F32)],
        scratch=[pltpu.VMEM((rows + rank, inner), LOW)],
        prefetch=(order,),
        flops=2 * rows * inner * width,
    )
    return results[: chips * CORES], results[-2], results[-1]


def row_call(name, kernel, order, given, whole, out_kinds, sums, prepare):
    share = min(v.shape[0] for v, _ in given)
    width = given[0][0].shape[1]
    halves = 2
    half = share // halves
    count = len(given)

    def run(order_ref, *refs):
        sources, rest = refs[:count], refs[count : -count - 1]
        held, sems = refs[-count - 1 : -1], refs[-1]

        def copies(part):
            for i, ((_, cut), source, target) in enumerate(zip(given, sources, held)):
                at = part * half
                if cut:
                    at = pl.multiple_of(order_ref[1] * share + at, half)
                yield pltpu.make_async_copy(
                    source.at[pl.ds(at, half), :],
                    target.at[pl.ds(part * half, half), :],
                    sems.at[part, i],
                )

        for part in range(halves):

            @pl.when(pl.program_id(0) == part)
            def _(part=part):
                if part == 0:
                    for each in range(halves):
                        for copy in copies(each):
                            copy.start()
                for copy in copies(part):
                    copy.wait()

        outs = rest[len(whole) : len(whole) + len(out_kinds)]
        totals, sums_held = rest[len(whole) + len(out_kinds) :][:sums], rest[len(rest) - sums :]
        tile = 32
        lines = prepare(*[ref[...] for ref in rest[: len(whole)]])
        for ref in sums_held:
            ref[...] = jnp.zeros_like(ref)

        def some(i, carry):
            inside = pl.ds(pl.multiple_of(i * tile, tile), tile)
            at = pl.ds(pl.multiple_of(pl.program_id(0) * half + i * tile, tile), tile)
            values = kernel([ref[at, :].astype(F32) for ref in held], *lines)
            for ref, value in zip(outs, values):
                ref[inside, :] = value.astype(ref.dtype)
            for ref, value in zip(sums_held, values[len(outs) :]):
                ref[...] += jnp.sum(value.reshape(tile // 8, 8, width), axis=0)
            return carry

        lax.fori_loop(0, half // tile, some, 0, unroll=2)
        for ref, held_ref in zip(totals, sums_held):
            add_column(ref, held_ref[...])

    line = pl.BlockSpec((1, width), lambda i, o: (0, 0))
    return call(
        name,
        run,
        (*[v for v, _ in given], *whole),
        (halves,),
        [pl.BlockSpec(memory_space=pl.ANY) for _ in given] + [line for _ in whole],
        [pl.BlockSpec((half, width), lambda i, o: (i, 0)) for _ in out_kinds]
        + [line for _ in range(sums)],
        [shape((share, width), kind) for kind in out_kinds]
        + [shape((1, width), F32) for _ in range(sums)],
        scratch=[pltpu.VMEM((8, width), F32) for _ in range(sums)]
        + [pltpu.VMEM((share, width), v.dtype) for v, _ in given]
        + [pltpu.SemaphoreType.DMA((halves, count))],
        prefetch=(order,),
        flops=20 * share * width,
    )


def sum_of(values):
    total = values[0]
    for value in values[1:]:
        total = total + value
    return total


def add_column(ref, values):
    part = jnp.sum(values, axis=0, keepdims=True)

    @pl.when(pl.program_id(0) == 0)
    def _():
        ref[...] = part

    @pl.when(pl.program_id(0) > 0)
    def _():
        ref[...] += part


def scale_first(squares, magnitude, *rest):
    norm = jnp.sqrt(squares)
    return (magnitude / norm, norm / magnitude, *rest)


def hidden_kernel(given, scale, inverse, gain):
    hidden = given[0] + sum_of(given[1:]) * scale
    return hidden, hidden * rms_rows(hidden) * gain


def mixed_kernel(given, scale, inverse):
    return (given[0] + sum_of(given[1:]) * scale,)


def norm_back(grad_normed, values, gain):
    factor = rms_rows(values)
    scaled = grad_normed * gain
    inner = jnp.mean(scaled * values, axis=1, keepdims=True)
    back = factor * scaled - values * (factor * factor * factor * inner)
    return back, grad_normed * values * factor


def hidden_back_kernel(given, scale, inverse, gain):
    cot, token, hidden = given[:3]
    back, gain_terms = norm_back(sum_of(given[3:]), hidden, gain)
    grad = cot + back
    return grad, grad * scale, grad * ((hidden - token) * inverse), gain_terms


def token_back_kernel(given, gain):
    back, gain_terms = norm_back(sum_of(given[2:]), given[0], gain)
    return given[1] + back, gain_terms


def shrink_back_kernel(places, order_ref, *refs):
    cots, (low_ref, squares_ref, magnitude_ref, product_ref, grad_ref, rows_all) = refs[:places], refs[places:]
    scale = magnitude_ref[0] / jnp.sqrt(squares_ref[0])
    share = cots[0].shape[0]
    for place, cot_ref in enumerate(cots):
        grad = (cot_ref[...].astype(F32) * scale).astype(LOW)
        grad_ref[place] = grad
        rows_all[place * share : (place + 1) * share, :] = grad
    result = dot(rows_all[...], low_ref[0], NT).astype(LOW)
    for place in range(places):
        product_ref[place] = result[place * share : (place + 1) * share]


def shrink_back(order, cotangent, low, squares, magnitude, groups):
    rows, width = cotangent.shape
    share, inner = rows // groups, low.shape[1]
    places = CORES
    line = pl.BlockSpec((1, 1, width), lambda j, o: (0, 0, 0))
    cot = lambda place: pl.BlockSpec((share, width), lambda j, o: (o[places * j + place], 0))
    return call(
        "shrink_back",
        functools.partial(shrink_back_kernel, places),
        (*[cotangent] * places, low, squares, magnitude),
        (groups // places,),
        [cot(place) for place in range(places)]
        + [pl.BlockSpec((1, inner, width), lambda j, o: (0, 0, 0)), line, line],
        [
            pl.BlockSpec((places, share, inner), lambda j, o: (j, 0, 0)),
            pl.BlockSpec((places, share, width), lambda j, o: (j, 0, 0)),
        ],
        [shape((groups, share, inner), LOW), shape((groups, share, width), LOW)],
        scratch=[pltpu.VMEM((places * share, width), LOW)],
        prefetch=(order,),
        flops=2 * rows * width * inner,
    )


def expand_kernel(step, first, last, n_totals, *refs):
    mine_ref, low_ref, grad_ref, squares_ref, magnitude_ref = refs[:5]
    refs = list(refs[5:])
    left_ref = refs.pop(0) if first else None
    right_ref = refs.pop(0) if last else None
    before = [refs.pop(0) for _ in range(n_totals)]
    product_ref, back_ref, rows_ref, total_ref, joined_ref = refs[:5]
    refs = refs[5:]
    across_ref = refs.pop(0) if first else None
    extra_ref = refs.pop(0) if last else None
    rows_all, low_all, grad_all, product_all, back_all, sent, got, in_sems, out_sems, send_sems, recv_sems = refs
    share, depth = mine_ref.shape
    sibling = sibling_id()
    greet([sibling])
    both = CORES * share
    width, ff = low_ref.shape[2], magnitude_ref.shape[1]
    tile = 256
    cuts = [slice(at, at + tile) for at in range(0, width, tile)]

    mine_copy = pltpu.make_async_copy(mine_ref, rows_all.at[pl.ds(share, share), :], in_sems.at[0])
    other_copy = remote(
        mine_ref,
        rows_all.at[pl.ds(0, share), :],
        send_sems.at[sent.shape[0]],
        recv_sems.at[sent.shape[0]],
        sibling,
    )
    tile_copies = []
    for n, cut in enumerate(cuts):
        lanes = pl.ds(cut.start, tile)
        tile_copies.append(
            [
                pltpu.make_async_copy(
                    low_ref.at[:, :, lanes], low_all.at[:, :, lanes], in_sems.at[2 + 2 * n]
                ),
                pltpu.make_async_copy(
                    grad_ref.at[pl.ds(CORES * step, CORES), :, lanes],
                    grad_all.at[:, :, lanes],
                    in_sems.at[3 + 2 * n],
                ),
            ]
        )
    mine_copy.start()
    for copy in tile_copies[0]:
        copy.start()
    greeted(1)
    other_copy.start()
    for copies in tile_copies[1:]:
        for copy in copies:
            copy.start()
    if first:
        rank = across_ref.shape[1]
        for m in range(2):
            rows_all[both + m * rank : both + (m + 1) * rank, :] = left_ref[m].astype(LOW)
    mine_copy.wait()
    other_copy.wait_recv()
    out_copies = [
        pltpu.make_async_copy(rows_all.at[pl.ds(0, both), :], rows_ref, out_sems.at[2 * len(cuts)])
    ]
    out_copies[0].start()
    lane = lax.broadcasted_iota(jnp.int32, (1, tile), 1)
    for n, cut in enumerate(cuts):
        for copy in tile_copies[n]:
            copy.wait()
        size = min(tile, ff - cut.start)
        pre = [dot(rows_all[...], low_all[m, :, cut]) for m in range(2)]
        if first:
            for m in range(2):
                rows = slice(both + m * rank, both + (m + 1) * rank)
                across_ref[m, :, cut.start : cut.start + size] = pre[m][rows, :size]
        magnitude, squares, scale = [], [], []
        for m in range(2):
            given = magnitude_ref[m : m + 1, cut.start : cut.start + size]
            if size < tile:
                given = jnp.concatenate([given, jnp.zeros((1, tile - size), F32)], axis=1)
            magnitude.append(given)
            squares.append(squares_ref[m, :, cut])
            scale.append(given / jnp.sqrt(squares[m]))
        sums = [jnp.zeros((1, tile), F32) for _ in range(2)]
        at = [slice(m * width + cut.start, m * width + cut.stop) for m in range(2)]
        for place in range(CORES):
            rows = slice(place * share, (place + 1) * share)
            gate_pre, up_pre = pre[0][rows], pre[1][rows]
            gate, up = gate_pre * scale[0], up_pre * scale[1]
            sigmoid = 0.5 + 0.5 * jnp.tanh(0.5 * gate)
            active = gate * sigmoid
            product_all[rows, cut] = (active * up).astype(LOW)
            upper = grad_all[place, :, cut].astype(F32)
            grad_up = upper * active
            grad_gate = upper * up * sigmoid * (1.0 + gate * (1.0 - sigmoid))
            sums[0] += jnp.sum(grad_gate * gate_pre, axis=0, keepdims=True)
            sums[1] += jnp.sum(grad_up * up_pre, axis=0, keepdims=True)
            back_all[rows, at[0]] = (grad_gate * scale[0]).astype(LOW)
            back_all[rows, at[1]] = (grad_up * scale[1]).astype(LOW)
        for m in range(2):
            total_ref[m, :, cut] = sums[m]
        if last:
            rank = extra_ref.shape[1]
            for m in range(2):
                total = sums[m]
                for ref in before:
                    total = total + ref[m, :, cut]
                right = right_ref[m, :, cut.start : cut.start + size]
                if size < tile:
                    spare = jnp.zeros((rank, tile - size), F32)
                    right = jnp.concatenate([right, spare], axis=1)
                weighted = right * norm_weight(total, squares[m], magnitude[m])
                rows = slice(both + m * rank, both + (m + 1) * rank)
                back_all[rows, at[m]] = weighted.astype(LOW)
                back_all[rows, at[1 - m]] = jnp.zeros((rank, tile), LOW)
    for m in range(2):
        lanes = pl.ds(m * width, width)
        copy = pltpu.make_async_copy(
            back_all.at[pl.ds(0, both), lanes], back_ref.at[m], out_sems.at[m]
        )
        copy.start()
        out_copies.append(copy)
    copy = pltpu.make_async_copy(product_all, product_ref, out_sems.at[2])
    copy.start()
    out_copies.append(copy)
    chunk = sent.shape[2]
    copies = [
        remote(sent.at[n], got.at[n], send_sems.at[n], recv_sems.at[n], sibling)
        for n in range(depth // chunk)
    ]

    def add(n):
        columns = slice(n * chunk, (n + 1) * chunk)
        copies[n].wait_recv()
        total = joined_ref[:, columns].astype(F32) + got[n].astype(F32)
        joined_ref[:, columns] = total.astype(LOW)

    for n in range(depth // chunk):
        columns = slice(n * chunk, (n + 1) * chunk)
        result = dot(back_all[:, :width], low_all[0, columns, :], NT)
        result = result + dot(back_all[:, width:], low_all[1, columns, :], NT)
        sent[n] = result[:share].astype(LOW)
        joined_ref[:, columns] = result[share:both].astype(LOW)
        copies[n].start()
        if n > 0:
            add(n - 1)
        if last:
            for m in range(2):
                extra_ref[m, :, columns] = result[both + m * rank : both + (m + 1) * rank]
    add(len(copies) - 1)
    for copy in out_copies:
        copy.wait()
    for copy in [other_copy, *copies]:
        copy.wait_send()


def expand(identity, mine, low, squares, magnitude, grad_product, step, left=None, right=None, before=()):
    share, depth = mine.shape
    width = low.shape[2]
    first, last = left is not None, right is not None
    rows = CORES * share
    hbm = pl.BlockSpec(memory_space=pl.ANY)
    fixed = lambda dims: pl.BlockSpec(tuple(dims), lambda i: (0,) * len(dims))
    operands = [mine, low, grad_product, squares, magnitude]
    in_specs = [hbm, hbm, hbm, fixed(squares.shape), fixed(magnitude.shape)]
    out_shape = [
        shape((rows, width), LOW),
        shape((2, rows, width), LOW),
        shape((rows, depth), LOW),
        shape((2, 1, width), F32),
        shape((share, depth), LOW),
    ]
    out_specs = [hbm, hbm, hbm] + [fixed(v.shape) for v in out_shape[3:]]
    extra_in = extra_out = 0
    if first:
        rank = left.shape[1]
        extra_in = 2 * rank
        operands.append(left)
        in_specs.append(fixed(left.shape))
        out_shape.append(shape((2, rank, magnitude.shape[1]), F32))
        out_specs.append(fixed(out_shape[-1].shape))
    if last:
        rank = right.shape[1]
        extra_out = 2 * rank
        operands += [right, *before]
        in_specs += [fixed(v.shape) for v in (right, *before)]
        out_shape.append(shape((2, rank, depth), F32))
        out_specs.append(fixed(out_shape[-1].shape))
    tiles, chunk = width // 256, tile_of(depth, 512)
    return call(
        "expand",
        functools.partial(expand_kernel, step, first, last, len(before)),
        tuple(operands),
        (1,),
        in_specs,
        out_specs,
        out_shape,
        scratch=[
            pltpu.VMEM((rows + extra_in, depth), LOW),
            pltpu.VMEM(low.shape, LOW),
            pltpu.VMEM((CORES, share, width), LOW),
            pltpu.VMEM((rows, width), LOW),
            pltpu.VMEM((rows + extra_out, 2 * width), LOW),
            pltpu.VMEM((depth // chunk, share, chunk), LOW),
            pltpu.VMEM((depth // chunk, share, chunk), LOW),
            pltpu.SemaphoreType.DMA((2 + 2 * tiles,)),
            pltpu.SemaphoreType.DMA((2 * tiles + 1,)),
            pltpu.SemaphoreType.DMA((depth // chunk + 1,)),
            pltpu.SemaphoreType.DMA((depth // chunk + 1,)),
        ],
        flops=8 * rows * depth * width,
        identity=identity,
    )


def adapter_kernel(plan, n_inputs, n_grads, corrections, n_before, order_ref, *refs):
    count = n_inputs + n_grads
    sources, held, sems = refs[:count], refs[-count - 1 : -1], refs[-1]
    left_ref, right_ref = refs[count : count + 2]
    *corrected, left_out, right_out = refs[count + 2 : -count - 1]
    members, rank, width = right_ref.shape
    chunks = list(plan(order_ref, held[:n_inputs], held[n_inputs:]))
    copies, used = [], 0
    for parts, _, _ in chunks:
        copies.append([])
        for which, index in parts:
            copies[-1].append(
                pltpu.make_async_copy(
                    sources[which].at[index], held[which].at[index], sems.at[used]
                )
            )
            used += 1
    for copy in copies[0]:
        copy.start()
    left_rows = jnp.concatenate([split_rows(left_ref[m]) for m in range(members)], axis=0)
    right_rows = [split_rows(right_ref[m]) for m in range(members)]
    before, corrected = corrected[:n_before], corrected[n_before:]
    for out, ref in zip((left_out, right_out), before or (None, None)):
        out[...] = jnp.zeros_like(out) if ref is None else ref[...]
    for n, (_, taken_of, grads_of) in enumerate(chunks):
        for copy in copies[n]:
            copy.wait()
        for copy in copies[n + 1] if n + 1 < len(chunks) else ():
            copy.start()
        taken = taken_of()
        across = dot(left_rows, taken, NT)
        downs = []
        for m in range(members):
            grad = grads_of(m)
            mine = split_rows(fold(across[2 * rank * m : 2 * rank * (m + 1)]))
            right_out[m] += fold(dot(mine, grad))
            downs.append(split_rows(fold(dot(right_rows[m], grad, NT))))
        left = dot(jnp.concatenate(downs, axis=0), taken)
        for m in range(members):
            left_out[m] += fold(left[2 * rank * m : 2 * rank * (m + 1)])
    if corrections:
        correct(corrections, right_ref, left_out, right_out, left_out, right_out, *corrected)


def correct(n_totals, right_ref, left_in, right_in, left_out, right_out, *refs):
    back_ref, across_ref, squares_ref, magnitude_ref = refs[:4]
    totals, magnitude_out = refs[4 : 4 + n_totals], refs[4 + n_totals]
    members, rank, width = right_ref.shape
    total = sum_refs(totals)[:, :, :width]
    squares = squares_ref[:, :, :width]
    magnitude_out[...] = total / jnp.sqrt(squares)
    for m in range(members):
        weight = norm_weight(total[m], squares[m], magnitude_ref[m : m + 1])
        if back_ref.dtype == LOW:
            low = back_ref[m, : left_in.shape[2], :]
            back = fold(dot(split_rows(right_ref[m] * weight), low, NT))
        else:
            back = back_ref[m]
        left_out[m] = ADAPT_SCALE * (left_in[m] - back)
        right_out[m] = ADAPT_SCALE * (right_in[m] - across_ref[m][:, :width] * weight)


def correct_kernel(n_totals, order_ref, right_ref, left_in, right_in, *refs):
    *rest, left_out, right_out = refs
    correct(n_totals, right_ref, left_in, right_in, left_out, right_out, *rest)


def correct_kernel(n_totals, right_ref, left_in, right_in, *refs):
    *rest, left_out, right_out = refs
    correct(n_totals, right_ref, left_in, right_in, left_out, right_out, *rest)


def corrected(name, sums, right, correction):
    members, rank, width = right.shape
    *given, totals = correction
    operands = (right, *sums, *given, *totals)
    outs = [(members, 1, width), sums[0].shape, sums[1].shape]
    full = lambda dims: pl.BlockSpec(tuple(dims), lambda i: (0,) * len(dims))
    return call(
        name,
        functools.partial(correct_kernel, len(totals)),
        operands,
        (1,),
        [full(v.shape) for v in operands],
        [full(dims) for dims in outs],
        [shape(dims, F32) for dims in outs],
        flops=sum(v.size for v in operands) * 64,
    )


def adapter(name, order, plan, inputs, grads, left, right, correction=None, before=()):
    members, rank, width = right.shape
    moved, fixed, n_totals = [*inputs, *grads], [left, right, *before], 0
    outs = [(members, rank, left.shape[2]), (members, rank, width)]
    if correction is not None:
        *given, totals = correction
        n_totals = len(totals)
        fixed += [*given, *totals]
        outs = [(members, 1, width)] + outs
    full = lambda dims: pl.BlockSpec(tuple(dims), lambda i, o: (0,) * len(dims))
    kernel = functools.partial(
        adapter_kernel, plan, len(inputs), len(grads), n_totals, len(before)
    )
    return call(
        name,
        kernel,
        (*moved, *fixed),
        (1,),
        [pl.BlockSpec(memory_space=pl.ANY) for _ in moved] + [full(v.shape) for v in fixed],
        [full(dims) for dims in outs],
        [shape(dims, F32) for dims in outs],
        scratch=[pltpu.VMEM(v.shape, v.dtype) for v in moved] + [pltpu.SemaphoreType.DMA((32,))],
        prefetch=(order,),
        flops=sum(v.size for v in moved) * 64,
    )


def copy_kernel(count, *refs):
    copies = [
        pltpu.make_async_copy(refs[i], refs[count + i], refs[-1].at[i]) for i in range(count)
    ]
    for copy in copies:
        copy.start()
    for copy in copies:
        copy.wait()


def copy_out(arrays):
    anywhere = pl.BlockSpec(memory_space=pl.ANY)
    return call(
        "copy_out",
        functools.partial(copy_kernel, len(arrays)),
        tuple(arrays),
        (1,),
        [anywhere for _ in arrays],
        [anywhere for _ in arrays],
        [shape(v.shape, F32) for v in arrays],
        scratch=[pltpu.SemaphoreType.DMA((len(arrays),))],
    )


GRAIN = 16


def pieces_of(width):
    return [(at, min(128, width - at)) for at in range(0, width, 128)]


def cells_of(blocks, lines, parts):
    cells, rows = [], []
    for n, block in enumerate(blocks):
        for m in range(block.shape[0]):
            for at, size in pieces_of(block.shape[2] // parts):
                cells.append((n, m, at, size))
    for n, line in enumerate(lines):
        for m in range(line.shape[0]):
            for at, size in pieces_of(line.shape[2] // parts):
                rows.append((n, m, at, size))
    return cells, rows


def pack(blocks, lines, wide_ref, part, parts, cells, rows):
    for i, (n, m, at, size) in enumerate(cells):
        start = part * (blocks[n].shape[2] // parts) + at
        wide_ref[part, i, :, :size] = blocks[n][m, :, start : start + size]
    for i, (n, m, at, size) in enumerate(rows):
        start = part * (lines[n].shape[2] // parts) + at
        cell, row = len(cells) + i // GRAIN, i % GRAIN
        wide_ref[part, cell, row : row + 1, :size] = lines[n][m, :, start : start + size]


def unpack(full_ref, blocks, lines, part, parts, cells, rows):
    for i, (n, m, at, size) in enumerate(cells):
        start = part * (blocks[n].shape[2] // parts) + at
        blocks[n][m, :, start : start + size] = full_ref[part, i].astype(F32)[:, :size]
    for i, (n, m, at, size) in enumerate(rows):
        start = part * (lines[n].shape[2] // parts) + at
        cell, row = len(cells) + i // GRAIN, i % GRAIN
        values = full_ref[part, cell].astype(F32)
        lines[n][m, :, start : start + size] = values[row : row + 1, :size]


def reduce_kernel(groups, lines, counts, *refs):
    n_all, n_all_lines, n_dp, n_dp_lines = counts
    count = sum(counts)
    taken, given, scratch = refs[:count], refs[count : 2 * count], refs[2 * count :]
    ends = [n_all, n_all + n_all_lines, n_all + n_all_lines + n_dp]
    parted = lambda v: (v[: ends[0]], v[ends[0] : ends[1]], v[ends[1] : ends[2]], v[ends[2] :])
    all_out, all_lines_out, dp_out, dp_lines_out = parted(given)
    (
        all_ref,
        line_ref,
        all_low,
        line_low,
        all_got,
        part,
        part_low,
        part_got,
        line_got,
        all_full,
        line_full,
        *sems,
    ) = scratch
    held, in_sems, sems = sems[:count], sems[count], sems[count + 1 :]
    loads = [
        pltpu.make_async_copy(source, target, in_sems.at[i])
        for i, (source, target) in enumerate(zip(taken, held))
    ]
    for load in loads:
        load.start()
    me, row = lax.axis_index("mp"), lax.axis_index("dp")
    piece, line_piece = part.shape[0] // lines, line_ref.shape[1] // lines
    mp_peer = [lax.rem(me + k, groups) for k in range(groups)]
    dp_peer = [lax.rem(row + k, lines) for k in range(lines)]
    barrier = pltpu.get_barrier_semaphore()
    for k in range(1, groups):
        pl.semaphore_signal(barrier, 1, device_id={"mp": mp_peer[k]}, device_id_type=MESH_IDS)
    for k in range(1, lines):
        pl.semaphore_signal(barrier, 1, device_id={"dp": dp_peer[k]}, device_id_type=MESH_IDS)
    all_in, all_lines_in, dp_in, dp_lines_in = parted(held)
    all_cells = cells_of(all_in, all_lines_in, groups)
    dp_cells = cells_of(dp_in, dp_lines_in, 1)
    all_ref[...] = jnp.zeros_like(all_ref)
    line_ref[...] = jnp.zeros_like(line_ref)
    for load in loads:
        load.wait()
    for q in range(groups):
        pack(all_in, all_lines_in, all_ref, q, groups, *all_cells)
    pack(dp_in, dp_lines_in, line_ref, 0, 1, *dp_cells)
    all_low[...] = all_ref[...].astype(LOW)
    line_low[...] = line_ref[...].astype(LOW)
    pl.semaphore_wait(barrier, groups + lines - 2)

    def send(source, target, stage, k, axis, peer):
        copy = pltpu.make_async_remote_copy(
            src_ref=source,
            dst_ref=target,
            send_sem=sems[2 * stage].at[k],
            recv_sem=sems[2 * stage + 1].at[k],
            device_id={axis: peer},
            device_id_type=MESH_IDS,
        )
        copy.start()
        return copy

    over_mp = [
        send(all_low.at[mp_peer[k]], all_got.at[k], 0, k, "mp", mp_peer[k])
        for k in range(1, groups)
    ]
    over_dp = [
        send(
            line_low.at[0, pl.ds(dp_peer[k] * line_piece, line_piece)],
            line_got.at[k],
            1,
            k,
            "dp",
            dp_peer[k],
        )
        for k in range(1, lines)
    ]
    total = all_ref[me]
    for k, copy in enumerate(over_mp, 1):
        copy.wait_recv()
        total = total + all_got[k].astype(F32)
    part[...] = total
    part_low[...] = total.astype(LOW)
    part_dp = [
        send(part_low.at[pl.ds(dp_peer[k] * piece, piece)], part_got.at[k], 2, k, "dp", dp_peer[k])
        for k in range(1, lines)
    ]
    held = pl.ds(row * piece, piece)
    total = part[held]
    for k, copy in enumerate(part_dp, 1):
        copy.wait_recv()
        total = total + part_got[k].astype(F32)
    all_full[me, held] = total.astype(LOW)
    part_back = [
        send(all_full.at[me, held], all_full.at[me, held], 4, k, "dp", dp_peer[k])
        for k in range(1, lines)
    ]
    mine = pl.ds(row * line_piece, line_piece)
    total = line_ref[0, mine]
    for k, copy in enumerate(over_dp, 1):
        copy.wait_recv()
        total = total + line_got[k].astype(F32)
    line_full[0, mine] = total.astype(LOW)
    line_back = [
        send(line_full.at[0, mine], line_full.at[0, mine], 3, k, "dp", dp_peer[k])
        for k in range(1, lines)
    ]
    for copy in part_back:
        copy.wait_recv()
    all_back = [
        send(all_full.at[me], all_full.at[me], 5, k, "mp", mp_peer[k]) for k in range(1, groups)
    ]
    for copy in line_back:
        copy.wait_recv()
    unpack(line_full, dp_out, dp_lines_out, 0, 1, *dp_cells)
    for copy in all_back:
        copy.wait_recv()
    for q in range(groups):
        unpack(all_full, all_out, all_lines_out, q, groups, *all_cells)
    for copy in over_mp + over_dp + part_dp + line_back + part_back + all_back:
        copy.wait_send()


def reduce_devices(name, identity, over_all, over_all_lines, over_dp, over_dp_lines):
    groups, lines = lax.axis_size("mp"), lax.axis_size("dp")

    def size_of(blocks, rows, parts):
        cells, lines_in = cells_of(blocks, rows, parts)
        size = len(cells) + -(-len(lines_in) // GRAIN)
        return -(-size // lines) * lines

    count, line_count = size_of(over_all, over_all_lines, groups), size_of(over_dp, over_dp_lines, 1)
    operands = (*over_all, *over_all_lines, *over_dp, *over_dp_lines)
    counts = (len(over_all), len(over_all_lines), len(over_dp), len(over_dp_lines))
    vmem = pl.BlockSpec(memory_space=pltpu.VMEM)
    tail = (GRAIN, 128)
    sizes = (groups, lines, lines, lines, lines, groups)
    every, line = (groups, count) + tail, (1, line_count) + tail
    results = pl.pallas_call(
        functools.partial(reduce_kernel, groups, lines, counts),
        name=name,
        out_shape=[shape(v.shape, F32) for v in operands],
        in_specs=[pl.BlockSpec(memory_space=pl.ANY) for _ in operands],
        out_specs=[vmem for _ in operands],
        scratch_shapes=[
            pltpu.VMEM(every, F32),
            pltpu.VMEM(line, F32),
            pltpu.VMEM(every, LOW),
            pltpu.VMEM(line, LOW),
            pltpu.VMEM(every, LOW),
            pltpu.VMEM((count,) + tail, F32),
            pltpu.VMEM((count,) + tail, LOW),
            pltpu.VMEM((lines, count // lines) + tail, LOW),
            pltpu.VMEM((lines, line_count // lines) + tail, LOW),
            pltpu.VMEM(every, LOW),
            pltpu.VMEM(line, LOW),
        ]
        + [pltpu.VMEM(v.shape, F32) for v in operands]
        + [pltpu.SemaphoreType.DMA((len(operands),))]
        + [pltpu.SemaphoreType.DMA((n,)) for n in sizes for _ in range(2)],
        compiler_params=pltpu.CompilerParams(
            collective_id=identity, has_side_effects=True, vmem_limit_bytes=62 * 2**20
        ),
        cost_estimate=pl.CostEstimate(flops=1000, bytes_accessed=2**20, transcendentals=0),
    )(*operands)
    return copy_out(results)


def body(
    tokens,
    cotangent,
    segment_ids,
    attend_gain,
    expand_gain,
    heads_base,
    heads_left,
    heads_right,
    heads_magnitude,
    output_base,
    output_left,
    output_right,
    output_magnitude,
    expand_base,
    expand_left,
    expand_right,
    expand_magnitude,
    shrink_base,
    shrink_left,
    shrink_right,
    shrink_magnitude,
):
    groups = lax.axis_size("mp")
    chips = groups // CORES
    index = lax.axis_index("mp")
    chip, core = index // CORES, index % CORES
    rows, width = tokens.shape
    share = rows // groups
    local_heads, ff = heads_base.shape[2], expand_base.shape[2]
    ff_wide = padded(ff)
    device = jnp.arange(groups, dtype=jnp.int32)
    order = jnp.concatenate(
        [
            (chip + device // CORES) % chips * CORES + (core + 1 + device) % CORES,
            (device // CORES + chips - chip) % chips * CORES + (device + CORES - core + 1) % CORES,
        ]
    ).astype(jnp.int32)

    def tie(*values):
        return lax.optimization_barrier(values)

    def sibling(values):
        return lax.ppermute(
            values, "mp", [(i, i // CORES * CORES + (i + 1) % CORES) for i in range(groups)]
        )

    def to_chip(values, step):
        return lax.ppermute(
            values,
            "mp",
            [((i, ((i // CORES + step) % chips) * CORES + i % CORES)) for i in range(groups)],
        )

    def join(pair):
        return (pair[1].astype(F32) + sibling(pair[0]).astype(F32)).astype(LOW)

    def chip_pairs(places):
        return [places[CORES * step : CORES * (step + 1)] for step in range(chips)]

    def arrive(own):
        return [to_chip(own, chips - step) for step in range(1, chips)]

    def pairs_of(own, near_sibling, arrived):
        return [(near_sibling, own)] + [(sibling(piece), piece) for piece in arrived]

    def in_pairs(order_ref, inputs, grads):
        for step, (taken, grad) in enumerate(zip(inputs, grads)):
            for place in range(CORES):
                rows = pl.ds(place * share, share)
                yield (
                    [(step, rows), (chips + step, (slice(None), rows))],
                    lambda taken=taken, rows=rows: taken[rows, :],
                    lambda m, grad=grad, rows=rows: grad[m, rows, :ff],
                )

    def in_shrink(order_ref, inputs, grads):
        for step, taken in enumerate(inputs):
            for place in range(CORES):
                rows = pl.ds(place * share, share)
                at = CORES * step + place
                yield (
                    [(step, rows), (chips, at)],
                    lambda taken=taken, rows=rows: taken[rows, :ff],
                    lambda m, at=at: grads[0][at],
                )

    def in_output(start):
        def plan(order_ref, inputs, grads):
            for n, grad in enumerate(grads):
                yield (
                    [(0, (0, start + n)), (1 + n, ...)],
                    lambda place=start + n: inputs[0][0, place],
                    lambda m, grad=grad: grad[...],
                )

        return plan

    def in_heads(order_ref, inputs, grads):
        for place in range(groups):
            at = pl.multiple_of(order_ref[place] * share, share)
            rows = pl.ds(place * share, share)
            yield (
                [(0, pl.ds(at, share)), (1, (slice(None), rows))],
                lambda at=at: inputs[0][pl.ds(at, share), :],
                lambda m, rows=rows: grads[0][m, rows, :],
            )

    heads_rows, output_rows = turned(heads_left), turned(output_left[None])
    expand_rows, shrink_rows = turned(expand_left), turned(shrink_left[None])
    heads_mag, output_mag = heads_magnitude, output_magnitude[None]
    expand_mag, shrink_mag = expand_magnitude, shrink_magnitude[None]
    attend_line, expand_line = attend_gain[None], expand_gain[None]

    output_low, shrink_low, squares_part = merge_pair(
        [(output_base, output_rows[0], output_right), (shrink_base, shrink_rows[0], shrink_right)]
    )
    output_low, shrink_low = output_low[None], shrink_low[None]
    (
        normed,
        heads_low,
        post,
        heads_sq,
        heads_across,
        cos_table,
        sine_table,
        squares,
        first,
    ) = project_heads(
        tokens,
        attend_line,
        heads_base,
        heads_rows,
        heads_right,
        heads_mag,
        segment_ids,
        squares_part,
        groups,
    )
    heads_out = attend(order, groups, post, first)
    output_sq, shrink_sq = squares[None, :1], squares[None, 1:]
    heads_parts = heads_out.reshape(1, groups, share, local_heads)
    joined, output_across = product(
        "output_product", 3, heads_parts, output_low, NN, left=output_rows
    )
    joined, expand_right_tied = tie(joined, expand_right)
    output_parts = [joined[0]] + [to_chip(joined[step], step) for step in range(1, chips)]
    expand_low, expand_sq = merge(
        expand_base, expand_rows, expand_right_tied, 1024, expand_base.shape[2]
    )
    grad_product, shrink_grad = shrink_back(
        order, cotangent, shrink_low, shrink_sq, shrink_mag[None], groups
    )
    output_parts, expand_low, grad_product = tie(output_parts, expand_low, grad_product)
    hidden, normed_own = row_call(
        "hidden",
        hidden_kernel,
        order,
        [(tokens, True)] + [(part, False) for part in output_parts],
        (output_sq[0], output_mag, expand_line),
        (F32, LOW),
        0,
        scale_first,
    )

    def feed(mine, step, **extra):
        return expand(
            4 + step, mine, expand_low, expand_sq, expand_mag, grad_product, step, **extra
        )

    arrived = arrive(normed_own)
    fed = [feed(normed_own, 0, left=expand_rows)]
    arrived, fed = tie(arrived, fed)
    fed = list(fed)
    for step in range(1, chips):
        extra = {}
        if step == chips - 1:
            extra = {"right": expand_right, "before": [f[3] for f in fed]}
        fed.append(feed(arrived[step - 1], step, **extra))
    expand_totals = [f[3] for f in fed]
    joined, shrink_rows_tied = tie([f[4] for f in fed], shrink_rows)
    mid_parts = [joined[0]] + [to_chip(joined[step], step) for step in range(1, chips)]
    shrink_places, shrink_total, shrink_across = shrink_product(
        order, [f[0] for f in fed], shrink_low, shrink_rows_tied, cotangent
    )
    shrink_pairs = chip_pairs(shrink_places)
    expand_adapter = adapter(
        "expand_adapter",
        order,
        in_pairs,
        [f[2] for f in fed],
        [f[1] for f in fed],
        expand_rows,
        expand_right,
        (fed[-1][5], fed[0][5], expand_sq, expand_mag, expand_totals),
    )
    mid_parts, shrink_pairs, expand_adapter = tie(mid_parts, shrink_pairs, expand_adapter)
    grad_hidden, output_grad_own, output_total, expand_gain_part = row_call(
        "hidden_back",
        hidden_back_kernel,
        order,
        [(cotangent, True), (tokens, True), (hidden, False)]
        + [(part, False) for part in mid_parts],
        (output_sq[0], output_mag, expand_line),
        (F32, LOW),
        2,
        scale_first,
    )
    arrived, near_sibling = arrive(output_grad_own), sibling(output_grad_own)
    shrink_joined = [join(pair) for pair in shrink_pairs[1:]]
    shrink_joined, shrink_rows_tied = tie(shrink_joined, shrink_rows)
    shrink_sums = adapter(
        "shrink_adapter",
        order,
        in_shrink,
        [f[0] for f in fed],
        [shrink_grad],
        shrink_rows_tied,
        shrink_right[None],
    )
    output_sums = adapter(
        "output_near_adapter",
        order,
        in_output(0),
        [heads_parts],
        [near_sibling, output_grad_own],
        output_rows,
        output_right[None],
    )
    arrived, near_sibling, shrink_joined, shrink_sums, output_sums = tie(
        arrived, near_sibling, shrink_joined, shrink_sums, output_sums
    )
    output_grad = [
        piece for pair in pairs_of(output_grad_own, near_sibling, arrived) for piece in pair
    ]
    shrink_parts = [shrink_pairs[0][1], sibling(shrink_pairs[0][0])] + [
        to_chip(values, step) for step, values in enumerate(shrink_joined, 1)
    ]
    heads_grads, heads_total = attend_back(
        order,
        groups,
        post,
        first,
        cos_table,
        sine_table,
        heads_mag,
        heads_sq,
        output_low,
        output_grad,
    )
    grad_parts = heads_grads.reshape(3, groups, share, local_heads)
    joined, both_totals, token_extra = product(
        "normed_product",
        20,
        grad_parts,
        heads_low,
        NT,
        correction=(heads_right, heads_sq, heads_mag, [heads_total]),
        lines=(output_total, shrink_total),
    )
    joined, shrink_parts, heads_rows_tied, output_rows_tied = tie(
        joined, shrink_parts, heads_rows, output_rows
    )
    output_total, shrink_total = both_totals[:1], both_totals[1:]
    token_parts = [joined[0]] + [to_chip(joined[step], step) for step in range(1, chips)]
    output_adapter = adapter(
        "output_far_adapter",
        order,
        in_output(CORES),
        [heads_parts],
        output_grad[CORES:],
        output_rows_tied,
        output_right[None],
        (output_low, output_across, output_sq, output_mag, [output_total[None]]),
        output_sums,
    )
    shrink_adapter = corrected(
        "shrink_correct",
        shrink_sums,
        shrink_right[None],
        (shrink_low, shrink_across, shrink_sq, shrink_mag, [shrink_total[None]]),
    )
    heads_adapter = adapter(
        "heads_adapter",
        order,
        in_heads,
        [normed],
        [heads_grads],
        heads_rows_tied,
        heads_right,
        (token_extra, heads_across, heads_sq, heads_mag, [heads_total]),
    )
    (mixed,) = row_call(
        "mixed",
        mixed_kernel,
        order,
        [(hidden, False)] + [(part, False) for part in shrink_parts],
        (shrink_sq[0], shrink_mag),
        (LOW,),
        0,
        scale_first,
    )
    token_parts, output_adapter, shrink_adapter, heads_adapter, mixed = tie(
        token_parts, output_adapter, shrink_adapter, heads_adapter, mixed
    )
    grad_tokens, attend_gain_part = row_call(
        "token_back",
        token_back_kernel,
        order,
        [(tokens, True), (grad_hidden, False)] + [(part, False) for part in token_parts],
        (attend_line,),
        (F32,),
        1,
        lambda gain: (gain,),
    )
    (
        expand_left_grad,
        shrink_right_grad,
        heads_left_grad,
        output_right_grad,
        expand_gain_grad,
        attend_gain_grad,
        expand_right_grad,
        shrink_left_grad,
        heads_right_grad,
        output_left_grad,
        expand_mag_grad,
        shrink_mag_grad,
        heads_mag_grad,
        output_mag_grad,
    ) = reduce_devices(
        "reduce_gradients",
        1,
        [expand_adapter[1], shrink_adapter[2], heads_adapter[1], output_adapter[2]],
        [expand_gain_part[None], attend_gain_part[None]],
        [expand_adapter[2], shrink_adapter[1], heads_adapter[2], output_adapter[1]],
        [expand_adapter[0], shrink_adapter[0], heads_adapter[0], output_adapter[0]],
    )
    return (
        mixed,
        grad_tokens,
        attend_gain_grad[0, 0],
        expand_gain_grad[0, 0],
        jnp.swapaxes(heads_left_grad, 1, 2),
        heads_right_grad,
        heads_mag_grad[:, 0],
        output_left_grad[0].T,
        output_right_grad[0],
        output_mag_grad[0, 0],
        jnp.swapaxes(expand_left_grad, 1, 2),
        expand_right_grad,
        expand_mag_grad[:, 0],
        shrink_left_grad[0].T,
        shrink_right_grad[0],
        shrink_mag_grad[0, 0],
    )


def solution(mesh):
    placed = (
        P("dp", None),
        P("dp", None),
        P("dp", None),
        P(),
        P(),
        P(None, None, "mp"),
        P(),
        P(None, None, "mp"),
        P(None, "mp"),
        P("mp", None),
        P("mp", None),
        P(),
        P(),
        P(None, None, "mp"),
        P(),
        P(None, None, "mp"),
        P(None, "mp"),
        P("mp", None),
        P("mp", None),
        P(),
        P(),
    )
    return jax.shard_map(
        body,
        mesh=mesh,
        in_specs=placed,
        out_specs=(
            P(("dp", "mp"), None),
            P(("dp", "mp"), None),
            P(),
            P(),
            P(),
            P(None, None, "mp"),
            P(None, "mp"),
            P("mp", None),
            P(),
            P(),
            P(),
            P(None, None, "mp"),
            P(None, "mp"),
            P("mp", None),
            P(),
            P(),
        ),
        check_vma=False,
    )
```

```python
import functools

import jax
import jax.numpy as jnp
import ml_dtypes
import numpy as np
from jax import lax
from jax.experimental import pallas as pl
from jax.experimental.pallas import tpu as pltpu
from jax.sharding import PartitionSpec as P

HEAD_DIM = 128
CORES = 2
LONGEST = 512
ATTEND_BLOCK = 256
ADAPT_SCALE = 2.0
NORM_EPS = 1e-05
ROPE_BASE = 10000.0
MASKED = -1e30

F32 = jnp.float32
LOW = jnp.bfloat16
NN = (((1,), (0,)), ((), ()))
NT = (((1,), (1,)), ((), ()))
TN = (((0,), (0,)), ((), ()))


MESH_IDS = pl.DeviceIdType.MESH


def sibling_id():
    me = lax.axis_index("mp")
    return me // CORES * CORES + lax.rem(me + 1, CORES)


def greet(peers):
    for peer in peers:
        pl.semaphore_signal(
            pltpu.get_barrier_semaphore(), 1, device_id={"mp": peer}, device_id_type=MESH_IDS
        )


def greeted(count):
    pl.semaphore_wait(pltpu.get_barrier_semaphore(), count)


def remote(source, target, send_sem, recv_sem, peer):
    return pltpu.make_async_remote_copy(
        src_ref=source,
        dst_ref=target,
        send_sem=send_sem,
        recv_sem=recv_sem,
        device_id={"mp": peer},
        device_id_type=MESH_IDS,
    )


def dot(left, right, dims=NN):
    return lax.dot_general(left, right, dims, preferred_element_type=F32)


def shape(dims, kind):
    return jax.ShapeDtypeStruct(tuple(dims), kind)


def call(name, kernel, operands, grid, in_specs, out_specs, out_shape, scratch=(), prefetch=(), flops=0, mib=63.5, identity=None):
    moved = sum(v.size * v.dtype.itemsize for v in operands)
    moved += sum(v.size * v.dtype.itemsize for v in out_shape)
    return pl.pallas_call(
        kernel,
        name=name,
        out_shape=out_shape,
        grid_spec=pltpu.PrefetchScalarGridSpec(
            num_scalar_prefetch=len(prefetch),
            grid=grid,
            in_specs=in_specs,
            out_specs=out_specs,
            scratch_shapes=scratch,
        ),
        compiler_params=pltpu.CompilerParams(
            vmem_limit_bytes=int(mib * 2**20), collective_id=identity, has_side_effects=identity is not None
        ),
        cost_estimate=pl.CostEstimate(flops=flops // 16, bytes_accessed=moved // 16, transcendentals=0),
    )(*prefetch, *operands)


def tile_of(size, most):
    return most if size % most == 0 else size


def split_rows(values):
    top = values.astype(LOW)
    rest = (values - top.astype(F32)).astype(LOW)
    return jnp.concatenate([top, rest], axis=0)


def turned(left_map):
    return jnp.swapaxes(left_map, -1, -2)


def norm_weight(total, squares, magnitude):
    norm = jnp.sqrt(squares)
    return total * magnitude / (norm * norm * norm)


def sum_refs(refs):
    total = refs[0][...]
    for ref in refs[1:]:
        total = total + ref[...]
    return total


def fold(values):
    half = values.shape[0] // 2
    return values[:half] + values[half:]


def merge_tile(base_at, low_put, left, right, depth):
    rank = right.shape[0]
    doubled = ADAPT_SCALE * right
    top = doubled.astype(LOW)
    rest = (doubled - top.astype(F32)).astype(LOW)
    right_stack = jnp.concatenate([top, rest, top], axis=0)
    left_pair = split_rows(left)
    left_stack = jnp.concatenate([left_pair[:rank], left_pair[:rank], left_pair[rank:]], axis=0)
    width = right.shape[1]
    wide = 256 if width == 512 else width
    step = tile_of(depth, 1024)
    squares = []
    for at in range(0, width, wide):
        columns = slice(at, at + wide)
        total = jnp.zeros((1, wide), F32)
        for start in range(0, depth, step):
            merged = base_at(start, step, columns).astype(F32) + dot(
                left_stack[:, start : start + step], right_stack[:, columns], TN
            )
            low_put(start, step, columns, merged.astype(LOW))
            total = total + jnp.sum(merged * merged, axis=0, keepdims=True)
        squares.append(total)
    return jnp.concatenate(squares, axis=1)


def merge_pair_kernel(*refs):
    for n in range(2):
        base_ref, left_ref, right_ref = refs[3 * n : 3 * n + 3]
        low_ref, squares_ref = refs[6 + n], refs[8]
        depth = base_ref.shape[0]
        if low_ref.shape[0] > depth:
            low_ref[depth:, :] = jnp.zeros((low_ref.shape[0] - depth, low_ref.shape[1]), LOW)

        def put(start, step, columns, tile, low_ref=low_ref):
            low_ref[start : start + step, columns] = tile

        squares_ref[n : n + 1, :] = merge_tile(
            lambda start, step, columns, base_ref=base_ref: base_ref[start : start + step, columns],
            put,
            left_ref[...],
            right_ref[...],
            depth,
        )


def merge_pair(triples):
    operands, in_specs, low_specs, low_shapes = [], [], [], []
    width = triples[0][0].shape[1]
    wide = tile_of(width, 512)
    for base, left, right in triples:
        depth, rank = base.shape[0], right.shape[0]
        operands += [base, left, right]
        in_specs += [
            pl.BlockSpec((depth, wide), lambda n: (0, n)),
            pl.BlockSpec((rank, depth), lambda n: (0, 0)),
            pl.BlockSpec((rank, wide), lambda n: (0, n)),
        ]
        low_specs.append(pl.BlockSpec((padded(depth), wide), lambda n: (0, n)))
        low_shapes.append(shape((padded(depth), width), LOW))
    return call(
        "merge_pair",
        merge_pair_kernel,
        tuple(operands),
        (width // wide,),
        in_specs,
        low_specs + [pl.BlockSpec((2, wide), lambda n: (0, n))],
        low_shapes + [shape((2, width), F32)],
        flops=2 * sum(v.size for v in operands) * 256,
    )


def merge_kernel(base_ref, left_ref, right_ref, low_ref, squares_ref):
    depth, width = base_ref.shape[1:]
    if low_ref.shape[1] > depth:
        low_ref[0, depth:, :] = jnp.zeros((low_ref.shape[1] - depth, low_ref.shape[2]), LOW)
    if low_ref.shape[2] > width:
        spare = low_ref.shape[2] - width
        low_ref[0, :, width:] = jnp.zeros((low_ref.shape[1], spare), LOW)
        squares_ref[0, :, width:] = jnp.ones((1, spare), F32)

    def put(start, step, columns, tile):
        low_ref[0, start : start + step, columns] = tile

    squares = merge_tile(
        lambda start, step, columns: base_ref[0, start : start + step, columns],
        put,
        left_ref[0],
        right_ref[0],
        depth,
    )

    @pl.when(pl.program_id(2) == 0)
    def _():
        squares_ref[0, :, :width] = squares

    @pl.when(pl.program_id(2) > 0)
    def _():
        squares_ref[0, :, :width] += squares


def padded(size):
    return -(-size // 256) * 256


def pad_last(values, size):
    return jnp.pad(values, [(0, 0)] * (values.ndim - 1) + [(0, size - values.shape[-1])])


def merge(base, left, right, deep, wide):
    members, depth, width = base.shape
    low_deep = padded(deep) if deep == depth else deep
    low_wide = padded(wide) if wide == width else wide
    low_shape = (members, depth // deep * low_deep, width // wide * low_wide)
    rank = right.shape[1]
    return call(
        "merge",
        merge_kernel,
        (base, left, right),
        (members, width // wide, depth // deep),
        [
            pl.BlockSpec((1, deep, wide), lambda m, n, k: (m, k, n)),
            pl.BlockSpec((1, rank, deep), lambda m, n, k: (m, 0, k)),
            pl.BlockSpec((1, rank, wide), lambda m, n, k: (m, 0, n)),
        ],
        [
            pl.BlockSpec((1, low_deep, low_wide), lambda m, n, k: (m, k, n)),
            pl.BlockSpec((1, 1, low_wide), lambda m, n, k: (m, 0, n)),
        ],
        [shape(low_shape, LOW), shape((members, 1, low_shape[2]), F32)],
        flops=2 * members * depth * width * 256,
    )


def rms_rows(values):
    return lax.rsqrt(jnp.mean(values * values, axis=1, keepdims=True) + NORM_EPS)


TABLE_STEP = 32


def table_pieces(places):
    half = np.arange(HEAD_DIM) % (HEAD_DIM // 2)
    angles = np.asarray(places)[:, None] * ROPE_BASE ** (-2.0 * half / HEAD_DIM)[None, :]
    rest = np.concatenate([np.cos(angles), np.sin(angles)], axis=1)
    pieces = []
    for _ in range(3):
        pieces.append(rest.astype(ml_dtypes.bfloat16))
        rest = rest - pieces[-1].astype(np.float64)
    return jnp.asarray(np.concatenate(pieces, axis=0))


def rotation(first, coarse, fine):
    rows = first.shape[0]
    position = lax.broadcasted_iota(jnp.int32, (rows, 1), 0) - first
    lane = lax.broadcasted_iota(jnp.int32, (rows, 3 * TABLE_STEP), 1) % TABLE_STEP
    pick = lambda place, table: dot((lane == place).astype(F32).astype(LOW), table)
    high = pick(position // TABLE_STEP, coarse)
    small = pick(position % TABLE_STEP, fine)
    cos_a, sin_a = high[:, :HEAD_DIM], high[:, HEAD_DIM:]
    cos_b, sin_b = small[:, :HEAD_DIM], small[:, HEAD_DIM:]
    sine = sin_a * cos_b + cos_a * sin_b
    left_half = lax.broadcasted_iota(jnp.int32, sine.shape, 1) < HEAD_DIM // 2
    return cos_a * cos_b - sin_a * sin_b, jnp.where(left_half, -sine, sine)


def heads_kernel(
    token_ref,
    gain_ref,
    base_ref,
    left_ref,
    right_ref,
    magnitude_ref,
    segment_ref,
    coarse_ref,
    fine_ref,
    part_ref,
    normed_ref,
    low_ref,
    post_ref,
    squares_ref,
    across_ref,
    cos_ref,
    sine_ref,
    sum_ref,
    first_ref,
    rows_all,
    part_mine,
    part_got,
    send_sems,
    recv_sems,
):
    total_rows = token_ref.shape[0]
    depth, width = base_ref.shape[1:]
    rank = right_ref.shape[1]
    groups = part_got.shape[0]
    me = lax.axis_index("mp")
    peers = [lax.rem(me + k, groups) for k in range(groups)]
    part_copies = [
        remote(part_mine, part_got.at[k], send_sems.at[k], recv_sems.at[k], peers[k])
        for k in range(1, groups)
    ]

    @pl.when(pl.program_id(0) == 0)
    def _():
        greet(peers[1:])
        part_mine[...] = part_ref[...]
        step = 128

        def some(i, carry):
            at = pl.ds(pl.multiple_of(i * step, step), step)
            values = token_ref[at, :].astype(F32)
            low = (values * rms_rows(values) * gain_ref[...]).astype(LOW)
            normed_ref[at, :] = low
            rows_all[at, :] = low
            return carry

        lax.fori_loop(0, total_rows // step, some, 0)
        ids = segment_ref[...].astype(F32)
        ids_down = jnp.transpose(jnp.broadcast_to(ids, (8, total_rows)))[:, :1]
        for start in range(0, total_rows, 256):
            rows = slice(start, start + 256)
            smaller = jnp.where(ids < ids_down[rows], 1.0, 0.0)
            first = jnp.sum(smaller, axis=1, keepdims=True).astype(jnp.int32)
            first_ref[rows, :] = first
            cosine, sine = rotation(first - start, coarse_ref[...], fine_ref[...])
            cos_ref[rows, :] = cosine
            sine_ref[rows, :] = sine
        greeted(groups - 1)
        for copy in part_copies:
            copy.start()

    @pl.when(pl.program_id(0) == pl.num_programs(0) - 1)
    def _():
        total = part_mine[...]
        for k, copy in enumerate(part_copies, 1):
            copy.wait_recv()
            total = total + part_got[k]
        sum_ref[...] = total
        for copy in part_copies:
            copy.wait_send()

    rows_all[total_rows:, :] = left_ref[0].astype(LOW)
    turning = pl.program_id(0) < 2
    wide = 256

    def put(start, step, columns, tile):
        low_ref[0, start : start + step, columns] = tile

    squares_ref[0] = merge_tile(
        lambda start, step, columns: base_ref[0, start : start + step, columns],
        put,
        left_ref[0],
        right_ref[0],
        depth,
    )
    for column in range(0, width, wide):
        columns = slice(column, column + wide)
        magnitude = magnitude_ref[pl.ds(pl.program_id(0), 1), columns]
        scale = magnitude / jnp.sqrt(squares_ref[0, :, columns])
        low = low_ref[0, :, columns]
        step = min(512, total_rows)
        for start in range(0, total_rows, step):
            last = start + step == total_rows
            rows = slice(start, start + step)
            pre = dot(rows_all[start : start + step + (rank if last else 0), :], low)
            if last:
                across_ref[0, :, columns] = pre[step:]
            post = pre[:step] * scale
            cos_table = jnp.where(turning, cos_ref[rows, :], 1.0)
            sine_table = jnp.where(turning, sine_ref[rows, :], 0.0)
            for head in range(0, wide, HEAD_DIM):
                piece = post[:, head : head + HEAD_DIM]
                other = pltpu.roll(piece, HEAD_DIM // 2, 1)
                post_ref[0, rows, column + head : column + head + HEAD_DIM] = (
                    piece * cos_table + other * sine_table
                ).astype(LOW)


def project_heads(tokens, gain, base, left, right, magnitude, segments, part, groups):
    members, depth, width = base.shape
    rows, rank = tokens.shape[0], right.shape[1]
    coarse = table_pieces(np.arange(TABLE_STEP) * TABLE_STEP)
    fine = table_pieces(np.arange(TABLE_STEP))
    whole = lambda v: pl.BlockSpec(v.shape, lambda m: (0,) * v.ndim)
    of_member = lambda *dims: pl.BlockSpec((1,) + dims, lambda m: (m, 0, 0))
    table = pl.BlockSpec((rows, HEAD_DIM), lambda m: (0, 0))
    return call(
        "project_heads",
        heads_kernel,
        (tokens, gain, base, left, right, magnitude, segments, coarse, fine, part),
        (members,),
        [
            whole(tokens),
            whole(gain),
            of_member(depth, width),
            of_member(rank, depth),
            of_member(rank, width),
            whole(magnitude),
            whole(segments),
            whole(coarse),
            whole(fine),
            whole(part),
        ],
        [
            whole(tokens),
            of_member(depth, width),
            of_member(rows, width),
            of_member(1, width),
            of_member(rank, width),
            table,
            table,
            whole(part),
            pl.BlockSpec((rows, 1), lambda m: (0, 0)),
        ],
        [
            shape((rows, depth), LOW),
            shape(base.shape, LOW),
            shape((members, rows, width), LOW),
            shape((members, 1, width), F32),
            shape((members, rank, width), F32),
            shape((rows, HEAD_DIM), F32),
            shape((rows, HEAD_DIM), F32),
            shape(part.shape, F32),
            shape((rows, 1), jnp.int32),
        ],
        scratch=[
            pltpu.VMEM((rows + rank, depth), LOW),
            pltpu.VMEM(part.shape, F32),
            pltpu.VMEM((groups,) + part.shape, F32),
            pltpu.SemaphoreType.DMA((groups,)),
            pltpu.SemaphoreType.DMA((groups,)),
        ],
        identity=2,
        flops=2 * members * rows * depth * width,
    )


def key_start(block):
    return max(0, (block * ATTEND_BLOCK - (LONGEST - 1)) // ATTEND_BLOCK * ATTEND_BLOCK)


def masked_probs(scores, first, row_at, key_at):
    scores = scores * HEAD_DIM ** (-0.5)
    places = row_at + lax.broadcasted_iota(jnp.int32, scores.shape, 0)
    others = key_at + lax.broadcasted_iota(jnp.int32, scores.shape, 1)
    scores = jnp.where((others >= first) & (others <= places), scores, MASKED)
    exp_scores = jnp.exp(scores - jnp.max(scores, axis=1, keepdims=True))
    return exp_scores * (1.0 / jnp.sum(exp_scores, axis=1, keepdims=True))


class Unit:
    def __init__(self, head, block):
        self.row_at, self.key_at = block * ATTEND_BLOCK, key_start(block)
        self.rows = slice(self.row_at, self.row_at + ATTEND_BLOCK)
        self.keys = slice(self.key_at, self.row_at + ATTEND_BLOCK)
        self.lanes = slice(head * HEAD_DIM, (head + 1) * HEAD_DIM)


def units_of(rows, width, most):
    units = [
        Unit(head, block)
        for block in range(rows // ATTEND_BLOCK)
        for head in range(width // HEAD_DIM)
    ]
    return [units[at : at + most] for at in range(0, len(units), most)]


def put_rows(ref, lead, row_at, lanes, values, order_ref, groups):
    share = ref.shape[len(lead)] // groups
    step = min(share, values.shape[0])
    for start in range(0, values.shape[0], step):
        group = (row_at + start) // share
        inside = (row_at + start) % share
        at = pl.multiple_of(order_ref[groups + group] * share + inside, step)
        ref[(*lead, pl.ds(at, step), lanes)] = values[start : start + step].astype(ref.dtype)


def attend_kernel(groups, order_ref, query_ref, key_ref, value_ref, first_ref, out_ref):
    for some in units_of(*query_ref.shape[1:], 4):
        scores = [
            dot(query_ref[0, u.rows, u.lanes], key_ref[0, u.keys, u.lanes], NT) for u in some
        ]
        probs = [
            masked_probs(s, first_ref[u.rows, :], u.row_at, u.key_at).astype(LOW)
            for u, s in zip(some, scores)
        ]
        for u, p in zip(some, probs):
            mixed = dot(p, value_ref[0, u.keys, u.lanes])
            put_rows(out_ref, (), u.row_at, u.lanes, mixed, order_ref, groups)


def attend(order, groups, post, first):
    rows, width = post.shape[1:]
    wide = 2 * HEAD_DIM
    member = lambda m: pl.BlockSpec((1, rows, wide), lambda h, o: (m, 0, h))
    return call(
        "attend",
        functools.partial(attend_kernel, groups),
        (post, post, post, first),
        (width // wide,),
        [member(0), member(1), member(2), pl.BlockSpec((rows, 1), lambda h, o: (0, 0))],
        [pl.BlockSpec((rows, wide), lambda h, o: (0, h))],
        [shape((rows, width), LOW)],
        prefetch=(order,),
        flops=4 * rows * rows * width,
    )[0]


def attend_back_kernel(
    groups,
    order_ref,
    query_ref,
    key_ref,
    value_ref,
    first_ref,
    cos_ref,
    sine_ref,
    magnitude_ref,
    squares_ref,
    low_ref,
    *rest,
):
    pieces, (grad_ref, total_ref, upper_all, heads_grad, key_grad, value_grad, sems) = rest[:-7], rest[-7:]
    rows_all, width = query_ref.shape[1:]
    share = rows_all // groups

    @pl.when(pl.program_id(0) == 0)
    def _():
        copies = []
        for place, piece in enumerate(pieces):
            at = pl.multiple_of(order_ref[place] * share, share)
            copies.append(
                pltpu.make_async_copy(piece, upper_all.at[pl.ds(at, share), :], sems.at[place])
            )
            copies[-1].start()
        for copy in copies:
            copy.wait()

    step = min(512, rows_all)
    for start in range(0, rows_all, step):
        at = slice(start, start + step)
        heads_grad[at, :] = dot(upper_all[at, :], low_ref[0], NT).astype(LOW)
    norm = [jnp.sqrt(squares_ref[m]) for m in range(3)]
    scale = [magnitude_ref[m : m + 1] / norm[m] for m in range(3)]
    heads = range(0, width, HEAD_DIM)
    totals = [jnp.zeros((1, width), F32) for _ in range(3)]
    filled = set()

    def back(values, rows):
        return values * cos_ref[rows, :] - pltpu.roll(values, HEAD_DIM // 2, 1) * sine_ref[rows, :]

    def add(ref, unit, values):
        for start in range(0, values.shape[0], ATTEND_BLOCK):
            at = unit.key_at + start
            rows = slice(at, at + ATTEND_BLOCK)
            name = (id(ref), at, unit.lanes.start)
            if name in filled:
                ref[rows, unit.lanes] += values[start : start + ATTEND_BLOCK]
            else:
                filled.add(name)
                ref[rows, unit.lanes] = values[start : start + ATTEND_BLOCK]

    def spread(per_head):
        return jnp.concatenate(per_head, axis=1)

    query_totals = [jnp.zeros((1, HEAD_DIM), F32) for _ in heads]
    for some in units_of(rows_all, width, 2):
        scores = [
            dot(query_ref[0, u.rows, u.lanes], key_ref[0, u.keys, u.lanes], NT) for u in some
        ]
        grad_weights = [
            dot(heads_grad[u.rows, u.lanes], value_ref[0, u.keys, u.lanes], NT) for u in some
        ]
        probs = [
            masked_probs(s, first_ref[u.rows, :], u.row_at, u.key_at)
            for u, s in zip(some, scores)
        ]
        grad_scores = [
            (p * (g - jnp.sum(p * g, axis=1, keepdims=True))).astype(LOW)
            for p, g in zip(probs, grad_weights)
        ]
        for u, p, g in zip(some, probs, grad_scores):
            add(value_grad, u, dot(p.astype(LOW), heads_grad[u.rows, u.lanes], TN))
            add(key_grad, u, dot(g, query_ref[0, u.rows, u.lanes], TN))
        for u, g in zip(some, grad_scores):
            grad = back(dot(g, key_ref[0, u.keys, u.lanes]) * HEAD_DIM ** (-0.5), u.rows)
            head = u.lanes.start // HEAD_DIM
            post = back(query_ref[0, u.rows, u.lanes].astype(F32), u.rows)
            query_totals[head] = query_totals[head] + jnp.sum(grad * post, axis=0, keepdims=True)
            put_rows(grad_ref, (0,), u.row_at, u.lanes, grad * scale[0][:, u.lanes], order_ref, groups)
    totals[0] = spread(query_totals)
    for row_at in range(0, rows_all, ATTEND_BLOCK):
        rows = slice(row_at, row_at + ATTEND_BLOCK)
        for head in heads:
            lanes = slice(head, head + HEAD_DIM)
            grad = back(key_grad[rows, lanes] * HEAD_DIM ** (-0.5), rows)
            post = back(key_ref[0, rows, lanes].astype(F32), rows)
            part = jnp.sum(grad * post, axis=0, keepdims=True)
            query_totals[head // HEAD_DIM] = part if row_at == 0 else query_totals[head // HEAD_DIM] + part
            put_rows(grad_ref, (1,), row_at, lanes, grad * scale[1][:, lanes], order_ref, groups)
        grad = value_grad[rows, :]
        totals[2] = totals[2] + jnp.sum(grad * value_ref[0, rows, :].astype(F32), axis=0, keepdims=True)
        put_rows(grad_ref, (2,), row_at, slice(0, width), grad * scale[2], order_ref, groups)
    totals[1] = spread(query_totals)
    for m in range(3):
        total_ref[m] = totals[m] / scale[m]


def attend_back(order, groups, post, first, cos_table, sine_table, magnitude, squares, low, pieces):
    rows, width = post.shape[1:]
    depth = low.shape[2]
    wide = 2 * HEAD_DIM
    member = lambda m: pl.BlockSpec((1, rows, wide), lambda h, o: (m, 0, h))
    table = pl.BlockSpec((rows, HEAD_DIM), lambda h, o: (0, 0))
    column = pl.BlockSpec((3, 1, wide), lambda h, o: (0, 0, h))
    return call(
        "attend_back",
        functools.partial(attend_back_kernel, groups),
        (post, post, post, first, cos_table, sine_table, magnitude, squares, low, *pieces),
        (width // wide,),
        [
            member(0),
            member(1),
            member(2),
            pl.BlockSpec((rows, 1), lambda h, o: (0, 0)),
            table,
            table,
            pl.BlockSpec((3, wide), lambda h, o: (0, h)),
            column,
            pl.BlockSpec((1, wide, depth), lambda h, o: (0, h, 0)),
            *[pl.BlockSpec(memory_space=pl.ANY) for _ in pieces],
        ],
        [pl.BlockSpec((3, rows, wide), lambda h, o: (0, 0, h)), column],
        [shape((3, rows, width), LOW), shape((3, 1, width), F32)],
        scratch=[
            pltpu.VMEM((rows, depth), LOW),
            pltpu.VMEM((rows, wide), LOW),
            pltpu.VMEM((rows, wide), F32),
            pltpu.VMEM((rows, wide), F32),
            pltpu.SemaphoreType.DMA((len(pieces),)),
        ],
        prefetch=(order,),
        flops=10 * rows * rows * width + 2 * rows * width * depth,
    )


def product_kernel(dims, n_totals, n_lines, steps, *refs):
    value_ref, weight_ref = refs[:2]
    if n_totals == 0:
        left_ref, *refs = refs[2:]
    else:
        right_ref, squares_ref, magnitude_ref = refs[2:5]
        totals, refs = refs[5 : 5 + n_totals], refs[5 + n_totals :]
    lines = []
    if n_lines > 0:
        lines, refs = refs[:n_lines], refs[n_lines:]
        *refs, line_mine, line_got, line_send_sems, line_recv_sems = refs
    *outs, extra_ref, rows_all, sent, got, send_sems, recv_sems = refs
    if n_lines > 0:
        *outs, line_out = outs
    members, groups, share, inner = value_ref.shape
    count, wide = groups * share, extra_ref.shape[2]
    now = pl.program_id(0)
    sibling = sibling_id()
    me = lax.axis_index("mp")
    peers = [lax.rem(me + k, groups) for k in range(1, groups)] if n_lines > 0 else [sibling]
    line_copies = [
        remote(line_mine, line_got.at[k], line_send_sems.at[k], line_recv_sems.at[k], peer)
        for k, peer in enumerate(peers if n_lines > 0 else [], 1)
    ]

    @pl.when(now == 0)
    def _():
        greet(peers)
        for n, ref in enumerate(lines):
            line_mine[n : n + 1, :] = ref[...]
        if n_totals > 0:
            total = sum_refs(totals)
        for m in range(members):
            rows_all[m, :count, :] = value_ref[m].reshape(count, inner)
            if n_totals == 0:
                rows_all[m, count:, :] = left_ref[m].astype(LOW)
            else:
                weight = norm_weight(total[m], squares_ref[m], magnitude_ref[m : m + 1])
                rows_all[m, count:, :] = (right_ref[m] * weight).astype(LOW)

    result = None
    for m in range(members):
        part = dot(rows_all[m], weight_ref[m], dims)
        extra_ref[m] = part[count:]
        result = part[:count] if result is None else result + part[:count]

    def columns(step):
        return pl.ds(pl.multiple_of(step * wide, wide), wide)

    def copy(step):
        return remote(sent.at[step], got.at[step], send_sems.at[step], recv_sems.at[step], sibling)

    def add(step):
        copy(step).wait_recv()
        for n, ref in enumerate(outs):
            total = ref[:, columns(step)].astype(F32) + got[step, n].astype(F32)
            ref[:, columns(step)] = total.astype(LOW)

    for n, ref in enumerate(outs):
        at = CORES * n * share
        sent[now, n] = result[at : at + share].astype(LOW)
        ref[:, columns(now)] = result[at + share : at + CORES * share].astype(LOW)

    @pl.when(now == 0)
    def _():
        greeted(len(peers))
        for each in line_copies:
            each.start()

    copy(now).start()

    @pl.when(now > 0)
    def _():
        add(now - 1)

    @pl.when(now == steps - 1)
    def _():
        add(now)
        for step in range(steps):
            copy(step).wait_send()
        if n_lines > 0:
            line_sum = line_mine[...]
            for k, each in enumerate(line_copies, 1):
                each.wait_recv()
                line_sum = line_sum + line_got[k]
            line_out[...] = line_sum
            for each in line_copies:
                each.wait_send()


def product(name, identity, values, weights, dims, left=None, correction=None, lines=()):
    members, groups, share, inner = values.shape
    chips = groups // CORES
    width = weights.shape[2] if dims is NN else weights.shape[1]
    wide = tile_of(width, 512)
    steps = width // wide
    if dims is NN:
        weight_spec = pl.BlockSpec((members, inner, wide), lambda n: (0, 0, n))
    else:
        weight_spec = pl.BlockSpec((members, wide, inner), lambda n: (0, n, 0))
    if correction is None:
        extra, n_totals, rank = (left,), 0, left.shape[1]
    else:
        right, squares, magnitude, totals = correction
        extra, n_totals, rank = (right, squares, magnitude, *totals), len(totals), right.shape[1]
    fixed = lambda v: pl.BlockSpec(v.shape, lambda n: (0,) * v.ndim)
    out = pl.BlockSpec((share, width), lambda n: (0, 0))
    line_specs, line_shapes, line_scratch = [], [], []
    if lines:
        line = (len(lines), width)
        line_specs = [pl.BlockSpec(line, lambda n: (0, 0))]
        line_shapes = [shape(line, F32)]
        line_scratch = [
            pltpu.VMEM(line, F32),
            pltpu.VMEM((groups,) + line, F32),
            pltpu.SemaphoreType.DMA((groups,)),
            pltpu.SemaphoreType.DMA((groups,)),
        ]
    results = call(
        name,
        functools.partial(product_kernel, dims, n_totals, len(lines), steps),
        (values, weights, *extra, *lines),
        (steps,),
        [fixed(values), weight_spec] + [fixed(v) for v in (*extra, *lines)],
        [out] * chips + line_specs + [pl.BlockSpec((members, rank, wide), lambda n: (0, 0, n))],
        [shape((share, width), LOW)] * chips
        + line_shapes
        + [shape((members, rank, width), F32)],
        scratch=[
            pltpu.VMEM((members, groups * share + rank, inner), LOW),
            pltpu.VMEM((steps, chips, share, wide), LOW),
            pltpu.VMEM((steps, chips, share, wide), LOW),
            pltpu.SemaphoreType.DMA((steps,)),
            pltpu.SemaphoreType.DMA((steps,)),
        ]
        + line_scratch,
        flops=2 * members * groups * share * inner * width,
        identity=identity,
    )
    return results[:chips], *results[chips:]


def shrink_kernel(chips, order_ref, *refs):
    values, (weight_ref, left_ref, cot_ref), outs = refs[:chips], refs[chips : chips + 3], refs[chips + 3 :]
    total_ref, across_ref, rows_all = outs[-3:]
    both, inner = values[0].shape
    share, depth = both // CORES, left_ref.shape[2]
    count = chips * both

    @pl.when(pl.program_id(0) == 0)
    def _():
        for step, ref in enumerate(values):
            rows_all[step * both : (step + 1) * both, :] = ref[...]
        if inner > depth:
            rows_all[count:, depth:] = jnp.zeros((rows_all.shape[0] - count, inner - depth), LOW)
        rows_all[count:, :depth] = left_ref[0].astype(LOW)

    result = dot(rows_all[...], weight_ref[0])
    across_ref[0] = result[count:]
    total = jnp.zeros((1, weight_ref.shape[2]), F32)
    for place in range(chips * CORES):
        pre = result[place * share : (place + 1) * share]
        outs[place][...] = pre.astype(LOW)
        at = pl.multiple_of(order_ref[place] * share, share)
        cot = cot_ref[pl.ds(at, share), :].astype(F32)
        total = total + jnp.sum(pre * cot, axis=0, keepdims=True)
    total_ref[...] = total


def shrink_product(order, values, weights, left, cotangent):
    chips = len(values)
    share, inner = values[0].shape[0] // CORES, values[0].shape[1]
    width, rank = weights.shape[2], left.shape[1]
    rows = chips * CORES * share
    wide = tile_of(width, 512)
    fixed = lambda v: pl.BlockSpec(v.shape, lambda n, o: (0,) * v.ndim)
    results = call(
        "shrink_product",
        functools.partial(shrink_kernel, chips),
        (*values, weights, left, cotangent),
        (width // wide,),
        [fixed(v) for v in values]
        + [
            pl.BlockSpec((1, inner, wide), lambda n, o: (0, 0, n)),
            fixed(left),
            pl.BlockSpec((rows, wide), lambda n, o: (0, n)),
        ],
        [pl.BlockSpec((share, wide), lambda n, o: (0, n))] * (chips * CORES)
        + [
            pl.BlockSpec((1, wide), lambda n, o: (0, n)),
            pl.BlockSpec((1, rank, wide), lambda n, o: (0, 0, n)),
        ],
        [shape((share, width), LOW)] * (chips * CORES)
        + [shape((1, width), F32), shape((1, rank, width), F32)],
        scratch=[pltpu.VMEM((rows + rank, inner), LOW)],
        prefetch=(order,),
        flops=2 * rows * inner * width,
    )
    return results[: chips * CORES], results[-2], results[-1]


def row_call(name, kernel, order, given, whole, out_kinds, sums, prepare):
    share = min(v.shape[0] for v, _ in given)
    width = given[0][0].shape[1]
    halves = 2
    half = share // halves
    count = len(given)

    def run(order_ref, *refs):
        sources, rest = refs[:count], refs[count : -count - 1]
        held, sems = refs[-count - 1 : -1], refs[-1]

        def copies(part):
            for i, ((_, cut), source, target) in enumerate(zip(given, sources, held)):
                at = part * half
                if cut:
                    at = pl.multiple_of(order_ref[1] * share + at, half)
                yield pltpu.make_async_copy(
                    source.at[pl.ds(at, half), :],
                    target.at[pl.ds(part * half, half), :],
                    sems.at[part, i],
                )

        for part in range(halves):

            @pl.when(pl.program_id(0) == part)
            def _(part=part):
                if part == 0:
                    for each in range(halves):
                        for copy in copies(each):
                            copy.start()
                for copy in copies(part):
                    copy.wait()

        outs = rest[len(whole) : len(whole) + len(out_kinds)]
        totals, sums_held = rest[len(whole) + len(out_kinds) :][:sums], rest[len(rest) - sums :]
        tile = 32
        lines = prepare(*[ref[...] for ref in rest[: len(whole)]])
        for ref in sums_held:
            ref[...] = jnp.zeros_like(ref)

        def some(i, carry):
            inside = pl.ds(pl.multiple_of(i * tile, tile), tile)
            at = pl.ds(pl.multiple_of(pl.program_id(0) * half + i * tile, tile), tile)
            values = kernel([ref[at, :].astype(F32) for ref in held], *lines)
            for ref, value in zip(outs, values):
                ref[inside, :] = value.astype(ref.dtype)
            for ref, value in zip(sums_held, values[len(outs) :]):
                ref[...] += jnp.sum(value.reshape(tile // 8, 8, width), axis=0)
            return carry

        lax.fori_loop(0, half // tile, some, 0, unroll=2)
        for ref, held_ref in zip(totals, sums_held):
            add_column(ref, held_ref[...])

    line = pl.BlockSpec((1, width), lambda i, o: (0, 0))
    return call(
        name,
        run,
        (*[v for v, _ in given], *whole),
        (halves,),
        [pl.BlockSpec(memory_space=pl.ANY) for _ in given] + [line for _ in whole],
        [pl.BlockSpec((half, width), lambda i, o: (i, 0)) for _ in out_kinds]
        + [line for _ in range(sums)],
        [shape((share, width), kind) for kind in out_kinds]
        + [shape((1, width), F32) for _ in range(sums)],
        scratch=[pltpu.VMEM((8, width), F32) for _ in range(sums)]
        + [pltpu.VMEM((share, width), v.dtype) for v, _ in given]
        + [pltpu.SemaphoreType.DMA((halves, count))],
        prefetch=(order,),
        flops=20 * share * width,
    )


def sum_of(values):
    total = values[0]
    for value in values[1:]:
        total = total + value
    return total


def add_column(ref, values):
    part = jnp.sum(values, axis=0, keepdims=True)

    @pl.when(pl.program_id(0) == 0)
    def _():
        ref[...] = part

    @pl.when(pl.program_id(0) > 0)
    def _():
        ref[...] += part


def scale_first(squares, magnitude, *rest):
    norm = jnp.sqrt(squares)
    return (magnitude / norm, norm / magnitude, *rest)


def hidden_kernel(given, scale, inverse, gain):
    hidden = given[0] + sum_of(given[1:]) * scale
    return hidden, hidden * rms_rows(hidden) * gain


def mixed_kernel(given, scale, inverse):
    return (given[0] + sum_of(given[1:]) * scale,)


def norm_back(grad_normed, values, gain):
    factor = rms_rows(values)
    scaled = grad_normed * gain
    inner = jnp.mean(scaled * values, axis=1, keepdims=True)
    back = factor * scaled - values * (factor * factor * factor * inner)
    return back, grad_normed * values * factor


def hidden_back_kernel(given, scale, inverse, gain):
    cot, token, hidden = given[:3]
    back, gain_terms = norm_back(sum_of(given[3:]), hidden, gain)
    grad = cot + back
    return grad, grad * scale, grad * ((hidden - token) * inverse), gain_terms


def token_back_kernel(given, gain):
    back, gain_terms = norm_back(sum_of(given[2:]), given[0], gain)
    return given[1] + back, gain_terms


def shrink_back_kernel(places, order_ref, *refs):
    cots, (low_ref, squares_ref, magnitude_ref, product_ref, grad_ref, rows_all) = refs[:places], refs[places:]
    scale = magnitude_ref[0] / jnp.sqrt(squares_ref[0])
    share = cots[0].shape[0]
    for place, cot_ref in enumerate(cots):
        grad = (cot_ref[...].astype(F32) * scale).astype(LOW)
        grad_ref[place] = grad
        rows_all[place * share : (place + 1) * share, :] = grad
    result = dot(rows_all[...], low_ref[0], NT).astype(LOW)
    for place in range(places):
        product_ref[place] = result[place * share : (place + 1) * share]


def shrink_back(order, cotangent, low, squares, magnitude, groups):
    rows, width = cotangent.shape
    share, inner = rows // groups, low.shape[1]
    places = CORES
    line = pl.BlockSpec((1, 1, width), lambda j, o: (0, 0, 0))
    cot = lambda place: pl.BlockSpec((share, width), lambda j, o: (o[places * j + place], 0))
    return call(
        "shrink_back",
        functools.partial(shrink_back_kernel, places),
        (*[cotangent] * places, low, squares, magnitude),
        (groups // places,),
        [cot(place) for place in range(places)]
        + [pl.BlockSpec((1, inner, width), lambda j, o: (0, 0, 0)), line, line],
        [
            pl.BlockSpec((places, share, inner), lambda j, o: (j, 0, 0)),
            pl.BlockSpec((places, share, width), lambda j, o: (j, 0, 0)),
        ],
        [shape((groups, share, inner), LOW), shape((groups, share, width), LOW)],
        scratch=[pltpu.VMEM((places * share, width), LOW)],
        prefetch=(order,),
        flops=2 * rows * width * inner,
    )


def expand_kernel(step, first, last, n_totals, *refs):
    mine_ref, low_ref, grad_ref, squares_ref, magnitude_ref = refs[:5]
    refs = list(refs[5:])
    left_ref = refs.pop(0) if first else None
    right_ref = refs.pop(0) if last else None
    before = [refs.pop(0) for _ in range(n_totals)]
    product_ref, back_ref, rows_ref, total_ref, joined_ref = refs[:5]
    refs = refs[5:]
    across_ref = refs.pop(0) if first else None
    extra_ref = refs.pop(0) if last else None
    rows_all, low_all, grad_all, product_all, back_all, sent, got, in_sems, out_sems, send_sems, recv_sems = refs
    share, depth = mine_ref.shape
    sibling = sibling_id()
    greet([sibling])
    both = CORES * share
    width, ff = low_ref.shape[2], magnitude_ref.shape[1]
    tile = 256
    cuts = [slice(at, at + tile) for at in range(0, width, tile)]

    mine_copy = pltpu.make_async_copy(mine_ref, rows_all.at[pl.ds(share, share), :], in_sems.at[0])
    other_copy = remote(
        mine_ref,
        rows_all.at[pl.ds(0, share), :],
        send_sems.at[sent.shape[0]],
        recv_sems.at[sent.shape[0]],
        sibling,
    )
    tile_copies = []
    for n, cut in enumerate(cuts):
        lanes = pl.ds(cut.start, tile)
        tile_copies.append(
            [
                pltpu.make_async_copy(
                    low_ref.at[:, :, lanes], low_all.at[:, :, lanes], in_sems.at[2 + 2 * n]
                ),
                pltpu.make_async_copy(
                    grad_ref.at[pl.ds(CORES * step, CORES), :, lanes],
                    grad_all.at[:, :, lanes],
                    in_sems.at[3 + 2 * n],
                ),
            ]
        )
    mine_copy.start()
    for copy in tile_copies[0]:
        copy.start()
    greeted(1)
    other_copy.start()
    for copies in tile_copies[1:]:
        for copy in copies:
            copy.start()
    if first:
        rank = across_ref.shape[1]
        for m in range(2):
            rows_all[both + m * rank : both + (m + 1) * rank, :] = left_ref[m].astype(LOW)
    mine_copy.wait()
    other_copy.wait_recv()
    out_copies = [
        pltpu.make_async_copy(rows_all.at[pl.ds(0, both), :], rows_ref, out_sems.at[2 * len(cuts)])
    ]
    out_copies[0].start()
    lane = lax.broadcasted_iota(jnp.int32, (1, tile), 1)
    for n, cut in enumerate(cuts):
        for copy in tile_copies[n]:
            copy.wait()
        size = min(tile, ff - cut.start)
        pre = [dot(rows_all[...], low_all[m, :, cut]) for m in range(2)]
        if first:
            for m in range(2):
                rows = slice(both + m * rank, both + (m + 1) * rank)
                across_ref[m, :, cut.start : cut.start + size] = pre[m][rows, :size]
        magnitude, squares, scale = [], [], []
        for m in range(2):
            given = magnitude_ref[m : m + 1, cut.start : cut.start + size]
            if size < tile:
                given = jnp.concatenate([given, jnp.zeros((1, tile - size), F32)], axis=1)
            magnitude.append(given)
            squares.append(squares_ref[m, :, cut])
            scale.append(given / jnp.sqrt(squares[m]))
        sums = [jnp.zeros((1, tile), F32) for _ in range(2)]
        at = [slice(m * width + cut.start, m * width + cut.stop) for m in range(2)]
        for place in range(CORES):
            rows = slice(place * share, (place + 1) * share)
            gate_pre, up_pre = pre[0][rows], pre[1][rows]
            gate, up = gate_pre * scale[0], up_pre * scale[1]
            sigmoid = 0.5 + 0.5 * jnp.tanh(0.5 * gate)
            active = gate * sigmoid
            product_all[rows, cut] = (active * up).astype(LOW)
            upper = grad_all[place, :, cut].astype(F32)
            grad_up = upper * active
            grad_gate = upper * up * sigmoid * (1.0 + gate * (1.0 - sigmoid))
            sums[0] += jnp.sum(grad_gate * gate_pre, axis=0, keepdims=True)
            sums[1] += jnp.sum(grad_up * up_pre, axis=0, keepdims=True)
            back_all[rows, at[0]] = (grad_gate * scale[0]).astype(LOW)
            back_all[rows, at[1]] = (grad_up * scale[1]).astype(LOW)
        for m in range(2):
            total_ref[m, :, cut] = sums[m]
        if last:
            rank = extra_ref.shape[1]
            for m in range(2):
                total = sums[m]
                for ref in before:
                    total = total + ref[m, :, cut]
                right = right_ref[m, :, cut.start : cut.start + size]
                if size < tile:
                    spare = jnp.zeros((rank, tile - size), F32)
                    right = jnp.concatenate([right, spare], axis=1)
                weighted = right * norm_weight(total, squares[m], magnitude[m])
                rows = slice(both + m * rank, both + (m + 1) * rank)
                back_all[rows, at[m]] = weighted.astype(LOW)
                back_all[rows, at[1 - m]] = jnp.zeros((rank, tile), LOW)
    for m in range(2):
        lanes = pl.ds(m * width, width)
        copy = pltpu.make_async_copy(
            back_all.at[pl.ds(0, both), lanes], back_ref.at[m], out_sems.at[m]
        )
        copy.start()
        out_copies.append(copy)
    copy = pltpu.make_async_copy(product_all, product_ref, out_sems.at[2])
    copy.start()
    out_copies.append(copy)
    chunk = sent.shape[2]
    copies = [
        remote(sent.at[n], got.at[n], send_sems.at[n], recv_sems.at[n], sibling)
        for n in range(depth // chunk)
    ]

    def add(n):
        columns = slice(n * chunk, (n + 1) * chunk)
        copies[n].wait_recv()
        total = joined_ref[:, columns].astype(F32) + got[n].astype(F32)
        joined_ref[:, columns] = total.astype(LOW)

    for n in range(depth // chunk):
        columns = slice(n * chunk, (n + 1) * chunk)
        result = dot(back_all[:, :width], low_all[0, columns, :], NT)
        result = result + dot(back_all[:, width:], low_all[1, columns, :], NT)
        sent[n] = result[:share].astype(LOW)
        joined_ref[:, columns] = result[share:both].astype(LOW)
        copies[n].start()
        if n > 0:
            add(n - 1)
        if last:
            for m in range(2):
                extra_ref[m, :, columns] = result[both + m * rank : both + (m + 1) * rank]
    add(len(copies) - 1)
    for copy in out_copies:
        copy.wait()
    for copy in [other_copy, *copies]:
        copy.wait_send()


def expand(identity, mine, low, squares, magnitude, grad_product, step, left=None, right=None, before=()):
    share, depth = mine.shape
    width = low.shape[2]
    first, last = left is not None, right is not None
    rows = CORES * share
    hbm = pl.BlockSpec(memory_space=pl.ANY)
    fixed = lambda dims: pl.BlockSpec(tuple(dims), lambda i: (0,) * len(dims))
    operands = [mine, low, grad_product, squares, magnitude]
    in_specs = [hbm, hbm, hbm, fixed(squares.shape), fixed(magnitude.shape)]
    out_shape = [
        shape((rows, width), LOW),
        shape((2, rows, width), LOW),
        shape((rows, depth), LOW),
        shape((2, 1, width), F32),
        shape((share, depth), LOW),
    ]
    out_specs = [hbm, hbm, hbm] + [fixed(v.shape) for v in out_shape[3:]]
    extra_in = extra_out = 0
    if first:
        rank = left.shape[1]
        extra_in = 2 * rank
        operands.append(left)
        in_specs.append(fixed(left.shape))
        out_shape.append(shape((2, rank, magnitude.shape[1]), F32))
        out_specs.append(fixed(out_shape[-1].shape))
    if last:
        rank = right.shape[1]
        extra_out = 2 * rank
        operands += [right, *before]
        in_specs += [fixed(v.shape) for v in (right, *before)]
        out_shape.append(shape((2, rank, depth), F32))
        out_specs.append(fixed(out_shape[-1].shape))
    tiles, chunk = width // 256, tile_of(depth, 512)
    return call(
        "expand",
        functools.partial(expand_kernel, step, first, last, len(before)),
        tuple(operands),
        (1,),
        in_specs,
        out_specs,
        out_shape,
        scratch=[
            pltpu.VMEM((rows + extra_in, depth), LOW),
            pltpu.VMEM(low.shape, LOW),
            pltpu.VMEM((CORES, share, width), LOW),
            pltpu.VMEM((rows, width), LOW),
            pltpu.VMEM((rows + extra_out, 2 * width), LOW),
            pltpu.VMEM((depth // chunk, share, chunk), LOW),
            pltpu.VMEM((depth // chunk, share, chunk), LOW),
            pltpu.SemaphoreType.DMA((2 + 2 * tiles,)),
            pltpu.SemaphoreType.DMA((2 * tiles + 1,)),
            pltpu.SemaphoreType.DMA((depth // chunk + 1,)),
            pltpu.SemaphoreType.DMA((depth // chunk + 1,)),
        ],
        flops=8 * rows * depth * width,
        identity=identity,
    )


def adapter_kernel(plan, n_inputs, n_grads, corrections, n_before, order_ref, *refs):
    for _ in adapter_steps(plan, n_inputs, n_grads, corrections, n_before, order_ref, *refs):
        pass


def adapter_steps(plan, n_inputs, n_grads, corrections, n_before, order_ref, *refs):
    count = n_inputs + n_grads
    sources, held, sems = refs[:count], refs[-count - 1 : -1], refs[-1]
    left_ref, right_ref = refs[count : count + 2]
    *corrected, left_out, right_out = refs[count + 2 : -count - 1]
    members, rank, width = right_ref.shape
    chunks = list(plan(order_ref, held[:n_inputs], held[n_inputs:]))
    copies, used = [], 0
    for parts, _, _ in chunks:
        copies.append([])
        for which, index in parts:
            copy = pltpu.make_async_copy(
                sources[which].at[index], held[which].at[index], sems.at[used]
            )
            copy.start()
            copies[-1].append(copy)
            used += 1
    yield
    left_rows = jnp.concatenate([split_rows(left_ref[m]) for m in range(members)], axis=0)
    right_rows = [split_rows(right_ref[m]) for m in range(members)]
    before, corrected = corrected[:n_before], corrected[n_before:]
    for out, ref in zip((left_out, right_out), before or (None, None)):
        out[...] = jnp.zeros_like(out) if ref is None else ref[...]
    for waits, (_, taken_of, grads_of) in zip(copies, chunks):
        for copy in waits:
            copy.wait()
        taken = taken_of()
        across = dot(left_rows, taken, NT)
        downs = []
        for m in range(members):
            grad = grads_of(m)
            mine = split_rows(fold(across[2 * rank * m : 2 * rank * (m + 1)]))
            right_out[m] += fold(dot(mine, grad))
            downs.append(split_rows(fold(dot(right_rows[m], grad, NT))))
        left = dot(jnp.concatenate(downs, axis=0), taken)
        for m in range(members):
            left_out[m] += fold(left[2 * rank * m : 2 * rank * (m + 1)])
        yield
    if corrections:
        correct(corrections, right_ref, left_out, right_out, left_out, right_out, *corrected)


def correct(n_totals, right_ref, left_in, right_in, left_out, right_out, *refs):
    back_ref, across_ref, squares_ref, magnitude_ref = refs[:4]
    totals, magnitude_out = refs[4 : 4 + n_totals], refs[4 + n_totals]
    members, rank, width = right_ref.shape
    total = sum_refs(totals)[:, :, :width]
    squares = squares_ref[:, :, :width]
    magnitude_out[...] = total / jnp.sqrt(squares)
    for m in range(members):
        weight = norm_weight(total[m], squares[m], magnitude_ref[m : m + 1])
        if back_ref.dtype == LOW:
            low = back_ref[m, : left_in.shape[2], :]
            back = fold(dot(split_rows(right_ref[m] * weight), low, NT))
        else:
            back = back_ref[m]
        left_out[m] = ADAPT_SCALE * (left_in[m] - back)
        right_out[m] = ADAPT_SCALE * (right_in[m] - across_ref[m][:, :width] * weight)


def adapter_parts(inputs, grads, left, right, correction, before):
    members, rank, width = right.shape
    moved, fixed, n_totals = [*inputs, *grads], [left, right, *before], 0
    outs = [(members, rank, left.shape[2]), (members, rank, width)]
    if correction is not None:
        *given, totals = correction
        n_totals = len(totals)
        fixed += [*given, *totals]
        outs = [(members, 1, width)] + outs
    scratch = [pltpu.VMEM(v.shape, v.dtype) for v in moved] + [pltpu.SemaphoreType.DMA((32,))]
    return moved, fixed, outs, scratch, (len(inputs), len(grads), n_totals, len(before))


def adapter(name, order, plan, inputs, grads, left, right, correction=None, before=(), other=None):
    moved, fixed, outs, scratch, counts = adapter_parts(inputs, grads, left, right, correction, before)
    kernel = functools.partial(adapter_kernel, plan, *counts)
    full = lambda dims: pl.BlockSpec(tuple(dims), lambda i, o: (0,) * len(dims))
    n_moved, n_fixed, n_outs = len(moved), len(fixed), len(outs)
    if other is not None:
        sums, other_right, (low, across, squares, magnitude, totals) = other
        moved = moved + [low]
        fixed = fixed + [other_right, *sums, across, squares, magnitude, *totals]
        outs = outs + [(1, 1, other_right.shape[2]), sums[0].shape, sums[1].shape]
        scratch = scratch + [pltpu.VMEM(low.shape, LOW), pltpu.SemaphoreType.DMA(())]

    def run(order_ref, *refs):
        if other is None:
            kernel(order_ref, *refs)
            return
        refs = list(refs)
        low_held, low_sem = refs[-2:]
        low_copy = pltpu.make_async_copy(refs[n_moved], low_held, low_sem)
        ends = [n_moved + 1, n_moved + 1 + len(fixed), n_moved + 1 + len(fixed) + len(outs)]
        fixed_refs, out_refs = refs[ends[0] : ends[1]], refs[ends[1] : ends[2]]
        steps = adapter_steps(
            plan,
            *counts,
            order_ref,
            *refs[:n_moved],
            *fixed_refs[:n_fixed],
            *out_refs[:n_outs],
            *refs[ends[2] : -2],
        )
        next(steps)
        low_copy.start()
        for _ in steps:
            pass
        low_copy.wait()
        right_ref, left_in, right_in, across_ref, squares_ref, magnitude_ref, *totals_refs = (
            fixed_refs[n_fixed:]
        )
        magnitude_out, left_out, right_out = out_refs[n_outs:]
        correct(
            len(totals_refs),
            right_ref,
            left_in,
            right_in,
            left_out,
            right_out,
            low_held,
            across_ref,
            squares_ref,
            magnitude_ref,
            *totals_refs,
            magnitude_out,
        )

    return call(
        name,
        run,
        (*moved, *fixed),
        (1,),
        [pl.BlockSpec(memory_space=pl.ANY) for _ in moved] + [full(v.shape) for v in fixed],
        [full(dims) for dims in outs],
        [shape(dims, F32) for dims in outs],
        scratch=scratch,
        prefetch=(order,),
        flops=sum(v.size for v in moved) * 64,
    )


def copy_kernel(count, *refs):
    for source, target in zip(refs[:count], refs[count:]):
        target[...] = source[...]


def copy_out(arrays):
    full = lambda v: pl.BlockSpec(v.shape, lambda i: (0,) * v.ndim)
    return call(
        "copy_out",
        functools.partial(copy_kernel, len(arrays)),
        tuple(arrays),
        (1,),
        [full(v) for v in arrays],
        [full(v) for v in arrays],
        [shape(v.shape, F32) for v in arrays],
    )


GRAIN = 16


def pieces_of(width):
    return [(at, min(128, width - at)) for at in range(0, width, 128)]


def cells_of(blocks, lines, parts):
    cells, rows = [], []
    for n, block in enumerate(blocks):
        for m in range(block.shape[0]):
            for at, size in pieces_of(block.shape[2] // parts):
                cells.append((n, m, at, size))
    for n, line in enumerate(lines):
        for m in range(line.shape[0]):
            for at, size in pieces_of(line.shape[2] // parts):
                rows.append((n, m, at, size))
    return cells, rows


def pack(blocks, lines, wide_ref, part, parts, cells, rows):
    for i, (n, m, at, size) in enumerate(cells):
        start = part * (blocks[n].shape[2] // parts) + at
        wide_ref[part, i, :, :size] = blocks[n][m, :, start : start + size]
    for i, (n, m, at, size) in enumerate(rows):
        start = part * (lines[n].shape[2] // parts) + at
        cell, row = len(cells) + i // GRAIN, i % GRAIN
        wide_ref[part, cell, row : row + 1, :size] = lines[n][m, :, start : start + size]


def unpack(full_ref, blocks, lines, part, parts, cells, rows):
    for i, (n, m, at, size) in enumerate(cells):
        start = part * (blocks[n].shape[2] // parts) + at
        blocks[n][m, :, start : start + size] = full_ref[part, i].astype(F32)[:, :size]
    for i, (n, m, at, size) in enumerate(rows):
        start = part * (lines[n].shape[2] // parts) + at
        cell, row = len(cells) + i // GRAIN, i % GRAIN
        values = full_ref[part, cell].astype(F32)
        lines[n][m, :, start : start + size] = values[row : row + 1, :size]


def reduce_steps(groups, lines, counts, *refs):
    n_all, n_all_lines, n_dp, n_dp_lines = counts
    count = sum(counts)
    taken, given, scratch = refs[:count], refs[count : 2 * count], refs[2 * count :]
    ends = [n_all, n_all + n_all_lines, n_all + n_all_lines + n_dp]
    parted = lambda v: (v[: ends[0]], v[ends[0] : ends[1]], v[ends[1] : ends[2]], v[ends[2] :])
    all_out, all_lines_out, dp_out, dp_lines_out = parted(given)
    (
        all_ref,
        line_ref,
        all_low,
        line_low,
        all_got,
        part,
        part_low,
        part_got,
        line_got,
        all_full,
        line_full,
        *sems,
    ) = scratch
    held, in_sems, sems = sems[:count], sems[count], sems[count + 1 :]
    loads = [
        pltpu.make_async_copy(source, target, in_sems.at[i])
        for i, (source, target) in enumerate(zip(taken, held))
    ]
    for load in loads:
        load.start()
    me, row = lax.axis_index("mp"), lax.axis_index("dp")
    piece, line_piece = part.shape[0] // lines, line_ref.shape[1] // lines
    mp_peer = [lax.rem(me + k, groups) for k in range(groups)]
    dp_peer = [lax.rem(row + k, lines) for k in range(lines)]
    barrier = pltpu.get_barrier_semaphore()
    for k in range(1, groups):
        pl.semaphore_signal(barrier, 1, device_id={"mp": mp_peer[k]}, device_id_type=MESH_IDS)
    for k in range(1, lines):
        pl.semaphore_signal(barrier, 1, device_id={"dp": dp_peer[k]}, device_id_type=MESH_IDS)
    all_in, all_lines_in, dp_in, dp_lines_in = parted(held)
    all_cells = cells_of(all_in, all_lines_in, groups)
    dp_cells = cells_of(dp_in, dp_lines_in, 1)
    all_ref[...] = jnp.zeros_like(all_ref)
    line_ref[...] = jnp.zeros_like(line_ref)
    for load in loads:
        load.wait()
    for q in range(groups):
        pack(all_in, all_lines_in, all_ref, q, groups, *all_cells)
    pack(dp_in, dp_lines_in, line_ref, 0, 1, *dp_cells)
    all_low[...] = all_ref[...].astype(LOW)
    line_low[...] = line_ref[...].astype(LOW)
    pl.semaphore_wait(barrier, groups + lines - 2)

    def send(source, target, stage, k, axis, peer):
        copy = pltpu.make_async_remote_copy(
            src_ref=source,
            dst_ref=target,
            send_sem=sems[2 * stage].at[k],
            recv_sem=sems[2 * stage + 1].at[k],
            device_id={axis: peer},
            device_id_type=MESH_IDS,
        )
        copy.start()
        return copy

    over_mp = [
        send(all_low.at[mp_peer[k]], all_got.at[k], 0, k, "mp", mp_peer[k])
        for k in range(1, groups)
    ]
    over_dp = [
        send(
            line_low.at[0, pl.ds(dp_peer[k] * line_piece, line_piece)],
            line_got.at[k],
            1,
            k,
            "dp",
            dp_peer[k],
        )
        for k in range(1, lines)
    ]
    yield
    total = all_ref[me]
    for k, copy in enumerate(over_mp, 1):
        copy.wait_recv()
        total = total + all_got[k].astype(F32)
    part[...] = total
    part_low[...] = total.astype(LOW)
    part_dp = [
        send(part_low.at[pl.ds(dp_peer[k] * piece, piece)], part_got.at[k], 2, k, "dp", dp_peer[k])
        for k in range(1, lines)
    ]
    yield
    held = pl.ds(row * piece, piece)
    total = part[held]
    for k, copy in enumerate(part_dp, 1):
        copy.wait_recv()
        total = total + part_got[k].astype(F32)
    all_full[me, held] = total.astype(LOW)
    part_back = [
        send(all_full.at[me, held], all_full.at[me, held], 4, k, "dp", dp_peer[k])
        for k in range(1, lines)
    ]
    mine = pl.ds(row * line_piece, line_piece)
    total = line_ref[0, mine]
    for k, copy in enumerate(over_dp, 1):
        copy.wait_recv()
        total = total + line_got[k].astype(F32)
    line_full[0, mine] = total.astype(LOW)
    line_back = [
        send(line_full.at[0, mine], line_full.at[0, mine], 3, k, "dp", dp_peer[k])
        for k in range(1, lines)
    ]
    yield
    for copy in part_back:
        copy.wait_recv()
    all_back = [
        send(all_full.at[me], all_full.at[me], 5, k, "mp", mp_peer[k]) for k in range(1, groups)
    ]
    yield
    for copy in line_back:
        copy.wait_recv()
    unpack(line_full, dp_out, dp_lines_out, 0, 1, *dp_cells)
    for copy in all_back:
        copy.wait_recv()
    for q in range(groups):
        unpack(all_full, all_out, all_lines_out, q, groups, *all_cells)
    for copy in over_mp + over_dp + part_dp + line_back + part_back + all_back:
        copy.wait_send()


def reduce_devices(name, identity, over_all, over_all_lines, over_dp, over_dp_lines, job=None):
    groups, lines = lax.axis_size("mp"), lax.axis_size("dp")

    def size_of(blocks, rows, parts):
        cells, lines_in = cells_of(blocks, rows, parts)
        size = len(cells) + -(-len(lines_in) // GRAIN)
        return -(-size // lines) * lines

    count, line_count = size_of(over_all, over_all_lines, groups), size_of(over_dp, over_dp_lines, 1)
    operands = [*over_all, *over_all_lines, *over_dp, *over_dp_lines]
    counts = (len(over_all), len(over_all_lines), len(over_dp), len(over_dp_lines))
    tail = (GRAIN, 128)
    sizes = (groups, lines, lines, lines, lines, groups)
    every, line = (groups, count) + tail, (1, line_count) + tail
    scratch = (
        [
            pltpu.VMEM(every, F32),
            pltpu.VMEM(line, F32),
            pltpu.VMEM(every, LOW),
            pltpu.VMEM(line, LOW),
            pltpu.VMEM(every, LOW),
            pltpu.VMEM((count,) + tail, F32),
            pltpu.VMEM((count,) + tail, LOW),
            pltpu.VMEM((lines, count // lines) + tail, LOW),
            pltpu.VMEM((lines, line_count // lines) + tail, LOW),
            pltpu.VMEM(every, LOW),
            pltpu.VMEM(line, LOW),
        ]
        + [pltpu.VMEM(v.shape, F32) for v in operands]
        + [pltpu.SemaphoreType.DMA((len(operands),))]
        + [pltpu.SemaphoreType.DMA((n,)) for n in sizes for _ in range(2)]
    )
    outs = [v.shape for v in operands]
    n_operands, n_scratch = len(operands), len(scratch)
    anywhere = lambda v: pl.BlockSpec(memory_space=pl.ANY)
    full = lambda v: pl.BlockSpec(v.shape, lambda i: (0,) * v.ndim)
    in_specs = [anywhere(v) for v in operands]
    plan, moved, fixed, job_counts = None, [], [], ()
    if job is not None:
        plan, (moved, fixed, job_outs, job_scratch, job_counts) = job
        operands = operands + [*moved, *fixed]
        in_specs += [anywhere(v) for v in moved] + [full(v) for v in fixed]
        outs = outs + job_outs
        scratch = scratch + job_scratch
    out_shape = [shape(dims, F32) for dims in outs]

    def run(*refs):
        given, refs = refs[: len(operands)], refs[len(operands) :]
        results, held = refs[: len(outs)], refs[len(outs) :]
        steps = reduce_steps(
            groups, lines, counts, *given[:n_operands], *results[:n_operands], *held[:n_scratch]
        )
        work = iter(())
        if job is not None:
            work = adapter_steps(
                plan, *job_counts, None, *given[n_operands:], *results[n_operands:], *held[n_scratch:]
            )
            next(work)
        for _ in steps:
            next(work, None)
        for _ in work:
            pass

    return call(
        name,
        run,
        tuple(operands),
        (1,),
        in_specs,
        [full(v) for v in out_shape],
        out_shape,
        scratch=scratch,
        flops=1000,
        identity=identity,
    )


def body(
    tokens,
    cotangent,
    segment_ids,
    attend_gain,
    expand_gain,
    heads_base,
    heads_left,
    heads_right,
    heads_magnitude,
    output_base,
    output_left,
    output_right,
    output_magnitude,
    expand_base,
    expand_left,
    expand_right,
    expand_magnitude,
    shrink_base,
    shrink_left,
    shrink_right,
    shrink_magnitude,
):
    groups = lax.axis_size("mp")
    chips = groups // CORES
    index = lax.axis_index("mp")
    chip, core = index // CORES, index % CORES
    rows, width = tokens.shape
    share = rows // groups
    local_heads, ff = heads_base.shape[2], expand_base.shape[2]
    ff_wide = padded(ff)
    device = jnp.arange(groups, dtype=jnp.int32)
    order = jnp.concatenate(
        [
            (chip + device // CORES) % chips * CORES + (core + 1 + device) % CORES,
            (device // CORES + chips - chip) % chips * CORES + (device + CORES - core + 1) % CORES,
        ]
    ).astype(jnp.int32)

    def tie(*values):
        return lax.optimization_barrier(values)

    def sibling(values):
        return lax.ppermute(
            values, "mp", [(i, i // CORES * CORES + (i + 1) % CORES) for i in range(groups)]
        )

    def to_chip(values, step):
        return lax.ppermute(
            values,
            "mp",
            [((i, ((i // CORES + step) % chips) * CORES + i % CORES)) for i in range(groups)],
        )

    def join(pair):
        return (pair[1].astype(F32) + sibling(pair[0]).astype(F32)).astype(LOW)

    def chip_pairs(places):
        return [places[CORES * step : CORES * (step + 1)] for step in range(chips)]

    def arrive(own):
        return [to_chip(own, chips - step) for step in range(1, chips)]

    def pairs_of(own, near_sibling, arrived):
        return [(near_sibling, own)] + [(sibling(piece), piece) for piece in arrived]

    def in_pairs(order_ref, inputs, grads):
        for step, (taken, grad) in enumerate(zip(inputs, grads)):
            yield (
                [(step, ...), (chips + step, ...)],
                lambda taken=taken: taken[...],
                lambda m, grad=grad: grad[m, :, :ff],
            )

    def in_shrink(order_ref, inputs, grads):
        for step, taken in enumerate(inputs):
            at = slice(CORES * step, CORES * (step + 1))
            yield (
                [(step, ...), (chips, pl.ds(CORES * step, CORES))],
                lambda taken=taken: taken[:, :ff],
                lambda m, at=at: grads[0][at].reshape(-1, grads[0].shape[-1]),
            )

    def in_output(start):
        def plan(order_ref, inputs, grads):
            for n, grad in enumerate(grads):
                yield (
                    [(0, (0, start + n)), (1 + n, ...)],
                    lambda place=start + n: inputs[0][0, place],
                    lambda m, grad=grad: grad[...],
                )

        return plan

    def in_heads(order_ref, inputs, grads):
        for place in range(groups):
            step, side = place // CORES, place % CORES
            me = lax.axis_index("mp")
            group = lax.rem(me // CORES + step, chips) * CORES + lax.rem(me + 1 + side, CORES)
            at = pl.multiple_of(group * share, share)
            rows = pl.ds(place * share, share)
            yield (
                [(0, pl.ds(at, share)), (1, (slice(None), rows))],
                lambda at=at: inputs[0][pl.ds(at, share), :],
                lambda m, rows=rows: grads[0][m, rows, :],
            )

    heads_rows, output_rows = turned(heads_left), turned(output_left[None])
    expand_rows, shrink_rows = turned(expand_left), turned(shrink_left[None])
    heads_mag, output_mag = heads_magnitude, output_magnitude[None]
    expand_mag, shrink_mag = expand_magnitude, shrink_magnitude[None]
    attend_line, expand_line = attend_gain[None], expand_gain[None]

    output_low, shrink_low, squares_part = merge_pair(
        [(output_base, output_rows[0], output_right), (shrink_base, shrink_rows[0], shrink_right)]
    )
    output_low, shrink_low = output_low[None], shrink_low[None]
    (
        normed,
        heads_low,
        post,
        heads_sq,
        heads_across,
        cos_table,
        sine_table,
        squares,
        first,
    ) = project_heads(
        tokens,
        attend_line,
        heads_base,
        heads_rows,
        heads_right,
        heads_mag,
        segment_ids,
        squares_part,
        groups,
    )
    heads_out = attend(order, groups, post, first)
    output_sq, shrink_sq = squares[None, :1], squares[None, 1:]
    heads_parts = heads_out.reshape(1, groups, share, local_heads)
    joined, output_across = product(
        "output_product", 3, heads_parts, output_low, NN, left=output_rows
    )
    joined, expand_right_tied = tie(joined, expand_right)
    output_parts = [joined[0]] + [to_chip(joined[step], step) for step in range(1, chips)]
    expand_low, expand_sq = merge(
        expand_base, expand_rows, expand_right_tied, 1024, expand_base.shape[2]
    )
    grad_product, shrink_grad = shrink_back(
        order, cotangent, shrink_low, shrink_sq, shrink_mag[None], groups
    )
    output_parts, expand_low, grad_product = tie(output_parts, expand_low, grad_product)
    hidden, normed_own = row_call(
        "hidden",
        hidden_kernel,
        order,
        [(tokens, True)] + [(part, False) for part in output_parts],
        (output_sq[0], output_mag, expand_line),
        (F32, LOW),
        0,
        scale_first,
    )

    def feed(mine, step, **extra):
        return expand(
            4 + step, mine, expand_low, expand_sq, expand_mag, grad_product, step, **extra
        )

    arrived = arrive(normed_own)
    fed = [feed(normed_own, 0, left=expand_rows)]
    arrived, fed = tie(arrived, fed)
    fed = list(fed)
    for step in range(1, chips):
        extra = {}
        if step == chips - 1:
            extra = {"right": expand_right, "before": [f[3] for f in fed]}
        fed.append(feed(arrived[step - 1], step, **extra))
    expand_totals = [f[3] for f in fed]
    joined, shrink_rows_tied = tie([f[4] for f in fed], shrink_rows)
    mid_parts = [joined[0]] + [to_chip(joined[step], step) for step in range(1, chips)]
    shrink_places, shrink_total, shrink_across = shrink_product(
        order, [f[0] for f in fed], shrink_low, shrink_rows_tied, cotangent
    )
    shrink_pairs = chip_pairs(shrink_places)
    expand_adapter = adapter(
        "expand_adapter",
        order,
        in_pairs,
        [f[2] for f in fed],
        [f[1] for f in fed],
        expand_rows,
        expand_right,
        (fed[-1][5], fed[0][5], expand_sq, expand_mag, expand_totals),
    )
    mid_parts, shrink_pairs, expand_adapter = tie(mid_parts, shrink_pairs, expand_adapter)
    grad_hidden, output_grad_own, output_total, expand_gain_part = row_call(
        "hidden_back",
        hidden_back_kernel,
        order,
        [(cotangent, True), (tokens, True), (hidden, False)]
        + [(part, False) for part in mid_parts],
        (output_sq[0], output_mag, expand_line),
        (F32, LOW),
        2,
        scale_first,
    )
    arrived, near_sibling = arrive(output_grad_own), sibling(output_grad_own)
    shrink_joined = [join(pair) for pair in shrink_pairs[1:]]
    shrink_joined, shrink_rows_tied = tie(shrink_joined, shrink_rows)
    shrink_sums = adapter(
        "shrink_adapter",
        order,
        in_shrink,
        [f[0] for f in fed],
        [shrink_grad],
        shrink_rows_tied,
        shrink_right[None],
    )
    output_sums = adapter(
        "output_near_adapter",
        order,
        in_output(0),
        [heads_parts],
        [near_sibling, output_grad_own],
        output_rows,
        output_right[None],
    )
    arrived, near_sibling, shrink_joined, shrink_sums, output_sums = tie(
        arrived, near_sibling, shrink_joined, shrink_sums, output_sums
    )
    output_grad = [
        piece for pair in pairs_of(output_grad_own, near_sibling, arrived) for piece in pair
    ]
    shrink_parts = [shrink_pairs[0][1], sibling(shrink_pairs[0][0])] + [
        to_chip(values, step) for step, values in enumerate(shrink_joined, 1)
    ]
    heads_grads, heads_total = attend_back(
        order,
        groups,
        post,
        first,
        cos_table,
        sine_table,
        heads_mag,
        heads_sq,
        output_low,
        output_grad,
    )
    grad_parts = heads_grads.reshape(3, groups, share, local_heads)
    joined, both_totals, token_extra = product(
        "normed_product",
        20,
        grad_parts,
        heads_low,
        NT,
        correction=(heads_right, heads_sq, heads_mag, [heads_total]),
        lines=(output_total, shrink_total),
    )
    joined, shrink_parts, heads_rows_tied, output_rows_tied = tie(
        joined, shrink_parts, heads_rows, output_rows
    )
    output_total, shrink_total = both_totals[:1], both_totals[1:]
    token_parts = [joined[0]] + [to_chip(joined[step], step) for step in range(1, chips)]
    output_mag_part, output_left_part, output_right_part, *shrink_adapter = adapter(
        "output_far_adapter",
        order,
        in_output(CORES),
        [heads_parts],
        output_grad[CORES:],
        output_rows_tied,
        output_right[None],
        (output_low, output_across, output_sq, output_mag, [output_total[None]]),
        output_sums,
        (
            shrink_sums,
            shrink_right[None],
            (shrink_low, shrink_across, shrink_sq, shrink_mag, [shrink_total[None]]),
        ),
    )
    (
        expand_left_grad,
        shrink_right_grad,
        output_right_grad,
        expand_right_grad,
        shrink_left_grad,
        output_left_grad,
        expand_mag_grad,
        *heads_adapter,
    ) = reduce_devices(
        "reduce_first",
        1,
        [expand_adapter[1], shrink_adapter[2], output_right_part],
        [],
        [expand_adapter[2], shrink_adapter[1], output_left_part],
        [expand_adapter[0]],
        (
            in_heads,
            adapter_parts(
                [normed],
                [heads_grads],
                heads_rows_tied,
                heads_right,
                (token_extra, heads_across, heads_sq, heads_mag, [heads_total]),
                (),
            ),
        ),
    )
    (mixed,) = row_call(
        "mixed",
        mixed_kernel,
        order,
        [(hidden, False)] + [(part, False) for part in shrink_parts],
        (shrink_sq[0], shrink_mag),
        (LOW,),
        0,
        scale_first,
    )
    token_parts, heads_adapter, mixed = tie(token_parts, heads_adapter, mixed)
    grad_tokens, attend_gain_part = row_call(
        "token_back",
        token_back_kernel,
        order,
        [(tokens, True), (grad_hidden, False)] + [(part, False) for part in token_parts],
        (attend_line,),
        (F32,),
        1,
        lambda gain: (gain,),
    )
    (
        heads_left_grad,
        expand_gain_grad,
        attend_gain_grad,
        heads_right_grad,
        heads_mag_grad,
        shrink_mag_grad,
        output_mag_grad,
    ) = reduce_devices(
        "reduce_last",
        30,
        [heads_adapter[1]],
        [expand_gain_part[None], attend_gain_part[None]],
        [heads_adapter[2]],
        [heads_adapter[0], shrink_adapter[0], output_mag_part],
    )
    (
        expand_left_grad,
        shrink_right_grad,
        output_right_grad,
        expand_right_grad,
        shrink_left_grad,
        output_left_grad,
        expand_mag_grad,
        heads_left_grad,
        expand_gain_grad,
        attend_gain_grad,
        heads_right_grad,
        heads_mag_grad,
        shrink_mag_grad,
        output_mag_grad,
    ) = copy_out(
        [
            expand_left_grad,
            shrink_right_grad,
            output_right_grad,
            expand_right_grad,
            shrink_left_grad,
            output_left_grad,
            expand_mag_grad,
            heads_left_grad,
            expand_gain_grad,
            attend_gain_grad,
            heads_right_grad,
            heads_mag_grad,
            shrink_mag_grad,
            output_mag_grad,
        ]
    )
    return (
        mixed,
        grad_tokens,
        attend_gain_grad[0, 0],
        expand_gain_grad[0, 0],
        jnp.swapaxes(heads_left_grad, 1, 2),
        heads_right_grad,
        heads_mag_grad[:, 0],
        output_left_grad[0].T,
        output_right_grad[0],
        output_mag_grad[0, 0],
        jnp.swapaxes(expand_left_grad, 1, 2),
        expand_right_grad,
        expand_mag_grad[:, 0],
        shrink_left_grad[0].T,
        shrink_right_grad[0],
        shrink_mag_grad[0, 0],
    )


def solution(mesh):
    placed = (
        P("dp", None),
        P("dp", None),
        P("dp", None),
        P(),
        P(),
        P(None, None, "mp"),
        P(),
        P(None, None, "mp"),
        P(None, "mp"),
        P("mp", None),
        P("mp", None),
        P(),
        P(),
        P(None, None, "mp"),
        P(),
        P(None, None, "mp"),
        P(None, "mp"),
        P("mp", None),
        P("mp", None),
        P(),
        P(),
    )
    return jax.shard_map(
        body,
        mesh=mesh,
        in_specs=placed,
        out_specs=(
            P(("dp", "mp"), None),
            P(("dp", "mp"), None),
            P(),
            P(),
            P(),
            P(None, None, "mp"),
            P(None, "mp"),
            P("mp", None),
            P(),
            P(),
            P(),
            P(None, None, "mp"),
            P(None, "mp"),
            P("mp", None),
            P(),
            P(),
        ),
        check_vma=False,
    )
```

```python
import functools

import jax
import jax.numpy as jnp
import ml_dtypes
import numpy as np
from jax import lax
from jax.experimental import pallas as pl
from jax.experimental.pallas import tpu as pltpu
from jax.sharding import PartitionSpec as P

HEAD_DIM = 128
CORES = 2
LONGEST = 512
ATTEND_BLOCK = 256
ADAPT_SCALE = 2.0
NORM_EPS = 1e-05
ROPE_BASE = 10000.0
MASKED = -1e30

F32 = jnp.float32
LOW = jnp.bfloat16
NN = (((1,), (0,)), ((), ()))
NT = (((1,), (1,)), ((), ()))
TN = (((0,), (0,)), ((), ()))


MESH_IDS = pl.DeviceIdType.MESH


def sibling_id():
    me = lax.axis_index("mp")
    return me // CORES * CORES + lax.rem(me + 1, CORES)


def greet(peers):
    for peer in peers:
        pl.semaphore_signal(
            pltpu.get_barrier_semaphore(), 1, device_id={"mp": peer}, device_id_type=MESH_IDS
        )


def greeted(count):
    pl.semaphore_wait(pltpu.get_barrier_semaphore(), count)


def remote(source, target, send_sem, recv_sem, peer):
    return pltpu.make_async_remote_copy(
        src_ref=source,
        dst_ref=target,
        send_sem=send_sem,
        recv_sem=recv_sem,
        device_id={"mp": peer},
        device_id_type=MESH_IDS,
    )


def dot(left, right, dims=NN):
    return lax.dot_general(left, right, dims, preferred_element_type=F32)


def shape(dims, kind):
    return jax.ShapeDtypeStruct(tuple(dims), kind)


def call(name, kernel, operands, grid, in_specs, out_specs, out_shape, scratch=(), prefetch=(), flops=0, mib=63.5, identity=None):
    moved = sum(v.size * v.dtype.itemsize for v in operands)
    moved += sum(v.size * v.dtype.itemsize for v in out_shape)
    return pl.pallas_call(
        kernel,
        name=name,
        out_shape=out_shape,
        grid_spec=pltpu.PrefetchScalarGridSpec(
            num_scalar_prefetch=len(prefetch),
            grid=grid,
            in_specs=in_specs,
            out_specs=out_specs,
            scratch_shapes=scratch,
        ),
        compiler_params=pltpu.CompilerParams(
            vmem_limit_bytes=int(mib * 2**20), collective_id=identity, has_side_effects=identity is not None
        ),
        cost_estimate=pl.CostEstimate(flops=flops // 16, bytes_accessed=moved // 16, transcendentals=0),
    )(*prefetch, *operands)


def tile_of(size, most):
    return most if size % most == 0 else size


def split_rows(values):
    top = values.astype(LOW)
    rest = (values - top.astype(F32)).astype(LOW)
    return jnp.concatenate([top, rest], axis=0)


def turned(left_map):
    return jnp.swapaxes(left_map, -1, -2)


def norm_weight(total, squares, magnitude):
    norm = jnp.sqrt(squares)
    return total * magnitude / (norm * norm * norm)


def sum_refs(refs):
    total = refs[0][...]
    for ref in refs[1:]:
        total = total + ref[...]
    return total


def fold(values):
    half = values.shape[0] // 2
    return values[:half] + values[half:]


def merge_tile(base_at, low_put, left, right, depth):
    rank = right.shape[0]
    doubled = ADAPT_SCALE * right
    top = doubled.astype(LOW)
    rest = (doubled - top.astype(F32)).astype(LOW)
    right_stack = jnp.concatenate([top, rest, top], axis=0)
    left_pair = split_rows(left)
    left_stack = jnp.concatenate([left_pair[:rank], left_pair[:rank], left_pair[rank:]], axis=0)
    width = right.shape[1]
    wide = 256 if width == 512 else width
    step = tile_of(depth, 1024)
    squares = []
    for at in range(0, width, wide):
        columns = slice(at, at + wide)
        total = jnp.zeros((1, wide), F32)
        for start in range(0, depth, step):
            merged = base_at(start, step, columns).astype(F32) + dot(
                left_stack[:, start : start + step], right_stack[:, columns], TN
            )
            low_put(start, step, columns, merged.astype(LOW))
            total = total + jnp.sum(merged * merged, axis=0, keepdims=True)
        squares.append(total)
    return jnp.concatenate(squares, axis=1)


def merge_pair_kernel(*refs):
    for n in range(2):
        base_ref, left_ref, right_ref = refs[3 * n : 3 * n + 3]
        low_ref, squares_ref = refs[6 + n], refs[8]
        depth = base_ref.shape[0]
        if low_ref.shape[0] > depth:
            low_ref[depth:, :] = jnp.zeros((low_ref.shape[0] - depth, low_ref.shape[1]), LOW)

        def put(start, step, columns, tile, low_ref=low_ref):
            low_ref[start : start + step, columns] = tile

        squares_ref[n : n + 1, :] = merge_tile(
            lambda start, step, columns, base_ref=base_ref: base_ref[start : start + step, columns],
            put,
            left_ref[...],
            right_ref[...],
            depth,
        )


def merge_pair(triples):
    operands, in_specs, low_specs, low_shapes = [], [], [], []
    width = triples[0][0].shape[1]
    wide = tile_of(width, 512)
    for base, left, right in triples:
        depth, rank = base.shape[0], right.shape[0]
        operands += [base, left, right]
        in_specs += [
            pl.BlockSpec((depth, wide), lambda n: (0, n)),
            pl.BlockSpec((rank, depth), lambda n: (0, 0)),
            pl.BlockSpec((rank, wide), lambda n: (0, n)),
        ]
        low_specs.append(pl.BlockSpec((padded(depth), wide), lambda n: (0, n)))
        low_shapes.append(shape((padded(depth), width), LOW))
    return call(
        "merge_pair",
        merge_pair_kernel,
        tuple(operands),
        (width // wide,),
        in_specs,
        low_specs + [pl.BlockSpec((2, wide), lambda n: (0, n))],
        low_shapes + [shape((2, width), F32)],
        flops=2 * sum(v.size for v in operands) * 256,
    )


def merge_kernel(base_ref, left_ref, right_ref, low_ref, squares_ref):
    depth, width = base_ref.shape[1:]
    if low_ref.shape[1] > depth:
        low_ref[0, depth:, :] = jnp.zeros((low_ref.shape[1] - depth, low_ref.shape[2]), LOW)
    if low_ref.shape[2] > width:
        spare = low_ref.shape[2] - width
        low_ref[0, :, width:] = jnp.zeros((low_ref.shape[1], spare), LOW)
        squares_ref[0, :, width:] = jnp.ones((1, spare), F32)

    def put(start, step, columns, tile):
        low_ref[0, start : start + step, columns] = tile

    squares = merge_tile(
        lambda start, step, columns: base_ref[0, start : start + step, columns],
        put,
        left_ref[0],
        right_ref[0],
        depth,
    )

    @pl.when(pl.program_id(2) == 0)
    def _():
        squares_ref[0, :, :width] = squares

    @pl.when(pl.program_id(2) > 0)
    def _():
        squares_ref[0, :, :width] += squares


def padded(size):
    return -(-size // 256) * 256


def pad_last(values, size):
    return jnp.pad(values, [(0, 0)] * (values.ndim - 1) + [(0, size - values.shape[-1])])


def merge(base, left, right, deep, wide):
    members, depth, width = base.shape
    low_deep = padded(deep) if deep == depth else deep
    low_wide = padded(wide) if wide == width else wide
    low_shape = (members, depth // deep * low_deep, width // wide * low_wide)
    rank = right.shape[1]
    return call(
        "merge",
        merge_kernel,
        (base, left, right),
        (members, width // wide, depth // deep),
        [
            pl.BlockSpec((1, deep, wide), lambda m, n, k: (m, k, n)),
            pl.BlockSpec((1, rank, deep), lambda m, n, k: (m, 0, k)),
            pl.BlockSpec((1, rank, wide), lambda m, n, k: (m, 0, n)),
        ],
        [
            pl.BlockSpec((1, low_deep, low_wide), lambda m, n, k: (m, k, n)),
            pl.BlockSpec((1, 1, low_wide), lambda m, n, k: (m, 0, n)),
        ],
        [shape(low_shape, LOW), shape((members, 1, low_shape[2]), F32)],
        flops=2 * members * depth * width * 256,
    )


def rms_rows(values):
    return lax.rsqrt(jnp.mean(values * values, axis=1, keepdims=True) + NORM_EPS)


TABLE_STEP = 32


def table_pieces(places):
    half = np.arange(HEAD_DIM) % (HEAD_DIM // 2)
    angles = np.asarray(places)[:, None] * ROPE_BASE ** (-2.0 * half / HEAD_DIM)[None, :]
    rest = np.concatenate([np.cos(angles), np.sin(angles)], axis=1)
    pieces = []
    for _ in range(3):
        pieces.append(rest.astype(ml_dtypes.bfloat16))
        rest = rest - pieces[-1].astype(np.float64)
    return jnp.asarray(np.concatenate(pieces, axis=0))


def rotation(first, coarse, fine):
    rows = first.shape[0]
    position = lax.broadcasted_iota(jnp.int32, (rows, 1), 0) - first
    lane = lax.broadcasted_iota(jnp.int32, (rows, 3 * TABLE_STEP), 1) % TABLE_STEP
    pick = lambda place, table: dot((lane == place).astype(F32).astype(LOW), table)
    high = pick(position // TABLE_STEP, coarse)
    small = pick(position % TABLE_STEP, fine)
    cos_a, sin_a = high[:, :HEAD_DIM], high[:, HEAD_DIM:]
    cos_b, sin_b = small[:, :HEAD_DIM], small[:, HEAD_DIM:]
    sine = sin_a * cos_b + cos_a * sin_b
    left_half = lax.broadcasted_iota(jnp.int32, sine.shape, 1) < HEAD_DIM // 2
    return cos_a * cos_b - sin_a * sin_b, jnp.where(left_half, -sine, sine)


def heads_kernel(
    token_ref,
    gain_ref,
    base_ref,
    left_ref,
    right_ref,
    magnitude_ref,
    segment_ref,
    coarse_ref,
    fine_ref,
    part_ref,
    normed_ref,
    low_ref,
    post_ref,
    squares_ref,
    across_ref,
    cos_ref,
    sine_ref,
    sum_ref,
    first_ref,
    rows_all,
    part_mine,
    part_got,
    send_sems,
    recv_sems,
):
    total_rows = token_ref.shape[0]
    depth, width = base_ref.shape[1:]
    rank = right_ref.shape[1]
    groups = part_got.shape[0]
    me = lax.axis_index("mp")
    peers = [lax.rem(me + k, groups) for k in range(groups)]
    part_copies = [
        remote(part_mine, part_got.at[k], send_sems.at[k], recv_sems.at[k], peers[k])
        for k in range(1, groups)
    ]

    @pl.when(pl.program_id(0) == 0)
    def _():
        greet(peers[1:])
        part_mine[...] = part_ref[...]
        step = 128

        def some(i, carry):
            at = pl.ds(pl.multiple_of(i * step, step), step)
            values = token_ref[at, :].astype(F32)
            low = (values * rms_rows(values) * gain_ref[...]).astype(LOW)
            normed_ref[at, :] = low
            rows_all[at, :] = low
            return carry

        lax.fori_loop(0, total_rows // step, some, 0)
        ids = segment_ref[...].astype(F32)
        ids_down = jnp.transpose(jnp.broadcast_to(ids, (8, total_rows)))[:, :1]
        for start in range(0, total_rows, 256):
            rows = slice(start, start + 256)
            smaller = jnp.where(ids < ids_down[rows], 1.0, 0.0)
            first = jnp.sum(smaller, axis=1, keepdims=True).astype(jnp.int32)
            first_ref[rows, :] = first
            cosine, sine = rotation(first - start, coarse_ref[...], fine_ref[...])
            cos_ref[rows, :] = cosine
            sine_ref[rows, :] = sine
        greeted(groups - 1)
        for copy in part_copies:
            copy.start()

    @pl.when(pl.program_id(0) == pl.num_programs(0) - 1)
    def _():
        total = part_mine[...]
        for k, copy in enumerate(part_copies, 1):
            copy.wait_recv()
            total = total + part_got[k]
        sum_ref[...] = total
        for copy in part_copies:
            copy.wait_send()

    rows_all[total_rows:, :] = left_ref[0].astype(LOW)
    turning = pl.program_id(0) < 2
    wide = 256

    def put(start, step, columns, tile):
        low_ref[0, start : start + step, columns] = tile

    squares_ref[0] = merge_tile(
        lambda start, step, columns: base_ref[0, start : start + step, columns],
        put,
        left_ref[0],
        right_ref[0],
        depth,
    )
    for column in range(0, width, wide):
        columns = slice(column, column + wide)
        magnitude = magnitude_ref[pl.ds(pl.program_id(0), 1), columns]
        scale = magnitude / jnp.sqrt(squares_ref[0, :, columns])
        low = low_ref[0, :, columns]
        step = min(512, total_rows)
        for start in range(0, total_rows, step):
            last = start + step == total_rows
            rows = slice(start, start + step)
            pre = dot(rows_all[start : start + step + (rank if last else 0), :], low)
            if last:
                across_ref[0, :, columns] = pre[step:]
            post = pre[:step] * scale
            cos_table = jnp.where(turning, cos_ref[rows, :], 1.0)
            sine_table = jnp.where(turning, sine_ref[rows, :], 0.0)
            for head in range(0, wide, HEAD_DIM):
                piece = post[:, head : head + HEAD_DIM]
                other = pltpu.roll(piece, HEAD_DIM // 2, 1)
                post_ref[0, rows, column + head : column + head + HEAD_DIM] = (
                    piece * cos_table + other * sine_table
                ).astype(LOW)


def project_heads(tokens, gain, base, left, right, magnitude, segments, part, groups):
    members, depth, width = base.shape
    rows, rank = tokens.shape[0], right.shape[1]
    coarse = table_pieces(np.arange(TABLE_STEP) * TABLE_STEP)
    fine = table_pieces(np.arange(TABLE_STEP))
    whole = lambda v: pl.BlockSpec(v.shape, lambda m: (0,) * v.ndim)
    of_member = lambda *dims: pl.BlockSpec((1,) + dims, lambda m: (m, 0, 0))
    table = pl.BlockSpec((rows, HEAD_DIM), lambda m: (0, 0))
    return call(
        "project_heads",
        heads_kernel,
        (tokens, gain, base, left, right, magnitude, segments, coarse, fine, part),
        (members,),
        [
            whole(tokens),
            whole(gain),
            of_member(depth, width),
            of_member(rank, depth),
            of_member(rank, width),
            whole(magnitude),
            whole(segments),
            whole(coarse),
            whole(fine),
            whole(part),
        ],
        [
            whole(tokens),
            of_member(depth, width),
            of_member(rows, width),
            of_member(1, width),
            of_member(rank, width),
            table,
            table,
            whole(part),
            pl.BlockSpec((rows, 1), lambda m: (0, 0)),
        ],
        [
            shape((rows, depth), LOW),
            shape(base.shape, LOW),
            shape((members, rows, width), LOW),
            shape((members, 1, width), F32),
            shape((members, rank, width), F32),
            shape((rows, HEAD_DIM), F32),
            shape((rows, HEAD_DIM), F32),
            shape(part.shape, F32),
            shape((rows, 1), jnp.int32),
        ],
        scratch=[
            pltpu.VMEM((rows + rank, depth), LOW),
            pltpu.VMEM(part.shape, F32),
            pltpu.VMEM((groups,) + part.shape, F32),
            pltpu.SemaphoreType.DMA((groups,)),
            pltpu.SemaphoreType.DMA((groups,)),
        ],
        identity=2,
        flops=2 * members * rows * depth * width,
    )


def key_start(block):
    return max(0, (block * ATTEND_BLOCK - (LONGEST - 1)) // ATTEND_BLOCK * ATTEND_BLOCK)


def masked_probs(scores, first, row_at, key_at):
    scores = scores * HEAD_DIM ** (-0.5)
    places = row_at + lax.broadcasted_iota(jnp.int32, scores.shape, 0)
    others = key_at + lax.broadcasted_iota(jnp.int32, scores.shape, 1)
    scores = jnp.where((others >= first) & (others <= places), scores, MASKED)
    exp_scores = jnp.exp(scores - jnp.max(scores, axis=1, keepdims=True))
    return exp_scores * (1.0 / jnp.sum(exp_scores, axis=1, keepdims=True))


class Unit:
    def __init__(self, head, block):
        self.row_at, self.key_at = block * ATTEND_BLOCK, key_start(block)
        self.rows = slice(self.row_at, self.row_at + ATTEND_BLOCK)
        self.keys = slice(self.key_at, self.row_at + ATTEND_BLOCK)
        self.lanes = slice(head * HEAD_DIM, (head + 1) * HEAD_DIM)


def units_of(rows, width, most):
    units = [
        Unit(head, block)
        for block in range(rows // ATTEND_BLOCK)
        for head in range(width // HEAD_DIM)
    ]
    return [units[at : at + most] for at in range(0, len(units), most)]


def put_rows(ref, lead, row_at, lanes, values, order_ref, groups):
    share = ref.shape[len(lead)] // groups
    step = min(share, values.shape[0])
    for start in range(0, values.shape[0], step):
        group = (row_at + start) // share
        inside = (row_at + start) % share
        at = pl.multiple_of(order_ref[groups + group] * share + inside, step)
        ref[(*lead, pl.ds(at, step), lanes)] = values[start : start + step].astype(ref.dtype)


def attend_kernel(groups, order_ref, query_ref, key_ref, value_ref, first_ref, out_ref):
    for some in units_of(*query_ref.shape[1:], 4):
        scores = [
            dot(query_ref[0, u.rows, u.lanes], key_ref[0, u.keys, u.lanes], NT) for u in some
        ]
        probs = [
            masked_probs(s, first_ref[u.rows, :], u.row_at, u.key_at).astype(LOW)
            for u, s in zip(some, scores)
        ]
        for u, p in zip(some, probs):
            mixed = dot(p, value_ref[0, u.keys, u.lanes])
            put_rows(out_ref, (), u.row_at, u.lanes, mixed, order_ref, groups)


def attend(order, groups, post, first):
    rows, width = post.shape[1:]
    wide = 2 * HEAD_DIM
    member = lambda m: pl.BlockSpec((1, rows, wide), lambda h, o: (m, 0, h))
    return call(
        "attend",
        functools.partial(attend_kernel, groups),
        (post, post, post, first),
        (width // wide,),
        [member(0), member(1), member(2), pl.BlockSpec((rows, 1), lambda h, o: (0, 0))],
        [pl.BlockSpec((rows, wide), lambda h, o: (0, h))],
        [shape((rows, width), LOW)],
        prefetch=(order,),
        flops=4 * rows * rows * width,
    )[0]


def attend_back_kernel(
    groups,
    order_ref,
    query_ref,
    key_ref,
    value_ref,
    first_ref,
    cos_ref,
    sine_ref,
    magnitude_ref,
    squares_ref,
    low_ref,
    *rest,
):
    pieces, (grad_ref, total_ref, upper_all, heads_grad, key_grad, value_grad, sems) = rest[:-7], rest[-7:]
    rows_all, width = query_ref.shape[1:]
    share = rows_all // groups

    @pl.when(pl.program_id(0) == 0)
    def _():
        copies = []
        for place, piece in enumerate(pieces):
            at = pl.multiple_of(order_ref[place] * share, share)
            copies.append(
                pltpu.make_async_copy(piece, upper_all.at[pl.ds(at, share), :], sems.at[place])
            )
            copies[-1].start()
        for copy in copies:
            copy.wait()

    step = min(512, rows_all)
    for start in range(0, rows_all, step):
        at = slice(start, start + step)
        heads_grad[at, :] = dot(upper_all[at, :], low_ref[0], NT).astype(LOW)
    norm = [jnp.sqrt(squares_ref[m]) for m in range(3)]
    scale = [magnitude_ref[m : m + 1] / norm[m] for m in range(3)]
    heads = range(0, width, HEAD_DIM)
    totals = [jnp.zeros((1, width), F32) for _ in range(3)]
    filled = set()

    def back(values, rows):
        return values * cos_ref[rows, :] - pltpu.roll(values, HEAD_DIM // 2, 1) * sine_ref[rows, :]

    def add(ref, unit, values):
        for start in range(0, values.shape[0], ATTEND_BLOCK):
            at = unit.key_at + start
            rows = slice(at, at + ATTEND_BLOCK)
            name = (id(ref), at, unit.lanes.start)
            if name in filled:
                ref[rows, unit.lanes] += values[start : start + ATTEND_BLOCK]
            else:
                filled.add(name)
                ref[rows, unit.lanes] = values[start : start + ATTEND_BLOCK]

    def spread(per_head):
        return jnp.concatenate(per_head, axis=1)

    query_totals = [jnp.zeros((1, HEAD_DIM), F32) for _ in heads]
    for some in units_of(rows_all, width, 2):
        scores = [
            dot(query_ref[0, u.rows, u.lanes], key_ref[0, u.keys, u.lanes], NT) for u in some
        ]
        grad_weights = [
            dot(heads_grad[u.rows, u.lanes], value_ref[0, u.keys, u.lanes], NT) for u in some
        ]
        probs = [
            masked_probs(s, first_ref[u.rows, :], u.row_at, u.key_at)
            for u, s in zip(some, scores)
        ]
        grad_scores = [
            (p * (g - jnp.sum(p * g, axis=1, keepdims=True))).astype(LOW)
            for p, g in zip(probs, grad_weights)
        ]
        for u, p, g in zip(some, probs, grad_scores):
            add(value_grad, u, dot(p.astype(LOW), heads_grad[u.rows, u.lanes], TN))
            add(key_grad, u, dot(g, query_ref[0, u.rows, u.lanes], TN))
        for u, g in zip(some, grad_scores):
            grad = back(dot(g, key_ref[0, u.keys, u.lanes]) * HEAD_DIM ** (-0.5), u.rows)
            head = u.lanes.start // HEAD_DIM
            post = back(query_ref[0, u.rows, u.lanes].astype(F32), u.rows)
            query_totals[head] = query_totals[head] + jnp.sum(grad * post, axis=0, keepdims=True)
            put_rows(grad_ref, (0,), u.row_at, u.lanes, grad * scale[0][:, u.lanes], order_ref, groups)
    totals[0] = spread(query_totals)
    for row_at in range(0, rows_all, ATTEND_BLOCK):
        rows = slice(row_at, row_at + ATTEND_BLOCK)
        for head in heads:
            lanes = slice(head, head + HEAD_DIM)
            grad = back(key_grad[rows, lanes] * HEAD_DIM ** (-0.5), rows)
            post = back(key_ref[0, rows, lanes].astype(F32), rows)
            part = jnp.sum(grad * post, axis=0, keepdims=True)
            query_totals[head // HEAD_DIM] = part if row_at == 0 else query_totals[head // HEAD_DIM] + part
            put_rows(grad_ref, (1,), row_at, lanes, grad * scale[1][:, lanes], order_ref, groups)
        grad = value_grad[rows, :]
        totals[2] = totals[2] + jnp.sum(grad * value_ref[0, rows, :].astype(F32), axis=0, keepdims=True)
        put_rows(grad_ref, (2,), row_at, slice(0, width), grad * scale[2], order_ref, groups)
    totals[1] = spread(query_totals)
    for m in range(3):
        total_ref[m] = totals[m] / scale[m]


def attend_back(order, groups, post, first, cos_table, sine_table, magnitude, squares, low, pieces):
    rows, width = post.shape[1:]
    depth = low.shape[2]
    wide = 2 * HEAD_DIM
    member = lambda m: pl.BlockSpec((1, rows, wide), lambda h, o: (m, 0, h))
    table = pl.BlockSpec((rows, HEAD_DIM), lambda h, o: (0, 0))
    column = pl.BlockSpec((3, 1, wide), lambda h, o: (0, 0, h))
    return call(
        "attend_back",
        functools.partial(attend_back_kernel, groups),
        (post, post, post, first, cos_table, sine_table, magnitude, squares, low, *pieces),
        (width // wide,),
        [
            member(0),
            member(1),
            member(2),
            pl.BlockSpec((rows, 1), lambda h, o: (0, 0)),
            table,
            table,
            pl.BlockSpec((3, wide), lambda h, o: (0, h)),
            column,
            pl.BlockSpec((1, wide, depth), lambda h, o: (0, h, 0)),
            *[pl.BlockSpec(memory_space=pl.ANY) for _ in pieces],
        ],
        [pl.BlockSpec((3, rows, wide), lambda h, o: (0, 0, h)), column],
        [shape((3, rows, width), LOW), shape((3, 1, width), F32)],
        scratch=[
            pltpu.VMEM((rows, depth), LOW),
            pltpu.VMEM((rows, wide), LOW),
            pltpu.VMEM((rows, wide), F32),
            pltpu.VMEM((rows, wide), F32),
            pltpu.SemaphoreType.DMA((len(pieces),)),
        ],
        prefetch=(order,),
        flops=10 * rows * rows * width + 2 * rows * width * depth,
    )


def product_kernel(dims, n_totals, n_lines, has_gain, steps, *refs):
    value_ref, weight_ref = refs[:2]
    if n_totals == 0:
        left_ref, *refs = refs[2:]
    else:
        right_ref, squares_ref, magnitude_ref = refs[2:5]
        totals, refs = refs[5 : 5 + n_totals], refs[5 + n_totals :]
    lines = []
    if has_gain:
        normed_ref, gain_ref, *refs = refs
    if n_lines > 0:
        lines, refs = refs[:n_lines], refs[n_lines:]
        *refs, line_mine, line_got, line_send_sems, line_recv_sems = refs
    *outs, extra_ref, rows_all, sent, got, send_sems, recv_sems = refs
    if has_gain:
        *outs, gain_out = outs
    if n_lines > 0:
        *outs, line_out = outs
    members, groups, share, inner = value_ref.shape
    count, wide = groups * share, extra_ref.shape[2]
    now = pl.program_id(0)
    sibling = sibling_id()
    me = lax.axis_index("mp")
    peers = [lax.rem(me + k, groups) for k in range(1, groups)] if n_lines > 0 else [sibling]
    line_copies = [
        remote(line_mine, line_got.at[k], line_send_sems.at[k], line_recv_sems.at[k], peer)
        for k, peer in enumerate(peers if n_lines > 0 else [], 1)
    ]

    @pl.when(now == 0)
    def _():
        greet(peers)
        for n, ref in enumerate(lines):
            line_mine[n : n + 1, :] = ref[...]
        if n_totals > 0:
            total = sum_refs(totals)
        for m in range(members):
            rows_all[m, :count, :] = value_ref[m].reshape(count, inner)
            if n_totals == 0:
                rows_all[m, count:, :] = left_ref[m].astype(LOW)
            else:
                weight = norm_weight(total[m], squares_ref[m], magnitude_ref[m : m + 1])
                rows_all[m, count:, :] = (right_ref[m] * weight).astype(LOW)

    result = None
    for m in range(members):
        part = dot(rows_all[m], weight_ref[m], dims)
        extra_ref[m] = part[count:]
        result = part[:count] if result is None else result + part[:count]

    def columns(step):
        return pl.ds(pl.multiple_of(step * wide, wide), wide)

    def copy(step):
        return remote(sent.at[step], got.at[step], send_sems.at[step], recv_sems.at[step], sibling)

    def add(step):
        copy(step).wait_recv()
        for n, ref in enumerate(outs):
            total = ref[:, columns(step)].astype(F32) + got[step, n].astype(F32)
            ref[:, columns(step)] = total.astype(LOW)

    if has_gain:
        terms = jnp.zeros((1, wide), F32)
        for place in range(groups):
            group = lax.rem(me // CORES + place // CORES, groups // CORES) * CORES
            group = group + lax.rem(me + 1 + place, CORES)
            rows = pl.ds(pl.multiple_of(group * share, share), share)
            mine = result[place * share : (place + 1) * share]
            terms = terms + jnp.sum(
                mine * normed_ref[rows, :].astype(F32), axis=0, keepdims=True
            )
        gain_out[...] = terms / gain_ref[...]
    for n, ref in enumerate(outs):
        at = CORES * n * share
        sent[now, n] = result[at : at + share].astype(LOW)
        ref[:, columns(now)] = result[at + share : at + CORES * share].astype(LOW)

    @pl.when(now == 0)
    def _():
        greeted(len(peers))
        for each in line_copies:
            each.start()

    copy(now).start()

    @pl.when(now > 0)
    def _():
        add(now - 1)

    @pl.when(now == steps - 1)
    def _():
        add(now)
        for step in range(steps):
            copy(step).wait_send()
        if n_lines > 0:
            line_sum = line_mine[...]
            for k, each in enumerate(line_copies, 1):
                each.wait_recv()
                line_sum = line_sum + line_got[k]
            line_out[...] = line_sum
            for each in line_copies:
                each.wait_send()


def product(name, identity, values, weights, dims, left=None, correction=None, lines=(), gain=()):
    members, groups, share, inner = values.shape
    chips = groups // CORES
    width = weights.shape[2] if dims is NN else weights.shape[1]
    wide = tile_of(width, 512)
    steps = width // wide
    if dims is NN:
        weight_spec = pl.BlockSpec((members, inner, wide), lambda n: (0, 0, n))
    else:
        weight_spec = pl.BlockSpec((members, wide, inner), lambda n: (0, n, 0))
    if correction is None:
        extra, n_totals, rank = (left,), 0, left.shape[1]
    else:
        right, squares, magnitude, totals = correction
        extra, n_totals, rank = (right, squares, magnitude, *totals), len(totals), right.shape[1]
    fixed = lambda v: pl.BlockSpec(v.shape, lambda n: (0,) * v.ndim)
    out = pl.BlockSpec((share, width), lambda n: (0, 0))
    line_specs, line_shapes, line_scratch = [], [], []
    if lines:
        line = (len(lines), width)
        line_specs = [pl.BlockSpec(line, lambda n: (0, 0))]
        line_shapes = [shape(line, F32)]
        line_scratch = [
            pltpu.VMEM(line, F32),
            pltpu.VMEM((groups,) + line, F32),
            pltpu.SemaphoreType.DMA((groups,)),
            pltpu.SemaphoreType.DMA((groups,)),
        ]
    gain_specs, gain_shapes, gain_in = [], [], []
    if gain:
        one = pl.BlockSpec((1, wide), lambda n: (0, n))
        gain_in = [pl.BlockSpec((gain[0].shape[0], wide), lambda n: (0, n)), one]
        gain_specs, gain_shapes = [one], [shape((1, width), F32)]
    results = call(
        name,
        functools.partial(product_kernel, dims, n_totals, len(lines), bool(gain), steps),
        (values, weights, *extra, *gain, *lines),
        (steps,),
        [fixed(values), weight_spec]
        + [fixed(v) for v in extra]
        + gain_in
        + [fixed(v) for v in lines],
        [out] * chips + line_specs + gain_specs + [pl.BlockSpec((members, rank, wide), lambda n: (0, 0, n))],
        [shape((share, width), LOW)] * chips
        + line_shapes
        + gain_shapes
        + [shape((members, rank, width), F32)],
        scratch=[
            pltpu.VMEM((members, groups * share + rank, inner), LOW),
            pltpu.VMEM((steps, chips, share, wide), LOW),
            pltpu.VMEM((steps, chips, share, wide), LOW),
            pltpu.SemaphoreType.DMA((steps,)),
            pltpu.SemaphoreType.DMA((steps,)),
        ]
        + line_scratch,
        flops=2 * members * groups * share * inner * width,
        identity=identity,
    )
    return results[:chips], *results[chips:]


def shrink_kernel(chips, order_ref, *refs):
    values, (weight_ref, left_ref, cot_ref), outs = refs[:chips], refs[chips : chips + 3], refs[chips + 3 :]
    total_ref, across_ref, rows_all = outs[-3:]
    both, inner = values[0].shape
    share, depth = both // CORES, left_ref.shape[2]
    count = chips * both

    @pl.when(pl.program_id(0) == 0)
    def _():
        for step, ref in enumerate(values):
            rows_all[step * both : (step + 1) * both, :] = ref[...]
        if inner > depth:
            rows_all[count:, depth:] = jnp.zeros((rows_all.shape[0] - count, inner - depth), LOW)
        rows_all[count:, :depth] = left_ref[0].astype(LOW)

    result = dot(rows_all[...], weight_ref[0])
    across_ref[0] = result[count:]
    total = jnp.zeros((1, weight_ref.shape[2]), F32)
    for place in range(chips * CORES):
        pre = result[place * share : (place + 1) * share]
        outs[place][...] = pre.astype(LOW)
        at = pl.multiple_of(order_ref[place] * share, share)
        cot = cot_ref[pl.ds(at, share), :].astype(F32)
        total = total + jnp.sum(pre * cot, axis=0, keepdims=True)
    total_ref[...] = total


def shrink_product(order, values, weights, left, cotangent):
    chips = len(values)
    share, inner = values[0].shape[0] // CORES, values[0].shape[1]
    width, rank = weights.shape[2], left.shape[1]
    rows = chips * CORES * share
    wide = tile_of(width, 512)
    fixed = lambda v: pl.BlockSpec(v.shape, lambda n, o: (0,) * v.ndim)
    results = call(
        "shrink_product",
        functools.partial(shrink_kernel, chips),
        (*values, weights, left, cotangent),
        (width // wide,),
        [fixed(v) for v in values]
        + [
            pl.BlockSpec((1, inner, wide), lambda n, o: (0, 0, n)),
            fixed(left),
            pl.BlockSpec((rows, wide), lambda n, o: (0, n)),
        ],
        [pl.BlockSpec((share, wide), lambda n, o: (0, n))] * (chips * CORES)
        + [
            pl.BlockSpec((1, wide), lambda n, o: (0, n)),
            pl.BlockSpec((1, rank, wide), lambda n, o: (0, 0, n)),
        ],
        [shape((share, width), LOW)] * (chips * CORES)
        + [shape((1, width), F32), shape((1, rank, width), F32)],
        scratch=[pltpu.VMEM((rows + rank, inner), LOW)],
        prefetch=(order,),
        flops=2 * rows * inner * width,
    )
    return results[: chips * CORES], results[-2], results[-1]


def row_call(name, kernel, order, given, whole, out_kinds, sums, prepare):
    share = min(v.shape[0] for v, _ in given)
    width = given[0][0].shape[1]
    halves = 2
    half = share // halves
    count = len(given)

    def run(order_ref, *refs):
        sources, rest = refs[:count], refs[count : -count - 1]
        held, sems = refs[-count - 1 : -1], refs[-1]

        def copies(part):
            for i, ((_, cut), source, target) in enumerate(zip(given, sources, held)):
                at = part * half
                if cut:
                    at = pl.multiple_of(order_ref[1] * share + at, half)
                yield pltpu.make_async_copy(
                    source.at[pl.ds(at, half), :],
                    target.at[pl.ds(part * half, half), :],
                    sems.at[part, i],
                )

        for part in range(halves):

            @pl.when(pl.program_id(0) == part)
            def _(part=part):
                if part == 0:
                    for each in range(halves):
                        for copy in copies(each):
                            copy.start()
                for copy in copies(part):
                    copy.wait()

        outs = rest[len(whole) : len(whole) + len(out_kinds)]
        totals, sums_held = rest[len(whole) + len(out_kinds) :][:sums], rest[len(rest) - sums :]
        tile = 32
        lines = prepare(*[ref[...] for ref in rest[: len(whole)]])
        for ref in sums_held:
            ref[...] = jnp.zeros_like(ref)

        def some(i, carry):
            inside = pl.ds(pl.multiple_of(i * tile, tile), tile)
            at = pl.ds(pl.multiple_of(pl.program_id(0) * half + i * tile, tile), tile)
            values = kernel([ref[at, :].astype(F32) for ref in held], *lines)
            for ref, value in zip(outs, values):
                ref[inside, :] = value.astype(ref.dtype)
            for ref, value in zip(sums_held, values[len(outs) :]):
                ref[...] += jnp.sum(value.reshape(tile // 8, 8, width), axis=0)
            return carry

        lax.fori_loop(0, half // tile, some, 0, unroll=2)
        for ref, held_ref in zip(totals, sums_held):
            add_column(ref, held_ref[...])

    line = pl.BlockSpec((1, width), lambda i, o: (0, 0))
    return call(
        name,
        run,
        (*[v for v, _ in given], *whole),
        (halves,),
        [pl.BlockSpec(memory_space=pl.ANY) for _ in given] + [line for _ in whole],
        [pl.BlockSpec((half, width), lambda i, o: (i, 0)) for _ in out_kinds]
        + [line for _ in range(sums)],
        [shape((share, width), kind) for kind in out_kinds]
        + [shape((1, width), F32) for _ in range(sums)],
        scratch=[pltpu.VMEM((8, width), F32) for _ in range(sums)]
        + [pltpu.VMEM((share, width), v.dtype) for v, _ in given]
        + [pltpu.SemaphoreType.DMA((halves, count))],
        prefetch=(order,),
        flops=20 * share * width,
    )


def sum_of(values):
    total = values[0]
    for value in values[1:]:
        total = total + value
    return total


def add_column(ref, values):
    part = jnp.sum(values, axis=0, keepdims=True)

    @pl.when(pl.program_id(0) == 0)
    def _():
        ref[...] = part

    @pl.when(pl.program_id(0) > 0)
    def _():
        ref[...] += part


def scale_first(squares, magnitude, *rest):
    norm = jnp.sqrt(squares)
    return (magnitude / norm, norm / magnitude, *rest)


def hidden_kernel(given, scale, inverse, gain):
    hidden = given[0] + sum_of(given[1:]) * scale
    return hidden, hidden * rms_rows(hidden) * gain


def mixed_kernel(given, scale, inverse):
    return (given[0] + sum_of(given[1:]) * scale,)


def norm_back(grad_normed, values, gain):
    factor = rms_rows(values)
    scaled = grad_normed * gain
    inner = jnp.mean(scaled * values, axis=1, keepdims=True)
    back = factor * scaled - values * (factor * factor * factor * inner)
    return back, grad_normed * values * factor


def hidden_back_kernel(given, scale, inverse, gain):
    cot, token, hidden = given[:3]
    back, gain_terms = norm_back(sum_of(given[3:]), hidden, gain)
    grad = cot + back
    return grad, grad * scale, grad * ((hidden - token) * inverse), gain_terms


def shrink_back_kernel(places, order_ref, *refs):
    cots, (low_ref, squares_ref, magnitude_ref, product_ref, grad_ref, rows_all) = refs[:places], refs[places:]
    scale = magnitude_ref[0] / jnp.sqrt(squares_ref[0])
    share = cots[0].shape[0]
    for place, cot_ref in enumerate(cots):
        grad = (cot_ref[...].astype(F32) * scale).astype(LOW)
        grad_ref[place] = grad
        rows_all[place * share : (place + 1) * share, :] = grad
    result = dot(rows_all[...], low_ref[0], NT).astype(LOW)
    for place in range(places):
        product_ref[place] = result[place * share : (place + 1) * share]


def shrink_back(order, cotangent, low, squares, magnitude, groups):
    rows, width = cotangent.shape
    share, inner = rows // groups, low.shape[1]
    places = CORES
    line = pl.BlockSpec((1, 1, width), lambda j, o: (0, 0, 0))
    cot = lambda place: pl.BlockSpec((share, width), lambda j, o: (o[places * j + place], 0))
    return call(
        "shrink_back",
        functools.partial(shrink_back_kernel, places),
        (*[cotangent] * places, low, squares, magnitude),
        (groups // places,),
        [cot(place) for place in range(places)]
        + [pl.BlockSpec((1, inner, width), lambda j, o: (0, 0, 0)), line, line],
        [
            pl.BlockSpec((places, share, inner), lambda j, o: (j, 0, 0)),
            pl.BlockSpec((places, share, width), lambda j, o: (j, 0, 0)),
        ],
        [shape((groups, share, inner), LOW), shape((groups, share, width), LOW)],
        scratch=[pltpu.VMEM((places * share, width), LOW)],
        prefetch=(order,),
        flops=2 * rows * width * inner,
    )


def expand_kernel(step, first, last, n_totals, *refs):
    mine_ref, low_ref, grad_ref, squares_ref, magnitude_ref = refs[:5]
    refs = list(refs[5:])
    left_ref = refs.pop(0) if first else None
    right_ref = refs.pop(0) if last else None
    before = [refs.pop(0) for _ in range(n_totals)]
    product_ref, back_ref, rows_ref, total_ref, joined_ref = refs[:5]
    refs = refs[5:]
    across_ref = refs.pop(0) if first else None
    extra_ref = refs.pop(0) if last else None
    rows_all, low_all, grad_all, product_all, back_all, sent, got, in_sems, out_sems, send_sems, recv_sems = refs
    share, depth = mine_ref.shape
    sibling = sibling_id()
    greet([sibling])
    both = CORES * share
    width, ff = low_ref.shape[2], magnitude_ref.shape[1]
    tile = 256
    cuts = [slice(at, at + tile) for at in range(0, width, tile)]

    mine_copy = pltpu.make_async_copy(mine_ref, rows_all.at[pl.ds(share, share), :], in_sems.at[0])
    other_copy = remote(
        mine_ref,
        rows_all.at[pl.ds(0, share), :],
        send_sems.at[sent.shape[0]],
        recv_sems.at[sent.shape[0]],
        sibling,
    )
    tile_copies = []
    for n, cut in enumerate(cuts):
        lanes = pl.ds(cut.start, tile)
        tile_copies.append(
            [
                pltpu.make_async_copy(
                    low_ref.at[:, :, lanes], low_all.at[:, :, lanes], in_sems.at[2 + 2 * n]
                ),
                pltpu.make_async_copy(
                    grad_ref.at[pl.ds(CORES * step, CORES), :, lanes],
                    grad_all.at[:, :, lanes],
                    in_sems.at[3 + 2 * n],
                ),
            ]
        )
    mine_copy.start()
    for copy in tile_copies[0]:
        copy.start()
    greeted(1)
    other_copy.start()
    for copies in tile_copies[1:]:
        for copy in copies:
            copy.start()
    if first:
        rank = across_ref.shape[1]
        for m in range(2):
            rows_all[both + m * rank : both + (m + 1) * rank, :] = left_ref[m].astype(LOW)
    mine_copy.wait()
    other_copy.wait_recv()
    out_copies = [
        pltpu.make_async_copy(rows_all.at[pl.ds(0, both), :], rows_ref, out_sems.at[2 * len(cuts)])
    ]
    out_copies[0].start()
    lane = lax.broadcasted_iota(jnp.int32, (1, tile), 1)
    for n, cut in enumerate(cuts):
        for copy in tile_copies[n]:
            copy.wait()
        size = min(tile, ff - cut.start)
        pre = [dot(rows_all[...], low_all[m, :, cut]) for m in range(2)]
        if first:
            for m in range(2):
                rows = slice(both + m * rank, both + (m + 1) * rank)
                across_ref[m, :, cut.start : cut.start + size] = pre[m][rows, :size]
        magnitude, squares, scale = [], [], []
        for m in range(2):
            given = magnitude_ref[m : m + 1, cut.start : cut.start + size]
            if size < tile:
                given = jnp.concatenate([given, jnp.zeros((1, tile - size), F32)], axis=1)
            magnitude.append(given)
            squares.append(squares_ref[m, :, cut])
            scale.append(given / jnp.sqrt(squares[m]))
        sums = [jnp.zeros((1, tile), F32) for _ in range(2)]
        at = [slice(m * width + cut.start, m * width + cut.stop) for m in range(2)]
        for place in range(CORES):
            rows = slice(place * share, (place + 1) * share)
            gate_pre, up_pre = pre[0][rows], pre[1][rows]
            gate, up = gate_pre * scale[0], up_pre * scale[1]
            sigmoid = 0.5 + 0.5 * jnp.tanh(0.5 * gate)
            active = gate * sigmoid
            product_all[rows, cut] = (active * up).astype(LOW)
            upper = grad_all[place, :, cut].astype(F32)
            grad_up = upper * active
            grad_gate = upper * up * sigmoid * (1.0 + gate * (1.0 - sigmoid))
            sums[0] += jnp.sum(grad_gate * gate_pre, axis=0, keepdims=True)
            sums[1] += jnp.sum(grad_up * up_pre, axis=0, keepdims=True)
            back_all[rows, at[0]] = (grad_gate * scale[0]).astype(LOW)
            back_all[rows, at[1]] = (grad_up * scale[1]).astype(LOW)
        for m in range(2):
            total_ref[m, :, cut] = sums[m]
        if last:
            rank = extra_ref.shape[1]
            for m in range(2):
                total = sums[m]
                for ref in before:
                    total = total + ref[m, :, cut]
                right = right_ref[m, :, cut.start : cut.start + size]
                if size < tile:
                    spare = jnp.zeros((rank, tile - size), F32)
                    right = jnp.concatenate([right, spare], axis=1)
                weighted = right * norm_weight(total, squares[m], magnitude[m])
                rows = slice(both + m * rank, both + (m + 1) * rank)
                back_all[rows, at[m]] = weighted.astype(LOW)
                back_all[rows, at[1 - m]] = jnp.zeros((rank, tile), LOW)
    for m in range(2):
        lanes = pl.ds(m * width, width)
        copy = pltpu.make_async_copy(
            back_all.at[pl.ds(0, both), lanes], back_ref.at[m], out_sems.at[m]
        )
        copy.start()
        out_copies.append(copy)
    copy = pltpu.make_async_copy(product_all, product_ref, out_sems.at[2])
    copy.start()
    out_copies.append(copy)
    chunk = sent.shape[2]
    copies = [
        remote(sent.at[n], got.at[n], send_sems.at[n], recv_sems.at[n], sibling)
        for n in range(depth // chunk)
    ]

    def add(n):
        columns = slice(n * chunk, (n + 1) * chunk)
        copies[n].wait_recv()
        total = joined_ref[:, columns].astype(F32) + got[n].astype(F32)
        joined_ref[:, columns] = total.astype(LOW)

    for n in range(depth // chunk):
        columns = slice(n * chunk, (n + 1) * chunk)
        result = dot(back_all[:, :width], low_all[0, columns, :], NT)
        result = result + dot(back_all[:, width:], low_all[1, columns, :], NT)
        sent[n] = result[:share].astype(LOW)
        joined_ref[:, columns] = result[share:both].astype(LOW)
        copies[n].start()
        if n > 0:
            add(n - 1)
        if last:
            for m in range(2):
                extra_ref[m, :, columns] = result[both + m * rank : both + (m + 1) * rank]
    add(len(copies) - 1)
    for copy in out_copies:
        copy.wait()
    for copy in [other_copy, *copies]:
        copy.wait_send()


def expand(identity, mine, low, squares, magnitude, grad_product, step, left=None, right=None, before=()):
    share, depth = mine.shape
    width = low.shape[2]
    first, last = left is not None, right is not None
    rows = CORES * share
    hbm = pl.BlockSpec(memory_space=pl.ANY)
    fixed = lambda dims: pl.BlockSpec(tuple(dims), lambda i: (0,) * len(dims))
    operands = [mine, low, grad_product, squares, magnitude]
    in_specs = [hbm, hbm, hbm, fixed(squares.shape), fixed(magnitude.shape)]
    out_shape = [
        shape((rows, width), LOW),
        shape((2, rows, width), LOW),
        shape((rows, depth), LOW),
        shape((2, 1, width), F32),
        shape((share, depth), LOW),
    ]
    out_specs = [hbm, hbm, hbm] + [fixed(v.shape) for v in out_shape[3:]]
    extra_in = extra_out = 0
    if first:
        rank = left.shape[1]
        extra_in = 2 * rank
        operands.append(left)
        in_specs.append(fixed(left.shape))
        out_shape.append(shape((2, rank, magnitude.shape[1]), F32))
        out_specs.append(fixed(out_shape[-1].shape))
    if last:
        rank = right.shape[1]
        extra_out = 2 * rank
        operands += [right, *before]
        in_specs += [fixed(v.shape) for v in (right, *before)]
        out_shape.append(shape((2, rank, depth), F32))
        out_specs.append(fixed(out_shape[-1].shape))
    tiles, chunk = width // 256, tile_of(depth, 512)
    return call(
        "expand",
        functools.partial(expand_kernel, step, first, last, len(before)),
        tuple(operands),
        (1,),
        in_specs,
        out_specs,
        out_shape,
        scratch=[
            pltpu.VMEM((rows + extra_in, depth), LOW),
            pltpu.VMEM(low.shape, LOW),
            pltpu.VMEM((CORES, share, width), LOW),
            pltpu.VMEM((rows, width), LOW),
            pltpu.VMEM((rows + extra_out, 2 * width), LOW),
            pltpu.VMEM((depth // chunk, share, chunk), LOW),
            pltpu.VMEM((depth // chunk, share, chunk), LOW),
            pltpu.SemaphoreType.DMA((2 + 2 * tiles,)),
            pltpu.SemaphoreType.DMA((2 * tiles + 1,)),
            pltpu.SemaphoreType.DMA((depth // chunk + 1,)),
            pltpu.SemaphoreType.DMA((depth // chunk + 1,)),
        ],
        flops=8 * rows * depth * width,
        identity=identity,
    )


def adapter_kernel(plan, n_inputs, n_grads, corrections, n_before, order_ref, *refs):
    for _ in adapter_steps(plan, n_inputs, n_grads, corrections, n_before, order_ref, *refs):
        pass


def adapter_steps(plan, n_inputs, n_grads, corrections, n_before, order_ref, *refs):
    count = n_inputs + n_grads
    sources, held, sems = refs[:count], refs[-count - 1 : -1], refs[-1]
    left_ref, right_ref = refs[count : count + 2]
    *corrected, left_out, right_out = refs[count + 2 : -count - 1]
    members, rank, width = right_ref.shape
    chunks = list(plan(order_ref, held[:n_inputs], held[n_inputs:]))
    copies, used = [], 0
    for parts, _, _ in chunks:
        copies.append([])
        for which, index in parts:
            copy = pltpu.make_async_copy(
                sources[which].at[index], held[which].at[index], sems.at[used]
            )
            copy.start()
            copies[-1].append(copy)
            used += 1
    yield
    left_rows = jnp.concatenate([split_rows(left_ref[m]) for m in range(members)], axis=0)
    right_rows = [split_rows(right_ref[m]) for m in range(members)]
    before, corrected = corrected[:n_before], corrected[n_before:]
    for out, ref in zip((left_out, right_out), before or (None, None)):
        out[...] = jnp.zeros_like(out) if ref is None else ref[...]
    for waits, (_, taken_of, grads_of) in zip(copies, chunks):
        for copy in waits:
            copy.wait()
        taken = taken_of()
        across = dot(left_rows, taken, NT)
        downs = []
        for m in range(members):
            grad = grads_of(m)
            mine = split_rows(fold(across[2 * rank * m : 2 * rank * (m + 1)]))
            right_out[m] += fold(dot(mine, grad))
            downs.append(split_rows(fold(dot(right_rows[m], grad, NT))))
        left = dot(jnp.concatenate(downs, axis=0), taken)
        for m in range(members):
            left_out[m] += fold(left[2 * rank * m : 2 * rank * (m + 1)])
        yield
    if corrections:
        correct(corrections, right_ref, left_out, right_out, left_out, right_out, *corrected)


def correct(n_totals, right_ref, left_in, right_in, left_out, right_out, *refs):
    back_ref, across_ref, squares_ref, magnitude_ref = refs[:4]
    totals, magnitude_out = refs[4 : 4 + n_totals], refs[4 + n_totals]
    members, rank, width = right_ref.shape
    total = sum_refs(totals)[:, :, :width]
    squares = squares_ref[:, :, :width]
    magnitude_out[...] = total / jnp.sqrt(squares)
    for m in range(members):
        weight = norm_weight(total[m], squares[m], magnitude_ref[m : m + 1])
        if back_ref.dtype == LOW:
            low = back_ref[m, : left_in.shape[2], :]
            back = fold(dot(split_rows(right_ref[m] * weight), low, NT))
        else:
            back = back_ref[m]
        left_out[m] = ADAPT_SCALE * (left_in[m] - back)
        right_out[m] = ADAPT_SCALE * (right_in[m] - across_ref[m][:, :width] * weight)


def adapter_parts(inputs, grads, left, right, correction, before):
    members, rank, width = right.shape
    moved, fixed, n_totals = [*inputs, *grads], [left, right, *before], 0
    outs = [(members, rank, left.shape[2]), (members, rank, width)]
    if correction is not None:
        *given, totals = correction
        n_totals = len(totals)
        fixed += [*given, *totals]
        outs = [(members, 1, width)] + outs
    scratch = [pltpu.VMEM(v.shape, v.dtype) for v in moved] + [pltpu.SemaphoreType.DMA((32,))]
    return moved, fixed, outs, scratch, (len(inputs), len(grads), n_totals, len(before))


def adapter(name, order, plan, inputs, grads, left, right, correction=None, before=(), other=None):
    moved, fixed, outs, scratch, counts = adapter_parts(inputs, grads, left, right, correction, before)
    kernel = functools.partial(adapter_kernel, plan, *counts)
    full = lambda dims: pl.BlockSpec(tuple(dims), lambda i, o: (0,) * len(dims))
    n_moved, n_fixed, n_outs = len(moved), len(fixed), len(outs)
    if other is not None:
        sums, other_right, (low, across, squares, magnitude, totals) = other
        moved = moved + [low]
        fixed = fixed + [other_right, *sums, across, squares, magnitude, *totals]
        outs = outs + [(1, 1, other_right.shape[2]), sums[0].shape, sums[1].shape]
        scratch = scratch + [pltpu.VMEM(low.shape, LOW), pltpu.SemaphoreType.DMA(())]

    def run(order_ref, *refs):
        if other is None:
            kernel(order_ref, *refs)
            return
        refs = list(refs)
        low_held, low_sem = refs[-2:]
        low_copy = pltpu.make_async_copy(refs[n_moved], low_held, low_sem)
        ends = [n_moved + 1, n_moved + 1 + len(fixed), n_moved + 1 + len(fixed) + len(outs)]
        fixed_refs, out_refs = refs[ends[0] : ends[1]], refs[ends[1] : ends[2]]
        steps = adapter_steps(
            plan,
            *counts,
            order_ref,
            *refs[:n_moved],
            *fixed_refs[:n_fixed],
            *out_refs[:n_outs],
            *refs[ends[2] : -2],
        )
        next(steps)
        low_copy.start()
        for _ in steps:
            pass
        low_copy.wait()
        right_ref, left_in, right_in, across_ref, squares_ref, magnitude_ref, *totals_refs = (
            fixed_refs[n_fixed:]
        )
        magnitude_out, left_out, right_out = out_refs[n_outs:]
        correct(
            len(totals_refs),
            right_ref,
            left_in,
            right_in,
            left_out,
            right_out,
            low_held,
            across_ref,
            squares_ref,
            magnitude_ref,
            *totals_refs,
            magnitude_out,
        )

    return call(
        name,
        run,
        (*moved, *fixed),
        (1,),
        [pl.BlockSpec(memory_space=pl.ANY) for _ in moved] + [full(v.shape) for v in fixed],
        [full(dims) for dims in outs],
        [shape(dims, F32) for dims in outs],
        scratch=scratch,
        prefetch=(order,),
        flops=sum(v.size for v in moved) * 64,
    )


def copy_kernel(count, *refs):
    for source, target in zip(refs[:count], refs[count:]):
        target[...] = source[...]


def copy_out(arrays):
    full = lambda v: pl.BlockSpec(v.shape, lambda i: (0,) * v.ndim)
    return call(
        "copy_out",
        functools.partial(copy_kernel, len(arrays)),
        tuple(arrays),
        (1,),
        [full(v) for v in arrays],
        [full(v) for v in arrays],
        [shape(v.shape, F32) for v in arrays],
    )


GRAIN = 16


def pieces_of(width):
    return [(at, min(128, width - at)) for at in range(0, width, 128)]


def cells_of(blocks, lines, parts):
    cells, rows = [], []
    for n, block in enumerate(blocks):
        for m in range(block.shape[0]):
            for at, size in pieces_of(block.shape[2] // parts):
                cells.append((n, m, at, size))
    for n, line in enumerate(lines):
        for m in range(line.shape[0]):
            for at, size in pieces_of(line.shape[2] // parts):
                rows.append((n, m, at, size))
    return cells, rows


def pack(blocks, lines, wide_ref, part, parts, cells, rows):
    for i, (n, m, at, size) in enumerate(cells):
        start = part * (blocks[n].shape[2] // parts) + at
        wide_ref[part, i, :, :size] = blocks[n][m, :, start : start + size]
    for i, (n, m, at, size) in enumerate(rows):
        start = part * (lines[n].shape[2] // parts) + at
        cell, row = len(cells) + i // GRAIN, i % GRAIN
        wide_ref[part, cell, row : row + 1, :size] = lines[n][m, :, start : start + size]


def unpack(full_ref, blocks, lines, part, parts, cells, rows):
    for i, (n, m, at, size) in enumerate(cells):
        start = part * (blocks[n].shape[2] // parts) + at
        blocks[n][m, :, start : start + size] = full_ref[part, i].astype(F32)[:, :size]
    for i, (n, m, at, size) in enumerate(rows):
        start = part * (lines[n].shape[2] // parts) + at
        cell, row = len(cells) + i // GRAIN, i % GRAIN
        values = full_ref[part, cell].astype(F32)
        lines[n][m, :, start : start + size] = values[row : row + 1, :size]


def reduce_steps(groups, lines, counts, *refs):
    n_all, n_all_lines, n_dp, n_dp_lines = counts
    count = sum(counts)
    taken, given, scratch = refs[:count], refs[count : 2 * count], refs[2 * count :]
    ends = [n_all, n_all + n_all_lines, n_all + n_all_lines + n_dp]
    parted = lambda v: (v[: ends[0]], v[ends[0] : ends[1]], v[ends[1] : ends[2]], v[ends[2] :])
    all_out, all_lines_out, dp_out, dp_lines_out = parted(given)
    (
        all_ref,
        line_ref,
        all_low,
        line_low,
        all_got,
        part,
        part_low,
        part_got,
        line_got,
        all_full,
        line_full,
        *sems,
    ) = scratch
    held, in_sems, sems = sems[:count], sems[count], sems[count + 1 :]
    loads = [
        pltpu.make_async_copy(source, target, in_sems.at[i])
        for i, (source, target) in enumerate(zip(taken, held))
    ]
    for load in loads:
        load.start()
    me, row = lax.axis_index("mp"), lax.axis_index("dp")
    piece, line_piece = part.shape[0] // lines, line_ref.shape[1] // lines
    mp_peer = [lax.rem(me + k, groups) for k in range(groups)]
    dp_peer = [lax.rem(row + k, lines) for k in range(lines)]
    barrier = pltpu.get_barrier_semaphore()
    for k in range(1, groups):
        pl.semaphore_signal(barrier, 1, device_id={"mp": mp_peer[k]}, device_id_type=MESH_IDS)
    for k in range(1, lines):
        pl.semaphore_signal(barrier, 1, device_id={"dp": dp_peer[k]}, device_id_type=MESH_IDS)
    all_in, all_lines_in, dp_in, dp_lines_in = parted(held)
    all_cells = cells_of(all_in, all_lines_in, groups)
    dp_cells = cells_of(dp_in, dp_lines_in, 1)
    all_ref[...] = jnp.zeros_like(all_ref)
    line_ref[...] = jnp.zeros_like(line_ref)
    for load in loads:
        load.wait()
    for q in range(groups):
        pack(all_in, all_lines_in, all_ref, q, groups, *all_cells)
    pack(dp_in, dp_lines_in, line_ref, 0, 1, *dp_cells)
    all_low[...] = all_ref[...].astype(LOW)
    line_low[...] = line_ref[...].astype(LOW)
    pl.semaphore_wait(barrier, groups + lines - 2)

    def send(source, target, stage, k, axis, peer):
        copy = pltpu.make_async_remote_copy(
            src_ref=source,
            dst_ref=target,
            send_sem=sems[2 * stage].at[k],
            recv_sem=sems[2 * stage + 1].at[k],
            device_id={axis: peer},
            device_id_type=MESH_IDS,
        )
        copy.start()
        return copy

    over_mp = [
        send(all_low.at[mp_peer[k]], all_got.at[k], 0, k, "mp", mp_peer[k])
        for k in range(1, groups)
    ]
    over_dp = [
        send(
            line_low.at[0, pl.ds(dp_peer[k] * line_piece, line_piece)],
            line_got.at[k],
            1,
            k,
            "dp",
            dp_peer[k],
        )
        for k in range(1, lines)
    ]
    yield
    total = all_ref[me]
    for k, copy in enumerate(over_mp, 1):
        copy.wait_recv()
        total = total + all_got[k].astype(F32)
    part[...] = total
    part_low[...] = total.astype(LOW)
    part_dp = [
        send(part_low.at[pl.ds(dp_peer[k] * piece, piece)], part_got.at[k], 2, k, "dp", dp_peer[k])
        for k in range(1, lines)
    ]
    yield
    held = pl.ds(row * piece, piece)
    total = part[held]
    for k, copy in enumerate(part_dp, 1):
        copy.wait_recv()
        total = total + part_got[k].astype(F32)
    all_full[me, held] = total.astype(LOW)
    part_back = [
        send(all_full.at[me, held], all_full.at[me, held], 4, k, "dp", dp_peer[k])
        for k in range(1, lines)
    ]
    mine = pl.ds(row * line_piece, line_piece)
    total = line_ref[0, mine]
    for k, copy in enumerate(over_dp, 1):
        copy.wait_recv()
        total = total + line_got[k].astype(F32)
    line_full[0, mine] = total.astype(LOW)
    line_back = [
        send(line_full.at[0, mine], line_full.at[0, mine], 3, k, "dp", dp_peer[k])
        for k in range(1, lines)
    ]
    yield
    for copy in part_back:
        copy.wait_recv()
    all_back = [
        send(all_full.at[me], all_full.at[me], 5, k, "mp", mp_peer[k]) for k in range(1, groups)
    ]
    yield
    for copy in line_back:
        copy.wait_recv()
    unpack(line_full, dp_out, dp_lines_out, 0, 1, *dp_cells)
    for copy in all_back:
        copy.wait_recv()
    for q in range(groups):
        unpack(all_full, all_out, all_lines_out, q, groups, *all_cells)
    for copy in over_mp + over_dp + part_dp + line_back + part_back + all_back:
        copy.wait_send()


def reduce_devices(name, identity, over_all, over_all_lines, over_dp, over_dp_lines, job):
    groups, lines = lax.axis_size("mp"), lax.axis_size("dp")

    def size_of(blocks, rows, parts):
        cells, lines_in = cells_of(blocks, rows, parts)
        size = len(cells) + -(-len(lines_in) // GRAIN)
        return -(-size // lines) * lines

    count, line_count = size_of(over_all, over_all_lines, groups), size_of(over_dp, over_dp_lines, 1)
    operands = [*over_all, *over_all_lines, *over_dp, *over_dp_lines]
    counts = (len(over_all), len(over_all_lines), len(over_dp), len(over_dp_lines))
    tail = (GRAIN, 128)
    sizes = (groups, lines, lines, lines, lines, groups)
    every, line = (groups, count) + tail, (1, line_count) + tail
    scratch = (
        [
            pltpu.VMEM(every, F32),
            pltpu.VMEM(line, F32),
            pltpu.VMEM(every, LOW),
            pltpu.VMEM(line, LOW),
            pltpu.VMEM(every, LOW),
            pltpu.VMEM((count,) + tail, F32),
            pltpu.VMEM((count,) + tail, LOW),
            pltpu.VMEM((lines, count // lines) + tail, LOW),
            pltpu.VMEM((lines, line_count // lines) + tail, LOW),
            pltpu.VMEM(every, LOW),
            pltpu.VMEM(line, LOW),
        ]
        + [pltpu.VMEM(v.shape, F32) for v in operands]
        + [pltpu.SemaphoreType.DMA((len(operands),))]
        + [pltpu.SemaphoreType.DMA((n,)) for n in sizes for _ in range(2)]
    )
    job_steps, moved, whole_rows, job_shape, job_scratch = job
    n_operands, n_scratch = len(operands), len(scratch)
    out_shape = [shape(v.shape, F32) for v in operands] + [job_shape]
    anywhere = pl.BlockSpec(memory_space=pl.ANY)
    full = lambda v: pl.BlockSpec(v.shape, lambda i: (0,) * v.ndim)
    operands = operands + [*moved, *whole_rows]

    def run(*refs):
        given, refs = refs[: len(operands)], refs[len(operands) :]
        results, held = refs[: len(out_shape)], refs[len(out_shape) :]
        steps = reduce_steps(
            groups, lines, counts, *given[:n_operands], *results[:n_operands], *held[:n_scratch]
        )
        work = job_steps(*given[n_operands:], results[n_operands], *held[n_scratch:])
        next(work)
        for _ in steps:
            next(work, None)
        for _ in work:
            pass

    return call(
        name,
        run,
        tuple(operands),
        (1,),
        [anywhere] * (n_operands + len(moved)) + [full(v) for v in whole_rows],
        [full(v) for v in out_shape[:-1]] + [anywhere],
        out_shape,
        scratch=scratch + job_scratch,
        flops=1000,
        identity=identity,
    )


def token_job(tokens, grad_hidden, parts, gain):
    share, width = grad_hidden.shape
    moved = [tokens, grad_hidden, *parts]

    def steps(*refs):
        sources, gain_ref, out_ref = refs[: len(moved)], refs[len(moved)], refs[len(moved) + 1]
        *held, result, sems = refs[len(moved) + 2 :]
        row = pl.multiple_of(lax.axis_index("mp") * share, share)
        copies = []
        for n, (source, target) in enumerate(zip(sources, held)):
            source = source.at[pl.ds(row, share), :] if n == 0 else source
            copies.append(pltpu.make_async_copy(source, target, sems.at[n]))
            copies[-1].start()
        yield
        for copy in copies:
            copy.wait()
        tile = 32
        gain = gain_ref[...]

        def some(i, carry):
            at = pl.ds(pl.multiple_of(i * tile, tile), tile)
            token, grad, *rest = [ref[at, :].astype(F32) for ref in held]
            result[at, :] = grad + norm_back(sum_of(rest), token, gain)[0]
            return carry

        lax.fori_loop(0, share // tile, some, 0, unroll=2)
        copy = pltpu.make_async_copy(result, out_ref, sems.at[len(moved)])
        copy.start()
        yield
        yield
        copy.wait()

    scratch = [pltpu.VMEM((share, width), v.dtype) for v in moved]
    scratch += [pltpu.VMEM((share, width), F32), pltpu.SemaphoreType.DMA((len(moved) + 1,))]
    return steps, moved, [gain], shape((share, width), F32), scratch


def body(
    tokens,
    cotangent,
    segment_ids,
    attend_gain,
    expand_gain,
    heads_base,
    heads_left,
    heads_right,
    heads_magnitude,
    output_base,
    output_left,
    output_right,
    output_magnitude,
    expand_base,
    expand_left,
    expand_right,
    expand_magnitude,
    shrink_base,
    shrink_left,
    shrink_right,
    shrink_magnitude,
):
    groups = lax.axis_size("mp")
    chips = groups // CORES
    index = lax.axis_index("mp")
    chip, core = index // CORES, index % CORES
    rows, width = tokens.shape
    share = rows // groups
    local_heads, ff = heads_base.shape[2], expand_base.shape[2]
    ff_wide = padded(ff)
    device = jnp.arange(groups, dtype=jnp.int32)
    order = jnp.concatenate(
        [
            (chip + device // CORES) % chips * CORES + (core + 1 + device) % CORES,
            (device // CORES + chips - chip) % chips * CORES + (device + CORES - core + 1) % CORES,
        ]
    ).astype(jnp.int32)

    def tie(*values):
        return lax.optimization_barrier(values)

    def sibling(values):
        return lax.ppermute(
            values, "mp", [(i, i // CORES * CORES + (i + 1) % CORES) for i in range(groups)]
        )

    def to_chip(values, step):
        return lax.ppermute(
            values,
            "mp",
            [((i, ((i // CORES + step) % chips) * CORES + i % CORES)) for i in range(groups)],
        )

    def join(pair):
        return (pair[1].astype(F32) + sibling(pair[0]).astype(F32)).astype(LOW)

    def chip_pairs(places):
        return [places[CORES * step : CORES * (step + 1)] for step in range(chips)]

    def arrive(own):
        return [to_chip(own, chips - step) for step in range(1, chips)]

    def pairs_of(own, near_sibling, arrived):
        return [(near_sibling, own)] + [(sibling(piece), piece) for piece in arrived]

    def in_pairs(order_ref, inputs, grads):
        for step, (taken, grad) in enumerate(zip(inputs, grads)):
            yield (
                [(step, ...), (chips + step, ...)],
                lambda taken=taken: taken[...],
                lambda m, grad=grad: grad[m, :, :ff],
            )

    def in_shrink(order_ref, inputs, grads):
        for step, taken in enumerate(inputs):
            at = slice(CORES * step, CORES * (step + 1))
            yield (
                [(step, ...), (chips, pl.ds(CORES * step, CORES))],
                lambda taken=taken: taken[:, :ff],
                lambda m, at=at: grads[0][at].reshape(-1, grads[0].shape[-1]),
            )

    def in_output(start):
        def plan(order_ref, inputs, grads):
            for n, grad in enumerate(grads):
                yield (
                    [(0, (0, start + n)), (1 + n, ...)],
                    lambda place=start + n: inputs[0][0, place],
                    lambda m, grad=grad: grad[...],
                )

        return plan

    def in_heads(order_ref, inputs, grads):
        for place in range(groups):
            step, side = place // CORES, place % CORES
            me = lax.axis_index("mp")
            group = lax.rem(me // CORES + step, chips) * CORES + lax.rem(me + 1 + side, CORES)
            at = pl.multiple_of(group * share, share)
            rows = pl.ds(place * share, share)
            yield (
                [(0, pl.ds(at, share)), (1, (slice(None), rows))],
                lambda at=at: inputs[0][pl.ds(at, share), :],
                lambda m, rows=rows: grads[0][m, rows, :],
            )

    heads_rows, output_rows = turned(heads_left), turned(output_left[None])
    expand_rows, shrink_rows = turned(expand_left), turned(shrink_left[None])
    heads_mag, output_mag = heads_magnitude, output_magnitude[None]
    expand_mag, shrink_mag = expand_magnitude, shrink_magnitude[None]
    attend_line, expand_line = attend_gain[None], expand_gain[None]

    output_low, shrink_low, squares_part = merge_pair(
        [(output_base, output_rows[0], output_right), (shrink_base, shrink_rows[0], shrink_right)]
    )
    output_low, shrink_low = output_low[None], shrink_low[None]
    (
        normed,
        heads_low,
        post,
        heads_sq,
        heads_across,
        cos_table,
        sine_table,
        squares,
        first,
    ) = project_heads(
        tokens,
        attend_line,
        heads_base,
        heads_rows,
        heads_right,
        heads_mag,
        segment_ids,
        squares_part,
        groups,
    )
    heads_out = attend(order, groups, post, first)
    output_sq, shrink_sq = squares[None, :1], squares[None, 1:]
    heads_parts = heads_out.reshape(1, groups, share, local_heads)
    joined, output_across = product(
        "output_product", 3, heads_parts, output_low, NN, left=output_rows
    )
    joined, expand_right_tied = tie(joined, expand_right)
    output_parts = [joined[0]] + [to_chip(joined[step], step) for step in range(1, chips)]
    expand_low, expand_sq = merge(
        expand_base, expand_rows, expand_right_tied, 1024, expand_base.shape[2]
    )
    grad_product, shrink_grad = shrink_back(
        order, cotangent, shrink_low, shrink_sq, shrink_mag[None], groups
    )
    output_parts, expand_low, grad_product = tie(output_parts, expand_low, grad_product)
    hidden, normed_own = row_call(
        "hidden",
        hidden_kernel,
        order,
        [(tokens, True)] + [(part, False) for part in output_parts],
        (output_sq[0], output_mag, expand_line),
        (F32, LOW),
        0,
        scale_first,
    )

    def feed(mine, step, **extra):
        return expand(
            4 + step, mine, expand_low, expand_sq, expand_mag, grad_product, step, **extra
        )

    arrived = arrive(normed_own)
    fed = [feed(normed_own, 0, left=expand_rows)]
    arrived, fed = tie(arrived, fed)
    fed = list(fed)
    for step in range(1, chips):
        extra = {}
        if step == chips - 1:
            extra = {"right": expand_right, "before": [f[3] for f in fed]}
        fed.append(feed(arrived[step - 1], step, **extra))
    expand_totals = [f[3] for f in fed]
    joined, shrink_rows_tied = tie([f[4] for f in fed], shrink_rows)
    mid_parts = [joined[0]] + [to_chip(joined[step], step) for step in range(1, chips)]
    shrink_places, shrink_total, shrink_across = shrink_product(
        order, [f[0] for f in fed], shrink_low, shrink_rows_tied, cotangent
    )
    shrink_pairs = chip_pairs(shrink_places)
    expand_adapter = adapter(
        "expand_adapter",
        order,
        in_pairs,
        [f[2] for f in fed],
        [f[1] for f in fed],
        expand_rows,
        expand_right,
        (fed[-1][5], fed[0][5], expand_sq, expand_mag, expand_totals),
    )
    mid_parts, shrink_pairs, expand_adapter = tie(mid_parts, shrink_pairs, expand_adapter)
    grad_hidden, output_grad_own, output_total, expand_gain_part = row_call(
        "hidden_back",
        hidden_back_kernel,
        order,
        [(cotangent, True), (tokens, True), (hidden, False)]
        + [(part, False) for part in mid_parts],
        (output_sq[0], output_mag, expand_line),
        (F32, LOW),
        2,
        scale_first,
    )
    arrived, near_sibling = arrive(output_grad_own), sibling(output_grad_own)
    shrink_joined = [join(pair) for pair in shrink_pairs[1:]]
    shrink_joined, shrink_rows_tied = tie(shrink_joined, shrink_rows)
    shrink_sums = adapter(
        "shrink_adapter",
        order,
        in_shrink,
        [f[0] for f in fed],
        [shrink_grad],
        shrink_rows_tied,
        shrink_right[None],
    )
    output_sums = adapter(
        "output_near_adapter",
        order,
        in_output(0),
        [heads_parts],
        [near_sibling, output_grad_own],
        output_rows,
        output_right[None],
    )
    arrived, near_sibling, shrink_joined, shrink_sums, output_sums = tie(
        arrived, near_sibling, shrink_joined, shrink_sums, output_sums
    )
    output_grad = [
        piece for pair in pairs_of(output_grad_own, near_sibling, arrived) for piece in pair
    ]
    shrink_parts = [shrink_pairs[0][1], sibling(shrink_pairs[0][0])] + [
        to_chip(values, step) for step, values in enumerate(shrink_joined, 1)
    ]
    heads_grads, heads_total = attend_back(
        order,
        groups,
        post,
        first,
        cos_table,
        sine_table,
        heads_mag,
        heads_sq,
        output_low,
        output_grad,
    )
    grad_parts = heads_grads.reshape(3, groups, share, local_heads)
    joined, both_totals, attend_gain_part, token_extra = product(
        "normed_product",
        20,
        grad_parts,
        heads_low,
        NT,
        correction=(heads_right, heads_sq, heads_mag, [heads_total]),
        lines=(output_total, shrink_total),
        gain=(normed, attend_line),
    )
    joined, shrink_parts, heads_rows_tied, output_rows_tied = tie(
        joined, shrink_parts, heads_rows, output_rows
    )
    output_total, shrink_total = both_totals[:1], both_totals[1:]
    token_parts = [joined[0]] + [to_chip(joined[step], step) for step in range(1, chips)]
    output_mag_part, output_left_part, output_right_part, *shrink_adapter = adapter(
        "output_far_adapter",
        order,
        in_output(CORES),
        [heads_parts],
        output_grad[CORES:],
        output_rows_tied,
        output_right[None],
        (output_low, output_across, output_sq, output_mag, [output_total[None]]),
        output_sums,
        (
            shrink_sums,
            shrink_right[None],
            (shrink_low, shrink_across, shrink_sq, shrink_mag, [shrink_total[None]]),
        ),
    )
    heads_adapter = adapter(
        "heads_adapter",
        order,
        in_heads,
        [normed],
        [heads_grads],
        heads_rows_tied,
        heads_right,
        (token_extra, heads_across, heads_sq, heads_mag, [heads_total]),
    )
    (mixed,) = row_call(
        "mixed",
        mixed_kernel,
        order,
        [(hidden, False)] + [(part, False) for part in shrink_parts],
        (shrink_sq[0], shrink_mag),
        (LOW,),
        0,
        scale_first,
    )
    token_parts, heads_adapter, mixed = tie(token_parts, heads_adapter, mixed)
    *reduced, grad_tokens = reduce_devices(
        "reduce_gradients",
        1,
        [expand_adapter[1], shrink_adapter[2], output_right_part, heads_adapter[1]],
        [expand_gain_part[None], attend_gain_part[None]],
        [expand_adapter[2], shrink_adapter[1], output_left_part, heads_adapter[2]],
        [expand_adapter[0], shrink_adapter[0], output_mag_part, heads_adapter[0]],
        token_job(tokens, grad_hidden, token_parts, attend_line),
    )
    (
        expand_left_grad,
        shrink_right_grad,
        output_right_grad,
        heads_left_grad,
        expand_gain_grad,
        attend_gain_grad,
        expand_right_grad,
        shrink_left_grad,
        output_left_grad,
        heads_right_grad,
        expand_mag_grad,
        shrink_mag_grad,
        output_mag_grad,
        heads_mag_grad,
        grad_tokens,
    ) = copy_out([*reduced, grad_tokens])
    return (
        mixed,
        grad_tokens,
        attend_gain_grad[0, 0],
        expand_gain_grad[0, 0],
        jnp.swapaxes(heads_left_grad, 1, 2),
        heads_right_grad,
        heads_mag_grad[:, 0],
        output_left_grad[0].T,
        output_right_grad[0],
        output_mag_grad[0, 0],
        jnp.swapaxes(expand_left_grad, 1, 2),
        expand_right_grad,
        expand_mag_grad[:, 0],
        shrink_left_grad[0].T,
        shrink_right_grad[0],
        shrink_mag_grad[0, 0],
    )


def solution(mesh):
    placed = (
        P("dp", None),
        P("dp", None),
        P("dp", None),
        P(),
        P(),
        P(None, None, "mp"),
        P(),
        P(None, None, "mp"),
        P(None, "mp"),
        P("mp", None),
        P("mp", None),
        P(),
        P(),
        P(None, None, "mp"),
        P(),
        P(None, None, "mp"),
        P(None, "mp"),
        P("mp", None),
        P("mp", None),
        P(),
        P(),
    )
    return jax.shard_map(
        body,
        mesh=mesh,
        in_specs=placed,
        out_specs=(
            P(("dp", "mp"), None),
            P(("dp", "mp"), None),
            P(),
            P(),
            P(),
            P(None, None, "mp"),
            P(None, "mp"),
            P("mp", None),
            P(),
            P(),
            P(),
            P(None, None, "mp"),
            P(None, "mp"),
            P("mp", None),
            P(),
            P(),
        ),
        check_vma=False,
    )
```

```python
import functools

import jax
import jax.numpy as jnp
import ml_dtypes
import numpy as np
from jax import lax
from jax.experimental import pallas as pl
from jax.experimental.pallas import tpu as pltpu
from jax.sharding import PartitionSpec as P

HEAD_DIM = 128
CORES = 2
LONGEST = 512
ATTEND_BLOCK = 256
ADAPT_SCALE = 2.0
NORM_EPS = 1e-05
ROPE_BASE = 10000.0
MASKED = -1e30

F32 = jnp.float32
LOW = jnp.bfloat16
NN = (((1,), (0,)), ((), ()))
NT = (((1,), (1,)), ((), ()))
TN = (((0,), (0,)), ((), ()))


MESH_IDS = pl.DeviceIdType.MESH


def sibling_id():
    me = lax.axis_index("mp")
    return me // CORES * CORES + lax.rem(me + 1, CORES)


def greet(peers):
    for peer in peers:
        pl.semaphore_signal(
            pltpu.get_barrier_semaphore(), 1, device_id={"mp": peer}, device_id_type=MESH_IDS
        )


def greeted(count):
    pl.semaphore_wait(pltpu.get_barrier_semaphore(), count)


def remote(source, target, send_sem, recv_sem, peer):
    return pltpu.make_async_remote_copy(
        src_ref=source,
        dst_ref=target,
        send_sem=send_sem,
        recv_sem=recv_sem,
        device_id={"mp": peer},
        device_id_type=MESH_IDS,
    )


def dot(left, right, dims=NN):
    return lax.dot_general(left, right, dims, preferred_element_type=F32)


def shape(dims, kind):
    return jax.ShapeDtypeStruct(tuple(dims), kind)


def call(name, kernel, operands, grid, in_specs, out_specs, out_shape, scratch=(), prefetch=(), flops=0, mib=63.5, identity=None):
    moved = sum(v.size * v.dtype.itemsize for v in operands)
    moved += sum(v.size * v.dtype.itemsize for v in out_shape)
    return pl.pallas_call(
        kernel,
        name=name,
        out_shape=out_shape,
        grid_spec=pltpu.PrefetchScalarGridSpec(
            num_scalar_prefetch=len(prefetch),
            grid=grid,
            in_specs=in_specs,
            out_specs=out_specs,
            scratch_shapes=scratch,
        ),
        compiler_params=pltpu.CompilerParams(
            vmem_limit_bytes=int(mib * 2**20), collective_id=identity, has_side_effects=identity is not None
        ),
        cost_estimate=pl.CostEstimate(flops=flops // 16, bytes_accessed=moved // 16, transcendentals=0),
    )(*prefetch, *operands)


def tile_of(size, most):
    return most if size % most == 0 else size


def split_rows(values):
    top = values.astype(LOW)
    rest = (values - top.astype(F32)).astype(LOW)
    return jnp.concatenate([top, rest], axis=0)


def turned(left_map):
    return jnp.swapaxes(left_map, -1, -2)


def norm_weight(total, squares, magnitude):
    norm = jnp.sqrt(squares)
    return total * magnitude / (norm * norm * norm)


def sum_refs(refs):
    total = refs[0][...]
    for ref in refs[1:]:
        total = total + ref[...]
    return total


def fold(values):
    half = values.shape[0] // 2
    return values[:half] + values[half:]


def merge_tile(base_at, low_put, left, right, depth):
    rank = right.shape[0]
    doubled = ADAPT_SCALE * right
    top = doubled.astype(LOW)
    rest = (doubled - top.astype(F32)).astype(LOW)
    right_stack = jnp.concatenate([top, rest, top], axis=0)
    left_pair = split_rows(left)
    left_stack = jnp.concatenate([left_pair[:rank], left_pair[:rank], left_pair[rank:]], axis=0)
    width = right.shape[1]
    wide = 256 if width == 512 else width
    step = tile_of(depth, 1024)
    squares = []
    for at in range(0, width, wide):
        columns = slice(at, at + wide)
        total = jnp.zeros((1, wide), F32)
        for start in range(0, depth, step):
            merged = base_at(start, step, columns).astype(F32) + dot(
                left_stack[:, start : start + step], right_stack[:, columns], TN
            )
            low_put(start, step, columns, merged.astype(LOW))
            total = total + jnp.sum(merged * merged, axis=0, keepdims=True)
        squares.append(total)
    return jnp.concatenate(squares, axis=1)


def merge_pair_kernel(*refs):
    for n in range(2):
        base_ref, left_ref, right_ref = refs[3 * n : 3 * n + 3]
        low_ref, squares_ref = refs[6 + n], refs[8]
        depth = base_ref.shape[0]
        if low_ref.shape[0] > depth:
            low_ref[depth:, :] = jnp.zeros((low_ref.shape[0] - depth, low_ref.shape[1]), LOW)

        def put(start, step, columns, tile, low_ref=low_ref):
            low_ref[start : start + step, columns] = tile

        squares_ref[n : n + 1, :] = merge_tile(
            lambda start, step, columns, base_ref=base_ref: base_ref[start : start + step, columns],
            put,
            left_ref[...],
            right_ref[...],
            depth,
        )


def merge_pair(triples):
    operands, in_specs, low_specs, low_shapes = [], [], [], []
    width = triples[0][0].shape[1]
    wide = tile_of(width, 512)
    for base, left, right in triples:
        depth, rank = base.shape[0], right.shape[0]
        operands += [base, left, right]
        in_specs += [
            pl.BlockSpec((depth, wide), lambda n: (0, n)),
            pl.BlockSpec((rank, depth), lambda n: (0, 0)),
            pl.BlockSpec((rank, wide), lambda n: (0, n)),
        ]
        low_specs.append(pl.BlockSpec((padded(depth), wide), lambda n: (0, n)))
        low_shapes.append(shape((padded(depth), width), LOW))
    return call(
        "merge_pair",
        merge_pair_kernel,
        tuple(operands),
        (width // wide,),
        in_specs,
        low_specs + [pl.BlockSpec((2, wide), lambda n: (0, n))],
        low_shapes + [shape((2, width), F32)],
        flops=2 * sum(v.size for v in operands) * 256,
    )


def merge_kernel(base_ref, left_ref, right_ref, low_ref, squares_ref):
    depth, width = base_ref.shape[1:]
    if low_ref.shape[1] > depth:
        low_ref[0, depth:, :] = jnp.zeros((low_ref.shape[1] - depth, low_ref.shape[2]), LOW)
    if low_ref.shape[2] > width:
        spare = low_ref.shape[2] - width
        low_ref[0, :, width:] = jnp.zeros((low_ref.shape[1], spare), LOW)
        squares_ref[0, :, width:] = jnp.ones((1, spare), F32)

    def put(start, step, columns, tile):
        low_ref[0, start : start + step, columns] = tile

    squares = merge_tile(
        lambda start, step, columns: base_ref[0, start : start + step, columns],
        put,
        left_ref[0],
        right_ref[0],
        depth,
    )

    @pl.when(pl.program_id(2) == 0)
    def _():
        squares_ref[0, :, :width] = squares

    @pl.when(pl.program_id(2) > 0)
    def _():
        squares_ref[0, :, :width] += squares


def padded(size):
    return -(-size // 256) * 256


def pad_last(values, size):
    return jnp.pad(values, [(0, 0)] * (values.ndim - 1) + [(0, size - values.shape[-1])])


def merge(base, left, right, deep, wide):
    members, depth, width = base.shape
    low_deep = padded(deep) if deep == depth else deep
    low_wide = padded(wide) if wide == width else wide
    low_shape = (members, depth // deep * low_deep, width // wide * low_wide)
    rank = right.shape[1]
    return call(
        "merge",
        merge_kernel,
        (base, left, right),
        (members, width // wide, depth // deep),
        [
            pl.BlockSpec((1, deep, wide), lambda m, n, k: (m, k, n)),
            pl.BlockSpec((1, rank, deep), lambda m, n, k: (m, 0, k)),
            pl.BlockSpec((1, rank, wide), lambda m, n, k: (m, 0, n)),
        ],
        [
            pl.BlockSpec((1, low_deep, low_wide), lambda m, n, k: (m, k, n)),
            pl.BlockSpec((1, 1, low_wide), lambda m, n, k: (m, 0, n)),
        ],
        [shape(low_shape, LOW), shape((members, 1, low_shape[2]), F32)],
        flops=2 * members * depth * width * 256,
    )


def rms_rows(values):
    return lax.rsqrt(jnp.mean(values * values, axis=1, keepdims=True) + NORM_EPS)


TABLE_STEP = 32


def table_pieces(places):
    half = np.arange(HEAD_DIM) % (HEAD_DIM // 2)
    angles = np.asarray(places)[:, None] * ROPE_BASE ** (-2.0 * half / HEAD_DIM)[None, :]
    rest = np.concatenate([np.cos(angles), np.sin(angles)], axis=1)
    pieces = []
    for _ in range(3):
        pieces.append(rest.astype(ml_dtypes.bfloat16))
        rest = rest - pieces[-1].astype(np.float64)
    return jnp.asarray(np.concatenate(pieces, axis=0))


def rotation(first, coarse, fine):
    rows = first.shape[0]
    position = lax.broadcasted_iota(jnp.int32, (rows, 1), 0) - first
    lane = lax.broadcasted_iota(jnp.int32, (rows, 3 * TABLE_STEP), 1) % TABLE_STEP
    pick = lambda place, table: dot((lane == place).astype(F32).astype(LOW), table)
    high = pick(position // TABLE_STEP, coarse)
    small = pick(position % TABLE_STEP, fine)
    cos_a, sin_a = high[:, :HEAD_DIM], high[:, HEAD_DIM:]
    cos_b, sin_b = small[:, :HEAD_DIM], small[:, HEAD_DIM:]
    sine = sin_a * cos_b + cos_a * sin_b
    left_half = lax.broadcasted_iota(jnp.int32, sine.shape, 1) < HEAD_DIM // 2
    return cos_a * cos_b - sin_a * sin_b, jnp.where(left_half, -sine, sine)


def heads_kernel(
    token_ref,
    gain_ref,
    base_ref,
    left_ref,
    right_ref,
    magnitude_ref,
    segment_ref,
    coarse_ref,
    fine_ref,
    part_ref,
    normed_ref,
    low_ref,
    post_ref,
    squares_ref,
    across_ref,
    cos_ref,
    sine_ref,
    output_sum_ref,
    shrink_sum_ref,
    first_ref,
    rows_all,
    part_mine,
    part_got,
    send_sems,
    recv_sems,
):
    total_rows = token_ref.shape[0]
    depth, width = base_ref.shape[1:]
    rank = right_ref.shape[1]
    groups = part_got.shape[0]
    me = lax.axis_index("mp")
    peers = [lax.rem(me + k, groups) for k in range(groups)]
    part_copies = [
        remote(part_mine, part_got.at[k], send_sems.at[k], recv_sems.at[k], peers[k])
        for k in range(1, groups)
    ]

    @pl.when(pl.program_id(0) == 0)
    def _():
        greet(peers[1:])
        part_mine[...] = part_ref[...]
        step = 128

        def some(i, carry):
            at = pl.ds(pl.multiple_of(i * step, step), step)
            values = token_ref[at, :].astype(F32)
            low = (values * rms_rows(values) * gain_ref[...]).astype(LOW)
            normed_ref[at, :] = low
            rows_all[at, :] = low
            return carry

        lax.fori_loop(0, total_rows // step, some, 0)
        ids = segment_ref[...].astype(F32)
        ids_down = jnp.transpose(jnp.broadcast_to(ids, (8, total_rows)))[:, :1]
        for start in range(0, total_rows, 256):
            rows = slice(start, start + 256)
            smaller = jnp.where(ids < ids_down[rows], 1.0, 0.0)
            first = jnp.sum(smaller, axis=1, keepdims=True).astype(jnp.int32)
            first_ref[rows, :] = first
            cosine, sine = rotation(first - start, coarse_ref[...], fine_ref[...])
            cos_ref[rows, :] = cosine
            sine_ref[rows, :] = sine
        greeted(groups - 1)
        for copy in part_copies:
            copy.start()

    @pl.when(pl.program_id(0) == pl.num_programs(0) - 1)
    def _():
        total = part_mine[...]
        for k, copy in enumerate(part_copies, 1):
            copy.wait_recv()
            total = total + part_got[k]
        output_sum_ref[0] = total[:1]
        shrink_sum_ref[0] = total[1:]
        for copy in part_copies:
            copy.wait_send()

    rows_all[total_rows:, :] = left_ref[0].astype(LOW)
    turning = pl.program_id(0) < 2
    wide = 256

    def put(start, step, columns, tile):
        low_ref[0, start : start + step, columns] = tile

    squares_ref[0] = merge_tile(
        lambda start, step, columns: base_ref[0, start : start + step, columns],
        put,
        left_ref[0],
        right_ref[0],
        depth,
    )
    for column in range(0, width, wide):
        columns = slice(column, column + wide)
        magnitude = magnitude_ref[pl.ds(pl.program_id(0), 1), columns]
        scale = magnitude / jnp.sqrt(squares_ref[0, :, columns])
        low = low_ref[0, :, columns]
        step = min(512, total_rows)
        for start in range(0, total_rows, step):
            last = start + step == total_rows
            rows = slice(start, start + step)
            pre = dot(rows_all[start : start + step + (rank if last else 0), :], low)
            if last:
                across_ref[0, :, columns] = pre[step:]
            post = pre[:step] * scale
            cos_table = jnp.where(turning, cos_ref[rows, :], 1.0)
            sine_table = jnp.where(turning, sine_ref[rows, :], 0.0)
            for head in range(0, wide, HEAD_DIM):
                piece = post[:, head : head + HEAD_DIM]
                other = pltpu.roll(piece, HEAD_DIM // 2, 1)
                post_ref[0, rows, column + head : column + head + HEAD_DIM] = (
                    piece * cos_table + other * sine_table
                ).astype(LOW)


def project_heads(tokens, gain, base, left, right, magnitude, segments, part, groups):
    members, depth, width = base.shape
    rows, rank = tokens.shape[0], right.shape[1]
    coarse = table_pieces(np.arange(TABLE_STEP) * TABLE_STEP)
    fine = table_pieces(np.arange(TABLE_STEP))
    whole = lambda v: pl.BlockSpec(v.shape, lambda m: (0,) * v.ndim)
    of_member = lambda *dims: pl.BlockSpec((1,) + dims, lambda m: (m, 0, 0))
    table = pl.BlockSpec((rows, HEAD_DIM), lambda m: (0, 0))
    return call(
        "project_heads",
        heads_kernel,
        (tokens, gain, base, left, right, magnitude, segments, coarse, fine, part),
        (members,),
        [
            whole(tokens),
            whole(gain),
            of_member(depth, width),
            of_member(rank, depth),
            of_member(rank, width),
            whole(magnitude),
            whole(segments),
            whole(coarse),
            whole(fine),
            whole(part),
        ],
        [
            whole(tokens),
            of_member(depth, width),
            of_member(rows, width),
            of_member(1, width),
            of_member(rank, width),
            table,
            table,
            pl.BlockSpec((1, 1, depth), lambda m: (0, 0, 0)),
            pl.BlockSpec((1, 1, depth), lambda m: (0, 0, 0)),
            pl.BlockSpec((rows, 1), lambda m: (0, 0)),
        ],
        [
            shape((rows, depth), LOW),
            shape(base.shape, LOW),
            shape((members, rows, width), LOW),
            shape((members, 1, width), F32),
            shape((members, rank, width), F32),
            shape((rows, HEAD_DIM), F32),
            shape((rows, HEAD_DIM), F32),
            shape((1, 1, depth), F32),
            shape((1, 1, depth), F32),
            shape((rows, 1), jnp.int32),
        ],
        scratch=[
            pltpu.VMEM((rows + rank, depth), LOW),
            pltpu.VMEM(part.shape, F32),
            pltpu.VMEM((groups,) + part.shape, F32),
            pltpu.SemaphoreType.DMA((groups,)),
            pltpu.SemaphoreType.DMA((groups,)),
        ],
        identity=2,
        flops=2 * members * rows * depth * width,
    )


def key_start(block):
    return max(0, (block * ATTEND_BLOCK - (LONGEST - 1)) // ATTEND_BLOCK * ATTEND_BLOCK)


def masked_probs(scores, first, row_at, key_at):
    scores = scores * HEAD_DIM ** (-0.5)
    places = row_at + lax.broadcasted_iota(jnp.int32, scores.shape, 0)
    others = key_at + lax.broadcasted_iota(jnp.int32, scores.shape, 1)
    scores = jnp.where((others >= first) & (others <= places), scores, MASKED)
    exp_scores = jnp.exp(scores - jnp.max(scores, axis=1, keepdims=True))
    return exp_scores * (1.0 / jnp.sum(exp_scores, axis=1, keepdims=True))


class Unit:
    def __init__(self, head, block):
        self.row_at, self.key_at = block * ATTEND_BLOCK, key_start(block)
        self.rows = slice(self.row_at, self.row_at + ATTEND_BLOCK)
        self.keys = slice(self.key_at, self.row_at + ATTEND_BLOCK)
        self.lanes = slice(head * HEAD_DIM, (head + 1) * HEAD_DIM)


def units_of(rows, width, most):
    units = [
        Unit(head, block)
        for block in range(rows // ATTEND_BLOCK)
        for head in range(width // HEAD_DIM)
    ]
    return [units[at : at + most] for at in range(0, len(units), most)]


def put_rows(ref, lead, row_at, lanes, values, order_ref, groups):
    share = ref.shape[len(lead)] // groups
    step = min(share, values.shape[0])
    for start in range(0, values.shape[0], step):
        group = (row_at + start) // share
        inside = (row_at + start) % share
        at = pl.multiple_of(order_ref[groups + group] * share + inside, step)
        ref[(*lead, pl.ds(at, step), lanes)] = values[start : start + step].astype(ref.dtype)


def attend_kernel(groups, order_ref, query_ref, key_ref, value_ref, first_ref, out_ref):
    for some in units_of(*query_ref.shape[1:], 4):
        scores = [
            dot(query_ref[0, u.rows, u.lanes], key_ref[0, u.keys, u.lanes], NT) for u in some
        ]
        probs = [
            masked_probs(s, first_ref[u.rows, :], u.row_at, u.key_at).astype(LOW)
            for u, s in zip(some, scores)
        ]
        for u, p in zip(some, probs):
            mixed = dot(p, value_ref[0, u.keys, u.lanes])
            put_rows(out_ref, (), u.row_at, u.lanes, mixed, order_ref, groups)


def attend(order, groups, post, first):
    rows, width = post.shape[1:]
    wide = 2 * HEAD_DIM
    member = lambda m: pl.BlockSpec((1, rows, wide), lambda h, o: (m, 0, h))
    return call(
        "attend",
        functools.partial(attend_kernel, groups),
        (post, post, post, first),
        (width // wide,),
        [member(0), member(1), member(2), pl.BlockSpec((rows, 1), lambda h, o: (0, 0))],
        [pl.BlockSpec((rows, wide), lambda h, o: (0, h))],
        [shape((rows, width), LOW)],
        prefetch=(order,),
        flops=4 * rows * rows * width,
    )[0]


def attend_back_kernel(
    groups,
    order_ref,
    query_ref,
    key_ref,
    value_ref,
    first_ref,
    cos_ref,
    sine_ref,
    magnitude_ref,
    squares_ref,
    low_ref,
    *rest,
):
    pieces, (grad_ref, total_ref, upper_all, heads_grad, key_grad, value_grad, sems) = rest[:-7], rest[-7:]
    rows_all, width = query_ref.shape[1:]
    share = rows_all // groups

    @pl.when(pl.program_id(0) == 0)
    def _():
        copies = []
        for place, piece in enumerate(pieces):
            at = pl.multiple_of(order_ref[place] * share, share)
            copies.append(
                pltpu.make_async_copy(piece, upper_all.at[pl.ds(at, share), :], sems.at[place])
            )
            copies[-1].start()
        for copy in copies:
            copy.wait()

    step = min(512, rows_all)
    for start in range(0, rows_all, step):
        at = slice(start, start + step)
        heads_grad[at, :] = dot(upper_all[at, :], low_ref[0], NT).astype(LOW)
    norm = [jnp.sqrt(squares_ref[m]) for m in range(3)]
    scale = [magnitude_ref[m : m + 1] / norm[m] for m in range(3)]
    heads = range(0, width, HEAD_DIM)
    totals = [jnp.zeros((1, width), F32) for _ in range(3)]
    filled = set()

    def back(values, rows):
        return values * cos_ref[rows, :] - pltpu.roll(values, HEAD_DIM // 2, 1) * sine_ref[rows, :]

    def add(ref, unit, values):
        for start in range(0, values.shape[0], ATTEND_BLOCK):
            at = unit.key_at + start
            rows = slice(at, at + ATTEND_BLOCK)
            name = (id(ref), at, unit.lanes.start)
            if name in filled:
                ref[rows, unit.lanes] += values[start : start + ATTEND_BLOCK]
            else:
                filled.add(name)
                ref[rows, unit.lanes] = values[start : start + ATTEND_BLOCK]

    def spread(per_head):
        return jnp.concatenate(per_head, axis=1)

    query_totals = [jnp.zeros((1, HEAD_DIM), F32) for _ in heads]
    for some in units_of(rows_all, width, 2):
        scores = [
            dot(query_ref[0, u.rows, u.lanes], key_ref[0, u.keys, u.lanes], NT) for u in some
        ]
        grad_weights = [
            dot(heads_grad[u.rows, u.lanes], value_ref[0, u.keys, u.lanes], NT) for u in some
        ]
        probs = [
            masked_probs(s, first_ref[u.rows, :], u.row_at, u.key_at)
            for u, s in zip(some, scores)
        ]
        grad_scores = [
            (p * (g - jnp.sum(p * g, axis=1, keepdims=True))).astype(LOW)
            for p, g in zip(probs, grad_weights)
        ]
        for u, p, g in zip(some, probs, grad_scores):
            add(value_grad, u, dot(p.astype(LOW), heads_grad[u.rows, u.lanes], TN))
            add(key_grad, u, dot(g, query_ref[0, u.rows, u.lanes], TN))
        for u, g in zip(some, grad_scores):
            grad = back(dot(g, key_ref[0, u.keys, u.lanes]) * HEAD_DIM ** (-0.5), u.rows)
            head = u.lanes.start // HEAD_DIM
            post = back(query_ref[0, u.rows, u.lanes].astype(F32), u.rows)
            query_totals[head] = query_totals[head] + jnp.sum(grad * post, axis=0, keepdims=True)
            put_rows(grad_ref, (0,), u.row_at, u.lanes, grad * scale[0][:, u.lanes], order_ref, groups)
    totals[0] = spread(query_totals)
    for row_at in range(0, rows_all, ATTEND_BLOCK):
        rows = slice(row_at, row_at + ATTEND_BLOCK)
        for head in heads:
            lanes = slice(head, head + HEAD_DIM)
            grad = back(key_grad[rows, lanes] * HEAD_DIM ** (-0.5), rows)
            post = back(key_ref[0, rows, lanes].astype(F32), rows)
            part = jnp.sum(grad * post, axis=0, keepdims=True)
            query_totals[head // HEAD_DIM] = part if row_at == 0 else query_totals[head // HEAD_DIM] + part
            put_rows(grad_ref, (1,), row_at, lanes, grad * scale[1][:, lanes], order_ref, groups)
        grad = value_grad[rows, :]
        totals[2] = totals[2] + jnp.sum(grad * value_ref[0, rows, :].astype(F32), axis=0, keepdims=True)
        put_rows(grad_ref, (2,), row_at, slice(0, width), grad * scale[2], order_ref, groups)
    totals[1] = spread(query_totals)
    for m in range(3):
        total_ref[m] = totals[m] / scale[m]


def attend_back(order, groups, post, first, cos_table, sine_table, magnitude, squares, low, pieces):
    rows, width = post.shape[1:]
    depth = low.shape[2]
    wide = 2 * HEAD_DIM
    member = lambda m: pl.BlockSpec((1, rows, wide), lambda h, o: (m, 0, h))
    table = pl.BlockSpec((rows, HEAD_DIM), lambda h, o: (0, 0))
    column = pl.BlockSpec((3, 1, wide), lambda h, o: (0, 0, h))
    return call(
        "attend_back",
        functools.partial(attend_back_kernel, groups),
        (post, post, post, first, cos_table, sine_table, magnitude, squares, low, *pieces),
        (width // wide,),
        [
            member(0),
            member(1),
            member(2),
            pl.BlockSpec((rows, 1), lambda h, o: (0, 0)),
            table,
            table,
            pl.BlockSpec((3, wide), lambda h, o: (0, h)),
            column,
            pl.BlockSpec((1, wide, depth), lambda h, o: (0, h, 0)),
            *[pl.BlockSpec(memory_space=pl.ANY) for _ in pieces],
        ],
        [pl.BlockSpec((3, rows, wide), lambda h, o: (0, 0, h)), column],
        [shape((3, rows, width), LOW), shape((3, 1, width), F32)],
        scratch=[
            pltpu.VMEM((rows, depth), LOW),
            pltpu.VMEM((rows, wide), LOW),
            pltpu.VMEM((rows, wide), F32),
            pltpu.VMEM((rows, wide), F32),
            pltpu.SemaphoreType.DMA((len(pieces),)),
        ],
        prefetch=(order,),
        flops=10 * rows * rows * width + 2 * rows * width * depth,
    )


def product_kernel(dims, n_totals, n_lines, has_gain, steps, *refs):
    value_ref, weight_ref = refs[:2]
    if n_totals == 0:
        left_ref, *refs = refs[2:]
    else:
        right_ref, squares_ref, magnitude_ref = refs[2:5]
        totals, refs = refs[5 : 5 + n_totals], refs[5 + n_totals :]
    lines = []
    if has_gain:
        normed_ref, gain_ref, *refs = refs
    if n_lines > 0:
        lines, refs = refs[:n_lines], refs[n_lines:]
        *refs, line_mine, line_got, line_send_sems, line_recv_sems = refs
    *outs, extra_ref, rows_all, sent, got, send_sems, recv_sems = refs
    if has_gain:
        *outs, gain_out = outs
    line_outs, outs = outs[len(outs) - n_lines :], outs[: len(outs) - n_lines]
    members, groups, share, inner = value_ref.shape
    count, wide = groups * share, extra_ref.shape[2]
    now = pl.program_id(0)
    sibling = sibling_id()
    me = lax.axis_index("mp")
    peers = [lax.rem(me + k, groups) for k in range(1, groups)] if n_lines > 0 else [sibling]
    line_copies = [
        remote(line_mine, line_got.at[k], line_send_sems.at[k], line_recv_sems.at[k], peer)
        for k, peer in enumerate(peers if n_lines > 0 else [], 1)
    ]

    @pl.when(now == 0)
    def _():
        greet(peers)
        for n, ref in enumerate(lines):
            line_mine[n : n + 1, :] = ref[...]
        if n_totals > 0:
            total = sum_refs(totals)
        for m in range(members):
            rows_all[m, :count, :] = value_ref[m].reshape(count, inner)
            if n_totals == 0:
                rows_all[m, count:, :] = left_ref[m].astype(LOW)
            else:
                weight = norm_weight(total[m], squares_ref[m], magnitude_ref[m : m + 1])
                rows_all[m, count:, :] = (right_ref[m] * weight).astype(LOW)

    result = None
    for m in range(members):
        part = dot(rows_all[m], weight_ref[m], dims)
        extra_ref[m] = part[count:]
        result = part[:count] if result is None else result + part[:count]

    def columns(step):
        return pl.ds(pl.multiple_of(step * wide, wide), wide)

    def copy(step):
        return remote(sent.at[step], got.at[step], send_sems.at[step], recv_sems.at[step], sibling)

    def add(step):
        copy(step).wait_recv()
        for n, ref in enumerate(outs):
            total = ref[:, columns(step)].astype(F32) + got[step, n].astype(F32)
            ref[:, columns(step)] = total.astype(LOW)

    if has_gain:
        terms = jnp.zeros((1, wide), F32)
        for place in range(groups):
            group = lax.rem(me // CORES + place // CORES, groups // CORES) * CORES
            group = group + lax.rem(me + 1 + place, CORES)
            rows = pl.ds(pl.multiple_of(group * share, share), share)
            mine = result[place * share : (place + 1) * share]
            terms = terms + jnp.sum(
                mine * normed_ref[rows, :].astype(F32), axis=0, keepdims=True
            )
        gain_out[...] = terms / gain_ref[...]
    for n, ref in enumerate(outs):
        at = CORES * n * share
        sent[now, n] = result[at : at + share].astype(LOW)
        ref[:, columns(now)] = result[at + share : at + CORES * share].astype(LOW)

    @pl.when(now == 0)
    def _():
        greeted(len(peers))
        for each in line_copies:
            each.start()

    copy(now).start()

    @pl.when(now > 0)
    def _():
        add(now - 1)

    @pl.when(now == steps - 1)
    def _():
        add(now)
        for step in range(steps):
            copy(step).wait_send()
        if n_lines > 0:
            line_sum = line_mine[...]
            for k, each in enumerate(line_copies, 1):
                each.wait_recv()
                line_sum = line_sum + line_got[k]
            for n, ref in enumerate(line_outs):
                ref[0] = line_sum[n : n + 1]
            for each in line_copies:
                each.wait_send()


def product(name, identity, values, weights, dims, left=None, correction=None, lines=(), gain=()):
    members, groups, share, inner = values.shape
    chips = groups // CORES
    width = weights.shape[2] if dims is NN else weights.shape[1]
    wide = tile_of(width, 512)
    steps = width // wide
    if dims is NN:
        weight_spec = pl.BlockSpec((members, inner, wide), lambda n: (0, 0, n))
    else:
        weight_spec = pl.BlockSpec((members, wide, inner), lambda n: (0, n, 0))
    if correction is None:
        extra, n_totals, rank = (left,), 0, left.shape[1]
    else:
        right, squares, magnitude, totals = correction
        extra, n_totals, rank = (right, squares, magnitude, *totals), len(totals), right.shape[1]
    fixed = lambda v: pl.BlockSpec(v.shape, lambda n: (0,) * v.ndim)
    out = pl.BlockSpec((share, width), lambda n: (0, 0))
    line_specs, line_shapes, line_scratch = [], [], []
    if lines:
        line = (len(lines), width)
        line_specs = [pl.BlockSpec((1, 1, width), lambda n: (0, 0, 0)) for _ in lines]
        line_shapes = [shape((1, 1, width), F32) for _ in lines]
        line_scratch = [
            pltpu.VMEM(line, F32),
            pltpu.VMEM((groups,) + line, F32),
            pltpu.SemaphoreType.DMA((groups,)),
            pltpu.SemaphoreType.DMA((groups,)),
        ]
    gain_specs, gain_shapes, gain_in = [], [], []
    if gain:
        one = pl.BlockSpec((1, wide), lambda n: (0, n))
        gain_in = [pl.BlockSpec((gain[0].shape[0], wide), lambda n: (0, n)), one]
        gain_specs, gain_shapes = [one], [shape((1, width), F32)]
    results = call(
        name,
        functools.partial(product_kernel, dims, n_totals, len(lines), bool(gain), steps),
        (values, weights, *extra, *gain, *lines),
        (steps,),
        [fixed(values), weight_spec]
        + [fixed(v) for v in extra]
        + gain_in
        + [fixed(v) for v in lines],
        [out] * chips + line_specs + gain_specs + [pl.BlockSpec((members, rank, wide), lambda n: (0, 0, n))],
        [shape((share, width), LOW)] * chips
        + line_shapes
        + gain_shapes
        + [shape((members, rank, width), F32)],
        scratch=[
            pltpu.VMEM((members, groups * share + rank, inner), LOW),
            pltpu.VMEM((steps, chips, share, wide), LOW),
            pltpu.VMEM((steps, chips, share, wide), LOW),
            pltpu.SemaphoreType.DMA((steps,)),
            pltpu.SemaphoreType.DMA((steps,)),
        ]
        + line_scratch,
        flops=2 * members * groups * share * inner * width,
        identity=identity,
    )
    return results[:chips], *results[chips:]


def shrink_kernel(chips, order_ref, *refs):
    values, (weight_ref, left_ref, cot_ref), outs = refs[:chips], refs[chips : chips + 3], refs[chips + 3 :]
    total_ref, across_ref, rows_all = outs[-3:]
    both, inner = values[0].shape
    share, depth = both // CORES, left_ref.shape[2]
    count = chips * both

    @pl.when(pl.program_id(0) == 0)
    def _():
        for step, ref in enumerate(values):
            rows_all[step * both : (step + 1) * both, :] = ref[...]
        if inner > depth:
            rows_all[count:, depth:] = jnp.zeros((rows_all.shape[0] - count, inner - depth), LOW)
        rows_all[count:, :depth] = left_ref[0].astype(LOW)

    result = dot(rows_all[...], weight_ref[0])
    across_ref[0] = result[count:]
    total = jnp.zeros((1, weight_ref.shape[2]), F32)
    for place in range(chips * CORES):
        pre = result[place * share : (place + 1) * share]
        outs[place][...] = pre.astype(LOW)
        at = pl.multiple_of(order_ref[place] * share, share)
        cot = cot_ref[pl.ds(at, share), :].astype(F32)
        total = total + jnp.sum(pre * cot, axis=0, keepdims=True)
    total_ref[...] = total


def shrink_product(order, values, weights, left, cotangent):
    chips = len(values)
    share, inner = values[0].shape[0] // CORES, values[0].shape[1]
    width, rank = weights.shape[2], left.shape[1]
    rows = chips * CORES * share
    wide = tile_of(width, 512)
    fixed = lambda v: pl.BlockSpec(v.shape, lambda n, o: (0,) * v.ndim)
    results = call(
        "shrink_product",
        functools.partial(shrink_kernel, chips),
        (*values, weights, left, cotangent),
        (width // wide,),
        [fixed(v) for v in values]
        + [
            pl.BlockSpec((1, inner, wide), lambda n, o: (0, 0, n)),
            fixed(left),
            pl.BlockSpec((rows, wide), lambda n, o: (0, n)),
        ],
        [pl.BlockSpec((share, wide), lambda n, o: (0, n))] * (chips * CORES)
        + [
            pl.BlockSpec((1, wide), lambda n, o: (0, n)),
            pl.BlockSpec((1, rank, wide), lambda n, o: (0, 0, n)),
        ],
        [shape((share, width), LOW)] * (chips * CORES)
        + [shape((1, width), F32), shape((1, rank, width), F32)],
        scratch=[pltpu.VMEM((rows + rank, inner), LOW)],
        prefetch=(order,),
        flops=2 * rows * inner * width,
    )
    return results[: chips * CORES], results[-2], results[-1]


def row_call(name, kernel, order, given, whole, out_kinds, sums, prepare):
    share = min(v.shape[0] for v, _ in given)
    width = given[0][0].shape[1]
    halves = 2
    half = share // halves
    count = len(given)

    def run(order_ref, *refs):
        sources, rest = refs[:count], refs[count : -count - 1]
        held, sems = refs[-count - 1 : -1], refs[-1]

        def copies(part):
            for i, ((_, cut), source, target) in enumerate(zip(given, sources, held)):
                at = part * half
                if cut:
                    at = pl.multiple_of(order_ref[1] * share + at, half)
                yield pltpu.make_async_copy(
                    source.at[pl.ds(at, half), :],
                    target.at[pl.ds(part * half, half), :],
                    sems.at[part, i],
                )

        for part in range(halves):

            @pl.when(pl.program_id(0) == part)
            def _(part=part):
                if part == 0:
                    for copy in copies(part):
                        copy.start()
                for copy in copies(part):
                    copy.wait()
                if part + 1 < halves:
                    for copy in copies(part + 1):
                        copy.start()

        outs = rest[len(whole) : len(whole) + len(out_kinds)]
        totals, sums_held = rest[len(whole) + len(out_kinds) :][:sums], rest[len(rest) - sums :]
        tile = 32
        lines = prepare(*[ref[...] for ref in rest[: len(whole)]])
        for ref in sums_held:
            ref[...] = jnp.zeros_like(ref)

        def some(i, carry):
            inside = pl.ds(pl.multiple_of(i * tile, tile), tile)
            at = pl.ds(pl.multiple_of(pl.program_id(0) * half + i * tile, tile), tile)
            values = kernel([ref[at, :].astype(F32) for ref in held], *lines)
            for ref, value in zip(outs, values):
                ref[inside, :] = value.astype(ref.dtype)
            for ref, value in zip(sums_held, values[len(outs) :]):
                ref[...] += jnp.sum(value.reshape(tile // 8, 8, width), axis=0)
            return carry

        lax.fori_loop(0, half // tile, some, 0, unroll=2)
        for ref, held_ref in zip(totals, sums_held):
            add_column(ref, held_ref[...])

    line = pl.BlockSpec((1, width), lambda i, o: (0, 0))
    return call(
        name,
        run,
        (*[v for v, _ in given], *whole),
        (halves,),
        [pl.BlockSpec(memory_space=pl.ANY) for _ in given] + [line for _ in whole],
        [pl.BlockSpec((half, width), lambda i, o: (i, 0)) for _ in out_kinds]
        + [line for _ in range(sums)],
        [shape((share, width), kind) for kind in out_kinds]
        + [shape((1, width), F32) for _ in range(sums)],
        scratch=[pltpu.VMEM((8, width), F32) for _ in range(sums)]
        + [pltpu.VMEM((share, width), v.dtype) for v, _ in given]
        + [pltpu.SemaphoreType.DMA((halves, count))],
        prefetch=(order,),
        flops=20 * share * width,
    )


def sum_of(values):
    total = values[0]
    for value in values[1:]:
        total = total + value
    return total


def add_column(ref, values):
    part = jnp.sum(values, axis=0, keepdims=True)

    @pl.when(pl.program_id(0) == 0)
    def _():
        ref[...] = part

    @pl.when(pl.program_id(0) > 0)
    def _():
        ref[...] += part


def scale_first(squares, magnitude, *rest):
    norm = jnp.sqrt(squares)
    return (magnitude / norm, norm / magnitude, *rest)


def hidden_kernel(given, scale, inverse, gain):
    hidden = given[0] + sum_of(given[1:]) * scale
    return hidden, hidden * rms_rows(hidden) * gain


def mixed_kernel(given, scale, inverse):
    return (given[0] + sum_of(given[1:]) * scale,)


def norm_back(grad_normed, values, gain):
    factor = rms_rows(values)
    scaled = grad_normed * gain
    inner = jnp.mean(scaled * values, axis=1, keepdims=True)
    back = factor * scaled - values * (factor * factor * factor * inner)
    return back, grad_normed * values * factor


def hidden_back_kernel(given, scale, inverse, gain):
    cot, token, hidden = given[:3]
    back, gain_terms = norm_back(sum_of(given[3:]), hidden, gain)
    grad = cot + back
    return grad, grad * scale, grad * ((hidden - token) * inverse), gain_terms


def shrink_back_kernel(places, order_ref, *refs):
    cots, (low_ref, squares_ref, magnitude_ref, product_ref, grad_ref, rows_all) = refs[:places], refs[places:]
    scale = magnitude_ref[0] / jnp.sqrt(squares_ref[0])
    share = cots[0].shape[0]
    for place, cot_ref in enumerate(cots):
        grad = (cot_ref[...].astype(F32) * scale).astype(LOW)
        grad_ref[place] = grad
        rows_all[place * share : (place + 1) * share, :] = grad
    result = dot(rows_all[...], low_ref[0], NT).astype(LOW)
    for place in range(places):
        product_ref[place] = result[place * share : (place + 1) * share]


def shrink_back(order, cotangent, low, squares, magnitude, groups):
    rows, width = cotangent.shape
    share, inner = rows // groups, low.shape[1]
    places = CORES
    line = pl.BlockSpec((1, 1, width), lambda j, o: (0, 0, 0))
    cot = lambda place: pl.BlockSpec((share, width), lambda j, o: (o[places * j + place], 0))
    return call(
        "shrink_back",
        functools.partial(shrink_back_kernel, places),
        (*[cotangent] * places, low, squares, magnitude),
        (groups // places,),
        [cot(place) for place in range(places)]
        + [pl.BlockSpec((1, inner, width), lambda j, o: (0, 0, 0)), line, line],
        [
            pl.BlockSpec((places, share, inner), lambda j, o: (j, 0, 0)),
            pl.BlockSpec((places, share, width), lambda j, o: (j, 0, 0)),
        ],
        [shape((groups, share, inner), LOW), shape((groups, share, width), LOW)],
        scratch=[pltpu.VMEM((places * share, width), LOW)],
        prefetch=(order,),
        flops=2 * rows * width * inner,
    )


def expand_kernel(step, first, last, n_totals, *refs):
    mine_ref, low_ref, grad_ref, squares_ref, magnitude_ref = refs[:5]
    refs = list(refs[5:])
    left_ref = refs.pop(0) if first else None
    right_ref = refs.pop(0) if last else None
    before = [refs.pop(0) for _ in range(n_totals)]
    product_ref, back_ref, rows_ref, total_ref, joined_ref = refs[:5]
    refs = refs[5:]
    across_ref = refs.pop(0) if first else None
    extra_ref = refs.pop(0) if last else None
    rows_all, low_all, grad_all, product_all, back_all, sent, got, in_sems, out_sems, send_sems, recv_sems = refs
    share, depth = mine_ref.shape
    sibling = sibling_id()
    greet([sibling])
    both = CORES * share
    width, ff = low_ref.shape[2], magnitude_ref.shape[1]
    tile = 256
    cuts = [slice(at, at + tile) for at in range(0, width, tile)]

    mine_copy = pltpu.make_async_copy(mine_ref, rows_all.at[pl.ds(share, share), :], in_sems.at[0])
    other_copy = remote(
        mine_ref,
        rows_all.at[pl.ds(0, share), :],
        send_sems.at[sent.shape[0]],
        recv_sems.at[sent.shape[0]],
        sibling,
    )
    tile_copies = []
    for n, cut in enumerate(cuts):
        lanes = pl.ds(cut.start, tile)
        tile_copies.append(
            [
                pltpu.make_async_copy(
                    low_ref.at[:, :, lanes], low_all.at[:, :, lanes], in_sems.at[2 + 2 * n]
                ),
                pltpu.make_async_copy(
                    grad_ref.at[pl.ds(CORES * step, CORES), :, lanes],
                    grad_all.at[:, :, lanes],
                    in_sems.at[3 + 2 * n],
                ),
            ]
        )
    ahead = 2
    mine_copy.start()
    for copy in tile_copies[0]:
        copy.start()
    greeted(1)
    other_copy.start()
    for copies in tile_copies[1:ahead]:
        for copy in copies:
            copy.start()
    if first:
        rank = across_ref.shape[1]
        for m in range(2):
            rows_all[both + m * rank : both + (m + 1) * rank, :] = left_ref[m].astype(LOW)
    mine_copy.wait()
    out_copies = [
        pltpu.make_async_copy(rows_all.at[pl.ds(0, both), :], rows_ref, out_sems.at[2 * len(cuts)])
    ]
    lane = lax.broadcasted_iota(jnp.int32, (1, tile), 1)
    for n, cut in enumerate(cuts):
        for copy in tile_copies[n]:
            copy.wait()
        for copy in tile_copies[n + ahead] if n + ahead < len(cuts) else ():
            copy.start()
        size = min(tile, ff - cut.start)
        if n == 0:
            mine = [dot(rows_all[share:, :], low_all[m, :, cut]) for m in range(2)]
            other_copy.wait_recv()
            out_copies[0].start()
            others = [dot(rows_all[:share, :], low_all[m, :, cut]) for m in range(2)]
            pre = [jnp.concatenate([others[m], mine[m]], axis=0) for m in range(2)]
        else:
            pre = [dot(rows_all[...], low_all[m, :, cut]) for m in range(2)]
        if first:
            for m in range(2):
                rows = slice(both + m * rank, both + (m + 1) * rank)
                across_ref[m, :, cut.start : cut.start + size] = pre[m][rows, :size]
        magnitude, squares, scale = [], [], []
        for m in range(2):
            given = magnitude_ref[m : m + 1, cut.start : cut.start + size]
            if size < tile:
                given = jnp.concatenate([given, jnp.zeros((1, tile - size), F32)], axis=1)
            magnitude.append(given)
            squares.append(squares_ref[m, :, cut])
            scale.append(given / jnp.sqrt(squares[m]))
        sums = [jnp.zeros((1, tile), F32) for _ in range(2)]
        at = [slice(m * width + cut.start, m * width + cut.stop) for m in range(2)]
        for place in range(CORES):
            rows = slice(place * share, (place + 1) * share)
            gate_pre, up_pre = pre[0][rows], pre[1][rows]
            gate, up = gate_pre * scale[0], up_pre * scale[1]
            sigmoid = 0.5 + 0.5 * jnp.tanh(0.5 * gate)
            active = gate * sigmoid
            product_all[rows, cut] = (active * up).astype(LOW)
            upper = grad_all[place, :, cut].astype(F32)
            grad_up = upper * active
            grad_gate = upper * up * sigmoid * (1.0 + gate * (1.0 - sigmoid))
            sums[0] += jnp.sum(grad_gate * gate_pre, axis=0, keepdims=True)
            sums[1] += jnp.sum(grad_up * up_pre, axis=0, keepdims=True)
            back_all[rows, at[0]] = (grad_gate * scale[0]).astype(LOW)
            back_all[rows, at[1]] = (grad_up * scale[1]).astype(LOW)
        for m in range(2):
            total_ref[m, :, cut] = sums[m]
        if last:
            rank = extra_ref.shape[1]
            for m in range(2):
                total = sums[m]
                for ref in before:
                    total = total + ref[m, :, cut]
                right = right_ref[m, :, cut.start : cut.start + size]
                if size < tile:
                    spare = jnp.zeros((rank, tile - size), F32)
                    right = jnp.concatenate([right, spare], axis=1)
                weighted = right * norm_weight(total, squares[m], magnitude[m])
                rows = slice(both + m * rank, both + (m + 1) * rank)
                back_all[rows, at[m]] = weighted.astype(LOW)
                back_all[rows, at[1 - m]] = jnp.zeros((rank, tile), LOW)
    for m in range(2):
        lanes = pl.ds(m * width, width)
        copy = pltpu.make_async_copy(
            back_all.at[pl.ds(0, both), lanes], back_ref.at[m], out_sems.at[m]
        )
        copy.start()
        out_copies.append(copy)
    copy = pltpu.make_async_copy(product_all, product_ref, out_sems.at[2])
    copy.start()
    out_copies.append(copy)
    chunk = sent.shape[2]
    copies = [
        remote(sent.at[n], got.at[n], send_sems.at[n], recv_sems.at[n], sibling)
        for n in range(depth // chunk)
    ]

    def add(n):
        columns = slice(n * chunk, (n + 1) * chunk)
        copies[n].wait_recv()
        total = joined_ref[:, columns].astype(F32) + got[n].astype(F32)
        joined_ref[:, columns] = total.astype(LOW)

    for n in range(depth // chunk):
        columns = slice(n * chunk, (n + 1) * chunk)
        result = dot(back_all[:, :width], low_all[0, columns, :], NT)
        result = result + dot(back_all[:, width:], low_all[1, columns, :], NT)
        sent[n] = result[:share].astype(LOW)
        joined_ref[:, columns] = result[share:both].astype(LOW)
        copies[n].start()
        if n > 0:
            add(n - 1)
        if last:
            for m in range(2):
                extra_ref[m, :, columns] = result[both + m * rank : both + (m + 1) * rank]
    add(len(copies) - 1)
    for copy in out_copies:
        copy.wait()
    for copy in [other_copy, *copies]:
        copy.wait_send()


def expand(identity, mine, low, squares, magnitude, grad_product, step, left=None, right=None, before=()):
    share, depth = mine.shape
    width = low.shape[2]
    first, last = left is not None, right is not None
    rows = CORES * share
    hbm = pl.BlockSpec(memory_space=pl.ANY)
    fixed = lambda dims: pl.BlockSpec(tuple(dims), lambda i: (0,) * len(dims))
    operands = [mine, low, grad_product, squares, magnitude]
    in_specs = [hbm, hbm, hbm, fixed(squares.shape), fixed(magnitude.shape)]
    out_shape = [
        shape((rows, width), LOW),
        shape((2, rows, width), LOW),
        shape((rows, depth), LOW),
        shape((2, 1, width), F32),
        shape((share, depth), LOW),
    ]
    out_specs = [hbm, hbm, hbm] + [fixed(v.shape) for v in out_shape[3:]]
    extra_in = extra_out = 0
    if first:
        rank = left.shape[1]
        extra_in = 2 * rank
        operands.append(left)
        in_specs.append(fixed(left.shape))
        out_shape.append(shape((2, rank, magnitude.shape[1]), F32))
        out_specs.append(fixed(out_shape[-1].shape))
    if last:
        rank = right.shape[1]
        extra_out = 2 * rank
        operands += [right, *before]
        in_specs += [fixed(v.shape) for v in (right, *before)]
        out_shape.append(shape((2, rank, depth), F32))
        out_specs.append(fixed(out_shape[-1].shape))
    tiles, chunk = width // 256, tile_of(depth, 256)
    return call(
        "expand",
        functools.partial(expand_kernel, step, first, last, len(before)),
        tuple(operands),
        (1,),
        in_specs,
        out_specs,
        out_shape,
        scratch=[
            pltpu.VMEM((rows + extra_in, depth), LOW),
            pltpu.VMEM(low.shape, LOW),
            pltpu.VMEM((CORES, share, width), LOW),
            pltpu.VMEM((rows, width), LOW),
            pltpu.VMEM((rows + extra_out, 2 * width), LOW),
            pltpu.VMEM((depth // chunk, share, chunk), LOW),
            pltpu.VMEM((depth // chunk, share, chunk), LOW),
            pltpu.SemaphoreType.DMA((2 + 2 * tiles,)),
            pltpu.SemaphoreType.DMA((2 * tiles + 1,)),
            pltpu.SemaphoreType.DMA((depth // chunk + 1,)),
            pltpu.SemaphoreType.DMA((depth // chunk + 1,)),
        ],
        flops=8 * rows * depth * width,
        identity=identity,
    )


def adapter_kernel(plan, n_inputs, n_grads, corrections, n_before, order_ref, *refs):
    for _ in adapter_steps(plan, n_inputs, n_grads, corrections, n_before, order_ref, *refs):
        pass


def adapter_steps(plan, n_inputs, n_grads, corrections, n_before, order_ref, *refs):
    count = n_inputs + n_grads
    sources, held, sems = refs[:count], refs[-count - 1 : -1], refs[-1]
    left_ref, right_ref = refs[count : count + 2]
    *corrected, left_out, right_out = refs[count + 2 : -count - 1]
    members, rank, width = right_ref.shape
    chunks = list(plan(order_ref, held[:n_inputs], held[n_inputs:]))
    copies, used = [], 0
    for parts, _, _ in chunks:
        copies.append([])
        for which, index in parts:
            copy = pltpu.make_async_copy(
                sources[which].at[index], held[which].at[index], sems.at[used]
            )
            copy.start()
            copies[-1].append(copy)
            used += 1
    yield
    left_rows = jnp.concatenate([split_rows(left_ref[m]) for m in range(members)], axis=0)
    right_rows = [split_rows(right_ref[m]) for m in range(members)]
    before, corrected = corrected[:n_before], corrected[n_before:]
    for out, ref in zip((left_out, right_out), before or (None, None)):
        out[...] = jnp.zeros_like(out) if ref is None else ref[...]
    for waits, (_, taken_of, grads_of) in zip(copies, chunks):
        for copy in waits:
            copy.wait()
        taken = taken_of()
        across = dot(left_rows, taken, NT)
        downs = []
        for m in range(members):
            grad = grads_of(m)
            mine = split_rows(fold(across[2 * rank * m : 2 * rank * (m + 1)]))
            right_out[m] += fold(dot(mine, grad))
            downs.append(split_rows(fold(dot(right_rows[m], grad, NT))))
        left = dot(jnp.concatenate(downs, axis=0), taken)
        for m in range(members):
            left_out[m] += fold(left[2 * rank * m : 2 * rank * (m + 1)])
        yield
    if corrections:
        correct(corrections, right_ref, left_out, right_out, left_out, right_out, *corrected)


def correct(n_totals, right_ref, left_in, right_in, left_out, right_out, *refs):
    back_ref, across_ref, squares_ref, magnitude_ref = refs[:4]
    totals, magnitude_out = refs[4 : 4 + n_totals], refs[4 + n_totals]
    members, rank, width = right_ref.shape
    total = sum_refs(totals)[:, :, :width]
    squares = squares_ref[:, :, :width]
    magnitude_out[...] = total / jnp.sqrt(squares)
    for m in range(members):
        weight = norm_weight(total[m], squares[m], magnitude_ref[m : m + 1])
        if back_ref.dtype == LOW:
            low = back_ref[m, : left_in.shape[2], :]
            back = fold(dot(split_rows(right_ref[m] * weight), low, NT))
        else:
            back = back_ref[m]
        left_out[m] = ADAPT_SCALE * (left_in[m] - back)
        right_out[m] = ADAPT_SCALE * (right_in[m] - across_ref[m][:, :width] * weight)


def adapter_parts(inputs, grads, left, right, correction, before):
    members, rank, width = right.shape
    moved, fixed, n_totals = [*inputs, *grads], [left, right, *before], 0
    outs = [(members, rank, left.shape[2]), (members, rank, width)]
    if correction is not None:
        *given, totals = correction
        n_totals = len(totals)
        fixed += [*given, *totals]
        outs = [(members, 1, width)] + outs
    scratch = [pltpu.VMEM(v.shape, v.dtype) for v in moved] + [pltpu.SemaphoreType.DMA((32,))]
    return moved, fixed, outs, scratch, (len(inputs), len(grads), n_totals, len(before))


def adapter(name, order, plan, inputs, grads, left, right, correction=None, before=(), other=None):
    moved, fixed, outs, scratch, counts = adapter_parts(inputs, grads, left, right, correction, before)
    kernel = functools.partial(adapter_kernel, plan, *counts)
    full = lambda dims: pl.BlockSpec(tuple(dims), lambda i, o: (0,) * len(dims))
    n_moved, n_fixed, n_outs = len(moved), len(fixed), len(outs)
    if other is not None:
        sums, other_right, (low, across, squares, magnitude, totals) = other
        moved = moved + [low]
        fixed = fixed + [other_right, *sums, across, squares, magnitude, *totals]
        outs = outs + [(1, 1, other_right.shape[2]), sums[0].shape, sums[1].shape]
        scratch = scratch + [pltpu.VMEM(low.shape, LOW), pltpu.SemaphoreType.DMA(())]

    def run(order_ref, *refs):
        if other is None:
            kernel(order_ref, *refs)
            return
        refs = list(refs)
        low_held, low_sem = refs[-2:]
        low_copy = pltpu.make_async_copy(refs[n_moved], low_held, low_sem)
        ends = [n_moved + 1, n_moved + 1 + len(fixed), n_moved + 1 + len(fixed) + len(outs)]
        fixed_refs, out_refs = refs[ends[0] : ends[1]], refs[ends[1] : ends[2]]
        steps = adapter_steps(
            plan,
            *counts,
            order_ref,
            *refs[:n_moved],
            *fixed_refs[:n_fixed],
            *out_refs[:n_outs],
            *refs[ends[2] : -2],
        )
        next(steps)
        low_copy.start()
        for _ in steps:
            pass
        low_copy.wait()
        right_ref, left_in, right_in, across_ref, squares_ref, magnitude_ref, *totals_refs = (
            fixed_refs[n_fixed:]
        )
        magnitude_out, left_out, right_out = out_refs[n_outs:]
        correct(
            len(totals_refs),
            right_ref,
            left_in,
            right_in,
            left_out,
            right_out,
            low_held,
            across_ref,
            squares_ref,
            magnitude_ref,
            *totals_refs,
            magnitude_out,
        )

    return call(
        name,
        run,
        (*moved, *fixed),
        (1,),
        [pl.BlockSpec(memory_space=pl.ANY) for _ in moved] + [full(v.shape) for v in fixed],
        [full(dims) for dims in outs],
        [shape(dims, F32) for dims in outs],
        scratch=scratch,
        prefetch=(order,),
        flops=sum(v.size for v in moved) * 64,
    )


def copy_kernel(count, *refs):
    for source, target in zip(refs[:count], refs[count:]):
        if len(target.shape) < len(source.shape):
            for m in range(source.shape[0]):
                target[m : m + 1, :] = source[m]
        else:
            target[...] = source[...]


def copy_out(arrays):
    full = lambda v: pl.BlockSpec(v.shape, lambda i: (0,) * len(v.shape))
    flat = lambda v: v.shape[:1] + v.shape[2:] if v.ndim == 3 and v.shape[1] == 1 else v.shape
    out_shape = [shape(flat(v), F32) for v in arrays]
    return call(
        "copy_out",
        functools.partial(copy_kernel, len(arrays)),
        tuple(arrays),
        (1,),
        [full(v) for v in arrays],
        [full(v) for v in out_shape],
        out_shape,
    )


GRAIN = 16


def pieces_of(width):
    return [(at, min(128, width - at)) for at in range(0, width, 128)]


def cells_of(blocks, lines, parts):
    cells, rows = [], []
    for n, block in enumerate(blocks):
        for m in range(block.shape[0]):
            for at, size in pieces_of(block.shape[2] // parts):
                cells.append((n, m, at, size))
    for n, line in enumerate(lines):
        for m in range(line.shape[0]):
            for at, size in pieces_of(line.shape[2] // parts):
                rows.append((n, m, at, size))
    return cells, rows


def pack(blocks, lines, wide_ref, part, parts, cells, rows):
    for i, (n, m, at, size) in enumerate(cells):
        start = part * (blocks[n].shape[2] // parts) + at
        wide_ref[part, i, :, :size] = blocks[n][m, :, start : start + size]
    for i, (n, m, at, size) in enumerate(rows):
        start = part * (lines[n].shape[2] // parts) + at
        cell, row = len(cells) + i // GRAIN, i % GRAIN
        wide_ref[part, cell, row : row + 1, :size] = lines[n][m, :, start : start + size]


def unpack(full_ref, blocks, lines, part, parts, cells, rows):
    for i, (n, m, at, size) in enumerate(cells):
        start = part * (blocks[n].shape[2] // parts) + at
        blocks[n][m, :, start : start + size] = full_ref[part, i].astype(F32)[:, :size]
    for i, (n, m, at, size) in enumerate(rows):
        start = part * (lines[n].shape[2] // parts) + at
        cell, row = len(cells) + i // GRAIN, i % GRAIN
        values = full_ref[part, cell].astype(F32)
        lines[n][m, :, start : start + size] = values[row : row + 1, :size]


def reduce_steps(groups, lines, counts, *refs):
    n_all, n_all_lines, n_dp, n_dp_lines = counts
    count = sum(counts)
    taken, given, scratch = refs[:count], refs[count : 2 * count], refs[2 * count :]
    ends = [n_all, n_all + n_all_lines, n_all + n_all_lines + n_dp]
    parted = lambda v: (v[: ends[0]], v[ends[0] : ends[1]], v[ends[1] : ends[2]], v[ends[2] :])
    all_out, all_lines_out, dp_out, dp_lines_out = parted(given)
    (
        all_ref,
        line_ref,
        all_low,
        line_low,
        all_got,
        part,
        part_low,
        part_got,
        line_got,
        all_full,
        line_full,
        *sems,
    ) = scratch
    held, in_sems, sems = sems[:count], sems[count], sems[count + 1 :]
    loads = [
        pltpu.make_async_copy(source, target, in_sems.at[i])
        for i, (source, target) in enumerate(zip(taken, held))
    ]
    for load in loads:
        load.start()
    me, row = lax.axis_index("mp"), lax.axis_index("dp")
    piece, line_piece = part.shape[0] // lines, line_ref.shape[1] // lines
    mp_peer = [lax.rem(me + k, groups) for k in range(groups)]
    dp_peer = [lax.rem(row + k, lines) for k in range(lines)]
    barrier = pltpu.get_barrier_semaphore()
    for k in range(1, groups):
        pl.semaphore_signal(barrier, 1, device_id={"mp": mp_peer[k]}, device_id_type=MESH_IDS)
    for k in range(1, lines):
        pl.semaphore_signal(barrier, 1, device_id={"dp": dp_peer[k]}, device_id_type=MESH_IDS)
    all_in, all_lines_in, dp_in, dp_lines_in = parted(held)
    all_cells = cells_of(all_in, all_lines_in, groups)
    dp_cells = cells_of(dp_in, dp_lines_in, 1)
    all_ref[...] = jnp.zeros_like(all_ref)
    line_ref[...] = jnp.zeros_like(line_ref)
    for load in loads:
        load.wait()
    for q in range(groups):
        pack(all_in, all_lines_in, all_ref, q, groups, *all_cells)
    pack(dp_in, dp_lines_in, line_ref, 0, 1, *dp_cells)
    all_low[...] = all_ref[...].astype(LOW)
    line_low[...] = line_ref[...].astype(LOW)
    pl.semaphore_wait(barrier, groups + lines - 2)

    def send(source, target, stage, k, axis, peer):
        copy = pltpu.make_async_remote_copy(
            src_ref=source,
            dst_ref=target,
            send_sem=sems[2 * stage].at[k],
            recv_sem=sems[2 * stage + 1].at[k],
            device_id={axis: peer},
            device_id_type=MESH_IDS,
        )
        copy.start()
        return copy

    over_mp = [
        send(all_low.at[mp_peer[k]], all_got.at[k], 0, k, "mp", mp_peer[k])
        for k in range(1, groups)
    ]
    over_dp = [
        send(
            line_low.at[0, pl.ds(dp_peer[k] * line_piece, line_piece)],
            line_got.at[k],
            1,
            k,
            "dp",
            dp_peer[k],
        )
        for k in range(1, lines)
    ]
    yield
    total = all_ref[me]
    for k, copy in enumerate(over_mp, 1):
        copy.wait_recv()
        total = total + all_got[k].astype(F32)
    part[...] = total
    part_low[...] = total.astype(LOW)
    part_dp = [
        send(part_low.at[pl.ds(dp_peer[k] * piece, piece)], part_got.at[k], 2, k, "dp", dp_peer[k])
        for k in range(1, lines)
    ]
    yield
    held = pl.ds(row * piece, piece)
    total = part[held]
    for k, copy in enumerate(part_dp, 1):
        copy.wait_recv()
        total = total + part_got[k].astype(F32)
    all_full[me, held] = total.astype(LOW)
    part_back = [
        send(all_full.at[me, held], all_full.at[me, held], 4, k, "dp", dp_peer[k])
        for k in range(1, lines)
    ]
    mine = pl.ds(row * line_piece, line_piece)
    total = line_ref[0, mine]
    for k, copy in enumerate(over_dp, 1):
        copy.wait_recv()
        total = total + line_got[k].astype(F32)
    line_full[0, mine] = total.astype(LOW)
    line_back = [
        send(line_full.at[0, mine], line_full.at[0, mine], 3, k, "dp", dp_peer[k])
        for k in range(1, lines)
    ]
    yield
    for copy in part_back:
        copy.wait_recv()
    all_back = [
        send(all_full.at[me], all_full.at[me], 5, k, "mp", mp_peer[k]) for k in range(1, groups)
    ]
    yield
    for copy in line_back:
        copy.wait_recv()
    unpack(line_full, dp_out, dp_lines_out, 0, 1, *dp_cells)
    for copy in all_back:
        copy.wait_recv()
    for q in range(groups):
        unpack(all_full, all_out, all_lines_out, q, groups, *all_cells)
    for copy in over_mp + over_dp + part_dp + line_back + part_back + all_back:
        copy.wait_send()


def reduce_devices(name, identity, over_all, over_all_lines, over_dp, over_dp_lines, job):
    groups, lines = lax.axis_size("mp"), lax.axis_size("dp")

    def size_of(blocks, rows, parts):
        cells, lines_in = cells_of(blocks, rows, parts)
        size = len(cells) + -(-len(lines_in) // GRAIN)
        return -(-size // lines) * lines

    count, line_count = size_of(over_all, over_all_lines, groups), size_of(over_dp, over_dp_lines, 1)
    operands = [*over_all, *over_all_lines, *over_dp, *over_dp_lines]
    counts = (len(over_all), len(over_all_lines), len(over_dp), len(over_dp_lines))
    tail = (GRAIN, 128)
    sizes = (groups, lines, lines, lines, lines, groups)
    every, line = (groups, count) + tail, (1, line_count) + tail
    scratch = (
        [
            pltpu.VMEM(every, F32),
            pltpu.VMEM(line, F32),
            pltpu.VMEM(every, LOW),
            pltpu.VMEM(line, LOW),
            pltpu.VMEM(every, LOW),
            pltpu.VMEM((count,) + tail, F32),
            pltpu.VMEM((count,) + tail, LOW),
            pltpu.VMEM((lines, count // lines) + tail, LOW),
            pltpu.VMEM((lines, line_count // lines) + tail, LOW),
            pltpu.VMEM(every, LOW),
            pltpu.VMEM(line, LOW),
        ]
        + [pltpu.VMEM(v.shape, F32) for v in operands]
        + [pltpu.SemaphoreType.DMA((len(operands),))]
        + [pltpu.SemaphoreType.DMA((n,)) for n in sizes for _ in range(2)]
    )
    job_steps, moved, whole_rows, job_shape, job_scratch = job
    n_operands, n_scratch = len(operands), len(scratch)
    out_shape = [shape(v.shape, F32) for v in operands] + [job_shape]
    anywhere = pl.BlockSpec(memory_space=pl.ANY)
    full = lambda v: pl.BlockSpec(v.shape, lambda i: (0,) * v.ndim)
    operands = operands + [*moved, *whole_rows]

    def run(*refs):
        given, refs = refs[: len(operands)], refs[len(operands) :]
        results, held = refs[: len(out_shape)], refs[len(out_shape) :]
        steps = reduce_steps(
            groups, lines, counts, *given[:n_operands], *results[:n_operands], *held[:n_scratch]
        )
        work = job_steps(*given[n_operands:], results[n_operands], *held[n_scratch:])
        next(work)
        for _ in steps:
            next(work, None)
        for _ in work:
            pass

    return call(
        name,
        run,
        tuple(operands),
        (1,),
        [anywhere] * (n_operands + len(moved)) + [full(v) for v in whole_rows],
        [full(v) for v in out_shape[:-1]] + [anywhere],
        out_shape,
        scratch=scratch + job_scratch,
        flops=1000,
        identity=identity,
    )


def token_job(tokens, grad_hidden, parts, gain):
    share, width = grad_hidden.shape
    moved = [tokens, grad_hidden, *parts]

    def steps(*refs):
        sources, gain_ref, out_ref = refs[: len(moved)], refs[len(moved)], refs[len(moved) + 1]
        *held, result, sems = refs[len(moved) + 2 :]
        row = pl.multiple_of(lax.axis_index("mp") * share, share)
        copies = []
        for n, (source, target) in enumerate(zip(sources, held)):
            source = source.at[pl.ds(row, share), :] if n == 0 else source
            copies.append(pltpu.make_async_copy(source, target, sems.at[n]))
            copies[-1].start()
        yield
        for copy in copies:
            copy.wait()
        tile = 32
        gain = gain_ref[...]

        def some(i, carry):
            at = pl.ds(pl.multiple_of(i * tile, tile), tile)
            token, grad, *rest = [ref[at, :].astype(F32) for ref in held]
            result[at, :] = grad + norm_back(sum_of(rest), token, gain)[0]
            return carry

        lax.fori_loop(0, share // tile, some, 0, unroll=2)
        copy = pltpu.make_async_copy(result, out_ref, sems.at[len(moved)])
        copy.start()
        yield
        yield
        copy.wait()

    scratch = [pltpu.VMEM((share, width), v.dtype) for v in moved]
    scratch += [pltpu.VMEM((share, width), F32), pltpu.SemaphoreType.DMA((len(moved) + 1,))]
    return steps, moved, [gain], shape((share, width), F32), scratch


def body(
    tokens,
    cotangent,
    segment_ids,
    attend_gain,
    expand_gain,
    heads_base,
    heads_left,
    heads_right,
    heads_magnitude,
    output_base,
    output_left,
    output_right,
    output_magnitude,
    expand_base,
    expand_left,
    expand_right,
    expand_magnitude,
    shrink_base,
    shrink_left,
    shrink_right,
    shrink_magnitude,
):
    groups = lax.axis_size("mp")
    chips = groups // CORES
    index = lax.axis_index("mp")
    chip, core = index // CORES, index % CORES
    rows, width = tokens.shape
    share = rows // groups
    local_heads, ff = heads_base.shape[2], expand_base.shape[2]
    ff_wide = padded(ff)
    device = jnp.arange(groups, dtype=jnp.int32)
    order = jnp.concatenate(
        [
            (chip + device // CORES) % chips * CORES + (core + 1 + device) % CORES,
            (device // CORES + chips - chip) % chips * CORES + (device + CORES - core + 1) % CORES,
        ]
    ).astype(jnp.int32)

    def tie(*values):
        return lax.optimization_barrier(values)

    def sibling(values):
        return lax.ppermute(
            values, "mp", [(i, i // CORES * CORES + (i + 1) % CORES) for i in range(groups)]
        )

    def to_chip(values, step):
        return lax.ppermute(
            values,
            "mp",
            [((i, ((i // CORES + step) % chips) * CORES + i % CORES)) for i in range(groups)],
        )

    def join(pair):
        return (pair[1].astype(F32) + sibling(pair[0]).astype(F32)).astype(LOW)

    def chip_pairs(places):
        return [places[CORES * step : CORES * (step + 1)] for step in range(chips)]

    def arrive(own):
        return [to_chip(own, chips - step) for step in range(1, chips)]

    def pairs_of(own, near_sibling, arrived):
        return [(near_sibling, own)] + [(sibling(piece), piece) for piece in arrived]

    def in_pairs(order_ref, inputs, grads):
        for step, (taken, grad) in enumerate(zip(inputs, grads)):
            yield (
                [(step, ...), (chips + step, ...)],
                lambda taken=taken: taken[...],
                lambda m, grad=grad: grad[m, :, :ff],
            )

    def in_shrink(order_ref, inputs, grads):
        for step, taken in enumerate(inputs):
            at = slice(CORES * step, CORES * (step + 1))
            yield (
                [(step, ...), (chips, pl.ds(CORES * step, CORES))],
                lambda taken=taken: taken[:, :ff],
                lambda m, at=at: grads[0][at].reshape(-1, grads[0].shape[-1]),
            )

    def in_output(start):
        def plan(order_ref, inputs, grads):
            for n, grad in enumerate(grads):
                yield (
                    [(0, (0, start + n)), (1 + n, ...)],
                    lambda place=start + n: inputs[0][0, place],
                    lambda m, grad=grad: grad[...],
                )

        return plan

    def in_heads(order_ref, inputs, grads):
        for place in range(groups):
            step, side = place // CORES, place % CORES
            me = lax.axis_index("mp")
            group = lax.rem(me // CORES + step, chips) * CORES + lax.rem(me + 1 + side, CORES)
            at = pl.multiple_of(group * share, share)
            rows = pl.ds(place * share, share)
            yield (
                [(0, pl.ds(at, share)), (1, (slice(None), rows))],
                lambda at=at: inputs[0][pl.ds(at, share), :],
                lambda m, rows=rows: grads[0][m, rows, :],
            )

    heads_rows, output_rows = turned(heads_left), turned(output_left[None])
    expand_rows, shrink_rows = turned(expand_left), turned(shrink_left[None])
    heads_mag, output_mag = heads_magnitude, output_magnitude[None]
    expand_mag, shrink_mag = expand_magnitude, shrink_magnitude[None]
    attend_line, expand_line = attend_gain[None], expand_gain[None]

    output_low, shrink_low, squares_part = merge_pair(
        [(output_base, output_rows[0], output_right), (shrink_base, shrink_rows[0], shrink_right)]
    )
    output_low, shrink_low = output_low[None], shrink_low[None]
    (
        normed,
        heads_low,
        post,
        heads_sq,
        heads_across,
        cos_table,
        sine_table,
        output_sq,
        shrink_sq,
        first,
    ) = project_heads(
        tokens,
        attend_line,
        heads_base,
        heads_rows,
        heads_right,
        heads_mag,
        segment_ids,
        squares_part,
        groups,
    )
    heads_out = attend(order, groups, post, first)
    heads_parts = heads_out.reshape(1, groups, share, local_heads)
    joined, output_across = product(
        "output_product", 3, heads_parts, output_low, NN, left=output_rows
    )
    joined, expand_right_tied = tie(joined, expand_right)
    output_parts = [joined[0]] + [to_chip(joined[step], step) for step in range(1, chips)]
    expand_low, expand_sq = merge(
        expand_base, expand_rows, expand_right_tied, 1024, expand_base.shape[2]
    )
    grad_product, shrink_grad = shrink_back(
        order, cotangent, shrink_low, shrink_sq, shrink_mag[None], groups
    )
    output_parts, expand_low, grad_product = tie(output_parts, expand_low, grad_product)
    hidden, normed_own = row_call(
        "hidden",
        hidden_kernel,
        order,
        [(tokens, True)] + [(part, False) for part in output_parts],
        (output_sq[0], output_mag, expand_line),
        (F32, LOW),
        0,
        scale_first,
    )

    def feed(mine, step, **extra):
        return expand(
            4 + step, mine, expand_low, expand_sq, expand_mag, grad_product, step, **extra
        )

    arrived = arrive(normed_own)
    fed = [feed(normed_own, 0, left=expand_rows)]
    arrived, fed = tie(arrived, fed)
    fed = list(fed)
    for step in range(1, chips):
        extra = {}
        if step == chips - 1:
            extra = {"right": expand_right, "before": [f[3] for f in fed]}
        fed.append(feed(arrived[step - 1], step, **extra))
    expand_totals = [f[3] for f in fed]
    joined, shrink_rows_tied = tie([f[4] for f in fed], shrink_rows)
    mid_parts = [joined[0]] + [to_chip(joined[step], step) for step in range(1, chips)]
    shrink_places, shrink_total, shrink_across = shrink_product(
        order, [f[0] for f in fed], shrink_low, shrink_rows_tied, cotangent
    )
    shrink_pairs = chip_pairs(shrink_places)
    expand_adapter = adapter(
        "expand_adapter",
        order,
        in_pairs,
        [f[2] for f in fed],
        [f[1] for f in fed],
        expand_rows,
        expand_right,
        (fed[-1][5], fed[0][5], expand_sq, expand_mag, expand_totals),
    )
    mid_parts, shrink_pairs, expand_adapter = tie(mid_parts, shrink_pairs, expand_adapter)
    grad_hidden, output_grad_own, output_total, expand_gain_part = row_call(
        "hidden_back",
        hidden_back_kernel,
        order,
        [(cotangent, True), (tokens, True), (hidden, False)]
        + [(part, False) for part in mid_parts],
        (output_sq[0], output_mag, expand_line),
        (F32, LOW),
        2,
        scale_first,
    )
    arrived, near_sibling = arrive(output_grad_own), sibling(output_grad_own)
    shrink_joined = [join(pair) for pair in shrink_pairs[1:]]
    shrink_joined, shrink_rows_tied = tie(shrink_joined, shrink_rows)
    shrink_sums = adapter(
        "shrink_adapter",
        order,
        in_shrink,
        [f[0] for f in fed],
        [shrink_grad],
        shrink_rows_tied,
        shrink_right[None],
    )
    output_sums = adapter(
        "output_near_adapter",
        order,
        in_output(0),
        [heads_parts],
        [near_sibling, output_grad_own],
        output_rows,
        output_right[None],
    )
    arrived, near_sibling, shrink_joined, shrink_sums, output_sums = tie(
        arrived, near_sibling, shrink_joined, shrink_sums, output_sums
    )
    output_grad = [
        piece for pair in pairs_of(output_grad_own, near_sibling, arrived) for piece in pair
    ]
    shrink_parts = [shrink_pairs[0][1], sibling(shrink_pairs[0][0])] + [
        to_chip(values, step) for step, values in enumerate(shrink_joined, 1)
    ]
    heads_grads, heads_total = attend_back(
        order,
        groups,
        post,
        first,
        cos_table,
        sine_table,
        heads_mag,
        heads_sq,
        output_low,
        output_grad,
    )
    grad_parts = heads_grads.reshape(3, groups, share, local_heads)
    joined, output_total, shrink_total, attend_gain_part, token_extra = product(
        "normed_product",
        20,
        grad_parts,
        heads_low,
        NT,
        correction=(heads_right, heads_sq, heads_mag, [heads_total]),
        lines=(output_total, shrink_total),
        gain=(normed, attend_line),
    )
    joined, shrink_parts, heads_rows_tied, output_rows_tied = tie(
        joined, shrink_parts, heads_rows, output_rows
    )
    token_parts = [joined[0]] + [to_chip(joined[step], step) for step in range(1, chips)]
    output_mag_part, output_left_part, output_right_part, *shrink_adapter = adapter(
        "output_far_adapter",
        order,
        in_output(CORES),
        [heads_parts],
        output_grad[CORES:],
        output_rows_tied,
        output_right[None],
        (output_low, output_across, output_sq, output_mag, [output_total]),
        output_sums,
        (
            shrink_sums,
            shrink_right[None],
            (shrink_low, shrink_across, shrink_sq, shrink_mag, [shrink_total]),
        ),
    )
    heads_adapter = adapter(
        "heads_adapter",
        order,
        in_heads,
        [normed],
        [heads_grads],
        heads_rows_tied,
        heads_right,
        (token_extra, heads_across, heads_sq, heads_mag, [heads_total]),
    )
    (mixed,) = row_call(
        "mixed",
        mixed_kernel,
        order,
        [(hidden, False)] + [(part, False) for part in shrink_parts],
        (shrink_sq[0], shrink_mag),
        (LOW,),
        0,
        scale_first,
    )
    token_parts, heads_adapter, mixed = tie(token_parts, heads_adapter, mixed)
    *reduced, grad_tokens = reduce_devices(
        "reduce_gradients",
        1,
        [expand_adapter[1], shrink_adapter[2], output_right_part, heads_adapter[1]],
        [expand_gain_part[None], attend_gain_part[None]],
        [expand_adapter[2], shrink_adapter[1], output_left_part, heads_adapter[2]],
        [expand_adapter[0], shrink_adapter[0], output_mag_part, heads_adapter[0]],
        token_job(tokens, grad_hidden, token_parts, attend_line),
    )
    (
        expand_left_grad,
        shrink_right_grad,
        output_right_grad,
        heads_left_grad,
        expand_gain_grad,
        attend_gain_grad,
        expand_right_grad,
        shrink_left_grad,
        output_left_grad,
        heads_right_grad,
        expand_mag_grad,
        shrink_mag_grad,
        output_mag_grad,
        heads_mag_grad,
        grad_tokens,
    ) = copy_out([*reduced, grad_tokens])
    return (
        mixed,
        grad_tokens,
        attend_gain_grad[0],
        expand_gain_grad[0],
        jnp.swapaxes(heads_left_grad, 1, 2),
        heads_right_grad,
        heads_mag_grad,
        output_left_grad[0].T,
        output_right_grad[0],
        output_mag_grad[0],
        jnp.swapaxes(expand_left_grad, 1, 2),
        expand_right_grad,
        expand_mag_grad,
        shrink_left_grad[0].T,
        shrink_right_grad[0],
        shrink_mag_grad[0],
    )


def solution(mesh):
    placed = (
        P("dp", None),
        P("dp", None),
        P("dp", None),
        P(),
        P(),
        P(None, None, "mp"),
        P(),
        P(None, None, "mp"),
        P(None, "mp"),
        P("mp", None),
        P("mp", None),
        P(),
        P(),
        P(None, None, "mp"),
        P(),
        P(None, None, "mp"),
        P(None, "mp"),
        P("mp", None),
        P("mp", None),
        P(),
        P(),
    )
    return jax.shard_map(
        body,
        mesh=mesh,
        in_specs=placed,
        out_specs=(
            P(("dp", "mp"), None),
            P(("dp", "mp"), None),
            P(),
            P(),
            P(),
            P(None, None, "mp"),
            P(None, "mp"),
            P("mp", None),
            P(),
            P(),
            P(),
            P(None, None, "mp"),
            P(None, "mp"),
            P("mp", None),
            P(),
            P(),
        ),
        check_vma=False,
    )
```

```python
import functools

import jax
import jax.numpy as jnp
import ml_dtypes
import numpy as np
from jax import lax
from jax.experimental import pallas as pl
from jax.experimental.pallas import tpu as pltpu
from jax.sharding import PartitionSpec as P

HEAD_DIM = 128
CORES = 2
LONGEST = 512
ATTEND_BLOCK = 256
ADAPT_SCALE = 2.0
NORM_EPS = 1e-05
ROPE_BASE = 10000.0
MASKED = -1e30

F32 = jnp.float32
LOW = jnp.bfloat16
NN = (((1,), (0,)), ((), ()))
NT = (((1,), (1,)), ((), ()))
TN = (((0,), (0,)), ((), ()))


MESH_IDS = pl.DeviceIdType.MESH


def sibling_id():
    me = lax.axis_index("mp")
    return me // CORES * CORES + lax.rem(me + 1, CORES)


def greet(peers):
    for peer in peers:
        pl.semaphore_signal(
            pltpu.get_barrier_semaphore(), 1, device_id={"mp": peer}, device_id_type=MESH_IDS
        )


def greeted(count):
    pl.semaphore_wait(pltpu.get_barrier_semaphore(), count)


def remote(source, target, send_sem, recv_sem, peer):
    return pltpu.make_async_remote_copy(
        src_ref=source,
        dst_ref=target,
        send_sem=send_sem,
        recv_sem=recv_sem,
        device_id={"mp": peer},
        device_id_type=MESH_IDS,
    )


def dot(left, right, dims=NN):
    return lax.dot_general(left, right, dims, preferred_element_type=F32)


def shape(dims, kind):
    return jax.ShapeDtypeStruct(tuple(dims), kind)


def call(name, kernel, operands, grid, in_specs, out_specs, out_shape, scratch=(), prefetch=(), flops=0, mib=63.5, identity=None):
    moved = sum(v.size * v.dtype.itemsize for v in operands)
    moved += sum(v.size * v.dtype.itemsize for v in out_shape)
    return pl.pallas_call(
        kernel,
        name=name,
        out_shape=out_shape,
        grid_spec=pltpu.PrefetchScalarGridSpec(
            num_scalar_prefetch=len(prefetch),
            grid=grid,
            in_specs=in_specs,
            out_specs=out_specs,
            scratch_shapes=scratch,
        ),
        compiler_params=pltpu.CompilerParams(
            vmem_limit_bytes=int(mib * 2**20), collective_id=identity, has_side_effects=identity is not None
        ),
        cost_estimate=pl.CostEstimate(flops=flops // 16, bytes_accessed=moved // 16, transcendentals=0),
    )(*prefetch, *operands)


def tile_of(size, most):
    return most if size % most == 0 else size


def split_rows(values):
    top = values.astype(LOW)
    rest = (values - top.astype(F32)).astype(LOW)
    return jnp.concatenate([top, rest], axis=0)


def turned(left_map):
    return jnp.swapaxes(left_map, -1, -2)


def norm_weight(total, squares, magnitude):
    norm = jnp.sqrt(squares)
    return total * magnitude / (norm * norm * norm)


def sum_refs(refs):
    total = refs[0][...]
    for ref in refs[1:]:
        total = total + ref[...]
    return total


def fold(values):
    half = values.shape[0] // 2
    return values[:half] + values[half:]


def merge_tile(base_at, low_put, left, right, depth):
    rank = right.shape[0]
    doubled = ADAPT_SCALE * right
    top = doubled.astype(LOW)
    rest = (doubled - top.astype(F32)).astype(LOW)
    right_stack = jnp.concatenate([top, rest, top], axis=0)
    left_pair = split_rows(left)
    left_stack = jnp.concatenate([left_pair[:rank], left_pair[:rank], left_pair[rank:]], axis=0)
    width = right.shape[1]
    wide = 256 if width == 512 else width
    step = tile_of(depth, 1024)
    squares = []
    for at in range(0, width, wide):
        columns = slice(at, at + wide)
        total = jnp.zeros((1, wide), F32)
        for start in range(0, depth, step):
            merged = base_at(start, step, columns).astype(F32) + dot(
                left_stack[:, start : start + step], right_stack[:, columns], TN
            )
            low_put(start, step, columns, merged.astype(LOW))
            total = total + jnp.sum(merged * merged, axis=0, keepdims=True)
        squares.append(total)
    return jnp.concatenate(squares, axis=1)


def merge_pair_kernel(*refs):
    for n in range(2):
        base_ref, left_ref, right_ref = refs[3 * n : 3 * n + 3]
        low_ref, squares_ref = refs[6 + n], refs[8]
        depth = base_ref.shape[0]
        if low_ref.shape[0] > depth:
            low_ref[depth:, :] = jnp.zeros((low_ref.shape[0] - depth, low_ref.shape[1]), LOW)

        def put(start, step, columns, tile, low_ref=low_ref):
            low_ref[start : start + step, columns] = tile

        squares_ref[n : n + 1, :] = merge_tile(
            lambda start, step, columns, base_ref=base_ref: base_ref[start : start + step, columns],
            put,
            left_ref[...],
            right_ref[...],
            depth,
        )


def merge_pair(triples):
    operands, in_specs, low_specs, low_shapes = [], [], [], []
    width = triples[0][0].shape[1]
    wide = tile_of(width, 512)
    for base, left, right in triples:
        depth, rank = base.shape[0], right.shape[0]
        operands += [base, left, right]
        in_specs += [
            pl.BlockSpec((depth, wide), lambda n: (0, n)),
            pl.BlockSpec((rank, depth), lambda n: (0, 0)),
            pl.BlockSpec((rank, wide), lambda n: (0, n)),
        ]
        low_specs.append(pl.BlockSpec((padded(depth), wide), lambda n: (0, n)))
        low_shapes.append(shape((padded(depth), width), LOW))
    return call(
        "merge_pair",
        merge_pair_kernel,
        tuple(operands),
        (width // wide,),
        in_specs,
        low_specs + [pl.BlockSpec((2, wide), lambda n: (0, n))],
        low_shapes + [shape((2, width), F32)],
        flops=2 * sum(v.size for v in operands) * 256,
    )


def merge_kernel(left_ref, right_ref, *refs):
    *bases, low_ref, squares_ref = refs
    part, width = bases[0].shape[1:]
    if low_ref.shape[2] > width:
        spare = low_ref.shape[2] - width
        low_ref[0, :, width:] = jnp.zeros((low_ref.shape[1], spare), LOW)
        squares_ref[0, :, width:] = jnp.ones((1, spare), F32)
    squares = jnp.zeros((1, width), F32)
    for n, base_ref in enumerate(bases):

        def put(start, step, columns, tile, at=n * part):
            low_ref[0, at + start : at + start + step, columns] = tile

        squares = squares + merge_tile(
            lambda start, step, columns, base_ref=base_ref: base_ref[
                0, start : start + step, columns
            ],
            put,
            left_ref[0, :, n * part : (n + 1) * part],
            right_ref[0],
            part,
        )

    @pl.when(pl.program_id(1) == 0)
    def _():
        squares_ref[0, :, :width] = squares

    @pl.when(pl.program_id(1) > 0)
    def _():
        squares_ref[0, :, :width] += squares


def padded(size):
    return -(-size // 256) * 256


def pad_last(values, size):
    return jnp.pad(values, [(0, 0)] * (values.ndim - 1) + [(0, size - values.shape[-1])])


def merge(base, left, right, deep):
    members, depth, width = base.shape
    rank, wide, cuts = right.shape[1], padded(width), 4
    part = lambda n: pl.BlockSpec(
        (1, deep // cuts, width), functools.partial(lambda n, m, k: (m, cuts * k + n, 0), n)
    )
    return call(
        "merge",
        merge_kernel,
        (left, right, *[base] * cuts),
        (members, depth // deep),
        [
            pl.BlockSpec((1, rank, deep), lambda m, k: (m, 0, k)),
            pl.BlockSpec((1, rank, width), lambda m, k: (m, 0, 0)),
        ]
        + [part(n) for n in range(cuts)],
        [
            pl.BlockSpec((1, deep, wide), lambda m, k: (m, k, 0)),
            pl.BlockSpec((1, 1, wide), lambda m, k: (m, 0, 0)),
        ],
        [shape((members, depth, wide), LOW), shape((members, 1, wide), F32)],
        flops=2 * members * depth * width * 256,
    )


def rms_rows(values):
    return lax.rsqrt(jnp.mean(values * values, axis=1, keepdims=True) + NORM_EPS)


TABLE_STEP = 32


def table_pieces(places):
    half = np.arange(HEAD_DIM) % (HEAD_DIM // 2)
    angles = np.asarray(places)[:, None] * ROPE_BASE ** (-2.0 * half / HEAD_DIM)[None, :]
    rest = np.concatenate([np.cos(angles), np.sin(angles)], axis=1)
    pieces = []
    for _ in range(3):
        pieces.append(rest.astype(ml_dtypes.bfloat16))
        rest = rest - pieces[-1].astype(np.float64)
    return jnp.asarray(np.concatenate(pieces, axis=0))


def rotation(first, coarse, fine):
    rows = first.shape[0]
    position = lax.broadcasted_iota(jnp.int32, (rows, 1), 0) - first
    lane = lax.broadcasted_iota(jnp.int32, (rows, 3 * TABLE_STEP), 1) % TABLE_STEP
    pick = lambda place, table: dot((lane == place).astype(F32).astype(LOW), table)
    high = pick(position // TABLE_STEP, coarse)
    small = pick(position % TABLE_STEP, fine)
    cos_a, sin_a = high[:, :HEAD_DIM], high[:, HEAD_DIM:]
    cos_b, sin_b = small[:, :HEAD_DIM], small[:, HEAD_DIM:]
    sine = sin_a * cos_b + cos_a * sin_b
    left_half = lax.broadcasted_iota(jnp.int32, sine.shape, 1) < HEAD_DIM // 2
    return cos_a * cos_b - sin_a * sin_b, jnp.where(left_half, -sine, sine)


def heads_kernel(
    token_ref,
    gain_ref,
    base_ref,
    left_ref,
    right_ref,
    magnitude_ref,
    segment_ref,
    coarse_ref,
    fine_ref,
    part_ref,
    normed_ref,
    low_ref,
    post_ref,
    squares_ref,
    across_ref,
    cos_ref,
    sine_ref,
    output_sum_ref,
    shrink_sum_ref,
    first_ref,
    rows_all,
    part_mine,
    part_got,
    send_sems,
    recv_sems,
):
    total_rows = token_ref.shape[0]
    depth, width = base_ref.shape[1:]
    rank = right_ref.shape[1]
    groups = part_got.shape[0]
    me = lax.axis_index("mp")
    peers = [lax.rem(me + k, groups) for k in range(groups)]
    part_copies = [
        remote(part_mine, part_got.at[k], send_sems.at[k], recv_sems.at[k], peers[k])
        for k in range(1, groups)
    ]

    @pl.when(pl.program_id(0) == 0)
    def _():
        greet(peers[1:])
        part_mine[...] = part_ref[...]
        step = 128

        def some(i, carry):
            at = pl.ds(pl.multiple_of(i * step, step), step)
            values = token_ref[at, :].astype(F32)
            low = (values * rms_rows(values) * gain_ref[...]).astype(LOW)
            normed_ref[at, :] = low
            rows_all[at, :] = low
            return carry

        lax.fori_loop(0, total_rows // step, some, 0)
        ids = segment_ref[...].astype(F32)
        ids_down = jnp.transpose(jnp.broadcast_to(ids, (8, total_rows)))[:, :1]
        for start in range(0, total_rows, 256):
            rows = slice(start, start + 256)
            smaller = jnp.where(ids < ids_down[rows], 1.0, 0.0)
            first = jnp.sum(smaller, axis=1, keepdims=True).astype(jnp.int32)
            first_ref[rows, :] = first
            cosine, sine = rotation(first - start, coarse_ref[...], fine_ref[...])
            cos_ref[rows, :] = cosine
            sine_ref[rows, :] = sine
        greeted(groups - 1)
        for copy in part_copies:
            copy.start()

    @pl.when(pl.program_id(0) == pl.num_programs(0) - 1)
    def _():
        total = part_mine[...]
        for k, copy in enumerate(part_copies, 1):
            copy.wait_recv()
            total = total + part_got[k]
        output_sum_ref[0] = total[:1]
        shrink_sum_ref[0] = total[1:]
        for copy in part_copies:
            copy.wait_send()

    rows_all[total_rows:, :] = left_ref[0].astype(LOW)
    turning = pl.program_id(0) < 2
    wide = 256

    def put(start, step, columns, tile):
        low_ref[0, start : start + step, columns] = tile

    squares_ref[0] = merge_tile(
        lambda start, step, columns: base_ref[0, start : start + step, columns],
        put,
        left_ref[0],
        right_ref[0],
        depth,
    )
    for column in range(0, width, wide):
        columns = slice(column, column + wide)
        magnitude = magnitude_ref[pl.ds(pl.program_id(0), 1), columns]
        scale = magnitude / jnp.sqrt(squares_ref[0, :, columns])
        low = low_ref[0, :, columns]
        step = min(512, total_rows)
        for start in range(0, total_rows, step):
            last = start + step == total_rows
            rows = slice(start, start + step)
            pre = dot(rows_all[start : start + step + (rank if last else 0), :], low)
            if last:
                across_ref[0, :, columns] = pre[step:]
            post = pre[:step] * scale
            cos_table = jnp.where(turning, cos_ref[rows, :], 1.0)
            sine_table = jnp.where(turning, sine_ref[rows, :], 0.0)
            for head in range(0, wide, HEAD_DIM):
                piece = post[:, head : head + HEAD_DIM]
                other = pltpu.roll(piece, HEAD_DIM // 2, 1)
                post_ref[0, rows, column + head : column + head + HEAD_DIM] = (
                    piece * cos_table + other * sine_table
                ).astype(LOW)


def project_heads(tokens, gain, base, left, right, magnitude, segments, part, groups):
    members, depth, width = base.shape
    rows, rank = tokens.shape[0], right.shape[1]
    coarse = table_pieces(np.arange(TABLE_STEP) * TABLE_STEP)
    fine = table_pieces(np.arange(TABLE_STEP))
    whole = lambda v: pl.BlockSpec(v.shape, lambda m: (0,) * v.ndim)
    of_member = lambda *dims: pl.BlockSpec((1,) + dims, lambda m: (m, 0, 0))
    table = pl.BlockSpec((rows, HEAD_DIM), lambda m: (0, 0))
    return call(
        "project_heads",
        heads_kernel,
        (tokens, gain, base, left, right, magnitude, segments, coarse, fine, part),
        (members,),
        [
            whole(tokens),
            whole(gain),
            of_member(depth, width),
            of_member(rank, depth),
            of_member(rank, width),
            whole(magnitude),
            whole(segments),
            whole(coarse),
            whole(fine),
            whole(part),
        ],
        [
            whole(tokens),
            of_member(depth, width),
            of_member(rows, width),
            of_member(1, width),
            of_member(rank, width),
            table,
            table,
            pl.BlockSpec((1, 1, depth), lambda m: (0, 0, 0)),
            pl.BlockSpec((1, 1, depth), lambda m: (0, 0, 0)),
            pl.BlockSpec((rows, 1), lambda m: (0, 0)),
        ],
        [
            shape((rows, depth), LOW),
            shape(base.shape, LOW),
            shape((members, rows, width), LOW),
            shape((members, 1, width), F32),
            shape((members, rank, width), F32),
            shape((rows, HEAD_DIM), F32),
            shape((rows, HEAD_DIM), F32),
            shape((1, 1, depth), F32),
            shape((1, 1, depth), F32),
            shape((rows, 1), jnp.int32),
        ],
        scratch=[
            pltpu.VMEM((rows + rank, depth), LOW),
            pltpu.VMEM(part.shape, F32),
            pltpu.VMEM((groups,) + part.shape, F32),
            pltpu.SemaphoreType.DMA((groups,)),
            pltpu.SemaphoreType.DMA((groups,)),
        ],
        identity=2,
        flops=2 * members * rows * depth * width,
    )


def key_start(block):
    return max(0, (block * ATTEND_BLOCK - (LONGEST - 1)) // ATTEND_BLOCK * ATTEND_BLOCK)


def masked_probs(scores, first, row_at, key_at):
    scores = scores * HEAD_DIM ** (-0.5)
    places = row_at + lax.broadcasted_iota(jnp.int32, scores.shape, 0)
    others = key_at + lax.broadcasted_iota(jnp.int32, scores.shape, 1)
    scores = jnp.where((others >= first) & (others <= places), scores, MASKED)
    exp_scores = jnp.exp(scores - jnp.max(scores, axis=1, keepdims=True))
    return exp_scores * (1.0 / jnp.sum(exp_scores, axis=1, keepdims=True))


class Unit:
    def __init__(self, head, block):
        self.row_at, self.key_at = block * ATTEND_BLOCK, key_start(block)
        self.rows = slice(self.row_at, self.row_at + ATTEND_BLOCK)
        self.keys = slice(self.key_at, self.row_at + ATTEND_BLOCK)
        self.lanes = slice(head * HEAD_DIM, (head + 1) * HEAD_DIM)


def units_of(rows, width, most):
    units = [
        Unit(head, block)
        for block in range(rows // ATTEND_BLOCK)
        for head in range(width // HEAD_DIM)
    ]
    return [units[at : at + most] for at in range(0, len(units), most)]


def put_rows(ref, lead, row_at, lanes, values, order_ref, groups):
    share = ref.shape[len(lead)] // groups
    step = min(share, values.shape[0])
    for start in range(0, values.shape[0], step):
        group = (row_at + start) // share
        inside = (row_at + start) % share
        at = pl.multiple_of(order_ref[groups + group] * share + inside, step)
        ref[(*lead, pl.ds(at, step), lanes)] = values[start : start + step].astype(ref.dtype)


def attend_kernel(groups, order_ref, query_ref, key_ref, value_ref, first_ref, out_ref):
    for some in units_of(*query_ref.shape[1:], 4):
        scores = [
            dot(query_ref[0, u.rows, u.lanes], key_ref[0, u.keys, u.lanes], NT) for u in some
        ]
        probs = [
            masked_probs(s, first_ref[u.rows, :], u.row_at, u.key_at).astype(LOW)
            for u, s in zip(some, scores)
        ]
        for u, p in zip(some, probs):
            mixed = dot(p, value_ref[0, u.keys, u.lanes])
            put_rows(out_ref, (), u.row_at, u.lanes, mixed, order_ref, groups)


def attend(order, groups, post, first):
    rows, width = post.shape[1:]
    wide = 2 * HEAD_DIM
    member = lambda m: pl.BlockSpec((1, rows, wide), lambda h, o: (m, 0, h))
    return call(
        "attend",
        functools.partial(attend_kernel, groups),
        (post, post, post, first),
        (width // wide,),
        [member(0), member(1), member(2), pl.BlockSpec((rows, 1), lambda h, o: (0, 0))],
        [pl.BlockSpec((rows, wide), lambda h, o: (0, h))],
        [shape((rows, width), LOW)],
        prefetch=(order,),
        flops=4 * rows * rows * width,
    )[0]


def attend_back_kernel(
    groups,
    order_ref,
    query_ref,
    key_ref,
    value_ref,
    first_ref,
    cos_ref,
    sine_ref,
    magnitude_ref,
    squares_ref,
    low_ref,
    *rest,
):
    pieces, (grad_ref, total_ref, upper_all, heads_grad, key_grad, value_grad, sems) = rest[:-7], rest[-7:]
    rows_all, width = query_ref.shape[1:]
    share = rows_all // groups

    @pl.when(pl.program_id(0) == 0)
    def _():
        copies = []
        for place, piece in enumerate(pieces):
            at = pl.multiple_of(order_ref[place] * share, share)
            copies.append(
                pltpu.make_async_copy(piece, upper_all.at[pl.ds(at, share), :], sems.at[place])
            )
            copies[-1].start()
        for copy in copies:
            copy.wait()

    step = min(512, rows_all)
    for start in range(0, rows_all, step):
        at = slice(start, start + step)
        heads_grad[at, :] = dot(upper_all[at, :], low_ref[0], NT).astype(LOW)
    norm = [jnp.sqrt(squares_ref[m]) for m in range(3)]
    scale = [magnitude_ref[m : m + 1] / norm[m] for m in range(3)]
    heads = range(0, width, HEAD_DIM)
    totals = [jnp.zeros((1, width), F32) for _ in range(3)]
    filled = set()

    def back(values, rows):
        return values * cos_ref[rows, :] - pltpu.roll(values, HEAD_DIM // 2, 1) * sine_ref[rows, :]

    def add(ref, unit, values):
        for start in range(0, values.shape[0], ATTEND_BLOCK):
            at = unit.key_at + start
            rows = slice(at, at + ATTEND_BLOCK)
            name = (id(ref), at, unit.lanes.start)
            if name in filled:
                ref[rows, unit.lanes] += values[start : start + ATTEND_BLOCK]
            else:
                filled.add(name)
                ref[rows, unit.lanes] = values[start : start + ATTEND_BLOCK]

    def spread(per_head):
        return jnp.concatenate(per_head, axis=1)

    query_totals = [jnp.zeros((1, HEAD_DIM), F32) for _ in heads]
    for some in units_of(rows_all, width, 2):
        scores = [
            dot(query_ref[0, u.rows, u.lanes], key_ref[0, u.keys, u.lanes], NT) for u in some
        ]
        grad_weights = [
            dot(heads_grad[u.rows, u.lanes], value_ref[0, u.keys, u.lanes], NT) for u in some
        ]
        probs = [
            masked_probs(s, first_ref[u.rows, :], u.row_at, u.key_at)
            for u, s in zip(some, scores)
        ]
        grad_scores = [
            (p * (g - jnp.sum(p * g, axis=1, keepdims=True))).astype(LOW)
            for p, g in zip(probs, grad_weights)
        ]
        for u, p, g in zip(some, probs, grad_scores):
            add(value_grad, u, dot(p.astype(LOW), heads_grad[u.rows, u.lanes], TN))
            add(key_grad, u, dot(g, query_ref[0, u.rows, u.lanes], TN))
        for u, g in zip(some, grad_scores):
            grad = back(dot(g, key_ref[0, u.keys, u.lanes]) * HEAD_DIM ** (-0.5), u.rows)
            head = u.lanes.start // HEAD_DIM
            post = back(query_ref[0, u.rows, u.lanes].astype(F32), u.rows)
            query_totals[head] = query_totals[head] + jnp.sum(grad * post, axis=0, keepdims=True)
            put_rows(grad_ref, (0,), u.row_at, u.lanes, grad * scale[0][:, u.lanes], order_ref, groups)
    totals[0] = spread(query_totals)
    for row_at in range(0, rows_all, ATTEND_BLOCK):
        rows = slice(row_at, row_at + ATTEND_BLOCK)
        for head in heads:
            lanes = slice(head, head + HEAD_DIM)
            grad = back(key_grad[rows, lanes] * HEAD_DIM ** (-0.5), rows)
            post = back(key_ref[0, rows, lanes].astype(F32), rows)
            part = jnp.sum(grad * post, axis=0, keepdims=True)
            query_totals[head // HEAD_DIM] = part if row_at == 0 else query_totals[head // HEAD_DIM] + part
            put_rows(grad_ref, (1,), row_at, lanes, grad * scale[1][:, lanes], order_ref, groups)
        grad = value_grad[rows, :]
        totals[2] = totals[2] + jnp.sum(grad * value_ref[0, rows, :].astype(F32), axis=0, keepdims=True)
        put_rows(grad_ref, (2,), row_at, slice(0, width), grad * scale[2], order_ref, groups)
    totals[1] = spread(query_totals)
    for m in range(3):
        total_ref[m] = totals[m] / scale[m]


def attend_back(order, groups, post, first, cos_table, sine_table, magnitude, squares, low, pieces):
    rows, width = post.shape[1:]
    depth = low.shape[2]
    wide = 2 * HEAD_DIM
    member = lambda m: pl.BlockSpec((1, rows, wide), lambda h, o: (m, 0, h))
    table = pl.BlockSpec((rows, HEAD_DIM), lambda h, o: (0, 0))
    column = pl.BlockSpec((3, 1, wide), lambda h, o: (0, 0, h))
    return call(
        "attend_back",
        functools.partial(attend_back_kernel, groups),
        (post, post, post, first, cos_table, sine_table, magnitude, squares, low, *pieces),
        (width // wide,),
        [
            member(0),
            member(1),
            member(2),
            pl.BlockSpec((rows, 1), lambda h, o: (0, 0)),
            table,
            table,
            pl.BlockSpec((3, wide), lambda h, o: (0, h)),
            column,
            pl.BlockSpec((1, wide, depth), lambda h, o: (0, h, 0)),
            *[pl.BlockSpec(memory_space=pl.ANY) for _ in pieces],
        ],
        [pl.BlockSpec((3, rows, wide), lambda h, o: (0, 0, h)), column],
        [shape((3, rows, width), LOW), shape((3, 1, width), F32)],
        scratch=[
            pltpu.VMEM((rows, depth), LOW),
            pltpu.VMEM((rows, wide), LOW),
            pltpu.VMEM((rows, wide), F32),
            pltpu.VMEM((rows, wide), F32),
            pltpu.SemaphoreType.DMA((len(pieces),)),
        ],
        prefetch=(order,),
        flops=10 * rows * rows * width + 2 * rows * width * depth,
    )


def product_kernel(dims, n_totals, n_lines, has_gain, steps, *refs):
    value_ref, weight_ref = refs[:2]
    if n_totals == 0:
        left_ref, *refs = refs[2:]
    else:
        right_ref, squares_ref, magnitude_ref = refs[2:5]
        totals, refs = refs[5 : 5 + n_totals], refs[5 + n_totals :]
    lines = []
    if has_gain:
        normed_ref, gain_ref, *refs = refs
    if n_lines > 0:
        lines, refs = refs[:n_lines], refs[n_lines:]
        *refs, line_mine, line_got, line_send_sems, line_recv_sems = refs
    *outs, extra_ref, rows_all, sent, got, send_sems, recv_sems = refs
    if has_gain:
        *outs, gain_out = outs
    line_outs, outs = outs[len(outs) - n_lines :], outs[: len(outs) - n_lines]
    members, groups, share, inner = value_ref.shape
    count, wide = groups * share, extra_ref.shape[2]
    now = pl.program_id(0)
    sibling = sibling_id()
    me = lax.axis_index("mp")
    peers = [lax.rem(me + k, groups) for k in range(1, groups)] if n_lines > 0 else [sibling]
    line_copies = [
        remote(line_mine, line_got.at[k], line_send_sems.at[k], line_recv_sems.at[k], peer)
        for k, peer in enumerate(peers if n_lines > 0 else [], 1)
    ]

    @pl.when(now == 0)
    def _():
        greet(peers)
        for n, ref in enumerate(lines):
            line_mine[n : n + 1, :] = ref[...]
        if n_totals > 0:
            total = sum_refs(totals)
        for m in range(members):
            rows_all[m, :count, :] = value_ref[m].reshape(count, inner)
            if n_totals == 0:
                rows_all[m, count:, :] = left_ref[m].astype(LOW)
            else:
                weight = norm_weight(total[m], squares_ref[m], magnitude_ref[m : m + 1])
                rows_all[m, count:, :] = (right_ref[m] * weight).astype(LOW)

    result = None
    for m in range(members):
        part = dot(rows_all[m], weight_ref[m], dims)
        extra_ref[m] = part[count:]
        result = part[:count] if result is None else result + part[:count]

    def columns(step):
        return pl.ds(pl.multiple_of(step * wide, wide), wide)

    def copy(step):
        return remote(sent.at[step], got.at[step], send_sems.at[step], recv_sems.at[step], sibling)

    def add(step):
        copy(step).wait_recv()
        for n, ref in enumerate(outs):
            total = ref[:, columns(step)].astype(F32) + got[step, n].astype(F32)
            ref[:, columns(step)] = total.astype(LOW)

    if has_gain:
        terms = jnp.zeros((1, wide), F32)
        for place in range(groups):
            group = lax.rem(me // CORES + place // CORES, groups // CORES) * CORES
            group = group + lax.rem(me + 1 + place, CORES)
            rows = pl.ds(pl.multiple_of(group * share, share), share)
            mine = result[place * share : (place + 1) * share]
            terms = terms + jnp.sum(
                mine * normed_ref[rows, :].astype(F32), axis=0, keepdims=True
            )
        gain_out[...] = terms / gain_ref[...]
    for n, ref in enumerate(outs):
        at = CORES * n * share
        sent[now, n] = result[at : at + share].astype(LOW)
        ref[:, columns(now)] = result[at + share : at + CORES * share].astype(LOW)

    @pl.when(now == 0)
    def _():
        greeted(len(peers))
        for each in line_copies:
            each.start()

    copy(now).start()

    @pl.when(now > 0)
    def _():
        add(now - 1)

    @pl.when(now == steps - 1)
    def _():
        add(now)
        for step in range(steps):
            copy(step).wait_send()
        if n_lines > 0:
            line_sum = line_mine[...]
            for k, each in enumerate(line_copies, 1):
                each.wait_recv()
                line_sum = line_sum + line_got[k]
            for n, ref in enumerate(line_outs):
                ref[0] = line_sum[n : n + 1]
            for each in line_copies:
                each.wait_send()


def product(name, identity, values, weights, dims, left=None, correction=None, lines=(), gain=()):
    members, groups, share, inner = values.shape
    chips = groups // CORES
    width = weights.shape[2] if dims is NN else weights.shape[1]
    wide = tile_of(width, 512)
    steps = width // wide
    if dims is NN:
        weight_spec = pl.BlockSpec((members, inner, wide), lambda n: (0, 0, n))
    else:
        weight_spec = pl.BlockSpec((members, wide, inner), lambda n: (0, n, 0))
    if correction is None:
        extra, n_totals, rank = (left,), 0, left.shape[1]
    else:
        right, squares, magnitude, totals = correction
        extra, n_totals, rank = (right, squares, magnitude, *totals), len(totals), right.shape[1]
    fixed = lambda v: pl.BlockSpec(v.shape, lambda n: (0,) * v.ndim)
    out = pl.BlockSpec((share, width), lambda n: (0, 0))
    line_specs, line_shapes, line_scratch = [], [], []
    if lines:
        line = (len(lines), width)
        line_specs = [pl.BlockSpec((1, 1, width), lambda n: (0, 0, 0)) for _ in lines]
        line_shapes = [shape((1, 1, width), F32) for _ in lines]
        line_scratch = [
            pltpu.VMEM(line, F32),
            pltpu.VMEM((groups,) + line, F32),
            pltpu.SemaphoreType.DMA((groups,)),
            pltpu.SemaphoreType.DMA((groups,)),
        ]
    gain_specs, gain_shapes, gain_in = [], [], []
    if gain:
        one = pl.BlockSpec((1, wide), lambda n: (0, n))
        gain_in = [pl.BlockSpec((gain[0].shape[0], wide), lambda n: (0, n)), one]
        gain_specs, gain_shapes = [one], [shape((1, width), F32)]
    results = call(
        name,
        functools.partial(product_kernel, dims, n_totals, len(lines), bool(gain), steps),
        (values, weights, *extra, *gain, *lines),
        (steps,),
        [fixed(values), weight_spec]
        + [fixed(v) for v in extra]
        + gain_in
        + [fixed(v) for v in lines],
        [out] * chips + line_specs + gain_specs + [pl.BlockSpec((members, rank, wide), lambda n: (0, 0, n))],
        [shape((share, width), LOW)] * chips
        + line_shapes
        + gain_shapes
        + [shape((members, rank, width), F32)],
        scratch=[
            pltpu.VMEM((members, groups * share + rank, inner), LOW),
            pltpu.VMEM((steps, chips, share, wide), LOW),
            pltpu.VMEM((steps, chips, share, wide), LOW),
            pltpu.SemaphoreType.DMA((steps,)),
            pltpu.SemaphoreType.DMA((steps,)),
        ]
        + line_scratch,
        flops=2 * members * groups * share * inner * width,
        identity=identity,
    )
    return results[:chips], *results[chips:]


def shrink_kernel(chips, order_ref, *refs):
    values, (weight_ref, left_ref, cot_ref), outs = refs[:chips], refs[chips : chips + 3], refs[chips + 3 :]
    total_ref, across_ref, rows_all = outs[-3:]
    both, inner = values[0].shape
    share, depth = both // CORES, left_ref.shape[2]
    count = chips * both

    @pl.when(pl.program_id(0) == 0)
    def _():
        for step, ref in enumerate(values):
            rows_all[step * both : (step + 1) * both, :] = ref[...]
        if inner > depth:
            rows_all[count:, depth:] = jnp.zeros((rows_all.shape[0] - count, inner - depth), LOW)
        rows_all[count:, :depth] = left_ref[0].astype(LOW)

    result = dot(rows_all[...], weight_ref[0])
    across_ref[0] = result[count:]
    total = jnp.zeros((1, weight_ref.shape[2]), F32)
    for place in range(chips * CORES):
        pre = result[place * share : (place + 1) * share]
        outs[place][...] = pre.astype(LOW)
        at = pl.multiple_of(order_ref[place] * share, share)
        cot = cot_ref[pl.ds(at, share), :].astype(F32)
        total = total + jnp.sum(pre * cot, axis=0, keepdims=True)
    total_ref[...] = total


def shrink_product(order, values, weights, left, cotangent):
    chips = len(values)
    share, inner = values[0].shape[0] // CORES, values[0].shape[1]
    width, rank = weights.shape[2], left.shape[1]
    rows = chips * CORES * share
    wide = tile_of(width, 512)
    fixed = lambda v: pl.BlockSpec(v.shape, lambda n, o: (0,) * v.ndim)
    results = call(
        "shrink_product",
        functools.partial(shrink_kernel, chips),
        (*values, weights, left, cotangent),
        (width // wide,),
        [fixed(v) for v in values]
        + [
            pl.BlockSpec((1, inner, wide), lambda n, o: (0, 0, n)),
            fixed(left),
            pl.BlockSpec((rows, wide), lambda n, o: (0, n)),
        ],
        [pl.BlockSpec((share, wide), lambda n, o: (0, n))] * (chips * CORES)
        + [
            pl.BlockSpec((1, wide), lambda n, o: (0, n)),
            pl.BlockSpec((1, rank, wide), lambda n, o: (0, 0, n)),
        ],
        [shape((share, width), LOW)] * (chips * CORES)
        + [shape((1, width), F32), shape((1, rank, width), F32)],
        scratch=[pltpu.VMEM((rows + rank, inner), LOW)],
        prefetch=(order,),
        flops=2 * rows * inner * width,
    )
    return results[: chips * CORES], results[-2], results[-1]


def row_call(name, kernel, order, given, whole, out_kinds, sums, prepare):
    share = min(v.shape[0] for v, _ in given)
    width = given[0][0].shape[1]
    halves = 2
    half = share // halves
    count = len(given)

    def run(order_ref, *refs):
        sources, rest = refs[:count], refs[count : -count - 1]
        held, sems = refs[-count - 1 : -1], refs[-1]

        def copies(part):
            for i, ((_, cut), source, target) in enumerate(zip(given, sources, held)):
                at = part * half
                if cut:
                    at = pl.multiple_of(order_ref[1] * share + at, half)
                yield pltpu.make_async_copy(
                    source.at[pl.ds(at, half), :],
                    target.at[pl.ds(part * half, half), :],
                    sems.at[part, i],
                )

        for part in range(halves):

            @pl.when(pl.program_id(0) == part)
            def _(part=part):
                if part == 0:
                    for each in range(halves):
                        for copy in copies(each):
                            copy.start()
                for copy in copies(part):
                    copy.wait()

        outs = rest[len(whole) : len(whole) + len(out_kinds)]
        totals, sums_held = rest[len(whole) + len(out_kinds) :][:sums], rest[len(rest) - sums :]
        tile = 32
        lines = prepare(*[ref[...] for ref in rest[: len(whole)]])
        for ref in sums_held:
            ref[...] = jnp.zeros_like(ref)

        def some(i, carry):
            inside = pl.ds(pl.multiple_of(i * tile, tile), tile)
            at = pl.ds(pl.multiple_of(pl.program_id(0) * half + i * tile, tile), tile)
            values = kernel([ref[at, :].astype(F32) for ref in held], *lines)
            for ref, value in zip(outs, values):
                ref[inside, :] = value.astype(ref.dtype)
            for ref, value in zip(sums_held, values[len(outs) :]):
                ref[...] += jnp.sum(value.reshape(tile // 8, 8, width), axis=0)
            return carry

        lax.fori_loop(0, half // tile, some, 0, unroll=2)
        for ref, held_ref in zip(totals, sums_held):
            add_column(ref, held_ref[...])

    line = pl.BlockSpec((1, width), lambda i, o: (0, 0))
    return call(
        name,
        run,
        (*[v for v, _ in given], *whole),
        (halves,),
        [pl.BlockSpec(memory_space=pl.ANY) for _ in given] + [line for _ in whole],
        [pl.BlockSpec((half, width), lambda i, o: (i, 0)) for _ in out_kinds]
        + [line for _ in range(sums)],
        [shape((share, width), kind) for kind in out_kinds]
        + [shape((1, width), F32) for _ in range(sums)],
        scratch=[pltpu.VMEM((8, width), F32) for _ in range(sums)]
        + [pltpu.VMEM((share, width), v.dtype) for v, _ in given]
        + [pltpu.SemaphoreType.DMA((halves, count))],
        prefetch=(order,),
        flops=20 * share * width,
    )


def sum_of(values):
    total = values[0]
    for value in values[1:]:
        total = total + value
    return total


def add_column(ref, values):
    part = jnp.sum(values, axis=0, keepdims=True)

    @pl.when(pl.program_id(0) == 0)
    def _():
        ref[...] = part

    @pl.when(pl.program_id(0) > 0)
    def _():
        ref[...] += part


def scale_first(squares, magnitude, *rest):
    norm = jnp.sqrt(squares)
    return (magnitude / norm, norm / magnitude, *rest)


def hidden_kernel(given, scale, inverse, gain):
    hidden = given[0] + sum_of(given[1:]) * scale
    return hidden, hidden * rms_rows(hidden) * gain


def mixed_kernel(given, scale, inverse):
    return (given[0] + sum_of(given[1:]) * scale,)


def norm_back(grad_normed, values, gain):
    factor = rms_rows(values)
    scaled = grad_normed * gain
    inner = jnp.mean(scaled * values, axis=1, keepdims=True)
    back = factor * scaled - values * (factor * factor * factor * inner)
    return back, grad_normed * values * factor


def hidden_back_kernel(given, scale, inverse, gain):
    cot, token, hidden = given[:3]
    back, gain_terms = norm_back(sum_of(given[3:]), hidden, gain)
    grad = cot + back
    return grad, grad * scale, grad * ((hidden - token) * inverse), gain_terms


def shrink_back_kernel(places, order_ref, *refs):
    cots, refs = refs[:places], refs[places:]
    *lows, squares_ref, magnitude_ref, product_ref, grad_ref, rows_all = refs
    scale = magnitude_ref[0] / jnp.sqrt(squares_ref[0])
    share = cots[0].shape[0]
    for place, cot_ref in enumerate(cots):
        grad = (cot_ref[...].astype(F32) * scale).astype(LOW)
        grad_ref[place] = grad
        rows_all[place * share : (place + 1) * share, :] = grad
    wide = lows[0].shape[1]
    for n, low_ref in enumerate(lows):
        result = dot(rows_all[...], low_ref[0], NT).astype(LOW)
        for place in range(places):
            product_ref[place, :, n * wide : (n + 1) * wide] = result[
                place * share : (place + 1) * share
            ]


def shrink_back(order, cotangent, low, squares, magnitude, groups):
    rows, width = cotangent.shape
    share, inner = rows // groups, low.shape[1]
    places, cuts = CORES, 3
    line = pl.BlockSpec((1, 1, width), lambda j, o: (0, 0, 0))
    cot = lambda place: pl.BlockSpec((share, width), lambda j, o: (o[places * j + place], 0))
    return call(
        "shrink_back",
        functools.partial(shrink_back_kernel, places),
        (*[cotangent] * places, *[low] * cuts, squares, magnitude),
        (groups // places,),
        [cot(place) for place in range(places)]
        + [
            pl.BlockSpec((1, inner // cuts, width), functools.partial(lambda n, j, o: (0, n, 0), n))
            for n in range(cuts)
        ]
        + [line, line],
        [
            pl.BlockSpec((places, share, inner), lambda j, o: (j, 0, 0)),
            pl.BlockSpec((places, share, width), lambda j, o: (j, 0, 0)),
        ],
        [shape((groups, share, inner), LOW), shape((groups, share, width), LOW)],
        scratch=[pltpu.VMEM((places * share, width), LOW)],
        prefetch=(order,),
        flops=2 * rows * width * inner,
    )


def expand_kernel(step, first, last, n_totals, *refs):
    mine_ref, low_ref, grad_ref, squares_ref, magnitude_ref = refs[:5]
    refs = list(refs[5:])
    left_ref = refs.pop(0) if first else None
    right_ref = refs.pop(0) if last else None
    before = [refs.pop(0) for _ in range(n_totals)]
    product_ref, back_ref, rows_ref, total_ref, joined_ref = refs[:5]
    refs = refs[5:]
    across_ref = refs.pop(0) if first else None
    extra_ref = refs.pop(0) if last else None
    rows_all, low_all, grad_all, product_all, back_all, sent, got, in_sems, out_sems, send_sems, recv_sems = refs
    share, depth = mine_ref.shape
    sibling = sibling_id()
    greet([sibling])
    both = CORES * share
    width, ff = low_ref.shape[2], magnitude_ref.shape[1]
    tile = 256
    cuts = [slice(at, at + tile) for at in range(0, width, tile)]

    mine_copy = pltpu.make_async_copy(mine_ref, rows_all.at[pl.ds(share, share), :], in_sems.at[0])
    other_copy = remote(
        mine_ref,
        rows_all.at[pl.ds(0, share), :],
        send_sems.at[sent.shape[0]],
        recv_sems.at[sent.shape[0]],
        sibling,
    )
    tile_copies = []
    for n, cut in enumerate(cuts):
        lanes = pl.ds(cut.start, tile)
        tile_copies.append(
            [
                pltpu.make_async_copy(
                    low_ref.at[:, :, lanes], low_all.at[:, :, lanes], in_sems.at[2 + 2 * n]
                ),
                pltpu.make_async_copy(
                    grad_ref.at[pl.ds(CORES * step, CORES), :, lanes],
                    grad_all.at[:, :, lanes],
                    in_sems.at[3 + 2 * n],
                ),
            ]
        )
    mine_copy.start()
    for copy in tile_copies[0]:
        copy.start()
    greeted(1)
    other_copy.start()
    for copies in tile_copies[1:]:
        for copy in copies:
            copy.start()
    if first:
        rank = across_ref.shape[1]
        for m in range(2):
            rows_all[both + m * rank : both + (m + 1) * rank, :] = left_ref[m].astype(LOW)
    mine_copy.wait()
    other_copy.wait_recv()
    out_copies = [
        pltpu.make_async_copy(rows_all.at[pl.ds(0, both), :], rows_ref, out_sems.at[2 * len(cuts)])
    ]
    out_copies[0].start()
    lane = lax.broadcasted_iota(jnp.int32, (1, tile), 1)
    for n, cut in enumerate(cuts):
        for copy in tile_copies[n]:
            copy.wait()
        size = min(tile, ff - cut.start)
        pre = [dot(rows_all[...], low_all[m, :, cut]) for m in range(2)]
        if first:
            for m in range(2):
                rows = slice(both + m * rank, both + (m + 1) * rank)
                across_ref[m, :, cut.start : cut.start + size] = pre[m][rows, :size]
        magnitude, squares, scale = [], [], []
        for m in range(2):
            given = magnitude_ref[m : m + 1, cut.start : cut.start + size]
            if size < tile:
                given = jnp.concatenate([given, jnp.zeros((1, tile - size), F32)], axis=1)
            magnitude.append(given)
            squares.append(squares_ref[m, :, cut])
            scale.append(given / jnp.sqrt(squares[m]))
        sums = [jnp.zeros((1, tile), F32) for _ in range(2)]
        at = [slice(m * width + cut.start, m * width + cut.stop) for m in range(2)]
        for place in range(CORES):
            rows = slice(place * share, (place + 1) * share)
            gate_pre, up_pre = pre[0][rows], pre[1][rows]
            gate, up = gate_pre * scale[0], up_pre * scale[1]
            sigmoid = 0.5 + 0.5 * jnp.tanh(0.5 * gate)
            active = gate * sigmoid
            product_all[rows, cut] = (active * up).astype(LOW)
            upper = grad_all[place, :, cut].astype(F32)
            grad_up = upper * active
            grad_gate = upper * up * sigmoid * (1.0 + gate * (1.0 - sigmoid))
            sums[0] += jnp.sum(grad_gate * gate_pre, axis=0, keepdims=True)
            sums[1] += jnp.sum(grad_up * up_pre, axis=0, keepdims=True)
            back_all[rows, at[0]] = (grad_gate * scale[0]).astype(LOW)
            back_all[rows, at[1]] = (grad_up * scale[1]).astype(LOW)
        for m in range(2):
            total_ref[m, :, cut] = sums[m]
        if last:
            rank = extra_ref.shape[1]
            for m in range(2):
                total = sums[m]
                for ref in before:
                    total = total + ref[m, :, cut]
                right = right_ref[m, :, cut.start : cut.start + size]
                if size < tile:
                    spare = jnp.zeros((rank, tile - size), F32)
                    right = jnp.concatenate([right, spare], axis=1)
                weighted = right * norm_weight(total, squares[m], magnitude[m])
                rows = slice(both + m * rank, both + (m + 1) * rank)
                back_all[rows, at[m]] = weighted.astype(LOW)
                back_all[rows, at[1 - m]] = jnp.zeros((rank, tile), LOW)
    for m in range(2):
        lanes = pl.ds(m * width, width)
        copy = pltpu.make_async_copy(
            back_all.at[pl.ds(0, both), lanes], back_ref.at[m], out_sems.at[m]
        )
        copy.start()
        out_copies.append(copy)
    copy = pltpu.make_async_copy(product_all, product_ref, out_sems.at[2])
    copy.start()
    out_copies.append(copy)
    chunk = sent.shape[2]
    copies = [
        remote(sent.at[n], got.at[n], send_sems.at[n], recv_sems.at[n], sibling)
        for n in range(depth // chunk)
    ]

    def add(n):
        columns = slice(n * chunk, (n + 1) * chunk)
        copies[n].wait_recv()
        total = joined_ref[:, columns].astype(F32) + got[n].astype(F32)
        joined_ref[:, columns] = total.astype(LOW)

    for n in range(depth // chunk):
        columns = slice(n * chunk, (n + 1) * chunk)
        result = dot(back_all[:, :width], low_all[0, columns, :], NT)
        result = result + dot(back_all[:, width:], low_all[1, columns, :], NT)
        sent[n] = result[:share].astype(LOW)
        joined_ref[:, columns] = result[share:both].astype(LOW)
        copies[n].start()
        if n > 0:
            add(n - 1)
        if last:
            for m in range(2):
                extra_ref[m, :, columns] = result[both + m * rank : both + (m + 1) * rank]
    add(len(copies) - 1)
    for copy in out_copies:
        copy.wait()
    for copy in [other_copy, *copies]:
        copy.wait_send()


def expand(identity, mine, low, squares, magnitude, grad_product, step, left=None, right=None, before=()):
    share, depth = mine.shape
    width = low.shape[2]
    first, last = left is not None, right is not None
    rows = CORES * share
    hbm = pl.BlockSpec(memory_space=pl.ANY)
    fixed = lambda dims: pl.BlockSpec(tuple(dims), lambda i: (0,) * len(dims))
    operands = [mine, low, grad_product, squares, magnitude]
    in_specs = [hbm, hbm, hbm, fixed(squares.shape), fixed(magnitude.shape)]
    out_shape = [
        shape((rows, width), LOW),
        shape((2, rows, width), LOW),
        shape((rows, depth), LOW),
        shape((2, 1, width), F32),
        shape((share, depth), LOW),
    ]
    out_specs = [hbm, hbm, hbm] + [fixed(v.shape) for v in out_shape[3:]]
    extra_in = extra_out = 0
    if first:
        rank = left.shape[1]
        extra_in = 2 * rank
        operands.append(left)
        in_specs.append(fixed(left.shape))
        out_shape.append(shape((2, rank, magnitude.shape[1]), F32))
        out_specs.append(fixed(out_shape[-1].shape))
    if last:
        rank = right.shape[1]
        extra_out = 2 * rank
        operands += [right, *before]
        in_specs += [fixed(v.shape) for v in (right, *before)]
        out_shape.append(shape((2, rank, depth), F32))
        out_specs.append(fixed(out_shape[-1].shape))
    tiles, chunk = width // 256, tile_of(depth, 512)
    return call(
        "expand",
        functools.partial(expand_kernel, step, first, last, len(before)),
        tuple(operands),
        (1,),
        in_specs,
        out_specs,
        out_shape,
        scratch=[
            pltpu.VMEM((rows + extra_in, depth), LOW),
            pltpu.VMEM(low.shape, LOW),
            pltpu.VMEM((CORES, share, width), LOW),
            pltpu.VMEM((rows, width), LOW),
            pltpu.VMEM((rows + extra_out, 2 * width), LOW),
            pltpu.VMEM((depth // chunk, share, chunk), LOW),
            pltpu.VMEM((depth // chunk, share, chunk), LOW),
            pltpu.SemaphoreType.DMA((2 + 2 * tiles,)),
            pltpu.SemaphoreType.DMA((2 * tiles + 1,)),
            pltpu.SemaphoreType.DMA((depth // chunk + 1,)),
            pltpu.SemaphoreType.DMA((depth // chunk + 1,)),
        ],
        flops=8 * rows * depth * width,
        identity=identity,
    )


def adapter_kernel(plan, n_inputs, n_grads, corrections, n_before, order_ref, *refs):
    for _ in adapter_steps(plan, n_inputs, n_grads, corrections, n_before, order_ref, *refs):
        pass


def adapter_steps(plan, n_inputs, n_grads, corrections, n_before, order_ref, *refs):
    count = n_inputs + n_grads
    sources, held, sems = refs[:count], refs[-count - 1 : -1], refs[-1]
    left_ref, right_ref = refs[count : count + 2]
    *corrected, left_out, right_out = refs[count + 2 : -count - 1]
    members, rank, width = right_ref.shape
    chunks = list(plan(order_ref, held[:n_inputs], held[n_inputs:]))
    copies, used = [], 0
    for parts, _, _ in chunks:
        copies.append([])
        for which, index in parts:
            copy = pltpu.make_async_copy(
                sources[which].at[index], held[which].at[index], sems.at[used]
            )
            copy.start()
            copies[-1].append(copy)
            used += 1
    yield
    left_rows = jnp.concatenate([split_rows(left_ref[m]) for m in range(members)], axis=0)
    right_rows = [split_rows(right_ref[m]) for m in range(members)]
    before, corrected = corrected[:n_before], corrected[n_before:]
    for out, ref in zip((left_out, right_out), before or (None, None)):
        out[...] = jnp.zeros_like(out) if ref is None else ref[...]
    for waits, (_, taken_of, grads_of) in zip(copies, chunks):
        for copy in waits:
            copy.wait()
        taken = taken_of()
        across = dot(left_rows, taken, NT)
        downs = []
        for m in range(members):
            grad = grads_of(m)
            mine = split_rows(fold(across[2 * rank * m : 2 * rank * (m + 1)]))
            right_out[m] += fold(dot(mine, grad))
            downs.append(split_rows(fold(dot(right_rows[m], grad, NT))))
        left = dot(jnp.concatenate(downs, axis=0), taken)
        for m in range(members):
            left_out[m] += fold(left[2 * rank * m : 2 * rank * (m + 1)])
        yield
    if corrections:
        correct(corrections, right_ref, left_out, right_out, left_out, right_out, *corrected)


def correct(n_totals, right_ref, left_in, right_in, left_out, right_out, *refs):
    back_ref, across_ref, squares_ref, magnitude_ref = refs[:4]
    totals, magnitude_out = refs[4 : 4 + n_totals], refs[4 + n_totals]
    members, rank, width = right_ref.shape
    total = sum_refs(totals)[:, :, :width]
    squares = squares_ref[:, :, :width]
    magnitude_out[...] = total / jnp.sqrt(squares)
    for m in range(members):
        weight = norm_weight(total[m], squares[m], magnitude_ref[m : m + 1])
        if back_ref.dtype == LOW:
            low = back_ref[m, : left_in.shape[2], :]
            back = fold(dot(split_rows(right_ref[m] * weight), low, NT))
        else:
            back = back_ref[m]
        left_out[m] = ADAPT_SCALE * (left_in[m] - back)
        right_out[m] = ADAPT_SCALE * (right_in[m] - across_ref[m][:, :width] * weight)


def adapter_parts(inputs, grads, left, right, correction, before):
    members, rank, width = right.shape
    moved, fixed, n_totals = [*inputs, *grads], [left, right, *before], 0
    outs = [(members, rank, left.shape[2]), (members, rank, width)]
    if correction is not None:
        *given, totals = correction
        n_totals = len(totals)
        fixed += [*given, *totals]
        outs = [(members, 1, width)] + outs
    scratch = [pltpu.VMEM(v.shape, v.dtype) for v in moved] + [pltpu.SemaphoreType.DMA((32,))]
    return moved, fixed, outs, scratch, (len(inputs), len(grads), n_totals, len(before))


def adapter(name, order, plan, inputs, grads, left, right, correction=None, before=(), other=None):
    moved, fixed, outs, scratch, counts = adapter_parts(inputs, grads, left, right, correction, before)
    kernel = functools.partial(adapter_kernel, plan, *counts)
    full = lambda dims: pl.BlockSpec(tuple(dims), lambda i, o: (0,) * len(dims))
    n_moved, n_fixed, n_outs = len(moved), len(fixed), len(outs)
    if other is not None:
        sums, other_right, (low, across, squares, magnitude, totals) = other
        moved = moved + [low]
        fixed = fixed + [other_right, *sums, across, squares, magnitude, *totals]
        outs = outs + [(1, 1, other_right.shape[2]), sums[0].shape, sums[1].shape]
        scratch = scratch + [pltpu.VMEM(low.shape, LOW), pltpu.SemaphoreType.DMA(())]

    def run(order_ref, *refs):
        if other is None:
            kernel(order_ref, *refs)
            return
        refs = list(refs)
        low_held, low_sem = refs[-2:]
        low_copy = pltpu.make_async_copy(refs[n_moved], low_held, low_sem)
        ends = [n_moved + 1, n_moved + 1 + len(fixed), n_moved + 1 + len(fixed) + len(outs)]
        fixed_refs, out_refs = refs[ends[0] : ends[1]], refs[ends[1] : ends[2]]
        steps = adapter_steps(
            plan,
            *counts,
            order_ref,
            *refs[:n_moved],
            *fixed_refs[:n_fixed],
            *out_refs[:n_outs],
            *refs[ends[2] : -2],
        )
        next(steps)
        low_copy.start()
        for _ in steps:
            pass
        low_copy.wait()
        right_ref, left_in, right_in, across_ref, squares_ref, magnitude_ref, *totals_refs = (
            fixed_refs[n_fixed:]
        )
        magnitude_out, left_out, right_out = out_refs[n_outs:]
        correct(
            len(totals_refs),
            right_ref,
            left_in,
            right_in,
            left_out,
            right_out,
            low_held,
            across_ref,
            squares_ref,
            magnitude_ref,
            *totals_refs,
            magnitude_out,
        )

    return call(
        name,
        run,
        (*moved, *fixed),
        (1,),
        [pl.BlockSpec(memory_space=pl.ANY) for _ in moved] + [full(v.shape) for v in fixed],
        [full(dims) for dims in outs],
        [shape(dims, F32) for dims in outs],
        scratch=scratch,
        prefetch=(order,),
        flops=sum(v.size for v in moved) * 64,
    )


def copy_kernel(count, *refs):
    for source, target in zip(refs[:count], refs[count:]):
        if len(target.shape) < len(source.shape):
            for m in range(source.shape[0]):
                target[m : m + 1, :] = source[m]
        else:
            target[...] = source[...]


def copy_out(arrays):
    full = lambda v: pl.BlockSpec(v.shape, lambda i: (0,) * len(v.shape))
    flat = lambda v: v.shape[:1] + v.shape[2:] if v.ndim == 3 and v.shape[1] == 1 else v.shape
    out_shape = [shape(flat(v), F32) for v in arrays]
    return call(
        "copy_out",
        functools.partial(copy_kernel, len(arrays)),
        tuple(arrays),
        (1,),
        [full(v) for v in arrays],
        [full(v) for v in out_shape],
        out_shape,
    )


GRAIN = 16


def pieces_of(width):
    return [(at, min(128, width - at)) for at in range(0, width, 128)]


def cells_of(blocks, lines, parts):
    cells, rows = [], []
    for n, block in enumerate(blocks):
        for m in range(block.shape[0]):
            for at, size in pieces_of(block.shape[2] // parts):
                cells.append((n, m, at, size))
    for n, line in enumerate(lines):
        for m in range(line.shape[0]):
            for at, size in pieces_of(line.shape[2] // parts):
                rows.append((n, m, at, size))
    return cells, rows


def pack(blocks, lines, wide_ref, part, parts, cells, rows):
    for i, (n, m, at, size) in enumerate(cells):
        start = part * (blocks[n].shape[2] // parts) + at
        wide_ref[part, i, :, :size] = blocks[n][m, :, start : start + size]
    for i, (n, m, at, size) in enumerate(rows):
        start = part * (lines[n].shape[2] // parts) + at
        cell, row = len(cells) + i // GRAIN, i % GRAIN
        wide_ref[part, cell, row : row + 1, :size] = lines[n][m, :, start : start + size]


def unpack(full_ref, blocks, lines, part, parts, cells, rows):
    for i, (n, m, at, size) in enumerate(cells):
        start = part * (blocks[n].shape[2] // parts) + at
        blocks[n][m, :, start : start + size] = full_ref[part, i].astype(F32)[:, :size]
    for i, (n, m, at, size) in enumerate(rows):
        start = part * (lines[n].shape[2] // parts) + at
        cell, row = len(cells) + i // GRAIN, i % GRAIN
        values = full_ref[part, cell].astype(F32)
        lines[n][m, :, start : start + size] = values[row : row + 1, :size]


def reduce_steps(groups, lines, counts, *refs):
    n_all, n_all_lines, n_dp, n_dp_lines = counts
    count = sum(counts)
    taken, given, scratch = refs[:count], refs[count : 2 * count], refs[2 * count :]
    ends = [n_all, n_all + n_all_lines, n_all + n_all_lines + n_dp]
    parted = lambda v: (v[: ends[0]], v[ends[0] : ends[1]], v[ends[1] : ends[2]], v[ends[2] :])
    all_out, all_lines_out, dp_out, dp_lines_out = parted(given)
    (
        all_ref,
        line_ref,
        all_low,
        line_low,
        all_got,
        part,
        part_low,
        part_got,
        line_got,
        all_full,
        line_full,
        *sems,
    ) = scratch
    held, in_sems, sems = sems[:count], sems[count], sems[count + 1 :]
    loads = [
        pltpu.make_async_copy(source, target, in_sems.at[i])
        for i, (source, target) in enumerate(zip(taken, held))
    ]
    for load in loads:
        load.start()
    me, row = lax.axis_index("mp"), lax.axis_index("dp")
    piece, line_piece = part.shape[0] // lines, line_ref.shape[1] // lines
    mp_peer = [lax.rem(me + k, groups) for k in range(groups)]
    dp_peer = [lax.rem(row + k, lines) for k in range(lines)]
    barrier = pltpu.get_barrier_semaphore()
    for k in range(1, groups):
        pl.semaphore_signal(barrier, 1, device_id={"mp": mp_peer[k]}, device_id_type=MESH_IDS)
    for k in range(1, lines):
        pl.semaphore_signal(barrier, 1, device_id={"dp": dp_peer[k]}, device_id_type=MESH_IDS)
    all_in, all_lines_in, dp_in, dp_lines_in = parted(held)
    all_cells = cells_of(all_in, all_lines_in, groups)
    dp_cells = cells_of(dp_in, dp_lines_in, 1)
    all_ref[...] = jnp.zeros_like(all_ref)
    line_ref[...] = jnp.zeros_like(line_ref)
    for load in loads:
        load.wait()
    for q in range(groups):
        pack(all_in, all_lines_in, all_ref, q, groups, *all_cells)
    pack(dp_in, dp_lines_in, line_ref, 0, 1, *dp_cells)
    all_low[...] = all_ref[...].astype(LOW)
    line_low[...] = line_ref[...].astype(LOW)
    pl.semaphore_wait(barrier, groups + lines - 2)

    def send(source, target, stage, k, axis, peer):
        copy = pltpu.make_async_remote_copy(
            src_ref=source,
            dst_ref=target,
            send_sem=sems[2 * stage].at[k],
            recv_sem=sems[2 * stage + 1].at[k],
            device_id={axis: peer},
            device_id_type=MESH_IDS,
        )
        copy.start()
        return copy

    over_mp = [
        send(all_low.at[mp_peer[k]], all_got.at[k], 0, k, "mp", mp_peer[k])
        for k in range(1, groups)
    ]
    over_dp = [
        send(
            line_low.at[0, pl.ds(dp_peer[k] * line_piece, line_piece)],
            line_got.at[k],
            1,
            k,
            "dp",
            dp_peer[k],
        )
        for k in range(1, lines)
    ]
    yield
    total = all_ref[me]
    for k, copy in enumerate(over_mp, 1):
        copy.wait_recv()
        total = total + all_got[k].astype(F32)
    part[...] = total
    part_low[...] = total.astype(LOW)
    part_dp = [
        send(part_low.at[pl.ds(dp_peer[k] * piece, piece)], part_got.at[k], 2, k, "dp", dp_peer[k])
        for k in range(1, lines)
    ]
    yield
    held = pl.ds(row * piece, piece)
    total = part[held]
    for k, copy in enumerate(part_dp, 1):
        copy.wait_recv()
        total = total + part_got[k].astype(F32)
    all_full[me, held] = total.astype(LOW)
    part_back = [
        send(all_full.at[me, held], all_full.at[me, held], 4, k, "dp", dp_peer[k])
        for k in range(1, lines)
    ]
    mine = pl.ds(row * line_piece, line_piece)
    total = line_ref[0, mine]
    for k, copy in enumerate(over_dp, 1):
        copy.wait_recv()
        total = total + line_got[k].astype(F32)
    line_full[0, mine] = total.astype(LOW)
    line_back = [
        send(line_full.at[0, mine], line_full.at[0, mine], 3, k, "dp", dp_peer[k])
        for k in range(1, lines)
    ]
    yield
    for copy in part_back:
        copy.wait_recv()
    all_back = [
        send(all_full.at[me], all_full.at[me], 5, k, "mp", mp_peer[k]) for k in range(1, groups)
    ]
    yield
    for copy in line_back:
        copy.wait_recv()
    unpack(line_full, dp_out, dp_lines_out, 0, 1, *dp_cells)
    for copy in all_back:
        copy.wait_recv()
    for q in range(groups):
        unpack(all_full, all_out, all_lines_out, q, groups, *all_cells)
    for copy in over_mp + over_dp + part_dp + line_back + part_back + all_back:
        copy.wait_send()


def reduce_devices(name, identity, over_all, over_all_lines, over_dp, over_dp_lines, job):
    groups, lines = lax.axis_size("mp"), lax.axis_size("dp")

    def size_of(blocks, rows, parts):
        cells, lines_in = cells_of(blocks, rows, parts)
        size = len(cells) + -(-len(lines_in) // GRAIN)
        return -(-size // lines) * lines

    count, line_count = size_of(over_all, over_all_lines, groups), size_of(over_dp, over_dp_lines, 1)
    operands = [*over_all, *over_all_lines, *over_dp, *over_dp_lines]
    counts = (len(over_all), len(over_all_lines), len(over_dp), len(over_dp_lines))
    tail = (GRAIN, 128)
    sizes = (groups, lines, lines, lines, lines, groups)
    every, line = (groups, count) + tail, (1, line_count) + tail
    scratch = (
        [
            pltpu.VMEM(every, F32),
            pltpu.VMEM(line, F32),
            pltpu.VMEM(every, LOW),
            pltpu.VMEM(line, LOW),
            pltpu.VMEM(every, LOW),
            pltpu.VMEM((count,) + tail, F32),
            pltpu.VMEM((count,) + tail, LOW),
            pltpu.VMEM((lines, count // lines) + tail, LOW),
            pltpu.VMEM((lines, line_count // lines) + tail, LOW),
            pltpu.VMEM(every, LOW),
            pltpu.VMEM(line, LOW),
        ]
        + [pltpu.VMEM(v.shape, F32) for v in operands]
        + [pltpu.SemaphoreType.DMA((len(operands),))]
        + [pltpu.SemaphoreType.DMA((n,)) for n in sizes for _ in range(2)]
    )
    job_steps, moved, whole_rows, job_shape, job_scratch = job
    n_operands, n_scratch = len(operands), len(scratch)
    out_shape = [shape(v.shape, F32) for v in operands] + [job_shape]
    anywhere = pl.BlockSpec(memory_space=pl.ANY)
    full = lambda v: pl.BlockSpec(v.shape, lambda i: (0,) * v.ndim)
    operands = operands + [*moved, *whole_rows]

    def run(*refs):
        given, refs = refs[: len(operands)], refs[len(operands) :]
        results, held = refs[: len(out_shape)], refs[len(out_shape) :]
        steps = reduce_steps(
            groups, lines, counts, *given[:n_operands], *results[:n_operands], *held[:n_scratch]
        )
        work = job_steps(*given[n_operands:], results[n_operands], *held[n_scratch:])
        next(work)
        for _ in steps:
            next(work, None)
        for _ in work:
            pass

    return call(
        name,
        run,
        tuple(operands),
        (1,),
        [anywhere] * (n_operands + len(moved)) + [full(v) for v in whole_rows],
        [full(v) for v in out_shape[:-1]] + [anywhere],
        out_shape,
        scratch=scratch + job_scratch,
        flops=1000,
        identity=identity,
    )


def token_job(tokens, grad_hidden, parts, gain):
    share, width = grad_hidden.shape
    moved = [tokens, grad_hidden, *parts]

    def steps(*refs):
        sources, gain_ref, out_ref = refs[: len(moved)], refs[len(moved)], refs[len(moved) + 1]
        *held, result, sems = refs[len(moved) + 2 :]
        row = pl.multiple_of(lax.axis_index("mp") * share, share)
        copies = []
        for n, (source, target) in enumerate(zip(sources, held)):
            source = source.at[pl.ds(row, share), :] if n == 0 else source
            copies.append(pltpu.make_async_copy(source, target, sems.at[n]))
            copies[-1].start()
        yield
        for copy in copies:
            copy.wait()
        tile = 32
        gain = gain_ref[...]

        def some(i, carry):
            at = pl.ds(pl.multiple_of(i * tile, tile), tile)
            token, grad, *rest = [ref[at, :].astype(F32) for ref in held]
            result[at, :] = grad + norm_back(sum_of(rest), token, gain)[0]
            return carry

        lax.fori_loop(0, share // tile, some, 0, unroll=2)
        copy = pltpu.make_async_copy(result, out_ref, sems.at[len(moved)])
        copy.start()
        yield
        yield
        copy.wait()

    scratch = [pltpu.VMEM((share, width), v.dtype) for v in moved]
    scratch += [pltpu.VMEM((share, width), F32), pltpu.SemaphoreType.DMA((len(moved) + 1,))]
    return steps, moved, [gain], shape((share, width), F32), scratch


def body(
    tokens,
    cotangent,
    segment_ids,
    attend_gain,
    expand_gain,
    heads_base,
    heads_left,
    heads_right,
    heads_magnitude,
    output_base,
    output_left,
    output_right,
    output_magnitude,
    expand_base,
    expand_left,
    expand_right,
    expand_magnitude,
    shrink_base,
    shrink_left,
    shrink_right,
    shrink_magnitude,
):
    groups = lax.axis_size("mp")
    chips = groups // CORES
    index = lax.axis_index("mp")
    chip, core = index // CORES, index % CORES
    rows, width = tokens.shape
    share = rows // groups
    local_heads, ff = heads_base.shape[2], expand_base.shape[2]
    ff_wide = padded(ff)
    device = jnp.arange(groups, dtype=jnp.int32)
    order = jnp.concatenate(
        [
            (chip + device // CORES) % chips * CORES + (core + 1 + device) % CORES,
            (device // CORES + chips - chip) % chips * CORES + (device + CORES - core + 1) % CORES,
        ]
    ).astype(jnp.int32)

    def tie(*values):
        return lax.optimization_barrier(values)

    def sibling(values):
        return lax.ppermute(
            values, "mp", [(i, i // CORES * CORES + (i + 1) % CORES) for i in range(groups)]
        )

    def to_chip(values, step):
        return lax.ppermute(
            values,
            "mp",
            [((i, ((i // CORES + step) % chips) * CORES + i % CORES)) for i in range(groups)],
        )

    def join(pair):
        return (pair[1].astype(F32) + sibling(pair[0]).astype(F32)).astype(LOW)

    def chip_pairs(places):
        return [places[CORES * step : CORES * (step + 1)] for step in range(chips)]

    def arrive(own):
        return [to_chip(own, chips - step) for step in range(1, chips)]

    def pairs_of(own, near_sibling, arrived):
        return [(near_sibling, own)] + [(sibling(piece), piece) for piece in arrived]

    def in_pairs(order_ref, inputs, grads):
        for step, (taken, grad) in enumerate(zip(inputs, grads)):
            yield (
                [(step, ...), (chips + step, ...)],
                lambda taken=taken: taken[...],
                lambda m, grad=grad: grad[m, :, :ff],
            )

    def in_shrink(order_ref, inputs, grads):
        for step, taken in enumerate(inputs):
            at = slice(CORES * step, CORES * (step + 1))
            yield (
                [(step, ...), (chips, pl.ds(CORES * step, CORES))],
                lambda taken=taken: taken[:, :ff],
                lambda m, at=at: grads[0][at].reshape(-1, grads[0].shape[-1]),
            )

    def in_output(start):
        def plan(order_ref, inputs, grads):
            for n, grad in enumerate(grads):
                yield (
                    [(0, (0, start + n)), (1 + n, ...)],
                    lambda place=start + n: inputs[0][0, place],
                    lambda m, grad=grad: grad[...],
                )

        return plan

    def in_heads(order_ref, inputs, grads):
        for place in range(groups):
            step, side = place // CORES, place % CORES
            me = lax.axis_index("mp")
            group = lax.rem(me // CORES + step, chips) * CORES + lax.rem(me + 1 + side, CORES)
            at = pl.multiple_of(group * share, share)
            rows = pl.ds(place * share, share)
            yield (
                [(0, pl.ds(at, share)), (1, (slice(None), rows))],
                lambda at=at: inputs[0][pl.ds(at, share), :],
                lambda m, rows=rows: grads[0][m, rows, :],
            )

    heads_rows, output_rows = turned(heads_left), turned(output_left[None])
    expand_rows, shrink_rows = turned(expand_left), turned(shrink_left[None])
    heads_mag, output_mag = heads_magnitude, output_magnitude[None]
    expand_mag, shrink_mag = expand_magnitude, shrink_magnitude[None]
    attend_line, expand_line = attend_gain[None], expand_gain[None]

    output_low, shrink_low, squares_part = merge_pair(
        [(output_base, output_rows[0], output_right), (shrink_base, shrink_rows[0], shrink_right)]
    )
    output_low, shrink_low = output_low[None], shrink_low[None]
    (
        normed,
        heads_low,
        post,
        heads_sq,
        heads_across,
        cos_table,
        sine_table,
        output_sq,
        shrink_sq,
        first,
    ) = project_heads(
        tokens,
        attend_line,
        heads_base,
        heads_rows,
        heads_right,
        heads_mag,
        segment_ids,
        squares_part,
        groups,
    )
    heads_out = attend(order, groups, post, first)
    heads_parts = heads_out.reshape(1, groups, share, local_heads)
    joined, output_across = product(
        "output_product", 3, heads_parts, output_low, NN, left=output_rows
    )
    joined, expand_right_tied = tie(joined, expand_right)
    output_parts = [joined[0]] + [to_chip(joined[step], step) for step in range(1, chips)]
    expand_low, expand_sq = merge(expand_base, expand_rows, expand_right_tied, 1024)
    grad_product, shrink_grad = shrink_back(
        order, cotangent, shrink_low, shrink_sq, shrink_mag[None], groups
    )
    output_parts, expand_low, grad_product = tie(output_parts, expand_low, grad_product)
    hidden, normed_own = row_call(
        "hidden",
        hidden_kernel,
        order,
        [(tokens, True)] + [(part, False) for part in output_parts],
        (output_sq[0], output_mag, expand_line),
        (F32, LOW),
        0,
        scale_first,
    )

    def feed(mine, step, **extra):
        return expand(
            4 + step, mine, expand_low, expand_sq, expand_mag, grad_product, step, **extra
        )

    arrived = arrive(normed_own)
    fed = [feed(normed_own, 0, left=expand_rows)]
    arrived, fed = tie(arrived, fed)
    fed = list(fed)
    for step in range(1, chips):
        extra = {}
        if step == chips - 1:
            extra = {"right": expand_right, "before": [f[3] for f in fed]}
        fed.append(feed(arrived[step - 1], step, **extra))
    expand_totals = [f[3] for f in fed]
    joined, shrink_rows_tied = tie([f[4] for f in fed], shrink_rows)
    mid_parts = [joined[0]] + [to_chip(joined[step], step) for step in range(1, chips)]
    shrink_places, shrink_total, shrink_across = shrink_product(
        order, [f[0] for f in fed], shrink_low, shrink_rows_tied, cotangent
    )
    shrink_pairs = chip_pairs(shrink_places)
    expand_adapter = adapter(
        "expand_adapter",
        order,
        in_pairs,
        [f[2] for f in fed],
        [f[1] for f in fed],
        expand_rows,
        expand_right,
        (fed[-1][5], fed[0][5], expand_sq, expand_mag, expand_totals),
    )
    mid_parts, shrink_pairs, expand_adapter = tie(mid_parts, shrink_pairs, expand_adapter)
    grad_hidden, output_grad_own, output_total, expand_gain_part = row_call(
        "hidden_back",
        hidden_back_kernel,
        order,
        [(cotangent, True), (tokens, True), (hidden, False)]
        + [(part, False) for part in mid_parts],
        (output_sq[0], output_mag, expand_line),
        (F32, LOW),
        2,
        scale_first,
    )
    arrived, near_sibling = arrive(output_grad_own), sibling(output_grad_own)
    shrink_joined = [join(pair) for pair in shrink_pairs[1:]]
    shrink_joined, shrink_rows_tied = tie(shrink_joined, shrink_rows)
    shrink_sums = adapter(
        "shrink_adapter",
        order,
        in_shrink,
        [f[0] for f in fed],
        [shrink_grad],
        shrink_rows_tied,
        shrink_right[None],
    )
    output_sums = adapter(
        "output_near_adapter",
        order,
        in_output(0),
        [heads_parts],
        [near_sibling, output_grad_own],
        output_rows,
        output_right[None],
    )
    arrived, near_sibling, shrink_joined, shrink_sums, output_sums = tie(
        arrived, near_sibling, shrink_joined, shrink_sums, output_sums
    )
    output_grad = [
        piece for pair in pairs_of(output_grad_own, near_sibling, arrived) for piece in pair
    ]
    shrink_parts = [shrink_pairs[0][1], sibling(shrink_pairs[0][0])] + [
        to_chip(values, step) for step, values in enumerate(shrink_joined, 1)
    ]
    heads_grads, heads_total = attend_back(
        order,
        groups,
        post,
        first,
        cos_table,
        sine_table,
        heads_mag,
        heads_sq,
        output_low,
        output_grad,
    )
    grad_parts = heads_grads.reshape(3, groups, share, local_heads)
    joined, output_total, shrink_total, attend_gain_part, token_extra = product(
        "normed_product",
        20,
        grad_parts,
        heads_low,
        NT,
        correction=(heads_right, heads_sq, heads_mag, [heads_total]),
        lines=(output_total, shrink_total),
        gain=(normed, attend_line),
    )
    joined, shrink_parts, heads_rows_tied, output_rows_tied = tie(
        joined, shrink_parts, heads_rows, output_rows
    )
    token_parts = [joined[0]] + [to_chip(joined[step], step) for step in range(1, chips)]
    output_mag_part, output_left_part, output_right_part, *shrink_adapter = adapter(
        "output_far_adapter",
        order,
        in_output(CORES),
        [heads_parts],
        output_grad[CORES:],
        output_rows_tied,
        output_right[None],
        (output_low, output_across, output_sq, output_mag, [output_total]),
        output_sums,
        (
            shrink_sums,
            shrink_right[None],
            (shrink_low, shrink_across, shrink_sq, shrink_mag, [shrink_total]),
        ),
    )
    heads_adapter = adapter(
        "heads_adapter",
        order,
        in_heads,
        [normed],
        [heads_grads],
        heads_rows_tied,
        heads_right,
        (token_extra, heads_across, heads_sq, heads_mag, [heads_total]),
    )
    (mixed,) = row_call(
        "mixed",
        mixed_kernel,
        order,
        [(hidden, False)] + [(part, False) for part in shrink_parts],
        (shrink_sq[0], shrink_mag),
        (LOW,),
        0,
        scale_first,
    )
    token_parts, heads_adapter, mixed = tie(token_parts, heads_adapter, mixed)
    *reduced, grad_tokens = reduce_devices(
        "reduce_gradients",
        1,
        [expand_adapter[1], shrink_adapter[2], output_right_part, heads_adapter[1]],
        [expand_gain_part[None], attend_gain_part[None]],
        [expand_adapter[2], shrink_adapter[1], output_left_part, heads_adapter[2]],
        [expand_adapter[0], shrink_adapter[0], output_mag_part, heads_adapter[0]],
        token_job(tokens, grad_hidden, token_parts, attend_line),
    )
    (
        expand_left_grad,
        shrink_right_grad,
        output_right_grad,
        heads_left_grad,
        expand_gain_grad,
        attend_gain_grad,
        expand_right_grad,
        shrink_left_grad,
        output_left_grad,
        heads_right_grad,
        expand_mag_grad,
        shrink_mag_grad,
        output_mag_grad,
        heads_mag_grad,
        grad_tokens,
    ) = copy_out([*reduced, grad_tokens])
    return (
        mixed,
        grad_tokens,
        attend_gain_grad[0],
        expand_gain_grad[0],
        jnp.swapaxes(heads_left_grad, 1, 2),
        heads_right_grad,
        heads_mag_grad,
        output_left_grad[0].T,
        output_right_grad[0],
        output_mag_grad[0],
        jnp.swapaxes(expand_left_grad, 1, 2),
        expand_right_grad,
        expand_mag_grad,
        shrink_left_grad[0].T,
        shrink_right_grad[0],
        shrink_mag_grad[0],
    )


def solution(mesh):
    placed = (
        P("dp", None),
        P("dp", None),
        P("dp", None),
        P(),
        P(),
        P(None, None, "mp"),
        P(),
        P(None, None, "mp"),
        P(None, "mp"),
        P("mp", None),
        P("mp", None),
        P(),
        P(),
        P(None, None, "mp"),
        P(),
        P(None, None, "mp"),
        P(None, "mp"),
        P("mp", None),
        P("mp", None),
        P(),
        P(),
    )
    return jax.shard_map(
        body,
        mesh=mesh,
        in_specs=placed,
        out_specs=(
            P(("dp", "mp"), None),
            P(("dp", "mp"), None),
            P(),
            P(),
            P(),
            P(None, None, "mp"),
            P(None, "mp"),
            P("mp", None),
            P(),
            P(),
            P(),
            P(None, None, "mp"),
            P(None, "mp"),
            P("mp", None),
            P(),
            P(),
        ),
        check_vma=False,
    )
```

```python
import functools

import jax
import jax.numpy as jnp
import ml_dtypes
import numpy as np
from jax import lax
from jax.experimental import pallas as pl
from jax.experimental.pallas import tpu as pltpu
from jax.sharding import PartitionSpec as P

HEAD_DIM = 128
CORES = 2
LONGEST = 512
ATTEND_BLOCK = 256
ADAPT_SCALE = 2.0
NORM_EPS = 1e-05
ROPE_BASE = 10000.0
MASKED = -1e30

F32 = jnp.float32
LOW = jnp.bfloat16
NN = (((1,), (0,)), ((), ()))
NT = (((1,), (1,)), ((), ()))
TN = (((0,), (0,)), ((), ()))


MESH_IDS = pl.DeviceIdType.MESH


def sibling_id():
    me = lax.axis_index("mp")
    return me // CORES * CORES + lax.rem(me + 1, CORES)


def greet(peers):
    for peer in peers:
        pl.semaphore_signal(
            pltpu.get_barrier_semaphore(), 1, device_id={"mp": peer}, device_id_type=MESH_IDS
        )


def greeted(count):
    pl.semaphore_wait(pltpu.get_barrier_semaphore(), count)


def remote(source, target, send_sem, recv_sem, peer):
    return pltpu.make_async_remote_copy(
        src_ref=source,
        dst_ref=target,
        send_sem=send_sem,
        recv_sem=recv_sem,
        device_id={"mp": peer},
        device_id_type=MESH_IDS,
    )


def dot(left, right, dims=NN):
    return lax.dot_general(left, right, dims, preferred_element_type=F32)


def shape(dims, kind):
    return jax.ShapeDtypeStruct(tuple(dims), kind)


def call(name, kernel, operands, grid, in_specs, out_specs, out_shape, scratch=(), prefetch=(), flops=0, mib=63.5, identity=None):
    moved = sum(v.size * v.dtype.itemsize for v in operands)
    moved += sum(v.size * v.dtype.itemsize for v in out_shape)
    return pl.pallas_call(
        kernel,
        name=name,
        out_shape=out_shape,
        grid_spec=pltpu.PrefetchScalarGridSpec(
            num_scalar_prefetch=len(prefetch),
            grid=grid,
            in_specs=in_specs,
            out_specs=out_specs,
            scratch_shapes=scratch,
        ),
        compiler_params=pltpu.CompilerParams(
            vmem_limit_bytes=int(mib * 2**20), collective_id=identity, has_side_effects=identity is not None
        ),
        cost_estimate=pl.CostEstimate(flops=flops // 16, bytes_accessed=moved // 16, transcendentals=0),
    )(*prefetch, *operands)


def tile_of(size, most):
    return most if size % most == 0 else size


def split_rows(values):
    top = values.astype(LOW)
    rest = (values - top.astype(F32)).astype(LOW)
    return jnp.concatenate([top, rest], axis=0)


def turned(left_map):
    return jnp.swapaxes(left_map, -1, -2)


def norm_weight(total, squares, magnitude):
    norm = jnp.sqrt(squares)
    return total * magnitude / (norm * norm * norm)


def sum_refs(refs):
    total = refs[0][...]
    for ref in refs[1:]:
        total = total + ref[...]
    return total


def fold(values):
    half = values.shape[0] // 2
    return values[:half] + values[half:]


def merge_tile(base_at, low_put, left, right, depth):
    rank = right.shape[0]
    doubled = ADAPT_SCALE * right
    top = doubled.astype(LOW)
    rest = (doubled - top.astype(F32)).astype(LOW)
    right_stack = jnp.concatenate([top, rest, top], axis=0)
    left_pair = split_rows(left)
    left_stack = jnp.concatenate([left_pair[:rank], left_pair[:rank], left_pair[rank:]], axis=0)
    width = right.shape[1]
    wide = 256 if width == 512 else width
    step = tile_of(depth, 1024)
    squares = []
    for at in range(0, width, wide):
        columns = slice(at, at + wide)
        total = jnp.zeros((1, wide), F32)
        for start in range(0, depth, step):
            merged = base_at(start, step, columns).astype(F32) + dot(
                left_stack[:, start : start + step], right_stack[:, columns], TN
            )
            low_put(start, step, columns, merged.astype(LOW))
            total = total + jnp.sum(merged * merged, axis=0, keepdims=True)
        squares.append(total)
    return jnp.concatenate(squares, axis=1)


def merge_pair_kernel(*refs):
    for n in range(2):
        base_ref, left_ref, right_ref = refs[3 * n : 3 * n + 3]
        low_ref, squares_ref = refs[6 + n], refs[8]
        depth = base_ref.shape[0]
        if low_ref.shape[0] > depth:
            low_ref[depth:, :] = jnp.zeros((low_ref.shape[0] - depth, low_ref.shape[1]), LOW)

        def put(start, step, columns, tile, low_ref=low_ref):
            low_ref[start : start + step, columns] = tile

        squares_ref[n : n + 1, :] = merge_tile(
            lambda start, step, columns, base_ref=base_ref: base_ref[start : start + step, columns],
            put,
            left_ref[...],
            right_ref[...],
            depth,
        )


def merge_pair(triples):
    operands, in_specs, low_specs, low_shapes = [], [], [], []
    width = triples[0][0].shape[1]
    wide = tile_of(width, 512)
    for base, left, right in triples:
        depth, rank = base.shape[0], right.shape[0]
        operands += [base, left, right]
        in_specs += [
            pl.BlockSpec((depth, wide), lambda n: (0, n)),
            pl.BlockSpec((rank, depth), lambda n: (0, 0)),
            pl.BlockSpec((rank, wide), lambda n: (0, n)),
        ]
        low_specs.append(pl.BlockSpec((padded(depth), wide), lambda n: (0, n)))
        low_shapes.append(shape((padded(depth), width), LOW))
    return call(
        "merge_pair",
        merge_pair_kernel,
        tuple(operands),
        (width // wide,),
        in_specs,
        low_specs + [pl.BlockSpec((2, wide), lambda n: (0, n))],
        low_shapes + [shape((2, width), F32)],
        flops=2 * sum(v.size for v in operands) * 256,
    )


def merge_kernel(left_ref, right_ref, *refs):
    *bases, low_ref, squares_ref = refs
    part, width = bases[0].shape[1:]
    if low_ref.shape[2] > width:
        spare = low_ref.shape[2] - width
        low_ref[0, :, width:] = jnp.zeros((low_ref.shape[1], spare), LOW)
        squares_ref[0, :, width:] = jnp.ones((1, spare), F32)
    squares = jnp.zeros((1, width), F32)
    for n, base_ref in enumerate(bases):

        def put(start, step, columns, tile, at=n * part):
            low_ref[0, at + start : at + start + step, columns] = tile

        squares = squares + merge_tile(
            lambda start, step, columns, base_ref=base_ref: base_ref[
                0, start : start + step, columns
            ],
            put,
            left_ref[0, :, n * part : (n + 1) * part],
            right_ref[0],
            part,
        )

    @pl.when(pl.program_id(1) == 0)
    def _():
        squares_ref[0, :, :width] = squares

    @pl.when(pl.program_id(1) > 0)
    def _():
        squares_ref[0, :, :width] += squares


def padded(size):
    return -(-size // 256) * 256


def pad_last(values, size):
    return jnp.pad(values, [(0, 0)] * (values.ndim - 1) + [(0, size - values.shape[-1])])


def merge(base, left, right, deep):
    members, depth, width = base.shape
    rank, wide, cuts = right.shape[1], padded(width), 4
    part = lambda n: pl.BlockSpec(
        (1, deep // cuts, width), functools.partial(lambda n, m, k: (m, cuts * k + n, 0), n)
    )
    return call(
        "merge",
        merge_kernel,
        (left, right, *[base] * cuts),
        (members, depth // deep),
        [
            pl.BlockSpec((1, rank, deep), lambda m, k: (m, 0, k)),
            pl.BlockSpec((1, rank, width), lambda m, k: (m, 0, 0)),
        ]
        + [part(n) for n in range(cuts)],
        [
            pl.BlockSpec((1, deep, wide), lambda m, k: (m, k, 0)),
            pl.BlockSpec((1, 1, wide), lambda m, k: (m, 0, 0)),
        ],
        [shape((members, depth, wide), LOW), shape((members, 1, wide), F32)],
        flops=2 * members * depth * width * 256,
    )


def rms_rows(values):
    return lax.rsqrt(jnp.mean(values * values, axis=1, keepdims=True) + NORM_EPS)


TABLE_STEP = 32


def table_pieces(places):
    half = np.arange(HEAD_DIM) % (HEAD_DIM // 2)
    angles = np.asarray(places)[:, None] * ROPE_BASE ** (-2.0 * half / HEAD_DIM)[None, :]
    rest = np.concatenate([np.cos(angles), np.sin(angles)], axis=1)
    pieces = []
    for _ in range(3):
        pieces.append(rest.astype(ml_dtypes.bfloat16))
        rest = rest - pieces[-1].astype(np.float64)
    return jnp.asarray(np.concatenate(pieces, axis=0))


def rotation(first, coarse, fine):
    rows = first.shape[0]
    position = lax.broadcasted_iota(jnp.int32, (rows, 1), 0) - first
    lane = lax.broadcasted_iota(jnp.int32, (rows, 3 * TABLE_STEP), 1) % TABLE_STEP
    pick = lambda place, table: dot((lane == place).astype(F32).astype(LOW), table)
    high = pick(position // TABLE_STEP, coarse)
    small = pick(position % TABLE_STEP, fine)
    cos_a, sin_a = high[:, :HEAD_DIM], high[:, HEAD_DIM:]
    cos_b, sin_b = small[:, :HEAD_DIM], small[:, HEAD_DIM:]
    sine = sin_a * cos_b + cos_a * sin_b
    left_half = lax.broadcasted_iota(jnp.int32, sine.shape, 1) < HEAD_DIM // 2
    return cos_a * cos_b - sin_a * sin_b, jnp.where(left_half, -sine, sine)


def heads_kernel(
    token_0,
    token_1,
    token_2,
    token_3,
    gain_ref,
    base_ref,
    left_ref,
    right_ref,
    magnitude_ref,
    segment_ref,
    coarse_ref,
    fine_ref,
    part_ref,
    normed_ref,
    low_ref,
    post_ref,
    squares_ref,
    across_ref,
    cos_ref,
    sine_ref,
    output_sum_ref,
    shrink_sum_ref,
    first_ref,
    rows_all,
    part_mine,
    part_got,
    send_sems,
    recv_sems,
):
    total_rows = normed_ref.shape[0]
    depth, width = base_ref.shape[1:]
    rank = right_ref.shape[1]
    groups = part_got.shape[0]
    me = lax.axis_index("mp")
    peers = [lax.rem(me + k, groups) for k in range(groups)]
    part_copies = [
        remote(part_mine, part_got.at[k], send_sems.at[k], recv_sems.at[k], peers[k])
        for k in range(1, groups)
    ]

    @pl.when(pl.program_id(0) == 0)
    def _():
        greet(peers[1:])
        part_mine[...] = part_ref[...]
        step = 128
        quarter = total_rows // 4
        for n, token_ref in enumerate((token_0, token_1, token_2, token_3)):

            def some(i, carry, token_ref=token_ref, start=n * quarter):
                here = pl.ds(pl.multiple_of(i * step, step), step)
                at = pl.ds(pl.multiple_of(start + i * step, step), step)
                values = token_ref[here, :].astype(F32)
                low = (values * rms_rows(values) * gain_ref[...]).astype(LOW)
                normed_ref[at, :] = low
                rows_all[at, :] = low
                return carry

            lax.fori_loop(0, quarter // step, some, 0)
        ids = segment_ref[...].astype(F32)
        ids_down = jnp.transpose(jnp.broadcast_to(ids, (8, total_rows)))[:, :1]
        for start in range(0, total_rows, 256):
            rows = slice(start, start + 256)
            smaller = jnp.where(ids < ids_down[rows], 1.0, 0.0)
            first = jnp.sum(smaller, axis=1, keepdims=True).astype(jnp.int32)
            first_ref[rows, :] = first
            cosine, sine = rotation(first - start, coarse_ref[...], fine_ref[...])
            cos_ref[rows, :] = cosine
            sine_ref[rows, :] = sine
        greeted(groups - 1)
        for copy in part_copies:
            copy.start()

    @pl.when(pl.program_id(0) == pl.num_programs(0) - 1)
    def _():
        total = part_mine[...]
        for k, copy in enumerate(part_copies, 1):
            copy.wait_recv()
            total = total + part_got[k]
        output_sum_ref[0] = total[:1]
        shrink_sum_ref[0] = total[1:]
        for copy in part_copies:
            copy.wait_send()

    rows_all[total_rows:, :] = left_ref[0].astype(LOW)
    turning = pl.program_id(0) < 2
    wide = 256

    def put(start, step, columns, tile):
        low_ref[0, start : start + step, columns] = tile

    squares_ref[0] = merge_tile(
        lambda start, step, columns: base_ref[0, start : start + step, columns],
        put,
        left_ref[0],
        right_ref[0],
        depth,
    )
    for column in range(0, width, wide):
        columns = slice(column, column + wide)
        magnitude = magnitude_ref[pl.ds(pl.program_id(0), 1), columns]
        scale = magnitude / jnp.sqrt(squares_ref[0, :, columns])
        low = low_ref[0, :, columns]
        step = min(512, total_rows)
        for start in range(0, total_rows, step):
            last = start + step == total_rows
            rows = slice(start, start + step)
            pre = dot(rows_all[start : start + step + (rank if last else 0), :], low)
            if last:
                across_ref[0, :, columns] = pre[step:]
            post = pre[:step] * scale
            cos_table = jnp.where(turning, cos_ref[rows, :], 1.0)
            sine_table = jnp.where(turning, sine_ref[rows, :], 0.0)
            for head in range(0, wide, HEAD_DIM):
                piece = post[:, head : head + HEAD_DIM]
                other = pltpu.roll(piece, HEAD_DIM // 2, 1)
                post_ref[0, rows, column + head : column + head + HEAD_DIM] = (
                    piece * cos_table + other * sine_table
                ).astype(LOW)


def project_heads(tokens, gain, base, left, right, magnitude, segments, part, groups):
    members, depth, width = base.shape
    rows, rank = tokens.shape[0], right.shape[1]
    coarse = table_pieces(np.arange(TABLE_STEP) * TABLE_STEP)
    fine = table_pieces(np.arange(TABLE_STEP))
    whole = lambda v: pl.BlockSpec(v.shape, lambda m: (0,) * v.ndim)
    of_member = lambda *dims: pl.BlockSpec((1,) + dims, lambda m: (m, 0, 0))
    table = pl.BlockSpec((rows, HEAD_DIM), lambda m: (0, 0))
    return call(
        "project_heads",
        heads_kernel,
        (*[tokens] * 4, gain, base, left, right, magnitude, segments, coarse, fine, part),
        (members,),
        [pl.BlockSpec((rows // 4, depth), functools.partial(lambda n, m: (n, 0), n)) for n in range(4)]
        + [
            whole(gain),
            of_member(depth, width),
            of_member(rank, depth),
            of_member(rank, width),
            whole(magnitude),
            whole(segments),
            whole(coarse),
            whole(fine),
            whole(part),
        ],
        [
            whole(tokens),
            of_member(depth, width),
            of_member(rows, width),
            of_member(1, width),
            of_member(rank, width),
            table,
            table,
            pl.BlockSpec((1, 1, depth), lambda m: (0, 0, 0)),
            pl.BlockSpec((1, 1, depth), lambda m: (0, 0, 0)),
            pl.BlockSpec((rows, 1), lambda m: (0, 0)),
        ],
        [
            shape((rows, depth), LOW),
            shape(base.shape, LOW),
            shape((members, rows, width), LOW),
            shape((members, 1, width), F32),
            shape((members, rank, width), F32),
            shape((rows, HEAD_DIM), F32),
            shape((rows, HEAD_DIM), F32),
            shape((1, 1, depth), F32),
            shape((1, 1, depth), F32),
            shape((rows, 1), jnp.int32),
        ],
        scratch=[
            pltpu.VMEM((rows + rank, depth), LOW),
            pltpu.VMEM(part.shape, F32),
            pltpu.VMEM((groups,) + part.shape, F32),
            pltpu.SemaphoreType.DMA((groups,)),
            pltpu.SemaphoreType.DMA((groups,)),
        ],
        identity=2,
        flops=2 * members * rows * depth * width,
    )


def key_start(block):
    return max(0, (block * ATTEND_BLOCK - (LONGEST - 1)) // ATTEND_BLOCK * ATTEND_BLOCK)


def masked_probs(scores, first, row_at, key_at):
    scores = scores * HEAD_DIM ** (-0.5)
    places = row_at + lax.broadcasted_iota(jnp.int32, scores.shape, 0)
    others = key_at + lax.broadcasted_iota(jnp.int32, scores.shape, 1)
    scores = jnp.where((others >= first) & (others <= places), scores, MASKED)
    exp_scores = jnp.exp(scores - jnp.max(scores, axis=1, keepdims=True))
    return exp_scores * (1.0 / jnp.sum(exp_scores, axis=1, keepdims=True))


class Unit:
    def __init__(self, head, block):
        self.row_at, self.key_at = block * ATTEND_BLOCK, key_start(block)
        self.rows = slice(self.row_at, self.row_at + ATTEND_BLOCK)
        self.keys = slice(self.key_at, self.row_at + ATTEND_BLOCK)
        self.lanes = slice(head * HEAD_DIM, (head + 1) * HEAD_DIM)


def units_of(rows, width, most):
    units = [
        Unit(head, block)
        for block in range(rows // ATTEND_BLOCK)
        for head in range(width // HEAD_DIM)
    ]
    return [units[at : at + most] for at in range(0, len(units), most)]


def put_rows(ref, lead, row_at, lanes, values, order_ref, groups):
    share = ref.shape[len(lead)] // groups
    step = min(share, values.shape[0])
    for start in range(0, values.shape[0], step):
        group = (row_at + start) // share
        inside = (row_at + start) % share
        at = pl.multiple_of(order_ref[groups + group] * share + inside, step)
        ref[(*lead, pl.ds(at, step), lanes)] = values[start : start + step].astype(ref.dtype)


def attend_kernel(groups, order_ref, query_ref, key_ref, value_ref, first_ref, out_ref):
    for some in units_of(*query_ref.shape[1:], 4):
        scores = [
            dot(query_ref[0, u.rows, u.lanes], key_ref[0, u.keys, u.lanes], NT) for u in some
        ]
        probs = [
            masked_probs(s, first_ref[u.rows, :], u.row_at, u.key_at).astype(LOW)
            for u, s in zip(some, scores)
        ]
        for u, p in zip(some, probs):
            mixed = dot(p, value_ref[0, u.keys, u.lanes])
            put_rows(out_ref, (), u.row_at, u.lanes, mixed, order_ref, groups)


def attend(order, groups, post, first):
    rows, width = post.shape[1:]
    wide = 2 * HEAD_DIM
    member = lambda m: pl.BlockSpec((1, rows, wide), lambda h, o: (m, 0, h))
    return call(
        "attend",
        functools.partial(attend_kernel, groups),
        (post, post, post, first),
        (width // wide,),
        [member(0), member(1), member(2), pl.BlockSpec((rows, 1), lambda h, o: (0, 0))],
        [pl.BlockSpec((rows, wide), lambda h, o: (0, h))],
        [shape((rows, width), LOW)],
        prefetch=(order,),
        flops=4 * rows * rows * width,
    )[0]


def heads_near_kernel(*refs):
    *pieces, low_ref, out_ref = refs
    for place, piece in enumerate(pieces):
        out_ref[place] = dot(piece[...], low_ref[0], NT).astype(LOW)


def heads_near(pieces, low):
    share, depth = pieces[0].shape
    width = low.shape[1]
    full = lambda v: pl.BlockSpec(v.shape, lambda i: (0,) * len(v.shape))
    out = shape((len(pieces), share, width), LOW)
    return call(
        "heads_near",
        heads_near_kernel,
        (*pieces, low),
        (1,),
        [full(v) for v in (*pieces, low)],
        [full(out)],
        [out],
        flops=2 * len(pieces) * share * depth * width,
    )[0]


def attend_back_kernel(
    groups,
    order_ref,
    query_ref,
    key_ref,
    value_ref,
    first_ref,
    cos_ref,
    sine_ref,
    magnitude_ref,
    squares_ref,
    low_ref,
    near_ref,
    *rest,
):
    pieces, (grad_ref, total_ref, upper_all, heads_grad, key_grad, value_grad, sems) = rest[:-7], rest[-7:]
    rows_all, width = query_ref.shape[1:]
    share = rows_all // groups

    @pl.when(pl.program_id(0) == 0)
    def _():
        copies = [
            pltpu.make_async_copy(piece, upper_all.at[pl.ds(n * share, share), :], sems.at[n])
            for n, piece in enumerate(pieces)
        ]
        for copy in copies:
            copy.start()
        for copy in copies:
            copy.wait()

    far = dot(upper_all[...], low_ref[0], NT).astype(LOW)
    for place in range(groups):
        at = pl.ds(pl.multiple_of(order_ref[place] * share, share), share)
        n = place - CORES
        heads_grad[at, :] = near_ref[place] if n < 0 else far[n * share : (n + 1) * share]
    norm = [jnp.sqrt(squares_ref[m]) for m in range(3)]
    scale = [magnitude_ref[m : m + 1] / norm[m] for m in range(3)]
    heads = range(0, width, HEAD_DIM)
    totals = [jnp.zeros((1, width), F32) for _ in range(3)]
    filled = set()

    def back(values, rows):
        return values * cos_ref[rows, :] - pltpu.roll(values, HEAD_DIM // 2, 1) * sine_ref[rows, :]

    def add(ref, unit, values):
        for start in range(0, values.shape[0], ATTEND_BLOCK):
            at = unit.key_at + start
            rows = slice(at, at + ATTEND_BLOCK)
            name = (id(ref), at, unit.lanes.start)
            if name in filled:
                ref[rows, unit.lanes] += values[start : start + ATTEND_BLOCK]
            else:
                filled.add(name)
                ref[rows, unit.lanes] = values[start : start + ATTEND_BLOCK]

    def spread(per_head):
        return jnp.concatenate(per_head, axis=1)

    query_totals = [jnp.zeros((1, HEAD_DIM), F32) for _ in heads]
    for some in units_of(rows_all, width, 2):
        scores = [
            dot(query_ref[0, u.rows, u.lanes], key_ref[0, u.keys, u.lanes], NT) for u in some
        ]
        grad_weights = [
            dot(heads_grad[u.rows, u.lanes], value_ref[0, u.keys, u.lanes], NT) for u in some
        ]
        probs = [
            masked_probs(s, first_ref[u.rows, :], u.row_at, u.key_at)
            for u, s in zip(some, scores)
        ]
        grad_scores = [
            (p * (g - jnp.sum(p * g, axis=1, keepdims=True))).astype(LOW)
            for p, g in zip(probs, grad_weights)
        ]
        for u, p, g in zip(some, probs, grad_scores):
            add(value_grad, u, dot(p.astype(LOW), heads_grad[u.rows, u.lanes], TN))
            add(key_grad, u, dot(g, query_ref[0, u.rows, u.lanes], TN))
        for u, g in zip(some, grad_scores):
            grad = back(dot(g, key_ref[0, u.keys, u.lanes]) * HEAD_DIM ** (-0.5), u.rows)
            head = u.lanes.start // HEAD_DIM
            post = back(query_ref[0, u.rows, u.lanes].astype(F32), u.rows)
            query_totals[head] = query_totals[head] + jnp.sum(grad * post, axis=0, keepdims=True)
            put_rows(grad_ref, (0,), u.row_at, u.lanes, grad * scale[0][:, u.lanes], order_ref, groups)
    totals[0] = spread(query_totals)
    for row_at in range(0, rows_all, ATTEND_BLOCK):
        rows = slice(row_at, row_at + ATTEND_BLOCK)
        for head in heads:
            lanes = slice(head, head + HEAD_DIM)
            grad = back(key_grad[rows, lanes] * HEAD_DIM ** (-0.5), rows)
            post = back(key_ref[0, rows, lanes].astype(F32), rows)
            part = jnp.sum(grad * post, axis=0, keepdims=True)
            query_totals[head // HEAD_DIM] = part if row_at == 0 else query_totals[head // HEAD_DIM] + part
            put_rows(grad_ref, (1,), row_at, lanes, grad * scale[1][:, lanes], order_ref, groups)
        grad = value_grad[rows, :]
        totals[2] = totals[2] + jnp.sum(grad * value_ref[0, rows, :].astype(F32), axis=0, keepdims=True)
        put_rows(grad_ref, (2,), row_at, slice(0, width), grad * scale[2], order_ref, groups)
    totals[1] = spread(query_totals)
    for m in range(3):
        total_ref[m] = totals[m] / scale[m]


def attend_back(order, groups, post, first, cos_table, sine_table, magnitude, squares, low, near, pieces):
    rows, width = post.shape[1:]
    depth = low.shape[2]
    wide = 2 * HEAD_DIM
    member = lambda m: pl.BlockSpec((1, rows, wide), lambda h, o: (m, 0, h))
    table = pl.BlockSpec((rows, HEAD_DIM), lambda h, o: (0, 0))
    column = pl.BlockSpec((3, 1, wide), lambda h, o: (0, 0, h))
    return call(
        "attend_back",
        functools.partial(attend_back_kernel, groups),
        (post, post, post, first, cos_table, sine_table, magnitude, squares, low, near, *pieces),
        (width // wide,),
        [
            member(0),
            member(1),
            member(2),
            pl.BlockSpec((rows, 1), lambda h, o: (0, 0)),
            table,
            table,
            pl.BlockSpec((3, wide), lambda h, o: (0, h)),
            column,
            pl.BlockSpec((1, wide, depth), lambda h, o: (0, h, 0)),
            pl.BlockSpec((CORES, near.shape[1], wide), lambda h, o: (0, 0, h)),
            *[pl.BlockSpec(memory_space=pl.ANY) for _ in pieces],
        ],
        [pl.BlockSpec((3, rows, wide), lambda h, o: (0, 0, h)), column],
        [shape((3, rows, width), LOW), shape((3, 1, width), F32)],
        scratch=[
            pltpu.VMEM((len(pieces) * near.shape[1], depth), LOW),
            pltpu.VMEM((rows, wide), LOW),
            pltpu.VMEM((rows, wide), F32),
            pltpu.VMEM((rows, wide), F32),
            pltpu.SemaphoreType.DMA((len(pieces),)),
        ],
        prefetch=(order,),
        flops=10 * rows * rows * width + 2 * rows * width * depth,
    )


def product_kernel(dims, n_totals, n_lines, has_gain, steps, *refs):
    value_ref, weight_ref = refs[:2]
    if n_totals == 0:
        left_ref, *refs = refs[2:]
    else:
        right_ref, squares_ref, magnitude_ref = refs[2:5]
        totals, refs = refs[5 : 5 + n_totals], refs[5 + n_totals :]
    lines = []
    if has_gain:
        normed_ref, gain_ref, *refs = refs
    if n_lines > 0:
        lines, refs = refs[:n_lines], refs[n_lines:]
        *refs, line_mine, line_got, line_send_sems, line_recv_sems = refs
    *outs, extra_ref, rows_all, sent, got, send_sems, recv_sems = refs
    if has_gain:
        *outs, gain_out = outs
    line_outs, outs = outs[len(outs) - n_lines :], outs[: len(outs) - n_lines]
    members, groups, share, inner = value_ref.shape
    count, wide = groups * share, extra_ref.shape[2]
    now = pl.program_id(0)
    sibling = sibling_id()
    me = lax.axis_index("mp")
    peers = [lax.rem(me + k, groups) for k in range(1, groups)] if n_lines > 0 else [sibling]
    line_copies = [
        remote(line_mine, line_got.at[k], line_send_sems.at[k], line_recv_sems.at[k], peer)
        for k, peer in enumerate(peers if n_lines > 0 else [], 1)
    ]

    @pl.when(now == 0)
    def _():
        greet(peers)
        for n, ref in enumerate(lines):
            line_mine[n : n + 1, :] = ref[...]
        if n_totals > 0:
            total = sum_refs(totals)
        for m in range(members):
            rows_all[m, :count, :] = value_ref[m].reshape(count, inner)
            if n_totals == 0:
                rows_all[m, count:, :] = left_ref[m].astype(LOW)
            else:
                weight = norm_weight(total[m], squares_ref[m], magnitude_ref[m : m + 1])
                rows_all[m, count:, :] = (right_ref[m] * weight).astype(LOW)

    result = None
    for m in range(members):
        part = dot(rows_all[m], weight_ref[m], dims)
        extra_ref[m] = part[count:]
        result = part[:count] if result is None else result + part[:count]

    def columns(step):
        return pl.ds(pl.multiple_of(step * wide, wide), wide)

    def copy(step):
        return remote(sent.at[step], got.at[step], send_sems.at[step], recv_sems.at[step], sibling)

    def add(step):
        copy(step).wait_recv()
        for n, ref in enumerate(outs):
            total = ref[:, columns(step)].astype(F32) + got[step, n].astype(F32)
            ref[:, columns(step)] = total.astype(LOW)

    if has_gain:
        terms = jnp.zeros((1, wide), F32)
        for place in range(groups):
            group = lax.rem(me // CORES + place // CORES, groups // CORES) * CORES
            group = group + lax.rem(me + 1 + place, CORES)
            rows = pl.ds(pl.multiple_of(group * share, share), share)
            mine = result[place * share : (place + 1) * share]
            terms = terms + jnp.sum(
                mine * normed_ref[rows, :].astype(F32), axis=0, keepdims=True
            )
        gain_out[...] = terms / gain_ref[...]
    for n, ref in enumerate(outs):
        at = CORES * n * share
        sent[now, n] = result[at : at + share].astype(LOW)
        ref[:, columns(now)] = result[at + share : at + CORES * share].astype(LOW)

    @pl.when(now == 0)
    def _():
        greeted(len(peers))
        for each in line_copies:
            each.start()

    copy(now).start()

    @pl.when(now > 0)
    def _():
        add(now - 1)

    @pl.when(now == steps - 1)
    def _():
        add(now)
        for step in range(steps):
            copy(step).wait_send()
        if n_lines > 0:
            line_sum = line_mine[...]
            for k, each in enumerate(line_copies, 1):
                each.wait_recv()
                line_sum = line_sum + line_got[k]
            for n, ref in enumerate(line_outs):
                ref[0] = line_sum[n : n + 1]
            for each in line_copies:
                each.wait_send()


def product(name, identity, values, weights, dims, left=None, correction=None, lines=(), gain=()):
    members, groups, share, inner = values.shape
    chips = groups // CORES
    width = weights.shape[2] if dims is NN else weights.shape[1]
    wide = tile_of(width, 512)
    steps = width // wide
    if dims is NN:
        weight_spec = pl.BlockSpec((members, inner, wide), lambda n: (0, 0, n))
    else:
        weight_spec = pl.BlockSpec((members, wide, inner), lambda n: (0, n, 0))
    if correction is None:
        extra, n_totals, rank = (left,), 0, left.shape[1]
    else:
        right, squares, magnitude, totals = correction
        extra, n_totals, rank = (right, squares, magnitude, *totals), len(totals), right.shape[1]
    fixed = lambda v: pl.BlockSpec(v.shape, lambda n: (0,) * v.ndim)
    out = pl.BlockSpec((share, width), lambda n: (0, 0))
    line_specs, line_shapes, line_scratch = [], [], []
    if lines:
        line = (len(lines), width)
        line_specs = [pl.BlockSpec((1, 1, width), lambda n: (0, 0, 0)) for _ in lines]
        line_shapes = [shape((1, 1, width), F32) for _ in lines]
        line_scratch = [
            pltpu.VMEM(line, F32),
            pltpu.VMEM((groups,) + line, F32),
            pltpu.SemaphoreType.DMA((groups,)),
            pltpu.SemaphoreType.DMA((groups,)),
        ]
    gain_specs, gain_shapes, gain_in = [], [], []
    if gain:
        one = pl.BlockSpec((1, wide), lambda n: (0, n))
        gain_in = [pl.BlockSpec((gain[0].shape[0], wide), lambda n: (0, n)), one]
        gain_specs, gain_shapes = [one], [shape((1, width), F32)]
    results = call(
        name,
        functools.partial(product_kernel, dims, n_totals, len(lines), bool(gain), steps),
        (values, weights, *extra, *gain, *lines),
        (steps,),
        [fixed(values), weight_spec]
        + [fixed(v) for v in extra]
        + gain_in
        + [fixed(v) for v in lines],
        [out] * chips + line_specs + gain_specs + [pl.BlockSpec((members, rank, wide), lambda n: (0, 0, n))],
        [shape((share, width), LOW)] * chips
        + line_shapes
        + gain_shapes
        + [shape((members, rank, width), F32)],
        scratch=[
            pltpu.VMEM((members, groups * share + rank, inner), LOW),
            pltpu.VMEM((steps, chips, share, wide), LOW),
            pltpu.VMEM((steps, chips, share, wide), LOW),
            pltpu.SemaphoreType.DMA((steps,)),
            pltpu.SemaphoreType.DMA((steps,)),
        ]
        + line_scratch,
        flops=2 * members * groups * share * inner * width,
        identity=identity,
    )
    return results[:chips], *results[chips:]


def shrink_kernel(chips, order_ref, *refs):
    values, (weight_ref, left_ref, cot_ref), outs = refs[:chips], refs[chips : chips + 3], refs[chips + 3 :]
    total_ref, across_ref, rows_all = outs[-3:]
    both, inner = values[0].shape
    share, depth = both // CORES, left_ref.shape[2]
    count = chips * both

    @pl.when(pl.program_id(0) == 0)
    def _():
        for step, ref in enumerate(values):
            rows_all[step * both : (step + 1) * both, :] = ref[...]
        if inner > depth:
            rows_all[count:, depth:] = jnp.zeros((rows_all.shape[0] - count, inner - depth), LOW)
        rows_all[count:, :depth] = left_ref[0].astype(LOW)

    result = dot(rows_all[...], weight_ref[0])
    across_ref[0] = result[count:]
    total = jnp.zeros((1, weight_ref.shape[2]), F32)
    for place in range(chips * CORES):
        pre = result[place * share : (place + 1) * share]
        outs[place][...] = pre.astype(LOW)
        at = pl.multiple_of(order_ref[place] * share, share)
        cot = cot_ref[pl.ds(at, share), :].astype(F32)
        total = total + jnp.sum(pre * cot, axis=0, keepdims=True)
    total_ref[...] = total


def shrink_product(order, values, weights, left, cotangent):
    chips = len(values)
    share, inner = values[0].shape[0] // CORES, values[0].shape[1]
    width, rank = weights.shape[2], left.shape[1]
    rows = chips * CORES * share
    wide = tile_of(width, 512)
    fixed = lambda v: pl.BlockSpec(v.shape, lambda n, o: (0,) * v.ndim)
    results = call(
        "shrink_product",
        functools.partial(shrink_kernel, chips),
        (*values, weights, left, cotangent),
        (width // wide,),
        [fixed(v) for v in values]
        + [
            pl.BlockSpec((1, inner, wide), lambda n, o: (0, 0, n)),
            fixed(left),
            pl.BlockSpec((rows, wide), lambda n, o: (0, n)),
        ],
        [pl.BlockSpec((share, wide), lambda n, o: (0, n))] * (chips * CORES)
        + [
            pl.BlockSpec((1, wide), lambda n, o: (0, n)),
            pl.BlockSpec((1, rank, wide), lambda n, o: (0, 0, n)),
        ],
        [shape((share, width), LOW)] * (chips * CORES)
        + [shape((1, width), F32), shape((1, rank, width), F32)],
        scratch=[pltpu.VMEM((rows + rank, inner), LOW)],
        prefetch=(order,),
        flops=2 * rows * inner * width,
    )
    return results[: chips * CORES], results[-2], results[-1]


def row_call(name, kernel, order, given, whole, out_kinds, sums, prepare):
    share = min(v.shape[0] for v, _ in given)
    width = given[0][0].shape[1]
    halves = 2
    half = share // halves
    count = len(given)

    def run(order_ref, *refs):
        sources, rest = refs[:count], refs[count : -count - 1]
        held, sems = refs[-count - 1 : -1], refs[-1]

        def copies(part):
            for i, ((_, cut), source, target) in enumerate(zip(given, sources, held)):
                at = part * half
                if cut:
                    at = pl.multiple_of(order_ref[1] * share + at, half)
                yield pltpu.make_async_copy(
                    source.at[pl.ds(at, half), :],
                    target.at[pl.ds(part * half, half), :],
                    sems.at[part, i],
                )

        for part in range(halves):

            @pl.when(pl.program_id(0) == part)
            def _(part=part):
                if part == 0:
                    for each in range(halves):
                        for copy in copies(each):
                            copy.start()
                for copy in copies(part):
                    copy.wait()

        outs = rest[len(whole) : len(whole) + len(out_kinds)]
        totals, sums_held = rest[len(whole) + len(out_kinds) :][:sums], rest[len(rest) - sums :]
        tile = 32
        lines = prepare(*[ref[...] for ref in rest[: len(whole)]])
        for ref in sums_held:
            ref[...] = jnp.zeros_like(ref)

        def some(i, carry):
            inside = pl.ds(pl.multiple_of(i * tile, tile), tile)
            at = pl.ds(pl.multiple_of(pl.program_id(0) * half + i * tile, tile), tile)
            values = kernel([ref[at, :].astype(F32) for ref in held], *lines)
            for ref, value in zip(outs, values):
                ref[inside, :] = value.astype(ref.dtype)
            for ref, value in zip(sums_held, values[len(outs) :]):
                ref[...] += jnp.sum(value.reshape(tile // 8, 8, width), axis=0)
            return carry

        lax.fori_loop(0, half // tile, some, 0, unroll=2)
        for ref, held_ref in zip(totals, sums_held):
            add_column(ref, held_ref[...])

    line = pl.BlockSpec((1, width), lambda i, o: (0, 0))
    return call(
        name,
        run,
        (*[v for v, _ in given], *whole),
        (halves,),
        [pl.BlockSpec(memory_space=pl.ANY) for _ in given] + [line for _ in whole],
        [pl.BlockSpec((half, width), lambda i, o: (i, 0)) for _ in out_kinds]
        + [line for _ in range(sums)],
        [shape((share, width), kind) for kind in out_kinds]
        + [shape((1, width), F32) for _ in range(sums)],
        scratch=[pltpu.VMEM((8, width), F32) for _ in range(sums)]
        + [pltpu.VMEM((share, width), v.dtype) for v, _ in given]
        + [pltpu.SemaphoreType.DMA((halves, count))],
        prefetch=(order,),
        flops=20 * share * width,
    )


def sum_of(values):
    total = values[0]
    for value in values[1:]:
        total = total + value
    return total


def add_column(ref, values):
    part = jnp.sum(values, axis=0, keepdims=True)

    @pl.when(pl.program_id(0) == 0)
    def _():
        ref[...] = part

    @pl.when(pl.program_id(0) > 0)
    def _():
        ref[...] += part


def scale_first(squares, magnitude, *rest):
    norm = jnp.sqrt(squares)
    return (magnitude / norm, norm / magnitude, *rest)


def hidden_kernel(given, scale, inverse, gain):
    hidden = given[0] + sum_of(given[1:]) * scale
    return hidden, hidden * rms_rows(hidden) * gain


def mixed_kernel(given, scale, inverse):
    return (given[0] + sum_of(given[1:]) * scale,)


def norm_back(grad_normed, values, gain):
    factor = rms_rows(values)
    scaled = grad_normed * gain
    inner = jnp.mean(scaled * values, axis=1, keepdims=True)
    back = factor * scaled - values * (factor * factor * factor * inner)
    return back, grad_normed * values * factor


def hidden_back_kernel(given, scale, inverse, gain):
    cot, token, hidden = given[:3]
    back, gain_terms = norm_back(sum_of(given[3:]), hidden, gain)
    grad = cot + back
    return grad, grad * scale, grad * ((hidden - token) * inverse), gain_terms


def shrink_back_kernel(places, order_ref, *refs):
    cots, refs = refs[:places], refs[places:]
    *lows, squares_ref, magnitude_ref, product_ref, grad_ref, rows_all = refs
    scale = magnitude_ref[0] / jnp.sqrt(squares_ref[0])
    share = cots[0].shape[0]
    for place, cot_ref in enumerate(cots):
        grad = (cot_ref[...].astype(F32) * scale).astype(LOW)
        grad_ref[place] = grad
        rows_all[place * share : (place + 1) * share, :] = grad
    wide = lows[0].shape[1]
    for n, low_ref in enumerate(lows):
        result = dot(rows_all[...], low_ref[0], NT).astype(LOW)
        for place in range(places):
            product_ref[place, :, n * wide : (n + 1) * wide] = result[
                place * share : (place + 1) * share
            ]


def shrink_back(order, cotangent, low, squares, magnitude, groups):
    rows, width = cotangent.shape
    share, inner = rows // groups, low.shape[1]
    places, cuts = CORES, 3
    line = pl.BlockSpec((1, 1, width), lambda j, o: (0, 0, 0))
    cot = lambda place: pl.BlockSpec((share, width), lambda j, o: (o[places * j + place], 0))
    return call(
        "shrink_back",
        functools.partial(shrink_back_kernel, places),
        (*[cotangent] * places, *[low] * cuts, squares, magnitude),
        (groups // places,),
        [cot(place) for place in range(places)]
        + [
            pl.BlockSpec((1, inner // cuts, width), functools.partial(lambda n, j, o: (0, n, 0), n))
            for n in range(cuts)
        ]
        + [line, line],
        [
            pl.BlockSpec((places, share, inner), lambda j, o: (j, 0, 0)),
            pl.BlockSpec((places, share, width), lambda j, o: (j, 0, 0)),
        ],
        [shape((groups, share, inner), LOW), shape((groups, share, width), LOW)],
        scratch=[pltpu.VMEM((places * share, width), LOW)],
        prefetch=(order,),
        flops=2 * rows * width * inner,
    )


def expand_kernel(step, first, last, n_totals, *refs):
    mine_ref, low_ref, grad_ref, squares_ref, magnitude_ref = refs[:5]
    refs = list(refs[5:])
    left_ref = refs.pop(0) if first else None
    right_ref = refs.pop(0) if last else None
    before = [refs.pop(0) for _ in range(n_totals)]
    product_ref, back_ref, rows_ref, total_ref, joined_ref = refs[:5]
    refs = refs[5:]
    across_ref = refs.pop(0) if first else None
    extra_ref = refs.pop(0) if last else None
    rows_all, low_all, grad_all, product_all, back_all, sent, got, in_sems, out_sems, send_sems, recv_sems = refs
    share, depth = mine_ref.shape
    sibling = sibling_id()
    greet([sibling])
    both = CORES * share
    width, ff = low_ref.shape[2], magnitude_ref.shape[1]
    tile = 256
    cuts = [slice(at, at + tile) for at in range(0, width, tile)]

    mine_copy = pltpu.make_async_copy(mine_ref, rows_all.at[pl.ds(share, share), :], in_sems.at[0])
    other_copy = remote(
        mine_ref,
        rows_all.at[pl.ds(0, share), :],
        send_sems.at[sent.shape[0]],
        recv_sems.at[sent.shape[0]],
        sibling,
    )
    tile_copies = []
    for n, cut in enumerate(cuts):
        lanes = pl.ds(cut.start, tile)
        tile_copies.append(
            [
                pltpu.make_async_copy(
                    low_ref.at[:, :, lanes], low_all.at[:, :, lanes], in_sems.at[2 + 2 * n]
                ),
                pltpu.make_async_copy(
                    grad_ref.at[pl.ds(CORES * step, CORES), :, lanes],
                    grad_all.at[:, :, lanes],
                    in_sems.at[3 + 2 * n],
                ),
            ]
        )
    mine_copy.start()
    for copy in tile_copies[0]:
        copy.start()
    greeted(1)
    other_copy.start()
    for copies in tile_copies[1:]:
        for copy in copies:
            copy.start()
    if first:
        rank = across_ref.shape[1]
        for m in range(2):
            rows_all[both + m * rank : both + (m + 1) * rank, :] = left_ref[m].astype(LOW)
    mine_copy.wait()
    other_copy.wait_recv()
    out_copies = [
        pltpu.make_async_copy(rows_all.at[pl.ds(0, both), :], rows_ref, out_sems.at[2 * len(cuts)])
    ]
    out_copies[0].start()
    lane = lax.broadcasted_iota(jnp.int32, (1, tile), 1)
    for n, cut in enumerate(cuts):
        for copy in tile_copies[n]:
            copy.wait()
        size = min(tile, ff - cut.start)
        pre = [dot(rows_all[...], low_all[m, :, cut]) for m in range(2)]
        if first:
            for m in range(2):
                rows = slice(both + m * rank, both + (m + 1) * rank)
                across_ref[m, :, cut.start : cut.start + size] = pre[m][rows, :size]
        magnitude, squares, scale = [], [], []
        for m in range(2):
            given = magnitude_ref[m : m + 1, cut.start : cut.start + size]
            if size < tile:
                given = jnp.concatenate([given, jnp.zeros((1, tile - size), F32)], axis=1)
            magnitude.append(given)
            squares.append(squares_ref[m, :, cut])
            scale.append(given / jnp.sqrt(squares[m]))
        sums = [jnp.zeros((1, tile), F32) for _ in range(2)]
        at = [slice(m * width + cut.start, m * width + cut.stop) for m in range(2)]
        for place in range(CORES):
            rows = slice(place * share, (place + 1) * share)
            gate_pre, up_pre = pre[0][rows], pre[1][rows]
            gate, up = gate_pre * scale[0], up_pre * scale[1]
            sigmoid = 0.5 + 0.5 * jnp.tanh(0.5 * gate)
            active = gate * sigmoid
            product_all[rows, cut] = (active * up).astype(LOW)
            upper = grad_all[place, :, cut].astype(F32)
            grad_up = upper * active
            grad_gate = upper * up * sigmoid * (1.0 + gate * (1.0 - sigmoid))
            sums[0] += jnp.sum(grad_gate * gate_pre, axis=0, keepdims=True)
            sums[1] += jnp.sum(grad_up * up_pre, axis=0, keepdims=True)
            back_all[rows, at[0]] = (grad_gate * scale[0]).astype(LOW)
            back_all[rows, at[1]] = (grad_up * scale[1]).astype(LOW)
        for m in range(2):
            total_ref[m, :, cut] = sums[m]
        if last:
            rank = extra_ref.shape[1]
            for m in range(2):
                total = sums[m]
                for ref in before:
                    total = total + ref[m, :, cut]
                right = right_ref[m, :, cut.start : cut.start + size]
                if size < tile:
                    spare = jnp.zeros((rank, tile - size), F32)
                    right = jnp.concatenate([right, spare], axis=1)
                weighted = right * norm_weight(total, squares[m], magnitude[m])
                rows = slice(both + m * rank, both + (m + 1) * rank)
                back_all[rows, at[m]] = weighted.astype(LOW)
                back_all[rows, at[1 - m]] = jnp.zeros((rank, tile), LOW)
    for m in range(2):
        lanes = pl.ds(m * width, width)
        copy = pltpu.make_async_copy(
            back_all.at[pl.ds(0, both), lanes], back_ref.at[m], out_sems.at[m]
        )
        copy.start()
        out_copies.append(copy)
    copy = pltpu.make_async_copy(product_all, product_ref, out_sems.at[2])
    copy.start()
    out_copies.append(copy)
    chunk = sent.shape[2]
    copies = [
        remote(sent.at[n], got.at[n], send_sems.at[n], recv_sems.at[n], sibling)
        for n in range(depth // chunk)
    ]

    def add(n):
        columns = slice(n * chunk, (n + 1) * chunk)
        copies[n].wait_recv()
        total = joined_ref[:, columns].astype(F32) + got[n].astype(F32)
        joined_ref[:, columns] = total.astype(LOW)

    for n in range(depth // chunk):
        columns = slice(n * chunk, (n + 1) * chunk)
        result = dot(back_all[:, :width], low_all[0, columns, :], NT)
        result = result + dot(back_all[:, width:], low_all[1, columns, :], NT)
        sent[n] = result[:share].astype(LOW)
        joined_ref[:, columns] = result[share:both].astype(LOW)
        copies[n].start()
        if n > 0:
            add(n - 1)
        if last:
            for m in range(2):
                extra_ref[m, :, columns] = result[both + m * rank : both + (m + 1) * rank]
    add(len(copies) - 1)
    for copy in out_copies:
        copy.wait()
    for copy in [other_copy, *copies]:
        copy.wait_send()


def expand(identity, mine, low, squares, magnitude, grad_product, step, left=None, right=None, before=()):
    share, depth = mine.shape
    width = low.shape[2]
    first, last = left is not None, right is not None
    rows = CORES * share
    hbm = pl.BlockSpec(memory_space=pl.ANY)
    fixed = lambda dims: pl.BlockSpec(tuple(dims), lambda i: (0,) * len(dims))
    operands = [mine, low, grad_product, squares, magnitude]
    in_specs = [hbm, hbm, hbm, fixed(squares.shape), fixed(magnitude.shape)]
    out_shape = [
        shape((rows, width), LOW),
        shape((2, rows, width), LOW),
        shape((rows, depth), LOW),
        shape((2, 1, width), F32),
        shape((share, depth), LOW),
    ]
    out_specs = [hbm, hbm, hbm] + [fixed(v.shape) for v in out_shape[3:]]
    extra_in = extra_out = 0
    if first:
        rank = left.shape[1]
        extra_in = 2 * rank
        operands.append(left)
        in_specs.append(fixed(left.shape))
        out_shape.append(shape((2, rank, magnitude.shape[1]), F32))
        out_specs.append(fixed(out_shape[-1].shape))
    if last:
        rank = right.shape[1]
        extra_out = 2 * rank
        operands += [right, *before]
        in_specs += [fixed(v.shape) for v in (right, *before)]
        out_shape.append(shape((2, rank, depth), F32))
        out_specs.append(fixed(out_shape[-1].shape))
    tiles, chunk = width // 256, tile_of(depth, 512)
    return call(
        "expand",
        functools.partial(expand_kernel, step, first, last, len(before)),
        tuple(operands),
        (1,),
        in_specs,
        out_specs,
        out_shape,
        scratch=[
            pltpu.VMEM((rows + extra_in, depth), LOW),
            pltpu.VMEM(low.shape, LOW),
            pltpu.VMEM((CORES, share, width), LOW),
            pltpu.VMEM((rows, width), LOW),
            pltpu.VMEM((rows + extra_out, 2 * width), LOW),
            pltpu.VMEM((depth // chunk, share, chunk), LOW),
            pltpu.VMEM((depth // chunk, share, chunk), LOW),
            pltpu.SemaphoreType.DMA((2 + 2 * tiles,)),
            pltpu.SemaphoreType.DMA((2 * tiles + 1,)),
            pltpu.SemaphoreType.DMA((depth // chunk + 1,)),
            pltpu.SemaphoreType.DMA((depth // chunk + 1,)),
        ],
        flops=8 * rows * depth * width,
        identity=identity,
    )


def adapter_kernel(plan, n_inputs, n_grads, corrections, n_before, order_ref, *refs):
    for _ in adapter_steps(plan, n_inputs, n_grads, corrections, n_before, order_ref, *refs):
        pass


def adapter_steps(plan, n_inputs, n_grads, corrections, n_before, order_ref, *refs):
    count = n_inputs + n_grads
    sources, held, sems = refs[:count], refs[-count - 1 : -1], refs[-1]
    left_ref, right_ref = refs[count : count + 2]
    *corrected, left_out, right_out = refs[count + 2 : -count - 1]
    members, rank, width = right_ref.shape
    chunks = list(plan(order_ref, held[:n_inputs], held[n_inputs:]))
    copies, used = [], 0
    for parts, _, _ in chunks:
        copies.append([])
        for which, index in parts:
            copy = pltpu.make_async_copy(
                sources[which].at[index], held[which].at[index], sems.at[used]
            )
            copy.start()
            copies[-1].append(copy)
            used += 1
    yield
    left_rows = jnp.concatenate([split_rows(left_ref[m]) for m in range(members)], axis=0)
    right_rows = [split_rows(right_ref[m]) for m in range(members)]
    before, corrected = corrected[:n_before], corrected[n_before:]
    for out, ref in zip((left_out, right_out), before or (None, None)):
        out[...] = jnp.zeros_like(out) if ref is None else ref[...]
    for waits, (_, taken_of, grads_of) in zip(copies, chunks):
        for copy in waits:
            copy.wait()
        taken = taken_of()
        across = dot(left_rows, taken, NT)
        downs = []
        for m in range(members):
            grad = grads_of(m)
            mine = split_rows(fold(across[2 * rank * m : 2 * rank * (m + 1)]))
            right_out[m] += fold(dot(mine, grad))
            downs.append(split_rows(fold(dot(right_rows[m], grad, NT))))
        left = dot(jnp.concatenate(downs, axis=0), taken)
        for m in range(members):
            left_out[m] += fold(left[2 * rank * m : 2 * rank * (m + 1)])
        yield
    if corrections:
        correct(corrections, right_ref, left_out, right_out, left_out, right_out, *corrected)


def correct(n_totals, right_ref, left_in, right_in, left_out, right_out, *refs):
    back_ref, across_ref, squares_ref, magnitude_ref = refs[:4]
    totals, magnitude_out = refs[4 : 4 + n_totals], refs[4 + n_totals]
    members, rank, width = right_ref.shape
    total = sum_refs(totals)[:, :, :width]
    squares = squares_ref[:, :, :width]
    magnitude_out[...] = total / jnp.sqrt(squares)
    for m in range(members):
        weight = norm_weight(total[m], squares[m], magnitude_ref[m : m + 1])
        if back_ref.dtype == LOW:
            low = back_ref[m, : left_in.shape[2], :]
            back = fold(dot(split_rows(right_ref[m] * weight), low, NT))
        else:
            back = back_ref[m]
        left_out[m] = ADAPT_SCALE * (left_in[m] - back)
        right_out[m] = ADAPT_SCALE * (right_in[m] - across_ref[m][:, :width] * weight)


def adapter_parts(inputs, grads, left, right, correction, before):
    members, rank, width = right.shape
    moved, fixed, n_totals = [*inputs, *grads], [left, right, *before], 0
    outs = [(members, rank, left.shape[2]), (members, rank, width)]
    if correction is not None:
        *given, totals = correction
        n_totals = len(totals)
        fixed += [*given, *totals]
        outs = [(members, 1, width)] + outs
    scratch = [pltpu.VMEM(v.shape, v.dtype) for v in moved] + [pltpu.SemaphoreType.DMA((32,))]
    return moved, fixed, outs, scratch, (len(inputs), len(grads), n_totals, len(before))


def adapter(name, order, plan, inputs, grads, left, right, correction=None, before=(), other=None):
    moved, fixed, outs, scratch, counts = adapter_parts(inputs, grads, left, right, correction, before)
    kernel = functools.partial(adapter_kernel, plan, *counts)
    full = lambda dims: pl.BlockSpec(tuple(dims), lambda i, o: (0,) * len(dims))
    n_moved, n_fixed, n_outs = len(moved), len(fixed), len(outs)
    if other is not None:
        sums, other_right, (low, across, squares, magnitude, totals) = other
        moved = moved + [low]
        fixed = fixed + [other_right, *sums, across, squares, magnitude, *totals]
        outs = outs + [(1, 1, other_right.shape[2]), sums[0].shape, sums[1].shape]
        scratch = scratch + [pltpu.VMEM(low.shape, LOW), pltpu.SemaphoreType.DMA(())]

    def run(order_ref, *refs):
        if other is None:
            kernel(order_ref, *refs)
            return
        refs = list(refs)
        low_held, low_sem = refs[-2:]
        low_copy = pltpu.make_async_copy(refs[n_moved], low_held, low_sem)
        ends = [n_moved + 1, n_moved + 1 + len(fixed), n_moved + 1 + len(fixed) + len(outs)]
        fixed_refs, out_refs = refs[ends[0] : ends[1]], refs[ends[1] : ends[2]]
        steps = adapter_steps(
            plan,
            *counts,
            order_ref,
            *refs[:n_moved],
            *fixed_refs[:n_fixed],
            *out_refs[:n_outs],
            *refs[ends[2] : -2],
        )
        next(steps)
        low_copy.start()
        for _ in steps:
            pass
        low_copy.wait()
        right_ref, left_in, right_in, across_ref, squares_ref, magnitude_ref, *totals_refs = (
            fixed_refs[n_fixed:]
        )
        magnitude_out, left_out, right_out = out_refs[n_outs:]
        correct(
            len(totals_refs),
            right_ref,
            left_in,
            right_in,
            left_out,
            right_out,
            low_held,
            across_ref,
            squares_ref,
            magnitude_ref,
            *totals_refs,
            magnitude_out,
        )

    return call(
        name,
        run,
        (*moved, *fixed),
        (1,),
        [pl.BlockSpec(memory_space=pl.ANY) for _ in moved] + [full(v.shape) for v in fixed],
        [full(dims) for dims in outs],
        [shape(dims, F32) for dims in outs],
        scratch=scratch,
        prefetch=(order,),
        flops=sum(v.size for v in moved) * 64,
    )


def copy_kernel(count, *refs):
    for source, target in zip(refs[:count], refs[count:]):
        if len(target.shape) < len(source.shape):
            for m in range(source.shape[0]):
                target[m : m + 1, :] = source[m]
        else:
            target[...] = source[...]


def copy_out(arrays):
    full = lambda v: pl.BlockSpec(v.shape, lambda i: (0,) * len(v.shape))
    flat = lambda v: v.shape[:1] + v.shape[2:] if v.ndim == 3 and v.shape[1] == 1 else v.shape
    out_shape = [shape(flat(v), F32) for v in arrays]
    return call(
        "copy_out",
        functools.partial(copy_kernel, len(arrays)),
        tuple(arrays),
        (1,),
        [full(v) for v in arrays],
        [full(v) for v in out_shape],
        out_shape,
    )


GRAIN = 16


def pieces_of(width):
    return [(at, min(128, width - at)) for at in range(0, width, 128)]


def cells_of(blocks, lines, parts):
    cells, rows = [], []
    for n, block in enumerate(blocks):
        for m in range(block.shape[0]):
            for at, size in pieces_of(block.shape[2] // parts):
                cells.append((n, m, at, size))
    for n, line in enumerate(lines):
        for m in range(line.shape[0]):
            for at, size in pieces_of(line.shape[2] // parts):
                rows.append((n, m, at, size))
    return cells, rows


def pack(blocks, lines, wide_ref, part, parts, cells, rows):
    for i, (n, m, at, size) in enumerate(cells):
        start = part * (blocks[n].shape[2] // parts) + at
        wide_ref[part, i, :, :size] = blocks[n][m, :, start : start + size]
    for i, (n, m, at, size) in enumerate(rows):
        start = part * (lines[n].shape[2] // parts) + at
        cell, row = len(cells) + i // GRAIN, i % GRAIN
        wide_ref[part, cell, row : row + 1, :size] = lines[n][m, :, start : start + size]


def unpack(full_ref, blocks, lines, part, parts, cells, rows):
    for i, (n, m, at, size) in enumerate(cells):
        start = part * (blocks[n].shape[2] // parts) + at
        blocks[n][m, :, start : start + size] = full_ref[part, i].astype(F32)[:, :size]
    for i, (n, m, at, size) in enumerate(rows):
        start = part * (lines[n].shape[2] // parts) + at
        cell, row = len(cells) + i // GRAIN, i % GRAIN
        values = full_ref[part, cell].astype(F32)
        lines[n][m, :, start : start + size] = values[row : row + 1, :size]


def reduce_steps(groups, lines, counts, *refs):
    n_all, n_all_lines, n_dp, n_dp_lines = counts
    count = sum(counts)
    taken, given, scratch = refs[:count], refs[count : 2 * count], refs[2 * count :]
    ends = [n_all, n_all + n_all_lines, n_all + n_all_lines + n_dp]
    parted = lambda v: (v[: ends[0]], v[ends[0] : ends[1]], v[ends[1] : ends[2]], v[ends[2] :])
    all_out, all_lines_out, dp_out, dp_lines_out = parted(given)
    (
        all_ref,
        line_ref,
        all_low,
        line_low,
        all_got,
        part,
        part_low,
        part_got,
        line_got,
        all_full,
        line_full,
        *sems,
    ) = scratch
    held, in_sems, sems = sems[:count], sems[count], sems[count + 1 :]
    loads = [
        pltpu.make_async_copy(source, target, in_sems.at[i])
        for i, (source, target) in enumerate(zip(taken, held))
    ]
    for load in loads:
        load.start()
    me, row = lax.axis_index("mp"), lax.axis_index("dp")
    piece, line_piece = part.shape[0] // lines, line_ref.shape[1] // lines
    mp_peer = [lax.rem(me + k, groups) for k in range(groups)]
    dp_peer = [lax.rem(row + k, lines) for k in range(lines)]
    barrier = pltpu.get_barrier_semaphore()
    for k in range(1, groups):
        pl.semaphore_signal(barrier, 1, device_id={"mp": mp_peer[k]}, device_id_type=MESH_IDS)
    for k in range(1, lines):
        pl.semaphore_signal(barrier, 1, device_id={"dp": dp_peer[k]}, device_id_type=MESH_IDS)
    all_in, all_lines_in, dp_in, dp_lines_in = parted(held)
    all_cells = cells_of(all_in, all_lines_in, groups)
    dp_cells = cells_of(dp_in, dp_lines_in, 1)
    all_ref[...] = jnp.zeros_like(all_ref)
    line_ref[...] = jnp.zeros_like(line_ref)
    for load in loads:
        load.wait()
    for q in range(groups):
        pack(all_in, all_lines_in, all_ref, q, groups, *all_cells)
    pack(dp_in, dp_lines_in, line_ref, 0, 1, *dp_cells)
    all_low[...] = all_ref[...].astype(LOW)
    line_low[...] = line_ref[...].astype(LOW)
    pl.semaphore_wait(barrier, groups + lines - 2)

    def send(source, target, stage, k, axis, peer):
        copy = pltpu.make_async_remote_copy(
            src_ref=source,
            dst_ref=target,
            send_sem=sems[2 * stage].at[k],
            recv_sem=sems[2 * stage + 1].at[k],
            device_id={axis: peer},
            device_id_type=MESH_IDS,
        )
        copy.start()
        return copy

    over_mp = [
        send(all_low.at[mp_peer[k]], all_got.at[k], 0, k, "mp", mp_peer[k])
        for k in range(1, groups)
    ]
    over_dp = [
        send(
            line_low.at[0, pl.ds(dp_peer[k] * line_piece, line_piece)],
            line_got.at[k],
            1,
            k,
            "dp",
            dp_peer[k],
        )
        for k in range(1, lines)
    ]
    yield
    total = all_ref[me]
    for k, copy in enumerate(over_mp, 1):
        copy.wait_recv()
        total = total + all_got[k].astype(F32)
    part[...] = total
    part_low[...] = total.astype(LOW)
    part_dp = [
        send(part_low.at[pl.ds(dp_peer[k] * piece, piece)], part_got.at[k], 2, k, "dp", dp_peer[k])
        for k in range(1, lines)
    ]
    yield
    held = pl.ds(row * piece, piece)
    total = part[held]
    for k, copy in enumerate(part_dp, 1):
        copy.wait_recv()
        total = total + part_got[k].astype(F32)
    all_full[me, held] = total.astype(LOW)
    part_back = [
        send(all_full.at[me, held], all_full.at[me, held], 4, k, "dp", dp_peer[k])
        for k in range(1, lines)
    ]
    mine = pl.ds(row * line_piece, line_piece)
    total = line_ref[0, mine]
    for k, copy in enumerate(over_dp, 1):
        copy.wait_recv()
        total = total + line_got[k].astype(F32)
    line_full[0, mine] = total.astype(LOW)
    line_back = [
        send(line_full.at[0, mine], line_full.at[0, mine], 3, k, "dp", dp_peer[k])
        for k in range(1, lines)
    ]
    yield
    for copy in part_back:
        copy.wait_recv()
    all_back = [
        send(all_full.at[me], all_full.at[me], 5, k, "mp", mp_peer[k]) for k in range(1, groups)
    ]
    yield
    for copy in line_back:
        copy.wait_recv()
    unpack(line_full, dp_out, dp_lines_out, 0, 1, *dp_cells)
    for copy in all_back:
        copy.wait_recv()
    for q in range(groups):
        unpack(all_full, all_out, all_lines_out, q, groups, *all_cells)
    for copy in over_mp + over_dp + part_dp + line_back + part_back + all_back:
        copy.wait_send()


def reduce_devices(name, identity, over_all, over_all_lines, over_dp, over_dp_lines, job):
    groups, lines = lax.axis_size("mp"), lax.axis_size("dp")

    def size_of(blocks, rows, parts):
        cells, lines_in = cells_of(blocks, rows, parts)
        size = len(cells) + -(-len(lines_in) // GRAIN)
        return -(-size // lines) * lines

    count, line_count = size_of(over_all, over_all_lines, groups), size_of(over_dp, over_dp_lines, 1)
    operands = [*over_all, *over_all_lines, *over_dp, *over_dp_lines]
    counts = (len(over_all), len(over_all_lines), len(over_dp), len(over_dp_lines))
    tail = (GRAIN, 128)
    sizes = (groups, lines, lines, lines, lines, groups)
    every, line = (groups, count) + tail, (1, line_count) + tail
    scratch = (
        [
            pltpu.VMEM(every, F32),
            pltpu.VMEM(line, F32),
            pltpu.VMEM(every, LOW),
            pltpu.VMEM(line, LOW),
            pltpu.VMEM(every, LOW),
            pltpu.VMEM((count,) + tail, F32),
            pltpu.VMEM((count,) + tail, LOW),
            pltpu.VMEM((lines, count // lines) + tail, LOW),
            pltpu.VMEM((lines, line_count // lines) + tail, LOW),
            pltpu.VMEM(every, LOW),
            pltpu.VMEM(line, LOW),
        ]
        + [pltpu.VMEM(v.shape, F32) for v in operands]
        + [pltpu.SemaphoreType.DMA((len(operands),))]
        + [pltpu.SemaphoreType.DMA((n,)) for n in sizes for _ in range(2)]
    )
    job_steps, moved, whole_rows, job_shape, job_scratch = job
    n_operands, n_scratch = len(operands), len(scratch)
    out_shape = [shape(v.shape, F32) for v in operands] + [job_shape]
    anywhere = pl.BlockSpec(memory_space=pl.ANY)
    full = lambda v: pl.BlockSpec(v.shape, lambda i: (0,) * v.ndim)
    operands = operands + [*moved, *whole_rows]

    def run(*refs):
        given, refs = refs[: len(operands)], refs[len(operands) :]
        results, held = refs[: len(out_shape)], refs[len(out_shape) :]
        steps = reduce_steps(
            groups, lines, counts, *given[:n_operands], *results[:n_operands], *held[:n_scratch]
        )
        work = job_steps(*given[n_operands:], results[n_operands], *held[n_scratch:])
        next(work)
        for _ in steps:
            next(work, None)
        for _ in work:
            pass

    return call(
        name,
        run,
        tuple(operands),
        (1,),
        [anywhere] * (n_operands + len(moved)) + [full(v) for v in whole_rows],
        [full(v) for v in out_shape[:-1]] + [anywhere],
        out_shape,
        scratch=scratch + job_scratch,
        flops=1000,
        identity=identity,
    )


def token_job(tokens, grad_hidden, parts, gain):
    share, width = grad_hidden.shape
    moved = [tokens, grad_hidden, *parts]

    def steps(*refs):
        sources, gain_ref, out_ref = refs[: len(moved)], refs[len(moved)], refs[len(moved) + 1]
        *held, result, sems = refs[len(moved) + 2 :]
        row = pl.multiple_of(lax.axis_index("mp") * share, share)
        copies = []
        for n, (source, target) in enumerate(zip(sources, held)):
            source = source.at[pl.ds(row, share), :] if n == 0 else source
            copies.append(pltpu.make_async_copy(source, target, sems.at[n]))
            copies[-1].start()
        yield
        for copy in copies:
            copy.wait()
        tile = 32
        gain = gain_ref[...]

        def some(i, carry):
            at = pl.ds(pl.multiple_of(i * tile, tile), tile)
            token, grad, *rest = [ref[at, :].astype(F32) for ref in held]
            result[at, :] = grad + norm_back(sum_of(rest), token, gain)[0]
            return carry

        lax.fori_loop(0, share // tile, some, 0, unroll=2)
        copy = pltpu.make_async_copy(result, out_ref, sems.at[len(moved)])
        copy.start()
        yield
        yield
        copy.wait()

    scratch = [pltpu.VMEM((share, width), v.dtype) for v in moved]
    scratch += [pltpu.VMEM((share, width), F32), pltpu.SemaphoreType.DMA((len(moved) + 1,))]
    return steps, moved, [gain], shape((share, width), F32), scratch


def body(
    tokens,
    cotangent,
    segment_ids,
    attend_gain,
    expand_gain,
    heads_base,
    heads_left,
    heads_right,
    heads_magnitude,
    output_base,
    output_left,
    output_right,
    output_magnitude,
    expand_base,
    expand_left,
    expand_right,
    expand_magnitude,
    shrink_base,
    shrink_left,
    shrink_right,
    shrink_magnitude,
):
    groups = lax.axis_size("mp")
    chips = groups // CORES
    index = lax.axis_index("mp")
    chip, core = index // CORES, index % CORES
    rows, width = tokens.shape
    share = rows // groups
    local_heads, ff = heads_base.shape[2], expand_base.shape[2]
    ff_wide = padded(ff)
    device = jnp.arange(groups, dtype=jnp.int32)
    order = jnp.concatenate(
        [
            (chip + device // CORES) % chips * CORES + (core + 1 + device) % CORES,
            (device // CORES + chips - chip) % chips * CORES + (device + CORES - core + 1) % CORES,
        ]
    ).astype(jnp.int32)

    def tie(*values):
        return lax.optimization_barrier(values)

    def sibling(values):
        return lax.ppermute(
            values, "mp", [(i, i // CORES * CORES + (i + 1) % CORES) for i in range(groups)]
        )

    def to_chip(values, step):
        return lax.ppermute(
            values,
            "mp",
            [((i, ((i // CORES + step) % chips) * CORES + i % CORES)) for i in range(groups)],
        )

    def join(pair):
        return (pair[1].astype(F32) + sibling(pair[0]).astype(F32)).astype(LOW)

    def chip_pairs(places):
        return [places[CORES * step : CORES * (step + 1)] for step in range(chips)]

    def arrive(own):
        return [to_chip(own, chips - step) for step in range(1, chips)]

    def pairs_of(own, near_sibling, arrived):
        return [(near_sibling, own)] + [(sibling(piece), piece) for piece in arrived]

    def in_pairs(order_ref, inputs, grads):
        for step, (taken, grad) in enumerate(zip(inputs, grads)):
            yield (
                [(step, ...), (chips + step, ...)],
                lambda taken=taken: taken[...],
                lambda m, grad=grad: grad[m, :, :ff],
            )

    def in_shrink(order_ref, inputs, grads):
        for step, taken in enumerate(inputs):
            at = slice(CORES * step, CORES * (step + 1))
            yield (
                [(step, ...), (chips, pl.ds(CORES * step, CORES))],
                lambda taken=taken: taken[:, :ff],
                lambda m, at=at: grads[0][at].reshape(-1, grads[0].shape[-1]),
            )

    def in_output(start):
        def plan(order_ref, inputs, grads):
            for n, grad in enumerate(grads):
                yield (
                    [(0, (0, start + n)), (1 + n, ...)],
                    lambda place=start + n: inputs[0][0, place],
                    lambda m, grad=grad: grad[...],
                )

        return plan

    def in_heads(order_ref, inputs, grads):
        for place in range(groups):
            step, side = place // CORES, place % CORES
            me = lax.axis_index("mp")
            group = lax.rem(me // CORES + step, chips) * CORES + lax.rem(me + 1 + side, CORES)
            at = pl.multiple_of(group * share, share)
            rows = pl.ds(place * share, share)
            yield (
                [(0, pl.ds(at, share)), (1, (slice(None), rows))],
                lambda at=at: inputs[0][pl.ds(at, share), :],
                lambda m, rows=rows: grads[0][m, rows, :],
            )

    heads_rows, output_rows = turned(heads_left), turned(output_left[None])
    expand_rows, shrink_rows = turned(expand_left), turned(shrink_left[None])
    heads_mag, output_mag = heads_magnitude, output_magnitude[None]
    expand_mag, shrink_mag = expand_magnitude, shrink_magnitude[None]
    attend_line, expand_line = attend_gain[None], expand_gain[None]

    output_low, shrink_low, squares_part = merge_pair(
        [(output_base, output_rows[0], output_right), (shrink_base, shrink_rows[0], shrink_right)]
    )
    output_low, shrink_low = output_low[None], shrink_low[None]
    (
        normed,
        heads_low,
        post,
        heads_sq,
        heads_across,
        cos_table,
        sine_table,
        output_sq,
        shrink_sq,
        first,
    ) = project_heads(
        tokens,
        attend_line,
        heads_base,
        heads_rows,
        heads_right,
        heads_mag,
        segment_ids,
        squares_part,
        groups,
    )
    heads_out = attend(order, groups, post, first)
    heads_parts = heads_out.reshape(1, groups, share, local_heads)
    joined, output_across = product(
        "output_product", 3, heads_parts, output_low, NN, left=output_rows
    )
    joined, expand_right_tied = tie(joined, expand_right)
    output_parts = [joined[0]] + [to_chip(joined[step], step) for step in range(1, chips)]
    expand_low, expand_sq = merge(expand_base, expand_rows, expand_right_tied, 1024)
    grad_product, shrink_grad = shrink_back(
        order, cotangent, shrink_low, shrink_sq, shrink_mag[None], groups
    )
    output_parts, expand_low, grad_product = tie(output_parts, expand_low, grad_product)
    hidden, normed_own = row_call(
        "hidden",
        hidden_kernel,
        order,
        [(tokens, True)] + [(part, False) for part in output_parts],
        (output_sq[0], output_mag, expand_line),
        (F32, LOW),
        0,
        scale_first,
    )

    def feed(mine, step, **extra):
        return expand(
            4 + step, mine, expand_low, expand_sq, expand_mag, grad_product, step, **extra
        )

    arrived = arrive(normed_own)
    fed = [feed(normed_own, 0, left=expand_rows)]
    arrived, fed = tie(arrived, fed)
    fed = list(fed)
    for step in range(1, chips):
        extra = {}
        if step == chips - 1:
            extra = {"right": expand_right, "before": [f[3] for f in fed]}
        fed.append(feed(arrived[step - 1], step, **extra))
    expand_totals = [f[3] for f in fed]
    joined, shrink_rows_tied = tie([f[4] for f in fed], shrink_rows)
    mid_parts = [joined[0]] + [to_chip(joined[step], step) for step in range(1, chips)]
    shrink_places, shrink_total, shrink_across = shrink_product(
        order, [f[0] for f in fed], shrink_low, shrink_rows_tied, cotangent
    )
    shrink_pairs = chip_pairs(shrink_places)
    expand_adapter = adapter(
        "expand_adapter",
        order,
        in_pairs,
        [f[2] for f in fed],
        [f[1] for f in fed],
        expand_rows,
        expand_right,
        (fed[-1][5], fed[0][5], expand_sq, expand_mag, expand_totals),
    )
    mid_parts, shrink_pairs, expand_adapter = tie(mid_parts, shrink_pairs, expand_adapter)
    grad_hidden, output_grad_own, output_total, expand_gain_part = row_call(
        "hidden_back",
        hidden_back_kernel,
        order,
        [(cotangent, True), (tokens, True), (hidden, False)]
        + [(part, False) for part in mid_parts],
        (output_sq[0], output_mag, expand_line),
        (F32, LOW),
        2,
        scale_first,
    )
    arrived, near_sibling = arrive(output_grad_own), sibling(output_grad_own)
    shrink_joined = [join(pair) for pair in shrink_pairs[1:]]
    shrink_joined, shrink_rows_tied = tie(shrink_joined, shrink_rows)
    shrink_sums = adapter(
        "shrink_adapter",
        order,
        in_shrink,
        [f[0] for f in fed],
        [shrink_grad],
        shrink_rows_tied,
        shrink_right[None],
    )
    output_sums = adapter(
        "output_near_adapter",
        order,
        in_output(0),
        [heads_parts],
        [near_sibling, output_grad_own],
        output_rows,
        output_right[None],
    )
    near_heads = heads_near([near_sibling, output_grad_own], output_low)
    arrived, near_sibling, shrink_joined, shrink_sums, output_sums, near_heads = tie(
        arrived, near_sibling, shrink_joined, shrink_sums, output_sums, near_heads
    )
    output_grad = [
        piece for pair in pairs_of(output_grad_own, near_sibling, arrived) for piece in pair
    ]
    shrink_parts = [shrink_pairs[0][1], sibling(shrink_pairs[0][0])] + [
        to_chip(values, step) for step, values in enumerate(shrink_joined, 1)
    ]
    heads_grads, heads_total = attend_back(
        order,
        groups,
        post,
        first,
        cos_table,
        sine_table,
        heads_mag,
        heads_sq,
        output_low,
        near_heads,
        output_grad[CORES:],
    )
    grad_parts = heads_grads.reshape(3, groups, share, local_heads)
    joined, output_total, shrink_total, attend_gain_part, token_extra = product(
        "normed_product",
        20,
        grad_parts,
        heads_low,
        NT,
        correction=(heads_right, heads_sq, heads_mag, [heads_total]),
        lines=(output_total, shrink_total),
        gain=(normed, attend_line),
    )
    joined, shrink_parts, heads_rows_tied, output_rows_tied = tie(
        joined, shrink_parts, heads_rows, output_rows
    )
    token_parts = [joined[0]] + [to_chip(joined[step], step) for step in range(1, chips)]
    output_mag_part, output_left_part, output_right_part, *shrink_adapter = adapter(
        "output_far_adapter",
        order,
        in_output(CORES),
        [heads_parts],
        output_grad[CORES:],
        output_rows_tied,
        output_right[None],
        (output_low, output_across, output_sq, output_mag, [output_total]),
        output_sums,
        (
            shrink_sums,
            shrink_right[None],
            (shrink_low, shrink_across, shrink_sq, shrink_mag, [shrink_total]),
        ),
    )
    heads_adapter = adapter(
        "heads_adapter",
        order,
        in_heads,
        [normed],
        [heads_grads],
        heads_rows_tied,
        heads_right,
        (token_extra, heads_across, heads_sq, heads_mag, [heads_total]),
    )
    (mixed,) = row_call(
        "mixed",
        mixed_kernel,
        order,
        [(hidden, False)] + [(part, False) for part in shrink_parts],
        (shrink_sq[0], shrink_mag),
        (LOW,),
        0,
        scale_first,
    )
    token_parts, heads_adapter, mixed = tie(token_parts, heads_adapter, mixed)
    *reduced, grad_tokens = reduce_devices(
        "reduce_gradients",
        1,
        [expand_adapter[1], shrink_adapter[2], output_right_part, heads_adapter[1]],
        [expand_gain_part[None], attend_gain_part[None]],
        [expand_adapter[2], shrink_adapter[1], output_left_part, heads_adapter[2]],
        [expand_adapter[0], shrink_adapter[0], output_mag_part, heads_adapter[0]],
        token_job(tokens, grad_hidden, token_parts, attend_line),
    )
    (
        expand_left_grad,
        shrink_right_grad,
        output_right_grad,
        heads_left_grad,
        expand_gain_grad,
        attend_gain_grad,
        expand_right_grad,
        shrink_left_grad,
        output_left_grad,
        heads_right_grad,
        expand_mag_grad,
        shrink_mag_grad,
        output_mag_grad,
        heads_mag_grad,
        grad_tokens,
    ) = copy_out([*reduced, grad_tokens])
    return (
        mixed,
        grad_tokens,
        attend_gain_grad[0],
        expand_gain_grad[0],
        jnp.swapaxes(heads_left_grad, 1, 2),
        heads_right_grad,
        heads_mag_grad,
        output_left_grad[0].T,
        output_right_grad[0],
        output_mag_grad[0],
        jnp.swapaxes(expand_left_grad, 1, 2),
        expand_right_grad,
        expand_mag_grad,
        shrink_left_grad[0].T,
        shrink_right_grad[0],
        shrink_mag_grad[0],
    )


def solution(mesh):
    placed = (
        P("dp", None),
        P("dp", None),
        P("dp", None),
        P(),
        P(),
        P(None, None, "mp"),
        P(),
        P(None, None, "mp"),
        P(None, "mp"),
        P("mp", None),
        P("mp", None),
        P(),
        P(),
        P(None, None, "mp"),
        P(),
        P(None, None, "mp"),
        P(None, "mp"),
        P("mp", None),
        P("mp", None),
        P(),
        P(),
    )
    return jax.shard_map(
        body,
        mesh=mesh,
        in_specs=placed,
        out_specs=(
            P(("dp", "mp"), None),
            P(("dp", "mp"), None),
            P(),
            P(),
            P(),
            P(None, None, "mp"),
            P(None, "mp"),
            P("mp", None),
            P(),
            P(),
            P(),
            P(None, None, "mp"),
            P(None, "mp"),
            P("mp", None),
            P(),
            P(),
        ),
        check_vma=False,
    )
```

```python
import functools

import jax
import jax.numpy as jnp
import ml_dtypes
import numpy as np
from jax import lax
from jax.experimental import pallas as pl
from jax.experimental.pallas import tpu as pltpu
from jax.sharding import PartitionSpec as P

HEAD_DIM = 128
CORES = 2
LONGEST = 512
ATTEND_BLOCK = 256
ADAPT_SCALE = 2.0
NORM_EPS = 1e-05
ROPE_BASE = 10000.0
MASKED = -1e30

F32 = jnp.float32
LOW = jnp.bfloat16
NN = (((1,), (0,)), ((), ()))
NT = (((1,), (1,)), ((), ()))
TN = (((0,), (0,)), ((), ()))


MESH_IDS = pl.DeviceIdType.MESH


def sibling_id():
    me = lax.axis_index("mp")
    return me // CORES * CORES + lax.rem(me + 1, CORES)


def greet(peers):
    for peer in peers:
        pl.semaphore_signal(
            pltpu.get_barrier_semaphore(), 1, device_id={"mp": peer}, device_id_type=MESH_IDS
        )


def greeted(count):
    pl.semaphore_wait(pltpu.get_barrier_semaphore(), count)


def remote(source, target, send_sem, recv_sem, peer):
    return pltpu.make_async_remote_copy(
        src_ref=source,
        dst_ref=target,
        send_sem=send_sem,
        recv_sem=recv_sem,
        device_id={"mp": peer},
        device_id_type=MESH_IDS,
    )


def dot(left, right, dims=NN):
    return lax.dot_general(left, right, dims, preferred_element_type=F32)


def shape(dims, kind):
    return jax.ShapeDtypeStruct(tuple(dims), kind)


def call(name, kernel, operands, grid, in_specs, out_specs, out_shape, scratch=(), prefetch=(), flops=0, mib=63.5, identity=None):
    moved = sum(v.size * v.dtype.itemsize for v in operands)
    moved += sum(v.size * v.dtype.itemsize for v in out_shape)
    return pl.pallas_call(
        kernel,
        name=name,
        out_shape=out_shape,
        grid_spec=pltpu.PrefetchScalarGridSpec(
            num_scalar_prefetch=len(prefetch),
            grid=grid,
            in_specs=in_specs,
            out_specs=out_specs,
            scratch_shapes=scratch,
        ),
        compiler_params=pltpu.CompilerParams(
            vmem_limit_bytes=int(mib * 2**20), collective_id=identity, has_side_effects=identity is not None
        ),
        cost_estimate=pl.CostEstimate(flops=flops // 16, bytes_accessed=moved // 16, transcendentals=0),
    )(*prefetch, *operands)


def tile_of(size, most):
    return most if size % most == 0 else size


def split_rows(values):
    top = values.astype(LOW)
    rest = (values - top.astype(F32)).astype(LOW)
    return jnp.concatenate([top, rest], axis=0)


def turned(left_map):
    return jnp.swapaxes(left_map, -1, -2)


def norm_weight(total, squares, magnitude):
    norm = jnp.sqrt(squares)
    return total * magnitude / (norm * norm * norm)


def sum_refs(refs):
    total = refs[0][...]
    for ref in refs[1:]:
        total = total + ref[...]
    return total


def fold(values):
    half = values.shape[0] // 2
    return values[:half] + values[half:]


def merge_tile(base_at, low_put, left, right, depth):
    rank = right.shape[0]
    doubled = ADAPT_SCALE * right
    top = doubled.astype(LOW)
    rest = (doubled - top.astype(F32)).astype(LOW)
    right_stack = jnp.concatenate([top, rest, top], axis=0)
    left_pair = split_rows(left)
    left_stack = jnp.concatenate([left_pair[:rank], left_pair[:rank], left_pair[rank:]], axis=0)
    width = right.shape[1]
    wide = 256 if width == 512 else width
    step = tile_of(depth, 1024)
    squares = []
    for at in range(0, width, wide):
        columns = slice(at, at + wide)
        total = jnp.zeros((1, wide), F32)
        for start in range(0, depth, step):
            merged = base_at(start, step, columns).astype(F32) + dot(
                left_stack[:, start : start + step], right_stack[:, columns], TN
            )
            low_put(start, step, columns, merged.astype(LOW))
            total = total + jnp.sum(merged * merged, axis=0, keepdims=True)
        squares.append(total)
    return jnp.concatenate(squares, axis=1)


def merge_pair_kernel(*refs):
    for n in range(2):
        base_ref, left_ref, right_ref = refs[3 * n : 3 * n + 3]
        low_ref, squares_ref = refs[6 + n], refs[8]
        depth = base_ref.shape[0]
        if low_ref.shape[0] > depth:
            low_ref[depth:, :] = jnp.zeros((low_ref.shape[0] - depth, low_ref.shape[1]), LOW)

        def put(start, step, columns, tile, low_ref=low_ref):
            low_ref[start : start + step, columns] = tile

        squares_ref[n : n + 1, :] = merge_tile(
            lambda start, step, columns, base_ref=base_ref: base_ref[start : start + step, columns],
            put,
            left_ref[...],
            right_ref[...],
            depth,
        )


def merge_pair(triples):
    operands, in_specs, low_specs, low_shapes = [], [], [], []
    width = triples[0][0].shape[1]
    wide = tile_of(width, 512)
    for base, left, right in triples:
        depth, rank = base.shape[0], right.shape[0]
        operands += [base, left, right]
        in_specs += [
            pl.BlockSpec((depth, wide), lambda n: (0, n)),
            pl.BlockSpec((rank, depth), lambda n: (0, 0)),
            pl.BlockSpec((rank, wide), lambda n: (0, n)),
        ]
        low_specs.append(pl.BlockSpec((padded(depth), wide), lambda n: (0, n)))
        low_shapes.append(shape((padded(depth), width), LOW))
    return call(
        "merge_pair",
        merge_pair_kernel,
        tuple(operands),
        (width // wide,),
        in_specs,
        low_specs + [pl.BlockSpec((2, wide), lambda n: (0, n))],
        low_shapes + [shape((2, width), F32)],
        flops=2 * sum(v.size for v in operands) * 256,
    )


def merge_kernel(left_ref, right_ref, *refs):
    *bases, low_ref, squares_ref = refs
    part, width = bases[0].shape[1:]
    if low_ref.shape[2] > width:
        spare = low_ref.shape[2] - width
        low_ref[0, :, width:] = jnp.zeros((low_ref.shape[1], spare), LOW)
        squares_ref[0, :, width:] = jnp.ones((1, spare), F32)
    squares = jnp.zeros((1, width), F32)
    for n, base_ref in enumerate(bases):

        def put(start, step, columns, tile, at=n * part):
            low_ref[0, at + start : at + start + step, columns] = tile

        squares = squares + merge_tile(
            lambda start, step, columns, base_ref=base_ref: base_ref[
                0, start : start + step, columns
            ],
            put,
            left_ref[0, :, n * part : (n + 1) * part],
            right_ref[0],
            part,
        )

    @pl.when(pl.program_id(1) == 0)
    def _():
        squares_ref[0, :, :width] = squares

    @pl.when(pl.program_id(1) > 0)
    def _():
        squares_ref[0, :, :width] += squares


def padded(size):
    return -(-size // 256) * 256


def pad_last(values, size):
    return jnp.pad(values, [(0, 0)] * (values.ndim - 1) + [(0, size - values.shape[-1])])


def merge(base, left, right, deep):
    members, depth, width = base.shape
    rank, wide, cuts = right.shape[1], padded(width), 4
    part = lambda n: pl.BlockSpec(
        (1, deep // cuts, width), functools.partial(lambda n, m, k: (m, cuts * k + n, 0), n)
    )
    return call(
        "merge",
        merge_kernel,
        (left, right, *[base] * cuts),
        (members, depth // deep),
        [
            pl.BlockSpec((1, rank, deep), lambda m, k: (m, 0, k)),
            pl.BlockSpec((1, rank, width), lambda m, k: (m, 0, 0)),
        ]
        + [part(n) for n in range(cuts)],
        [
            pl.BlockSpec((1, deep, wide), lambda m, k: (m, k, 0)),
            pl.BlockSpec((1, 1, wide), lambda m, k: (m, 0, 0)),
        ],
        [shape((members, depth, wide), LOW), shape((members, 1, wide), F32)],
        flops=2 * members * depth * width * 256,
    )


def rms_rows(values):
    return lax.rsqrt(jnp.mean(values * values, axis=1, keepdims=True) + NORM_EPS)


TABLE_STEP = 32


def table_pieces(places):
    half = np.arange(HEAD_DIM) % (HEAD_DIM // 2)
    angles = np.asarray(places)[:, None] * ROPE_BASE ** (-2.0 * half / HEAD_DIM)[None, :]
    rest = np.concatenate([np.cos(angles), np.sin(angles)], axis=1)
    pieces = []
    for _ in range(3):
        pieces.append(rest.astype(ml_dtypes.bfloat16))
        rest = rest - pieces[-1].astype(np.float64)
    return jnp.asarray(np.concatenate(pieces, axis=0))


def rotation(first, coarse, fine):
    rows = first.shape[0]
    position = lax.broadcasted_iota(jnp.int32, (rows, 1), 0) - first
    lane = lax.broadcasted_iota(jnp.int32, (rows, 3 * TABLE_STEP), 1) % TABLE_STEP
    pick = lambda place, table: dot((lane == place).astype(F32).astype(LOW), table)
    high = pick(position // TABLE_STEP, coarse)
    small = pick(position % TABLE_STEP, fine)
    cos_a, sin_a = high[:, :HEAD_DIM], high[:, HEAD_DIM:]
    cos_b, sin_b = small[:, :HEAD_DIM], small[:, HEAD_DIM:]
    sine = sin_a * cos_b + cos_a * sin_b
    left_half = lax.broadcasted_iota(jnp.int32, sine.shape, 1) < HEAD_DIM // 2
    return cos_a * cos_b - sin_a * sin_b, jnp.where(left_half, -sine, sine)


def heads_kernel(
    token_ref,
    gain_ref,
    base_ref,
    left_ref,
    right_ref,
    magnitude_ref,
    segment_ref,
    coarse_ref,
    fine_ref,
    part_ref,
    normed_ref,
    low_ref,
    post_ref,
    squares_ref,
    across_ref,
    cos_ref,
    sine_ref,
    output_sum_ref,
    shrink_sum_ref,
    first_ref,
    rows_all,
    part_mine,
    part_got,
    send_sems,
    recv_sems,
):
    total_rows = token_ref.shape[0]
    depth, width = base_ref.shape[1:]
    rank = right_ref.shape[1]
    groups = part_got.shape[0]
    me = lax.axis_index("mp")
    peers = [lax.rem(me + k, groups) for k in range(groups)]
    part_copies = [
        remote(part_mine, part_got.at[k], send_sems.at[k], recv_sems.at[k], peers[k])
        for k in range(1, groups)
    ]

    @pl.when(pl.program_id(0) == 0)
    def _():
        greet(peers[1:])
        part_mine[...] = part_ref[...]
        step = 128

        def some(i, carry):
            at = pl.ds(pl.multiple_of(i * step, step), step)
            values = token_ref[at, :].astype(F32)
            low = (values * rms_rows(values) * gain_ref[...]).astype(LOW)
            normed_ref[at, :] = low
            rows_all[at, :] = low
            return carry

        lax.fori_loop(0, total_rows // step, some, 0)
        ids = segment_ref[...].astype(F32)
        ids_down = jnp.transpose(jnp.broadcast_to(ids, (8, total_rows)))[:, :1]
        for start in range(0, total_rows, 256):
            rows = slice(start, start + 256)
            smaller = jnp.where(ids < ids_down[rows], 1.0, 0.0)
            first = jnp.sum(smaller, axis=1, keepdims=True).astype(jnp.int32)
            first_ref[rows, :] = first
            cosine, sine = rotation(first - start, coarse_ref[...], fine_ref[...])
            cos_ref[rows, :] = cosine
            sine_ref[rows, :] = sine
        greeted(groups - 1)
        for copy in part_copies:
            copy.start()

    @pl.when(pl.program_id(0) == pl.num_programs(0) - 1)
    def _():
        total = part_mine[...]
        for k, copy in enumerate(part_copies, 1):
            copy.wait_recv()
            total = total + part_got[k]
        output_sum_ref[0] = total[:1]
        shrink_sum_ref[0] = total[1:]
        for copy in part_copies:
            copy.wait_send()

    rows_all[total_rows:, :] = left_ref[0].astype(LOW)
    turning = pl.program_id(0) < 2
    wide = 256

    def put(start, step, columns, tile):
        low_ref[0, start : start + step, columns] = tile

    squares_ref[0] = merge_tile(
        lambda start, step, columns: base_ref[0, start : start + step, columns],
        put,
        left_ref[0],
        right_ref[0],
        depth,
    )
    for column in range(0, width, wide):
        columns = slice(column, column + wide)
        magnitude = magnitude_ref[pl.ds(pl.program_id(0), 1), columns]
        scale = magnitude / jnp.sqrt(squares_ref[0, :, columns])
        low = low_ref[0, :, columns]
        step = min(512, total_rows)
        for start in range(0, total_rows, step):
            last = start + step == total_rows
            rows = slice(start, start + step)
            pre = dot(rows_all[start : start + step + (rank if last else 0), :], low)
            if last:
                across_ref[0, :, columns] = pre[step:]
            post = pre[:step] * scale
            cos_table = jnp.where(turning, cos_ref[rows, :], 1.0)
            sine_table = jnp.where(turning, sine_ref[rows, :], 0.0)
            for head in range(0, wide, HEAD_DIM):
                piece = post[:, head : head + HEAD_DIM]
                other = pltpu.roll(piece, HEAD_DIM // 2, 1)
                post_ref[0, rows, column + head : column + head + HEAD_DIM] = (
                    piece * cos_table + other * sine_table
                ).astype(LOW)


def project_heads(tokens, gain, base, left, right, magnitude, segments, part, groups):
    members, depth, width = base.shape
    rows, rank = tokens.shape[0], right.shape[1]
    coarse = table_pieces(np.arange(TABLE_STEP) * TABLE_STEP)
    fine = table_pieces(np.arange(TABLE_STEP))
    whole = lambda v: pl.BlockSpec(v.shape, lambda m: (0,) * v.ndim)
    of_member = lambda *dims: pl.BlockSpec((1,) + dims, lambda m: (m, 0, 0))
    table = pl.BlockSpec((rows, HEAD_DIM), lambda m: (0, 0))
    return call(
        "project_heads",
        heads_kernel,
        (tokens, gain, base, left, right, magnitude, segments, coarse, fine, part),
        (members,),
        [
            whole(tokens),
            whole(gain),
            of_member(depth, width),
            of_member(rank, depth),
            of_member(rank, width),
            whole(magnitude),
            whole(segments),
            whole(coarse),
            whole(fine),
            whole(part),
        ],
        [
            whole(tokens),
            of_member(depth, width),
            of_member(rows, width),
            of_member(1, width),
            of_member(rank, width),
            table,
            table,
            pl.BlockSpec((1, 1, depth), lambda m: (0, 0, 0)),
            pl.BlockSpec((1, 1, depth), lambda m: (0, 0, 0)),
            pl.BlockSpec((rows, 1), lambda m: (0, 0)),
        ],
        [
            shape((rows, depth), LOW),
            shape(base.shape, LOW),
            shape((members, rows, width), LOW),
            shape((members, 1, width), F32),
            shape((members, rank, width), F32),
            shape((rows, HEAD_DIM), F32),
            shape((rows, HEAD_DIM), F32),
            shape((1, 1, depth), F32),
            shape((1, 1, depth), F32),
            shape((rows, 1), jnp.int32),
        ],
        scratch=[
            pltpu.VMEM((rows + rank, depth), LOW),
            pltpu.VMEM(part.shape, F32),
            pltpu.VMEM((groups,) + part.shape, F32),
            pltpu.SemaphoreType.DMA((groups,)),
            pltpu.SemaphoreType.DMA((groups,)),
        ],
        identity=2,
        flops=2 * members * rows * depth * width,
    )


def key_start(block):
    return max(0, (block * ATTEND_BLOCK - (LONGEST - 1)) // ATTEND_BLOCK * ATTEND_BLOCK)


def masked_probs(scores, first, row_at, key_at):
    scores = scores * HEAD_DIM ** (-0.5)
    places = row_at + lax.broadcasted_iota(jnp.int32, scores.shape, 0)
    others = key_at + lax.broadcasted_iota(jnp.int32, scores.shape, 1)
    scores = jnp.where((others >= first) & (others <= places), scores, MASKED)
    exp_scores = jnp.exp(scores - jnp.max(scores, axis=1, keepdims=True))
    return exp_scores * (1.0 / jnp.sum(exp_scores, axis=1, keepdims=True))


class Unit:
    def __init__(self, head, block):
        self.row_at, self.key_at = block * ATTEND_BLOCK, key_start(block)
        self.rows = slice(self.row_at, self.row_at + ATTEND_BLOCK)
        self.keys = slice(self.key_at, self.row_at + ATTEND_BLOCK)
        self.lanes = slice(head * HEAD_DIM, (head + 1) * HEAD_DIM)


def units_of(rows, width, most):
    units = [
        Unit(head, block)
        for block in range(rows // ATTEND_BLOCK)
        for head in range(width // HEAD_DIM)
    ]
    return [units[at : at + most] for at in range(0, len(units), most)]


def put_rows(ref, lead, row_at, lanes, values, order_ref, groups):
    share = ref.shape[len(lead)] // groups
    step = min(share, values.shape[0])
    for start in range(0, values.shape[0], step):
        group = (row_at + start) // share
        inside = (row_at + start) % share
        at = pl.multiple_of(order_ref[groups + group] * share + inside, step)
        ref[(*lead, pl.ds(at, step), lanes)] = values[start : start + step].astype(ref.dtype)


def attend_kernel(groups, order_ref, query_ref, key_ref, value_ref, first_ref, out_ref):
    for some in units_of(*query_ref.shape[1:], 4):
        scores = [
            dot(query_ref[0, u.rows, u.lanes], key_ref[0, u.keys, u.lanes], NT) for u in some
        ]
        probs = [
            masked_probs(s, first_ref[u.rows, :], u.row_at, u.key_at).astype(LOW)
            for u, s in zip(some, scores)
        ]
        for u, p in zip(some, probs):
            mixed = dot(p, value_ref[0, u.keys, u.lanes])
            put_rows(out_ref, (), u.row_at, u.lanes, mixed, order_ref, groups)


def attend(order, groups, post, first):
    rows, width = post.shape[1:]
    wide = 2 * HEAD_DIM
    member = lambda m: pl.BlockSpec((1, rows, wide), lambda h, o: (m, 0, h))
    return call(
        "attend",
        functools.partial(attend_kernel, groups),
        (post, post, post, first),
        (width // wide,),
        [member(0), member(1), member(2), pl.BlockSpec((rows, 1), lambda h, o: (0, 0))],
        [pl.BlockSpec((rows, wide), lambda h, o: (0, h))],
        [shape((rows, width), LOW)],
        prefetch=(order,),
        flops=4 * rows * rows * width,
    )[0]


def attend_back_kernel(
    groups,
    order_ref,
    query_ref,
    key_ref,
    value_ref,
    first_ref,
    cos_ref,
    sine_ref,
    magnitude_ref,
    squares_ref,
    low_ref,
    *rest,
):
    pieces, (grad_ref, total_ref, upper_all, heads_grad, key_grad, value_grad, sems) = rest[:-7], rest[-7:]
    rows_all, width = query_ref.shape[1:]
    share = rows_all // groups

    @pl.when(pl.program_id(0) == 0)
    def _():
        copies = []
        for place, piece in enumerate(pieces):
            at = pl.multiple_of(order_ref[place] * share, share)
            copies.append(
                pltpu.make_async_copy(piece, upper_all.at[pl.ds(at, share), :], sems.at[place])
            )
            copies[-1].start()
        for copy in copies:
            copy.wait()

    step = min(512, rows_all)
    for start in range(0, rows_all, step):
        at = slice(start, start + step)
        heads_grad[at, :] = dot(upper_all[at, :], low_ref[0], NT).astype(LOW)
    norm = [jnp.sqrt(squares_ref[m]) for m in range(3)]
    scale = [magnitude_ref[m : m + 1] / norm[m] for m in range(3)]
    heads = range(0, width, HEAD_DIM)
    totals = [jnp.zeros((1, width), F32) for _ in range(3)]
    filled = set()

    def back(values, rows):
        return values * cos_ref[rows, :] - pltpu.roll(values, HEAD_DIM // 2, 1) * sine_ref[rows, :]

    def add(ref, unit, values):
        for start in range(0, values.shape[0], ATTEND_BLOCK):
            at = unit.key_at + start
            rows = slice(at, at + ATTEND_BLOCK)
            name = (id(ref), at, unit.lanes.start)
            if name in filled:
                ref[rows, unit.lanes] += values[start : start + ATTEND_BLOCK]
            else:
                filled.add(name)
                ref[rows, unit.lanes] = values[start : start + ATTEND_BLOCK]

    def spread(per_head):
        return jnp.concatenate(per_head, axis=1)

    query_totals = [jnp.zeros((1, HEAD_DIM), F32) for _ in heads]
    for some in units_of(rows_all, width, 4):
        scores = [
            dot(query_ref[0, u.rows, u.lanes], key_ref[0, u.keys, u.lanes], NT) for u in some
        ]
        grad_weights = [
            dot(heads_grad[u.rows, u.lanes], value_ref[0, u.keys, u.lanes], NT) for u in some
        ]
        probs = [
            masked_probs(s, first_ref[u.rows, :], u.row_at, u.key_at)
            for u, s in zip(some, scores)
        ]
        grad_scores = [
            (p * (g - jnp.sum(p * g, axis=1, keepdims=True))).astype(LOW)
            for p, g in zip(probs, grad_weights)
        ]
        for u, p, g in zip(some, probs, grad_scores):
            add(value_grad, u, dot(p.astype(LOW), heads_grad[u.rows, u.lanes], TN))
            add(key_grad, u, dot(g, query_ref[0, u.rows, u.lanes], TN))
        for u, g in zip(some, grad_scores):
            grad = back(dot(g, key_ref[0, u.keys, u.lanes]) * HEAD_DIM ** (-0.5), u.rows)
            head = u.lanes.start // HEAD_DIM
            post = back(query_ref[0, u.rows, u.lanes].astype(F32), u.rows)
            query_totals[head] = query_totals[head] + jnp.sum(grad * post, axis=0, keepdims=True)
            put_rows(grad_ref, (0,), u.row_at, u.lanes, grad * scale[0][:, u.lanes], order_ref, groups)
    totals[0] = spread(query_totals)
    for row_at in range(0, rows_all, ATTEND_BLOCK):
        rows = slice(row_at, row_at + ATTEND_BLOCK)
        for head in heads:
            lanes = slice(head, head + HEAD_DIM)
            grad = back(key_grad[rows, lanes] * HEAD_DIM ** (-0.5), rows)
            post = back(key_ref[0, rows, lanes].astype(F32), rows)
            part = jnp.sum(grad * post, axis=0, keepdims=True)
            query_totals[head // HEAD_DIM] = part if row_at == 0 else query_totals[head // HEAD_DIM] + part
            put_rows(grad_ref, (1,), row_at, lanes, grad * scale[1][:, lanes], order_ref, groups)
        grad = value_grad[rows, :]
        totals[2] = totals[2] + jnp.sum(grad * value_ref[0, rows, :].astype(F32), axis=0, keepdims=True)
        put_rows(grad_ref, (2,), row_at, slice(0, width), grad * scale[2], order_ref, groups)
    totals[1] = spread(query_totals)
    for m in range(3):
        total_ref[m] = totals[m] / scale[m]


def attend_back(order, groups, post, first, cos_table, sine_table, magnitude, squares, low, pieces):
    rows, width = post.shape[1:]
    depth = low.shape[2]
    wide = 2 * HEAD_DIM
    member = lambda m: pl.BlockSpec((1, rows, wide), lambda h, o: (m, 0, h))
    table = pl.BlockSpec((rows, HEAD_DIM), lambda h, o: (0, 0))
    column = pl.BlockSpec((3, 1, wide), lambda h, o: (0, 0, h))
    return call(
        "attend_back",
        functools.partial(attend_back_kernel, groups),
        (post, post, post, first, cos_table, sine_table, magnitude, squares, low, *pieces),
        (width // wide,),
        [
            member(0),
            member(1),
            member(2),
            pl.BlockSpec((rows, 1), lambda h, o: (0, 0)),
            table,
            table,
            pl.BlockSpec((3, wide), lambda h, o: (0, h)),
            column,
            pl.BlockSpec((1, wide, depth), lambda h, o: (0, h, 0)),
            *[pl.BlockSpec(memory_space=pl.ANY) for _ in pieces],
        ],
        [pl.BlockSpec((3, rows, wide), lambda h, o: (0, 0, h)), column],
        [shape((3, rows, width), LOW), shape((3, 1, width), F32)],
        scratch=[
            pltpu.VMEM((rows, depth), LOW),
            pltpu.VMEM((rows, wide), LOW),
            pltpu.VMEM((rows, wide), F32),
            pltpu.VMEM((rows, wide), F32),
            pltpu.SemaphoreType.DMA((len(pieces),)),
        ],
        prefetch=(order,),
        flops=10 * rows * rows * width + 2 * rows * width * depth,
    )


def product_kernel(dims, n_totals, n_lines, has_gain, steps, *refs):
    value_ref, weight_ref = refs[:2]
    if n_totals == 0:
        left_ref, *refs = refs[2:]
    else:
        right_ref, squares_ref, magnitude_ref = refs[2:5]
        totals, refs = refs[5 : 5 + n_totals], refs[5 + n_totals :]
    lines = []
    if has_gain:
        normed_ref, gain_ref, *refs = refs
    if n_lines > 0:
        lines, refs = refs[:n_lines], refs[n_lines:]
        *refs, line_mine, line_got, line_send_sems, line_recv_sems = refs
    *outs, extra_ref, rows_all, sent, got, send_sems, recv_sems = refs
    if has_gain:
        *outs, gain_out = outs
    line_outs, outs = outs[len(outs) - n_lines :], outs[: len(outs) - n_lines]
    members, groups, share, inner = value_ref.shape
    count, wide = groups * share, extra_ref.shape[2]
    now = pl.program_id(0)
    sibling = sibling_id()
    me = lax.axis_index("mp")
    peers = [lax.rem(me + k, groups) for k in range(1, groups)] if n_lines > 0 else [sibling]
    line_copies = [
        remote(line_mine, line_got.at[k], line_send_sems.at[k], line_recv_sems.at[k], peer)
        for k, peer in enumerate(peers if n_lines > 0 else [], 1)
    ]

    @pl.when(now == 0)
    def _():
        greet(peers)
        for n, ref in enumerate(lines):
            line_mine[n : n + 1, :] = ref[...]
        if n_totals > 0:
            total = sum_refs(totals)
        for m in range(members):
            rows_all[m, :count, :] = value_ref[m].reshape(count, inner)
            if n_totals == 0:
                rows_all[m, count:, :] = left_ref[m].astype(LOW)
            else:
                weight = norm_weight(total[m], squares_ref[m], magnitude_ref[m : m + 1])
                rows_all[m, count:, :] = (right_ref[m] * weight).astype(LOW)

    result = None
    for m in range(members):
        part = dot(rows_all[m], weight_ref[m], dims)
        extra_ref[m] = part[count:]
        result = part[:count] if result is None else result + part[:count]

    def columns(step):
        return pl.ds(pl.multiple_of(step * wide, wide), wide)

    def copy(step):
        return remote(sent.at[step], got.at[step], send_sems.at[step], recv_sems.at[step], sibling)

    def add(step):
        copy(step).wait_recv()
        for n, ref in enumerate(outs):
            total = ref[:, columns(step)].astype(F32) + got[step, n].astype(F32)
            ref[:, columns(step)] = total.astype(LOW)

    if has_gain:
        terms = jnp.zeros((1, wide), F32)
        for place in range(groups):
            group = lax.rem(me // CORES + place // CORES, groups // CORES) * CORES
            group = group + lax.rem(me + 1 + place, CORES)
            rows = pl.ds(pl.multiple_of(group * share, share), share)
            mine = result[place * share : (place + 1) * share]
            terms = terms + jnp.sum(
                mine * normed_ref[rows, :].astype(F32), axis=0, keepdims=True
            )
        gain_out[...] = terms / gain_ref[...]
    for n, ref in enumerate(outs):
        at = CORES * n * share
        sent[now, n] = result[at : at + share].astype(LOW)
        ref[:, columns(now)] = result[at + share : at + CORES * share].astype(LOW)

    @pl.when(now == 0)
    def _():
        greeted(len(peers))
        for each in line_copies:
            each.start()

    copy(now).start()

    @pl.when(now > 0)
    def _():
        add(now - 1)

    @pl.when(now == steps - 1)
    def _():
        add(now)
        for step in range(steps):
            copy(step).wait_send()
        if n_lines > 0:
            line_sum = line_mine[...]
            for k, each in enumerate(line_copies, 1):
                each.wait_recv()
                line_sum = line_sum + line_got[k]
            for n, ref in enumerate(line_outs):
                ref[0] = line_sum[n : n + 1]
            for each in line_copies:
                each.wait_send()


def product(name, identity, values, weights, dims, left=None, correction=None, lines=(), gain=()):
    members, groups, share, inner = values.shape
    chips = groups // CORES
    width = weights.shape[2] if dims is NN else weights.shape[1]
    wide = tile_of(width, 512)
    steps = width // wide
    if dims is NN:
        weight_spec = pl.BlockSpec((members, inner, wide), lambda n: (0, 0, n))
    else:
        weight_spec = pl.BlockSpec((members, wide, inner), lambda n: (0, n, 0))
    if correction is None:
        extra, n_totals, rank = (left,), 0, left.shape[1]
    else:
        right, squares, magnitude, totals = correction
        extra, n_totals, rank = (right, squares, magnitude, *totals), len(totals), right.shape[1]
    fixed = lambda v: pl.BlockSpec(v.shape, lambda n: (0,) * v.ndim)
    out = pl.BlockSpec((share, width), lambda n: (0, 0))
    line_specs, line_shapes, line_scratch = [], [], []
    if lines:
        line = (len(lines), width)
        line_specs = [pl.BlockSpec((1, 1, width), lambda n: (0, 0, 0)) for _ in lines]
        line_shapes = [shape((1, 1, width), F32) for _ in lines]
        line_scratch = [
            pltpu.VMEM(line, F32),
            pltpu.VMEM((groups,) + line, F32),
            pltpu.SemaphoreType.DMA((groups,)),
            pltpu.SemaphoreType.DMA((groups,)),
        ]
    gain_specs, gain_shapes, gain_in = [], [], []
    if gain:
        one = pl.BlockSpec((1, wide), lambda n: (0, n))
        gain_in = [pl.BlockSpec((gain[0].shape[0], wide), lambda n: (0, n)), one]
        gain_specs, gain_shapes = [one], [shape((1, width), F32)]
    results = call(
        name,
        functools.partial(product_kernel, dims, n_totals, len(lines), bool(gain), steps),
        (values, weights, *extra, *gain, *lines),
        (steps,),
        [fixed(values), weight_spec]
        + [fixed(v) for v in extra]
        + gain_in
        + [fixed(v) for v in lines],
        [out] * chips + line_specs + gain_specs + [pl.BlockSpec((members, rank, wide), lambda n: (0, 0, n))],
        [shape((share, width), LOW)] * chips
        + line_shapes
        + gain_shapes
        + [shape((members, rank, width), F32)],
        scratch=[
            pltpu.VMEM((members, groups * share + rank, inner), LOW),
            pltpu.VMEM((steps, chips, share, wide), LOW),
            pltpu.VMEM((steps, chips, share, wide), LOW),
            pltpu.SemaphoreType.DMA((steps,)),
            pltpu.SemaphoreType.DMA((steps,)),
        ]
        + line_scratch,
        flops=2 * members * groups * share * inner * width,
        identity=identity,
    )
    return results[:chips], *results[chips:]


def shrink_kernel(chips, order_ref, *refs):
    values, (weight_ref, left_ref, cot_ref), outs = refs[:chips], refs[chips : chips + 3], refs[chips + 3 :]
    total_ref, across_ref, rows_all = outs[-3:]
    both, inner = values[0].shape
    share, depth = both // CORES, left_ref.shape[2]
    count = chips * both

    @pl.when(pl.program_id(0) == 0)
    def _():
        for step, ref in enumerate(values):
            rows_all[step * both : (step + 1) * both, :] = ref[...]
        if inner > depth:
            rows_all[count:, depth:] = jnp.zeros((rows_all.shape[0] - count, inner - depth), LOW)
        rows_all[count:, :depth] = left_ref[0].astype(LOW)

    result = dot(rows_all[...], weight_ref[0])
    across_ref[0] = result[count:]
    total = jnp.zeros((1, weight_ref.shape[2]), F32)
    for place in range(chips * CORES):
        pre = result[place * share : (place + 1) * share]
        outs[place][...] = pre.astype(LOW)
        at = pl.multiple_of(order_ref[place] * share, share)
        cot = cot_ref[pl.ds(at, share), :].astype(F32)
        total = total + jnp.sum(pre * cot, axis=0, keepdims=True)
    total_ref[...] = total


def shrink_product(order, values, weights, left, cotangent):
    chips = len(values)
    share, inner = values[0].shape[0] // CORES, values[0].shape[1]
    width, rank = weights.shape[2], left.shape[1]
    rows = chips * CORES * share
    wide = tile_of(width, 512)
    fixed = lambda v: pl.BlockSpec(v.shape, lambda n, o: (0,) * v.ndim)
    results = call(
        "shrink_product",
        functools.partial(shrink_kernel, chips),
        (*values, weights, left, cotangent),
        (width // wide,),
        [fixed(v) for v in values]
        + [
            pl.BlockSpec((1, inner, wide), lambda n, o: (0, 0, n)),
            fixed(left),
            pl.BlockSpec((rows, wide), lambda n, o: (0, n)),
        ],
        [pl.BlockSpec((share, wide), lambda n, o: (0, n))] * (chips * CORES)
        + [
            pl.BlockSpec((1, wide), lambda n, o: (0, n)),
            pl.BlockSpec((1, rank, wide), lambda n, o: (0, 0, n)),
        ],
        [shape((share, width), LOW)] * (chips * CORES)
        + [shape((1, width), F32), shape((1, rank, width), F32)],
        scratch=[pltpu.VMEM((rows + rank, inner), LOW)],
        prefetch=(order,),
        flops=2 * rows * inner * width,
    )
    return results[: chips * CORES], results[-2], results[-1]


def row_call(name, kernel, order, given, whole, out_kinds, sums, prepare):
    share = min(v.shape[0] for v, _ in given)
    width = given[0][0].shape[1]
    halves = 2
    half = share // halves
    count = len(given)

    def run(order_ref, *refs):
        sources, rest = refs[:count], refs[count : -count - 1]
        held, sems = refs[-count - 1 : -1], refs[-1]

        def copies(part):
            for i, ((_, cut), source, target) in enumerate(zip(given, sources, held)):
                at = part * half
                if cut:
                    at = pl.multiple_of(order_ref[1] * share + at, half)
                yield pltpu.make_async_copy(
                    source.at[pl.ds(at, half), :],
                    target.at[pl.ds(part * half, half), :],
                    sems.at[part, i],
                )

        for part in range(halves):

            @pl.when(pl.program_id(0) == part)
            def _(part=part):
                if part == 0:
                    for each in range(halves):
                        for copy in copies(each):
                            copy.start()
                for copy in copies(part):
                    copy.wait()

        outs = rest[len(whole) : len(whole) + len(out_kinds)]
        totals, sums_held = rest[len(whole) + len(out_kinds) :][:sums], rest[len(rest) - sums :]
        tile = 32
        lines = prepare(*[ref[...] for ref in rest[: len(whole)]])
        for ref in sums_held:
            ref[...] = jnp.zeros_like(ref)

        def some(i, carry):
            inside = pl.ds(pl.multiple_of(i * tile, tile), tile)
            at = pl.ds(pl.multiple_of(pl.program_id(0) * half + i * tile, tile), tile)
            values = kernel([ref[at, :].astype(F32) for ref in held], *lines)
            for ref, value in zip(outs, values):
                ref[inside, :] = value.astype(ref.dtype)
            for ref, value in zip(sums_held, values[len(outs) :]):
                ref[...] += jnp.sum(value.reshape(tile // 8, 8, width), axis=0)
            return carry

        lax.fori_loop(0, half // tile, some, 0, unroll=2)
        for ref, held_ref in zip(totals, sums_held):
            add_column(ref, held_ref[...])

    line = pl.BlockSpec((1, width), lambda i, o: (0, 0))
    return call(
        name,
        run,
        (*[v for v, _ in given], *whole),
        (halves,),
        [pl.BlockSpec(memory_space=pl.ANY) for _ in given] + [line for _ in whole],
        [pl.BlockSpec((half, width), lambda i, o: (i, 0)) for _ in out_kinds]
        + [line for _ in range(sums)],
        [shape((share, width), kind) for kind in out_kinds]
        + [shape((1, width), F32) for _ in range(sums)],
        scratch=[pltpu.VMEM((8, width), F32) for _ in range(sums)]
        + [pltpu.VMEM((share, width), v.dtype) for v, _ in given]
        + [pltpu.SemaphoreType.DMA((halves, count))],
        prefetch=(order,),
        flops=20 * share * width,
    )


def sum_of(values):
    total = values[0]
    for value in values[1:]:
        total = total + value
    return total


def add_column(ref, values):
    part = jnp.sum(values, axis=0, keepdims=True)

    @pl.when(pl.program_id(0) == 0)
    def _():
        ref[...] = part

    @pl.when(pl.program_id(0) > 0)
    def _():
        ref[...] += part


def scale_first(squares, magnitude, *rest):
    norm = jnp.sqrt(squares)
    return (magnitude / norm, norm / magnitude, *rest)


def hidden_kernel(given, scale, inverse, gain):
    hidden = given[0] + sum_of(given[1:]) * scale
    return hidden, hidden * rms_rows(hidden) * gain


def mixed_kernel(given, scale, inverse):
    return (given[0] + sum_of(given[1:]) * scale,)


def norm_back(grad_normed, values, gain):
    factor = rms_rows(values)
    scaled = grad_normed * gain
    inner = jnp.mean(scaled * values, axis=1, keepdims=True)
    back = factor * scaled - values * (factor * factor * factor * inner)
    return back, grad_normed * values * factor


def hidden_back_kernel(given, scale, inverse, gain):
    cot, token, hidden = given[:3]
    back, gain_terms = norm_back(sum_of(given[3:]), hidden, gain)
    grad = cot + back
    return grad, grad * scale, grad * ((hidden - token) * inverse), gain_terms


def shrink_back_kernel(places, order_ref, *refs):
    cots, refs = refs[:places], refs[places:]
    *lows, squares_ref, magnitude_ref, product_ref, grad_ref, rows_all = refs
    scale = magnitude_ref[0] / jnp.sqrt(squares_ref[0])
    share = cots[0].shape[0]
    for place, cot_ref in enumerate(cots):
        grad = (cot_ref[...].astype(F32) * scale).astype(LOW)
        grad_ref[place] = grad
        rows_all[place * share : (place + 1) * share, :] = grad
    wide = lows[0].shape[1]
    for n, low_ref in enumerate(lows):
        result = dot(rows_all[...], low_ref[0], NT).astype(LOW)
        for place in range(places):
            product_ref[place, :, n * wide : (n + 1) * wide] = result[
                place * share : (place + 1) * share
            ]


def shrink_back(order, cotangent, low, squares, magnitude, groups):
    rows, width = cotangent.shape
    share, inner = rows // groups, low.shape[1]
    places, cuts = CORES, 3
    line = pl.BlockSpec((1, 1, width), lambda j, o: (0, 0, 0))
    cot = lambda place: pl.BlockSpec((share, width), lambda j, o: (o[places * j + place], 0))
    return call(
        "shrink_back",
        functools.partial(shrink_back_kernel, places),
        (*[cotangent] * places, *[low] * cuts, squares, magnitude),
        (groups // places,),
        [cot(place) for place in range(places)]
        + [
            pl.BlockSpec((1, inner // cuts, width), functools.partial(lambda n, j, o: (0, n, 0), n))
            for n in range(cuts)
        ]
        + [line, line],
        [
            pl.BlockSpec((places, share, inner), lambda j, o: (j, 0, 0)),
            pl.BlockSpec((places, share, width), lambda j, o: (j, 0, 0)),
        ],
        [shape((groups, share, inner), LOW), shape((groups, share, width), LOW)],
        scratch=[pltpu.VMEM((places * share, width), LOW)],
        prefetch=(order,),
        flops=2 * rows * width * inner,
    )


def expand_kernel(step, first, last, n_totals, *refs):
    mine_ref, low_ref, grad_ref, squares_ref, magnitude_ref = refs[:5]
    refs = list(refs[5:])
    left_ref = refs.pop(0) if first else None
    right_ref = refs.pop(0) if last else None
    before = [refs.pop(0) for _ in range(n_totals)]
    product_ref, back_ref, rows_ref, total_ref, joined_ref = refs[:5]
    refs = refs[5:]
    across_ref = refs.pop(0) if first else None
    extra_ref = refs.pop(0) if last else None
    rows_all, low_all, grad_all, product_all, back_all, sent, got, in_sems, out_sems, send_sems, recv_sems = refs
    share, depth = mine_ref.shape
    sibling = sibling_id()
    greet([sibling])
    both = CORES * share
    width, ff = low_ref.shape[2], magnitude_ref.shape[1]
    tile = 256
    cuts = [slice(at, at + tile) for at in range(0, width, tile)]

    mine_copy = pltpu.make_async_copy(mine_ref, rows_all.at[pl.ds(share, share), :], in_sems.at[0])
    other_copy = remote(
        mine_ref,
        rows_all.at[pl.ds(0, share), :],
        send_sems.at[sent.shape[0]],
        recv_sems.at[sent.shape[0]],
        sibling,
    )
    tile_copies = []
    for n, cut in enumerate(cuts):
        lanes = pl.ds(cut.start, tile)
        tile_copies.append(
            [
                pltpu.make_async_copy(
                    low_ref.at[:, :, lanes], low_all.at[:, :, lanes], in_sems.at[2 + 2 * n]
                ),
                pltpu.make_async_copy(
                    grad_ref.at[pl.ds(CORES * step, CORES), :, lanes],
                    grad_all.at[:, :, lanes],
                    in_sems.at[3 + 2 * n],
                ),
            ]
        )
    mine_copy.start()
    for copy in tile_copies[0]:
        copy.start()
    greeted(1)
    other_copy.start()
    for copies in tile_copies[1:]:
        for copy in copies:
            copy.start()
    if first:
        rank = across_ref.shape[1]
        for m in range(2):
            rows_all[both + m * rank : both + (m + 1) * rank, :] = left_ref[m].astype(LOW)
    mine_copy.wait()
    other_copy.wait_recv()
    out_copies = [
        pltpu.make_async_copy(rows_all.at[pl.ds(0, both), :], rows_ref, out_sems.at[2 * len(cuts)])
    ]
    out_copies[0].start()
    lane = lax.broadcasted_iota(jnp.int32, (1, tile), 1)
    for n, cut in enumerate(cuts):
        for copy in tile_copies[n]:
            copy.wait()
        size = min(tile, ff - cut.start)
        pre = [dot(rows_all[...], low_all[m, :, cut]) for m in range(2)]
        if first:
            for m in range(2):
                rows = slice(both + m * rank, both + (m + 1) * rank)
                across_ref[m, :, cut.start : cut.start + size] = pre[m][rows, :size]
        magnitude, squares, scale = [], [], []
        for m in range(2):
            given = magnitude_ref[m : m + 1, cut.start : cut.start + size]
            if size < tile:
                given = jnp.concatenate([given, jnp.zeros((1, tile - size), F32)], axis=1)
            magnitude.append(given)
            squares.append(squares_ref[m, :, cut])
            scale.append(given / jnp.sqrt(squares[m]))
        sums = [jnp.zeros((1, tile), F32) for _ in range(2)]
        at = [slice(m * width + cut.start, m * width + cut.stop) for m in range(2)]
        for place in range(CORES):
            rows = slice(place * share, (place + 1) * share)
            gate_pre, up_pre = pre[0][rows], pre[1][rows]
            gate, up = gate_pre * scale[0], up_pre * scale[1]
            sigmoid = 0.5 + 0.5 * jnp.tanh(0.5 * gate)
            active = gate * sigmoid
            product_all[rows, cut] = (active * up).astype(LOW)
            upper = grad_all[place, :, cut].astype(F32)
            grad_up = upper * active
            grad_gate = upper * up * sigmoid * (1.0 + gate * (1.0 - sigmoid))
            sums[0] += jnp.sum(grad_gate * gate_pre, axis=0, keepdims=True)
            sums[1] += jnp.sum(grad_up * up_pre, axis=0, keepdims=True)
            back_all[rows, at[0]] = (grad_gate * scale[0]).astype(LOW)
            back_all[rows, at[1]] = (grad_up * scale[1]).astype(LOW)
        for m in range(2):
            total_ref[m, :, cut] = sums[m]
        if last:
            rank = extra_ref.shape[1]
            for m in range(2):
                total = sums[m]
                for ref in before:
                    total = total + ref[m, :, cut]
                right = right_ref[m, :, cut.start : cut.start + size]
                if size < tile:
                    spare = jnp.zeros((rank, tile - size), F32)
                    right = jnp.concatenate([right, spare], axis=1)
                weighted = right * norm_weight(total, squares[m], magnitude[m])
                rows = slice(both + m * rank, both + (m + 1) * rank)
                back_all[rows, at[m]] = weighted.astype(LOW)
                back_all[rows, at[1 - m]] = jnp.zeros((rank, tile), LOW)
    for m in range(2):
        lanes = pl.ds(m * width, width)
        copy = pltpu.make_async_copy(
            back_all.at[pl.ds(0, both), lanes], back_ref.at[m], out_sems.at[m]
        )
        copy.start()
        out_copies.append(copy)
    copy = pltpu.make_async_copy(product_all, product_ref, out_sems.at[2])
    copy.start()
    out_copies.append(copy)
    chunk = sent.shape[2]
    copies = [
        remote(sent.at[n], got.at[n], send_sems.at[n], recv_sems.at[n], sibling)
        for n in range(depth // chunk)
    ]

    def add(n):
        columns = slice(n * chunk, (n + 1) * chunk)
        copies[n].wait_recv()
        total = joined_ref[:, columns].astype(F32) + got[n].astype(F32)
        joined_ref[:, columns] = total.astype(LOW)

    for n in range(depth // chunk):
        columns = slice(n * chunk, (n + 1) * chunk)
        result = dot(back_all[:, :width], low_all[0, columns, :], NT)
        result = result + dot(back_all[:, width:], low_all[1, columns, :], NT)
        sent[n] = result[:share].astype(LOW)
        joined_ref[:, columns] = result[share:both].astype(LOW)
        copies[n].start()
        if n > 0:
            add(n - 1)
        if last:
            for m in range(2):
                extra_ref[m, :, columns] = result[both + m * rank : both + (m + 1) * rank]
    add(len(copies) - 1)
    for copy in out_copies:
        copy.wait()
    for copy in [other_copy, *copies]:
        copy.wait_send()


def expand(identity, mine, low, squares, magnitude, grad_product, step, left=None, right=None, before=()):
    share, depth = mine.shape
    width = low.shape[2]
    first, last = left is not None, right is not None
    rows = CORES * share
    hbm = pl.BlockSpec(memory_space=pl.ANY)
    fixed = lambda dims: pl.BlockSpec(tuple(dims), lambda i: (0,) * len(dims))
    operands = [mine, low, grad_product, squares, magnitude]
    in_specs = [hbm, hbm, hbm, fixed(squares.shape), fixed(magnitude.shape)]
    out_shape = [
        shape((rows, width), LOW),
        shape((2, rows, width), LOW),
        shape((rows, depth), LOW),
        shape((2, 1, width), F32),
        shape((share, depth), LOW),
    ]
    out_specs = [hbm, hbm, hbm] + [fixed(v.shape) for v in out_shape[3:]]
    extra_in = extra_out = 0
    if first:
        rank = left.shape[1]
        extra_in = 2 * rank
        operands.append(left)
        in_specs.append(fixed(left.shape))
        out_shape.append(shape((2, rank, magnitude.shape[1]), F32))
        out_specs.append(fixed(out_shape[-1].shape))
    if last:
        rank = right.shape[1]
        extra_out = 2 * rank
        operands += [right, *before]
        in_specs += [fixed(v.shape) for v in (right, *before)]
        out_shape.append(shape((2, rank, depth), F32))
        out_specs.append(fixed(out_shape[-1].shape))
    tiles, chunk = width // 256, tile_of(depth, 512)
    return call(
        "expand",
        functools.partial(expand_kernel, step, first, last, len(before)),
        tuple(operands),
        (1,),
        in_specs,
        out_specs,
        out_shape,
        scratch=[
            pltpu.VMEM((rows + extra_in, depth), LOW),
            pltpu.VMEM(low.shape, LOW),
            pltpu.VMEM((CORES, share, width), LOW),
            pltpu.VMEM((rows, width), LOW),
            pltpu.VMEM((rows + extra_out, 2 * width), LOW),
            pltpu.VMEM((depth // chunk, share, chunk), LOW),
            pltpu.VMEM((depth // chunk, share, chunk), LOW),
            pltpu.SemaphoreType.DMA((2 + 2 * tiles,)),
            pltpu.SemaphoreType.DMA((2 * tiles + 1,)),
            pltpu.SemaphoreType.DMA((depth // chunk + 1,)),
            pltpu.SemaphoreType.DMA((depth // chunk + 1,)),
        ],
        flops=8 * rows * depth * width,
        identity=identity,
    )


def adapter_kernel(plan, n_inputs, n_grads, corrections, n_before, order_ref, *refs):
    for _ in adapter_steps(plan, n_inputs, n_grads, corrections, n_before, order_ref, *refs):
        pass


def adapter_steps(plan, n_inputs, n_grads, corrections, n_before, order_ref, *refs):
    count = n_inputs + n_grads
    sources, held, sems = refs[:count], refs[-count - 1 : -1], refs[-1]
    left_ref, right_ref = refs[count : count + 2]
    *corrected, left_out, right_out = refs[count + 2 : -count - 1]
    members, rank, width = right_ref.shape
    chunks = list(plan(order_ref, held[:n_inputs], held[n_inputs:]))
    copies, used = [], 0
    for parts, _, _ in chunks:
        copies.append([])
        for which, index in parts:
            copy = pltpu.make_async_copy(
                sources[which].at[index], held[which].at[index], sems.at[used]
            )
            copy.start()
            copies[-1].append(copy)
            used += 1
    yield
    left_rows = jnp.concatenate([split_rows(left_ref[m]) for m in range(members)], axis=0)
    right_rows = [split_rows(right_ref[m]) for m in range(members)]
    before, corrected = corrected[:n_before], corrected[n_before:]
    for out, ref in zip((left_out, right_out), before or (None, None)):
        out[...] = jnp.zeros_like(out) if ref is None else ref[...]
    for waits, (_, taken_of, grads_of) in zip(copies, chunks):
        for copy in waits:
            copy.wait()
        taken = taken_of()
        across = dot(left_rows, taken, NT)
        downs = []
        for m in range(members):
            grad = grads_of(m)
            mine = split_rows(fold(across[2 * rank * m : 2 * rank * (m + 1)]))
            right_out[m] += fold(dot(mine, grad))
            downs.append(split_rows(fold(dot(right_rows[m], grad, NT))))
        left = dot(jnp.concatenate(downs, axis=0), taken)
        for m in range(members):
            left_out[m] += fold(left[2 * rank * m : 2 * rank * (m + 1)])
        yield
    if corrections:
        correct(corrections, right_ref, left_out, right_out, left_out, right_out, *corrected)


def correct(n_totals, right_ref, left_in, right_in, left_out, right_out, *refs):
    back_ref, across_ref, squares_ref, magnitude_ref = refs[:4]
    totals, magnitude_out = refs[4 : 4 + n_totals], refs[4 + n_totals]
    members, rank, width = right_ref.shape
    total = sum_refs(totals)[:, :, :width]
    squares = squares_ref[:, :, :width]
    magnitude_out[...] = total / jnp.sqrt(squares)
    for m in range(members):
        weight = norm_weight(total[m], squares[m], magnitude_ref[m : m + 1])
        if back_ref.dtype == LOW:
            low = back_ref[m, : left_in.shape[2], :]
            back = fold(dot(split_rows(right_ref[m] * weight), low, NT))
        else:
            back = back_ref[m]
        left_out[m] = ADAPT_SCALE * (left_in[m] - back)
        right_out[m] = ADAPT_SCALE * (right_in[m] - across_ref[m][:, :width] * weight)


def adapter_parts(inputs, grads, left, right, correction, before):
    members, rank, width = right.shape
    moved, fixed, n_totals = [*inputs, *grads], [left, right, *before], 0
    outs = [(members, rank, left.shape[2]), (members, rank, width)]
    if correction is not None:
        *given, totals = correction
        n_totals = len(totals)
        fixed += [*given, *totals]
        outs = [(members, 1, width)] + outs
    scratch = [pltpu.VMEM(v.shape, v.dtype) for v in moved] + [pltpu.SemaphoreType.DMA((32,))]
    return moved, fixed, outs, scratch, (len(inputs), len(grads), n_totals, len(before))


def adapter(name, order, plan, inputs, grads, left, right, correction=None, before=(), other=None):
    moved, fixed, outs, scratch, counts = adapter_parts(inputs, grads, left, right, correction, before)
    kernel = functools.partial(adapter_kernel, plan, *counts)
    full = lambda dims: pl.BlockSpec(tuple(dims), lambda i, o: (0,) * len(dims))
    n_moved, n_fixed, n_outs = len(moved), len(fixed), len(outs)
    if other is not None:
        sums, other_right, (low, across, squares, magnitude, totals) = other
        moved = moved + [low]
        fixed = fixed + [other_right, *sums, across, squares, magnitude, *totals]
        outs = outs + [(1, 1, other_right.shape[2]), sums[0].shape, sums[1].shape]
        scratch = scratch + [pltpu.VMEM(low.shape, LOW), pltpu.SemaphoreType.DMA(())]

    def run(order_ref, *refs):
        if other is None:
            kernel(order_ref, *refs)
            return
        refs = list(refs)
        low_held, low_sem = refs[-2:]
        low_copy = pltpu.make_async_copy(refs[n_moved], low_held, low_sem)
        ends = [n_moved + 1, n_moved + 1 + len(fixed), n_moved + 1 + len(fixed) + len(outs)]
        fixed_refs, out_refs = refs[ends[0] : ends[1]], refs[ends[1] : ends[2]]
        steps = adapter_steps(
            plan,
            *counts,
            order_ref,
            *refs[:n_moved],
            *fixed_refs[:n_fixed],
            *out_refs[:n_outs],
            *refs[ends[2] : -2],
        )
        next(steps)
        low_copy.start()
        for _ in steps:
            pass
        low_copy.wait()
        right_ref, left_in, right_in, across_ref, squares_ref, magnitude_ref, *totals_refs = (
            fixed_refs[n_fixed:]
        )
        magnitude_out, left_out, right_out = out_refs[n_outs:]
        correct(
            len(totals_refs),
            right_ref,
            left_in,
            right_in,
            left_out,
            right_out,
            low_held,
            across_ref,
            squares_ref,
            magnitude_ref,
            *totals_refs,
            magnitude_out,
        )

    return call(
        name,
        run,
        (*moved, *fixed),
        (1,),
        [pl.BlockSpec(memory_space=pl.ANY) for _ in moved] + [full(v.shape) for v in fixed],
        [full(dims) for dims in outs],
        [shape(dims, F32) for dims in outs],
        scratch=scratch,
        prefetch=(order,),
        flops=sum(v.size for v in moved) * 64,
    )


def copy_kernel(count, *refs):
    for source, target in zip(refs[:count], refs[count:]):
        if len(target.shape) < len(source.shape):
            for m in range(source.shape[0]):
                target[m : m + 1, :] = source[m]
        else:
            target[...] = source[...]


def copy_out(arrays):
    full = lambda v: pl.BlockSpec(v.shape, lambda i: (0,) * len(v.shape))
    flat = lambda v: v.shape[:1] + v.shape[2:] if v.ndim == 3 and v.shape[1] == 1 else v.shape
    out_shape = [shape(flat(v), F32) for v in arrays]
    return call(
        "copy_out",
        functools.partial(copy_kernel, len(arrays)),
        tuple(arrays),
        (1,),
        [full(v) for v in arrays],
        [full(v) for v in out_shape],
        out_shape,
    )


GRAIN = 16


def pieces_of(width):
    return [(at, min(128, width - at)) for at in range(0, width, 128)]


def cells_of(blocks, lines, parts):
    cells, rows = [], []
    for n, block in enumerate(blocks):
        for m in range(block.shape[0]):
            for at, size in pieces_of(block.shape[2] // parts):
                cells.append((n, m, at, size))
    for n, line in enumerate(lines):
        for m in range(line.shape[0]):
            for at, size in pieces_of(line.shape[2] // parts):
                rows.append((n, m, at, size))
    return cells, rows


def pack(blocks, lines, wide_ref, part, parts, cells, rows):
    for i, (n, m, at, size) in enumerate(cells):
        start = part * (blocks[n].shape[2] // parts) + at
        wide_ref[part, i, :, :size] = blocks[n][m, :, start : start + size]
    for i, (n, m, at, size) in enumerate(rows):
        start = part * (lines[n].shape[2] // parts) + at
        cell, row = len(cells) + i // GRAIN, i % GRAIN
        wide_ref[part, cell, row : row + 1, :size] = lines[n][m, :, start : start + size]


def unpack(full_ref, blocks, lines, part, parts, cells, rows):
    for i, (n, m, at, size) in enumerate(cells):
        start = part * (blocks[n].shape[2] // parts) + at
        blocks[n][m, :, start : start + size] = full_ref[part, i].astype(F32)[:, :size]
    for i, (n, m, at, size) in enumerate(rows):
        start = part * (lines[n].shape[2] // parts) + at
        cell, row = len(cells) + i // GRAIN, i % GRAIN
        values = full_ref[part, cell].astype(F32)
        lines[n][m, :, start : start + size] = values[row : row + 1, :size]


def reduce_steps(groups, lines, counts, *refs):
    n_all, n_all_lines, n_dp, n_dp_lines = counts
    count = sum(counts)
    taken, given, scratch = refs[:count], refs[count : 2 * count], refs[2 * count :]
    ends = [n_all, n_all + n_all_lines, n_all + n_all_lines + n_dp]
    parted = lambda v: (v[: ends[0]], v[ends[0] : ends[1]], v[ends[1] : ends[2]], v[ends[2] :])
    all_out, all_lines_out, dp_out, dp_lines_out = parted(given)
    (
        all_ref,
        line_ref,
        all_low,
        line_low,
        all_got,
        part,
        part_low,
        part_got,
        line_got,
        all_full,
        line_full,
        *sems,
    ) = scratch
    held, in_sems, sems = sems[:count], sems[count], sems[count + 1 :]
    loads = [
        pltpu.make_async_copy(source, target, in_sems.at[i])
        for i, (source, target) in enumerate(zip(taken, held))
    ]
    for load in loads:
        load.start()
    me, row = lax.axis_index("mp"), lax.axis_index("dp")
    piece, line_piece = part.shape[0] // lines, line_ref.shape[1] // lines
    mp_peer = [lax.rem(me + k, groups) for k in range(groups)]
    dp_peer = [lax.rem(row + k, lines) for k in range(lines)]
    barrier = pltpu.get_barrier_semaphore()
    for k in range(1, groups):
        pl.semaphore_signal(barrier, 1, device_id={"mp": mp_peer[k]}, device_id_type=MESH_IDS)
    for k in range(1, lines):
        pl.semaphore_signal(barrier, 1, device_id={"dp": dp_peer[k]}, device_id_type=MESH_IDS)
    all_in, all_lines_in, dp_in, dp_lines_in = parted(held)
    all_cells = cells_of(all_in, all_lines_in, groups)
    dp_cells = cells_of(dp_in, dp_lines_in, 1)
    all_ref[...] = jnp.zeros_like(all_ref)
    line_ref[...] = jnp.zeros_like(line_ref)
    for load in loads:
        load.wait()
    for q in range(groups):
        pack(all_in, all_lines_in, all_ref, q, groups, *all_cells)
    pack(dp_in, dp_lines_in, line_ref, 0, 1, *dp_cells)
    all_low[...] = all_ref[...].astype(LOW)
    line_low[...] = line_ref[...].astype(LOW)
    pl.semaphore_wait(barrier, groups + lines - 2)

    def send(source, target, stage, k, axis, peer):
        copy = pltpu.make_async_remote_copy(
            src_ref=source,
            dst_ref=target,
            send_sem=sems[2 * stage].at[k],
            recv_sem=sems[2 * stage + 1].at[k],
            device_id={axis: peer},
            device_id_type=MESH_IDS,
        )
        copy.start()
        return copy

    over_mp = [
        send(all_low.at[mp_peer[k]], all_got.at[k], 0, k, "mp", mp_peer[k])
        for k in range(1, groups)
    ]
    over_dp = [
        send(
            line_low.at[0, pl.ds(dp_peer[k] * line_piece, line_piece)],
            line_got.at[k],
            1,
            k,
            "dp",
            dp_peer[k],
        )
        for k in range(1, lines)
    ]
    yield
    total = all_ref[me]
    for k, copy in enumerate(over_mp, 1):
        copy.wait_recv()
        total = total + all_got[k].astype(F32)
    part[...] = total
    part_low[...] = total.astype(LOW)
    part_dp = [
        send(part_low.at[pl.ds(dp_peer[k] * piece, piece)], part_got.at[k], 2, k, "dp", dp_peer[k])
        for k in range(1, lines)
    ]
    yield
    held = pl.ds(row * piece, piece)
    total = part[held]
    for k, copy in enumerate(part_dp, 1):
        copy.wait_recv()
        total = total + part_got[k].astype(F32)
    all_full[me, held] = total.astype(LOW)
    part_back = [
        send(all_full.at[me, held], all_full.at[me, held], 4, k, "dp", dp_peer[k])
        for k in range(1, lines)
    ]
    mine = pl.ds(row * line_piece, line_piece)
    total = line_ref[0, mine]
    for k, copy in enumerate(over_dp, 1):
        copy.wait_recv()
        total = total + line_got[k].astype(F32)
    line_full[0, mine] = total.astype(LOW)
    line_back = [
        send(line_full.at[0, mine], line_full.at[0, mine], 3, k, "dp", dp_peer[k])
        for k in range(1, lines)
    ]
    yield
    for copy in part_back:
        copy.wait_recv()
    all_back = [
        send(all_full.at[me], all_full.at[me], 5, k, "mp", mp_peer[k]) for k in range(1, groups)
    ]
    yield
    for copy in line_back:
        copy.wait_recv()
    unpack(line_full, dp_out, dp_lines_out, 0, 1, *dp_cells)
    for copy in all_back:
        copy.wait_recv()
    for q in range(groups):
        unpack(all_full, all_out, all_lines_out, q, groups, *all_cells)
    for copy in over_mp + over_dp + part_dp + line_back + part_back + all_back:
        copy.wait_send()


def reduce_devices(name, identity, over_all, over_all_lines, over_dp, over_dp_lines, job):
    groups, lines = lax.axis_size("mp"), lax.axis_size("dp")

    def size_of(blocks, rows, parts):
        cells, lines_in = cells_of(blocks, rows, parts)
        size = len(cells) + -(-len(lines_in) // GRAIN)
        return -(-size // lines) * lines

    count, line_count = size_of(over_all, over_all_lines, groups), size_of(over_dp, over_dp_lines, 1)
    operands = [*over_all, *over_all_lines, *over_dp, *over_dp_lines]
    counts = (len(over_all), len(over_all_lines), len(over_dp), len(over_dp_lines))
    tail = (GRAIN, 128)
    sizes = (groups, lines, lines, lines, lines, groups)
    every, line = (groups, count) + tail, (1, line_count) + tail
    scratch = (
        [
            pltpu.VMEM(every, F32),
            pltpu.VMEM(line, F32),
            pltpu.VMEM(every, LOW),
            pltpu.VMEM(line, LOW),
            pltpu.VMEM(every, LOW),
            pltpu.VMEM((count,) + tail, F32),
            pltpu.VMEM((count,) + tail, LOW),
            pltpu.VMEM((lines, count // lines) + tail, LOW),
            pltpu.VMEM((lines, line_count // lines) + tail, LOW),
            pltpu.VMEM(every, LOW),
            pltpu.VMEM(line, LOW),
        ]
        + [pltpu.VMEM(v.shape, F32) for v in operands]
        + [pltpu.SemaphoreType.DMA((len(operands),))]
        + [pltpu.SemaphoreType.DMA((n,)) for n in sizes for _ in range(2)]
    )
    job_steps, moved, whole_rows, job_shape, job_scratch = job
    n_operands, n_scratch = len(operands), len(scratch)
    out_shape = [shape(v.shape, F32) for v in operands] + [job_shape]
    anywhere = pl.BlockSpec(memory_space=pl.ANY)
    full = lambda v: pl.BlockSpec(v.shape, lambda i: (0,) * v.ndim)
    operands = operands + [*moved, *whole_rows]

    def run(*refs):
        given, refs = refs[: len(operands)], refs[len(operands) :]
        results, held = refs[: len(out_shape)], refs[len(out_shape) :]
        steps = reduce_steps(
            groups, lines, counts, *given[:n_operands], *results[:n_operands], *held[:n_scratch]
        )
        work = job_steps(*given[n_operands:], results[n_operands], *held[n_scratch:])
        next(work)
        for _ in steps:
            next(work, None)
        for _ in work:
            pass

    return call(
        name,
        run,
        tuple(operands),
        (1,),
        [anywhere] * (n_operands + len(moved)) + [full(v) for v in whole_rows],
        [full(v) for v in out_shape[:-1]] + [anywhere],
        out_shape,
        scratch=scratch + job_scratch,
        flops=1000,
        identity=identity,
    )


def token_job(tokens, grad_hidden, parts, gain):
    share, width = grad_hidden.shape
    moved = [tokens, grad_hidden, *parts]

    def steps(*refs):
        sources, gain_ref, out_ref = refs[: len(moved)], refs[len(moved)], refs[len(moved) + 1]
        *held, result, sems = refs[len(moved) + 2 :]
        row = pl.multiple_of(lax.axis_index("mp") * share, share)
        copies = []
        for n, (source, target) in enumerate(zip(sources, held)):
            source = source.at[pl.ds(row, share), :] if n == 0 else source
            copies.append(pltpu.make_async_copy(source, target, sems.at[n]))
            copies[-1].start()
        yield
        for copy in copies:
            copy.wait()
        tile = 32
        gain = gain_ref[...]

        def some(i, carry):
            at = pl.ds(pl.multiple_of(i * tile, tile), tile)
            token, grad, *rest = [ref[at, :].astype(F32) for ref in held]
            result[at, :] = grad + norm_back(sum_of(rest), token, gain)[0]
            return carry

        lax.fori_loop(0, share // tile, some, 0, unroll=2)
        copy = pltpu.make_async_copy(result, out_ref, sems.at[len(moved)])
        copy.start()
        yield
        yield
        copy.wait()

    scratch = [pltpu.VMEM((share, width), v.dtype) for v in moved]
    scratch += [pltpu.VMEM((share, width), F32), pltpu.SemaphoreType.DMA((len(moved) + 1,))]
    return steps, moved, [gain], shape((share, width), F32), scratch


def body(
    tokens,
    cotangent,
    segment_ids,
    attend_gain,
    expand_gain,
    heads_base,
    heads_left,
    heads_right,
    heads_magnitude,
    output_base,
    output_left,
    output_right,
    output_magnitude,
    expand_base,
    expand_left,
    expand_right,
    expand_magnitude,
    shrink_base,
    shrink_left,
    shrink_right,
    shrink_magnitude,
):
    groups = lax.axis_size("mp")
    chips = groups // CORES
    index = lax.axis_index("mp")
    chip, core = index // CORES, index % CORES
    rows, width = tokens.shape
    share = rows // groups
    local_heads, ff = heads_base.shape[2], expand_base.shape[2]
    ff_wide = padded(ff)
    device = jnp.arange(groups, dtype=jnp.int32)
    order = jnp.concatenate(
        [
            (chip + device // CORES) % chips * CORES + (core + 1 + device) % CORES,
            (device // CORES + chips - chip) % chips * CORES + (device + CORES - core + 1) % CORES,
        ]
    ).astype(jnp.int32)

    def tie(*values):
        return lax.optimization_barrier(values)

    def sibling(values):
        return lax.ppermute(
            values, "mp", [(i, i // CORES * CORES + (i + 1) % CORES) for i in range(groups)]
        )

    def to_chip(values, step):
        return lax.ppermute(
            values,
            "mp",
            [((i, ((i // CORES + step) % chips) * CORES + i % CORES)) for i in range(groups)],
        )

    def join(pair):
        return (pair[1].astype(F32) + sibling(pair[0]).astype(F32)).astype(LOW)

    def chip_pairs(places):
        return [places[CORES * step : CORES * (step + 1)] for step in range(chips)]

    def arrive(own):
        return [to_chip(own, chips - step) for step in range(1, chips)]

    def pairs_of(own, near_sibling, arrived):
        return [(near_sibling, own)] + [(sibling(piece), piece) for piece in arrived]

    def in_pairs(order_ref, inputs, grads):
        for step, (taken, grad) in enumerate(zip(inputs, grads)):
            yield (
                [(step, ...), (chips + step, ...)],
                lambda taken=taken: taken[...],
                lambda m, grad=grad: grad[m, :, :ff],
            )

    def in_shrink(order_ref, inputs, grads):
        for step, taken in enumerate(inputs):
            at = slice(CORES * step, CORES * (step + 1))
            yield (
                [(step, ...), (chips, pl.ds(CORES * step, CORES))],
                lambda taken=taken: taken[:, :ff],
                lambda m, at=at: grads[0][at].reshape(-1, grads[0].shape[-1]),
            )

    def in_output(start):
        def plan(order_ref, inputs, grads):
            for n, grad in enumerate(grads):
                yield (
                    [(0, (0, start + n)), (1 + n, ...)],
                    lambda place=start + n: inputs[0][0, place],
                    lambda m, grad=grad: grad[...],
                )

        return plan

    def in_heads(order_ref, inputs, grads):
        for place in range(groups):
            step, side = place // CORES, place % CORES
            me = lax.axis_index("mp")
            group = lax.rem(me // CORES + step, chips) * CORES + lax.rem(me + 1 + side, CORES)
            at = pl.multiple_of(group * share, share)
            rows = pl.ds(place * share, share)
            yield (
                [(0, pl.ds(at, share)), (1, (slice(None), rows))],
                lambda at=at: inputs[0][pl.ds(at, share), :],
                lambda m, rows=rows: grads[0][m, rows, :],
            )

    heads_rows, output_rows = turned(heads_left), turned(output_left[None])
    expand_rows, shrink_rows = turned(expand_left), turned(shrink_left[None])
    heads_mag, output_mag = heads_magnitude, output_magnitude[None]
    expand_mag, shrink_mag = expand_magnitude, shrink_magnitude[None]
    attend_line, expand_line = attend_gain[None], expand_gain[None]

    output_low, shrink_low, squares_part = merge_pair(
        [(output_base, output_rows[0], output_right), (shrink_base, shrink_rows[0], shrink_right)]
    )
    output_low, shrink_low = output_low[None], shrink_low[None]
    (
        normed,
        heads_low,
        post,
        heads_sq,
        heads_across,
        cos_table,
        sine_table,
        output_sq,
        shrink_sq,
        first,
    ) = project_heads(
        tokens,
        attend_line,
        heads_base,
        heads_rows,
        heads_right,
        heads_mag,
        segment_ids,
        squares_part,
        groups,
    )
    heads_out = attend(order, groups, post, first)
    heads_parts = heads_out.reshape(1, groups, share, local_heads)
    joined, output_across = product(
        "output_product", 3, heads_parts, output_low, NN, left=output_rows
    )
    joined, expand_right_tied = tie(joined, expand_right)
    output_parts = [joined[0]] + [to_chip(joined[step], step) for step in range(1, chips)]
    expand_low, expand_sq = merge(expand_base, expand_rows, expand_right_tied, 1024)
    grad_product, shrink_grad = shrink_back(
        order, cotangent, shrink_low, shrink_sq, shrink_mag[None], groups
    )
    output_parts, expand_low, grad_product = tie(output_parts, expand_low, grad_product)
    hidden, normed_own = row_call(
        "hidden",
        hidden_kernel,
        order,
        [(tokens, True)] + [(part, False) for part in output_parts],
        (output_sq[0], output_mag, expand_line),
        (F32, LOW),
        0,
        scale_first,
    )

    def feed(mine, step, **extra):
        return expand(
            4 + step, mine, expand_low, expand_sq, expand_mag, grad_product, step, **extra
        )

    arrived = arrive(normed_own)
    fed = [feed(normed_own, 0, left=expand_rows)]
    arrived, fed = tie(arrived, fed)
    fed = list(fed)
    for step in range(1, chips):
        extra = {}
        if step == chips - 1:
            extra = {"right": expand_right, "before": [f[3] for f in fed]}
        fed.append(feed(arrived[step - 1], step, **extra))
    expand_totals = [f[3] for f in fed]
    joined, shrink_rows_tied = tie([f[4] for f in fed], shrink_rows)
    mid_parts = [joined[0]] + [to_chip(joined[step], step) for step in range(1, chips)]
    shrink_places, shrink_total, shrink_across = shrink_product(
        order, [f[0] for f in fed], shrink_low, shrink_rows_tied, cotangent
    )
    shrink_pairs = chip_pairs(shrink_places)
    expand_adapter = adapter(
        "expand_adapter",
        order,
        in_pairs,
        [f[2] for f in fed],
        [f[1] for f in fed],
        expand_rows,
        expand_right,
        (fed[-1][5], fed[0][5], expand_sq, expand_mag, expand_totals),
    )
    mid_parts, shrink_pairs, expand_adapter = tie(mid_parts, shrink_pairs, expand_adapter)
    grad_hidden, output_grad_own, output_total, expand_gain_part = row_call(
        "hidden_back",
        hidden_back_kernel,
        order,
        [(cotangent, True), (tokens, True), (hidden, False)]
        + [(part, False) for part in mid_parts],
        (output_sq[0], output_mag, expand_line),
        (F32, LOW),
        2,
        scale_first,
    )
    arrived, near_sibling = arrive(output_grad_own), sibling(output_grad_own)
    shrink_joined = [join(pair) for pair in shrink_pairs[1:]]
    shrink_joined, shrink_rows_tied = tie(shrink_joined, shrink_rows)
    shrink_sums = adapter(
        "shrink_adapter",
        order,
        in_shrink,
        [f[0] for f in fed],
        [shrink_grad],
        shrink_rows_tied,
        shrink_right[None],
    )
    output_sums = adapter(
        "output_near_adapter",
        order,
        in_output(0),
        [heads_parts],
        [near_sibling, output_grad_own],
        output_rows,
        output_right[None],
    )
    arrived, near_sibling, shrink_joined, shrink_sums, output_sums = tie(
        arrived, near_sibling, shrink_joined, shrink_sums, output_sums
    )
    output_grad = [
        piece for pair in pairs_of(output_grad_own, near_sibling, arrived) for piece in pair
    ]
    shrink_parts = [shrink_pairs[0][1], sibling(shrink_pairs[0][0])] + [
        to_chip(values, step) for step, values in enumerate(shrink_joined, 1)
    ]
    heads_grads, heads_total = attend_back(
        order,
        groups,
        post,
        first,
        cos_table,
        sine_table,
        heads_mag,
        heads_sq,
        output_low,
        output_grad,
    )
    grad_parts = heads_grads.reshape(3, groups, share, local_heads)
    joined, output_total, shrink_total, attend_gain_part, token_extra = product(
        "normed_product",
        20,
        grad_parts,
        heads_low,
        NT,
        correction=(heads_right, heads_sq, heads_mag, [heads_total]),
        lines=(output_total, shrink_total),
        gain=(normed, attend_line),
    )
    joined, shrink_parts, heads_rows_tied, output_rows_tied = tie(
        joined, shrink_parts, heads_rows, output_rows
    )
    token_parts = [joined[0]] + [to_chip(joined[step], step) for step in range(1, chips)]
    output_mag_part, output_left_part, output_right_part, *shrink_adapter = adapter(
        "output_far_adapter",
        order,
        in_output(CORES),
        [heads_parts],
        output_grad[CORES:],
        output_rows_tied,
        output_right[None],
        (output_low, output_across, output_sq, output_mag, [output_total]),
        output_sums,
        (
            shrink_sums,
            shrink_right[None],
            (shrink_low, shrink_across, shrink_sq, shrink_mag, [shrink_total]),
        ),
    )
    heads_adapter = adapter(
        "heads_adapter",
        order,
        in_heads,
        [normed],
        [heads_grads],
        heads_rows_tied,
        heads_right,
        (token_extra, heads_across, heads_sq, heads_mag, [heads_total]),
    )
    (mixed,) = row_call(
        "mixed",
        mixed_kernel,
        order,
        [(hidden, False)] + [(part, False) for part in shrink_parts],
        (shrink_sq[0], shrink_mag),
        (LOW,),
        0,
        scale_first,
    )
    token_parts, heads_adapter, mixed = tie(token_parts, heads_adapter, mixed)
    *reduced, grad_tokens = reduce_devices(
        "reduce_gradients",
        1,
        [expand_adapter[1], shrink_adapter[2], output_right_part, heads_adapter[1]],
        [expand_gain_part[None], attend_gain_part[None]],
        [expand_adapter[2], shrink_adapter[1], output_left_part, heads_adapter[2]],
        [expand_adapter[0], shrink_adapter[0], output_mag_part, heads_adapter[0]],
        token_job(tokens, grad_hidden, token_parts, attend_line),
    )
    (
        expand_left_grad,
        shrink_right_grad,
        output_right_grad,
        heads_left_grad,
        expand_gain_grad,
        attend_gain_grad,
        expand_right_grad,
        shrink_left_grad,
        output_left_grad,
        heads_right_grad,
        expand_mag_grad,
        shrink_mag_grad,
        output_mag_grad,
        heads_mag_grad,
        grad_tokens,
    ) = copy_out([*reduced, grad_tokens])
    return (
        mixed,
        grad_tokens,
        attend_gain_grad[0],
        expand_gain_grad[0],
        jnp.swapaxes(heads_left_grad, 1, 2),
        heads_right_grad,
        heads_mag_grad,
        output_left_grad[0].T,
        output_right_grad[0],
        output_mag_grad[0],
        jnp.swapaxes(expand_left_grad, 1, 2),
        expand_right_grad,
        expand_mag_grad,
        shrink_left_grad[0].T,
        shrink_right_grad[0],
        shrink_mag_grad[0],
    )


def solution(mesh):
    placed = (
        P("dp", None),
        P("dp", None),
        P("dp", None),
        P(),
        P(),
        P(None, None, "mp"),
        P(),
        P(None, None, "mp"),
        P(None, "mp"),
        P("mp", None),
        P("mp", None),
        P(),
        P(),
        P(None, None, "mp"),
        P(),
        P(None, None, "mp"),
        P(None, "mp"),
        P("mp", None),
        P("mp", None),
        P(),
        P(),
    )
    return jax.shard_map(
        body,
        mesh=mesh,
        in_specs=placed,
        out_specs=(
            P(("dp", "mp"), None),
            P(("dp", "mp"), None),
            P(),
            P(),
            P(),
            P(None, None, "mp"),
            P(None, "mp"),
            P("mp", None),
            P(),
            P(),
            P(),
            P(None, None, "mp"),
            P(None, "mp"),
            P("mp", None),
            P(),
            P(),
        ),
        check_vma=False,
    )
```
